32 devices in a mesh: section: 4 (over y, x), tensor: 4 (over z), dp: 2 (over core).
Axes of the slice: x: 2, y: 2, z: 4, core: 2. Of those that a mesh axis runs over, the one named last changes fastest.
Arguments:
- patches: bfloat16 [1536, 8192], P(('section', 'dp'), 'tensor'), may hold values from -12 to 12
- teacher: bfloat16 [1536, 8192], P(('section', 'dp'), 'tensor'), may hold values from -6 to 6
- critic_pairs: int32 [1536, 2], P(('section', 'dp')), may hold values from 0 to 3, as said below
- left_factors: bfloat16 [4, 4, 64, 128, 128], P('section', None, 'tensor'), may hold values from -0.5 to 0.5
- right_factors: bfloat16 [4, 4, 64, 128, 128], P('section', None, 'tensor'), may hold values from -0.5 to 0.5
- norm_gains: bfloat16 [4, 5, 8192], P('section', None, 'tensor'), may hold values from 0.099609375 to 1.8984375
Outputs:
- d_patches: bfloat16 [1536, 8192], P(('section', 'dp'), 'tensor')
- grad_left: float32 [4, 4, 64, 128, 128], P('section', None, 'tensor')
- grad_right: float32 [4, 4, 64, 128, 128], P('section', None, 'tensor')
The draws below stay inside these ranges and needn't reach their ends.
Inputs may be any that keep to these rules, and one draw needn't show every extreme that they name: `critic_pairs`: each row names two different critics. The rows are cut into aligned blocks, each block being the 192 rows of one index of section+dp. In each block, exactly one third of the rows name the pair of critics 0 and 1. Exactly one sixth of the rows name each of the pairs 0 and 2, 0 and 3, 1 and 2, and 1 and 3. No row names critics 2 and 3 together. So critics 0 and 1 are each named by two thirds of a block's rows, and critics 2 and 3 by one third each. Which rows and which column order are random.
All inputs are finite; a program needn't handle non-finite values.
Results may differ from the reference program's by a relative error of at most 0.012.
Values may be sent and summed in bfloat16 or wider, within the bound.
No kernel may reach another device: no remote copies, remote signals or barrier semaphores. Data moves between devices by JAX's collectives and lax.ppermute only.
A program may use at most 128 MiB of HBM per device.

```python
import math
import jax
import jax.numpy as jnp
from jax import lax

NB = 64
BS = 128
D = 8192
CRITICS = 4
LAYERS = 4
TOK_DEV = 192
TOKENS = 1536


def draw_patches(key, part):
    base_key, rough_key = jax.random.split(jax.random.fold_in(key, 21), 2)
    position = jnp.arange(D, dtype=jnp.float32) / D
    roughness = jax.random.uniform(rough_key, (D,), jnp.float32, 0.5, 1.5)
    rising = jnp.exp(jnp.log(3.0) * position)
    values = jax.random.normal(base_key, (TOKENS, D), jnp.float32)
    return jnp.clip(values * roughness[None, :] * rising[None, :], -12.0, 12.0).astype(jnp.bfloat16)


def draw_teacher(key, part):
    noise_key, size_key, sign_key = jax.random.split(jax.random.fold_in(key, 31), 3)
    magnitude = jax.random.uniform(size_key, (TOKENS, 1), jnp.float32, 2.0, 3.5)
    direction = 2.0 * jax.random.randint(sign_key, (TOKENS, 1), 0, 2).astype(jnp.float32) - 1.0
    noise = jnp.clip(jax.random.normal(noise_key, (TOKENS, D), jnp.float32), -2.5, 2.5)
    return jnp.clip(noise + direction * magnitude, -6.0, 6.0).astype(jnp.bfloat16)


def draw_critic_pairs(key, part):
    blocks = TOKENS // TOK_DEV
    block_keys = jax.random.split(jax.random.fold_in(key, 11), blocks)
    rank_order = jax.vmap(lambda block_key: jax.random.permutation(block_key, TOK_DEV))(block_keys).astype(jnp.int32)
    pair_class = rank_order * 6 // TOK_DEV
    first_ids = jnp.array([0, 0, 0, 0, 1, 1], jnp.int32)
    second_ids = jnp.array([1, 1, 2, 3, 2, 3], jnp.int32)
    smaller = first_ids[pair_class]
    larger = second_ids[pair_class]
    swapped = jax.random.randint(jax.random.fold_in(key, 12), (blocks, TOK_DEV), 0, 2)
    column_one = jnp.where(swapped == 1, larger, smaller)
    column_two = jnp.where(swapped == 1, smaller, larger)
    return jnp.stack([column_one, column_two], axis=-1).reshape(TOKENS, 2).astype(jnp.int32)


def block_levels(own_key, dims, cuts, smallest, top_value):
    def one(axis_at, blocks):
        draws = jax.random.uniform(jax.random.fold_in(jax.random.fold_in(own_key, 6), axis_at), (blocks,), jnp.float32, smallest / len(cuts), top_value / len(cuts))
        return jnp.repeat(jnp.exp(draws), dims[axis_at] // blocks).reshape((-1,) + (1,) * (len(dims) - axis_at - 1))

    loudness = one(*cuts[0])
    for cut in cuts[1:]:
        loudness = loudness * one(*cut)
    return loudness


def bell_draw(own_key, shape, deviation, reach, shards=(), held_as=jnp.bfloat16):
    drawn = jax.random.normal(own_key, shape, jnp.float32) * deviation
    if len(shards) > 0:
        drawn = block_levels(own_key, shape, shards, -0.22, 0.18) * drawn
    return jnp.clip(drawn, min=-reach, max=reach).astype(held_as)


def setup_inputs(seed: int = 0) -> dict:
    splits = jax.random.split(jax.random.key(seed), 7)
    patches = draw_patches(jax.random.fold_in(splits[6], 71), 0)
    teacher = draw_teacher(jax.random.fold_in(splits[6], 71), 0)
    critic_pairs = draw_critic_pairs(jax.random.fold_in(splits[6], 71), 0)
    left_factors = bell_draw(splits[3], (CRITICS, LAYERS, NB, BS, BS), BS ** -0.5, 0.5, ((0, 4), (2, 4)))
    right_factors = bell_draw(splits[4], (CRITICS, LAYERS, NB, BS, BS), BS ** -0.5, 0.5, ((0, 4), (2, 4)))
    norm_gains = jnp.clip(1.0 + 0.18 * jax.random.normal(splits[5], (CRITICS, LAYERS + 1, D), jnp.float32), 0.099609375, 1.8984375).astype(jnp.bfloat16)
    return dict(patches=patches, teacher=teacher, critic_pairs=critic_pairs, left_factors=left_factors, right_factors=right_factors, norm_gains=norm_gains)


EPSILON = 1e-06
TANH_SLOPE = 0.7978845608028654
CUBIC_TERM = 0.044715

def gelu_value(values):
    tangent = jnp.tanh(TANH_SLOPE * (values + CUBIC_TERM * values * values * values))
    return 0.5 * values * (1.0 + tangent)

def gelu_slope(values):
    tangent = jnp.tanh(TANH_SLOPE * (values + CUBIC_TERM * values * values * values))
    return 0.5 * (1.0 + tangent) + 0.5 * values * (1.0 - tangent * tangent) * TANH_SLOPE * (1.0 + 3.0 * CUBIC_TERM * values * values)

def norm_forward(residual, gain_row):
    squares = lax.optimization_barrier(jnp.sum(residual * residual, axis=(1, 2)))
    factor = lax.rsqrt(squares / D + EPSILON)
    return (factor, residual * factor[:, None, None] * gain_row.astype(jnp.float32).reshape(1, NB, BS))

def norm_backward(residual, factor, gain_row, grad_normed, carried):
    weighted = grad_normed * gain_row.astype(jnp.float32).reshape(1, NB, BS)
    inners = lax.optimization_barrier(jnp.sum(weighted * residual, axis=(1, 2)))
    return carried + factor[:, None, None] * weighted - residual * (factor ** 3 * inners / D)[:, None, None]

def critic_pass(residual, target, left_blocks, right_blocks, gain_set):
    row_count = residual.shape[0]
    fold_ratio = BS // NB
    stored = []
    for layer_index in range(LAYERS):
        factor, normed = norm_forward(residual, gain_set[layer_index])
        normed = normed.astype(jnp.bfloat16)
        first_out = jnp.einsum('nki,kij->nkj', normed.astype(jnp.float32), left_blocks[layer_index].astype(jnp.float32)).astype(jnp.bfloat16)
        permuted = first_out.reshape(row_count, NB, NB, fold_ratio)
        right_quad = right_blocks[layer_index].reshape(NB, fold_ratio, NB, BS).astype(jnp.float32)
        mixture = jnp.einsum('nkmp,mpkl->nml', permuted.astype(jnp.float32), right_quad)
        stored.append((residual, factor, normed, permuted, mixture, right_quad))
        residual = residual + gelu_value(mixture)
    factor, output = norm_forward(residual, gain_set[LAYERS])
    gradient = norm_backward(residual, factor, gain_set[LAYERS], output - target.astype(jnp.float32), jnp.zeros_like(residual))
    left_list = []
    right_list = []
    for layer_index in range(LAYERS - 1, -1, -1):
        inputs, factor, normed, permuted, mixture, right_quad = stored[layer_index]
        slopes = (gradient * gelu_slope(mixture)).astype(jnp.bfloat16)
        right_grad = jnp.einsum('nkmp,nml->mpkl', permuted.astype(jnp.float32), slopes.astype(jnp.float32)).reshape(NB, BS, BS)
        arrived = jnp.einsum('nml,mpkl->nkmp', slopes.astype(jnp.float32), right_quad).astype(jnp.bfloat16).reshape(row_count, NB, BS)
        left_grad = jnp.einsum('nki,nkj->kij', normed.astype(jnp.float32), arrived.astype(jnp.float32))
        grad_normed = jnp.einsum('nkj,kij->nki', arrived.astype(jnp.float32), left_blocks[layer_index].astype(jnp.float32))
        gradient = norm_backward(inputs, factor, gain_set[layer_index], grad_normed, gradient)
        left_list.insert(0, left_grad)
        right_list.insert(0, right_grad)
    return (gradient.astype(jnp.bfloat16), jnp.stack(left_list), jnp.stack(right_list))

def reference(patches, teacher, critic_pairs, left_factors, right_factors, norm_gains):
    accumulated = jnp.zeros((TOKENS, D), jnp.float32)
    left_all = []
    right_all = []
    for critic in range(CRITICS):
        member_count = TOKENS // 6 * (4 if critic < 2 else 2)
        named_by = jnp.any(critic_pairs == critic, axis=1)
        sort_keys = jnp.where(named_by, 0, 1).astype(jnp.int32)
        row_ids = jnp.argsort(sort_keys, stable=True)[:member_count].astype(jnp.int32)
        residual = patches[row_ids].astype(jnp.float32).reshape(member_count, NB, BS)
        target = teacher[row_ids].reshape(member_count, NB, BS)
        returned, left_grad, right_grad = critic_pass(residual, target, left_factors[critic], right_factors[critic], norm_gains[critic])
        accumulated = accumulated.at[row_ids].add(returned.reshape(member_count, D).astype(jnp.float32))
        left_all.append(left_grad)
        right_all.append(right_grad)
    grad_factor = 1.0 / math.sqrt(2 * TOKENS)
    return ((accumulated * 0.5).astype(jnp.bfloat16), jnp.stack(left_all) * grad_factor, jnp.stack(right_all) * grad_factor)
```

```python
import math

import jax
import jax.numpy as jnp
from jax import lax
from jax.experimental import pallas as pl
from jax.experimental.pallas import tpu as pltpu
from jax.sharding import PartitionSpec as P

EPSILON = 1e-06
TANH_SLOPE = 0.7978845608028654
CUBIC_TERM = 0.044715


def shifted(value, axis, steps):
    count = lax.axis_size(axis)
    first, last = (max(0, -steps), min(count, count - steps))
    return lax.ppermute(value, axis, [(source, source + steps) for source in range(first, last)])


def gelu_value(values):
    tangent = jnp.tanh(TANH_SLOPE * (values + CUBIC_TERM * values * values * values))
    return 0.5 * values * (1.0 + tangent)


def gelu_slope(values):
    tangent = jnp.tanh(TANH_SLOPE * (values + CUBIC_TERM * values * values * values))
    return 0.5 * (1.0 + tangent) + 0.5 * values * (1.0 - tangent * tangent) * TANH_SLOPE * (
        1.0 + 3.0 * CUBIC_TERM * values * values
    )


def norm_pair(residuals, gain_pair, model_width):
    squares = lax.psum(
        (
            jnp.sum(residuals[0] * residuals[0], axis=(1, 2)),
            jnp.sum(residuals[1] * residuals[1], axis=(1, 2)),
        ),
        "tensor",
    )
    factors = [lax.rsqrt(squares[member] / model_width + EPSILON) for member in range(2)]
    normed = [
        residuals[member] * factors[member][:, None, None] * gain_pair[member][None]
        for member in range(2)
    ]
    return (factors, normed)


def norm_back_pair(residuals, factors, gain_pair, grad_normed, carried, model_width):
    weighted = [grad_normed[member] * gain_pair[member][None] for member in range(2)]
    inners = lax.psum(
        (
            jnp.sum(weighted[0] * residuals[0], axis=(1, 2)),
            jnp.sum(weighted[1] * residuals[1], axis=(1, 2)),
        ),
        "tensor",
    )
    return [
        carried[member]
        + factors[member][:, None, None] * weighted[member]
        - residuals[member] * (factors[member] ** 3 * inners[member] / model_width)[:, None, None]
        for member in range(2)
    ]


def layered_shards(patches, teacher, critic_pairs, left_factors, right_factors, norm_gains):
    sections = lax.axis_size("section")
    tensor_width = lax.axis_size("tensor")
    replicas = lax.axis_size("dp")
    tok_rows = patches.shape[0]
    feat_local = patches.shape[1]
    layer_count = left_factors.shape[1]
    local_blocks = left_factors.shape[2]
    block_size = left_factors.shape[3]
    all_blocks = local_blocks * tensor_width
    fold_ratio = block_size // all_blocks
    model_width = feat_local * tensor_width
    sixth_rows = tok_rows // 6
    leading = 2 * sixth_rows
    critic_ids = jnp.arange(4, dtype=jnp.int32)
    named_by = (
        (critic_pairs[:, 0:1] == critic_ids[None, :])
        | (critic_pairs[:, 1:2] == critic_ids[None, :])
    ).astype(jnp.int32)
    ranking = jnp.cumsum(named_by, axis=0) - 1
    wide_ids = critic_ids[None, :] < 2
    slot_width = 3 * sixth_rows
    spilled = wide_ids & (ranking >= 3 * sixth_rows)
    destination = jnp.where(spilled, critic_ids[None, :] + 2, critic_ids[None, :])
    slot_index = jnp.where(spilled, ranking - sixth_rows, ranking)
    flat_slot = destination * slot_width + slot_index
    chosen = jnp.take_along_axis(flat_slot, critic_pairs, axis=1)
    slot_total = sections * slot_width
    row_ids = jnp.broadcast_to(jnp.arange(tok_rows, dtype=jnp.int32)[:, None], chosen.shape)
    source_row = (
        jnp.full((slot_total,), tok_rows, jnp.int32).at[chosen.reshape(-1)].set(row_ids.reshape(-1))
    )
    send_patch = (
        patches.at[source_row]
        .get(mode="fill", fill_value=0)
        .reshape(sections, slot_width, local_blocks, block_size)
    )
    send_target = (
        teacher.at[source_row]
        .get(mode="fill", fill_value=0)
        .reshape(sections, slot_width, local_blocks, block_size)
    )
    recv_patch, recv_target = (
        lax.all_to_all(send_patch, "section", split_axis=0, concat_axis=0, tiled=True),
        lax.all_to_all(send_target, "section", split_axis=0, concat_axis=0, tiled=True),
    )
    residuals = [
        recv_patch[:, :leading].reshape(-1, local_blocks, block_size).astype(jnp.float32),
        recv_patch[:, leading:].reshape(-1, local_blocks, block_size).astype(jnp.float32),
    ]
    targets = [
        recv_target[:, :leading].reshape(-1, local_blocks, block_size).astype(jnp.float32),
        recv_target[:, leading:].reshape(-1, local_blocks, block_size).astype(jnp.float32),
    ]
    native = (left_factors[0], right_factors[0], norm_gains[0])
    borrowed = shifted((left_factors, right_factors, norm_gains), "section", 2)
    is_wide = lax.axis_index("section") < 2
    second = (
        jnp.where(is_wide, left_factors, borrowed[0])[0],
        jnp.where(is_wide, right_factors, borrowed[1])[0],
        jnp.where(is_wide, norm_gains, borrowed[2])[0],
    )
    left_sets = (native[0], second[0])
    right_sets = (native[1], second[1])
    gain_sets = (
        native[2].astype(jnp.float32).reshape(layer_count + 1, local_blocks, block_size),
        second[2].astype(jnp.float32).reshape(layer_count + 1, local_blocks, block_size),
    )
    stored = []
    for layer_index in range(layer_count):
        gain_pair = [gain_sets[0][layer_index], gain_sets[1][layer_index]]
        factors, normed = norm_pair(residuals, gain_pair, model_width)
        normed = [normed[member].astype(jnp.bfloat16) for member in range(2)]
        first_out = [
            jnp.einsum(
                "nki,kij->nkj",
                normed[member],
                left_sets[member][layer_index],
                preferred_element_type=jnp.float32,
            ).astype(jnp.bfloat16)
            for member in range(2)
        ]
        permuted = (
            lax.all_to_all(first_out[0], "tensor", split_axis=2, concat_axis=1, tiled=True),
            lax.all_to_all(first_out[1], "tensor", split_axis=2, concat_axis=1, tiled=True),
        )
        permuted = [
            permuted[member].reshape(
                permuted[member].shape[0], all_blocks, local_blocks, fold_ratio
            )
            for member in range(2)
        ]
        right_quads = [
            right_sets[member][layer_index].reshape(
                local_blocks, fold_ratio, all_blocks, block_size
            )
            for member in range(2)
        ]
        mixture = [
            jnp.einsum(
                "nkmp,mpkl->nml",
                permuted[member],
                right_quads[member],
                preferred_element_type=jnp.float32,
            )
            for member in range(2)
        ]
        stored.append((residuals, factors, normed, permuted, mixture, right_quads, gain_pair))
        residuals = [residuals[member] + gelu_value(mixture[member]) for member in range(2)]
    final_gains = [gain_sets[0][layer_count], gain_sets[1][layer_count]]
    factors, outputs = norm_pair(residuals, final_gains, model_width)
    gradients = norm_back_pair(
        residuals,
        factors,
        final_gains,
        [outputs[member] - targets[member] for member in range(2)],
        [jnp.zeros_like(residuals[member]) for member in range(2)],
        model_width,
    )
    left_terms = []
    right_terms = []
    for layer_index in range(layer_count - 1, -1, -1):
        inputs, factors, normed, permuted, mixture, right_quads, gain_pair = stored[layer_index]
        slopes = [
            (gradients[member] * gelu_slope(mixture[member])).astype(jnp.bfloat16)
            for member in range(2)
        ]
        right_grad = [
            jnp.einsum(
                "nkmp,nml->mpkl",
                permuted[member],
                slopes[member],
                preferred_element_type=jnp.float32,
            ).reshape(local_blocks, block_size, block_size)
            for member in range(2)
        ]
        back_moved = [
            jnp.einsum(
                "nml,mpkl->nkmp",
                slopes[member],
                right_quads[member],
                preferred_element_type=jnp.float32,
            )
            .astype(jnp.bfloat16)
            .reshape(slopes[member].shape[0], all_blocks, local_blocks * fold_ratio)
            for member in range(2)
        ]
        arrived = (
            lax.all_to_all(back_moved[0], "tensor", split_axis=1, concat_axis=2, tiled=True),
            lax.all_to_all(back_moved[1], "tensor", split_axis=1, concat_axis=2, tiled=True),
        )
        left_grad = [
            jnp.einsum(
                "nki,nkj->kij", normed[member], arrived[member], preferred_element_type=jnp.float32
            )
            for member in range(2)
        ]
        grad_normed = [
            jnp.einsum(
                "nkj,kij->nki",
                arrived[member],
                left_sets[member][layer_index],
                preferred_element_type=jnp.float32,
            )
            for member in range(2)
        ]
        gradients = norm_back_pair(inputs, factors, gain_pair, grad_normed, gradients, model_width)
        layer_left = jnp.stack(left_grad)
        layer_right = jnp.stack(right_grad)
        layer_left, layer_right = (
            lax.psum(layer_left.astype(jnp.bfloat16), "dp").astype(jnp.float32),
            lax.psum(layer_right.astype(jnp.bfloat16), "dp").astype(jnp.float32),
        )
        left_terms.insert(0, layer_left)
        right_terms.insert(0, layer_right)
    left_stack = jnp.stack(left_terms)
    right_stack = jnp.stack(right_terms)
    repaid = (
        shifted(left_stack[:, 1].astype(jnp.bfloat16), "section", -2).astype(jnp.float32),
        shifted(right_stack[:, 1].astype(jnp.bfloat16), "section", -2).astype(jnp.float32),
    )
    is_wide = lax.axis_index("section") < 2
    left_total = left_stack[:, 0] + jnp.where(is_wide, left_stack[:, 1] + repaid[0], 0.0)
    right_total = right_stack[:, 0] + jnp.where(is_wide, right_stack[:, 1] + repaid[1], 0.0)
    grad_factor = 1.0 / math.sqrt(2 * tok_rows * sections * replicas)
    returned = [
        gradients[member].astype(jnp.bfloat16).reshape(sections, -1, local_blocks, block_size)
        for member in range(2)
    ]
    back_lead, back_trail = (
        lax.all_to_all(returned[0], "section", split_axis=0, concat_axis=0, tiled=True),
        lax.all_to_all(returned[1], "section", split_axis=0, concat_axis=0, tiled=True),
    )
    gathered = jnp.concatenate((back_lead, back_trail), axis=1).reshape(
        slot_total, local_blocks, block_size
    )
    combined = (
        gathered[chosen[:, 0]].astype(jnp.float32) + gathered[chosen[:, 1]].astype(jnp.float32)
    ) * 0.5
    d_patches = combined.astype(jnp.bfloat16).reshape(tok_rows, feat_local)
    return (d_patches, (left_total * grad_factor)[None], (right_total * grad_factor)[None])


VMEM_LIMIT = 56 * 1024 * 1024


def planes_fit(mesh):
    return mesh.shape["tensor"] == mesh.shape["section"]


def inner_dot(left, right, left_dim, right_dim):
    return lax.dot_general(
        left,
        right,
        (((left_dim,), (right_dim,)), ((), ())),
        preferred_element_type=jnp.float32,
    )


def fold_rows(values):
    return jnp.sum(values.reshape(values.shape[0] // 8, 8, values.shape[1]), axis=0)


def gathered_place(block, layout):
    width, replicas, pieces, chunk = layout
    local = replicas * pieces * chunk
    source = block // local
    rest = block % local
    replica = rest // (pieces * chunk)
    piece = (rest % (pieces * chunk)) // chunk
    owner = (source + piece) % width
    return (owner * replicas + replica) * pieces + piece, rest % chunk


def forward_kernel(layout, h_ref, w_ref, gain_ref, out_ref, u_ref, z_ref, slope_ref, scale_ref, mid_ref):
    features, slots = h_ref.shape
    size = w_ref.shape[-1]
    blocks = features // size
    fold = size // blocks

    def squares(block, total):
        part = h_ref[pl.ds(pl.multiple_of(block * size, size), size), :].astype(jnp.float32)
        return total + fold_rows(part * part)

    total = lax.fori_loop(0, blocks, squares, jnp.zeros((8, slots), jnp.float32), unroll=4)
    scale = lax.rsqrt(jnp.sum(total, axis=0, keepdims=True) / features + EPSILON)
    scale_ref[...] = jnp.broadcast_to(scale, scale_ref.shape)

    def left(block, carry):
        rows = pl.ds(pl.multiple_of(block * size, size), size)
        place, at = gathered_place(block, layout)
        normed = h_ref[rows, :].astype(jnp.float32) * scale * gain_ref[rows, :].astype(jnp.float32)
        normed = normed.astype(jnp.bfloat16)
        u_ref[rows, :] = normed
        mid_ref[rows, :] = inner_dot(w_ref[place, 0, at], normed, 0, 0)
        return carry

    lax.fori_loop(0, blocks, left, 0, unroll=4)

    def right(block, carry):
        rows = pl.ds(pl.multiple_of(block * size, size), size)
        place, at = gathered_place(block, layout)
        moved = [mid_ref[pl.ds(block * fold + q, blocks, stride=size), :] for q in range(fold)]
        moved = jnp.concatenate(moved, axis=0).astype(jnp.bfloat16)
        z_ref[rows, :] = moved
        mixture = inner_dot(w_ref[place, 1, at], moved, 0, 0)
        squared = mixture * mixture
        tangent = jnp.tanh(TANH_SLOPE * mixture * (1.0 + CUBIC_TERM * squared))
        half = 0.5 * (1.0 + tangent)
        out_ref[rows, :] = h_ref[rows, :].astype(jnp.float32) + mixture * half
        slope = half + (0.5 * TANH_SLOPE) * mixture * (1.0 - tangent * tangent) * (
            1.0 + 3.0 * CUBIC_TERM * squared
        )
        slope_ref[rows, :] = slope.astype(jnp.bfloat16)
        return carry

    lax.fori_loop(0, blocks, right, 0, unroll=4)


def turn_kernel(size, h_ref, target_ref, gain_ref, out_ref):
    features, slots = h_ref.shape
    blocks = features // size
    zero = jnp.zeros((8, slots), jnp.float32)

    def sums(block, totals):
        rows = pl.ds(pl.multiple_of(block * size, size), size)
        part = h_ref[rows, :]
        gain = gain_ref[rows, :].astype(jnp.float32)
        scaled = part * gain
        target = target_ref[rows, :].astype(jnp.float32)
        return (
            totals[0] + fold_rows(part * part),
            totals[1] + fold_rows(scaled * scaled),
            totals[2] + fold_rows(scaled * target),
        )

    totals = lax.fori_loop(0, blocks, sums, (zero, zero, zero), unroll=4)
    squares, gained, crossed = [jnp.sum(total, axis=0, keepdims=True) for total in totals]
    scale = lax.rsqrt(squares / features + EPSILON)
    inner = scale * gained - crossed
    back = scale * scale * scale * inner / features

    def write(block, carry):
        rows = pl.ds(pl.multiple_of(block * size, size), size)
        part = h_ref[rows, :]
        gain = gain_ref[rows, :].astype(jnp.float32)
        error = (part * scale * gain - target_ref[rows, :].astype(jnp.float32)) * gain
        out_ref[rows, :] = scale * error - part * back
        return carry

    lax.fori_loop(0, blocks, write, 0, unroll=4)


def backward_kernel(
    layout, g_ref, slope_ref, z_ref, u_ref, h_ref, scale_ref, w_ref, gain_ref, out_ref, gw_ref, mid_ref, turned_ref, e_ref
):
    features, slots = h_ref.shape
    size = w_ref.shape[-1]
    blocks = features // size
    fold = size // blocks

    def right(block, carry):
        rows = pl.ds(pl.multiple_of(block * size, size), size)
        place, at = gathered_place(block, layout)
        steep = (g_ref[rows, :] * slope_ref[rows, :].astype(jnp.float32)).astype(jnp.bfloat16)
        gw_ref[place, 1, at] = inner_dot(z_ref[rows, :], steep, 1, 1).astype(jnp.bfloat16)
        mid_ref[rows, :] = inner_dot(w_ref[place, 1, at], steep, 1, 0)
        return carry

    lax.fori_loop(0, blocks, right, 0, unroll=4)
    scale = scale_ref[0:1, :]

    def left(block, total):
        rows = pl.ds(pl.multiple_of(block * size, size), size)
        place, at = gathered_place(block, layout)
        slot = block % turned_ref.shape[0]
        for q in range(fold):
            turned_ref[slot, pl.ds(q, blocks, stride=fold), :] = mid_ref[
                pl.ds(q * blocks + block, blocks, stride=size), :
            ]
        arrived = turned_ref[slot].astype(jnp.bfloat16)
        gw_ref[place, 0, at] = inner_dot(u_ref[rows, :], arrived, 1, 1).astype(jnp.bfloat16)
        weighted = inner_dot(w_ref[place, 0, at], arrived, 1, 0) * gain_ref[rows, :].astype(jnp.float32)
        e_ref[rows, :] = weighted
        return total + fold_rows(weighted * h_ref[rows, :].astype(jnp.float32))

    total = lax.fori_loop(0, blocks, left, jnp.zeros((8, slots), jnp.float32), unroll=4)
    inner = jnp.sum(total, axis=0, keepdims=True)
    back = scale * scale * scale * inner / features

    def write(block, carry):
        rows = pl.ds(pl.multiple_of(block * size, size), size)
        part = h_ref[rows, :].astype(jnp.float32)
        out_ref[rows, :] = (g_ref[rows, :] + scale * e_ref[rows, :] - part * back).astype(out_ref.dtype)
        return carry

    lax.fori_loop(0, blocks, write, 0, unroll=4)


def shape_of(shape, dtype):
    return jax.ShapeDtypeStruct(shape, dtype)


def run_forward(h, weights, gain, layout):
    features, slots = h.shape
    whole = (features, slots)
    flops = 4 * features * slots * weights.shape[-1]
    return pl.pallas_call(
        lambda *refs: forward_kernel(layout, *refs),
        out_shape=(
            shape_of(whole, jnp.float32),
            shape_of(whole, jnp.bfloat16),
            shape_of(whole, jnp.bfloat16),
            shape_of(whole, jnp.bfloat16),
            shape_of((8, slots), jnp.float32),
        ),
        scratch_shapes=[pltpu.VMEM(whole, jnp.float32)],
        compiler_params=pltpu.CompilerParams(vmem_limit_bytes=VMEM_LIMIT),
        cost_estimate=pl.CostEstimate(
            flops=4 * flops, bytes_accessed=20 * features * slots, transcendentals=features * slots
        ),
        name="forward_layer",
    )(h, weights, gain)


def run_turn(h, target, gain, size):
    return pl.pallas_call(
        lambda *refs: turn_kernel(size, *refs),
        out_shape=shape_of(h.shape, jnp.float32),
        compiler_params=pltpu.CompilerParams(vmem_limit_bytes=VMEM_LIMIT),
        cost_estimate=pl.CostEstimate(flops=20 * h.size, bytes_accessed=12 * h.size, transcendentals=0),
        name="turn",
    )(h, target, gain)


def run_backward(g, slope, z, u, h, scale, weights, gain, layout, out_type):
    features, slots = h.shape
    size = weights.shape[-1]
    flops = 8 * features * slots * size
    return pl.pallas_call(
        lambda *refs: backward_kernel(layout, *refs),
        out_shape=(shape_of(h.shape, out_type), shape_of(weights.shape, jnp.bfloat16)),
        scratch_shapes=[
            pltpu.VMEM(h.shape, jnp.float32),
            pltpu.VMEM((4, size, slots), jnp.float32),
            pltpu.VMEM(h.shape, jnp.float32),
        ],
        compiler_params=pltpu.CompilerParams(vmem_limit_bytes=VMEM_LIMIT),
        cost_estimate=pl.CostEstimate(
            flops=4 * flops, bytes_accessed=30 * features * slots, transcendentals=0
        ),
        name="backward_layer",
    )(g, slope, z, u, h, scale, weights, gain)


def homeward(pairs):
    return [(target, source) for source, target in pairs]


def plane_shards(patches, teacher, critic_pairs, left_factors, right_factors, norm_gains):
    width = lax.axis_size("section")
    replicas = lax.axis_size("dp")
    tok_rows, feat_local = patches.shape
    layer_count, local_blocks, size = left_factors.shape[1:4]
    features = feat_local * width
    wide = 2 * tok_rows // 3
    pieces = width
    chunk = local_blocks // (replicas * pieces)
    layout = (width, replicas, pieces, chunk)
    routes = [
        [
            (c * width + t, ((t + k) % width) * width + c)
            for c in range(width)
            for t in range(width)
        ]
        for k in range(pieces)
    ]
    axes = ("section", "tensor")

    critic_ids = jnp.arange(width, dtype=jnp.int32)
    named = (critic_pairs[:, 0:1] == critic_ids) | (critic_pairs[:, 1:2] == critic_ids)
    earlier = jnp.tril(jnp.ones((tok_rows, tok_rows), jnp.bfloat16), -1)
    rank = jnp.dot(earlier, named.astype(jnp.bfloat16), preferred_element_type=jnp.float32)
    rank = rank.astype(jnp.int32)
    places = jnp.arange(wide, dtype=jnp.int32)
    chosen = (named[:, :, None] & (rank[:, :, None] == places)).astype(jnp.bfloat16)

    def dispatch(values):
        sent = jnp.stack(
            [inner_dot(values, chosen[:, c], 0, 0).astype(jnp.bfloat16) for c in range(width)]
        )
        got = lax.all_to_all(sent, "tensor", split_axis=0, concat_axis=0, tiled=True)
        return got.reshape(features, wide)

    residual = dispatch(patches)

    own_half = lax.axis_index("dp") * (pieces * chunk)
    halves = [
        lax.dynamic_slice_in_dim(factor[0], own_half, pieces * chunk, axis=1).reshape(
            layer_count, pieces, chunk, size, size
        )
        for factor in (left_factors, right_factors)
    ]
    halves = jnp.stack(halves, axis=2)
    came = [lax.ppermute(halves[:, k], axes, routes[k]) for k in range(pieces)]
    came_gains = [lax.ppermute(norm_gains[0], axes, routes[k]) for k in range(pieces)]
    me = lax.axis_index("section")
    order = (me - jnp.arange(width)) % width
    gains = jnp.stack(came_gains)[order]
    gains = gains.transpose(1, 0, 2).reshape(layer_count + 1, features)
    gains = jnp.broadcast_to(gains[:, :, None], (layer_count + 1, features, wide))

    weights = []
    for layer in range(layer_count):
        mine = jnp.stack([came[k][layer] for k in range(pieces)])
        every = lax.all_gather(mine, ("section", "dp"), axis=0, tiled=True)
        weights.append(every)
    target = dispatch(teacher)

    stored = []
    for layer in range(layer_count):
        following, u, z, slope, scale = run_forward(residual, weights[layer], gains[layer], layout)
        stored.append((slope, z, u, residual, scale))
        residual = following
    gradient = run_turn(residual, target, gains[layer_count], size)
    home = []
    for layer in range(layer_count - 1, -1, -1):
        out_type = jnp.float32 if layer > 0 else jnp.bfloat16
        gradient, factor_grads = run_backward(
            gradient, *stored[layer], weights[layer], gains[layer], layout, out_type
        )
        summed = lax.psum_scatter(factor_grads, ("section", "dp"), scatter_dimension=0, tiled=True)
        back = [lax.ppermute(summed[k], axes, homeward(routes[k])) for k in range(pieces)]
        back = jnp.stack(back, axis=1).reshape(2, pieces * chunk, size, size)
        home.insert(0, lax.all_gather(back, "dp", axis=1, tiled=True))
    grad_factor = 1.0 / math.sqrt(2 * tok_rows * width * replicas)
    grads = jnp.stack(home, axis=1).astype(jnp.float32) * grad_factor

    returned = gradient.reshape(width, feat_local, wide)
    returned = lax.all_to_all(returned, "tensor", split_axis=0, concat_axis=0, tiled=True)
    combined = sum(inner_dot(chosen[:, c], returned[c], 1, 1) for c in range(width))
    d_patches = (0.5 * combined).astype(jnp.bfloat16)
    return (d_patches, grads[0][None], grads[1][None])


def solution(mesh):
    in_specs = (
        P(("section", "dp"), "tensor"),
        P(("section", "dp"), "tensor"),
        P(("section", "dp"), None),
        P("section", None, "tensor", None, None),
        P("section", None, "tensor", None, None),
        P("section", None, "tensor"),
    )
    out_specs = (
        P(("section", "dp"), "tensor"),
        P("section", None, "tensor", None, None),
        P("section", None, "tensor", None, None),
    )
    body = plane_shards if planes_fit(mesh) else layered_shards
    return jax.shard_map(
        body, mesh=mesh, in_specs=in_specs, out_specs=out_specs, check_vma=False)
```

```python
import math

import jax
import jax.numpy as jnp
from jax import lax
from jax.experimental import pallas as pl
from jax.experimental.pallas import tpu as pltpu
from jax.sharding import PartitionSpec as P

EPSILON = 1e-06
TANH_SLOPE = 0.7978845608028654
CUBIC_TERM = 0.044715


def shifted(value, axis, steps):
    count = lax.axis_size(axis)
    first, last = (max(0, -steps), min(count, count - steps))
    return lax.ppermute(value, axis, [(source, source + steps) for source in range(first, last)])


def gelu_value(values):
    tangent = jnp.tanh(TANH_SLOPE * (values + CUBIC_TERM * values * values * values))
    return 0.5 * values * (1.0 + tangent)


def gelu_slope(values):
    tangent = jnp.tanh(TANH_SLOPE * (values + CUBIC_TERM * values * values * values))
    return 0.5 * (1.0 + tangent) + 0.5 * values * (1.0 - tangent * tangent) * TANH_SLOPE * (
        1.0 + 3.0 * CUBIC_TERM * values * values
    )


def norm_pair(residuals, gain_pair, model_width):
    squares = lax.psum(
        (
            jnp.sum(residuals[0] * residuals[0], axis=(1, 2)),
            jnp.sum(residuals[1] * residuals[1], axis=(1, 2)),
        ),
        "tensor",
    )
    factors = [lax.rsqrt(squares[member] / model_width + EPSILON) for member in range(2)]
    normed = [
        residuals[member] * factors[member][:, None, None] * gain_pair[member][None]
        for member in range(2)
    ]
    return (factors, normed)


def norm_back_pair(residuals, factors, gain_pair, grad_normed, carried, model_width):
    weighted = [grad_normed[member] * gain_pair[member][None] for member in range(2)]
    inners = lax.psum(
        (
            jnp.sum(weighted[0] * residuals[0], axis=(1, 2)),
            jnp.sum(weighted[1] * residuals[1], axis=(1, 2)),
        ),
        "tensor",
    )
    return [
        carried[member]
        + factors[member][:, None, None] * weighted[member]
        - residuals[member] * (factors[member] ** 3 * inners[member] / model_width)[:, None, None]
        for member in range(2)
    ]


def layered_shards(patches, teacher, critic_pairs, left_factors, right_factors, norm_gains):
    sections = lax.axis_size("section")
    tensor_width = lax.axis_size("tensor")
    replicas = lax.axis_size("dp")
    tok_rows = patches.shape[0]
    feat_local = patches.shape[1]
    layer_count = left_factors.shape[1]
    local_blocks = left_factors.shape[2]
    block_size = left_factors.shape[3]
    all_blocks = local_blocks * tensor_width
    fold_ratio = block_size // all_blocks
    model_width = feat_local * tensor_width
    sixth_rows = tok_rows // 6
    leading = 2 * sixth_rows
    critic_ids = jnp.arange(4, dtype=jnp.int32)
    named_by = (
        (critic_pairs[:, 0:1] == critic_ids[None, :])
        | (critic_pairs[:, 1:2] == critic_ids[None, :])
    ).astype(jnp.int32)
    ranking = jnp.cumsum(named_by, axis=0) - 1
    wide_ids = critic_ids[None, :] < 2
    slot_width = 3 * sixth_rows
    spilled = wide_ids & (ranking >= 3 * sixth_rows)
    destination = jnp.where(spilled, critic_ids[None, :] + 2, critic_ids[None, :])
    slot_index = jnp.where(spilled, ranking - sixth_rows, ranking)
    flat_slot = destination * slot_width + slot_index
    chosen = jnp.take_along_axis(flat_slot, critic_pairs, axis=1)
    slot_total = sections * slot_width
    row_ids = jnp.broadcast_to(jnp.arange(tok_rows, dtype=jnp.int32)[:, None], chosen.shape)
    source_row = (
        jnp.full((slot_total,), tok_rows, jnp.int32).at[chosen.reshape(-1)].set(row_ids.reshape(-1))
    )
    send_patch = (
        patches.at[source_row]
        .get(mode="fill", fill_value=0)
        .reshape(sections, slot_width, local_blocks, block_size)
    )
    send_target = (
        teacher.at[source_row]
        .get(mode="fill", fill_value=0)
        .reshape(sections, slot_width, local_blocks, block_size)
    )
    recv_patch, recv_target = (
        lax.all_to_all(send_patch, "section", split_axis=0, concat_axis=0, tiled=True),
        lax.all_to_all(send_target, "section", split_axis=0, concat_axis=0, tiled=True),
    )
    residuals = [
        recv_patch[:, :leading].reshape(-1, local_blocks, block_size).astype(jnp.float32),
        recv_patch[:, leading:].reshape(-1, local_blocks, block_size).astype(jnp.float32),
    ]
    targets = [
        recv_target[:, :leading].reshape(-1, local_blocks, block_size).astype(jnp.float32),
        recv_target[:, leading:].reshape(-1, local_blocks, block_size).astype(jnp.float32),
    ]
    native = (left_factors[0], right_factors[0], norm_gains[0])
    borrowed = shifted((left_factors, right_factors, norm_gains), "section", 2)
    is_wide = lax.axis_index("section") < 2
    second = (
        jnp.where(is_wide, left_factors, borrowed[0])[0],
        jnp.where(is_wide, right_factors, borrowed[1])[0],
        jnp.where(is_wide, norm_gains, borrowed[2])[0],
    )
    left_sets = (native[0], second[0])
    right_sets = (native[1], second[1])
    gain_sets = (
        native[2].astype(jnp.float32).reshape(layer_count + 1, local_blocks, block_size),
        second[2].astype(jnp.float32).reshape(layer_count + 1, local_blocks, block_size),
    )
    stored = []
    for layer_index in range(layer_count):
        gain_pair = [gain_sets[0][layer_index], gain_sets[1][layer_index]]
        factors, normed = norm_pair(residuals, gain_pair, model_width)
        normed = [normed[member].astype(jnp.bfloat16) for member in range(2)]
        first_out = [
            jnp.einsum(
                "nki,kij->nkj",
                normed[member],
                left_sets[member][layer_index],
                preferred_element_type=jnp.float32,
            ).astype(jnp.bfloat16)
            for member in range(2)
        ]
        permuted = (
            lax.all_to_all(first_out[0], "tensor", split_axis=2, concat_axis=1, tiled=True),
            lax.all_to_all(first_out[1], "tensor", split_axis=2, concat_axis=1, tiled=True),
        )
        permuted = [
            permuted[member].reshape(
                permuted[member].shape[0], all_blocks, local_blocks, fold_ratio
            )
            for member in range(2)
        ]
        right_quads = [
            right_sets[member][layer_index].reshape(
                local_blocks, fold_ratio, all_blocks, block_size
            )
            for member in range(2)
        ]
        mixture = [
            jnp.einsum(
                "nkmp,mpkl->nml",
                permuted[member],
                right_quads[member],
                preferred_element_type=jnp.float32,
            )
            for member in range(2)
        ]
        stored.append((residuals, factors, normed, permuted, mixture, right_quads, gain_pair))
        residuals = [residuals[member] + gelu_value(mixture[member]) for member in range(2)]
    final_gains = [gain_sets[0][layer_count], gain_sets[1][layer_count]]
    factors, outputs = norm_pair(residuals, final_gains, model_width)
    gradients = norm_back_pair(
        residuals,
        factors,
        final_gains,
        [outputs[member] - targets[member] for member in range(2)],
        [jnp.zeros_like(residuals[member]) for member in range(2)],
        model_width,
    )
    left_terms = []
    right_terms = []
    for layer_index in range(layer_count - 1, -1, -1):
        inputs, factors, normed, permuted, mixture, right_quads, gain_pair = stored[layer_index]
        slopes = [
            (gradients[member] * gelu_slope(mixture[member])).astype(jnp.bfloat16)
            for member in range(2)
        ]
        right_grad = [
            jnp.einsum(
                "nkmp,nml->mpkl",
                permuted[member],
                slopes[member],
                preferred_element_type=jnp.float32,
            ).reshape(local_blocks, block_size, block_size)
            for member in range(2)
        ]
        back_moved = [
            jnp.einsum(
                "nml,mpkl->nkmp",
                slopes[member],
                right_quads[member],
                preferred_element_type=jnp.float32,
            )
            .astype(jnp.bfloat16)
            .reshape(slopes[member].shape[0], all_blocks, local_blocks * fold_ratio)
            for member in range(2)
        ]
        arrived = (
            lax.all_to_all(back_moved[0], "tensor", split_axis=1, concat_axis=2, tiled=True),
            lax.all_to_all(back_moved[1], "tensor", split_axis=1, concat_axis=2, tiled=True),
        )
        left_grad = [
            jnp.einsum(
                "nki,nkj->kij", normed[member], arrived[member], preferred_element_type=jnp.float32
            )
            for member in range(2)
        ]
        grad_normed = [
            jnp.einsum(
                "nkj,kij->nki",
                arrived[member],
                left_sets[member][layer_index],
                preferred_element_type=jnp.float32,
            )
            for member in range(2)
        ]
        gradients = norm_back_pair(inputs, factors, gain_pair, grad_normed, gradients, model_width)
        layer_left = jnp.stack(left_grad)
        layer_right = jnp.stack(right_grad)
        layer_left, layer_right = (
            lax.psum(layer_left.astype(jnp.bfloat16), "dp").astype(jnp.float32),
            lax.psum(layer_right.astype(jnp.bfloat16), "dp").astype(jnp.float32),
        )
        left_terms.insert(0, layer_left)
        right_terms.insert(0, layer_right)
    left_stack = jnp.stack(left_terms)
    right_stack = jnp.stack(right_terms)
    repaid = (
        shifted(left_stack[:, 1].astype(jnp.bfloat16), "section", -2).astype(jnp.float32),
        shifted(right_stack[:, 1].astype(jnp.bfloat16), "section", -2).astype(jnp.float32),
    )
    is_wide = lax.axis_index("section") < 2
    left_total = left_stack[:, 0] + jnp.where(is_wide, left_stack[:, 1] + repaid[0], 0.0)
    right_total = right_stack[:, 0] + jnp.where(is_wide, right_stack[:, 1] + repaid[1], 0.0)
    grad_factor = 1.0 / math.sqrt(2 * tok_rows * sections * replicas)
    returned = [
        gradients[member].astype(jnp.bfloat16).reshape(sections, -1, local_blocks, block_size)
        for member in range(2)
    ]
    back_lead, back_trail = (
        lax.all_to_all(returned[0], "section", split_axis=0, concat_axis=0, tiled=True),
        lax.all_to_all(returned[1], "section", split_axis=0, concat_axis=0, tiled=True),
    )
    gathered = jnp.concatenate((back_lead, back_trail), axis=1).reshape(
        slot_total, local_blocks, block_size
    )
    combined = (
        gathered[chosen[:, 0]].astype(jnp.float32) + gathered[chosen[:, 1]].astype(jnp.float32)
    ) * 0.5
    d_patches = combined.astype(jnp.bfloat16).reshape(tok_rows, feat_local)
    return (d_patches, (left_total * grad_factor)[None], (right_total * grad_factor)[None])


VMEM_LIMIT = 56 * 1024 * 1024


def planes_fit(mesh):
    sections = mesh.shape["section"]
    paired = mesh.shape["dp"] == 2 and sections & (sections - 1) == 0
    return paired and mesh.shape["tensor"] == sections


def inner_dot(left, right, left_dim, right_dim):
    return lax.dot_general(
        left,
        right,
        (((left_dim,), (right_dim,)), ((), ())),
        preferred_element_type=jnp.float32,
    )


def fold_rows(values):
    return jnp.sum(values.reshape(values.shape[0] // 8, 8, values.shape[1]), axis=0)


def over_blocks(table_ref, parts, step, carry):
    start = 0
    for part in parts:
        weights = part[0] if isinstance(part, tuple) else part
        chunk = weights.shape[2]
        count = weights.shape[0] * chunk

        def body(index, carry, part=part, chunk=chunk, start=start):
            block = table_ref[start + index]
            return step(block, part, (index // chunk, index % chunk), carry)

        carry = lax.fori_loop(0, count, body, carry, unroll=4)
        start += count
    return carry


def forward_kernel(
    table_ref, h_ref, own_ref, peer_ref, gain_ref, out_ref, u_ref, z_ref, slope_ref, scale_ref, mid_ref
):
    features, slots = h_ref.shape
    size = own_ref.shape[-1]
    blocks = features // size
    fold = size // blocks

    def squares(block, total):
        part = h_ref[pl.ds(pl.multiple_of(block * size, size), size), :].astype(jnp.float32)
        return total + fold_rows(part * part)

    total = lax.fori_loop(0, blocks, squares, jnp.zeros((8, slots), jnp.float32), unroll=4)
    scale = lax.rsqrt(jnp.sum(total, axis=0, keepdims=True) / features + EPSILON)
    scale_ref[...] = jnp.broadcast_to(scale, scale_ref.shape)

    def left(block, part, at, carry):
        rows = pl.ds(pl.multiple_of(block * size, size), size)
        normed = h_ref[rows, :].astype(jnp.float32) * scale * gain_ref[rows, :].astype(jnp.float32)
        normed = normed.astype(jnp.bfloat16)
        u_ref[rows, :] = normed
        mid_ref[rows, :] = inner_dot(part[at[0], 0, at[1]], normed, 0, 0)
        return carry

    over_blocks(table_ref, (own_ref, peer_ref), left, 0)

    def right(block, part, at, carry):
        rows = pl.ds(pl.multiple_of(block * size, size), size)
        moved = [mid_ref[pl.ds(block * fold + q, blocks, stride=size), :] for q in range(fold)]
        moved = jnp.concatenate(moved, axis=0).astype(jnp.bfloat16)
        z_ref[rows, :] = moved
        mixture = inner_dot(part[at[0], 1, at[1]], moved, 0, 0)
        squared = mixture * mixture
        tangent = jnp.tanh(TANH_SLOPE * mixture * (1.0 + CUBIC_TERM * squared))
        half = 0.5 * (1.0 + tangent)
        out_ref[rows, :] = h_ref[rows, :].astype(jnp.float32) + mixture * half
        slope = half + (0.5 * TANH_SLOPE) * mixture * (1.0 - tangent * tangent) * (
            1.0 + 3.0 * CUBIC_TERM * squared
        )
        slope_ref[rows, :] = slope.astype(jnp.bfloat16)
        return carry

    over_blocks(table_ref, (own_ref, peer_ref), right, 0)


def turn_kernel(size, h_ref, target_ref, gain_ref, out_ref):
    features, slots = h_ref.shape
    blocks = features // size
    zero = jnp.zeros((8, slots), jnp.float32)

    def sums(block, totals):
        rows = pl.ds(pl.multiple_of(block * size, size), size)
        part = h_ref[rows, :]
        gain = gain_ref[rows, :].astype(jnp.float32)
        scaled = part * gain
        target = target_ref[rows, :].astype(jnp.float32)
        return (
            totals[0] + fold_rows(part * part),
            totals[1] + fold_rows(scaled * scaled),
            totals[2] + fold_rows(scaled * target),
        )

    totals = lax.fori_loop(0, blocks, sums, (zero, zero, zero), unroll=4)
    squares, gained, crossed = [jnp.sum(total, axis=0, keepdims=True) for total in totals]
    scale = lax.rsqrt(squares / features + EPSILON)
    inner = scale * gained - crossed
    back = scale * scale * scale * inner / features

    def write(block, carry):
        rows = pl.ds(pl.multiple_of(block * size, size), size)
        part = h_ref[rows, :]
        gain = gain_ref[rows, :].astype(jnp.float32)
        error = (part * scale * gain - target_ref[rows, :].astype(jnp.float32)) * gain
        out_ref[rows, :] = scale * error - part * back
        return carry

    lax.fori_loop(0, blocks, write, 0, unroll=4)


def backward_kernel(
    table_ref, g_ref, slope_ref, z_ref, u_ref, h_ref, scale_ref, own_ref, peer_ref, gain_ref,
    out_ref, own_grad_ref, peer_grad_ref, mid_ref, turned_ref, e_ref
):
    features, slots = h_ref.shape
    size = own_ref.shape[-1]
    blocks = features // size
    fold = size // blocks
    parts = ((own_ref, own_grad_ref), (peer_ref, peer_grad_ref))

    def right(block, part, at, carry):
        rows = pl.ds(pl.multiple_of(block * size, size), size)
        weights, grads = part
        steep = (g_ref[rows, :] * slope_ref[rows, :].astype(jnp.float32)).astype(jnp.bfloat16)
        grads[at[0], 1, at[1]] = inner_dot(z_ref[rows, :], steep, 1, 1).astype(jnp.bfloat16)
        mid_ref[rows, :] = inner_dot(weights[at[0], 1, at[1]], steep, 1, 0)
        return carry

    over_blocks(table_ref, parts, right, 0)
    scale = scale_ref[0:1, :]

    def left(block, part, at, total):
        rows = pl.ds(pl.multiple_of(block * size, size), size)
        weights, grads = part
        slot = block % turned_ref.shape[0]
        for q in range(fold):
            turned_ref[slot, pl.ds(q, blocks, stride=fold), :] = mid_ref[
                pl.ds(q * blocks + block, blocks, stride=size), :
            ]
        arrived = turned_ref[slot].astype(jnp.bfloat16)
        grads[at[0], 0, at[1]] = inner_dot(u_ref[rows, :], arrived, 1, 1).astype(jnp.bfloat16)
        weighted = inner_dot(weights[at[0], 0, at[1]], arrived, 1, 0) * gain_ref[rows, :].astype(jnp.float32)
        e_ref[rows, :] = weighted
        return total + fold_rows(weighted * h_ref[rows, :].astype(jnp.float32))

    total = over_blocks(table_ref, parts, left, jnp.zeros((8, slots), jnp.float32))
    inner = jnp.sum(total, axis=0, keepdims=True)
    back = scale * scale * scale * inner / features

    def write(block, carry):
        rows = pl.ds(pl.multiple_of(block * size, size), size)
        part = h_ref[rows, :].astype(jnp.float32)
        out_ref[rows, :] = (g_ref[rows, :] + scale * e_ref[rows, :] - part * back).astype(out_ref.dtype)
        return carry

    lax.fori_loop(0, blocks, write, 0, unroll=4)


def shape_of(shape, dtype):
    return jax.ShapeDtypeStruct(shape, dtype)


def in_vmem(count):
    return [pl.BlockSpec(memory_space=pltpu.VMEM)] * count


def run_forward(table, h, weights, gain):
    features, slots = h.shape
    whole = (features, slots)
    flops = 4 * features * slots * weights[0].shape[-1]
    return pl.pallas_call(
        forward_kernel,
        in_specs=[pl.BlockSpec(memory_space=pltpu.SMEM)] + in_vmem(4),
        out_shape=(
            shape_of(whole, jnp.float32),
            shape_of(whole, jnp.bfloat16),
            shape_of(whole, jnp.bfloat16),
            shape_of(whole, jnp.bfloat16),
            shape_of((8, slots), jnp.float32),
        ),
        scratch_shapes=[pltpu.VMEM(whole, jnp.float32)],
        compiler_params=pltpu.CompilerParams(vmem_limit_bytes=VMEM_LIMIT),
        cost_estimate=pl.CostEstimate(
            flops=4 * flops, bytes_accessed=20 * features * slots, transcendentals=features * slots
        ),
        name="forward_layer",
    )(table, h, *weights, gain)


def run_turn(h, target, gain, size):
    return pl.pallas_call(
        lambda *refs: turn_kernel(size, *refs),
        out_shape=shape_of(h.shape, jnp.float32),
        compiler_params=pltpu.CompilerParams(vmem_limit_bytes=VMEM_LIMIT),
        cost_estimate=pl.CostEstimate(flops=20 * h.size, bytes_accessed=12 * h.size, transcendentals=0),
        name="turn",
    )(h, target, gain)


def run_backward(table, g, slope, z, u, h, scale, weights, gain, out_type):
    features, slots = h.shape
    size = weights[0].shape[-1]
    flops = 8 * features * slots * size
    return pl.pallas_call(
        backward_kernel,
        in_specs=[pl.BlockSpec(memory_space=pltpu.SMEM)] + in_vmem(9),
        out_shape=(
            shape_of(h.shape, out_type),
            shape_of(weights[0].shape, jnp.bfloat16),
            shape_of(weights[1].shape, jnp.bfloat16),
        ),
        scratch_shapes=[
            pltpu.VMEM(h.shape, jnp.float32),
            pltpu.VMEM((4, size, slots), jnp.float32),
            pltpu.VMEM(h.shape, jnp.float32),
        ],
        compiler_params=pltpu.CompilerParams(vmem_limit_bytes=VMEM_LIMIT),
        cost_estimate=pl.CostEstimate(
            flops=4 * flops, bytes_accessed=30 * features * slots, transcendentals=0
        ),
        name="backward_layer",
    )(table, g, slope, z, u, h, scale, *weights, gain)


def plane_routes(width, replicas):
    bits = width.bit_length() - 1
    orders = [[(step + d) % bits for step in range(bits)] for d in range(replicas)]

    def index(s, t, d):
        return (s * width + t) * replicas + d

    every = [(s, t, d) for s in range(width) for t in range(width) for d in range(replicas)]
    across = [
        [(index(s, t, d), index(s ^ (1 << orders[d][step]), t, d)) for s, t, d in every]
        for step in range(bits)
    ]
    cores = [(index(s, t, d), index(s, t, 1 - d)) for s, t, d in every]
    offsets = [
        [sum(((r >> step) & 1) << orders[d][step] for step in range(bits)) for r in range(width)]
        for d in range(replicas)
    ]
    return across, cores, offsets


def plane_shards(patches, teacher, critic_pairs, left_factors, right_factors, norm_gains):
    width = lax.axis_size("section")
    replicas = lax.axis_size("dp")
    tok_rows, feat_local = patches.shape
    layer_count, local_blocks, size = left_factors.shape[1:4]
    features = feat_local * width
    wide = 2 * tok_rows // 3
    chunk = local_blocks // (replicas * width)
    axes = ("section", "tensor", "dp")
    across, cores, offsets = plane_routes(width, replicas)
    section = lax.axis_index("section")
    core = lax.axis_index("dp")

    replica = jnp.stack([core, 1 - core])[:, None, None, None]
    owner = section ^ jnp.array(offsets, jnp.int32)[replica[:, 0, 0, 0]][:, :, None, None]
    quarter = jnp.arange(width, dtype=jnp.int32)[None, None, :, None]
    within = jnp.arange(chunk, dtype=jnp.int32)[None, None, None, :]
    table = quarter * local_blocks + (replica * width + owner) * chunk + within
    table = table.reshape(-1).astype(jnp.int32)

    held = jnp.stack([left_factors[0], right_factors[0]], axis=1)
    held = lax.dynamic_slice_in_dim(held, core * (width * chunk), width * chunk, axis=2)
    held = held.reshape(layer_count, 2, width, chunk, size, size).transpose(2, 0, 1, 3, 4, 5)
    layer_rows = 2 * chunk * size
    held = held.reshape(width, layer_count * layer_rows, size)
    gain_rows = norm_gains[0].reshape(1, -1, size)
    gain_rows = jnp.broadcast_to(gain_rows, (width,) + gain_rows.shape[1:])
    groups = [
        jnp.concatenate([held[:, :layer_rows], gain_rows], axis=1),
        held[:, layer_rows:],
    ]

    def to_plane(value):
        value = lax.all_to_all(value, "section", split_axis=0, concat_axis=0, tiled=True)
        return lax.all_to_all(value, "tensor", split_axis=0, concat_axis=0, tiled=True)

    critic_ids = jnp.arange(width, dtype=jnp.int32)
    named = (critic_pairs[:, 0:1] == critic_ids) | (critic_pairs[:, 1:2] == critic_ids)
    earlier = jnp.tril(jnp.ones((tok_rows, tok_rows), jnp.bfloat16), -1)
    rank = jnp.dot(earlier, named.astype(jnp.bfloat16), preferred_element_type=jnp.float32)
    rank = rank.astype(jnp.int32)
    places = jnp.arange(wide, dtype=jnp.int32)
    chosen = (named[:, :, None] & (rank[:, :, None] == places)).astype(jnp.bfloat16)

    def dispatch(values):
        sent = jnp.stack(
            [inner_dot(values, chosen[:, c], 0, 0).astype(jnp.bfloat16) for c in range(width)]
        )
        got = lax.all_to_all(sent, "tensor", split_axis=0, concat_axis=0, tiled=True)
        return got.reshape(features, wide)

    residual = dispatch(patches)
    first = to_plane(groups[0])
    rest = to_plane(groups[1])
    gains = first[:, layer_rows:].reshape(width, layer_count + 1, feat_local)
    gains = gains.transpose(1, 0, 2).reshape(layer_count + 1, features)
    gains = jnp.broadcast_to(gains[:, :, None], (layer_count + 1, features, wide))

    weights = []
    for layer in range(layer_count):
        if layer == 0:
            mine = first[:, :layer_rows]
        else:
            mine = rest[:, (layer - 1) * layer_rows : layer * layer_rows]
        for route in across:
            mine = jnp.concatenate([mine, lax.ppermute(mine, axes, route)], axis=0)
        other = lax.ppermute(mine, axes, cores)
        weights.append([part.reshape(-1, 2, chunk, size, size) for part in (mine, other)])
    target = dispatch(teacher)

    stored = []
    for layer in range(layer_count):
        following, u, z, slope, scale = run_forward(table, residual, weights[layer], gains[layer])
        stored.append((slope, z, u, residual, scale))
        residual = following
    gradient = run_turn(residual, target, gains[layer_count], size)

    def added(one, two):
        return (one.astype(jnp.float32) + two.astype(jnp.float32)).astype(jnp.bfloat16)

    summed = []
    for layer in range(layer_count - 1, -1, -1):
        out_type = jnp.float32 if layer > 0 else jnp.bfloat16
        gradient, mine, other = run_backward(
            table, gradient, *stored[layer], weights[layer], gains[layer], out_type
        )
        mine = added(mine, lax.ppermute(other, axes, cores))
        for route in across[::-1]:
            half = mine.shape[0] // 2
            mine = added(mine[:half], lax.ppermute(mine[half:], axes, route))
        summed.insert(0, mine.reshape(width, layer_rows, size))

    def to_home(value):
        value = lax.all_to_all(value, "tensor", split_axis=0, concat_axis=0, tiled=True)
        value = lax.all_to_all(value, "section", split_axis=0, concat_axis=0, tiled=True)
        return value, lax.ppermute(value, axes, cores)

    returned = gradient.reshape(width, feat_local, wide)
    returned = lax.all_to_all(returned, "tensor", split_axis=0, concat_axis=0, tiled=True)
    combined = sum(inner_dot(chosen[:, c], returned[c], 1, 1) for c in range(width))
    d_patches = (0.5 * combined).astype(jnp.bfloat16)

    grad_factor = 1.0 / math.sqrt(2 * tok_rows * width * replicas)
    late = to_home(jnp.concatenate(summed[1:], axis=1))
    early = to_home(summed[0])
    pair = [jnp.concatenate([one, two], axis=1) for one, two in zip(early, late)]
    pair = [
        value.reshape(width, layer_count, 2, chunk, size, size).transpose(2, 1, 0, 3, 4, 5)
        for value in pair
    ]
    pair = [value.reshape(2, layer_count, width * chunk, size, size) for value in pair]
    low = jnp.where(core == 0, pair[0], pair[1])
    high = jnp.where(core == 0, pair[1], pair[0])
    grads = jnp.concatenate([low, high], axis=2).astype(jnp.float32) * grad_factor
    return (d_patches, grads[0][None], grads[1][None])


def solution(mesh):
    in_specs = (
        P(("section", "dp"), "tensor"),
        P(("section", "dp"), "tensor"),
        P(("section", "dp"), None),
        P("section", None, "tensor", None, None),
        P("section", None, "tensor", None, None),
        P("section", None, "tensor"),
    )
    out_specs = (
        P(("section", "dp"), "tensor"),
        P("section", None, "tensor", None, None),
        P("section", None, "tensor", None, None),
    )
    body = plane_shards if planes_fit(mesh) else layered_shards
    return jax.shard_map(
        body, mesh=mesh, in_specs=in_specs, out_specs=out_specs, check_vma=False)
```

```python
import math

import jax
import jax.numpy as jnp
from jax import lax
from jax.experimental import pallas as pl
from jax.experimental.pallas import tpu as pltpu
from jax.sharding import PartitionSpec as P

EPSILON = 1e-06
TANH_SLOPE = 0.7978845608028654
CUBIC_TERM = 0.044715


def shifted(value, axis, steps):
    count = lax.axis_size(axis)
    first, last = (max(0, -steps), min(count, count - steps))
    return lax.ppermute(value, axis, [(source, source + steps) for source in range(first, last)])


def gelu_value(values):
    tangent = jnp.tanh(TANH_SLOPE * (values + CUBIC_TERM * values * values * values))
    return 0.5 * values * (1.0 + tangent)


def gelu_slope(values):
    tangent = jnp.tanh(TANH_SLOPE * (values + CUBIC_TERM * values * values * values))
    return 0.5 * (1.0 + tangent) + 0.5 * values * (1.0 - tangent * tangent) * TANH_SLOPE * (
        1.0 + 3.0 * CUBIC_TERM * values * values
    )


def norm_pair(residuals, gain_pair, model_width):
    squares = lax.psum(
        (
            jnp.sum(residuals[0] * residuals[0], axis=(1, 2)),
            jnp.sum(residuals[1] * residuals[1], axis=(1, 2)),
        ),
        "tensor",
    )
    factors = [lax.rsqrt(squares[member] / model_width + EPSILON) for member in range(2)]
    normed = [
        residuals[member] * factors[member][:, None, None] * gain_pair[member][None]
        for member in range(2)
    ]
    return (factors, normed)


def norm_back_pair(residuals, factors, gain_pair, grad_normed, carried, model_width):
    weighted = [grad_normed[member] * gain_pair[member][None] for member in range(2)]
    inners = lax.psum(
        (
            jnp.sum(weighted[0] * residuals[0], axis=(1, 2)),
            jnp.sum(weighted[1] * residuals[1], axis=(1, 2)),
        ),
        "tensor",
    )
    return [
        carried[member]
        + factors[member][:, None, None] * weighted[member]
        - residuals[member] * (factors[member] ** 3 * inners[member] / model_width)[:, None, None]
        for member in range(2)
    ]


def layered_shards(patches, teacher, critic_pairs, left_factors, right_factors, norm_gains):
    sections = lax.axis_size("section")
    tensor_width = lax.axis_size("tensor")
    replicas = lax.axis_size("dp")
    tok_rows = patches.shape[0]
    feat_local = patches.shape[1]
    layer_count = left_factors.shape[1]
    local_blocks = left_factors.shape[2]
    block_size = left_factors.shape[3]
    all_blocks = local_blocks * tensor_width
    fold_ratio = block_size // all_blocks
    model_width = feat_local * tensor_width
    sixth_rows = tok_rows // 6
    leading = 2 * sixth_rows
    critic_ids = jnp.arange(4, dtype=jnp.int32)
    named_by = (
        (critic_pairs[:, 0:1] == critic_ids[None, :])
        | (critic_pairs[:, 1:2] == critic_ids[None, :])
    ).astype(jnp.int32)
    ranking = jnp.cumsum(named_by, axis=0) - 1
    wide_ids = critic_ids[None, :] < 2
    slot_width = 3 * sixth_rows
    spilled = wide_ids & (ranking >= 3 * sixth_rows)
    destination = jnp.where(spilled, critic_ids[None, :] + 2, critic_ids[None, :])
    slot_index = jnp.where(spilled, ranking - sixth_rows, ranking)
    flat_slot = destination * slot_width + slot_index
    chosen = jnp.take_along_axis(flat_slot, critic_pairs, axis=1)
    slot_total = sections * slot_width
    row_ids = jnp.broadcast_to(jnp.arange(tok_rows, dtype=jnp.int32)[:, None], chosen.shape)
    source_row = (
        jnp.full((slot_total,), tok_rows, jnp.int32).at[chosen.reshape(-1)].set(row_ids.reshape(-1))
    )
    send_patch = (
        patches.at[source_row]
        .get(mode="fill", fill_value=0)
        .reshape(sections, slot_width, local_blocks, block_size)
    )
    send_target = (
        teacher.at[source_row]
        .get(mode="fill", fill_value=0)
        .reshape(sections, slot_width, local_blocks, block_size)
    )
    recv_patch, recv_target = (
        lax.all_to_all(send_patch, "section", split_axis=0, concat_axis=0, tiled=True),
        lax.all_to_all(send_target, "section", split_axis=0, concat_axis=0, tiled=True),
    )
    residuals = [
        recv_patch[:, :leading].reshape(-1, local_blocks, block_size).astype(jnp.float32),
        recv_patch[:, leading:].reshape(-1, local_blocks, block_size).astype(jnp.float32),
    ]
    targets = [
        recv_target[:, :leading].reshape(-1, local_blocks, block_size).astype(jnp.float32),
        recv_target[:, leading:].reshape(-1, local_blocks, block_size).astype(jnp.float32),
    ]
    native = (left_factors[0], right_factors[0], norm_gains[0])
    borrowed = shifted((left_factors, right_factors, norm_gains), "section", 2)
    is_wide = lax.axis_index("section") < 2
    second = (
        jnp.where(is_wide, left_factors, borrowed[0])[0],
        jnp.where(is_wide, right_factors, borrowed[1])[0],
        jnp.where(is_wide, norm_gains, borrowed[2])[0],
    )
    left_sets = (native[0], second[0])
    right_sets = (native[1], second[1])
    gain_sets = (
        native[2].astype(jnp.float32).reshape(layer_count + 1, local_blocks, block_size),
        second[2].astype(jnp.float32).reshape(layer_count + 1, local_blocks, block_size),
    )
    stored = []
    for layer_index in range(layer_count):
        gain_pair = [gain_sets[0][layer_index], gain_sets[1][layer_index]]
        factors, normed = norm_pair(residuals, gain_pair, model_width)
        normed = [normed[member].astype(jnp.bfloat16) for member in range(2)]
        first_out = [
            jnp.einsum(
                "nki,kij->nkj",
                normed[member],
                left_sets[member][layer_index],
                preferred_element_type=jnp.float32,
            ).astype(jnp.bfloat16)
            for member in range(2)
        ]
        permuted = (
            lax.all_to_all(first_out[0], "tensor", split_axis=2, concat_axis=1, tiled=True),
            lax.all_to_all(first_out[1], "tensor", split_axis=2, concat_axis=1, tiled=True),
        )
        permuted = [
            permuted[member].reshape(
                permuted[member].shape[0], all_blocks, local_blocks, fold_ratio
            )
            for member in range(2)
        ]
        right_quads = [
            right_sets[member][layer_index].reshape(
                local_blocks, fold_ratio, all_blocks, block_size
            )
            for member in range(2)
        ]
        mixture = [
            jnp.einsum(
                "nkmp,mpkl->nml",
                permuted[member],
                right_quads[member],
                preferred_element_type=jnp.float32,
            )
            for member in range(2)
        ]
        stored.append((residuals, factors, normed, permuted, mixture, right_quads, gain_pair))
        residuals = [residuals[member] + gelu_value(mixture[member]) for member in range(2)]
    final_gains = [gain_sets[0][layer_count], gain_sets[1][layer_count]]
    factors, outputs = norm_pair(residuals, final_gains, model_width)
    gradients = norm_back_pair(
        residuals,
        factors,
        final_gains,
        [outputs[member] - targets[member] for member in range(2)],
        [jnp.zeros_like(residuals[member]) for member in range(2)],
        model_width,
    )
    left_terms = []
    right_terms = []
    for layer_index in range(layer_count - 1, -1, -1):
        inputs, factors, normed, permuted, mixture, right_quads, gain_pair = stored[layer_index]
        slopes = [
            (gradients[member] * gelu_slope(mixture[member])).astype(jnp.bfloat16)
            for member in range(2)
        ]
        right_grad = [
            jnp.einsum(
                "nkmp,nml->mpkl",
                permuted[member],
                slopes[member],
                preferred_element_type=jnp.float32,
            ).reshape(local_blocks, block_size, block_size)
            for member in range(2)
        ]
        back_moved = [
            jnp.einsum(
                "nml,mpkl->nkmp",
                slopes[member],
                right_quads[member],
                preferred_element_type=jnp.float32,
            )
            .astype(jnp.bfloat16)
            .reshape(slopes[member].shape[0], all_blocks, local_blocks * fold_ratio)
            for member in range(2)
        ]
        arrived = (
            lax.all_to_all(back_moved[0], "tensor", split_axis=1, concat_axis=2, tiled=True),
            lax.all_to_all(back_moved[1], "tensor", split_axis=1, concat_axis=2, tiled=True),
        )
        left_grad = [
            jnp.einsum(
                "nki,nkj->kij", normed[member], arrived[member], preferred_element_type=jnp.float32
            )
            for member in range(2)
        ]
        grad_normed = [
            jnp.einsum(
                "nkj,kij->nki",
                arrived[member],
                left_sets[member][layer_index],
                preferred_element_type=jnp.float32,
            )
            for member in range(2)
        ]
        gradients = norm_back_pair(inputs, factors, gain_pair, grad_normed, gradients, model_width)
        layer_left = jnp.stack(left_grad)
        layer_right = jnp.stack(right_grad)
        layer_left, layer_right = (
            lax.psum(layer_left.astype(jnp.bfloat16), "dp").astype(jnp.float32),
            lax.psum(layer_right.astype(jnp.bfloat16), "dp").astype(jnp.float32),
        )
        left_terms.insert(0, layer_left)
        right_terms.insert(0, layer_right)
    left_stack = jnp.stack(left_terms)
    right_stack = jnp.stack(right_terms)
    repaid = (
        shifted(left_stack[:, 1].astype(jnp.bfloat16), "section", -2).astype(jnp.float32),
        shifted(right_stack[:, 1].astype(jnp.bfloat16), "section", -2).astype(jnp.float32),
    )
    is_wide = lax.axis_index("section") < 2
    left_total = left_stack[:, 0] + jnp.where(is_wide, left_stack[:, 1] + repaid[0], 0.0)
    right_total = right_stack[:, 0] + jnp.where(is_wide, right_stack[:, 1] + repaid[1], 0.0)
    grad_factor = 1.0 / math.sqrt(2 * tok_rows * sections * replicas)
    returned = [
        gradients[member].astype(jnp.bfloat16).reshape(sections, -1, local_blocks, block_size)
        for member in range(2)
    ]
    back_lead, back_trail = (
        lax.all_to_all(returned[0], "section", split_axis=0, concat_axis=0, tiled=True),
        lax.all_to_all(returned[1], "section", split_axis=0, concat_axis=0, tiled=True),
    )
    gathered = jnp.concatenate((back_lead, back_trail), axis=1).reshape(
        slot_total, local_blocks, block_size
    )
    combined = (
        gathered[chosen[:, 0]].astype(jnp.float32) + gathered[chosen[:, 1]].astype(jnp.float32)
    ) * 0.5
    d_patches = combined.astype(jnp.bfloat16).reshape(tok_rows, feat_local)
    return (d_patches, (left_total * grad_factor)[None], (right_total * grad_factor)[None])


VMEM_LIMIT = 60 * 1024 * 1024
CHUNKS = 8
AXES = ("section", "tensor", "dp")


def planes_fit(mesh):
    sections = mesh.shape["section"]
    paired = mesh.shape["dp"] == 2 and sections & (sections - 1) == 0
    return paired and mesh.shape["tensor"] == sections


def inner_dot(left, right, left_dim, right_dim):
    return lax.dot_general(
        left,
        right,
        (((left_dim,), (right_dim,)), ((), ())),
        preferred_element_type=jnp.float32,
    )


def fold_rows(values):
    return jnp.sum(values.reshape(values.shape[0] // 8, 8, values.shape[1]), axis=0)


def block_rows(block, size):
    return pl.ds(pl.multiple_of(block * size, size), size)


def column(gain_ref, block, slots):
    blocks = gain_ref.shape[1]
    picked = lax.broadcasted_iota(jnp.int32, (blocks, slots), 0) == block
    return inner_dot(gain_ref[...], picked.astype(jnp.bfloat16), 1, 0)


def chunk_copy(source, target, sems, chunk):
    rows = target.shape[0] // CHUNKS
    at = pl.ds(pl.multiple_of(chunk * rows, rows), rows)
    return pltpu.make_async_copy(source.at[at], target.at[at], sems.at[chunk])


def start_chunks(source, target, sems):
    for chunk in range(CHUNKS):
        chunk_copy(source, target, sems, chunk).start()


def wait_chunks(source, target, sems):
    for chunk in range(CHUNKS):
        chunk_copy(source, target, sems, chunk).wait()


def quarter_copies(pieces, whole, sems, me, outward=False):
    rows = pieces[0].shape[0]
    copies = []
    for k, piece in enumerate(pieces):
        part = whole.at[pl.ds(pl.multiple_of((me ^ k) * rows, rows), rows)]
        ends = (part, piece) if outward else (piece, part)
        copies.append(pltpu.make_async_copy(*ends, sems.at[k]))
    return copies


def factor_copies(own, peer, held, sems, side, outward=False):
    half = own.shape[0]
    copies = []
    for part, ref in enumerate((own, peer)):
        inside = held.at[pl.ds(part * half, half), side]
        ends = (inside, ref.at[:, side]) if outward else (ref.at[:, side], inside)
        copies.append(pltpu.make_async_copy(*ends, sems.at[2 * side + part]))
    return copies


def by_chunk(blocks, step, carry, before=None, after=None):
    per_chunk = blocks // CHUNKS

    def one(chunk, carry):
        if before is not None:
            before(chunk)
        carry = lax.fori_loop(
            0, per_chunk, lambda at, now: step(chunk * per_chunk + at, now), carry, unroll=True
        )
        if after is not None:
            after(chunk)
        return carry

    return lax.fori_loop(0, CHUNKS, one, carry)


def forward_kernel(first, inputs, table_ref, gain_ref, sums_ref, *refs):
    sources, refs = refs[:inputs], refs[inputs:]
    own, peer = sources[-2:]
    out_ref, u_ref, z_ref, slope_ref, scale_ref, next_ref = refs[:6]
    raw, h, w, u, z, slope, mid, in_sems, w_sems, out_sems = refs[6:]
    features, slots = h.shape
    size = w.shape[-1]
    chunk_blocks = w.shape[2]
    blocks = features // size
    fold = size // blocks

    left_in = factor_copies(own, peer, w, w_sems, 0)
    right_in = factor_copies(own, peer, w, w_sems, 1)
    if first:
        pieces = quarter_copies(sources[:-2], raw, in_sems, table_ref[blocks])
        for copy in pieces + left_in + right_in:
            copy.start()
        for copy in pieces:
            copy.wait()

        def squares(block, total):
            rows = block_rows(block, size)
            part = raw[rows, :].astype(jnp.float32)
            h[rows, :] = part
            return total + fold_rows(part * part)

        total = by_chunk(blocks, squares, jnp.zeros((8, slots), jnp.float32))
    else:
        for copy in left_in:
            copy.start()
        start_chunks(sources[0], h, in_sems)
        for copy in right_in:
            copy.start()
        total = sums_ref[...]
    scale = lax.rsqrt(jnp.sum(total, axis=0, keepdims=True) / features + EPSILON)
    scale_ref[...] = jnp.broadcast_to(scale, scale_ref.shape)
    for copy in left_in:
        copy.wait()

    def arrive(chunk):
        if not first:
            chunk_copy(sources[0], h, in_sems, chunk).wait()

    def left(block, carry):
        rows = block_rows(block, size)
        place = table_ref[block]
        normed = (h[rows, :] * scale * column(gain_ref, block, slots)).astype(jnp.bfloat16)
        u[rows, :] = normed
        weight = w[place // chunk_blocks, 0, place % chunk_blocks]
        mid[rows, :] = inner_dot(weight, normed, 0, 0)
        return carry

    def leave_left(chunk):
        chunk_copy(u, u_ref, out_sems.at[0], chunk).start()

    by_chunk(blocks, left, 0, arrive, leave_left)
    for copy in right_in:
        copy.wait()

    def right(block, total):
        rows = block_rows(block, size)
        place = table_ref[block]
        moved = [mid[pl.ds(block * fold + q, blocks, stride=size), :] for q in range(fold)]
        moved = jnp.concatenate(moved, axis=0).astype(jnp.bfloat16)
        z[rows, :] = moved
        weight = w[place // chunk_blocks, 1, place % chunk_blocks]
        mixture = inner_dot(weight, moved, 0, 0)
        squared = mixture * mixture
        tangent = jnp.tanh(mixture * (TANH_SLOPE + (TANH_SLOPE * CUBIC_TERM) * squared))
        half = 0.5 + 0.5 * tangent
        following = h[rows, :] + mixture * half
        h[rows, :] = following
        steep = half + mixture * (1.0 - tangent * tangent) * (
            0.5 * TANH_SLOPE + (1.5 * TANH_SLOPE * CUBIC_TERM) * squared
        )
        slope[rows, :] = steep.astype(jnp.bfloat16)
        return total + fold_rows(following * following)

    leaving = ((h, out_ref, 1), (z, z_ref, 2), (slope, slope_ref, 3))

    def leave_right(chunk):
        for source, target, at in leaving:
            chunk_copy(source, target, out_sems.at[at], chunk).start()

    next_ref[...] = by_chunk(blocks, right, jnp.zeros((8, slots), jnp.float32), None, leave_right)
    for source, target, at in ((u, u_ref, 0),) + leaving:
        wait_chunks(source, target, out_sems.at[at])


def backward_kernel(turning, last, inputs, table_ref, gain_ref, end_gain_ref, scale_ref, *refs):
    sources, refs = refs[:inputs], refs[inputs:]
    slope_ref, z_ref, u_ref, own, peer = sources[:5]
    sources = sources[5:]
    count = 4 if last else 1
    outs, refs = refs[:count], refs[count:]
    own_grad, peer_grad = refs[:2]
    g, slope, z, u, h, w, gw, mid, turned, top, goal = refs[2:13]
    in_sems, w_sems, out_sems, gw_sems = refs[13:]
    features, slots = g.shape
    size = w.shape[-1]
    chunk_blocks = w.shape[2]
    blocks = features // size
    fold = size // blocks
    me = table_ref[blocks]

    left_in = factor_copies(own, peer, w, w_sems, 0)
    right_in = factor_copies(own, peer, w, w_sems, 1)
    if turning:
        h_ref, top_ref = sources[:2]
        goals = quarter_copies(sources[2:], goal, in_sems.at[5], me)
        start_chunks(top_ref, top, in_sems.at[0])
        for copy in goals:
            copy.start()
    elif last:
        starts = quarter_copies(sources[1:], h, in_sems.at[5], me)
        start_chunks(sources[0], g, in_sems.at[0])
    else:
        h_ref, g_ref = sources
        start_chunks(g_ref, g, in_sems.at[0])
    for copy in right_in:
        copy.start()
    start_chunks(slope_ref, slope, in_sems.at[1])
    start_chunks(z_ref, z, in_sems.at[2])
    for copy in left_in:
        copy.start()
    start_chunks(u_ref, u, in_sems.at[3])
    if last:
        for copy in starts:
            copy.start()
    else:
        start_chunks(h_ref, h, in_sems.at[4])

    if turning:
        zero = jnp.zeros((8, slots), jnp.float32)

        def sums(block, totals):
            rows = block_rows(block, size)
            part = top[rows, :]
            scaled = part * column(end_gain_ref, block, slots)
            return (
                totals[0] + fold_rows(part * part),
                totals[1] + fold_rows(scaled * scaled),
                totals[2] + fold_rows(scaled * goal[rows, :].astype(jnp.float32)),
            )

        for copy in goals:
            copy.wait()
        totals = by_chunk(
            blocks, sums, (zero, zero, zero), lambda chunk: chunk_copy(top_ref, top, in_sems.at[0], chunk).wait()
        )
        squares, gained, crossed = [jnp.sum(total, axis=0, keepdims=True) for total in totals]
        end_scale = lax.rsqrt(squares / features + EPSILON)
        end_back = end_scale * end_scale * end_scale * (end_scale * gained - crossed) / features

    for copy in right_in:
        copy.wait()

    def arrive_right(chunk):
        if not turning:
            chunk_copy(sources[0] if last else g_ref, g, in_sems.at[0], chunk).wait()
        chunk_copy(slope_ref, slope, in_sems.at[1], chunk).wait()
        chunk_copy(z_ref, z, in_sems.at[2], chunk).wait()

    def right(block, carry):
        rows = block_rows(block, size)
        place = table_ref[block]
        at = (place // chunk_blocks, 1, place % chunk_blocks)
        if turning:
            part = top[rows, :]
            gain = column(end_gain_ref, block, slots)
            error = (part * end_scale * gain - goal[rows, :].astype(jnp.float32)) * gain
            gradient = end_scale * error - part * end_back
            g[rows, :] = gradient
        else:
            gradient = g[rows, :]
        steep = (gradient * slope[rows, :].astype(jnp.float32)).astype(jnp.bfloat16)
        gw[at] = inner_dot(z[rows, :], steep, 1, 1).astype(jnp.bfloat16)
        mid[rows, :] = inner_dot(w[at], steep, 1, 0)
        return carry

    by_chunk(blocks, right, 0, arrive_right)
    right_out = factor_copies(own_grad, peer_grad, gw, gw_sems, 1, outward=True)
    for copy in right_out:
        copy.start()
    for copy in left_in:
        copy.wait()
    scale = scale_ref[0:1, :]
    if last:
        for copy in starts:
            copy.wait()

    def arrive_left(chunk):
        chunk_copy(u_ref, u, in_sems.at[3], chunk).wait()
        if not last:
            chunk_copy(h_ref, h, in_sems.at[4], chunk).wait()

    def left(block, total):
        rows = block_rows(block, size)
        place = table_ref[block]
        at = (place // chunk_blocks, 0, place % chunk_blocks)
        slot = block % turned.shape[0]
        for q in range(fold):
            turned[slot, pl.ds(q, blocks, stride=fold), :] = mid[
                pl.ds(q * blocks + block, blocks, stride=size), :
            ]
        arrived = turned[slot].astype(jnp.bfloat16)
        gw[at] = inner_dot(u[rows, :], arrived, 1, 1).astype(jnp.bfloat16)
        weighted = inner_dot(w[at], arrived, 1, 0) * column(gain_ref, block, slots)
        g[rows, :] = g[rows, :] + scale * weighted
        return total + fold_rows(weighted * h[rows, :].astype(jnp.float32))

    total = by_chunk(blocks, left, jnp.zeros((8, slots), jnp.float32), arrive_left)
    left_out = factor_copies(own_grad, peer_grad, gw, gw_sems, 0, outward=True)
    for copy in left_out:
        copy.start()
    back = scale * scale * scale * jnp.sum(total, axis=0, keepdims=True) / features

    def finish(block, carry):
        rows = block_rows(block, size)
        ended = g[rows, :] - h[rows, :].astype(jnp.float32) * back
        if last:
            u[rows, :] = ended.astype(jnp.bfloat16)
        else:
            g[rows, :] = ended
        return carry

    if last:
        by_chunk(blocks, finish, 0)
        ends = quarter_copies(outs, u, out_sems, me, outward=True)
        for copy in ends:
            copy.start()
        for copy in ends:
            copy.wait()
    else:
        by_chunk(blocks, finish, 0, None, lambda chunk: chunk_copy(g, outs[0], out_sems, chunk).start())
        wait_chunks(g, outs[0], out_sems)
    for copy in right_out + left_out:
        copy.wait()


def shape_of(shape, dtype):
    return jax.ShapeDtypeStruct(shape, dtype)


SMEM = pl.BlockSpec(memory_space=pltpu.SMEM)
INSIDE = pl.BlockSpec(memory_space=pltpu.VMEM)
OUTSIDE = pl.BlockSpec(memory_space=pl.ANY)


def run_forward(table, gain, sums, held, weights, whole, after=()):
    first = len(held) > 1
    sources = (*held, *weights)
    half = weights[0].shape
    out_shape = (
        shape_of(whole, jnp.float32),
        shape_of(whole, jnp.bfloat16),
        shape_of(whole, jnp.bfloat16),
        shape_of(whole, jnp.bfloat16),
        shape_of((8, whole[1]), jnp.float32),
        shape_of((8, whole[1]), jnp.float32),
    )

    def kernel(table_ref, gain_ref, sums_ref, *refs):
        extra = len(sources) + len(after)
        used = refs[: len(sources)] + refs[extra:]
        forward_kernel(first, len(sources), table_ref, gain_ref, sums_ref, *used)

    return pl.pallas_call(
        kernel,
        in_specs=[SMEM, INSIDE, INSIDE] + [OUTSIDE] * (len(sources) + len(after)),
        out_specs=[OUTSIDE] * 4 + [INSIDE] * 2,
        out_shape=out_shape,
        scratch_shapes=[
            pltpu.VMEM(whole if first else (16, 128), jnp.bfloat16),
            pltpu.VMEM(whole, jnp.float32),
            pltpu.VMEM((2 * half[0],) + half[1:], jnp.bfloat16),
            pltpu.VMEM(whole, jnp.bfloat16),
            pltpu.VMEM(whole, jnp.bfloat16),
            pltpu.VMEM(whole, jnp.bfloat16),
            pltpu.VMEM(whole, jnp.float32),
            pltpu.SemaphoreType.DMA((CHUNKS,)),
            pltpu.SemaphoreType.DMA((4,)),
            pltpu.SemaphoreType.DMA((4, CHUNKS)),
        ],
        compiler_params=pltpu.CompilerParams(vmem_limit_bytes=VMEM_LIMIT),
        cost_estimate=pl.CostEstimate(
            flops=FORWARD_COST, bytes_accessed=20 * whole[0] * whole[1], transcendentals=0
        ),
        name="forward_layer",
    )(table, gain, sums, *sources, *after)


def run_backward(table, gain, end_gain, scale, kept, weights, sources, turning, last, after=()):
    whole = kept[0].shape
    sources = (*kept, *weights, *sources)
    half = weights[0].shape
    width = 4
    ends = [shape_of((whole[0] // width, whole[1]), jnp.bfloat16)] * width if last else [
        shape_of(whole, jnp.float32)
    ]

    def kernel(table_ref, gain_ref, end_gain_ref, scale_ref, *refs):
        extra = len(sources) + len(after)
        used = refs[: len(sources)] + refs[extra:]
        backward_kernel(
            turning, last, len(sources), table_ref, gain_ref, end_gain_ref, scale_ref, *used
        )

    small = (16, 128)
    return pl.pallas_call(
        kernel,
        in_specs=[SMEM] + [INSIDE] * 3 + [OUTSIDE] * (len(sources) + len(after)),
        out_specs=[OUTSIDE] * (len(ends) + 2),
        out_shape=ends + [shape_of(half, jnp.bfloat16)] * 2,
        scratch_shapes=[
            pltpu.VMEM(whole, jnp.float32),
            pltpu.VMEM(whole, jnp.bfloat16),
            pltpu.VMEM(whole, jnp.bfloat16),
            pltpu.VMEM(whole, jnp.bfloat16),
            pltpu.VMEM(whole, jnp.bfloat16 if last else jnp.float32),
            pltpu.VMEM((2 * half[0],) + half[1:], jnp.bfloat16),
            pltpu.VMEM((2 * half[0],) + half[1:], jnp.bfloat16),
            pltpu.VMEM(whole, jnp.float32),
            pltpu.VMEM((8, half[-1], whole[1]), jnp.float32),
            pltpu.VMEM(whole if turning else small, jnp.float32),
            pltpu.VMEM(whole if turning else small, jnp.bfloat16),
            pltpu.SemaphoreType.DMA((6, CHUNKS)),
            pltpu.SemaphoreType.DMA((4,)),
            pltpu.SemaphoreType.DMA((CHUNKS,)),
            pltpu.SemaphoreType.DMA((4,)),
        ],
        compiler_params=pltpu.CompilerParams(vmem_limit_bytes=VMEM_LIMIT),
        cost_estimate=pl.CostEstimate(
            flops=BACKWARD_COST, bytes_accessed=30 * whole[0] * whole[1], transcendentals=0
        ),
        name="backward_layer",
    )(table, gain, end_gain, scale, *sources, *after)


FORWARD_COST = 15_000_000_000
BACKWARD_COST = 18_000_000_000


def plane_routes(width, replicas):
    bits = width.bit_length() - 1
    orders = [[(step + d) % bits for step in range(bits)] for d in range(replicas)]
    every = [(s, t, d) for s in range(width) for t in range(width) for d in range(replicas)]

    def route(move):
        def index(s, t, d):
            return (s * width + t) * replicas + d

        return [(index(*place), index(*move(*place))) for place in every]

    across = [route(lambda s, t, d, at=at: (s ^ (1 << orders[d][at]), t, d)) for at in range(bits)]
    cores = route(lambda s, t, d: (s, t, 1 - d))
    sections = [route(lambda s, t, d, k=k: (s ^ k, t, d)) for k in range(width)]
    planes = [route(lambda s, t, d, k=k: (s, t ^ k, d)) for k in range(width)]
    homes = [route(lambda s, t, d, k=k: (t, s ^ k, d)) for k in range(width)]
    ranks = [[0] * width for d in range(replicas)]
    for d in range(replicas):
        for r in range(width):
            ranks[d][sum(((r >> at) & 1) << orders[d][at] for at in range(bits))] = r
    return across, cores, sections, planes, homes, ranks


def plane_shards(patches, teacher, critic_pairs, left_factors, right_factors, norm_gains):
    width = lax.axis_size("section")
    replicas = lax.axis_size("dp")
    tok_rows, feat_local = patches.shape
    layer_count, local_blocks, size = left_factors.shape[1:4]
    features = feat_local * width
    blocks = features // size
    wide = 2 * tok_rows // 3
    whole = (features, wide)
    chunk = local_blocks // (replicas * width)
    across, cores, sections, planes, homes, ranks = plane_routes(width, replicas)
    section = lax.axis_index("section")
    tensor = lax.axis_index("tensor")
    core = lax.axis_index("dp")

    layer_rows = 2 * chunk * size

    def piece_for(distance):
        start = (core * width + (section ^ distance)) * chunk
        parts = [
            lax.dynamic_slice_in_dim(factors[0], start, chunk, axis=1)
            for factors in (left_factors, right_factors)
        ]
        return jnp.stack(parts, axis=1).reshape(layer_count, layer_rows, size)

    pieces = [piece_for(distance) for distance in range(width)]
    gain_rows = norm_gains[0].reshape(-1, size)
    groups = [(0,), (1,), tuple(range(2, layer_count))]
    weights = []
    arrived_gains = None
    for group in groups:
        sent = [piece[group[0] : group[-1] + 1].reshape(-1, size) for piece in pieces]
        if group[0] == 0:
            sent = [jnp.concatenate([value, gain_rows], axis=0) for value in sent]
        sent = [sent[0]] + [
            lax.ppermute(sent[distance], AXES, sections[distance]) for distance in range(1, width)
        ]
        spread = jnp.stack(sent)
        sent = [
            lax.dynamic_index_in_dim(spread, section ^ tensor ^ distance, 0, keepdims=False)
            for distance in range(width)
        ]
        sent = [sent[0]] + [
            lax.ppermute(sent[distance], AXES, planes[distance]) for distance in range(1, width)
        ]
        if group[0] == 0:
            arrived_gains = jnp.stack([value[layer_rows:] for value in sent])
        for at in range(len(group)):
            rows = slice(at * layer_rows, (at + 1) * layer_rows)
            mine = jnp.stack([value[rows] for value in sent])
            for route in across:
                mine = jnp.concatenate([mine, lax.ppermute(mine, AXES, route)], axis=0)
            other = lax.ppermute(mine, AXES, cores)
            weights.append([part.reshape(-1, 2, chunk, size, size) for part in (mine, other)])
    gains = arrived_gains[jnp.arange(width) ^ tensor]
    gains = gains.reshape(width, layer_count + 1, local_blocks, size).transpose(1, 3, 0, 2)
    gains = gains.reshape(layer_count + 1, size, blocks)

    block = jnp.arange(blocks, dtype=jnp.int32)
    rest = block % local_blocks
    replica = rest // (width * chunk)
    rank = jnp.array(ranks, jnp.int32)[replica, section ^ ((rest // chunk) % width)]
    part = (replica != core).astype(jnp.int32)
    table = ((part * width + rank) * width + (tensor ^ (block // local_blocks))) * chunk + rest % chunk
    table = jnp.concatenate([table, tensor[None]]).astype(jnp.int32)

    critic_ids = jnp.arange(width, dtype=jnp.int32) ^ tensor
    named = (critic_pairs[:, 0:1] == critic_ids) | (critic_pairs[:, 1:2] == critic_ids)
    earlier = jnp.tril(jnp.ones((tok_rows, tok_rows), jnp.bfloat16), -1)
    rank = jnp.dot(earlier, named.astype(jnp.bfloat16), preferred_element_type=jnp.float32)
    rank = rank.astype(jnp.int32)
    places = jnp.arange(wide, dtype=jnp.int32)
    chosen = [
        (named[:, k : k + 1] & (rank[:, k : k + 1] == places)).astype(jnp.bfloat16) for k in range(width)
    ]

    def dispatch(values):
        sent = [inner_dot(values, chosen[k], 0, 0).astype(jnp.bfloat16) for k in range(width)]
        return [sent[0]] + [lax.ppermute(sent[k], AXES, planes[k]) for k in range(1, width)]

    start = dispatch(patches)
    target = dispatch(teacher)

    stored = []
    residual = start
    sums = jnp.zeros((8, wide), jnp.float32)
    for layer in range(layer_count):
        following, u, z, slope, scale, sums = run_forward(
            table, gains[layer], sums, residual, weights[layer], whole
        )
        stored.append(((slope, z, u), scale, residual))
        residual = (following,)

    def added(one, two):
        return (one.astype(jnp.float32) + two.astype(jnp.float32)).astype(jnp.bfloat16)

    summed = []
    gradient = None
    for layer in range(layer_count - 1, -1, -1):
        turning = layer == layer_count - 1
        last = layer == 0
        kept, scale, inputs = stored[layer]
        if turning:
            sources = (*inputs, *residual, *target)
        elif last:
            sources = (gradient, *inputs)
        else:
            sources = (*inputs, gradient)
        *gradient, mine, other = run_backward(
            table, gains[layer], gains[layer_count], scale, kept, weights[layer], sources, turning, last
        )
        gradient = gradient if last else gradient[0]
        mine = added(mine, lax.ppermute(other, AXES, cores))
        for route in across[::-1]:
            half = mine.shape[0] // 2
            mine = added(mine[:half], lax.ppermute(mine[half:], AXES, route))
        summed.insert(0, mine.reshape(width, layer_rows, size))

    def to_home(value):
        sent = [
            lax.dynamic_index_in_dim(value, section ^ tensor ^ k, 0, keepdims=False) for k in range(width)
        ]
        came = jnp.stack([lax.ppermute(sent[k], AXES, homes[k]) for k in range(width)])
        return came, lax.ppermute(came, AXES, cores)

    returned = [gradient[0]] + [lax.ppermute(gradient[k], AXES, planes[k]) for k in range(1, width)]
    combined = sum(inner_dot(chosen[k], returned[k], 1, 1) for k in range(width))
    d_patches = (0.5 * combined).astype(jnp.bfloat16)

    grad_factor = 1.0 / math.sqrt(2 * tok_rows * width * replicas)
    late = to_home(jnp.concatenate(summed[1:], axis=1))
    early = to_home(summed[0])
    pair = [jnp.concatenate([one, two], axis=1) for one, two in zip(early, late)]
    order = jnp.arange(width) ^ tensor
    pair = [
        value[order].reshape(width, layer_count, 2, chunk, size, size).transpose(2, 1, 0, 3, 4, 5)
        for value in pair
    ]
    pair = [value.reshape(2, layer_count, width * chunk, size, size) for value in pair]
    low = jnp.where(core == 0, pair[0], pair[1])
    high = jnp.where(core == 0, pair[1], pair[0])
    grads = jnp.concatenate([low, high], axis=2).astype(jnp.float32) * grad_factor
    return (d_patches, grads[0][None], grads[1][None])


def solution(mesh):
    in_specs = (
        P(("section", "dp"), "tensor"),
        P(("section", "dp"), "tensor"),
        P(("section", "dp"), None),
        P("section", None, "tensor", None, None),
        P("section", None, "tensor", None, None),
        P("section", None, "tensor"),
    )
    out_specs = (
        P(("section", "dp"), "tensor"),
        P("section", None, "tensor", None, None),
        P("section", None, "tensor", None, None),
    )
    body = plane_shards if planes_fit(mesh) else layered_shards
    return jax.shard_map(
        body, mesh=mesh, in_specs=in_specs, out_specs=out_specs, check_vma=False)
```

```python
import math

import jax
import jax.numpy as jnp
from jax import lax
from jax.experimental import pallas as pl
from jax.experimental.pallas import tpu as pltpu
from jax.sharding import PartitionSpec as P

EPSILON = 1e-06
TANH_SLOPE = 0.7978845608028654
CUBIC_TERM = 0.044715


def shifted(value, axis, steps):
    count = lax.axis_size(axis)
    first, last = (max(0, -steps), min(count, count - steps))
    return lax.ppermute(value, axis, [(source, source + steps) for source in range(first, last)])


def gelu_value(values):
    tangent = jnp.tanh(TANH_SLOPE * (values + CUBIC_TERM * values * values * values))
    return 0.5 * values * (1.0 + tangent)


def gelu_slope(values):
    tangent = jnp.tanh(TANH_SLOPE * (values + CUBIC_TERM * values * values * values))
    return 0.5 * (1.0 + tangent) + 0.5 * values * (1.0 - tangent * tangent) * TANH_SLOPE * (
        1.0 + 3.0 * CUBIC_TERM * values * values
    )


def norm_pair(residuals, gain_pair, model_width):
    squares = lax.psum(
        (
            jnp.sum(residuals[0] * residuals[0], axis=(1, 2)),
            jnp.sum(residuals[1] * residuals[1], axis=(1, 2)),
        ),
        "tensor",
    )
    factors = [lax.rsqrt(squares[member] / model_width + EPSILON) for member in range(2)]
    normed = [
        residuals[member] * factors[member][:, None, None] * gain_pair[member][None]
        for member in range(2)
    ]
    return (factors, normed)


def norm_back_pair(residuals, factors, gain_pair, grad_normed, carried, model_width):
    weighted = [grad_normed[member] * gain_pair[member][None] for member in range(2)]
    inners = lax.psum(
        (
            jnp.sum(weighted[0] * residuals[0], axis=(1, 2)),
            jnp.sum(weighted[1] * residuals[1], axis=(1, 2)),
        ),
        "tensor",
    )
    return [
        carried[member]
        + factors[member][:, None, None] * weighted[member]
        - residuals[member] * (factors[member] ** 3 * inners[member] / model_width)[:, None, None]
        for member in range(2)
    ]


def layered_shards(patches, teacher, critic_pairs, left_factors, right_factors, norm_gains):
    sections = lax.axis_size("section")
    tensor_width = lax.axis_size("tensor")
    replicas = lax.axis_size("dp")
    tok_rows = patches.shape[0]
    feat_local = patches.shape[1]
    layer_count = left_factors.shape[1]
    local_blocks = left_factors.shape[2]
    block_size = left_factors.shape[3]
    all_blocks = local_blocks * tensor_width
    fold_ratio = block_size // all_blocks
    model_width = feat_local * tensor_width
    sixth_rows = tok_rows // 6
    leading = 2 * sixth_rows
    critic_ids = jnp.arange(4, dtype=jnp.int32)
    named_by = (
        (critic_pairs[:, 0:1] == critic_ids[None, :])
        | (critic_pairs[:, 1:2] == critic_ids[None, :])
    ).astype(jnp.int32)
    ranking = jnp.cumsum(named_by, axis=0) - 1
    wide_ids = critic_ids[None, :] < 2
    slot_width = 3 * sixth_rows
    spilled = wide_ids & (ranking >= 3 * sixth_rows)
    destination = jnp.where(spilled, critic_ids[None, :] + 2, critic_ids[None, :])
    slot_index = jnp.where(spilled, ranking - sixth_rows, ranking)
    flat_slot = destination * slot_width + slot_index
    chosen = jnp.take_along_axis(flat_slot, critic_pairs, axis=1)
    slot_total = sections * slot_width
    row_ids = jnp.broadcast_to(jnp.arange(tok_rows, dtype=jnp.int32)[:, None], chosen.shape)
    source_row = (
        jnp.full((slot_total,), tok_rows, jnp.int32).at[chosen.reshape(-1)].set(row_ids.reshape(-1))
    )
    send_patch = (
        patches.at[source_row]
        .get(mode="fill", fill_value=0)
        .reshape(sections, slot_width, local_blocks, block_size)
    )
    send_target = (
        teacher.at[source_row]
        .get(mode="fill", fill_value=0)
        .reshape(sections, slot_width, local_blocks, block_size)
    )
    recv_patch, recv_target = (
        lax.all_to_all(send_patch, "section", split_axis=0, concat_axis=0, tiled=True),
        lax.all_to_all(send_target, "section", split_axis=0, concat_axis=0, tiled=True),
    )
    residuals = [
        recv_patch[:, :leading].reshape(-1, local_blocks, block_size).astype(jnp.float32),
        recv_patch[:, leading:].reshape(-1, local_blocks, block_size).astype(jnp.float32),
    ]
    targets = [
        recv_target[:, :leading].reshape(-1, local_blocks, block_size).astype(jnp.float32),
        recv_target[:, leading:].reshape(-1, local_blocks, block_size).astype(jnp.float32),
    ]
    native = (left_factors[0], right_factors[0], norm_gains[0])
    borrowed = shifted((left_factors, right_factors, norm_gains), "section", 2)
    is_wide = lax.axis_index("section") < 2
    second = (
        jnp.where(is_wide, left_factors, borrowed[0])[0],
        jnp.where(is_wide, right_factors, borrowed[1])[0],
        jnp.where(is_wide, norm_gains, borrowed[2])[0],
    )
    left_sets = (native[0], second[0])
    right_sets = (native[1], second[1])
    gain_sets = (
        native[2].astype(jnp.float32).reshape(layer_count + 1, local_blocks, block_size),
        second[2].astype(jnp.float32).reshape(layer_count + 1, local_blocks, block_size),
    )
    stored = []
    for layer_index in range(layer_count):
        gain_pair = [gain_sets[0][layer_index], gain_sets[1][layer_index]]
        factors, normed = norm_pair(residuals, gain_pair, model_width)
        normed = [normed[member].astype(jnp.bfloat16) for member in range(2)]
        first_out = [
            jnp.einsum(
                "nki,kij->nkj",
                normed[member],
                left_sets[member][layer_index],
                preferred_element_type=jnp.float32,
            ).astype(jnp.bfloat16)
            for member in range(2)
        ]
        permuted = (
            lax.all_to_all(first_out[0], "tensor", split_axis=2, concat_axis=1, tiled=True),
            lax.all_to_all(first_out[1], "tensor", split_axis=2, concat_axis=1, tiled=True),
        )
        permuted = [
            permuted[member].reshape(
                permuted[member].shape[0], all_blocks, local_blocks, fold_ratio
            )
            for member in range(2)
        ]
        right_quads = [
            right_sets[member][layer_index].reshape(
                local_blocks, fold_ratio, all_blocks, block_size
            )
            for member in range(2)
        ]
        mixture = [
            jnp.einsum(
                "nkmp,mpkl->nml",
                permuted[member],
                right_quads[member],
                preferred_element_type=jnp.float32,
            )
            for member in range(2)
        ]
        stored.append((residuals, factors, normed, permuted, mixture, right_quads, gain_pair))
        residuals = [residuals[member] + gelu_value(mixture[member]) for member in range(2)]
    final_gains = [gain_sets[0][layer_count], gain_sets[1][layer_count]]
    factors, outputs = norm_pair(residuals, final_gains, model_width)
    gradients = norm_back_pair(
        residuals,
        factors,
        final_gains,
        [outputs[member] - targets[member] for member in range(2)],
        [jnp.zeros_like(residuals[member]) for member in range(2)],
        model_width,
    )
    left_terms = []
    right_terms = []
    for layer_index in range(layer_count - 1, -1, -1):
        inputs, factors, normed, permuted, mixture, right_quads, gain_pair = stored[layer_index]
        slopes = [
            (gradients[member] * gelu_slope(mixture[member])).astype(jnp.bfloat16)
            for member in range(2)
        ]
        right_grad = [
            jnp.einsum(
                "nkmp,nml->mpkl",
                permuted[member],
                slopes[member],
                preferred_element_type=jnp.float32,
            ).reshape(local_blocks, block_size, block_size)
            for member in range(2)
        ]
        back_moved = [
            jnp.einsum(
                "nml,mpkl->nkmp",
                slopes[member],
                right_quads[member],
                preferred_element_type=jnp.float32,
            )
            .astype(jnp.bfloat16)
            .reshape(slopes[member].shape[0], all_blocks, local_blocks * fold_ratio)
            for member in range(2)
        ]
        arrived = (
            lax.all_to_all(back_moved[0], "tensor", split_axis=1, concat_axis=2, tiled=True),
            lax.all_to_all(back_moved[1], "tensor", split_axis=1, concat_axis=2, tiled=True),
        )
        left_grad = [
            jnp.einsum(
                "nki,nkj->kij", normed[member], arrived[member], preferred_element_type=jnp.float32
            )
            for member in range(2)
        ]
        grad_normed = [
            jnp.einsum(
                "nkj,kij->nki",
                arrived[member],
                left_sets[member][layer_index],
                preferred_element_type=jnp.float32,
            )
            for member in range(2)
        ]
        gradients = norm_back_pair(inputs, factors, gain_pair, grad_normed, gradients, model_width)
        layer_left = jnp.stack(left_grad)
        layer_right = jnp.stack(right_grad)
        layer_left, layer_right = (
            lax.psum(layer_left.astype(jnp.bfloat16), "dp").astype(jnp.float32),
            lax.psum(layer_right.astype(jnp.bfloat16), "dp").astype(jnp.float32),
        )
        left_terms.insert(0, layer_left)
        right_terms.insert(0, layer_right)
    left_stack = jnp.stack(left_terms)
    right_stack = jnp.stack(right_terms)
    repaid = (
        shifted(left_stack[:, 1].astype(jnp.bfloat16), "section", -2).astype(jnp.float32),
        shifted(right_stack[:, 1].astype(jnp.bfloat16), "section", -2).astype(jnp.float32),
    )
    is_wide = lax.axis_index("section") < 2
    left_total = left_stack[:, 0] + jnp.where(is_wide, left_stack[:, 1] + repaid[0], 0.0)
    right_total = right_stack[:, 0] + jnp.where(is_wide, right_stack[:, 1] + repaid[1], 0.0)
    grad_factor = 1.0 / math.sqrt(2 * tok_rows * sections * replicas)
    returned = [
        gradients[member].astype(jnp.bfloat16).reshape(sections, -1, local_blocks, block_size)
        for member in range(2)
    ]
    back_lead, back_trail = (
        lax.all_to_all(returned[0], "section", split_axis=0, concat_axis=0, tiled=True),
        lax.all_to_all(returned[1], "section", split_axis=0, concat_axis=0, tiled=True),
    )
    gathered = jnp.concatenate((back_lead, back_trail), axis=1).reshape(
        slot_total, local_blocks, block_size
    )
    combined = (
        gathered[chosen[:, 0]].astype(jnp.float32) + gathered[chosen[:, 1]].astype(jnp.float32)
    ) * 0.5
    d_patches = combined.astype(jnp.bfloat16).reshape(tok_rows, feat_local)
    return (d_patches, (left_total * grad_factor)[None], (right_total * grad_factor)[None])


VMEM_LIMIT = 60 * 1024 * 1024
CHUNKS = 8
AXES = ("section", "tensor", "dp")


def planes_fit(mesh):
    sections = mesh.shape["section"]
    paired = mesh.shape["dp"] == 2 and sections & (sections - 1) == 0
    return paired and mesh.shape["tensor"] == sections


def inner_dot(left, right, left_dim, right_dim):
    return lax.dot_general(
        left,
        right,
        (((left_dim,), (right_dim,)), ((), ())),
        preferred_element_type=jnp.float32,
    )


def fold_rows(values):
    return jnp.sum(values.reshape(values.shape[0] // 8, 8, values.shape[1]), axis=0)


def block_rows(block, size):
    return pl.ds(pl.multiple_of(block * size, size), size)


def column(gain_ref, block, slots):
    blocks = gain_ref.shape[1]
    picked = lax.broadcasted_iota(jnp.int32, (blocks, slots), 0) == block
    return inner_dot(gain_ref[...], picked.astype(jnp.bfloat16), 1, 0)


def chunk_copy(source, target, sems, chunk):
    rows = target.shape[0] // CHUNKS
    at = pl.ds(pl.multiple_of(chunk * rows, rows), rows)
    return pltpu.make_async_copy(source.at[at], target.at[at], sems.at[chunk])


def start_chunks(source, target, sems):
    for chunk in range(CHUNKS):
        chunk_copy(source, target, sems, chunk).start()


def wait_chunks(source, target, sems):
    for chunk in range(CHUNKS):
        chunk_copy(source, target, sems, chunk).wait()


def factor_copies(own, peer, held, sems, side, outward=False):
    half = own.shape[0]
    copies = []
    for part, ref in enumerate((own, peer)):
        inside = held.at[pl.ds(part * half, half), side]
        ends = (inside, ref.at[:, side]) if outward else (ref.at[:, side], inside)
        copies.append(pltpu.make_async_copy(*ends, sems.at[2 * side + part]))
    return copies


def by_chunk(blocks, step, carry, before=None, after=None):
    per_chunk = blocks // CHUNKS

    def one(chunk, carry):
        if before is not None:
            before(chunk)
        carry = lax.fori_loop(
            0, per_chunk, lambda at, now: step(chunk * per_chunk + at, now), carry, unroll=True
        )
        if after is not None:
            after(chunk)
        return carry

    return lax.fori_loop(0, CHUNKS, one, carry)


def forward_kernel(first, inputs, table_ref, gain_ref, sums_ref, *refs):
    sources, refs = refs[:inputs], refs[inputs:]
    own, peer = sources[-2:]
    out_ref, u_ref, z_ref, slope_ref, scale_ref, next_ref = refs[:6]
    raw, h, w, u, z, slope, mid, in_sems, w_sems, out_sems = refs[6:]
    features, slots = h.shape
    size = w.shape[-1]
    chunk_blocks = w.shape[2]
    blocks = features // size
    fold = size // blocks

    left_in = factor_copies(own, peer, w, w_sems, 0)
    right_in = factor_copies(own, peer, w, w_sems, 1)
    if first:
        start_chunks(sources[0], raw, in_sems)
        for copy in left_in + right_in:
            copy.start()

        def squares(block, total):
            rows = block_rows(block, size)
            part = raw[rows, :].astype(jnp.float32)
            h[rows, :] = part
            return total + fold_rows(part * part)

        total = by_chunk(
            blocks,
            squares,
            jnp.zeros((8, slots), jnp.float32),
            lambda chunk: chunk_copy(sources[0], raw, in_sems, chunk).wait(),
        )
    else:
        for copy in left_in:
            copy.start()
        start_chunks(sources[0], h, in_sems)
        for copy in right_in:
            copy.start()
        total = sums_ref[...]
    scale = lax.rsqrt(jnp.sum(total, axis=0, keepdims=True) / features + EPSILON)
    scale_ref[...] = jnp.broadcast_to(scale, scale_ref.shape)
    for copy in left_in:
        copy.wait()

    def arrive(chunk):
        if not first:
            chunk_copy(sources[0], h, in_sems, chunk).wait()

    def left(block, carry):
        rows = block_rows(block, size)
        place = table_ref[block]
        normed = (h[rows, :] * scale * column(gain_ref, block, slots)).astype(jnp.bfloat16)
        u[rows, :] = normed
        weight = w[place // chunk_blocks, 0, place % chunk_blocks]
        mid[rows, :] = inner_dot(weight, normed, 0, 0)
        return carry

    def leave_left(chunk):
        chunk_copy(u, u_ref, out_sems.at[0], chunk).start()

    by_chunk(blocks, left, 0, arrive, leave_left)
    for copy in right_in:
        copy.wait()

    def right(block, total):
        rows = block_rows(block, size)
        place = table_ref[block]
        moved = [mid[pl.ds(block * fold + q, blocks, stride=size), :] for q in range(fold)]
        moved = jnp.concatenate(moved, axis=0).astype(jnp.bfloat16)
        z[rows, :] = moved
        weight = w[place // chunk_blocks, 1, place % chunk_blocks]
        mixture = inner_dot(weight, moved, 0, 0)
        squared = mixture * mixture
        tangent = jnp.tanh(mixture * (TANH_SLOPE + (TANH_SLOPE * CUBIC_TERM) * squared))
        half = 0.5 + 0.5 * tangent
        following = h[rows, :] + mixture * half
        h[rows, :] = following
        steep = half + mixture * (1.0 - tangent * tangent) * (
            0.5 * TANH_SLOPE + (1.5 * TANH_SLOPE * CUBIC_TERM) * squared
        )
        slope[rows, :] = steep.astype(jnp.bfloat16)
        return total + fold_rows(following * following)

    leaving = ((h, out_ref, 1), (z, z_ref, 2), (slope, slope_ref, 3))

    def leave_right(chunk):
        for source, target, at in leaving:
            chunk_copy(source, target, out_sems.at[at], chunk).start()

    next_ref[...] = by_chunk(blocks, right, jnp.zeros((8, slots), jnp.float32), None, leave_right)
    for source, target, at in ((u, u_ref, 0),) + leaving:
        wait_chunks(source, target, out_sems.at[at])


def backward_kernel(turning, last, inputs, table_ref, gain_ref, end_gain_ref, scale_ref, *refs):
    sources, refs = refs[:inputs], refs[inputs:]
    slope_ref, z_ref, u_ref, own, peer = sources[:5]
    sources = sources[5:]
    out_ref, own_grad, peer_grad = refs[:3]
    g, slope, z, u, h, w, gw, mid, turned, top, goal = refs[3:14]
    in_sems, w_sems, out_sems, gw_sems = refs[14:]
    features, slots = g.shape
    size = w.shape[-1]
    chunk_blocks = w.shape[2]
    blocks = features // size
    fold = size // blocks

    left_in = factor_copies(own, peer, w, w_sems, 0)
    right_in = factor_copies(own, peer, w, w_sems, 1)
    h_ref, g_ref = sources[:2]
    if turning:
        goal_ref = sources[2]
        start_chunks(g_ref, top, in_sems.at[0])
        start_chunks(goal_ref, goal, in_sems.at[5])
    else:
        start_chunks(g_ref, g, in_sems.at[0])
    for copy in right_in:
        copy.start()
    start_chunks(slope_ref, slope, in_sems.at[1])
    start_chunks(z_ref, z, in_sems.at[2])
    for copy in left_in:
        copy.start()
    start_chunks(u_ref, u, in_sems.at[3])
    start_chunks(h_ref, h, in_sems.at[4])

    if turning:
        zero = jnp.zeros((8, slots), jnp.float32)

        def sums(block, totals):
            rows = block_rows(block, size)
            part = top[rows, :]
            scaled = part * column(end_gain_ref, block, slots)
            return (
                totals[0] + fold_rows(part * part),
                totals[1] + fold_rows(scaled * scaled),
                totals[2] + fold_rows(scaled * goal[rows, :].astype(jnp.float32)),
            )

        def arrive_top(chunk):
            chunk_copy(g_ref, top, in_sems.at[0], chunk).wait()
            chunk_copy(goal_ref, goal, in_sems.at[5], chunk).wait()

        totals = by_chunk(blocks, sums, (zero, zero, zero), arrive_top)
        squares, gained, crossed = [jnp.sum(total, axis=0, keepdims=True) for total in totals]
        end_scale = lax.rsqrt(squares / features + EPSILON)
        end_back = end_scale * end_scale * end_scale * (end_scale * gained - crossed) / features

    for copy in right_in:
        copy.wait()

    def arrive_right(chunk):
        if not turning:
            chunk_copy(g_ref, g, in_sems.at[0], chunk).wait()
        chunk_copy(slope_ref, slope, in_sems.at[1], chunk).wait()
        chunk_copy(z_ref, z, in_sems.at[2], chunk).wait()

    def right(block, carry):
        rows = block_rows(block, size)
        place = table_ref[block]
        at = (place // chunk_blocks, 1, place % chunk_blocks)
        if turning:
            part = top[rows, :]
            gain = column(end_gain_ref, block, slots)
            error = (part * end_scale * gain - goal[rows, :].astype(jnp.float32)) * gain
            gradient = end_scale * error - part * end_back
            g[rows, :] = gradient
        else:
            gradient = g[rows, :]
        steep = (gradient * slope[rows, :].astype(jnp.float32)).astype(jnp.bfloat16)
        gw[at] = inner_dot(z[rows, :], steep, 1, 1).astype(jnp.bfloat16)
        mid[rows, :] = inner_dot(w[at], steep, 1, 0)
        return carry

    by_chunk(blocks, right, 0, arrive_right)
    right_out = factor_copies(own_grad, peer_grad, gw, gw_sems, 1, outward=True)
    for copy in right_out:
        copy.start()
    for copy in left_in:
        copy.wait()
    scale = scale_ref[0:1, :]

    def arrive_left(chunk):
        chunk_copy(u_ref, u, in_sems.at[3], chunk).wait()
        chunk_copy(h_ref, h, in_sems.at[4], chunk).wait()

    def left(block, total):
        rows = block_rows(block, size)
        place = table_ref[block]
        at = (place // chunk_blocks, 0, place % chunk_blocks)
        slot = block % turned.shape[0]
        for q in range(fold):
            turned[slot, pl.ds(q, blocks, stride=fold), :] = mid[
                pl.ds(q * blocks + block, blocks, stride=size), :
            ]
        arrived = turned[slot].astype(jnp.bfloat16)
        gw[at] = inner_dot(u[rows, :], arrived, 1, 1).astype(jnp.bfloat16)
        weighted = inner_dot(w[at], arrived, 1, 0) * column(gain_ref, block, slots)
        g[rows, :] = g[rows, :] + scale * weighted
        return total + fold_rows(weighted * h[rows, :].astype(jnp.float32))

    total = by_chunk(blocks, left, jnp.zeros((8, slots), jnp.float32), arrive_left)
    left_out = factor_copies(own_grad, peer_grad, gw, gw_sems, 0, outward=True)
    for copy in left_out:
        copy.start()
    back = scale * scale * scale * jnp.sum(total, axis=0, keepdims=True) / features

    def finish(block, carry):
        rows = block_rows(block, size)
        ended = g[rows, :] - h[rows, :].astype(jnp.float32) * back
        if last:
            u[rows, :] = ended.astype(jnp.bfloat16)
        else:
            g[rows, :] = ended
        return carry

    ended = u if last else g
    by_chunk(blocks, finish, 0, None, lambda chunk: chunk_copy(ended, out_ref, out_sems, chunk).start())
    wait_chunks(ended, out_ref, out_sems)
    for copy in right_out + left_out:
        copy.wait()


def shape_of(shape, dtype):
    return jax.ShapeDtypeStruct(shape, dtype)


SMEM = pl.BlockSpec(memory_space=pltpu.SMEM)
INSIDE = pl.BlockSpec(memory_space=pltpu.VMEM)
OUTSIDE = pl.BlockSpec(memory_space=pl.ANY)


def run_forward(table, gain, sums, residual, weights, after=()):
    whole = residual.shape
    first = residual.dtype == jnp.bfloat16
    sources = (residual, *weights)
    half = weights[0].shape
    out_shape = (
        shape_of(whole, jnp.float32),
        shape_of(whole, jnp.bfloat16),
        shape_of(whole, jnp.bfloat16),
        shape_of(whole, jnp.bfloat16),
        shape_of((8, whole[1]), jnp.float32),
        shape_of((8, whole[1]), jnp.float32),
    )

    def kernel(table_ref, gain_ref, sums_ref, *refs):
        extra = len(sources) + len(after)
        used = refs[: len(sources)] + refs[extra:]
        forward_kernel(first, len(sources), table_ref, gain_ref, sums_ref, *used)

    return pl.pallas_call(
        kernel,
        in_specs=[SMEM, INSIDE, INSIDE] + [OUTSIDE] * (len(sources) + len(after)),
        out_specs=[OUTSIDE] * 4 + [INSIDE] * 2,
        out_shape=out_shape,
        scratch_shapes=[
            pltpu.VMEM(whole if first else (16, 128), jnp.bfloat16),
            pltpu.VMEM(whole, jnp.float32),
            pltpu.VMEM((2 * half[0],) + half[1:], jnp.bfloat16),
            pltpu.VMEM(whole, jnp.bfloat16),
            pltpu.VMEM(whole, jnp.bfloat16),
            pltpu.VMEM(whole, jnp.bfloat16),
            pltpu.VMEM(whole, jnp.float32),
            pltpu.SemaphoreType.DMA((CHUNKS,)),
            pltpu.SemaphoreType.DMA((4,)),
            pltpu.SemaphoreType.DMA((4, CHUNKS)),
        ],
        compiler_params=pltpu.CompilerParams(vmem_limit_bytes=VMEM_LIMIT),
        cost_estimate=pl.CostEstimate(
            flops=FORWARD_COST, bytes_accessed=20 * whole[0] * whole[1], transcendentals=0
        ),
        name="forward_layer",
    )(table, gain, sums, *sources, *after)


def run_backward(table, gain, end_gain, scale, kept, weights, sources, turning, last, after=()):
    whole = kept[0].shape
    sources = (*kept, *weights, *sources)
    half = weights[0].shape
    ended = shape_of(whole, jnp.bfloat16 if last else jnp.float32)

    def kernel(table_ref, gain_ref, end_gain_ref, scale_ref, *refs):
        extra = len(sources) + len(after)
        used = refs[: len(sources)] + refs[extra:]
        backward_kernel(
            turning, last, len(sources), table_ref, gain_ref, end_gain_ref, scale_ref, *used
        )

    small = (16, 128)
    return pl.pallas_call(
        kernel,
        in_specs=[SMEM] + [INSIDE] * 3 + [OUTSIDE] * (len(sources) + len(after)),
        out_specs=[OUTSIDE] * 3,
        out_shape=[ended] + [shape_of(half, jnp.bfloat16)] * 2,
        scratch_shapes=[
            pltpu.VMEM(whole, jnp.float32),
            pltpu.VMEM(whole, jnp.bfloat16),
            pltpu.VMEM(whole, jnp.bfloat16),
            pltpu.VMEM(whole, jnp.bfloat16),
            pltpu.VMEM(whole, jnp.bfloat16 if last else jnp.float32),
            pltpu.VMEM((2 * half[0],) + half[1:], jnp.bfloat16),
            pltpu.VMEM((2 * half[0],) + half[1:], jnp.bfloat16),
            pltpu.VMEM(whole, jnp.float32),
            pltpu.VMEM((8, half[-1], whole[1]), jnp.float32),
            pltpu.VMEM(whole if turning else small, jnp.float32),
            pltpu.VMEM(whole if turning else small, jnp.bfloat16),
            pltpu.SemaphoreType.DMA((6, CHUNKS)),
            pltpu.SemaphoreType.DMA((4,)),
            pltpu.SemaphoreType.DMA((CHUNKS,)),
            pltpu.SemaphoreType.DMA((4,)),
        ],
        compiler_params=pltpu.CompilerParams(vmem_limit_bytes=VMEM_LIMIT),
        cost_estimate=pl.CostEstimate(
            flops=BACKWARD_COST, bytes_accessed=30 * whole[0] * whole[1], transcendentals=0
        ),
        name="backward_layer",
    )(table, gain, end_gain, scale, *sources, *after)


FORWARD_COST = 15_000_000_000
BACKWARD_COST = 18_000_000_000


def assemble_kernel(layer_count, factor, place_ref, *refs):
    sources, (left_ref, right_ref) = refs[: 2 * layer_count], refs[2 * layer_count : 2 * layer_count + 2]
    held, wide, in_sems, out_sems = refs[2 * layer_count + 2 :]
    width, chunk = held.shape[1], held.shape[3]
    core, tensor = place_ref[0], place_ref[1]
    arrivals = [
        pltpu.make_async_copy(source, held.at[at], in_sems.at[at]) for at, source in enumerate(sources)
    ]
    for copy in arrivals:
        copy.start()
    leaving = []
    for at in range(2 * layer_count):
        arrivals[at].wait()
        layer, side = at // 2, at % 2
        half = core if side == 0 else 1 - core
        wide[at] = held[at].astype(jnp.float32) * factor
        for k in range(width):
            start = (half * width + (tensor ^ k)) * chunk
            for which, target in enumerate((left_ref, right_ref)):
                copy = pltpu.make_async_copy(
                    wide.at[at, k, which],
                    target.at[layer, pl.ds(start, chunk)],
                    out_sems.at[(at * width + k) * 2 + which],
                )
                copy.start()
                leaving.append(copy)
    for copy in leaving:
        copy.wait()


def run_assemble(places, pieces, layer_count, factor):
    piece = pieces[0].shape
    blocks = 2 * piece[0] * piece[2]
    out = shape_of((layer_count, blocks) + piece[3:], jnp.float32)
    return pl.pallas_call(
        lambda *refs: assemble_kernel(layer_count, factor, *refs),
        in_specs=[SMEM] + [OUTSIDE] * len(pieces),
        out_specs=[OUTSIDE] * 2,
        out_shape=[out] * 2,
        scratch_shapes=[
            pltpu.VMEM((2 * layer_count,) + piece, jnp.bfloat16),
            pltpu.VMEM((2 * layer_count,) + piece, jnp.float32),
            pltpu.SemaphoreType.DMA((2 * layer_count,)),
            pltpu.SemaphoreType.DMA((4 * layer_count * piece[0],)),
        ],
        compiler_params=pltpu.CompilerParams(vmem_limit_bytes=VMEM_LIMIT),
        cost_estimate=pl.CostEstimate(
            flops=0, bytes_accessed=12 * layer_count * math.prod(piece), transcendentals=0
        ),
        name="assemble",
    )(places, *pieces)


def plane_routes(width, replicas):
    every = [(s, t, d) for s in range(width) for t in range(width) for d in range(replicas)]

    def route(move):
        def index(s, t, d):
            return (s * width + t) * replicas + d

        return [(index(*place), index(*move(*place))) for place in every]

    cores = route(lambda s, t, d: (s, t, 1 - d))
    sections = [route(lambda s, t, d, k=k: (s ^ k, t, d)) for k in range(width)]
    planes = [route(lambda s, t, d, k=k: (s, t ^ k, d)) for k in range(width)]
    homes = [route(lambda s, t, d, k=k: (t, s ^ k, d)) for k in range(width)]
    return cores, sections, planes, homes


def added(*parts):
    return sum(part.astype(jnp.float32) for part in parts).astype(jnp.bfloat16)


def plane_shards(patches, teacher, critic_pairs, left_factors, right_factors, norm_gains):
    width = lax.axis_size("section")
    replicas = lax.axis_size("dp")
    tok_rows, feat_local = patches.shape
    layer_count, local_blocks, size = left_factors.shape[1:4]
    features = feat_local * width
    blocks = features // size
    wide = 2 * tok_rows // 3
    chunk = local_blocks // (replicas * width)
    layer_rows = 2 * chunk * size
    cores, sections, planes, homes = plane_routes(width, replicas)
    section = lax.axis_index("section")
    tensor = lax.axis_index("tensor")
    core = lax.axis_index("dp")
    away = range(1, width)
    tie = lax.optimization_barrier

    def send(values, routes):
        return [values[0]] + [lax.ppermute(values[k], AXES, routes[k]) for k in away]

    def crossed(values):
        spread = jnp.stack(values)
        return [
            lax.dynamic_index_in_dim(spread, section ^ tensor ^ k, 0, keepdims=False) for k in range(width)
        ]

    critic_ids = jnp.arange(width, dtype=jnp.int32) ^ tensor
    named = (critic_pairs[:, 0:1] == critic_ids) | (critic_pairs[:, 1:2] == critic_ids)
    earlier = jnp.tril(jnp.ones((tok_rows, tok_rows), jnp.bfloat16), -1)
    rank = jnp.dot(earlier, named.astype(jnp.bfloat16), preferred_element_type=jnp.float32)
    rank = rank.astype(jnp.int32)
    places = jnp.arange(wide, dtype=jnp.int32)
    chosen = [
        (named[:, k : k + 1] & (rank[:, k : k + 1] == places)).astype(jnp.bfloat16) for k in range(width)
    ]

    def picked(values):
        return [inner_dot(values, chosen[k], 0, 0).astype(jnp.bfloat16) for k in range(width)]

    def in_order(values):
        spread = jnp.stack(values)
        return spread[jnp.arange(width) ^ tensor].reshape((features,) + spread.shape[2:])

    def piece_for(distance):
        start = (core * width + (section ^ distance)) * chunk
        parts = [
            lax.dynamic_slice_in_dim(factors[0], start, chunk, axis=1)
            for factors in (left_factors, right_factors)
        ]
        return jnp.stack(parts, axis=1).reshape(layer_count, layer_rows, size)

    pieces = [piece_for(distance) for distance in range(width)]
    gain_rows = norm_gains[0].reshape(-1, size)
    front = [jnp.concatenate([piece[0], gain_rows], axis=0) for piece in pieces]
    rest = [piece[1:] for piece in pieces]
    patch_sent = picked(patches)
    front = send(front, sections)
    patch_came = send(patch_sent, planes)
    front, rest = tie((front, rest))
    rest = send(rest, sections)
    front = send(crossed(front), planes)
    gains = jnp.stack([value[layer_rows:] for value in front])[jnp.arange(width) ^ tensor]
    gains = gains.reshape(width, layer_count + 1, local_blocks, size).transpose(1, 3, 0, 2)
    gains = gains.reshape(layer_count + 1, size, blocks)
    arrived = [jnp.stack([value[:layer_rows] for value in front])]
    for layer in range(1, layer_count):
        arrived.append([value[layer - 1] for value in rest])

    def to_plane(values, after):
        values, _ = tie((crossed(values), after))
        return send(values, planes)

    def over_plane(mine):
        return send([mine] * width, sections)

    def both_cores(parts):
        mine = jnp.concatenate(parts, axis=0)
        return mine, lax.ppermute(mine, AXES, cores)

    def as_weights(parts):
        return [part.reshape(-1, 2, chunk, size, size) for part in parts]

    spread = [over_plane(arrived[0])]
    arrived[1] = jnp.stack(to_plane(arrived[1], front))
    spread.append(over_plane(arrived[1]))
    arrived[2] = to_plane(arrived[2], arrived[1])
    weights = [as_weights(both_cores(spread[0]))]

    block = jnp.arange(blocks, dtype=jnp.int32)
    inside = block % local_blocks
    part = (inside // (width * chunk) != core).astype(jnp.int32)
    rank_of = section ^ ((inside // chunk) % width)
    table = ((part * width + rank_of) * width + (tensor ^ (block // local_blocks))) * chunk + inside % chunk
    table = table.astype(jnp.int32)

    residual = in_order(patch_came)
    sums = jnp.zeros((8, wide), jnp.float32)
    target_sent = picked(teacher)
    (residual, spread[1], arrived[2], target_sent) = tie((residual, spread[1], arrived[2], target_sent))
    arrived[2] = jnp.stack(arrived[2])
    stored = []
    for layer in range(layer_count):
        flying = []
        if layer + 1 < layer_count:
            flying.append(both_cores(spread[layer + 1]))
        if layer + 2 < layer_count:
            flying.append(over_plane(arrived[layer + 2]))
        if layer + 3 < layer_count:
            flying.append(to_plane(arrived[layer + 3], arrived[layer + 2]))
        following, u, z, slope, scale, sums = run_forward(
            table, gains[layer], sums, residual, weights[layer]
        )
        stored.append(((slope, z, u), scale, residual))
        residual, flying = tie((following, flying))
        if layer + 1 < layer_count:
            weights.append(as_weights(flying[0]))
        if layer + 2 < layer_count:
            spread.append(flying[1])
        if layer + 3 < layer_count:
            arrived[layer + 3] = jnp.stack(flying[2])
        if layer == 0:
            target_sent, sums = tie((target_sent, sums))
            target = in_order(send(target_sent, planes))

    def core_sum(mine, other):
        return (mine, lax.ppermute(other, AXES, cores))

    def plane_sum(value):
        value = value.reshape(width, width, layer_rows, size)
        return send([value[k] for k in range(width)], sections)

    def homeward(value):
        sent = crossed([value[k] for k in range(width)])
        return [lax.ppermute(sent[k], AXES, homes[k]) for k in range(width)]

    steps = (
        lambda state: core_sum(*state),
        lambda state: plane_sum(added(*state)),
        lambda state: homeward(added(*state)),
        lambda state: (jnp.stack(state), lax.ppermute(jnp.stack(state), AXES, cores)),
    )
    gradient = residual
    underway = []
    for layer in range(layer_count - 1, -1, -1):
        turning = layer == layer_count - 1
        last = layer == 0
        kept, scale, inputs = stored[layer]
        sources = (inputs, gradient, target) if turning else (inputs, gradient)
        underway = [(at + 1, steps[at](state)) for at, state in underway]
        gradient, mine, other = run_backward(
            table, gains[layer], gains[layer_count], scale, kept, weights[layer], sources, turning, last
        )
        gradient, mine, other, states = tie((gradient, mine, other, [state for _, state in underway]))
        underway = [(at, state) for (at, _), state in zip(underway, states)]
        underway.append((0, (mine, other)))

    returned = gradient.reshape(width, feat_local, wide)
    returned = [lax.dynamic_index_in_dim(returned, tensor ^ k, 0, keepdims=False) for k in range(width)]
    returned = send(returned, planes)
    homes_of = []
    for at, state in underway:
        for step in steps[at:]:
            state = step(state)
        homes_of.append(state)
    combined = sum(inner_dot(chosen[k], returned[k], 1, 1) for k in range(width))
    d_patches = (0.5 * combined).astype(jnp.bfloat16)
    grad_factor = 1.0 / math.sqrt(2 * tok_rows * width * replicas)
    parts = [part.reshape(width, 2, chunk, size, size) for pair in homes_of[::-1] for part in pair]
    grad_left, grad_right = run_assemble(
        jnp.stack([core, tensor]).astype(jnp.int32), parts, layer_count, grad_factor
    )
    return (d_patches, grad_left[None], grad_right[None])


def solution(mesh):
    in_specs = (
        P(("section", "dp"), "tensor"),
        P(("section", "dp"), "tensor"),
        P(("section", "dp"), None),
        P("section", None, "tensor", None, None),
        P("section", None, "tensor", None, None),
        P("section", None, "tensor"),
    )
    out_specs = (
        P(("section", "dp"), "tensor"),
        P("section", None, "tensor", None, None),
        P("section", None, "tensor", None, None),
    )
    body = plane_shards if planes_fit(mesh) else layered_shards
    return jax.shard_map(
        body, mesh=mesh, in_specs=in_specs, out_specs=out_specs, check_vma=False)
```

```python
import math

import jax
import jax.numpy as jnp
from jax import lax
from jax.experimental import pallas as pl
from jax.experimental.pallas import tpu as pltpu
from jax.sharding import PartitionSpec as P

EPSILON = 1e-06
TANH_SLOPE = 0.7978845608028654
CUBIC_TERM = 0.044715


def shifted(value, axis, steps):
    count = lax.axis_size(axis)
    first, last = (max(0, -steps), min(count, count - steps))
    return lax.ppermute(value, axis, [(source, source + steps) for source in range(first, last)])


def gelu_value(values):
    tangent = jnp.tanh(TANH_SLOPE * (values + CUBIC_TERM * values * values * values))
    return 0.5 * values * (1.0 + tangent)


def gelu_slope(values):
    tangent = jnp.tanh(TANH_SLOPE * (values + CUBIC_TERM * values * values * values))
    return 0.5 * (1.0 + tangent) + 0.5 * values * (1.0 - tangent * tangent) * TANH_SLOPE * (
        1.0 + 3.0 * CUBIC_TERM * values * values
    )


def norm_pair(residuals, gain_pair, model_width):
    squares = lax.psum(
        (
            jnp.sum(residuals[0] * residuals[0], axis=(1, 2)),
            jnp.sum(residuals[1] * residuals[1], axis=(1, 2)),
        ),
        "tensor",
    )
    factors = [lax.rsqrt(squares[member] / model_width + EPSILON) for member in range(2)]
    normed = [
        residuals[member] * factors[member][:, None, None] * gain_pair[member][None]
        for member in range(2)
    ]
    return (factors, normed)


def norm_back_pair(residuals, factors, gain_pair, grad_normed, carried, model_width):
    weighted = [grad_normed[member] * gain_pair[member][None] for member in range(2)]
    inners = lax.psum(
        (
            jnp.sum(weighted[0] * residuals[0], axis=(1, 2)),
            jnp.sum(weighted[1] * residuals[1], axis=(1, 2)),
        ),
        "tensor",
    )
    return [
        carried[member]
        + factors[member][:, None, None] * weighted[member]
        - residuals[member] * (factors[member] ** 3 * inners[member] / model_width)[:, None, None]
        for member in range(2)
    ]


def layered_shards(patches, teacher, critic_pairs, left_factors, right_factors, norm_gains):
    sections = lax.axis_size("section")
    tensor_width = lax.axis_size("tensor")
    replicas = lax.axis_size("dp")
    tok_rows = patches.shape[0]
    feat_local = patches.shape[1]
    layer_count = left_factors.shape[1]
    local_blocks = left_factors.shape[2]
    block_size = left_factors.shape[3]
    all_blocks = local_blocks * tensor_width
    fold_ratio = block_size // all_blocks
    model_width = feat_local * tensor_width
    sixth_rows = tok_rows // 6
    leading = 2 * sixth_rows
    critic_ids = jnp.arange(4, dtype=jnp.int32)
    named_by = (
        (critic_pairs[:, 0:1] == critic_ids[None, :])
        | (critic_pairs[:, 1:2] == critic_ids[None, :])
    ).astype(jnp.int32)
    ranking = jnp.cumsum(named_by, axis=0) - 1
    wide_ids = critic_ids[None, :] < 2
    slot_width = 3 * sixth_rows
    spilled = wide_ids & (ranking >= 3 * sixth_rows)
    destination = jnp.where(spilled, critic_ids[None, :] + 2, critic_ids[None, :])
    slot_index = jnp.where(spilled, ranking - sixth_rows, ranking)
    flat_slot = destination * slot_width + slot_index
    chosen = jnp.take_along_axis(flat_slot, critic_pairs, axis=1)
    slot_total = sections * slot_width
    row_ids = jnp.broadcast_to(jnp.arange(tok_rows, dtype=jnp.int32)[:, None], chosen.shape)
    source_row = (
        jnp.full((slot_total,), tok_rows, jnp.int32).at[chosen.reshape(-1)].set(row_ids.reshape(-1))
    )
    send_patch = (
        patches.at[source_row]
        .get(mode="fill", fill_value=0)
        .reshape(sections, slot_width, local_blocks, block_size)
    )
    send_target = (
        teacher.at[source_row]
        .get(mode="fill", fill_value=0)
        .reshape(sections, slot_width, local_blocks, block_size)
    )
    recv_patch, recv_target = (
        lax.all_to_all(send_patch, "section", split_axis=0, concat_axis=0, tiled=True),
        lax.all_to_all(send_target, "section", split_axis=0, concat_axis=0, tiled=True),
    )
    residuals = [
        recv_patch[:, :leading].reshape(-1, local_blocks, block_size).astype(jnp.float32),
        recv_patch[:, leading:].reshape(-1, local_blocks, block_size).astype(jnp.float32),
    ]
    targets = [
        recv_target[:, :leading].reshape(-1, local_blocks, block_size).astype(jnp.float32),
        recv_target[:, leading:].reshape(-1, local_blocks, block_size).astype(jnp.float32),
    ]
    native = (left_factors[0], right_factors[0], norm_gains[0])
    borrowed = shifted((left_factors, right_factors, norm_gains), "section", 2)
    is_wide = lax.axis_index("section") < 2
    second = (
        jnp.where(is_wide, left_factors, borrowed[0])[0],
        jnp.where(is_wide, right_factors, borrowed[1])[0],
        jnp.where(is_wide, norm_gains, borrowed[2])[0],
    )
    left_sets = (native[0], second[0])
    right_sets = (native[1], second[1])
    gain_sets = (
        native[2].astype(jnp.float32).reshape(layer_count + 1, local_blocks, block_size),
        second[2].astype(jnp.float32).reshape(layer_count + 1, local_blocks, block_size),
    )
    stored = []
    for layer_index in range(layer_count):
        gain_pair = [gain_sets[0][layer_index], gain_sets[1][layer_index]]
        factors, normed = norm_pair(residuals, gain_pair, model_width)
        normed = [normed[member].astype(jnp.bfloat16) for member in range(2)]
        first_out = [
            jnp.einsum(
                "nki,kij->nkj",
                normed[member],
                left_sets[member][layer_index],
                preferred_element_type=jnp.float32,
            ).astype(jnp.bfloat16)
            for member in range(2)
        ]
        permuted = (
            lax.all_to_all(first_out[0], "tensor", split_axis=2, concat_axis=1, tiled=True),
            lax.all_to_all(first_out[1], "tensor", split_axis=2, concat_axis=1, tiled=True),
        )
        permuted = [
            permuted[member].reshape(
                permuted[member].shape[0], all_blocks, local_blocks, fold_ratio
            )
            for member in range(2)
        ]
        right_quads = [
            right_sets[member][layer_index].reshape(
                local_blocks, fold_ratio, all_blocks, block_size
            )
            for member in range(2)
        ]
        mixture = [
            jnp.einsum(
                "nkmp,mpkl->nml",
                permuted[member],
                right_quads[member],
                preferred_element_type=jnp.float32,
            )
            for member in range(2)
        ]
        stored.append((residuals, factors, normed, permuted, mixture, right_quads, gain_pair))
        residuals = [residuals[member] + gelu_value(mixture[member]) for member in range(2)]
    final_gains = [gain_sets[0][layer_count], gain_sets[1][layer_count]]
    factors, outputs = norm_pair(residuals, final_gains, model_width)
    gradients = norm_back_pair(
        residuals,
        factors,
        final_gains,
        [outputs[member] - targets[member] for member in range(2)],
        [jnp.zeros_like(residuals[member]) for member in range(2)],
        model_width,
    )
    left_terms = []
    right_terms = []
    for layer_index in range(layer_count - 1, -1, -1):
        inputs, factors, normed, permuted, mixture, right_quads, gain_pair = stored[layer_index]
        slopes = [
            (gradients[member] * gelu_slope(mixture[member])).astype(jnp.bfloat16)
            for member in range(2)
        ]
        right_grad = [
            jnp.einsum(
                "nkmp,nml->mpkl",
                permuted[member],
                slopes[member],
                preferred_element_type=jnp.float32,
            ).reshape(local_blocks, block_size, block_size)
            for member in range(2)
        ]
        back_moved = [
            jnp.einsum(
                "nml,mpkl->nkmp",
                slopes[member],
                right_quads[member],
                preferred_element_type=jnp.float32,
            )
            .astype(jnp.bfloat16)
            .reshape(slopes[member].shape[0], all_blocks, local_blocks * fold_ratio)
            for member in range(2)
        ]
        arrived = (
            lax.all_to_all(back_moved[0], "tensor", split_axis=1, concat_axis=2, tiled=True),
            lax.all_to_all(back_moved[1], "tensor", split_axis=1, concat_axis=2, tiled=True),
        )
        left_grad = [
            jnp.einsum(
                "nki,nkj->kij", normed[member], arrived[member], preferred_element_type=jnp.float32
            )
            for member in range(2)
        ]
        grad_normed = [
            jnp.einsum(
                "nkj,kij->nki",
                arrived[member],
                left_sets[member][layer_index],
                preferred_element_type=jnp.float32,
            )
            for member in range(2)
        ]
        gradients = norm_back_pair(inputs, factors, gain_pair, grad_normed, gradients, model_width)
        layer_left = jnp.stack(left_grad)
        layer_right = jnp.stack(right_grad)
        layer_left, layer_right = (
            lax.psum(layer_left.astype(jnp.bfloat16), "dp").astype(jnp.float32),
            lax.psum(layer_right.astype(jnp.bfloat16), "dp").astype(jnp.float32),
        )
        left_terms.insert(0, layer_left)
        right_terms.insert(0, layer_right)
    left_stack = jnp.stack(left_terms)
    right_stack = jnp.stack(right_terms)
    repaid = (
        shifted(left_stack[:, 1].astype(jnp.bfloat16), "section", -2).astype(jnp.float32),
        shifted(right_stack[:, 1].astype(jnp.bfloat16), "section", -2).astype(jnp.float32),
    )
    is_wide = lax.axis_index("section") < 2
    left_total = left_stack[:, 0] + jnp.where(is_wide, left_stack[:, 1] + repaid[0], 0.0)
    right_total = right_stack[:, 0] + jnp.where(is_wide, right_stack[:, 1] + repaid[1], 0.0)
    grad_factor = 1.0 / math.sqrt(2 * tok_rows * sections * replicas)
    returned = [
        gradients[member].astype(jnp.bfloat16).reshape(sections, -1, local_blocks, block_size)
        for member in range(2)
    ]
    back_lead, back_trail = (
        lax.all_to_all(returned[0], "section", split_axis=0, concat_axis=0, tiled=True),
        lax.all_to_all(returned[1], "section", split_axis=0, concat_axis=0, tiled=True),
    )
    gathered = jnp.concatenate((back_lead, back_trail), axis=1).reshape(
        slot_total, local_blocks, block_size
    )
    combined = (
        gathered[chosen[:, 0]].astype(jnp.float32) + gathered[chosen[:, 1]].astype(jnp.float32)
    ) * 0.5
    d_patches = combined.astype(jnp.bfloat16).reshape(tok_rows, feat_local)
    return (d_patches, (left_total * grad_factor)[None], (right_total * grad_factor)[None])


VMEM_LIMIT = 60 * 1024 * 1024
CHUNKS = 8
PARTS = 4
SMALL = (16, 128)
AXES = ("section", "tensor", "dp")


def planes_fit(mesh):
    sections = mesh.shape["section"]
    paired = mesh.shape["dp"] == 2 and sections & (sections - 1) == 0
    return paired and mesh.shape["tensor"] == sections


def inner_dot(left, right, left_dim, right_dim):
    return lax.dot_general(
        left,
        right,
        (((left_dim,), (right_dim,)), ((), ())),
        preferred_element_type=jnp.float32,
    )


def fold_rows(values):
    return jnp.sum(values.reshape(values.shape[0] // 8, 8, values.shape[1]), axis=0)


def block_rows(block, size):
    return pl.ds(pl.multiple_of(block * size, size), size)


def column(gain_ref, block, slots):
    blocks = gain_ref.shape[1]
    picked = lax.broadcasted_iota(jnp.int32, (blocks, slots), 0) == block
    return inner_dot(gain_ref[...], picked.astype(jnp.bfloat16), 1, 0)


def chunk_copy(source, target, sems, chunk):
    rows = target.shape[0] // CHUNKS
    at = pl.ds(pl.multiple_of(chunk * rows, rows), rows)
    return pltpu.make_async_copy(source.at[at], target.at[at], sems.at[chunk])


def start_chunks(source, target, sems):
    for chunk in range(CHUNKS):
        chunk_copy(source, target, sems, chunk).start()


def wait_chunks(source, target, sems):
    for chunk in range(CHUNKS):
        chunk_copy(source, target, sems, chunk).wait()


def quarter_copies(pieces, whole, sems, me, outward=False):
    rows = pieces[0].shape[0]
    copies = []
    for k, piece in enumerate(pieces):
        part = whole.at[pl.ds(pl.multiple_of((me ^ k) * rows, rows), rows)]
        ends = (part, piece) if outward else (piece, part)
        copies.append(pltpu.make_async_copy(*ends, sems.at[k]))
    return copies


def factor_copies(parts, held, sems, side, outward=False):
    count = parts[0].shape[0]
    copies = []
    for at, ref in enumerate(parts):
        inside = held.at[pl.ds(at * count, count), side]
        ends = (inside, ref.at[:, side]) if outward else (ref.at[:, side], inside)
        copies.append(pltpu.make_async_copy(*ends, sems.at[side, at]))
    return copies


def by_chunk(blocks, step, carry, before=None, after=None):
    per_chunk = blocks // CHUNKS

    def one(chunk, carry):
        if before is not None:
            before(chunk)
        carry = lax.fori_loop(
            0, per_chunk, lambda at, now: step(chunk * per_chunk + at, now), carry, unroll=True
        )
        if after is not None:
            after(chunk)
        return carry

    return lax.fori_loop(0, CHUNKS, one, carry)


def forward_kernel(first, inputs, table_ref, gain_ref, sums_ref, *refs):
    sources, refs = refs[:inputs], refs[inputs:]
    parts, sources = sources[:PARTS], sources[PARTS:]
    out_ref, u_ref, z_ref, slope_ref, scale_ref, next_ref = refs[:6]
    raw, h, w, u, z, slope, mid, in_sems, w_sems, out_sems = refs[6:]
    features, slots = h.shape
    size = w.shape[-1]
    chunk_blocks = w.shape[2]
    blocks = features // size
    fold = size // blocks

    left_in = factor_copies(parts, w, w_sems, 0)
    right_in = factor_copies(parts, w, w_sems, 1)
    if first:
        pieces = quarter_copies(sources, raw, in_sems, table_ref[2, 0])
        for copy in pieces + left_in + right_in:
            copy.start()
        for copy in pieces:
            copy.wait()

        def squares(block, total):
            rows = block_rows(block, size)
            part = raw[rows, :].astype(jnp.float32)
            h[rows, :] = part
            return total + fold_rows(part * part)

        total = by_chunk(blocks, squares, jnp.zeros((8, slots), jnp.float32))
    else:
        for copy in left_in:
            copy.start()
        start_chunks(sources[0], h, in_sems)
        for copy in right_in:
            copy.start()
        total = sums_ref[...]
    scale = lax.rsqrt(jnp.sum(total, axis=0, keepdims=True) / features + EPSILON)
    scale_ref[...] = jnp.broadcast_to(scale, scale_ref.shape)
    for copy in left_in:
        copy.wait()

    def arrive(chunk):
        if not first:
            chunk_copy(sources[0], h, in_sems, chunk).wait()

    def left(block, carry):
        rows = block_rows(block, size)
        place = table_ref[0, block]
        normed = (h[rows, :] * scale * column(gain_ref, block, slots)).astype(jnp.bfloat16)
        u[rows, :] = normed
        weight = w[place // chunk_blocks, 0, place % chunk_blocks]
        mid[rows, :] = inner_dot(weight, normed, 0, 0)
        return carry

    def leave_left(chunk):
        chunk_copy(u, u_ref, out_sems.at[0], chunk).start()

    by_chunk(blocks, left, 0, arrive, leave_left)
    for copy in right_in:
        copy.wait()

    def right(block, total):
        rows = block_rows(block, size)
        place = table_ref[0, block]
        moved = [mid[pl.ds(block * fold + q, blocks, stride=size), :] for q in range(fold)]
        moved = jnp.concatenate(moved, axis=0).astype(jnp.bfloat16)
        z[rows, :] = moved
        weight = w[place // chunk_blocks, 1, place % chunk_blocks]
        mixture = inner_dot(weight, moved, 0, 0)
        squared = mixture * mixture
        tangent = jnp.tanh(mixture * (TANH_SLOPE + (TANH_SLOPE * CUBIC_TERM) * squared))
        half = 0.5 + 0.5 * tangent
        following = h[rows, :] + mixture * half
        h[rows, :] = following
        steep = half + mixture * (1.0 - tangent * tangent) * (
            0.5 * TANH_SLOPE + (1.5 * TANH_SLOPE * CUBIC_TERM) * squared
        )
        slope[rows, :] = steep.astype(jnp.bfloat16)
        return total + fold_rows(following * following)

    leaving = ((h, out_ref, 1), (z, z_ref, 2), (slope, slope_ref, 3))

    def leave_right(chunk):
        for source, target, at in leaving:
            chunk_copy(source, target, out_sems.at[at], chunk).start()

    next_ref[...] = by_chunk(blocks, right, jnp.zeros((8, slots), jnp.float32), None, leave_right)
    for source, target, at in ((u, u_ref, 0),) + leaving:
        wait_chunks(source, target, out_sems.at[at])


def backward_kernel(turning, last, inputs, table_ref, gain_ref, end_gain_ref, scale_ref, *refs):
    sources, refs = refs[:inputs], refs[inputs:]
    slope_ref, z_ref, u_ref = sources[:3]
    parts, sources = sources[3 : 3 + PARTS], sources[3 + PARTS :]
    count = len(refs) - 17
    outs, refs = refs[:count], refs[count:]
    own_grad, peer_grad = refs[:2]
    g, slope, z, u, h, w, gw, mid, turned, top, goal = refs[2:13]
    in_sems, w_sems, out_sems, gw_sems = refs[13:]
    me = table_ref[2, 0]
    features, slots = g.shape
    size = w.shape[-1]
    chunk_blocks = w.shape[2]
    blocks = features // size
    fold = size // blocks

    left_in = factor_copies(parts, w, w_sems, 0)
    right_in = factor_copies(parts, w, w_sems, 1)
    g_ref, sources = sources[0], sources[1:]
    if turning:
        goals = quarter_copies(sources[1:], goal, in_sems.at[5], me)
        start_chunks(g_ref, top, in_sems.at[0])
        for copy in goals:
            copy.start()
    else:
        start_chunks(g_ref, g, in_sems.at[0])
    for copy in right_in:
        copy.start()
    start_chunks(slope_ref, slope, in_sems.at[1])
    start_chunks(z_ref, z, in_sems.at[2])
    for copy in left_in:
        copy.start()
    start_chunks(u_ref, u, in_sems.at[3])
    if last:
        starts = quarter_copies(sources, h, in_sems.at[5], me)
        for copy in starts:
            copy.start()
    else:
        start_chunks(sources[0], h, in_sems.at[4])

    if turning:
        zero = jnp.zeros((8, slots), jnp.float32)

        def sums(block, totals):
            rows = block_rows(block, size)
            part = top[rows, :]
            scaled = part * column(end_gain_ref, block, slots)
            return (
                totals[0] + fold_rows(part * part),
                totals[1] + fold_rows(scaled * scaled),
                totals[2] + fold_rows(scaled * goal[rows, :].astype(jnp.float32)),
            )

        def arrive_top(chunk):
            chunk_copy(g_ref, top, in_sems.at[0], chunk).wait()

        for copy in goals:
            copy.wait()
        totals = by_chunk(blocks, sums, (zero, zero, zero), arrive_top)
        squares, gained, crossed = [jnp.sum(total, axis=0, keepdims=True) for total in totals]
        end_scale = lax.rsqrt(squares / features + EPSILON)
        end_back = end_scale * end_scale * end_scale * (end_scale * gained - crossed) / features

    for copy in right_in:
        copy.wait()

    def arrive_right(chunk):
        if not turning:
            chunk_copy(g_ref, g, in_sems.at[0], chunk).wait()
        chunk_copy(slope_ref, slope, in_sems.at[1], chunk).wait()
        chunk_copy(z_ref, z, in_sems.at[2], chunk).wait()

    def right(block, carry):
        rows = block_rows(block, size)
        place, home = table_ref[0, block], table_ref[1, block]
        at = (place // chunk_blocks, 1, place % chunk_blocks)
        to = (home // chunk_blocks, 1, home % chunk_blocks)
        if turning:
            part = top[rows, :]
            gain = column(end_gain_ref, block, slots)
            error = (part * end_scale * gain - goal[rows, :].astype(jnp.float32)) * gain
            gradient = end_scale * error - part * end_back
            g[rows, :] = gradient
        else:
            gradient = g[rows, :]
        steep = (gradient * slope[rows, :].astype(jnp.float32)).astype(jnp.bfloat16)
        gw[to] = inner_dot(z[rows, :], steep, 1, 1).astype(jnp.bfloat16)
        mid[rows, :] = inner_dot(w[at], steep, 1, 0)
        return carry

    by_chunk(blocks, right, 0, arrive_right)
    right_out = factor_copies((own_grad, peer_grad), gw, gw_sems, 1, outward=True)
    for copy in right_out:
        copy.start()
    for copy in left_in:
        copy.wait()
    scale = scale_ref[0:1, :]

    if last:
        for copy in starts:
            copy.wait()

    def arrive_left(chunk):
        chunk_copy(u_ref, u, in_sems.at[3], chunk).wait()
        if not last:
            chunk_copy(sources[0], h, in_sems.at[4], chunk).wait()

    def left(block, total):
        rows = block_rows(block, size)
        place, home = table_ref[0, block], table_ref[1, block]
        at = (place // chunk_blocks, 0, place % chunk_blocks)
        to = (home // chunk_blocks, 0, home % chunk_blocks)
        slot = block % turned.shape[0]
        for q in range(fold):
            turned[slot, pl.ds(q, blocks, stride=fold), :] = mid[
                pl.ds(q * blocks + block, blocks, stride=size), :
            ]
        arrived = turned[slot].astype(jnp.bfloat16)
        gw[to] = inner_dot(u[rows, :], arrived, 1, 1).astype(jnp.bfloat16)
        weighted = inner_dot(w[at], arrived, 1, 0) * column(gain_ref, block, slots)
        g[rows, :] = g[rows, :] + scale * weighted
        return total + fold_rows(weighted * h[rows, :].astype(jnp.float32))

    total = by_chunk(blocks, left, jnp.zeros((8, slots), jnp.float32), arrive_left)
    left_out = factor_copies((own_grad, peer_grad), gw, gw_sems, 0, outward=True)
    for copy in left_out:
        copy.start()
    back = scale * scale * scale * jnp.sum(total, axis=0, keepdims=True) / features

    def finish(block, carry):
        rows = block_rows(block, size)
        ended = g[rows, :] - h[rows, :].astype(jnp.float32) * back
        if last:
            u[rows, :] = ended.astype(jnp.bfloat16)
        else:
            g[rows, :] = ended
        return carry

    if last:
        by_chunk(blocks, finish, 0)
        ends = quarter_copies(outs, u, out_sems, me, outward=True)
        for copy in ends:
            copy.start()
        for copy in ends:
            copy.wait()
    else:
        by_chunk(blocks, finish, 0, None, lambda chunk: chunk_copy(g, outs[0], out_sems, chunk).start())
        wait_chunks(g, outs[0], out_sems)
    for copy in right_out + left_out:
        copy.wait()


def shape_of(shape, dtype):
    return jax.ShapeDtypeStruct(shape, dtype)


SMEM = pl.BlockSpec(memory_space=pltpu.SMEM)
INSIDE = pl.BlockSpec(memory_space=pltpu.VMEM)
OUTSIDE = pl.BlockSpec(memory_space=pl.ANY)


def run_forward(table, gain, sums, residual, weights):
    first = len(residual) > 1
    whole = (residual[0].shape[0] * len(residual), residual[0].shape[1])
    sources = (*weights, *residual)
    held = (PARTS * weights[0].shape[0],) + weights[0].shape[1:]
    out_shape = (
        shape_of(whole, jnp.float32),
        shape_of(whole, jnp.bfloat16),
        shape_of(whole, jnp.bfloat16),
        shape_of(whole, jnp.bfloat16),
        shape_of((8, whole[1]), jnp.float32),
        shape_of((8, whole[1]), jnp.float32),
    )
    return pl.pallas_call(
        lambda *refs: forward_kernel(first, len(sources), *refs),
        in_specs=[SMEM, INSIDE, INSIDE] + [OUTSIDE] * len(sources),
        out_specs=[OUTSIDE] * 4 + [INSIDE] * 2,
        out_shape=out_shape,
        scratch_shapes=[
            pltpu.VMEM(whole if first else SMALL, jnp.bfloat16),
            pltpu.VMEM(whole, jnp.float32),
            pltpu.VMEM(held, jnp.bfloat16),
            pltpu.VMEM(whole, jnp.bfloat16),
            pltpu.VMEM(whole, jnp.bfloat16),
            pltpu.VMEM(whole, jnp.bfloat16),
            pltpu.VMEM(whole, jnp.float32),
            pltpu.SemaphoreType.DMA((CHUNKS,)),
            pltpu.SemaphoreType.DMA((2, PARTS)),
            pltpu.SemaphoreType.DMA((4, CHUNKS)),
        ],
        compiler_params=pltpu.CompilerParams(vmem_limit_bytes=VMEM_LIMIT),
        cost_estimate=pl.CostEstimate(
            flops=FORWARD_COST, bytes_accessed=20 * whole[0] * whole[1], transcendentals=0
        ),
        name="forward_layer",
    )(table, gain, sums, *sources)


def run_backward(table, gain, end_gain, scale, kept, weights, sources, turning, last):
    whole = kept[0].shape
    width = len(sources) - 1
    sources = (*kept, *weights, *sources)
    held = (PARTS * weights[0].shape[0],) + weights[0].shape[1:]
    half = (held[0] // 2,) + held[1:]
    ends = [shape_of(whole, jnp.float32)]
    if last:
        ends = [shape_of((whole[0] // width, whole[1]), jnp.bfloat16)] * width
    out_shape = ends + [shape_of(half, jnp.bfloat16)] * 2
    return pl.pallas_call(
        lambda *refs: backward_kernel(turning, last, len(sources), *refs),
        in_specs=[SMEM] + [INSIDE] * 3 + [OUTSIDE] * len(sources),
        out_specs=[OUTSIDE] * len(out_shape),
        out_shape=out_shape,
        scratch_shapes=[
            pltpu.VMEM(whole, jnp.float32),
            pltpu.VMEM(whole, jnp.bfloat16),
            pltpu.VMEM(whole, jnp.bfloat16),
            pltpu.VMEM(whole, jnp.bfloat16),
            pltpu.VMEM(whole, jnp.bfloat16 if last else jnp.float32),
            pltpu.VMEM(held, jnp.bfloat16),
            pltpu.VMEM(held, jnp.bfloat16),
            pltpu.VMEM(whole, jnp.float32),
            pltpu.VMEM((8, held[-1], whole[1]), jnp.float32),
            pltpu.VMEM(whole if turning else SMALL, jnp.float32),
            pltpu.VMEM(whole if turning else SMALL, jnp.bfloat16),
            pltpu.SemaphoreType.DMA((6, CHUNKS)),
            pltpu.SemaphoreType.DMA((2, PARTS)),
            pltpu.SemaphoreType.DMA((CHUNKS,)),
            pltpu.SemaphoreType.DMA((2, PARTS)),
        ],
        compiler_params=pltpu.CompilerParams(vmem_limit_bytes=VMEM_LIMIT),
        cost_estimate=pl.CostEstimate(
            flops=BACKWARD_COST, bytes_accessed=30 * whole[0] * whole[1], transcendentals=0
        ),
        name="backward_layer",
    )(table, gain, end_gain, scale, *sources)


def copies_kernel(plan, inputs, outputs, *refs):
    sems = refs[-1]
    copies = [
        pltpu.make_async_copy(source, target, sems.at[at])
        for at, (source, target) in enumerate(plan(refs[:inputs], refs[inputs : inputs + outputs]))
    ]
    for copy in copies:
        copy.start()
    for copy in copies:
        copy.wait()


def run_copies(plan, scalars, inputs, out_shape, most, name):
    extra = [] if scalars is None else [scalars]
    size = sum(math.prod(out.shape) for out in out_shape)
    return pl.pallas_call(
        lambda *refs: copies_kernel(plan, len(extra) + len(inputs), len(out_shape), *refs),
        in_specs=[SMEM] * len(extra) + [OUTSIDE] * len(inputs),
        out_specs=[OUTSIDE] * len(out_shape),
        out_shape=out_shape,
        scratch_shapes=[pltpu.SemaphoreType.DMA((most,))],
        cost_estimate=pl.CostEstimate(flops=0, bytes_accessed=4 * size, transcendentals=0),
        name=name,
    )(*extra, *inputs)


def joined(parts):
    rows = parts[0].shape[0]
    whole = shape_of((rows * len(parts),) + parts[0].shape[1:], parts[0].dtype)

    def plan(sources, targets):
        return [(source, targets[0].at[pl.ds(at * rows, rows)]) for at, source in enumerate(sources)]

    return run_copies(plan, None, parts, [whole], len(parts), "join")[0]


def factor_pieces(place, left, right, gain_rows, groups, chunk):
    width = 4
    size = left.shape[-1]
    shapes = []
    for group in groups:
        rows = len(group) * 2 * chunk * size + (gain_rows.shape[0] if group[0] == 0 else 0)
        shapes += [shape_of((rows, size), jnp.bfloat16)] * width

    def plan(sources, targets):
        place_ref, left_ref, right_ref, gain_ref = sources
        copies = []
        for at, group in enumerate(groups):
            for j in range(width):
                target = targets[at * width + j]
                start = (place_ref[2] * width + (place_ref[0] ^ place_ref[1] ^ j)) * chunk
                row = 0
                for layer in group:
                    for ref in (left_ref, right_ref):
                        for inside in range(chunk):
                            copies.append((ref.at[layer, start + inside], target.at[pl.ds(row, size)]))
                            row += size
                if group[0] == 0:
                    copies.append((gain_ref, target.at[pl.ds(row, gain_rows.shape[0])]))
        return copies

    most = width * (sum(len(group) for group in groups) * 2 * chunk + 1)
    flat = run_copies(plan, place, (left, right, gain_rows), shapes, most, "pieces")
    return [flat[at * width : (at + 1) * width] for at in range(len(groups))]


def choice(pairs, critic, slots):
    rows = pairs.shape[0]
    named = (pairs[:, 0:1] == critic) | (pairs[:, 1:2] == critic)
    named = jnp.broadcast_to(named.astype(jnp.float32), (rows, slots))
    before = lax.broadcasted_iota(jnp.int32, (rows, rows), 1) < lax.broadcasted_iota(jnp.int32, (rows, rows), 0)
    rank = inner_dot(before.astype(jnp.bfloat16), named.astype(jnp.bfloat16), 1, 0)
    at = lax.broadcasted_iota(jnp.int32, (rows, slots), 1).astype(jnp.float32)
    return jnp.where(rank == at, named, 0.0).astype(jnp.bfloat16)


def pick_kernel(place_ref, pairs_ref, values_ref, *out_refs):
    width = len(out_refs)
    features, slots = out_refs[0].shape
    pairs = pairs_ref[...]
    chosen = [choice(pairs, place_ref[1] ^ k, slots) for k in range(width)]
    step = 512
    for start in range(0, features, step):
        part = values_ref[:, pl.ds(start, step)]
        for k in range(width):
            out_refs[k][pl.ds(start, step), :] = inner_dot(part, chosen[k], 0, 0).astype(jnp.bfloat16)


def run_pick(place, pairs, values, width, slots):
    rows, features = values.shape
    return pl.pallas_call(
        pick_kernel,
        in_specs=[SMEM] + [INSIDE] * 2,
        out_specs=[INSIDE] * width,
        out_shape=[shape_of((features, slots), jnp.bfloat16)] * width,
        compiler_params=pltpu.CompilerParams(vmem_limit_bytes=VMEM_LIMIT),
        cost_estimate=pl.CostEstimate(
            flops=2 * rows * features * slots * width, bytes_accessed=8 * rows * features, transcendentals=0
        ),
        name="pick",
    )(place, pairs, values)


def combine_kernel(place_ref, pairs_ref, *refs):
    came, out_ref = refs[:-1], refs[-1]
    width = len(came)
    features, slots = came[0].shape
    pairs = pairs_ref[...]
    chosen = [choice(pairs, place_ref[1] ^ k, slots) for k in range(width)]
    step = 512
    for start in range(0, features, step):
        total = sum(inner_dot(chosen[k], came[k][pl.ds(start, step), :], 1, 1) for k in range(width))
        out_ref[:, pl.ds(start, step)] = (0.5 * total).astype(jnp.bfloat16)


def run_combine(place, pairs, came):
    rows = pairs.shape[0]
    features = came[0].shape[0]
    return pl.pallas_call(
        combine_kernel,
        in_specs=[SMEM] + [INSIDE] * (1 + len(came)),
        out_specs=INSIDE,
        out_shape=shape_of((rows, features), jnp.bfloat16),
        compiler_params=pltpu.CompilerParams(vmem_limit_bytes=VMEM_LIMIT),
        cost_estimate=pl.CostEstimate(
            flops=2 * rows * came[0].size * len(came), bytes_accessed=4 * came[0].size * len(came), transcendentals=0
        ),
        name="combine",
    )(place, pairs, *came)


FORWARD_COST = 15_000_000_000
BACKWARD_COST = 18_000_000_000


def assemble_kernel(layer_count, factor, place_ref, *refs):
    sources, (left_ref, right_ref) = refs[: 2 * layer_count], refs[2 * layer_count : 2 * layer_count + 2]
    held, wide, in_sems, out_sems = refs[2 * layer_count + 2 :]
    width, chunk = held.shape[1], held.shape[3]
    origin, core = place_ref[0] ^ place_ref[1], place_ref[2]
    arrivals = [
        pltpu.make_async_copy(source, held.at[at], in_sems.at[at]) for at, source in enumerate(sources)
    ]
    for copy in arrivals:
        copy.start()
    leaving = []
    for at in range(2 * layer_count):
        arrivals[at].wait()
        layer, side = at // 2, at % 2
        half = core if side == 0 else 1 - core
        wide[at] = held[at].astype(jnp.float32) * factor
        for k in range(width):
            start = (half * width + (origin ^ k)) * chunk
            for which, target in enumerate((left_ref, right_ref)):
                copy = pltpu.make_async_copy(
                    wide.at[at, k, which],
                    target.at[layer, pl.ds(start, chunk)],
                    out_sems.at[(at * width + k) * 2 + which],
                )
                copy.start()
                leaving.append(copy)
    for copy in leaving:
        copy.wait()


def run_assemble(places, pieces, layer_count, factor):
    piece = pieces[0].shape
    blocks = 2 * piece[0] * piece[2]
    out = shape_of((layer_count, blocks) + piece[3:], jnp.float32)
    return pl.pallas_call(
        lambda *refs: assemble_kernel(layer_count, factor, *refs),
        in_specs=[SMEM] + [OUTSIDE] * len(pieces),
        out_specs=[OUTSIDE] * 2,
        out_shape=[out] * 2,
        scratch_shapes=[
            pltpu.VMEM((2 * layer_count,) + piece, jnp.bfloat16),
            pltpu.VMEM((2 * layer_count,) + piece, jnp.float32),
            pltpu.SemaphoreType.DMA((2 * layer_count,)),
            pltpu.SemaphoreType.DMA((4 * layer_count * piece[0],)),
        ],
        compiler_params=pltpu.CompilerParams(vmem_limit_bytes=VMEM_LIMIT),
        cost_estimate=pl.CostEstimate(
            flops=0, bytes_accessed=12 * layer_count * math.prod(piece), transcendentals=0
        ),
        name="assemble",
    )(places, *pieces)


def plane_routes(width, replicas):
    bits = width.bit_length() - 1
    orders = [[(step + d) % bits for step in range(bits)] for d in range(replicas)]
    every = [(s, t, d) for s in range(width) for t in range(width) for d in range(replicas)]

    def route(move):
        def index(s, t, d):
            return (s * width + t) * replicas + d

        return [(index(*place), index(*move(*place))) for place in every]

    ranks = [[0] * width for _ in range(replicas)]
    for d in range(replicas):
        for r in range(width):
            ranks[d][sum(((r >> at) & 1) << orders[d][at] for at in range(bits))] = r
    return {
        "spread": [route(lambda s, t, d, j=j: (s ^ t ^ j, t, d)) for j in range(width)],
        "lift": [route(lambda s, t, d, j=j: (s, t ^ s ^ j, d)) for j in range(width)],
        "across": [route(lambda s, t, d, at=at: (s ^ (1 << orders[d][at]), t, d)) for at in range(bits)],
        "cores": route(lambda s, t, d: (s, t, 1 - d)),
        "sections": [route(lambda s, t, d, k=k: (s ^ k, t, d)) for k in range(width)],
        "planes": [route(lambda s, t, d, k=k: (s, t ^ k, d)) for k in range(width)],
        "homes": [route(lambda s, t, d, j=j: (t, t ^ s ^ j, d)) for j in range(width)],
    }, ranks


def added(*parts):
    return sum(part.astype(jnp.float32) for part in parts).astype(jnp.bfloat16)


def plane_shards(patches, teacher, critic_pairs, left_factors, right_factors, norm_gains):
    width = lax.axis_size("section")
    replicas = lax.axis_size("dp")
    tok_rows, feat_local = patches.shape
    layer_count, local_blocks, size = left_factors.shape[1:4]
    blocks = feat_local * width // size
    wide = 2 * tok_rows // 3
    chunk = local_blocks // (replicas * width)
    layer_rows = 2 * chunk * size
    routes, ranks = plane_routes(width, replicas)
    section = lax.axis_index("section")
    tensor = lax.axis_index("tensor")
    core = lax.axis_index("dp")
    place = jnp.stack([section, tensor, core]).astype(jnp.int32)
    tie = lax.optimization_barrier

    def move(value, route):
        return lax.ppermute(value, AXES, route)

    def move_all(values, name):
        return [move(value, route) for value, route in zip(values, routes[name])]

    def send(values, name):
        return [values[0]] + [move(values[k], routes[name][k]) for k in range(1, width)]

    def gather_one(mine):
        return joined([mine, move(mine, routes["across"][0])])

    def gather_two(pair):
        return pair, move(pair, routes["across"][1]), move(pair, routes["cores"])

    def gather_three(pair, other, peer):
        return [pair, other, peer, move(other, routes["cores"])]

    def as_weights(parts):
        return [part.reshape(-1, 2, chunk, size, size) for part in parts]

    block = jnp.arange(blocks, dtype=jnp.int32)
    inside = block % local_blocks
    replica = inside // (width * chunk)
    part = (replica != core).astype(jnp.int32)
    distance = section ^ ((inside // chunk) % width)
    piece = tensor ^ (section ^ distance) ^ (block // local_blocks)
    rank = jnp.array(ranks, jnp.int32)[replica, distance]
    table = jnp.stack(
        [
            ((part * width + rank) * width + piece) * chunk + inside % chunk,
            ((part * width + distance) * width + piece) * chunk + inside % chunk,
            jnp.broadcast_to(tensor, block.shape),
        ]
    ).astype(jnp.int32)

    patch_sent = run_pick(place, critic_pairs, patches, width, wide)
    patch_sent, factors = tie((patch_sent, (left_factors[0], right_factors[0])))
    groups = [(0,), (1,), tuple(range(2, layer_count))]
    gain_rows = norm_gains[0].reshape(-1, size)
    pieces = factor_pieces(place, *factors, gain_rows, groups, chunk)

    patch_came = send(patch_sent, "planes")
    near = [move_all(pieces[0], "spread")]
    near[0], pieces[1] = tie((near[0], pieces[1]))
    near.append(move_all(pieces[1], "spread"))
    front = move_all(near[0], "lift")
    near[1], pieces[2] = tie((near[1], pieces[2]))
    near.append(move_all(pieces[2], "spread"))
    front, near[1] = tie((front, near[1]))
    second = move_all(near[1], "lift")
    gains = jnp.stack([value[layer_rows:] for value in front])[jnp.arange(width) ^ section ^ tensor]
    gains = gains.reshape(width, layer_count + 1, local_blocks, size).transpose(1, 3, 0, 2)
    gains = gains.reshape(layer_count + 1, size, blocks)
    lowest = [joined([value[:layer_rows].reshape(1, layer_rows, size) for value in front])]
    pair = gather_one(lowest[0])
    gathered = gather_two(pair)
    weights = [as_weights(gather_three(*gathered))]
    lowest.append(joined([value.reshape(1, layer_rows, size) for value in second]))
    pair = gather_one(lowest[1])
    patch_came, second, near[2] = tie((patch_came, second, near[2]))
    later = move_all(near[2], "lift")
    pairs = [None, pair] + [None] * (layer_count - 2)
    pairs[1], later, teacher = tie((pairs[1], later, teacher))
    for layer in range(2, layer_count):
        at = (layer - 2) * layer_rows
        lowest.append(joined([value[at : at + layer_rows].reshape(1, layer_rows, size) for value in later]))
    target_sent = run_pick(place, critic_pairs, teacher, width, wide)

    residual = patch_came
    sums = jnp.zeros((8, wide), jnp.float32)
    flying = {1: gather_two(pairs[1])}
    if layer_count > 2:
        pairs[2] = gather_one(lowest[2])
    residual, flying, pairs, target_sent = tie((residual, flying, pairs, target_sent))
    stored = []
    for layer in range(layer_count):
        ahead = {}
        if layer + 1 < layer_count:
            ahead["weights"] = gather_three(*flying.pop(layer + 1))
        if layer + 2 < layer_count:
            ahead["two"] = gather_two(pairs[layer + 2])
        if layer + 3 < layer_count:
            ahead["one"] = (lowest[layer + 3], move(lowest[layer + 3], routes["across"][0]))
        following, u, z, slope, scale, sums = run_forward(
            table, gains[layer], sums, residual, weights[layer]
        )
        stored.append(((slope, z, u), scale, residual))
        following, ahead = tie((following, ahead))
        residual = (following,)
        if layer + 1 < layer_count:
            weights.append(as_weights(ahead["weights"]))
        if layer + 2 < layer_count:
            flying[layer + 2] = ahead["two"]
        if layer + 3 < layer_count:
            pairs[layer + 3] = joined(list(ahead["one"]))
        if layer == 0:
            target_sent, sums = tie((target_sent, sums))
            target = send(target_sent, "planes")

    def core_sum(mine, other):
        return (mine, move(other, routes["cores"]))

    def plane_sum(value):
        value = value.reshape(width, width, layer_rows, size)
        return send([value[k] for k in range(width)], "sections")

    def homeward(value):
        return move_all([value[j] for j in range(width)], "homes")

    def both_halves(parts):
        whole = joined([part.reshape(1, layer_rows, size) for part in parts])
        return whole, move(whole, routes["cores"])

    steps = (
        lambda state: core_sum(*state),
        lambda state: plane_sum(added(*state)),
        lambda state: homeward(added(*state)),
        both_halves,
    )
    gradient = residual[0]
    underway = []
    for layer in range(layer_count - 1, -1, -1):
        turning = layer == layer_count - 1
        last = layer == 0
        kept, scale, inputs = stored[layer]
        sources = (gradient, *inputs, *target) if turning else (gradient, *inputs)
        underway = [(at + 1, steps[at](state)) for at, state in underway]
        *gradient, mine, other = run_backward(
            table, gains[layer], gains[layer_count], scale, kept, weights[layer], sources, turning, last
        )
        gradient, mine, other, states = tie((gradient, mine, other, [state for _, state in underway]))
        underway = [(at, state) for (at, _), state in zip(underway, states)]
        underway.append((0, (mine, other)))
        if not last:
            gradient = gradient[0]

    returned = send(gradient, "planes")
    homes_of = []
    for at, state in underway:
        for step in steps[at:]:
            state = step(state)
        homes_of.append(state)
    d_patches = run_combine(place, critic_pairs, returned)
    grad_factor = 1.0 / math.sqrt(2 * tok_rows * width * replicas)
    parts = [part.reshape(width, 2, chunk, size, size) for pair in homes_of[::-1] for part in pair]
    grad_left, grad_right = run_assemble(place, parts, layer_count, grad_factor)
    return (d_patches, grad_left[None], grad_right[None])


def solution(mesh):
    in_specs = (
        P(("section", "dp"), "tensor"),
        P(("section", "dp"), "tensor"),
        P(("section", "dp"), None),
        P("section", None, "tensor", None, None),
        P("section", None, "tensor", None, None),
        P("section", None, "tensor"),
    )
    out_specs = (
        P(("section", "dp"), "tensor"),
        P("section", None, "tensor", None, None),
        P("section", None, "tensor", None, None),
    )
    body = plane_shards if planes_fit(mesh) else layered_shards
    return jax.shard_map(
        body, mesh=mesh, in_specs=in_specs, out_specs=out_specs, check_vma=False)
```

```python
import math

import jax
import jax.numpy as jnp
from jax import lax
from jax.experimental import pallas as pl
from jax.experimental.pallas import tpu as pltpu
from jax.sharding import PartitionSpec as P

EPSILON = 1e-06
TANH_SLOPE = 0.7978845608028654
CUBIC_TERM = 0.044715


def shifted(value, axis, steps):
    count = lax.axis_size(axis)
    first, last = (max(0, -steps), min(count, count - steps))
    return lax.ppermute(value, axis, [(source, source + steps) for source in range(first, last)])


def gelu_value(values):
    tangent = jnp.tanh(TANH_SLOPE * (values + CUBIC_TERM * values * values * values))
    return 0.5 * values * (1.0 + tangent)


def gelu_slope(values):
    tangent = jnp.tanh(TANH_SLOPE * (values + CUBIC_TERM * values * values * values))
    return 0.5 * (1.0 + tangent) + 0.5 * values * (1.0 - tangent * tangent) * TANH_SLOPE * (
        1.0 + 3.0 * CUBIC_TERM * values * values
    )


def norm_pair(residuals, gain_pair, model_width):
    squares = lax.psum(
        (
            jnp.sum(residuals[0] * residuals[0], axis=(1, 2)),
            jnp.sum(residuals[1] * residuals[1], axis=(1, 2)),
        ),
        "tensor",
    )
    factors = [lax.rsqrt(squares[member] / model_width + EPSILON) for member in range(2)]
    normed = [
        residuals[member] * factors[member][:, None, None] * gain_pair[member][None]
        for member in range(2)
    ]
    return (factors, normed)


def norm_back_pair(residuals, factors, gain_pair, grad_normed, carried, model_width):
    weighted = [grad_normed[member] * gain_pair[member][None] for member in range(2)]
    inners = lax.psum(
        (
            jnp.sum(weighted[0] * residuals[0], axis=(1, 2)),
            jnp.sum(weighted[1] * residuals[1], axis=(1, 2)),
        ),
        "tensor",
    )
    return [
        carried[member]
        + factors[member][:, None, None] * weighted[member]
        - residuals[member] * (factors[member] ** 3 * inners[member] / model_width)[:, None, None]
        for member in range(2)
    ]


def layered_shards(patches, teacher, critic_pairs, left_factors, right_factors, norm_gains):
    sections = lax.axis_size("section")
    tensor_width = lax.axis_size("tensor")
    replicas = lax.axis_size("dp")
    tok_rows = patches.shape[0]
    feat_local = patches.shape[1]
    layer_count = left_factors.shape[1]
    local_blocks = left_factors.shape[2]
    block_size = left_factors.shape[3]
    all_blocks = local_blocks * tensor_width
    fold_ratio = block_size // all_blocks
    model_width = feat_local * tensor_width
    sixth_rows = tok_rows // 6
    leading = 2 * sixth_rows
    critic_ids = jnp.arange(4, dtype=jnp.int32)
    named_by = (
        (critic_pairs[:, 0:1] == critic_ids[None, :])
        | (critic_pairs[:, 1:2] == critic_ids[None, :])
    ).astype(jnp.int32)
    ranking = jnp.cumsum(named_by, axis=0) - 1
    wide_ids = critic_ids[None, :] < 2
    slot_width = 3 * sixth_rows
    spilled = wide_ids & (ranking >= 3 * sixth_rows)
    destination = jnp.where(spilled, critic_ids[None, :] + 2, critic_ids[None, :])
    slot_index = jnp.where(spilled, ranking - sixth_rows, ranking)
    flat_slot = destination * slot_width + slot_index
    chosen = jnp.take_along_axis(flat_slot, critic_pairs, axis=1)
    slot_total = sections * slot_width
    row_ids = jnp.broadcast_to(jnp.arange(tok_rows, dtype=jnp.int32)[:, None], chosen.shape)
    source_row = (
        jnp.full((slot_total,), tok_rows, jnp.int32).at[chosen.reshape(-1)].set(row_ids.reshape(-1))
    )
    send_patch = (
        patches.at[source_row]
        .get(mode="fill", fill_value=0)
        .reshape(sections, slot_width, local_blocks, block_size)
    )
    send_target = (
        teacher.at[source_row]
        .get(mode="fill", fill_value=0)
        .reshape(sections, slot_width, local_blocks, block_size)
    )
    recv_patch, recv_target = (
        lax.all_to_all(send_patch, "section", split_axis=0, concat_axis=0, tiled=True),
        lax.all_to_all(send_target, "section", split_axis=0, concat_axis=0, tiled=True),
    )
    residuals = [
        recv_patch[:, :leading].reshape(-1, local_blocks, block_size).astype(jnp.float32),
        recv_patch[:, leading:].reshape(-1, local_blocks, block_size).astype(jnp.float32),
    ]
    targets = [
        recv_target[:, :leading].reshape(-1, local_blocks, block_size).astype(jnp.float32),
        recv_target[:, leading:].reshape(-1, local_blocks, block_size).astype(jnp.float32),
    ]
    native = (left_factors[0], right_factors[0], norm_gains[0])
    borrowed = shifted((left_factors, right_factors, norm_gains), "section", 2)
    is_wide = lax.axis_index("section") < 2
    second = (
        jnp.where(is_wide, left_factors, borrowed[0])[0],
        jnp.where(is_wide, right_factors, borrowed[1])[0],
        jnp.where(is_wide, norm_gains, borrowed[2])[0],
    )
    left_sets = (native[0], second[0])
    right_sets = (native[1], second[1])
    gain_sets = (
        native[2].astype(jnp.float32).reshape(layer_count + 1, local_blocks, block_size),
        second[2].astype(jnp.float32).reshape(layer_count + 1, local_blocks, block_size),
    )
    stored = []
    for layer_index in range(layer_count):
        gain_pair = [gain_sets[0][layer_index], gain_sets[1][layer_index]]
        factors, normed = norm_pair(residuals, gain_pair, model_width)
        normed = [normed[member].astype(jnp.bfloat16) for member in range(2)]
        first_out = [
            jnp.einsum(
                "nki,kij->nkj",
                normed[member],
                left_sets[member][layer_index],
                preferred_element_type=jnp.float32,
            ).astype(jnp.bfloat16)
            for member in range(2)
        ]
        permuted = (
            lax.all_to_all(first_out[0], "tensor", split_axis=2, concat_axis=1, tiled=True),
            lax.all_to_all(first_out[1], "tensor", split_axis=2, concat_axis=1, tiled=True),
        )
        permuted = [
            permuted[member].reshape(
                permuted[member].shape[0], all_blocks, local_blocks, fold_ratio
            )
            for member in range(2)
        ]
        right_quads = [
            right_sets[member][layer_index].reshape(
                local_blocks, fold_ratio, all_blocks, block_size
            )
            for member in range(2)
        ]
        mixture = [
            jnp.einsum(
                "nkmp,mpkl->nml",
                permuted[member],
                right_quads[member],
                preferred_element_type=jnp.float32,
            )
            for member in range(2)
        ]
        stored.append((residuals, factors, normed, permuted, mixture, right_quads, gain_pair))
        residuals = [residuals[member] + gelu_value(mixture[member]) for member in range(2)]
    final_gains = [gain_sets[0][layer_count], gain_sets[1][layer_count]]
    factors, outputs = norm_pair(residuals, final_gains, model_width)
    gradients = norm_back_pair(
        residuals,
        factors,
        final_gains,
        [outputs[member] - targets[member] for member in range(2)],
        [jnp.zeros_like(residuals[member]) for member in range(2)],
        model_width,
    )
    left_terms = []
    right_terms = []
    for layer_index in range(layer_count - 1, -1, -1):
        inputs, factors, normed, permuted, mixture, right_quads, gain_pair = stored[layer_index]
        slopes = [
            (gradients[member] * gelu_slope(mixture[member])).astype(jnp.bfloat16)
            for member in range(2)
        ]
        right_grad = [
            jnp.einsum(
                "nkmp,nml->mpkl",
                permuted[member],
                slopes[member],
                preferred_element_type=jnp.float32,
            ).reshape(local_blocks, block_size, block_size)
            for member in range(2)
        ]
        back_moved = [
            jnp.einsum(
                "nml,mpkl->nkmp",
                slopes[member],
                right_quads[member],
                preferred_element_type=jnp.float32,
            )
            .astype(jnp.bfloat16)
            .reshape(slopes[member].shape[0], all_blocks, local_blocks * fold_ratio)
            for member in range(2)
        ]
        arrived = (
            lax.all_to_all(back_moved[0], "tensor", split_axis=1, concat_axis=2, tiled=True),
            lax.all_to_all(back_moved[1], "tensor", split_axis=1, concat_axis=2, tiled=True),
        )
        left_grad = [
            jnp.einsum(
                "nki,nkj->kij", normed[member], arrived[member], preferred_element_type=jnp.float32
            )
            for member in range(2)
        ]
        grad_normed = [
            jnp.einsum(
                "nkj,kij->nki",
                arrived[member],
                left_sets[member][layer_index],
                preferred_element_type=jnp.float32,
            )
            for member in range(2)
        ]
        gradients = norm_back_pair(inputs, factors, gain_pair, grad_normed, gradients, model_width)
        layer_left = jnp.stack(left_grad)
        layer_right = jnp.stack(right_grad)
        layer_left, layer_right = (
            lax.psum(layer_left.astype(jnp.bfloat16), "dp").astype(jnp.float32),
            lax.psum(layer_right.astype(jnp.bfloat16), "dp").astype(jnp.float32),
        )
        left_terms.insert(0, layer_left)
        right_terms.insert(0, layer_right)
    left_stack = jnp.stack(left_terms)
    right_stack = jnp.stack(right_terms)
    repaid = (
        shifted(left_stack[:, 1].astype(jnp.bfloat16), "section", -2).astype(jnp.float32),
        shifted(right_stack[:, 1].astype(jnp.bfloat16), "section", -2).astype(jnp.float32),
    )
    is_wide = lax.axis_index("section") < 2
    left_total = left_stack[:, 0] + jnp.where(is_wide, left_stack[:, 1] + repaid[0], 0.0)
    right_total = right_stack[:, 0] + jnp.where(is_wide, right_stack[:, 1] + repaid[1], 0.0)
    grad_factor = 1.0 / math.sqrt(2 * tok_rows * sections * replicas)
    returned = [
        gradients[member].astype(jnp.bfloat16).reshape(sections, -1, local_blocks, block_size)
        for member in range(2)
    ]
    back_lead, back_trail = (
        lax.all_to_all(returned[0], "section", split_axis=0, concat_axis=0, tiled=True),
        lax.all_to_all(returned[1], "section", split_axis=0, concat_axis=0, tiled=True),
    )
    gathered = jnp.concatenate((back_lead, back_trail), axis=1).reshape(
        slot_total, local_blocks, block_size
    )
    combined = (
        gathered[chosen[:, 0]].astype(jnp.float32) + gathered[chosen[:, 1]].astype(jnp.float32)
    ) * 0.5
    d_patches = combined.astype(jnp.bfloat16).reshape(tok_rows, feat_local)
    return (d_patches, (left_total * grad_factor)[None], (right_total * grad_factor)[None])


VMEM_LIMIT = 60 * 1024 * 1024
CHUNKS = 8
PARTS = 4
SMALL = (16, 128)
AXES = ("section", "tensor", "dp")


def planes_fit(mesh):
    sections = mesh.shape["section"]
    paired = mesh.shape["dp"] == 2 and sections & (sections - 1) == 0
    return paired and mesh.shape["tensor"] == sections


def inner_dot(left, right, left_dim, right_dim):
    return lax.dot_general(
        left,
        right,
        (((left_dim,), (right_dim,)), ((), ())),
        preferred_element_type=jnp.float32,
    )


def fold_rows(values):
    return jnp.sum(values.reshape(values.shape[0] // 8, 8, values.shape[1]), axis=0)


def block_rows(block, size):
    return pl.ds(pl.multiple_of(block * size, size), size)


def column(gain_ref, block, slots):
    blocks = gain_ref.shape[1]
    picked = lax.broadcasted_iota(jnp.int32, (blocks, slots), 0) == block
    return inner_dot(gain_ref[...], picked.astype(jnp.bfloat16), 1, 0)


def chunk_copy(source, target, sems, chunk):
    rows = target.shape[0] // CHUNKS
    at = pl.ds(pl.multiple_of(chunk * rows, rows), rows)
    return pltpu.make_async_copy(source.at[at], target.at[at], sems.at[chunk])


def start_chunks(source, target, sems):
    for chunk in range(CHUNKS):
        chunk_copy(source, target, sems, chunk).start()


def wait_chunks(source, target, sems):
    for chunk in range(CHUNKS):
        chunk_copy(source, target, sems, chunk).wait()


def factor_copies(parts, held, sems, side, outward=False):
    count = parts[0].shape[0]
    copies = []
    for at, ref in enumerate(parts):
        inside = held.at[pl.ds(at * count, count), side]
        ends = (inside, ref.at[:, side]) if outward else (ref.at[:, side], inside)
        copies.append(pltpu.make_async_copy(*ends, sems.at[side, at]))
    return copies


def by_chunk(blocks, step, carry, before=None, after=None):
    per_chunk = blocks // CHUNKS

    def one(chunk, carry):
        if before is not None:
            before(chunk)
        carry = lax.fori_loop(
            0, per_chunk, lambda at, now: step(chunk * per_chunk + at, now), carry, unroll=True
        )
        if after is not None:
            after(chunk)
        return carry

    return lax.fori_loop(0, CHUNKS, one, carry)


def forward_kernel(first, inputs, table_ref, gain_ref, sums_ref, *refs):
    sources, refs = refs[:inputs], refs[inputs:]
    parts, sources = sources[:PARTS], sources[PARTS:]
    out_ref, u_ref, z_ref, slope_ref, scale_ref, next_ref = refs[:6]
    raw, h, w, u, z, slope, mid, in_sems, w_sems, out_sems = refs[6:]
    features, slots = h.shape
    size = w.shape[-1]
    chunk_blocks = w.shape[2]
    blocks = features // size
    fold = size // blocks

    left_in = factor_copies(parts, w, w_sems, 0)
    right_in = factor_copies(parts, w, w_sems, 1)
    if first:
        start_chunks(sources[0], raw, in_sems)
        for copy in left_in + right_in:
            copy.start()

        def squares(block, total):
            rows = block_rows(block, size)
            part = raw[rows, :].astype(jnp.float32)
            h[rows, :] = part
            return total + fold_rows(part * part)

        total = by_chunk(
            blocks,
            squares,
            jnp.zeros((8, slots), jnp.float32),
            lambda chunk: chunk_copy(sources[0], raw, in_sems, chunk).wait(),
        )
    else:
        for copy in left_in:
            copy.start()
        start_chunks(sources[0], h, in_sems)
        for copy in right_in:
            copy.start()
        total = sums_ref[...]
    scale = lax.rsqrt(jnp.sum(total, axis=0, keepdims=True) / features + EPSILON)
    scale_ref[...] = jnp.broadcast_to(scale, scale_ref.shape)
    for copy in left_in:
        copy.wait()

    def arrive(chunk):
        if not first:
            chunk_copy(sources[0], h, in_sems, chunk).wait()

    def left(block, carry):
        rows = block_rows(block, size)
        place = table_ref[0, block]
        normed = (h[rows, :] * scale * column(gain_ref, block, slots)).astype(jnp.bfloat16)
        u[rows, :] = normed
        weight = w[place // chunk_blocks, 0, place % chunk_blocks]
        mid[rows, :] = inner_dot(weight, normed, 0, 0)
        return carry

    def leave_left(chunk):
        chunk_copy(u, u_ref, out_sems.at[0], chunk).start()

    by_chunk(blocks, left, 0, arrive, leave_left)
    for copy in right_in:
        copy.wait()

    def right(block, total):
        rows = block_rows(block, size)
        place = table_ref[0, block]
        moved = [mid[pl.ds(block * fold + q, blocks, stride=size), :] for q in range(fold)]
        moved = jnp.concatenate(moved, axis=0).astype(jnp.bfloat16)
        z[rows, :] = moved
        weight = w[place // chunk_blocks, 1, place % chunk_blocks]
        mixture = inner_dot(weight, moved, 0, 0)
        squared = mixture * mixture
        tangent = jnp.tanh(mixture * (TANH_SLOPE + (TANH_SLOPE * CUBIC_TERM) * squared))
        half = 0.5 + 0.5 * tangent
        following = h[rows, :] + mixture * half
        h[rows, :] = following
        steep = half + mixture * (1.0 - tangent * tangent) * (
            0.5 * TANH_SLOPE + (1.5 * TANH_SLOPE * CUBIC_TERM) * squared
        )
        slope[rows, :] = steep.astype(jnp.bfloat16)
        return total + fold_rows(following * following)

    leaving = ((h, out_ref, 1), (z, z_ref, 2), (slope, slope_ref, 3))

    def leave_right(chunk):
        for source, target, at in leaving:
            chunk_copy(source, target, out_sems.at[at], chunk).start()

    next_ref[...] = by_chunk(blocks, right, jnp.zeros((8, slots), jnp.float32), None, leave_right)
    for source, target, at in ((u, u_ref, 0),) + leaving:
        wait_chunks(source, target, out_sems.at[at])


def backward_kernel(turning, last, inputs, table_ref, gain_ref, end_gain_ref, scale_ref, *refs):
    sources, refs = refs[:inputs], refs[inputs:]
    slope_ref, z_ref, u_ref = sources[:3]
    parts, sources = sources[3 : 3 + PARTS], sources[3 + PARTS :]
    out_ref, own_grad, peer_grad = refs[:3]
    g, slope, z, u, h, w, gw, mid, turned, top, goal = refs[3:14]
    in_sems, w_sems, out_sems, gw_sems = refs[14:]
    features, slots = g.shape
    size = w.shape[-1]
    chunk_blocks = w.shape[2]
    blocks = features // size
    fold = size // blocks

    left_in = factor_copies(parts, w, w_sems, 0)
    right_in = factor_copies(parts, w, w_sems, 1)
    g_ref, h_ref = sources[:2]
    if turning:
        start_chunks(g_ref, top, in_sems.at[0])
        start_chunks(sources[2], goal, in_sems.at[5])
    else:
        start_chunks(g_ref, g, in_sems.at[0])
    for copy in right_in:
        copy.start()
    start_chunks(slope_ref, slope, in_sems.at[1])
    start_chunks(z_ref, z, in_sems.at[2])
    for copy in left_in:
        copy.start()
    start_chunks(u_ref, u, in_sems.at[3])
    start_chunks(h_ref, h, in_sems.at[4])

    if turning:
        zero = jnp.zeros((8, slots), jnp.float32)

        def sums(block, totals):
            rows = block_rows(block, size)
            part = top[rows, :]
            scaled = part * column(end_gain_ref, block, slots)
            return (
                totals[0] + fold_rows(part * part),
                totals[1] + fold_rows(scaled * scaled),
                totals[2] + fold_rows(scaled * goal[rows, :].astype(jnp.float32)),
            )

        def arrive_top(chunk):
            chunk_copy(g_ref, top, in_sems.at[0], chunk).wait()
            chunk_copy(sources[2], goal, in_sems.at[5], chunk).wait()

        totals = by_chunk(blocks, sums, (zero, zero, zero), arrive_top)
        squares, gained, crossed = [jnp.sum(total, axis=0, keepdims=True) for total in totals]
        end_scale = lax.rsqrt(squares / features + EPSILON)
        end_back = end_scale * end_scale * end_scale * (end_scale * gained - crossed) / features

    for copy in right_in:
        copy.wait()

    def arrive_right(chunk):
        if not turning:
            chunk_copy(g_ref, g, in_sems.at[0], chunk).wait()
        chunk_copy(slope_ref, slope, in_sems.at[1], chunk).wait()
        chunk_copy(z_ref, z, in_sems.at[2], chunk).wait()

    def right(block, carry):
        rows = block_rows(block, size)
        place, home = table_ref[0, block], table_ref[1, block]
        at = (place // chunk_blocks, 1, place % chunk_blocks)
        to = (home // chunk_blocks, 1, home % chunk_blocks)
        if turning:
            part = top[rows, :]
            gain = column(end_gain_ref, block, slots)
            error = (part * end_scale * gain - goal[rows, :].astype(jnp.float32)) * gain
            gradient = end_scale * error - part * end_back
            g[rows, :] = gradient
        else:
            gradient = g[rows, :]
        steep = (gradient * slope[rows, :].astype(jnp.float32)).astype(jnp.bfloat16)
        gw[to] = inner_dot(z[rows, :], steep, 1, 1).astype(jnp.bfloat16)
        mid[rows, :] = inner_dot(w[at], steep, 1, 0)
        return carry

    by_chunk(blocks, right, 0, arrive_right)
    right_out = factor_copies((own_grad, peer_grad), gw, gw_sems, 1, outward=True)
    for copy in right_out:
        copy.start()
    for copy in left_in:
        copy.wait()
    scale = scale_ref[0:1, :]

    def arrive_left(chunk):
        chunk_copy(u_ref, u, in_sems.at[3], chunk).wait()
        chunk_copy(h_ref, h, in_sems.at[4], chunk).wait()

    def left(block, total):
        rows = block_rows(block, size)
        place, home = table_ref[0, block], table_ref[1, block]
        at = (place // chunk_blocks, 0, place % chunk_blocks)
        to = (home // chunk_blocks, 0, home % chunk_blocks)
        slot = block % turned.shape[0]
        for q in range(fold):
            turned[slot, pl.ds(q, blocks, stride=fold), :] = mid[
                pl.ds(q * blocks + block, blocks, stride=size), :
            ]
        arrived = turned[slot].astype(jnp.bfloat16)
        gw[to] = inner_dot(u[rows, :], arrived, 1, 1).astype(jnp.bfloat16)
        weighted = inner_dot(w[at], arrived, 1, 0) * column(gain_ref, block, slots)
        g[rows, :] = g[rows, :] + scale * weighted
        return total + fold_rows(weighted * h[rows, :].astype(jnp.float32))

    total = by_chunk(blocks, left, jnp.zeros((8, slots), jnp.float32), arrive_left)
    left_out = factor_copies((own_grad, peer_grad), gw, gw_sems, 0, outward=True)
    for copy in left_out:
        copy.start()
    back = scale * scale * scale * jnp.sum(total, axis=0, keepdims=True) / features

    def finish(block, carry):
        rows = block_rows(block, size)
        ended = g[rows, :] - h[rows, :].astype(jnp.float32) * back
        if last:
            u[rows, :] = ended.astype(jnp.bfloat16)
        else:
            g[rows, :] = ended
        return carry

    ended = u if last else g
    by_chunk(blocks, finish, 0, None, lambda chunk: chunk_copy(ended, out_ref, out_sems, chunk).start())
    wait_chunks(ended, out_ref, out_sems)
    for copy in right_out + left_out:
        copy.wait()


def shape_of(shape, dtype):
    return jax.ShapeDtypeStruct(shape, dtype)


SMEM = pl.BlockSpec(memory_space=pltpu.SMEM)
INSIDE = pl.BlockSpec(memory_space=pltpu.VMEM)
OUTSIDE = pl.BlockSpec(memory_space=pl.ANY)


def run_forward(table, gain, sums, residual, weights):
    first = residual.dtype == jnp.bfloat16
    whole = residual.shape
    sources = (*weights, residual)
    held = (PARTS * weights[0].shape[0],) + weights[0].shape[1:]
    out_shape = (
        shape_of(whole, jnp.float32),
        shape_of(whole, jnp.bfloat16),
        shape_of(whole, jnp.bfloat16),
        shape_of(whole, jnp.bfloat16),
        shape_of((8, whole[1]), jnp.float32),
        shape_of((8, whole[1]), jnp.float32),
    )
    return pl.pallas_call(
        lambda *refs: forward_kernel(first, len(sources), *refs),
        in_specs=[SMEM, INSIDE, INSIDE] + [OUTSIDE] * len(sources),
        out_specs=[OUTSIDE] * 4 + [INSIDE] * 2,
        out_shape=out_shape,
        scratch_shapes=[
            pltpu.VMEM(whole if first else SMALL, jnp.bfloat16),
            pltpu.VMEM(whole, jnp.float32),
            pltpu.VMEM(held, jnp.bfloat16),
            pltpu.VMEM(whole, jnp.bfloat16),
            pltpu.VMEM(whole, jnp.bfloat16),
            pltpu.VMEM(whole, jnp.bfloat16),
            pltpu.VMEM(whole, jnp.float32),
            pltpu.SemaphoreType.DMA((CHUNKS,)),
            pltpu.SemaphoreType.DMA((2, PARTS)),
            pltpu.SemaphoreType.DMA((4, CHUNKS)),
        ],
        compiler_params=pltpu.CompilerParams(vmem_limit_bytes=VMEM_LIMIT),
        cost_estimate=pl.CostEstimate(
            flops=FORWARD_COST, bytes_accessed=20 * whole[0] * whole[1], transcendentals=0
        ),
        name="forward_layer",
    )(table, gain, sums, *sources)


def run_backward(table, gain, end_gain, scale, kept, weights, sources, turning, last):
    whole = kept[0].shape
    sources = (*kept, *weights, *sources)
    held = (PARTS * weights[0].shape[0],) + weights[0].shape[1:]
    half = (held[0] // 2,) + held[1:]
    out_shape = [shape_of(whole, jnp.bfloat16 if last else jnp.float32)] + [shape_of(half, jnp.bfloat16)] * 2
    return pl.pallas_call(
        lambda *refs: backward_kernel(turning, last, len(sources), *refs),
        in_specs=[SMEM] + [INSIDE] * 3 + [OUTSIDE] * len(sources),
        out_specs=[OUTSIDE] * len(out_shape),
        out_shape=out_shape,
        scratch_shapes=[
            pltpu.VMEM(whole, jnp.float32),
            pltpu.VMEM(whole, jnp.bfloat16),
            pltpu.VMEM(whole, jnp.bfloat16),
            pltpu.VMEM(whole, jnp.bfloat16),
            pltpu.VMEM(whole, jnp.bfloat16 if last else jnp.float32),
            pltpu.VMEM(held, jnp.bfloat16),
            pltpu.VMEM(held, jnp.bfloat16),
            pltpu.VMEM(whole, jnp.float32),
            pltpu.VMEM((8, held[-1], whole[1]), jnp.float32),
            pltpu.VMEM(whole if turning else SMALL, jnp.float32),
            pltpu.VMEM(whole if turning else SMALL, jnp.bfloat16),
            pltpu.SemaphoreType.DMA((6, CHUNKS)),
            pltpu.SemaphoreType.DMA((2, PARTS)),
            pltpu.SemaphoreType.DMA((CHUNKS,)),
            pltpu.SemaphoreType.DMA((2, PARTS)),
        ],
        compiler_params=pltpu.CompilerParams(vmem_limit_bytes=VMEM_LIMIT),
        cost_estimate=pl.CostEstimate(
            flops=BACKWARD_COST, bytes_accessed=30 * whole[0] * whole[1], transcendentals=0
        ),
        name="backward_layer",
    )(table, gain, end_gain, scale, *sources)


def copies_kernel(plan, inputs, outputs, *refs):
    sems = refs[-1]
    copies = [
        pltpu.make_async_copy(source, target, sems.at[at])
        for at, (source, target) in enumerate(plan(refs[:inputs], refs[inputs : inputs + outputs]))
    ]
    for copy in copies:
        copy.start()
    for copy in copies:
        copy.wait()


def run_copies(plan, scalars, inputs, out_shape, most, name):
    extra = [] if scalars is None else [scalars]
    size = sum(math.prod(out.shape) for out in out_shape)
    return pl.pallas_call(
        lambda *refs: copies_kernel(plan, len(extra) + len(inputs), len(out_shape), *refs),
        in_specs=[SMEM] * len(extra) + [OUTSIDE] * len(inputs),
        out_specs=[INSIDE] * len(out_shape),
        out_shape=out_shape,
        scratch_shapes=[pltpu.SemaphoreType.DMA((most,))],
        compiler_params=pltpu.CompilerParams(vmem_limit_bytes=VMEM_LIMIT),
        cost_estimate=pl.CostEstimate(flops=0, bytes_accessed=4 * size, transcendentals=0),
        name=name,
    )(*extra, *inputs)


def joined(parts):
    rows = parts[0].shape[0]
    whole = shape_of((rows * len(parts),) + parts[0].shape[1:], parts[0].dtype)

    def plan(sources, targets):
        return [(source, targets[0].at[pl.ds(at * rows, rows)]) for at, source in enumerate(sources)]

    return run_copies(plan, None, parts, [whole], len(parts), "join")[0]


def factor_pieces(place, left, right, gain_rows, groups, chunk):
    width = 4
    size = left.shape[-1]
    shapes = []
    for group in groups:
        rows = len(group) * 2 * chunk * size + (gain_rows.shape[0] if group[0] == 0 else 0)
        shapes += [shape_of((rows, size), jnp.bfloat16)] * width

    def plan(sources, targets):
        place_ref, left_ref, right_ref, gain_ref = sources
        copies = []
        for at, group in enumerate(groups):
            for j in range(width):
                target = targets[at * width + j]
                start = (place_ref[2] * width + (place_ref[0] ^ place_ref[1] ^ j)) * chunk
                row = 0
                for layer in group:
                    for ref in (left_ref, right_ref):
                        for inside in range(chunk):
                            copies.append((ref.at[layer, start + inside], target.at[pl.ds(row, size)]))
                            row += size
                if group[0] == 0:
                    copies.append((gain_ref, target.at[pl.ds(row, gain_rows.shape[0])]))
        return copies

    most = width * (sum(len(group) for group in groups) * 2 * chunk + 1)
    flat = run_copies(plan, place, (left, right, gain_rows), shapes, most, "pieces")
    return [flat[at * width : (at + 1) * width] for at in range(len(groups))]


def choice(pairs, critic, slots):
    rows = pairs.shape[0]
    named = (pairs[:, 0:1] == critic) | (pairs[:, 1:2] == critic)
    named = jnp.broadcast_to(named.astype(jnp.float32), (rows, slots))
    before = lax.broadcasted_iota(jnp.int32, (rows, rows), 1) < lax.broadcasted_iota(jnp.int32, (rows, rows), 0)
    rank = inner_dot(before.astype(jnp.bfloat16), named.astype(jnp.bfloat16), 1, 0)
    at = lax.broadcasted_iota(jnp.int32, (rows, slots), 1).astype(jnp.float32)
    return jnp.where(rank == at, named, 0.0).astype(jnp.bfloat16)


def pick_kernel(pairs_ref, values_ref, out_ref):
    width, features, slots = out_ref.shape
    pairs = pairs_ref[...]
    chosen = [choice(pairs, critic, slots) for critic in range(width)]
    step = 512
    for start in range(0, features, step):
        part = values_ref[:, pl.ds(start, step)]
        for k in range(width):
            out_ref[k, pl.ds(start, step), :] = inner_dot(part, chosen[k], 0, 0).astype(jnp.bfloat16)


def run_pick(pairs, values, width, slots):
    rows, features = values.shape
    return pl.pallas_call(
        pick_kernel,
        in_specs=[INSIDE] * 2,
        out_specs=INSIDE,
        out_shape=shape_of((width, features, slots), jnp.bfloat16),
        compiler_params=pltpu.CompilerParams(vmem_limit_bytes=VMEM_LIMIT),
        cost_estimate=pl.CostEstimate(
            flops=2 * rows * features * slots * width, bytes_accessed=8 * rows * features, transcendentals=0
        ),
        name="pick",
    )(pairs, values)


def combine_kernel(pairs_ref, came_ref, out_ref):
    width, features, slots = came_ref.shape
    pairs = pairs_ref[...]
    chosen = [choice(pairs, critic, slots) for critic in range(width)]
    step = 512
    for start in range(0, features, step):
        total = sum(inner_dot(chosen[k], came_ref[k, pl.ds(start, step), :], 1, 1) for k in range(width))
        out_ref[:, pl.ds(start, step)] = (0.5 * total).astype(jnp.bfloat16)


def run_combine(pairs, came):
    rows = pairs.shape[0]
    return pl.pallas_call(
        combine_kernel,
        in_specs=[INSIDE] * 2,
        out_specs=INSIDE,
        out_shape=shape_of((rows, came.shape[1]), jnp.bfloat16),
        compiler_params=pltpu.CompilerParams(vmem_limit_bytes=VMEM_LIMIT),
        cost_estimate=pl.CostEstimate(
            flops=2 * rows * came.size, bytes_accessed=4 * came.size, transcendentals=0
        ),
        name="combine",
    )(pairs, came)


FORWARD_COST = 15_000_000_000
BACKWARD_COST = 18_000_000_000


def assemble_kernel(layer_count, factor, place_ref, *refs):
    sources, (left_ref, right_ref) = refs[: 2 * layer_count], refs[2 * layer_count : 2 * layer_count + 2]
    held, wide, in_sems, out_sems = refs[2 * layer_count + 2 :]
    width, chunk = held.shape[1], held.shape[3]
    origin, core = place_ref[0] ^ place_ref[1], place_ref[2]
    arrivals = [
        pltpu.make_async_copy(source, held.at[at], in_sems.at[at]) for at, source in enumerate(sources)
    ]
    for copy in arrivals:
        copy.start()
    leaving = []
    for at in range(2 * layer_count):
        arrivals[at].wait()
        layer, side = at // 2, at % 2
        half = core if side == 0 else 1 - core
        wide[at] = held[at].astype(jnp.float32) * factor
        for k in range(width):
            start = (half * width + (origin ^ k)) * chunk
            for which, target in enumerate((left_ref, right_ref)):
                copy = pltpu.make_async_copy(
                    wide.at[at, k, which],
                    target.at[layer, pl.ds(start, chunk)],
                    out_sems.at[(at * width + k) * 2 + which],
                )
                copy.start()
                leaving.append(copy)
    for copy in leaving:
        copy.wait()


def run_assemble(places, pieces, layer_count, factor):
    piece = pieces[0].shape
    blocks = 2 * piece[0] * piece[2]
    out = shape_of((layer_count, blocks) + piece[3:], jnp.float32)
    return pl.pallas_call(
        lambda *refs: assemble_kernel(layer_count, factor, *refs),
        in_specs=[SMEM] + [OUTSIDE] * len(pieces),
        out_specs=[OUTSIDE] * 2,
        out_shape=[out] * 2,
        scratch_shapes=[
            pltpu.VMEM((2 * layer_count,) + piece, jnp.bfloat16),
            pltpu.VMEM((2 * layer_count,) + piece, jnp.float32),
            pltpu.SemaphoreType.DMA((2 * layer_count,)),
            pltpu.SemaphoreType.DMA((4 * layer_count * piece[0],)),
        ],
        compiler_params=pltpu.CompilerParams(vmem_limit_bytes=VMEM_LIMIT),
        cost_estimate=pl.CostEstimate(
            flops=0, bytes_accessed=12 * layer_count * math.prod(piece), transcendentals=0
        ),
        name="assemble",
    )(places, *pieces)


def plane_routes(width, replicas):
    bits = width.bit_length() - 1
    orders = [[(step + d) % bits for step in range(bits)] for d in range(replicas)]
    every = [(s, t, d) for s in range(width) for t in range(width) for d in range(replicas)]

    def route(move):
        def index(s, t, d):
            return (s * width + t) * replicas + d

        return [(index(*place), index(*move(*place))) for place in every]

    ranks = [[0] * width for _ in range(replicas)]
    for d in range(replicas):
        for r in range(width):
            ranks[d][sum(((r >> at) & 1) << orders[d][at] for at in range(bits))] = r
    return {
        "spread": [route(lambda s, t, d, j=j: (s ^ t ^ j, t, d)) for j in range(width)],
        "lift": [route(lambda s, t, d, j=j: (s, t ^ s ^ j, d)) for j in range(width)],
        "across": [route(lambda s, t, d, at=at: (s ^ (1 << orders[d][at]), t, d)) for at in range(bits)],
        "cores": route(lambda s, t, d: (s, t, 1 - d)),
        "sections": [route(lambda s, t, d, k=k: (s ^ k, t, d)) for k in range(width)],
        "planes": [route(lambda s, t, d, k=k: (s, t ^ k, d)) for k in range(width)],
        "homes": [route(lambda s, t, d, j=j: (t, t ^ s ^ j, d)) for j in range(width)],
    }, ranks


def added(*parts):
    return sum(part.astype(jnp.float32) for part in parts).astype(jnp.bfloat16)


def plane_shards(patches, teacher, critic_pairs, left_factors, right_factors, norm_gains):
    width = lax.axis_size("section")
    replicas = lax.axis_size("dp")
    tok_rows, feat_local = patches.shape
    layer_count, local_blocks, size = left_factors.shape[1:4]
    blocks = feat_local * width // size
    wide = 2 * tok_rows // 3
    chunk = local_blocks // (replicas * width)
    layer_rows = 2 * chunk * size
    routes, ranks = plane_routes(width, replicas)
    section = lax.axis_index("section")
    tensor = lax.axis_index("tensor")
    core = lax.axis_index("dp")
    place = jnp.stack([section, tensor, core]).astype(jnp.int32)
    tie = lax.optimization_barrier

    def move(value, route):
        return lax.ppermute(value, AXES, route)

    def move_all(values, name):
        return [move(value, route) for value, route in zip(values, routes[name])]

    def send(values, name):
        return [values[0]] + [move(values[k], routes[name][k]) for k in range(1, width)]

    def gather_one(mine):
        return joined([mine, move(mine, routes["across"][0])])

    def gather_two(pair):
        return pair, move(pair, routes["across"][1]), move(pair, routes["cores"])

    def gather_three(pair, other, peer):
        return [pair, other, peer, move(other, routes["cores"])]

    def as_weights(parts):
        return [part.reshape(-1, 2, chunk, size, size) for part in parts]

    block = jnp.arange(blocks, dtype=jnp.int32)
    inside = block % local_blocks
    replica = inside // (width * chunk)
    part = (replica != core).astype(jnp.int32)
    distance = section ^ ((inside // chunk) % width)
    piece = tensor ^ (section ^ distance) ^ (block // local_blocks)
    rank = jnp.array(ranks, jnp.int32)[replica, distance]
    table = jnp.stack(
        [
            ((part * width + rank) * width + piece) * chunk + inside % chunk,
            ((part * width + distance) * width + piece) * chunk + inside % chunk,
        ]
    ).astype(jnp.int32)

    def to_planes(value):
        return lax.all_to_all(value, "tensor", split_axis=0, concat_axis=0, tiled=True)

    patch_sent = run_pick(critic_pairs, patches, width, wide)
    factors = (left_factors[0], right_factors[0])
    groups = [tuple(range(0, 2)), tuple(range(2, layer_count))]
    gain_rows = norm_gains[0].reshape(-1, size)
    pieces = factor_pieces(place, *factors, gain_rows, groups, chunk)

    patch_came = to_planes(patch_sent).reshape(-1, wide)
    near = [move_all(pieces[0], "spread")]
    near[0], pieces[1] = tie((near[0], pieces[1]))
    front = move_all(near[0], "lift")
    near.append(move_all(pieces[1], "spread"))

    def lowest_of(values, at):
        at = at * layer_rows
        return joined([value[at : at + layer_rows].reshape(1, layer_rows, size) for value in values])

    gains = jnp.stack([value[2 * layer_rows :] for value in front])[jnp.arange(width) ^ section ^ tensor]
    gains = gains.reshape(width, layer_count + 1, local_blocks, size).transpose(1, 3, 0, 2)
    gains = gains.reshape(layer_count + 1, size, blocks)
    lowest = [lowest_of(front, 0), lowest_of(front, 1)]
    pairs = [gather_one(lowest[0]), gather_one(lowest[1])] + [None] * (layer_count - 2)
    weights = [as_weights(gather_three(*gather_two(pairs[0])))]
    patch_came, near[1] = tie((patch_came, near[1]))
    later = move_all(near[1], "lift")
    pairs[1], later, teacher = tie((pairs[1], later, teacher))
    for layer in range(2, layer_count):
        lowest.append(lowest_of(later, layer - 2))
    target_sent = run_pick(critic_pairs, teacher, width, wide)

    residual = patch_came
    sums = jnp.zeros((8, wide), jnp.float32)
    flying = {1: gather_two(pairs[1])}
    if layer_count > 2:
        pairs[2] = gather_one(lowest[2])
    residual, flying, pairs, target_sent = tie((residual, flying, pairs, target_sent))
    stored = []
    for layer in range(layer_count):
        ahead = {}
        if layer + 1 < layer_count:
            ahead["weights"] = gather_three(*flying.pop(layer + 1))
        if layer + 2 < layer_count:
            ahead["two"] = gather_two(pairs[layer + 2])
        if layer + 3 < layer_count:
            ahead["one"] = (lowest[layer + 3], move(lowest[layer + 3], routes["across"][0]))
        following, u, z, slope, scale, sums = run_forward(
            table, gains[layer], sums, residual, weights[layer]
        )
        stored.append(((slope, z, u), scale, residual))
        following, ahead = tie((following, ahead))
        residual = following
        if layer + 1 < layer_count:
            weights.append(as_weights(ahead["weights"]))
        if layer + 2 < layer_count:
            flying[layer + 2] = ahead["two"]
        if layer + 3 < layer_count:
            pairs[layer + 3] = joined(list(ahead["one"]))
        if layer == 0:
            target_sent, sums = tie((target_sent, sums))
            target = to_planes(target_sent).reshape(-1, wide)

    def core_sum(mine, other):
        return (mine, move(other, routes["cores"]))

    def plane_sum(value):
        value = value.reshape(width, width, layer_rows, size)
        return send([value[k] for k in range(width)], "sections")

    def homeward(value):
        return move_all([value[j] for j in range(width)], "homes")

    def both_halves(parts):
        whole = joined([part.reshape(1, layer_rows, size) for part in parts])
        return whole, move(whole, routes["cores"])

    steps = (
        lambda state: core_sum(*state),
        lambda state: plane_sum(added(*state)),
        lambda state: homeward(added(*state)),
        both_halves,
    )
    gradient = residual
    underway = []
    for layer in range(layer_count - 1, -1, -1):
        turning = layer == layer_count - 1
        last = layer == 0
        kept, scale, inputs = stored[layer]
        sources = (gradient, inputs, target) if turning else (gradient, inputs)
        underway = [(at + 1, steps[at](state)) for at, state in underway]
        gradient, mine, other = run_backward(
            table, gains[layer], gains[layer_count], scale, kept, weights[layer], sources, turning, last
        )
        gradient, mine, other, states = tie((gradient, mine, other, [state for _, state in underway]))
        underway = [(at, state) for (at, _), state in zip(underway, states)]
        underway.append((0, (mine, other)))

    returned = to_planes(gradient.reshape(width, feat_local, wide))
    homes_of = []
    for at, state in underway:
        for step in steps[at:]:
            state = step(state)
        homes_of.append(state)
    d_patches = run_combine(critic_pairs, returned)
    grad_factor = 1.0 / math.sqrt(2 * tok_rows * width * replicas)
    parts = [part.reshape(width, 2, chunk, size, size) for pair in homes_of[::-1] for part in pair]
    grad_left, grad_right = run_assemble(place, parts, layer_count, grad_factor)
    return (d_patches, grad_left[None], grad_right[None])


def solution(mesh):
    in_specs = (
        P(("section", "dp"), "tensor"),
        P(("section", "dp"), "tensor"),
        P(("section", "dp"), None),
        P("section", None, "tensor", None, None),
        P("section", None, "tensor", None, None),
        P("section", None, "tensor"),
    )
    out_specs = (
        P(("section", "dp"), "tensor"),
        P("section", None, "tensor", None, None),
        P("section", None, "tensor", None, None),
    )
    body = plane_shards if planes_fit(mesh) else layered_shards
    return jax.shard_map(
        body, mesh=mesh, in_specs=in_specs, out_specs=out_specs, check_vma=False)
```

```python
import math

import jax
import jax.numpy as jnp
from jax import lax
from jax.experimental import pallas as pl
from jax.experimental.pallas import tpu as pltpu
from jax.sharding import PartitionSpec as P

EPSILON = 1e-06
TANH_SLOPE = 0.7978845608028654
CUBIC_TERM = 0.044715


def shifted(value, axis, steps):
    count = lax.axis_size(axis)
    first, last = (max(0, -steps), min(count, count - steps))
    return lax.ppermute(value, axis, [(source, source + steps) for source in range(first, last)])


def gelu_value(values):
    tangent = jnp.tanh(TANH_SLOPE * (values + CUBIC_TERM * values * values * values))
    return 0.5 * values * (1.0 + tangent)


def gelu_slope(values):
    tangent = jnp.tanh(TANH_SLOPE * (values + CUBIC_TERM * values * values * values))
    return 0.5 * (1.0 + tangent) + 0.5 * values * (1.0 - tangent * tangent) * TANH_SLOPE * (
        1.0 + 3.0 * CUBIC_TERM * values * values
    )


def norm_pair(residuals, gain_pair, model_width):
    squares = lax.psum(
        (
            jnp.sum(residuals[0] * residuals[0], axis=(1, 2)),
            jnp.sum(residuals[1] * residuals[1], axis=(1, 2)),
        ),
        "tensor",
    )
    factors = [lax.rsqrt(squares[member] / model_width + EPSILON) for member in range(2)]
    normed = [
        residuals[member] * factors[member][:, None, None] * gain_pair[member][None]
        for member in range(2)
    ]
    return (factors, normed)


def norm_back_pair(residuals, factors, gain_pair, grad_normed, carried, model_width):
    weighted = [grad_normed[member] * gain_pair[member][None] for member in range(2)]
    inners = lax.psum(
        (
            jnp.sum(weighted[0] * residuals[0], axis=(1, 2)),
            jnp.sum(weighted[1] * residuals[1], axis=(1, 2)),
        ),
        "tensor",
    )
    return [
        carried[member]
        + factors[member][:, None, None] * weighted[member]
        - residuals[member] * (factors[member] ** 3 * inners[member] / model_width)[:, None, None]
        for member in range(2)
    ]


def layered_shards(patches, teacher, critic_pairs, left_factors, right_factors, norm_gains):
    sections = lax.axis_size("section")
    tensor_width = lax.axis_size("tensor")
    replicas = lax.axis_size("dp")
    tok_rows = patches.shape[0]
    feat_local = patches.shape[1]
    layer_count = left_factors.shape[1]
    local_blocks = left_factors.shape[2]
    block_size = left_factors.shape[3]
    all_blocks = local_blocks * tensor_width
    fold_ratio = block_size // all_blocks
    model_width = feat_local * tensor_width
    sixth_rows = tok_rows // 6
    leading = 2 * sixth_rows
    critic_ids = jnp.arange(4, dtype=jnp.int32)
    named_by = (
        (critic_pairs[:, 0:1] == critic_ids[None, :])
        | (critic_pairs[:, 1:2] == critic_ids[None, :])
    ).astype(jnp.int32)
    ranking = jnp.cumsum(named_by, axis=0) - 1
    wide_ids = critic_ids[None, :] < 2
    slot_width = 3 * sixth_rows
    spilled = wide_ids & (ranking >= 3 * sixth_rows)
    destination = jnp.where(spilled, critic_ids[None, :] + 2, critic_ids[None, :])
    slot_index = jnp.where(spilled, ranking - sixth_rows, ranking)
    flat_slot = destination * slot_width + slot_index
    chosen = jnp.take_along_axis(flat_slot, critic_pairs, axis=1)
    slot_total = sections * slot_width
    row_ids = jnp.broadcast_to(jnp.arange(tok_rows, dtype=jnp.int32)[:, None], chosen.shape)
    source_row = (
        jnp.full((slot_total,), tok_rows, jnp.int32).at[chosen.reshape(-1)].set(row_ids.reshape(-1))
    )
    send_patch = (
        patches.at[source_row]
        .get(mode="fill", fill_value=0)
        .reshape(sections, slot_width, local_blocks, block_size)
    )
    send_target = (
        teacher.at[source_row]
        .get(mode="fill", fill_value=0)
        .reshape(sections, slot_width, local_blocks, block_size)
    )
    recv_patch, recv_target = (
        lax.all_to_all(send_patch, "section", split_axis=0, concat_axis=0, tiled=True),
        lax.all_to_all(send_target, "section", split_axis=0, concat_axis=0, tiled=True),
    )
    residuals = [
        recv_patch[:, :leading].reshape(-1, local_blocks, block_size).astype(jnp.float32),
        recv_patch[:, leading:].reshape(-1, local_blocks, block_size).astype(jnp.float32),
    ]
    targets = [
        recv_target[:, :leading].reshape(-1, local_blocks, block_size).astype(jnp.float32),
        recv_target[:, leading:].reshape(-1, local_blocks, block_size).astype(jnp.float32),
    ]
    native = (left_factors[0], right_factors[0], norm_gains[0])
    borrowed = shifted((left_factors, right_factors, norm_gains), "section", 2)
    is_wide = lax.axis_index("section") < 2
    second = (
        jnp.where(is_wide, left_factors, borrowed[0])[0],
        jnp.where(is_wide, right_factors, borrowed[1])[0],
        jnp.where(is_wide, norm_gains, borrowed[2])[0],
    )
    left_sets = (native[0], second[0])
    right_sets = (native[1], second[1])
    gain_sets = (
        native[2].astype(jnp.float32).reshape(layer_count + 1, local_blocks, block_size),
        second[2].astype(jnp.float32).reshape(layer_count + 1, local_blocks, block_size),
    )
    stored = []
    for layer_index in range(layer_count):
        gain_pair = [gain_sets[0][layer_index], gain_sets[1][layer_index]]
        factors, normed = norm_pair(residuals, gain_pair, model_width)
        normed = [normed[member].astype(jnp.bfloat16) for member in range(2)]
        first_out = [
            jnp.einsum(
                "nki,kij->nkj",
                normed[member],
                left_sets[member][layer_index],
                preferred_element_type=jnp.float32,
            ).astype(jnp.bfloat16)
            for member in range(2)
        ]
        permuted = (
            lax.all_to_all(first_out[0], "tensor", split_axis=2, concat_axis=1, tiled=True),
            lax.all_to_all(first_out[1], "tensor", split_axis=2, concat_axis=1, tiled=True),
        )
        permuted = [
            permuted[member].reshape(
                permuted[member].shape[0], all_blocks, local_blocks, fold_ratio
            )
            for member in range(2)
        ]
        right_quads = [
            right_sets[member][layer_index].reshape(
                local_blocks, fold_ratio, all_blocks, block_size
            )
            for member in range(2)
        ]
        mixture = [
            jnp.einsum(
                "nkmp,mpkl->nml",
                permuted[member],
                right_quads[member],
                preferred_element_type=jnp.float32,
            )
            for member in range(2)
        ]
        stored.append((residuals, factors, normed, permuted, mixture, right_quads, gain_pair))
        residuals = [residuals[member] + gelu_value(mixture[member]) for member in range(2)]
    final_gains = [gain_sets[0][layer_count], gain_sets[1][layer_count]]
    factors, outputs = norm_pair(residuals, final_gains, model_width)
    gradients = norm_back_pair(
        residuals,
        factors,
        final_gains,
        [outputs[member] - targets[member] for member in range(2)],
        [jnp.zeros_like(residuals[member]) for member in range(2)],
        model_width,
    )
    left_terms = []
    right_terms = []
    for layer_index in range(layer_count - 1, -1, -1):
        inputs, factors, normed, permuted, mixture, right_quads, gain_pair = stored[layer_index]
        slopes = [
            (gradients[member] * gelu_slope(mixture[member])).astype(jnp.bfloat16)
            for member in range(2)
        ]
        right_grad = [
            jnp.einsum(
                "nkmp,nml->mpkl",
                permuted[member],
                slopes[member],
                preferred_element_type=jnp.float32,
            ).reshape(local_blocks, block_size, block_size)
            for member in range(2)
        ]
        back_moved = [
            jnp.einsum(
                "nml,mpkl->nkmp",
                slopes[member],
                right_quads[member],
                preferred_element_type=jnp.float32,
            )
            .astype(jnp.bfloat16)
            .reshape(slopes[member].shape[0], all_blocks, local_blocks * fold_ratio)
            for member in range(2)
        ]
        arrived = (
            lax.all_to_all(back_moved[0], "tensor", split_axis=1, concat_axis=2, tiled=True),
            lax.all_to_all(back_moved[1], "tensor", split_axis=1, concat_axis=2, tiled=True),
        )
        left_grad = [
            jnp.einsum(
                "nki,nkj->kij", normed[member], arrived[member], preferred_element_type=jnp.float32
            )
            for member in range(2)
        ]
        grad_normed = [
            jnp.einsum(
                "nkj,kij->nki",
                arrived[member],
                left_sets[member][layer_index],
                preferred_element_type=jnp.float32,
            )
            for member in range(2)
        ]
        gradients = norm_back_pair(inputs, factors, gain_pair, grad_normed, gradients, model_width)
        layer_left = jnp.stack(left_grad)
        layer_right = jnp.stack(right_grad)
        layer_left, layer_right = (
            lax.psum(layer_left.astype(jnp.bfloat16), "dp").astype(jnp.float32),
            lax.psum(layer_right.astype(jnp.bfloat16), "dp").astype(jnp.float32),
        )
        left_terms.insert(0, layer_left)
        right_terms.insert(0, layer_right)
    left_stack = jnp.stack(left_terms)
    right_stack = jnp.stack(right_terms)
    repaid = (
        shifted(left_stack[:, 1].astype(jnp.bfloat16), "section", -2).astype(jnp.float32),
        shifted(right_stack[:, 1].astype(jnp.bfloat16), "section", -2).astype(jnp.float32),
    )
    is_wide = lax.axis_index("section") < 2
    left_total = left_stack[:, 0] + jnp.where(is_wide, left_stack[:, 1] + repaid[0], 0.0)
    right_total = right_stack[:, 0] + jnp.where(is_wide, right_stack[:, 1] + repaid[1], 0.0)
    grad_factor = 1.0 / math.sqrt(2 * tok_rows * sections * replicas)
    returned = [
        gradients[member].astype(jnp.bfloat16).reshape(sections, -1, local_blocks, block_size)
        for member in range(2)
    ]
    back_lead, back_trail = (
        lax.all_to_all(returned[0], "section", split_axis=0, concat_axis=0, tiled=True),
        lax.all_to_all(returned[1], "section", split_axis=0, concat_axis=0, tiled=True),
    )
    gathered = jnp.concatenate((back_lead, back_trail), axis=1).reshape(
        slot_total, local_blocks, block_size
    )
    combined = (
        gathered[chosen[:, 0]].astype(jnp.float32) + gathered[chosen[:, 1]].astype(jnp.float32)
    ) * 0.5
    d_patches = combined.astype(jnp.bfloat16).reshape(tok_rows, feat_local)
    return (d_patches, (left_total * grad_factor)[None], (right_total * grad_factor)[None])


VMEM_LIMIT = 60 * 1024 * 1024
CHUNKS = 8
PARTS = 4
SMALL = (16, 128)
AXES = ("section", "tensor", "dp")


def planes_fit(mesh):
    sections = mesh.shape["section"]
    paired = mesh.shape["dp"] == 2 and sections & (sections - 1) == 0
    return paired and mesh.shape["tensor"] == sections


def inner_dot(left, right, left_dim, right_dim):
    return lax.dot_general(
        left,
        right,
        (((left_dim,), (right_dim,)), ((), ())),
        preferred_element_type=jnp.float32,
    )


def fold_rows(values):
    return jnp.sum(values.reshape(values.shape[0] // 8, 8, values.shape[1]), axis=0)


def block_rows(block, size):
    return pl.ds(pl.multiple_of(block * size, size), size)


def column(gain_ref, block, slots):
    blocks = gain_ref.shape[1]
    picked = lax.broadcasted_iota(jnp.int32, (blocks, slots), 0) == block
    return inner_dot(gain_ref[...], picked.astype(jnp.bfloat16), 1, 0)


def chunk_copy(source, target, sems, chunk):
    rows = target.shape[0] // CHUNKS
    at = pl.ds(pl.multiple_of(chunk * rows, rows), rows)
    return pltpu.make_async_copy(source.at[at], target.at[at], sems.at[chunk])


def start_chunks(source, target, sems):
    for chunk in range(CHUNKS):
        chunk_copy(source, target, sems, chunk).start()


def wait_chunks(source, target, sems):
    for chunk in range(CHUNKS):
        chunk_copy(source, target, sems, chunk).wait()


def factor_copies(parts, layer, held, sems, side):
    count = parts[0].shape[0]
    return [
        pltpu.make_async_copy(
            ref.at[:, layer, side], held.at[pl.ds(at * count, count), side], sems.at[side, at]
        )
        for at, ref in enumerate(parts)
    ]


def gradient_copies(held, parts, sems, side):
    count = parts[0].shape[0]
    return [
        pltpu.make_async_copy(
            held.at[pl.ds(at * count, count), side], ref.at[:, side], sems.at[side, at]
        )
        for at, ref in enumerate(parts)
    ]


def by_chunk(blocks, step, carry, before=None, after=None):
    per_chunk = blocks // CHUNKS

    def one(chunk, carry):
        if before is not None:
            before(chunk)
        carry = lax.fori_loop(
            0, per_chunk, lambda at, now: step(chunk * per_chunk + at, now), carry, unroll=True
        )
        if after is not None:
            after(chunk)
        return carry

    return lax.fori_loop(0, CHUNKS, one, carry)


def forward_kernel(first, layer, inputs, table_ref, gain_ref, sums_ref, *refs):
    sources, refs = refs[:inputs], refs[inputs:]
    parts, sources = sources[:PARTS], sources[PARTS:]
    out_ref, u_ref, z_ref, slope_ref, scale_ref, next_ref = refs[:6]
    raw, h, w, u, z, slope, mid, in_sems, w_sems, out_sems = refs[6:]
    features, slots = h.shape
    size = w.shape[-1]
    chunk_blocks = w.shape[2]
    blocks = features // size
    fold = size // blocks

    left_in = factor_copies(parts, layer, w, w_sems, 0)
    right_in = factor_copies(parts, layer, w, w_sems, 1)
    if first:
        start_chunks(sources[0], raw, in_sems)
        for copy in left_in + right_in:
            copy.start()

        def squares(block, total):
            rows = block_rows(block, size)
            part = raw[rows, :].astype(jnp.float32)
            h[rows, :] = part
            return total + fold_rows(part * part)

        total = by_chunk(
            blocks,
            squares,
            jnp.zeros((8, slots), jnp.float32),
            lambda chunk: chunk_copy(sources[0], raw, in_sems, chunk).wait(),
        )
    else:
        for copy in left_in:
            copy.start()
        start_chunks(sources[0], h, in_sems)
        for copy in right_in:
            copy.start()
        total = sums_ref[...]
    scale = lax.rsqrt(jnp.sum(total, axis=0, keepdims=True) / features + EPSILON)
    scale_ref[...] = jnp.broadcast_to(scale, scale_ref.shape)
    for copy in left_in:
        copy.wait()

    def arrive(chunk):
        if not first:
            chunk_copy(sources[0], h, in_sems, chunk).wait()

    def left(block, carry):
        rows = block_rows(block, size)
        place = table_ref[0, block]
        normed = (h[rows, :] * scale * column(gain_ref, block, slots)).astype(jnp.bfloat16)
        u[rows, :] = normed
        weight = w[place // chunk_blocks, 0, place % chunk_blocks]
        mid[rows, :] = inner_dot(weight, normed, 0, 0)
        return carry

    def leave_left(chunk):
        chunk_copy(u, u_ref, out_sems.at[0], chunk).start()

    by_chunk(blocks, left, 0, arrive, leave_left)
    for copy in right_in:
        copy.wait()

    def right(block, total):
        rows = block_rows(block, size)
        place = table_ref[0, block]
        moved = [mid[pl.ds(block * fold + q, blocks, stride=size), :] for q in range(fold)]
        moved = jnp.concatenate(moved, axis=0).astype(jnp.bfloat16)
        z[rows, :] = moved
        weight = w[place // chunk_blocks, 1, place % chunk_blocks]
        mixture = inner_dot(weight, moved, 0, 0)
        squared = mixture * mixture
        tangent = jnp.tanh(mixture * (TANH_SLOPE + (TANH_SLOPE * CUBIC_TERM) * squared))
        half = 0.5 + 0.5 * tangent
        following = h[rows, :] + mixture * half
        h[rows, :] = following
        steep = half + mixture * (1.0 - tangent * tangent) * (
            0.5 * TANH_SLOPE + (1.5 * TANH_SLOPE * CUBIC_TERM) * squared
        )
        slope[rows, :] = steep.astype(jnp.bfloat16)
        return total + fold_rows(following * following)

    leaving = ((h, out_ref, 1), (z, z_ref, 2), (slope, slope_ref, 3))

    def leave_right(chunk):
        for source, target, at in leaving:
            chunk_copy(source, target, out_sems.at[at], chunk).start()

    next_ref[...] = by_chunk(blocks, right, jnp.zeros((8, slots), jnp.float32), None, leave_right)
    for source, target, at in ((u, u_ref, 0),) + leaving:
        wait_chunks(source, target, out_sems.at[at])


def backward_kernel(turning, last, layer, inputs, table_ref, gain_ref, end_gain_ref, scale_ref, *refs):
    sources, refs = refs[:inputs], refs[inputs:]
    slope_ref, z_ref, u_ref = sources[:3]
    parts, sources = sources[3 : 3 + PARTS], sources[3 + PARTS :]
    out_ref, own_grad, peer_grad = refs[:3]
    g, slope, z, u, h, w, gw, mid, turned, top, goal = refs[3:14]
    in_sems, w_sems, out_sems, gw_sems = refs[14:]
    features, slots = g.shape
    size = w.shape[-1]
    chunk_blocks = w.shape[2]
    blocks = features // size
    fold = size // blocks

    left_in = factor_copies(parts, layer, w, w_sems, 0)
    right_in = factor_copies(parts, layer, w, w_sems, 1)
    g_ref, h_ref = sources[:2]
    if turning:
        start_chunks(g_ref, top, in_sems.at[0])
        start_chunks(sources[2], goal, in_sems.at[5])
    else:
        start_chunks(g_ref, g, in_sems.at[0])
    for copy in right_in:
        copy.start()
    start_chunks(slope_ref, slope, in_sems.at[1])
    start_chunks(z_ref, z, in_sems.at[2])
    for copy in left_in:
        copy.start()
    start_chunks(u_ref, u, in_sems.at[3])
    start_chunks(h_ref, h, in_sems.at[4])

    if turning:
        zero = jnp.zeros((8, slots), jnp.float32)

        def sums(block, totals):
            rows = block_rows(block, size)
            part = top[rows, :]
            scaled = part * column(end_gain_ref, block, slots)
            return (
                totals[0] + fold_rows(part * part),
                totals[1] + fold_rows(scaled * scaled),
                totals[2] + fold_rows(scaled * goal[rows, :].astype(jnp.float32)),
            )

        def arrive_top(chunk):
            chunk_copy(g_ref, top, in_sems.at[0], chunk).wait()
            chunk_copy(sources[2], goal, in_sems.at[5], chunk).wait()

        totals = by_chunk(blocks, sums, (zero, zero, zero), arrive_top)
        squares, gained, crossed = [jnp.sum(total, axis=0, keepdims=True) for total in totals]
        end_scale = lax.rsqrt(squares / features + EPSILON)
        end_back = end_scale * end_scale * end_scale * (end_scale * gained - crossed) / features

    for copy in right_in:
        copy.wait()

    def arrive_right(chunk):
        if not turning:
            chunk_copy(g_ref, g, in_sems.at[0], chunk).wait()
        chunk_copy(slope_ref, slope, in_sems.at[1], chunk).wait()
        chunk_copy(z_ref, z, in_sems.at[2], chunk).wait()

    def right(block, carry):
        rows = block_rows(block, size)
        place, home = table_ref[0, block], table_ref[1, block]
        at = (place // chunk_blocks, 1, place % chunk_blocks)
        to = (home // chunk_blocks, 1, home % chunk_blocks)
        if turning:
            part = top[rows, :]
            gain = column(end_gain_ref, block, slots)
            error = (part * end_scale * gain - goal[rows, :].astype(jnp.float32)) * gain
            gradient = end_scale * error - part * end_back
            g[rows, :] = gradient
        else:
            gradient = g[rows, :]
        steep = (gradient * slope[rows, :].astype(jnp.float32)).astype(jnp.bfloat16)
        gw[to] = inner_dot(z[rows, :], steep, 1, 1).astype(jnp.bfloat16)
        mid[rows, :] = inner_dot(w[at], steep, 1, 0)
        return carry

    by_chunk(blocks, right, 0, arrive_right)
    right_out = gradient_copies(gw, (own_grad, peer_grad), gw_sems, 1)
    for copy in right_out:
        copy.start()
    for copy in left_in:
        copy.wait()
    scale = scale_ref[0:1, :]

    def arrive_left(chunk):
        chunk_copy(u_ref, u, in_sems.at[3], chunk).wait()
        chunk_copy(h_ref, h, in_sems.at[4], chunk).wait()

    def left(block, total):
        rows = block_rows(block, size)
        place, home = table_ref[0, block], table_ref[1, block]
        at = (place // chunk_blocks, 0, place % chunk_blocks)
        to = (home // chunk_blocks, 0, home % chunk_blocks)
        slot = block % turned.shape[0]
        for q in range(fold):
            turned[slot, pl.ds(q, blocks, stride=fold), :] = mid[
                pl.ds(q * blocks + block, blocks, stride=size), :
            ]
        arrived = turned[slot].astype(jnp.bfloat16)
        gw[to] = inner_dot(u[rows, :], arrived, 1, 1).astype(jnp.bfloat16)
        weighted = inner_dot(w[at], arrived, 1, 0) * column(gain_ref, block, slots)
        g[rows, :] = g[rows, :] + scale * weighted
        return total + fold_rows(weighted * h[rows, :].astype(jnp.float32))

    total = by_chunk(blocks, left, jnp.zeros((8, slots), jnp.float32), arrive_left)
    left_out = gradient_copies(gw, (own_grad, peer_grad), gw_sems, 0)
    for copy in left_out:
        copy.start()
    back = scale * scale * scale * jnp.sum(total, axis=0, keepdims=True) / features

    def finish(block, carry):
        rows = block_rows(block, size)
        ended = g[rows, :] - h[rows, :].astype(jnp.float32) * back
        if last:
            u[rows, :] = ended.astype(jnp.bfloat16)
        else:
            g[rows, :] = ended
        return carry

    ended = u if last else g
    by_chunk(blocks, finish, 0, None, lambda chunk: chunk_copy(ended, out_ref, out_sems, chunk).start())
    wait_chunks(ended, out_ref, out_sems)
    for copy in right_out + left_out:
        copy.wait()


def shape_of(shape, dtype):
    return jax.ShapeDtypeStruct(shape, dtype)


SMEM = pl.BlockSpec(memory_space=pltpu.SMEM)
INSIDE = pl.BlockSpec(memory_space=pltpu.VMEM)
OUTSIDE = pl.BlockSpec(memory_space=pl.ANY)


def run_forward(table, gain, sums, residual, weights, layer):
    first = residual.dtype == jnp.bfloat16
    whole = residual.shape
    sources = (*weights, residual)
    held = (PARTS * weights[0].shape[0],) + weights[0].shape[2:]
    out_shape = (
        shape_of(whole, jnp.float32),
        shape_of(whole, jnp.bfloat16),
        shape_of(whole, jnp.bfloat16),
        shape_of(whole, jnp.bfloat16),
        shape_of((8, whole[1]), jnp.float32),
        shape_of((8, whole[1]), jnp.float32),
    )
    return pl.pallas_call(
        lambda *refs: forward_kernel(first, layer, len(sources), *refs),
        in_specs=[SMEM, INSIDE, INSIDE] + [OUTSIDE] * len(sources),
        out_specs=[OUTSIDE] * 4 + [INSIDE] * 2,
        out_shape=out_shape,
        scratch_shapes=[
            pltpu.VMEM(whole if first else SMALL, jnp.bfloat16),
            pltpu.VMEM(whole, jnp.float32),
            pltpu.VMEM(held, jnp.bfloat16),
            pltpu.VMEM(whole, jnp.bfloat16),
            pltpu.VMEM(whole, jnp.bfloat16),
            pltpu.VMEM(whole, jnp.bfloat16),
            pltpu.VMEM(whole, jnp.float32),
            pltpu.SemaphoreType.DMA((CHUNKS,)),
            pltpu.SemaphoreType.DMA((2, PARTS)),
            pltpu.SemaphoreType.DMA((4, CHUNKS)),
        ],
        compiler_params=pltpu.CompilerParams(vmem_limit_bytes=VMEM_LIMIT),
        cost_estimate=pl.CostEstimate(
            flops=FORWARD_COST, bytes_accessed=20 * whole[0] * whole[1], transcendentals=0
        ),
        name="forward_layer",
    )(table, gain, sums, *sources)


def run_backward(table, gain, end_gain, scale, kept, weights, layer, sources, turning, last):
    whole = kept[0].shape
    sources = (*kept, *weights, *sources)
    held = (PARTS * weights[0].shape[0],) + weights[0].shape[2:]
    half = (held[0] // 2,) + held[1:]
    out_shape = [shape_of(whole, jnp.bfloat16 if last else jnp.float32)] + [shape_of(half, jnp.bfloat16)] * 2
    return pl.pallas_call(
        lambda *refs: backward_kernel(turning, last, layer, len(sources), *refs),
        in_specs=[SMEM] + [INSIDE] * 3 + [OUTSIDE] * len(sources),
        out_specs=[OUTSIDE] * len(out_shape),
        out_shape=out_shape,
        scratch_shapes=[
            pltpu.VMEM(whole, jnp.float32),
            pltpu.VMEM(whole, jnp.bfloat16),
            pltpu.VMEM(whole, jnp.bfloat16),
            pltpu.VMEM(whole, jnp.bfloat16),
            pltpu.VMEM(whole, jnp.bfloat16 if last else jnp.float32),
            pltpu.VMEM(held, jnp.bfloat16),
            pltpu.VMEM(held, jnp.bfloat16),
            pltpu.VMEM(whole, jnp.float32),
            pltpu.VMEM((8, held[-1], whole[1]), jnp.float32),
            pltpu.VMEM(whole if turning else SMALL, jnp.float32),
            pltpu.VMEM(whole if turning else SMALL, jnp.bfloat16),
            pltpu.SemaphoreType.DMA((6, CHUNKS)),
            pltpu.SemaphoreType.DMA((2, PARTS)),
            pltpu.SemaphoreType.DMA((CHUNKS,)),
            pltpu.SemaphoreType.DMA((2, PARTS)),
        ],
        compiler_params=pltpu.CompilerParams(vmem_limit_bytes=VMEM_LIMIT),
        cost_estimate=pl.CostEstimate(
            flops=BACKWARD_COST, bytes_accessed=30 * whole[0] * whole[1], transcendentals=0
        ),
        name="backward_layer",
    )(table, gain, end_gain, scale, *sources)


def copies_kernel(plan, inputs, outputs, *refs):
    sems = refs[-1]
    copies = [
        pltpu.make_async_copy(source, target, sems.at[at])
        for at, (source, target) in enumerate(plan(refs[:inputs], refs[inputs : inputs + outputs]))
    ]
    for copy in copies:
        copy.start()
    for copy in copies:
        copy.wait()


def run_copies(plan, scalars, inputs, out_shape, most, name):
    extra = [] if scalars is None else [scalars]
    size = sum(math.prod(out.shape) for out in out_shape)
    return pl.pallas_call(
        lambda *refs: copies_kernel(plan, len(extra) + len(inputs), len(out_shape), *refs),
        in_specs=[SMEM] * len(extra) + [OUTSIDE] * len(inputs),
        out_specs=[INSIDE] * len(out_shape),
        out_shape=out_shape,
        scratch_shapes=[pltpu.SemaphoreType.DMA((most,))],
        compiler_params=pltpu.CompilerParams(vmem_limit_bytes=VMEM_LIMIT),
        cost_estimate=pl.CostEstimate(flops=0, bytes_accessed=4 * size, transcendentals=0),
        name=name,
    )(*extra, *inputs)


def joined(parts, rows=None):
    rows = parts[0].shape[0] if rows is None else rows
    whole = shape_of((rows * len(parts),) + parts[0].shape[1:], parts[0].dtype)

    def plan(sources, targets):
        return [
            (source.at[pl.ds(0, rows)], targets[0].at[pl.ds(at * rows, rows)])
            for at, source in enumerate(sources)
        ]

    return run_copies(plan, None, parts, [whole], len(parts), "join")[0]


def sum_kernel(terms, refs_in, *refs):
    sources, outs = refs[:refs_in], refs[refs_in:]
    groups = refs_in // terms
    count = len(outs)
    for group in range(groups):
        mine = sources[group * terms : (group + 1) * terms]
        rows = mine[0].shape[0] // count
        for at, out in enumerate(outs):
            total = sum(ref[pl.ds(at * rows, rows), :].astype(jnp.float32) for ref in mine)
            out[pl.ds(group * rows, rows), :] = total.astype(jnp.bfloat16)


def run_sum(groups, outputs):
    flat = [term.reshape(-1, term.shape[-1]) for terms in groups for term in terms]
    rows, lanes = flat[0].shape
    return pl.pallas_call(
        lambda *refs: sum_kernel(len(groups[0]), len(flat), *refs),
        in_specs=[INSIDE] * len(flat),
        out_specs=[INSIDE] * outputs,
        out_shape=[shape_of((len(groups) * rows // outputs, lanes), jnp.bfloat16)] * outputs,
        compiler_params=pltpu.CompilerParams(vmem_limit_bytes=VMEM_LIMIT),
        cost_estimate=pl.CostEstimate(
            flops=rows * lanes * len(flat), bytes_accessed=2 * rows * lanes * (len(flat) + 1), transcendentals=0
        ),
        name="sum",
    )(*flat)


def factor_pieces(place, left, right, gain_rows, groups, chunk):
    width = 4
    size = left.shape[-1]
    shapes = []
    for group in groups:
        rows = len(group) * 2 * chunk * size + (gain_rows.shape[0] if group[0] == 0 else 0)
        shapes += [shape_of((rows, size), jnp.bfloat16)] * width

    def plan(sources, targets):
        place_ref, left_ref, right_ref, gain_ref = sources
        copies = []
        for at, group in enumerate(groups):
            for j in range(width):
                target = targets[at * width + j]
                start = (place_ref[2] * width + (place_ref[0] ^ place_ref[1] ^ j)) * chunk
                row = 0
                for layer in group:
                    for ref in (left_ref, right_ref):
                        for inside in range(chunk):
                            copies.append((ref.at[layer, start + inside], target.at[pl.ds(row, size)]))
                            row += size
                if group[0] == 0:
                    copies.append((gain_ref, target.at[pl.ds(row, gain_rows.shape[0])]))
        return copies

    most = width * (sum(len(group) for group in groups) * 2 * chunk + 1)
    flat = run_copies(plan, place, (left, right, gain_rows), shapes, most, "pieces")
    return [flat[at * width : (at + 1) * width] for at in range(len(groups))]


def choice(pairs, critic, slots):
    rows = pairs.shape[0]
    named = (pairs[:, 0:1] == critic) | (pairs[:, 1:2] == critic)
    named = jnp.broadcast_to(named.astype(jnp.float32), (rows, slots))
    before = lax.broadcasted_iota(jnp.int32, (rows, rows), 1) < lax.broadcasted_iota(jnp.int32, (rows, rows), 0)
    rank = inner_dot(before.astype(jnp.bfloat16), named.astype(jnp.bfloat16), 1, 0)
    at = lax.broadcasted_iota(jnp.int32, (rows, slots), 1).astype(jnp.float32)
    return jnp.where(rank == at, named, 0.0).astype(jnp.bfloat16)


def pick_kernel(pairs_ref, values_ref, out_ref):
    width, features, slots = out_ref.shape
    pairs = pairs_ref[...]
    chosen = [choice(pairs, critic, slots) for critic in range(width)]
    step = 512
    for start in range(0, features, step):
        part = values_ref[:, pl.ds(start, step)]
        for k in range(width):
            out_ref[k, pl.ds(start, step), :] = inner_dot(part, chosen[k], 0, 0).astype(jnp.bfloat16)


def run_pick(pairs, values, width, slots):
    rows, features = values.shape
    return pl.pallas_call(
        pick_kernel,
        in_specs=[INSIDE] * 2,
        out_specs=INSIDE,
        out_shape=shape_of((width, features, slots), jnp.bfloat16),
        compiler_params=pltpu.CompilerParams(vmem_limit_bytes=VMEM_LIMIT),
        cost_estimate=pl.CostEstimate(
            flops=2 * rows * features * slots * width, bytes_accessed=8 * rows * features, transcendentals=0
        ),
        name="pick",
    )(pairs, values)


def combine_kernel(pairs_ref, came_ref, out_ref):
    width, features, slots = came_ref.shape
    pairs = pairs_ref[...]
    chosen = [choice(pairs, critic, slots) for critic in range(width)]
    step = 512
    for start in range(0, features, step):
        total = sum(inner_dot(chosen[k], came_ref[k, pl.ds(start, step), :], 1, 1) for k in range(width))
        out_ref[:, pl.ds(start, step)] = (0.5 * total).astype(jnp.bfloat16)


def run_combine(pairs, came):
    rows = pairs.shape[0]
    return pl.pallas_call(
        combine_kernel,
        in_specs=[INSIDE] * 2,
        out_specs=INSIDE,
        out_shape=shape_of((rows, came.shape[1]), jnp.bfloat16),
        compiler_params=pltpu.CompilerParams(vmem_limit_bytes=VMEM_LIMIT),
        cost_estimate=pl.CostEstimate(
            flops=2 * rows * came.size, bytes_accessed=4 * came.size, transcendentals=0
        ),
        name="combine",
    )(pairs, came)


FORWARD_COST = 15_000_000_000
BACKWARD_COST = 18_000_000_000


def assemble_kernel(layers, factor, place_ref, *refs):
    count = 2 * len(layers)
    sources, (left_ref, right_ref) = refs[:count], refs[count : count + 2]
    held, wide, in_sems, out_sems = refs[count + 2 :]
    width, chunk = held.shape[1], held.shape[4]
    origin, core = place_ref[0] ^ place_ref[1], place_ref[2]
    arrivals = [
        pltpu.make_async_copy(source, held.at[at], in_sems.at[at]) for at, source in enumerate(sources)
    ]
    for copy in arrivals:
        copy.start()
    leaving = []
    for at in range(count):
        arrivals[at].wait()
        half = core if at % 2 == 0 else 1 - core
        for k in range(width):
            wide[at, k] = held[at, k].astype(jnp.float32) * factor
            start = (half * width + (origin ^ k)) * chunk
            for inside, layer in enumerate(layers[at // 2]):
                for which, target in enumerate((left_ref, right_ref)):
                    copy = pltpu.make_async_copy(
                        wide.at[at, k, inside, which],
                        target.at[layer, pl.ds(start, chunk)],
                        out_sems.at[len(leaving)],
                    )
                    copy.start()
                    leaving.append(copy)
    for copy in leaving:
        copy.wait()


def run_assemble(place, pieces, layers, factor):
    piece = pieces[0].shape
    layer_count = sum(len(group) for group in layers)
    out = shape_of((layer_count, 2 * piece[0] * piece[3]) + piece[4:], jnp.float32)
    return pl.pallas_call(
        lambda *refs: assemble_kernel(layers, factor, *refs),
        in_specs=[SMEM] + [OUTSIDE] * len(pieces),
        out_specs=[OUTSIDE] * 2,
        out_shape=[out] * 2,
        scratch_shapes=[
            pltpu.VMEM((len(pieces),) + piece, jnp.bfloat16),
            pltpu.VMEM((len(pieces),) + piece, jnp.float32),
            pltpu.SemaphoreType.DMA((len(pieces),)),
            pltpu.SemaphoreType.DMA((4 * layer_count * piece[0],)),
        ],
        compiler_params=pltpu.CompilerParams(vmem_limit_bytes=VMEM_LIMIT),
        cost_estimate=pl.CostEstimate(
            flops=0, bytes_accessed=6 * len(pieces) * math.prod(piece), transcendentals=0
        ),
        name="assemble",
    )(place, *pieces)


def plane_routes(width, replicas):
    bits = width.bit_length() - 1
    orders = [[(step + d) % bits for step in range(bits)] for d in range(replicas)]
    every = [(s, t, d) for s in range(width) for t in range(width) for d in range(replicas)]

    def route(move):
        def index(s, t, d):
            return (s * width + t) * replicas + d

        return [(index(*place), index(*move(*place))) for place in every]

    ranks = [[0] * width for _ in range(replicas)]
    for d in range(replicas):
        for r in range(width):
            ranks[d][sum(((r >> at) & 1) << orders[d][at] for at in range(bits))] = r
    return {
        "spread": [route(lambda s, t, d, j=j: (s ^ t ^ j, t, d)) for j in range(width)],
        "lift": [route(lambda s, t, d, j=j: (s, t ^ s ^ j, d)) for j in range(width)],
        "across": [route(lambda s, t, d, at=at: (s ^ (1 << orders[d][at]), t, d)) for at in range(bits)],
        "cores": route(lambda s, t, d: (s, t, 1 - d)),
        "sections": [route(lambda s, t, d, k=k: (s ^ k, t, d)) for k in range(width)],
        "planes": [route(lambda s, t, d, k=k: (s, t ^ k, d)) for k in range(width)],
        "homes": [route(lambda s, t, d, j=j: (t, t ^ s ^ j, d)) for j in range(width)],
    }, ranks


def plane_shards(patches, teacher, critic_pairs, left_factors, right_factors, norm_gains):
    width = lax.axis_size("section")
    replicas = lax.axis_size("dp")
    tok_rows, feat_local = patches.shape
    layer_count, local_blocks, size = left_factors.shape[1:4]
    blocks = feat_local * width // size
    wide = 2 * tok_rows // 3
    chunk = local_blocks // (replicas * width)
    layer_rows = 2 * chunk * size
    routes, ranks = plane_routes(width, replicas)
    section = lax.axis_index("section")
    tensor = lax.axis_index("tensor")
    core = lax.axis_index("dp")
    place = jnp.stack([section, tensor, core]).astype(jnp.int32)
    tie = lax.optimization_barrier

    def move(value, route):
        return lax.ppermute(value, AXES, route)

    def move_all(values, name):
        return [move(value, route) for value, route in zip(values, routes[name])]

    def send(values, name):
        return [values[0]] + [move(values[k], routes[name][k]) for k in range(1, width)]

    def gather_one(mine):
        return joined([mine, move(mine, routes["across"][0])])

    def gather_two(pair):
        return pair, move(pair, routes["across"][1]), move(pair, routes["cores"])

    def gather_three(pair, other, peer):
        return [pair, other, peer, move(other, routes["cores"])]

    def as_weights(parts):
        return [part.reshape(2 * width, -1, 2, chunk, size, size) for part in parts]

    block = jnp.arange(blocks, dtype=jnp.int32)
    inside = block % local_blocks
    replica = inside // (width * chunk)
    part = (replica != core).astype(jnp.int32)
    distance = section ^ ((inside // chunk) % width)
    piece = tensor ^ (section ^ distance) ^ (block // local_blocks)
    rank = jnp.array(ranks, jnp.int32)[replica, distance]
    table = jnp.stack(
        [
            ((part * width + rank) * width + piece) * chunk + inside % chunk,
            ((part * width + distance) * width + piece) * chunk + inside % chunk,
        ]
    ).astype(jnp.int32)

    def to_planes(value):
        return lax.all_to_all(value, "tensor", split_axis=0, concat_axis=0, tiled=True)

    patch_sent = run_pick(critic_pairs, patches, width, wide)
    factors = (left_factors[0], right_factors[0])
    groups = [tuple(range(0, 2)), tuple(range(2, layer_count))]
    gain_rows = norm_gains[0].reshape(-1, size)
    pieces = factor_pieces(place, *factors, gain_rows, groups, chunk)

    patch_came = to_planes(patch_sent).reshape(-1, wide)
    near = [move_all(pieces[0], "spread")]
    near[0], pieces[1] = tie((near[0], pieces[1]))
    came = [move_all(near[0], "lift")]
    near.append(move_all(pieces[1], "spread"))
    group_rows = [len(group) * layer_rows for group in groups]

    def lowest_of(at):
        mine = joined(came[at], group_rows[at])
        return mine.reshape(width, group_rows[at], size)

    gains = jnp.stack([value[group_rows[0] :] for value in came[0]])[jnp.arange(width) ^ section ^ tensor]
    gains = gains.reshape(width, layer_count + 1, local_blocks, size).transpose(1, 3, 0, 2)
    gains = gains.reshape(layer_count + 1, size, blocks)
    pair = gather_one(lowest_of(0))
    came.append(move_all(near[1], "lift"))
    weights = [as_weights(gather_three(*gather_two(pair)))]
    later = gather_one(lowest_of(1))
    target_sent = run_pick(critic_pairs, teacher, width, wide)

    residual = patch_came
    residual, weights, later, target_sent = tie((residual, weights, later, target_sent))
    flying = gather_two(later)
    sums = jnp.zeros((8, wide), jnp.float32)
    stored = []
    for layer in range(layer_count):
        group = 0 if layer in groups[0] else 1
        following, u, z, slope, scale, sums = run_forward(
            table, gains[layer], sums, residual, weights[group], layer - groups[group][0]
        )
        stored.append(((slope, z, u), scale, residual))
        residual = following
        if layer == 0:
            residual, sums, flying, target_sent = tie((residual, sums, flying, target_sent))
            weights.append(as_weights(gather_three(*flying)))
            target = to_planes(target_sent).reshape(-1, wide)
        if layer == groups[0][-1]:
            residual, sums, weights[1] = tie((residual, sums, weights[1]))

    def core_sum(mine, other):
        return (mine, move(other, routes["cores"]))

    def plane_sum(mine, other):
        return send(run_sum([(mine, other)], width), "sections")

    def homeward(parts):
        return move_all(run_sum(parts, width), "homes")

    def both_halves(parts):
        whole = joined(parts)
        return [part.reshape(width, -1, 2, chunk, size, size) for part in (whole, move(whole, routes["cores"]))]

    steps = (core_sum, plane_sum)
    gradient = residual
    underway = []
    for layer in range(layer_count - 1, -1, -1):
        turning = layer == layer_count - 1
        last = layer == 0
        kept, scale, inputs = stored[layer]
        group = 0 if layer in groups[0] else 1
        sources = (gradient, inputs, target) if turning else (gradient, inputs)
        underway = [(at + 1, steps[at](*state)) if at < len(steps) else (at, state) for at, state in underway]
        gradient, mine, other = run_backward(
            table,
            gains[layer],
            gains[layer_count],
            scale,
            kept,
            weights[group],
            layer - groups[group][0],
            sources,
            turning,
            last,
        )
        gradient, mine, other, states = tie((gradient, mine, other, [state for _, state in underway]))
        underway = [(at, state) for (at, _), state in zip(underway, states)]
        underway.append((0, (mine, other)))

    returned = to_planes(gradient.reshape(width, feat_local, wide))
    homes_of = [None, None]
    ended = []
    for at, state in underway:
        for step in steps[at:]:
            state = step(*state)
        ended.insert(0, state)
    ended[1:] = tie(ended[1:])
    homes_of[1] = both_halves(homeward(ended[groups[1][0] :]))
    home = homeward(ended[: groups[1][0]])
    d_patches = run_combine(critic_pairs, returned)
    d_patches, home, homes_of[1] = tie((d_patches, home, homes_of[1]))
    homes_of[0] = both_halves(home)
    grad_factor = 1.0 / math.sqrt(2 * tok_rows * width * replicas)
    grad_left, grad_right = run_assemble(place, homes_of[0] + homes_of[1], groups, grad_factor)
    return (d_patches, grad_left[None], grad_right[None])


def solution(mesh):
    in_specs = (
        P(("section", "dp"), "tensor"),
        P(("section", "dp"), "tensor"),
        P(("section", "dp"), None),
        P("section", None, "tensor", None, None),
        P("section", None, "tensor", None, None),
        P("section", None, "tensor"),
    )
    out_specs = (
        P(("section", "dp"), "tensor"),
        P("section", None, "tensor", None, None),
        P("section", None, "tensor", None, None),
    )
    body = plane_shards if planes_fit(mesh) else layered_shards
    return jax.shard_map(
        body, mesh=mesh, in_specs=in_specs, out_specs=out_specs, check_vma=False)
```

```python
import math

import jax
import jax.numpy as jnp
from jax import lax
from jax.experimental import pallas as pl
from jax.experimental.pallas import tpu as pltpu
from jax.sharding import PartitionSpec as P

EPSILON = 1e-06
TANH_SLOPE = 0.7978845608028654
CUBIC_TERM = 0.044715


def shifted(value, axis, steps):
    count = lax.axis_size(axis)
    first, last = (max(0, -steps), min(count, count - steps))
    return lax.ppermute(value, axis, [(source, source + steps) for source in range(first, last)])


def gelu_value(values):
    tangent = jnp.tanh(TANH_SLOPE * (values + CUBIC_TERM * values * values * values))
    return 0.5 * values * (1.0 + tangent)


def gelu_slope(values):
    tangent = jnp.tanh(TANH_SLOPE * (values + CUBIC_TERM * values * values * values))
    return 0.5 * (1.0 + tangent) + 0.5 * values * (1.0 - tangent * tangent) * TANH_SLOPE * (
        1.0 + 3.0 * CUBIC_TERM * values * values
    )


def norm_pair(residuals, gain_pair, model_width):
    squares = lax.psum(
        (
            jnp.sum(residuals[0] * residuals[0], axis=(1, 2)),
            jnp.sum(residuals[1] * residuals[1], axis=(1, 2)),
        ),
        "tensor",
    )
    factors = [lax.rsqrt(squares[member] / model_width + EPSILON) for member in range(2)]
    normed = [
        residuals[member] * factors[member][:, None, None] * gain_pair[member][None]
        for member in range(2)
    ]
    return (factors, normed)


def norm_back_pair(residuals, factors, gain_pair, grad_normed, carried, model_width):
    weighted = [grad_normed[member] * gain_pair[member][None] for member in range(2)]
    inners = lax.psum(
        (
            jnp.sum(weighted[0] * residuals[0], axis=(1, 2)),
            jnp.sum(weighted[1] * residuals[1], axis=(1, 2)),
        ),
        "tensor",
    )
    return [
        carried[member]
        + factors[member][:, None, None] * weighted[member]
        - residuals[member] * (factors[member] ** 3 * inners[member] / model_width)[:, None, None]
        for member in range(2)
    ]


def layered_shards(patches, teacher, critic_pairs, left_factors, right_factors, norm_gains):
    sections = lax.axis_size("section")
    tensor_width = lax.axis_size("tensor")
    replicas = lax.axis_size("dp")
    tok_rows = patches.shape[0]
    feat_local = patches.shape[1]
    layer_count = left_factors.shape[1]
    local_blocks = left_factors.shape[2]
    block_size = left_factors.shape[3]
    all_blocks = local_blocks * tensor_width
    fold_ratio = block_size // all_blocks
    model_width = feat_local * tensor_width
    sixth_rows = tok_rows // 6
    leading = 2 * sixth_rows
    critic_ids = jnp.arange(4, dtype=jnp.int32)
    named_by = (
        (critic_pairs[:, 0:1] == critic_ids[None, :])
        | (critic_pairs[:, 1:2] == critic_ids[None, :])
    ).astype(jnp.int32)
    ranking = jnp.cumsum(named_by, axis=0) - 1
    wide_ids = critic_ids[None, :] < 2
    slot_width = 3 * sixth_rows
    spilled = wide_ids & (ranking >= 3 * sixth_rows)
    destination = jnp.where(spilled, critic_ids[None, :] + 2, critic_ids[None, :])
    slot_index = jnp.where(spilled, ranking - sixth_rows, ranking)
    flat_slot = destination * slot_width + slot_index
    chosen = jnp.take_along_axis(flat_slot, critic_pairs, axis=1)
    slot_total = sections * slot_width
    row_ids = jnp.broadcast_to(jnp.arange(tok_rows, dtype=jnp.int32)[:, None], chosen.shape)
    source_row = (
        jnp.full((slot_total,), tok_rows, jnp.int32).at[chosen.reshape(-1)].set(row_ids.reshape(-1))
    )
    send_patch = (
        patches.at[source_row]
        .get(mode="fill", fill_value=0)
        .reshape(sections, slot_width, local_blocks, block_size)
    )
    send_target = (
        teacher.at[source_row]
        .get(mode="fill", fill_value=0)
        .reshape(sections, slot_width, local_blocks, block_size)
    )
    recv_patch, recv_target = (
        lax.all_to_all(send_patch, "section", split_axis=0, concat_axis=0, tiled=True),
        lax.all_to_all(send_target, "section", split_axis=0, concat_axis=0, tiled=True),
    )
    residuals = [
        recv_patch[:, :leading].reshape(-1, local_blocks, block_size).astype(jnp.float32),
        recv_patch[:, leading:].reshape(-1, local_blocks, block_size).astype(jnp.float32),
    ]
    targets = [
        recv_target[:, :leading].reshape(-1, local_blocks, block_size).astype(jnp.float32),
        recv_target[:, leading:].reshape(-1, local_blocks, block_size).astype(jnp.float32),
    ]
    native = (left_factors[0], right_factors[0], norm_gains[0])
    borrowed = shifted((left_factors, right_factors, norm_gains), "section", 2)
    is_wide = lax.axis_index("section") < 2
    second = (
        jnp.where(is_wide, left_factors, borrowed[0])[0],
        jnp.where(is_wide, right_factors, borrowed[1])[0],
        jnp.where(is_wide, norm_gains, borrowed[2])[0],
    )
    left_sets = (native[0], second[0])
    right_sets = (native[1], second[1])
    gain_sets = (
        native[2].astype(jnp.float32).reshape(layer_count + 1, local_blocks, block_size),
        second[2].astype(jnp.float32).reshape(layer_count + 1, local_blocks, block_size),
    )
    stored = []
    for layer_index in range(layer_count):
        gain_pair = [gain_sets[0][layer_index], gain_sets[1][layer_index]]
        factors, normed = norm_pair(residuals, gain_pair, model_width)
        normed = [normed[member].astype(jnp.bfloat16) for member in range(2)]
        first_out = [
            jnp.einsum(
                "nki,kij->nkj",
                normed[member],
                left_sets[member][layer_index],
                preferred_element_type=jnp.float32,
            ).astype(jnp.bfloat16)
            for member in range(2)
        ]
        permuted = (
            lax.all_to_all(first_out[0], "tensor", split_axis=2, concat_axis=1, tiled=True),
            lax.all_to_all(first_out[1], "tensor", split_axis=2, concat_axis=1, tiled=True),
        )
        permuted = [
            permuted[member].reshape(
                permuted[member].shape[0], all_blocks, local_blocks, fold_ratio
            )
            for member in range(2)
        ]
        right_quads = [
            right_sets[member][layer_index].reshape(
                local_blocks, fold_ratio, all_blocks, block_size
            )
            for member in range(2)
        ]
        mixture = [
            jnp.einsum(
                "nkmp,mpkl->nml",
                permuted[member],
                right_quads[member],
                preferred_element_type=jnp.float32,
            )
            for member in range(2)
        ]
        stored.append((residuals, factors, normed, permuted, mixture, right_quads, gain_pair))
        residuals = [residuals[member] + gelu_value(mixture[member]) for member in range(2)]
    final_gains = [gain_sets[0][layer_count], gain_sets[1][layer_count]]
    factors, outputs = norm_pair(residuals, final_gains, model_width)
    gradients = norm_back_pair(
        residuals,
        factors,
        final_gains,
        [outputs[member] - targets[member] for member in range(2)],
        [jnp.zeros_like(residuals[member]) for member in range(2)],
        model_width,
    )
    left_terms = []
    right_terms = []
    for layer_index in range(layer_count - 1, -1, -1):
        inputs, factors, normed, permuted, mixture, right_quads, gain_pair = stored[layer_index]
        slopes = [
            (gradients[member] * gelu_slope(mixture[member])).astype(jnp.bfloat16)
            for member in range(2)
        ]
        right_grad = [
            jnp.einsum(
                "nkmp,nml->mpkl",
                permuted[member],
                slopes[member],
                preferred_element_type=jnp.float32,
            ).reshape(local_blocks, block_size, block_size)
            for member in range(2)
        ]
        back_moved = [
            jnp.einsum(
                "nml,mpkl->nkmp",
                slopes[member],
                right_quads[member],
                preferred_element_type=jnp.float32,
            )
            .astype(jnp.bfloat16)
            .reshape(slopes[member].shape[0], all_blocks, local_blocks * fold_ratio)
            for member in range(2)
        ]
        arrived = (
            lax.all_to_all(back_moved[0], "tensor", split_axis=1, concat_axis=2, tiled=True),
            lax.all_to_all(back_moved[1], "tensor", split_axis=1, concat_axis=2, tiled=True),
        )
        left_grad = [
            jnp.einsum(
                "nki,nkj->kij", normed[member], arrived[member], preferred_element_type=jnp.float32
            )
            for member in range(2)
        ]
        grad_normed = [
            jnp.einsum(
                "nkj,kij->nki",
                arrived[member],
                left_sets[member][layer_index],
                preferred_element_type=jnp.float32,
            )
            for member in range(2)
        ]
        gradients = norm_back_pair(inputs, factors, gain_pair, grad_normed, gradients, model_width)
        layer_left = jnp.stack(left_grad)
        layer_right = jnp.stack(right_grad)
        layer_left, layer_right = (
            lax.psum(layer_left.astype(jnp.bfloat16), "dp").astype(jnp.float32),
            lax.psum(layer_right.astype(jnp.bfloat16), "dp").astype(jnp.float32),
        )
        left_terms.insert(0, layer_left)
        right_terms.insert(0, layer_right)
    left_stack = jnp.stack(left_terms)
    right_stack = jnp.stack(right_terms)
    repaid = (
        shifted(left_stack[:, 1].astype(jnp.bfloat16), "section", -2).astype(jnp.float32),
        shifted(right_stack[:, 1].astype(jnp.bfloat16), "section", -2).astype(jnp.float32),
    )
    is_wide = lax.axis_index("section") < 2
    left_total = left_stack[:, 0] + jnp.where(is_wide, left_stack[:, 1] + repaid[0], 0.0)
    right_total = right_stack[:, 0] + jnp.where(is_wide, right_stack[:, 1] + repaid[1], 0.0)
    grad_factor = 1.0 / math.sqrt(2 * tok_rows * sections * replicas)
    returned = [
        gradients[member].astype(jnp.bfloat16).reshape(sections, -1, local_blocks, block_size)
        for member in range(2)
    ]
    back_lead, back_trail = (
        lax.all_to_all(returned[0], "section", split_axis=0, concat_axis=0, tiled=True),
        lax.all_to_all(returned[1], "section", split_axis=0, concat_axis=0, tiled=True),
    )
    gathered = jnp.concatenate((back_lead, back_trail), axis=1).reshape(
        slot_total, local_blocks, block_size
    )
    combined = (
        gathered[chosen[:, 0]].astype(jnp.float32) + gathered[chosen[:, 1]].astype(jnp.float32)
    ) * 0.5
    d_patches = combined.astype(jnp.bfloat16).reshape(tok_rows, feat_local)
    return (d_patches, (left_total * grad_factor)[None], (right_total * grad_factor)[None])


VMEM_LIMIT = 60 * 1024 * 1024
CHUNKS = 8
PARTS = 4
SMALL = (16, 128)
AXES = ("section", "tensor", "dp")


def planes_fit(mesh):
    sections = mesh.shape["section"]
    paired = mesh.shape["dp"] == 2 and sections & (sections - 1) == 0
    return paired and mesh.shape["tensor"] == sections


def inner_dot(left, right, left_dim, right_dim):
    return lax.dot_general(
        left,
        right,
        (((left_dim,), (right_dim,)), ((), ())),
        preferred_element_type=jnp.float32,
    )


def fold_rows(values):
    return jnp.sum(values.reshape(values.shape[0] // 8, 8, values.shape[1]), axis=0)


def block_rows(block, size):
    return pl.ds(pl.multiple_of(block * size, size), size)


def chunk_copy(source, target, sems, chunk):
    rows = target.shape[0] // CHUNKS
    at = pl.ds(pl.multiple_of(chunk * rows, rows), rows)
    return pltpu.make_async_copy(source.at[at], target.at[at], sems.at[chunk])


def start_chunks(source, target, sems):
    for chunk in range(CHUNKS):
        chunk_copy(source, target, sems, chunk).start()


def wait_chunks(source, target, sems):
    for chunk in range(CHUNKS):
        chunk_copy(source, target, sems, chunk).wait()


def factor_copies(parts, layer, held, sems, side):
    count = parts[0].shape[0]
    return [
        pltpu.make_async_copy(
            ref.at[:, layer, side], held.at[pl.ds(at * count, count), side], sems.at[side, at]
        )
        for at, ref in enumerate(parts)
    ]


def gradient_copies(held, parts, sems, side):
    count = parts[0].shape[0]
    return [
        pltpu.make_async_copy(
            held.at[pl.ds(at * count, count), side], ref.at[:, side], sems.at[side, at]
        )
        for at, ref in enumerate(parts)
    ]


def by_chunk(blocks, step, carry, before=None, after=None):
    per_chunk = blocks // CHUNKS

    def one(chunk, carry):
        if before is not None:
            before(chunk)
        carry = lax.fori_loop(
            0, per_chunk, lambda at, now: step(chunk * per_chunk + at, now), carry, unroll=True
        )
        if after is not None:
            after(chunk)
        return carry

    return lax.fori_loop(0, CHUNKS, one, carry)


def forward_kernel(first, layer, inputs, table_ref, sums_ref, gain_ref, *refs):
    sources, refs = refs[:inputs], refs[inputs:]
    parts, sources = sources[:PARTS], sources[PARTS:]
    out_ref, u_ref, z_ref, slope_ref, scale_ref, next_ref = refs[:6]
    raw, h, w, u, z, slope, mid, gain, in_sems, gain_sems, w_sems, out_sems = refs[6:]
    features, slots = h.shape
    size = w.shape[-1]
    chunk_blocks = w.shape[2]
    blocks = features // size
    fold = size // blocks

    left_in = factor_copies(parts, layer, w, w_sems, 0)
    right_in = factor_copies(parts, layer, w, w_sems, 1)
    if first:
        start_chunks(sources[0], raw, in_sems)
        for copy in left_in:
            copy.start()
        start_chunks(gain_ref, gain, gain_sems)
        for copy in right_in:
            copy.start()

        def squares(block, total):
            rows = block_rows(block, size)
            part = raw[rows, :].astype(jnp.float32)
            h[rows, :] = part
            return total + fold_rows(part * part)

        total = by_chunk(
            blocks,
            squares,
            jnp.zeros((8, slots), jnp.float32),
            lambda chunk: chunk_copy(sources[0], raw, in_sems, chunk).wait(),
        )
    else:
        for copy in left_in:
            copy.start()
        start_chunks(sources[0], h, in_sems)
        start_chunks(gain_ref, gain, gain_sems)
        for copy in right_in:
            copy.start()
        total = sums_ref[...]
    scale = lax.rsqrt(jnp.sum(total, axis=0, keepdims=True) / features + EPSILON)
    scale_ref[...] = jnp.broadcast_to(scale, scale_ref.shape)
    for copy in left_in:
        copy.wait()

    def arrive(chunk):
        chunk_copy(gain_ref, gain, gain_sems, chunk).wait()
        if not first:
            chunk_copy(sources[0], h, in_sems, chunk).wait()

    def left(block, carry):
        rows = block_rows(block, size)
        place = table_ref[0, block]
        normed = (h[rows, :] * scale * gain[rows, :].astype(jnp.float32)).astype(jnp.bfloat16)
        u[rows, :] = normed
        weight = w[place // chunk_blocks, 0, place % chunk_blocks]
        mid[rows, :] = inner_dot(weight, normed, 0, 0)
        return carry

    def leave_left(chunk):
        chunk_copy(u, u_ref, out_sems.at[0], chunk).start()

    by_chunk(blocks, left, 0, arrive, leave_left)
    for copy in right_in:
        copy.wait()

    def right(block, total):
        rows = block_rows(block, size)
        place = table_ref[0, block]
        moved = [mid[pl.ds(block * fold + q, blocks, stride=size), :] for q in range(fold)]
        moved = jnp.concatenate(moved, axis=0).astype(jnp.bfloat16)
        z[rows, :] = moved
        weight = w[place // chunk_blocks, 1, place % chunk_blocks]
        mixture = inner_dot(weight, moved, 0, 0)
        squared = mixture * mixture
        tangent = jnp.tanh(mixture * (TANH_SLOPE + (TANH_SLOPE * CUBIC_TERM) * squared))
        half = 0.5 + 0.5 * tangent
        following = h[rows, :] + mixture * half
        h[rows, :] = following
        steep = half + mixture * (1.0 - tangent * tangent) * (
            0.5 * TANH_SLOPE + (1.5 * TANH_SLOPE * CUBIC_TERM) * squared
        )
        slope[rows, :] = steep.astype(jnp.bfloat16)
        return total + fold_rows(following * following)

    leaving = ((h, out_ref, 1), (z, z_ref, 2), (slope, slope_ref, 3))

    def leave_right(chunk):
        for source, target, at in leaving:
            chunk_copy(source, target, out_sems.at[at], chunk).start()

    next_ref[...] = by_chunk(blocks, right, jnp.zeros((8, slots), jnp.float32), None, leave_right)
    for source, target, at in ((u, u_ref, 0),) + leaving:
        wait_chunks(source, target, out_sems.at[at])


def backward_kernel(turning, last, layer, inputs, table_ref, scale_ref, gain_ref, end_gain_ref, *refs):
    sources, refs = refs[:inputs], refs[inputs:]
    slope_ref, z_ref, u_ref = sources[:3]
    parts, sources = sources[3 : 3 + PARTS], sources[3 + PARTS :]
    out_ref, own_grad, peer_grad = refs[:3]
    g, slope, z, u, h, w, gw, mid, turned, gain, top, goal, end_gain = refs[3:16]
    in_sems, w_sems, out_sems, gw_sems = refs[16:]
    features, slots = g.shape
    size = w.shape[-1]
    chunk_blocks = w.shape[2]
    blocks = features // size
    fold = size // blocks

    left_in = factor_copies(parts, layer, w, w_sems, 0)
    right_in = factor_copies(parts, layer, w, w_sems, 1)
    g_ref, h_ref = sources[:2]
    if turning:
        start_chunks(g_ref, top, in_sems.at[0])
        start_chunks(end_gain_ref, end_gain, in_sems.at[6])
        start_chunks(sources[2], goal, in_sems.at[5])
    else:
        start_chunks(g_ref, g, in_sems.at[0])
    for copy in right_in:
        copy.start()
    start_chunks(slope_ref, slope, in_sems.at[1])
    start_chunks(z_ref, z, in_sems.at[2])
    for copy in left_in:
        copy.start()
    start_chunks(u_ref, u, in_sems.at[3])
    start_chunks(gain_ref, gain, in_sems.at[7])
    start_chunks(h_ref, h, in_sems.at[4])

    if turning:
        zero = jnp.zeros((8, slots), jnp.float32)

        def sums(block, totals):
            rows = block_rows(block, size)
            part = top[rows, :]
            scaled = part * end_gain[rows, :].astype(jnp.float32)
            return (
                totals[0] + fold_rows(part * part),
                totals[1] + fold_rows(scaled * scaled),
                totals[2] + fold_rows(scaled * goal[rows, :].astype(jnp.float32)),
            )

        def arrive_top(chunk):
            chunk_copy(g_ref, top, in_sems.at[0], chunk).wait()
            chunk_copy(end_gain_ref, end_gain, in_sems.at[6], chunk).wait()
            chunk_copy(sources[2], goal, in_sems.at[5], chunk).wait()

        totals = by_chunk(blocks, sums, (zero, zero, zero), arrive_top)
        squares, gained, crossed = [jnp.sum(total, axis=0, keepdims=True) for total in totals]
        end_scale = lax.rsqrt(squares / features + EPSILON)
        end_back = end_scale * end_scale * end_scale * (end_scale * gained - crossed) / features

    for copy in right_in:
        copy.wait()

    def arrive_right(chunk):
        if not turning:
            chunk_copy(g_ref, g, in_sems.at[0], chunk).wait()
        chunk_copy(slope_ref, slope, in_sems.at[1], chunk).wait()
        chunk_copy(z_ref, z, in_sems.at[2], chunk).wait()

    def right(block, carry):
        rows = block_rows(block, size)
        place, home = table_ref[0, block], table_ref[1, block]
        at = (place // chunk_blocks, 1, place % chunk_blocks)
        to = (home // chunk_blocks, 1, home % chunk_blocks)
        if turning:
            part = top[rows, :]
            factor = end_gain[rows, :].astype(jnp.float32)
            error = (part * end_scale * factor - goal[rows, :].astype(jnp.float32)) * factor
            gradient = end_scale * error - part * end_back
            g[rows, :] = gradient
        else:
            gradient = g[rows, :]
        steep = (gradient * slope[rows, :].astype(jnp.float32)).astype(jnp.bfloat16)
        gw[to] = inner_dot(z[rows, :], steep, 1, 1).astype(jnp.bfloat16)
        mid[rows, :] = inner_dot(w[at], steep, 1, 0)
        return carry

    by_chunk(blocks, right, 0, arrive_right)
    right_out = gradient_copies(gw, (own_grad, peer_grad), gw_sems, 1)
    for copy in right_out:
        copy.start()
    for copy in left_in:
        copy.wait()
    scale = scale_ref[0:1, :]

    def arrive_left(chunk):
        chunk_copy(u_ref, u, in_sems.at[3], chunk).wait()
        chunk_copy(gain_ref, gain, in_sems.at[7], chunk).wait()
        chunk_copy(h_ref, h, in_sems.at[4], chunk).wait()

    def left(block, total):
        rows = block_rows(block, size)
        place, home = table_ref[0, block], table_ref[1, block]
        at = (place // chunk_blocks, 0, place % chunk_blocks)
        to = (home // chunk_blocks, 0, home % chunk_blocks)
        slot = block % turned.shape[0]
        for q in range(fold):
            turned[slot, pl.ds(q, blocks, stride=fold), :] = mid[
                pl.ds(q * blocks + block, blocks, stride=size), :
            ]
        arrived = turned[slot].astype(jnp.bfloat16)
        gw[to] = inner_dot(u[rows, :], arrived, 1, 1).astype(jnp.bfloat16)
        weighted = inner_dot(w[at], arrived, 1, 0) * gain[rows, :].astype(jnp.float32)
        g[rows, :] = g[rows, :] + scale * weighted
        return total + fold_rows(weighted * h[rows, :].astype(jnp.float32))

    total = by_chunk(blocks, left, jnp.zeros((8, slots), jnp.float32), arrive_left)
    left_out = gradient_copies(gw, (own_grad, peer_grad), gw_sems, 0)
    for copy in left_out:
        copy.start()
    back = scale * scale * scale * jnp.sum(total, axis=0, keepdims=True) / features

    def finish(block, carry):
        rows = block_rows(block, size)
        ended = g[rows, :] - h[rows, :].astype(jnp.float32) * back
        if last:
            u[rows, :] = ended.astype(jnp.bfloat16)
        else:
            g[rows, :] = ended
        return carry

    ended = u if last else g
    by_chunk(blocks, finish, 0, None, lambda chunk: chunk_copy(ended, out_ref, out_sems, chunk).start())
    wait_chunks(ended, out_ref, out_sems)
    for copy in right_out + left_out:
        copy.wait()


def shape_of(shape, dtype):
    return jax.ShapeDtypeStruct(shape, dtype)


SMEM = pl.BlockSpec(memory_space=pltpu.SMEM)
INSIDE = pl.BlockSpec(memory_space=pltpu.VMEM)
OUTSIDE = pl.BlockSpec(memory_space=pl.ANY)


def run_forward(table, gain, sums, residual, weights, layer):
    first = residual.dtype == jnp.bfloat16
    whole = residual.shape
    sources = (*weights, residual)
    held = (PARTS * weights[0].shape[0],) + weights[0].shape[2:]
    out_shape = (
        shape_of(whole, jnp.float32),
        shape_of(whole, jnp.bfloat16),
        shape_of(whole, jnp.bfloat16),
        shape_of(whole, jnp.bfloat16),
        shape_of((8, whole[1]), jnp.float32),
        shape_of((8, whole[1]), jnp.float32),
    )
    return pl.pallas_call(
        lambda *refs: forward_kernel(first, layer, len(sources), *refs),
        in_specs=[SMEM, INSIDE, OUTSIDE] + [OUTSIDE] * len(sources),
        out_specs=[OUTSIDE] * 4 + [INSIDE] * 2,
        out_shape=out_shape,
        scratch_shapes=[
            pltpu.VMEM(whole if first else SMALL, jnp.bfloat16),
            pltpu.VMEM(whole, jnp.float32),
            pltpu.VMEM(held, jnp.bfloat16),
            pltpu.VMEM(whole, jnp.bfloat16),
            pltpu.VMEM(whole, jnp.bfloat16),
            pltpu.VMEM(whole, jnp.bfloat16),
            pltpu.VMEM(whole, jnp.float32),
            pltpu.VMEM(whole, jnp.bfloat16),
            pltpu.SemaphoreType.DMA((CHUNKS,)),
            pltpu.SemaphoreType.DMA((CHUNKS,)),
            pltpu.SemaphoreType.DMA((2, PARTS)),
            pltpu.SemaphoreType.DMA((4, CHUNKS)),
        ],
        compiler_params=pltpu.CompilerParams(vmem_limit_bytes=VMEM_LIMIT),
        cost_estimate=pl.CostEstimate(
            flops=FORWARD_COST, bytes_accessed=20 * whole[0] * whole[1], transcendentals=0
        ),
        name="forward_layer",
    )(table, sums, gain, *sources)


def run_backward(table, gain, end_gain, scale, kept, weights, layer, sources, turning, last):
    whole = kept[0].shape
    sources = (*kept, *weights, *sources)
    held = (PARTS * weights[0].shape[0],) + weights[0].shape[2:]
    half = (held[0] // 2,) + held[1:]
    out_shape = [shape_of(whole, jnp.bfloat16 if last else jnp.float32)] + [shape_of(half, jnp.bfloat16)] * 2
    return pl.pallas_call(
        lambda *refs: backward_kernel(turning, last, layer, len(sources), *refs),
        in_specs=[SMEM, INSIDE] + [OUTSIDE] * (2 + len(sources)),
        out_specs=[OUTSIDE] * len(out_shape),
        out_shape=out_shape,
        scratch_shapes=[
            pltpu.VMEM(whole, jnp.float32),
            pltpu.VMEM(whole, jnp.bfloat16),
            pltpu.VMEM(whole, jnp.bfloat16),
            pltpu.VMEM(whole, jnp.bfloat16),
            pltpu.VMEM(whole, jnp.bfloat16 if last else jnp.float32),
            pltpu.VMEM(held, jnp.bfloat16),
            pltpu.VMEM(held, jnp.bfloat16),
            pltpu.VMEM(whole, jnp.float32),
            pltpu.VMEM((8, held[-1], whole[1]), jnp.float32),
            pltpu.VMEM(whole, jnp.bfloat16),
            pltpu.VMEM(whole if turning else SMALL, jnp.float32),
            pltpu.VMEM(whole if turning else SMALL, jnp.bfloat16),
            pltpu.VMEM(whole if turning else SMALL, jnp.bfloat16),
            pltpu.SemaphoreType.DMA((8, CHUNKS)),
            pltpu.SemaphoreType.DMA((2, PARTS)),
            pltpu.SemaphoreType.DMA((CHUNKS,)),
            pltpu.SemaphoreType.DMA((2, PARTS)),
        ],
        compiler_params=pltpu.CompilerParams(vmem_limit_bytes=VMEM_LIMIT),
        cost_estimate=pl.CostEstimate(
            flops=BACKWARD_COST, bytes_accessed=30 * whole[0] * whole[1], transcendentals=0
        ),
        name="backward_layer",
    )(table, scale, gain, end_gain, *sources)


def copies_kernel(plan, inputs, outputs, *refs):
    sems = refs[-1]
    copies = [
        pltpu.make_async_copy(source, target, sems.at[at])
        for at, (source, target) in enumerate(plan(refs[:inputs], refs[inputs : inputs + outputs]))
    ]
    for copy in copies:
        copy.start()
    for copy in copies:
        copy.wait()


def run_copies(plan, scalars, inputs, out_shape, most, name):
    extra = [] if scalars is None else [scalars]
    size = sum(math.prod(out.shape) for out in out_shape)
    return pl.pallas_call(
        lambda *refs: copies_kernel(plan, len(extra) + len(inputs), len(out_shape), *refs),
        in_specs=[SMEM] * len(extra) + [OUTSIDE] * len(inputs),
        out_specs=[INSIDE] * len(out_shape),
        out_shape=out_shape,
        scratch_shapes=[pltpu.SemaphoreType.DMA((most,))],
        compiler_params=pltpu.CompilerParams(vmem_limit_bytes=VMEM_LIMIT),
        cost_estimate=pl.CostEstimate(flops=0, bytes_accessed=4 * size, transcendentals=0),
        name=name,
    )(*extra, *inputs)


def joined(parts, rows=None):
    rows = parts[0].shape[0] if rows is None else rows
    whole = shape_of((rows * len(parts),) + parts[0].shape[1:], parts[0].dtype)

    def plan(sources, targets):
        return [
            (source.at[pl.ds(0, rows)], targets[0].at[pl.ds(at * rows, rows)])
            for at, source in enumerate(sources)
        ]

    return run_copies(plan, None, parts, [whole], len(parts), "join")[0]


def sum_kernel(terms, refs_in, *refs):
    sources, outs = refs[:refs_in], refs[refs_in:]
    groups = refs_in // terms
    count = len(outs)
    for group in range(groups):
        mine = sources[group * terms : (group + 1) * terms]
        rows = mine[0].shape[0] // count
        for at, out in enumerate(outs):
            total = sum(ref[pl.ds(at * rows, rows), :].astype(jnp.float32) for ref in mine)
            out[pl.ds(group * rows, rows), :] = total.astype(jnp.bfloat16)


def run_sum(groups, outputs):
    flat = [term.reshape(-1, term.shape[-1]) for terms in groups for term in terms]
    rows, lanes = flat[0].shape
    return pl.pallas_call(
        lambda *refs: sum_kernel(len(groups[0]), len(flat), *refs),
        in_specs=[INSIDE] * len(flat),
        out_specs=[INSIDE] * outputs,
        out_shape=[shape_of((len(groups) * rows // outputs, lanes), jnp.bfloat16)] * outputs,
        compiler_params=pltpu.CompilerParams(vmem_limit_bytes=VMEM_LIMIT),
        cost_estimate=pl.CostEstimate(
            flops=rows * lanes * len(flat), bytes_accessed=2 * rows * lanes * (len(flat) + 1), transcendentals=0
        ),
        name="sum",
    )(*flat)


def factor_pieces(place, left, right, gain_rows, groups, chunk):
    width = 4
    size = left.shape[-1]
    shapes = []
    for group in groups:
        rows = len(group) * 2 * chunk * size + (gain_rows.shape[0] if group[0] == 0 else 0)
        shapes += [shape_of((rows, size), jnp.bfloat16)] * width

    def plan(sources, targets):
        place_ref, left_ref, right_ref, gain_ref = sources
        copies = []
        for at, group in enumerate(groups):
            for j in range(width):
                target = targets[at * width + j]
                start = (place_ref[2] * width + (place_ref[0] ^ place_ref[1] ^ j)) * chunk
                row = 0
                for layer in group:
                    for ref in (left_ref, right_ref):
                        for inside in range(chunk):
                            copies.append((ref.at[layer, start + inside], target.at[pl.ds(row, size)]))
                            row += size
                if group[0] == 0:
                    copies.append((gain_ref, target.at[pl.ds(row, gain_rows.shape[0])]))
        return copies

    most = width * (sum(len(group) for group in groups) * 2 * chunk + 1)
    flat = run_copies(plan, place, (left, right, gain_rows), shapes, most, "pieces")
    return [flat[at * width : (at + 1) * width] for at in range(len(groups))]


def choice(pairs, critic, slots):
    rows = pairs.shape[0]
    named = (pairs[:, 0:1] == critic) | (pairs[:, 1:2] == critic)
    named = jnp.broadcast_to(named.astype(jnp.float32), (rows, slots))
    before = lax.broadcasted_iota(jnp.int32, (rows, rows), 1) < lax.broadcasted_iota(jnp.int32, (rows, rows), 0)
    rank = inner_dot(before.astype(jnp.bfloat16), named.astype(jnp.bfloat16), 1, 0)
    at = lax.broadcasted_iota(jnp.int32, (rows, slots), 1).astype(jnp.float32)
    return jnp.where(rank == at, named, 0.0).astype(jnp.bfloat16)


def pick_kernel(pairs_ref, values_ref, out_ref):
    width, features, slots = out_ref.shape
    pairs = pairs_ref[...]
    chosen = [choice(pairs, critic, slots) for critic in range(width)]
    step = 512
    for start in range(0, features, step):
        part = values_ref[:, pl.ds(start, step)]
        for k in range(width):
            out_ref[k, pl.ds(start, step), :] = inner_dot(part, chosen[k], 0, 0).astype(jnp.bfloat16)


def run_pick(pairs, values, width, slots):
    rows, features = values.shape
    return pl.pallas_call(
        pick_kernel,
        in_specs=[INSIDE] * 2,
        out_specs=INSIDE,
        out_shape=shape_of((width, features, slots), jnp.bfloat16),
        compiler_params=pltpu.CompilerParams(vmem_limit_bytes=VMEM_LIMIT),
        cost_estimate=pl.CostEstimate(
            flops=2 * rows * features * slots * width, bytes_accessed=8 * rows * features, transcendentals=0
        ),
        name="pick",
    )(pairs, values)


def combine_kernel(pairs_ref, came_ref, out_ref):
    width, features, slots = came_ref.shape
    pairs = pairs_ref[...]
    chosen = [choice(pairs, critic, slots) for critic in range(width)]
    step = 512
    for start in range(0, features, step):
        total = sum(inner_dot(chosen[k], came_ref[k, pl.ds(start, step), :], 1, 1) for k in range(width))
        out_ref[:, pl.ds(start, step)] = (0.5 * total).astype(jnp.bfloat16)


def run_combine(pairs, came):
    rows = pairs.shape[0]
    return pl.pallas_call(
        combine_kernel,
        in_specs=[INSIDE] * 2,
        out_specs=INSIDE,
        out_shape=shape_of((rows, came.shape[1]), jnp.bfloat16),
        compiler_params=pltpu.CompilerParams(vmem_limit_bytes=VMEM_LIMIT),
        cost_estimate=pl.CostEstimate(
            flops=2 * rows * came.size, bytes_accessed=4 * came.size, transcendentals=0
        ),
        name="combine",
    )(pairs, came)


FORWARD_COST = 15_000_000_000
BACKWARD_COST = 18_000_000_000


def assemble_kernel(layers, factor, place_ref, *refs):
    count = 2 * len(layers)
    sources, (left_ref, right_ref) = refs[:count], refs[count : count + 2]
    held, wide, in_sems, out_sems = refs[count + 2 :]
    width, chunk = held.shape[1], held.shape[4]
    origin, core = place_ref[0] ^ place_ref[1], place_ref[2]
    arrivals = [
        pltpu.make_async_copy(source, held.at[at], in_sems.at[at]) for at, source in enumerate(sources)
    ]
    for copy in arrivals:
        copy.start()
    leaving = []
    for at in range(count):
        arrivals[at].wait()
        half = core if at % 2 == 0 else 1 - core
        for k in range(width):
            wide[at, k] = held[at, k].astype(jnp.float32) * factor
            start = (half * width + (origin ^ k)) * chunk
            for inside, layer in enumerate(layers[at // 2]):
                for which, target in enumerate((left_ref, right_ref)):
                    copy = pltpu.make_async_copy(
                        wide.at[at, k, inside, which],
                        target.at[layer, pl.ds(start, chunk)],
                        out_sems.at[len(leaving)],
                    )
                    copy.start()
                    leaving.append(copy)
    for copy in leaving:
        copy.wait()


def run_assemble(place, pieces, layers, factor):
    piece = pieces[0].shape
    layer_count = sum(len(group) for group in layers)
    out = shape_of((layer_count, 2 * piece[0] * piece[3]) + piece[4:], jnp.float32)
    return pl.pallas_call(
        lambda *refs: assemble_kernel(layers, factor, *refs),
        in_specs=[SMEM] + [OUTSIDE] * len(pieces),
        out_specs=[OUTSIDE] * 2,
        out_shape=[out] * 2,
        scratch_shapes=[
            pltpu.VMEM((len(pieces),) + piece, jnp.bfloat16),
            pltpu.VMEM((len(pieces),) + piece, jnp.float32),
            pltpu.SemaphoreType.DMA((len(pieces),)),
            pltpu.SemaphoreType.DMA((4 * layer_count * piece[0],)),
        ],
        compiler_params=pltpu.CompilerParams(vmem_limit_bytes=VMEM_LIMIT),
        cost_estimate=pl.CostEstimate(
            flops=0, bytes_accessed=6 * len(pieces) * math.prod(piece), transcendentals=0
        ),
        name="assemble",
    )(place, *pieces)


def plane_routes(width, replicas):
    bits = width.bit_length() - 1
    orders = [[(step + d) % bits for step in range(bits)] for d in range(replicas)]
    every = [(s, t, d) for s in range(width) for t in range(width) for d in range(replicas)]

    def route(move):
        def index(s, t, d):
            return (s * width + t) * replicas + d

        return [(index(*place), index(*move(*place))) for place in every]

    ranks = [[0] * width for _ in range(replicas)]
    for d in range(replicas):
        for r in range(width):
            ranks[d][sum(((r >> at) & 1) << orders[d][at] for at in range(bits))] = r
    return {
        "spread": [route(lambda s, t, d, j=j: (s ^ t ^ j, t, d)) for j in range(width)],
        "lift": [route(lambda s, t, d, j=j: (s, t ^ s ^ j, d)) for j in range(width)],
        "across": [route(lambda s, t, d, at=at: (s ^ (1 << orders[d][at]), t, d)) for at in range(bits)],
        "cores": route(lambda s, t, d: (s, t, 1 - d)),
        "sections": [route(lambda s, t, d, k=k: (s ^ k, t, d)) for k in range(width)],
        "planes": [route(lambda s, t, d, k=k: (s, t ^ k, d)) for k in range(width)],
        "homes": [route(lambda s, t, d, j=j: (t, t ^ s ^ j, d)) for j in range(width)],
    }, ranks


def plane_shards(patches, teacher, critic_pairs, left_factors, right_factors, norm_gains):
    width = lax.axis_size("section")
    replicas = lax.axis_size("dp")
    tok_rows, feat_local = patches.shape
    layer_count, local_blocks, size = left_factors.shape[1:4]
    blocks = feat_local * width // size
    wide = 2 * tok_rows // 3
    chunk = local_blocks // (replicas * width)
    layer_rows = 2 * chunk * size
    routes, ranks = plane_routes(width, replicas)
    section = lax.axis_index("section")
    tensor = lax.axis_index("tensor")
    core = lax.axis_index("dp")
    place = jnp.stack([section, tensor, core]).astype(jnp.int32)
    tie = lax.optimization_barrier

    def move(value, route):
        return lax.ppermute(value, AXES, route)

    def move_all(values, name):
        return [move(value, route) for value, route in zip(values, routes[name])]

    def send(values, name):
        return [values[0]] + [move(values[k], routes[name][k]) for k in range(1, width)]

    def gather_one(mine):
        return joined([mine, move(mine, routes["across"][0])])

    def gather_two(pair):
        return pair, move(pair, routes["across"][1]), move(pair, routes["cores"])

    def gather_three(pair, other, peer):
        return [pair, other, peer, move(other, routes["cores"])]

    def as_weights(parts):
        return [part.reshape(2 * width, -1, 2, chunk, size, size) for part in parts]

    block = jnp.arange(blocks, dtype=jnp.int32)
    inside = block % local_blocks
    replica = inside // (width * chunk)
    part = (replica != core).astype(jnp.int32)
    distance = section ^ ((inside // chunk) % width)
    piece = tensor ^ (section ^ distance) ^ (block // local_blocks)
    rank = jnp.array(ranks, jnp.int32)[replica, distance]
    table = jnp.stack(
        [
            ((part * width + rank) * width + piece) * chunk + inside % chunk,
            ((part * width + distance) * width + piece) * chunk + inside % chunk,
        ]
    ).astype(jnp.int32)

    def to_planes(value):
        return lax.all_to_all(value, "tensor", split_axis=0, concat_axis=0, tiled=True)

    factors = (left_factors[0], right_factors[0])
    groups = [tuple(range(0, 2)), tuple(range(2, layer_count))]
    gain_rows = norm_gains[0].reshape(-1, size)
    pieces = factor_pieces(place, *factors, gain_rows, groups, chunk)

    group_rows = [len(group) * layer_rows for group in groups]

    def lowest_of(came, at):
        return joined(came, group_rows[at]).reshape(width, group_rows[at], size)

    near = move_all(pieces[0], "spread")
    patch_sent = run_pick(critic_pairs, patches, width, wide)
    near, patch_sent, pieces[1] = tie((near, patch_sent, pieces[1]))
    patch_came = to_planes(patch_sent).reshape(-1, wide)
    came = move_all(near, "lift")
    far = move_all(pieces[1], "spread")
    came, far = tie((came, far))
    lowest = lowest_of(came, 0)
    beside = move(lowest, routes["across"][0])
    late = move_all(far, "lift")
    gains = jnp.stack([value[group_rows[0] :] for value in came])[jnp.arange(width) ^ section ^ tensor]
    gains = gains.reshape(width, layer_count + 1, feat_local).transpose(1, 0, 2).reshape(layer_count + 1, -1)
    lowest, beside, late, patch_came = tie((lowest, beside, late, patch_came))
    first_two = gather_two(joined([lowest, beside]))
    columns = [jnp.broadcast_to(gain[:, None], (gain.shape[0], wide)) for gain in gains]
    target_sent = run_pick(critic_pairs, teacher, width, wide)
    first_two, late, columns, target_sent = tie((first_two, late, columns, target_sent))
    weights = [as_weights(gather_three(*first_two))]
    later = gather_one(lowest_of(late, 1))

    residual = patch_came
    residual, weights, later = tie((residual, weights, later))
    flying = gather_two(later)
    sums = jnp.zeros((8, wide), jnp.float32)
    stored = []
    for layer in range(layer_count):
        group = 0 if layer in groups[0] else 1
        following, u, z, slope, scale, sums = run_forward(
            table, columns[layer], sums, residual, weights[group], layer - groups[group][0]
        )
        stored.append(((slope, z, u), scale, residual))
        residual = following
        if layer == 0:
            residual, sums, flying, target_sent = tie((residual, sums, flying, target_sent))
            weights.append(as_weights(gather_three(*flying)))
            target = to_planes(target_sent).reshape(-1, wide)
        if layer == groups[0][-1]:
            residual, sums, weights[1] = tie((residual, sums, weights[1]))

    def core_sum(mine, other):
        return (mine, move(other, routes["cores"]))

    def plane_sum(mine, other):
        return send(run_sum([(mine, other)], width), "sections")

    def homeward(parts):
        return move_all(run_sum(parts, width), "homes")

    def both_halves(parts):
        whole = joined(parts)
        return [part.reshape(width, -1, 2, chunk, size, size) for part in (whole, move(whole, routes["cores"]))]

    steps = (core_sum, plane_sum)
    gradient = residual
    underway = []
    for layer in range(layer_count - 1, -1, -1):
        turning = layer == layer_count - 1
        last = layer == 0
        kept, scale, inputs = stored[layer]
        group = 0 if layer in groups[0] else 1
        sources = (gradient, inputs, target) if turning else (gradient, inputs)
        underway = [(at + 1, steps[at](*state)) if at < len(steps) else (at, state) for at, state in underway]
        gradient, mine, other = run_backward(
            table,
            columns[layer],
            columns[layer_count],
            scale,
            kept,
            weights[group],
            layer - groups[group][0],
            sources,
            turning,
            last,
        )
        gradient, mine, other, states = tie((gradient, mine, other, [state for _, state in underway]))
        underway = [(at, state) for (at, _), state in zip(underway, states)]
        underway.append((0, (mine, other)))

    returned = to_planes(gradient.reshape(width, feat_local, wide))
    ended = [steps[at](*state) if at < len(steps) else state for at, state in underway][::-1]
    ended = tie(ended)
    ended[0] = plane_sum(*ended[0])
    homes_of = [None, homeward(ended[groups[1][0] :])]
    returned, ended[: groups[1][0]], homes_of[1] = tie((returned, ended[: groups[1][0]], homes_of[1]))
    home = homeward(ended[: groups[1][0]])
    homes_of[1] = both_halves(homes_of[1])
    d_patches = run_combine(critic_pairs, returned)
    d_patches, home, homes_of[1] = tie((d_patches, home, homes_of[1]))
    homes_of[0] = both_halves(home)
    grad_factor = 1.0 / math.sqrt(2 * tok_rows * width * replicas)
    grad_left, grad_right = run_assemble(place, homes_of[0] + homes_of[1], groups, grad_factor)
    return (d_patches, grad_left[None], grad_right[None])


def solution(mesh):
    in_specs = (
        P(("section", "dp"), "tensor"),
        P(("section", "dp"), "tensor"),
        P(("section", "dp"), None),
        P("section", None, "tensor", None, None),
        P("section", None, "tensor", None, None),
        P("section", None, "tensor"),
    )
    out_specs = (
        P(("section", "dp"), "tensor"),
        P("section", None, "tensor", None, None),
        P("section", None, "tensor", None, None),
    )
    body = plane_shards if planes_fit(mesh) else layered_shards
    return jax.shard_map(
        body, mesh=mesh, in_specs=in_specs, out_specs=out_specs, check_vma=False)
```

```python
import math

import jax
import jax.numpy as jnp
from jax import lax
from jax.experimental import pallas as pl
from jax.experimental.pallas import tpu as pltpu
from jax.sharding import PartitionSpec as P

EPSILON = 1e-06
TANH_SLOPE = 0.7978845608028654
CUBIC_TERM = 0.044715


def shifted(value, axis, steps):
    count = lax.axis_size(axis)
    first, last = (max(0, -steps), min(count, count - steps))
    return lax.ppermute(value, axis, [(source, source + steps) for source in range(first, last)])


def gelu_value(values):
    tangent = jnp.tanh(TANH_SLOPE * (values + CUBIC_TERM * values * values * values))
    return 0.5 * values * (1.0 + tangent)


def gelu_slope(values):
    tangent = jnp.tanh(TANH_SLOPE * (values + CUBIC_TERM * values * values * values))
    return 0.5 * (1.0 + tangent) + 0.5 * values * (1.0 - tangent * tangent) * TANH_SLOPE * (
        1.0 + 3.0 * CUBIC_TERM * values * values
    )


def norm_pair(residuals, gain_pair, model_width):
    squares = lax.psum(
        (
            jnp.sum(residuals[0] * residuals[0], axis=(1, 2)),
            jnp.sum(residuals[1] * residuals[1], axis=(1, 2)),
        ),
        "tensor",
    )
    factors = [lax.rsqrt(squares[member] / model_width + EPSILON) for member in range(2)]
    normed = [
        residuals[member] * factors[member][:, None, None] * gain_pair[member][None]
        for member in range(2)
    ]
    return (factors, normed)


def norm_back_pair(residuals, factors, gain_pair, grad_normed, carried, model_width):
    weighted = [grad_normed[member] * gain_pair[member][None] for member in range(2)]
    inners = lax.psum(
        (
            jnp.sum(weighted[0] * residuals[0], axis=(1, 2)),
            jnp.sum(weighted[1] * residuals[1], axis=(1, 2)),
        ),
        "tensor",
    )
    return [
        carried[member]
        + factors[member][:, None, None] * weighted[member]
        - residuals[member] * (factors[member] ** 3 * inners[member] / model_width)[:, None, None]
        for member in range(2)
    ]


def layered_shards(patches, teacher, critic_pairs, left_factors, right_factors, norm_gains):
    sections = lax.axis_size("section")
    tensor_width = lax.axis_size("tensor")
    replicas = lax.axis_size("dp")
    tok_rows = patches.shape[0]
    feat_local = patches.shape[1]
    layer_count = left_factors.shape[1]
    local_blocks = left_factors.shape[2]
    block_size = left_factors.shape[3]
    all_blocks = local_blocks * tensor_width
    fold_ratio = block_size // all_blocks
    model_width = feat_local * tensor_width
    sixth_rows = tok_rows // 6
    leading = 2 * sixth_rows
    critic_ids = jnp.arange(4, dtype=jnp.int32)
    named_by = (
        (critic_pairs[:, 0:1] == critic_ids[None, :])
        | (critic_pairs[:, 1:2] == critic_ids[None, :])
    ).astype(jnp.int32)
    ranking = jnp.cumsum(named_by, axis=0) - 1
    wide_ids = critic_ids[None, :] < 2
    slot_width = 3 * sixth_rows
    spilled = wide_ids & (ranking >= 3 * sixth_rows)
    destination = jnp.where(spilled, critic_ids[None, :] + 2, critic_ids[None, :])
    slot_index = jnp.where(spilled, ranking - sixth_rows, ranking)
    flat_slot = destination * slot_width + slot_index
    chosen = jnp.take_along_axis(flat_slot, critic_pairs, axis=1)
    slot_total = sections * slot_width
    row_ids = jnp.broadcast_to(jnp.arange(tok_rows, dtype=jnp.int32)[:, None], chosen.shape)
    source_row = (
        jnp.full((slot_total,), tok_rows, jnp.int32).at[chosen.reshape(-1)].set(row_ids.reshape(-1))
    )
    send_patch = (
        patches.at[source_row]
        .get(mode="fill", fill_value=0)
        .reshape(sections, slot_width, local_blocks, block_size)
    )
    send_target = (
        teacher.at[source_row]
        .get(mode="fill", fill_value=0)
        .reshape(sections, slot_width, local_blocks, block_size)
    )
    recv_patch, recv_target = (
        lax.all_to_all(send_patch, "section", split_axis=0, concat_axis=0, tiled=True),
        lax.all_to_all(send_target, "section", split_axis=0, concat_axis=0, tiled=True),
    )
    residuals = [
        recv_patch[:, :leading].reshape(-1, local_blocks, block_size).astype(jnp.float32),
        recv_patch[:, leading:].reshape(-1, local_blocks, block_size).astype(jnp.float32),
    ]
    targets = [
        recv_target[:, :leading].reshape(-1, local_blocks, block_size).astype(jnp.float32),
        recv_target[:, leading:].reshape(-1, local_blocks, block_size).astype(jnp.float32),
    ]
    native = (left_factors[0], right_factors[0], norm_gains[0])
    borrowed = shifted((left_factors, right_factors, norm_gains), "section", 2)
    is_wide = lax.axis_index("section") < 2
    second = (
        jnp.where(is_wide, left_factors, borrowed[0])[0],
        jnp.where(is_wide, right_factors, borrowed[1])[0],
        jnp.where(is_wide, norm_gains, borrowed[2])[0],
    )
    left_sets = (native[0], second[0])
    right_sets = (native[1], second[1])
    gain_sets = (
        native[2].astype(jnp.float32).reshape(layer_count + 1, local_blocks, block_size),
        second[2].astype(jnp.float32).reshape(layer_count + 1, local_blocks, block_size),
    )
    stored = []
    for layer_index in range(layer_count):
        gain_pair = [gain_sets[0][layer_index], gain_sets[1][layer_index]]
        factors, normed = norm_pair(residuals, gain_pair, model_width)
        normed = [normed[member].astype(jnp.bfloat16) for member in range(2)]
        first_out = [
            jnp.einsum(
                "nki,kij->nkj",
                normed[member],
                left_sets[member][layer_index],
                preferred_element_type=jnp.float32,
            ).astype(jnp.bfloat16)
            for member in range(2)
        ]
        permuted = (
            lax.all_to_all(first_out[0], "tensor", split_axis=2, concat_axis=1, tiled=True),
            lax.all_to_all(first_out[1], "tensor", split_axis=2, concat_axis=1, tiled=True),
        )
        permuted = [
            permuted[member].reshape(
                permuted[member].shape[0], all_blocks, local_blocks, fold_ratio
            )
            for member in range(2)
        ]
        right_quads = [
            right_sets[member][layer_index].reshape(
                local_blocks, fold_ratio, all_blocks, block_size
            )
            for member in range(2)
        ]
        mixture = [
            jnp.einsum(
                "nkmp,mpkl->nml",
                permuted[member],
                right_quads[member],
                preferred_element_type=jnp.float32,
            )
            for member in range(2)
        ]
        stored.append((residuals, factors, normed, permuted, mixture, right_quads, gain_pair))
        residuals = [residuals[member] + gelu_value(mixture[member]) for member in range(2)]
    final_gains = [gain_sets[0][layer_count], gain_sets[1][layer_count]]
    factors, outputs = norm_pair(residuals, final_gains, model_width)
    gradients = norm_back_pair(
        residuals,
        factors,
        final_gains,
        [outputs[member] - targets[member] for member in range(2)],
        [jnp.zeros_like(residuals[member]) for member in range(2)],
        model_width,
    )
    left_terms = []
    right_terms = []
    for layer_index in range(layer_count - 1, -1, -1):
        inputs, factors, normed, permuted, mixture, right_quads, gain_pair = stored[layer_index]
        slopes = [
            (gradients[member] * gelu_slope(mixture[member])).astype(jnp.bfloat16)
            for member in range(2)
        ]
        right_grad = [
            jnp.einsum(
                "nkmp,nml->mpkl",
                permuted[member],
                slopes[member],
                preferred_element_type=jnp.float32,
            ).reshape(local_blocks, block_size, block_size)
            for member in range(2)
        ]
        back_moved = [
            jnp.einsum(
                "nml,mpkl->nkmp",
                slopes[member],
                right_quads[member],
                preferred_element_type=jnp.float32,
            )
            .astype(jnp.bfloat16)
            .reshape(slopes[member].shape[0], all_blocks, local_blocks * fold_ratio)
            for member in range(2)
        ]
        arrived = (
            lax.all_to_all(back_moved[0], "tensor", split_axis=1, concat_axis=2, tiled=True),
            lax.all_to_all(back_moved[1], "tensor", split_axis=1, concat_axis=2, tiled=True),
        )
        left_grad = [
            jnp.einsum(
                "nki,nkj->kij", normed[member], arrived[member], preferred_element_type=jnp.float32
            )
            for member in range(2)
        ]
        grad_normed = [
            jnp.einsum(
                "nkj,kij->nki",
                arrived[member],
                left_sets[member][layer_index],
                preferred_element_type=jnp.float32,
            )
            for member in range(2)
        ]
        gradients = norm_back_pair(inputs, factors, gain_pair, grad_normed, gradients, model_width)
        layer_left = jnp.stack(left_grad)
        layer_right = jnp.stack(right_grad)
        layer_left, layer_right = (
            lax.psum(layer_left.astype(jnp.bfloat16), "dp").astype(jnp.float32),
            lax.psum(layer_right.astype(jnp.bfloat16), "dp").astype(jnp.float32),
        )
        left_terms.insert(0, layer_left)
        right_terms.insert(0, layer_right)
    left_stack = jnp.stack(left_terms)
    right_stack = jnp.stack(right_terms)
    repaid = (
        shifted(left_stack[:, 1].astype(jnp.bfloat16), "section", -2).astype(jnp.float32),
        shifted(right_stack[:, 1].astype(jnp.bfloat16), "section", -2).astype(jnp.float32),
    )
    is_wide = lax.axis_index("section") < 2
    left_total = left_stack[:, 0] + jnp.where(is_wide, left_stack[:, 1] + repaid[0], 0.0)
    right_total = right_stack[:, 0] + jnp.where(is_wide, right_stack[:, 1] + repaid[1], 0.0)
    grad_factor = 1.0 / math.sqrt(2 * tok_rows * sections * replicas)
    returned = [
        gradients[member].astype(jnp.bfloat16).reshape(sections, -1, local_blocks, block_size)
        for member in range(2)
    ]
    back_lead, back_trail = (
        lax.all_to_all(returned[0], "section", split_axis=0, concat_axis=0, tiled=True),
        lax.all_to_all(returned[1], "section", split_axis=0, concat_axis=0, tiled=True),
    )
    gathered = jnp.concatenate((back_lead, back_trail), axis=1).reshape(
        slot_total, local_blocks, block_size
    )
    combined = (
        gathered[chosen[:, 0]].astype(jnp.float32) + gathered[chosen[:, 1]].astype(jnp.float32)
    ) * 0.5
    d_patches = combined.astype(jnp.bfloat16).reshape(tok_rows, feat_local)
    return (d_patches, (left_total * grad_factor)[None], (right_total * grad_factor)[None])


VMEM_LIMIT = 60 * 1024 * 1024
CHUNKS = 8
PARTS = 4
SMALL = (16, 128)
AXES = ("section", "tensor", "dp")


def planes_fit(mesh):
    sections = mesh.shape["section"]
    paired = mesh.shape["dp"] == 2 and sections & (sections - 1) == 0
    return paired and mesh.shape["tensor"] == sections


def inner_dot(left, right, left_dim, right_dim):
    return lax.dot_general(
        left,
        right,
        (((left_dim,), (right_dim,)), ((), ())),
        preferred_element_type=jnp.float32,
    )


def fold_rows(values):
    return jnp.sum(values.reshape(values.shape[0] // 8, 8, values.shape[1]), axis=0)


def block_rows(block, size):
    return pl.ds(pl.multiple_of(block * size, size), size)


def chunk_copy(source, target, sems, chunk):
    rows = target.shape[0] // CHUNKS
    at = pl.ds(pl.multiple_of(chunk * rows, rows), rows)
    return pltpu.make_async_copy(source.at[at], target.at[at], sems.at[chunk])


def start_chunks(source, target, sems):
    for chunk in range(CHUNKS):
        chunk_copy(source, target, sems, chunk).start()


def wait_chunks(source, target, sems):
    for chunk in range(CHUNKS):
        chunk_copy(source, target, sems, chunk).wait()


def factor_copies(parts, layer, held, sems, side):
    count = parts[0].shape[0]
    return [
        pltpu.make_async_copy(
            ref.at[:, layer, side], held.at[pl.ds(at * count, count), side], sems.at[side, at]
        )
        for at, ref in enumerate(parts)
    ]


def gradient_copies(held, parts, sems, side):
    count = parts[0].shape[0]
    return [
        pltpu.make_async_copy(
            held.at[pl.ds(at * count, count), side], ref.at[:, side], sems.at[side, at]
        )
        for at, ref in enumerate(parts)
    ]


def by_chunk(blocks, step, carry, before=None, after=None):
    per_chunk = blocks // CHUNKS

    def one(chunk, carry):
        if before is not None:
            before(chunk)
        carry = lax.fori_loop(
            0, per_chunk, lambda at, now: step(chunk * per_chunk + at, now), carry, unroll=True
        )
        if after is not None:
            after(chunk)
        return carry

    return lax.fori_loop(0, CHUNKS, one, carry)


def forward_kernel(first, layer, inputs, table_ref, sums_ref, gain_ref, *refs):
    sources, refs = refs[:inputs], refs[inputs:]
    parts, sources = sources[:PARTS], sources[PARTS:]
    out_ref, u_ref, z_ref, slope_ref, scale_ref, next_ref = refs[:6]
    raw, h, w, u, z, slope, mid, gain, in_sems, gain_sems, w_sems, out_sems = refs[6:]
    features, slots = h.shape
    size = w.shape[-1]
    chunk_blocks = w.shape[2]
    blocks = features // size
    fold = size // blocks

    left_in = factor_copies(parts, layer, w, w_sems, 0)
    right_in = factor_copies(parts, layer, w, w_sems, 1)
    if first:
        start_chunks(sources[0], raw, in_sems)
        for copy in left_in:
            copy.start()
        start_chunks(gain_ref, gain, gain_sems)
        for copy in right_in:
            copy.start()

        def squares(block, total):
            rows = block_rows(block, size)
            part = raw[rows, :].astype(jnp.float32)
            h[rows, :] = part
            return total + fold_rows(part * part)

        total = by_chunk(
            blocks,
            squares,
            jnp.zeros((8, slots), jnp.float32),
            lambda chunk: chunk_copy(sources[0], raw, in_sems, chunk).wait(),
        )
    else:
        for copy in left_in:
            copy.start()
        start_chunks(sources[0], h, in_sems)
        start_chunks(gain_ref, gain, gain_sems)
        for copy in right_in:
            copy.start()
        total = sums_ref[...]
    scale = lax.rsqrt(jnp.sum(total, axis=0, keepdims=True) / features + EPSILON)
    scale_ref[...] = jnp.broadcast_to(scale, scale_ref.shape)
    for copy in left_in:
        copy.wait()

    def arrive(chunk):
        chunk_copy(gain_ref, gain, gain_sems, chunk).wait()
        if not first:
            chunk_copy(sources[0], h, in_sems, chunk).wait()

    def left(block, carry):
        rows = block_rows(block, size)
        place = table_ref[0, block]
        normed = (h[rows, :] * scale * gain[rows, :].astype(jnp.float32)).astype(jnp.bfloat16)
        u[rows, :] = normed
        weight = w[place // chunk_blocks, 0, place % chunk_blocks]
        mid[rows, :] = inner_dot(weight, normed, 0, 0)
        return carry

    def leave_left(chunk):
        chunk_copy(u, u_ref, out_sems.at[0], chunk).start()

    by_chunk(blocks, left, 0, arrive, leave_left)
    for copy in right_in:
        copy.wait()

    def right(block, total):
        rows = block_rows(block, size)
        place = table_ref[0, block]
        moved = [mid[pl.ds(q * blocks + block, blocks, stride=size), :] for q in range(fold)]
        moved = jnp.concatenate(moved, axis=0).astype(jnp.bfloat16)
        z[rows, :] = moved
        weight = w[place // chunk_blocks, 1, place % chunk_blocks]
        mixture = inner_dot(weight, moved, 0, 0)
        squared = mixture * mixture
        tangent = jnp.tanh(mixture * (TANH_SLOPE + (TANH_SLOPE * CUBIC_TERM) * squared))
        half = 0.5 + 0.5 * tangent
        following = h[rows, :] + mixture * half
        h[rows, :] = following
        steep = half + mixture * (1.0 - tangent * tangent) * (
            0.5 * TANH_SLOPE + (1.5 * TANH_SLOPE * CUBIC_TERM) * squared
        )
        slope[rows, :] = steep.astype(jnp.bfloat16)
        return total + fold_rows(following * following)

    leaving = ((h, out_ref, 1), (z, z_ref, 2), (slope, slope_ref, 3))

    def leave_right(chunk):
        for source, target, at in leaving:
            chunk_copy(source, target, out_sems.at[at], chunk).start()

    next_ref[...] = by_chunk(blocks, right, jnp.zeros((8, slots), jnp.float32), None, leave_right)
    for source, target, at in ((u, u_ref, 0),) + leaving:
        wait_chunks(source, target, out_sems.at[at])


def backward_kernel(turning, last, layer, inputs, table_ref, scale_ref, gain_ref, end_gain_ref, *refs):
    sources, refs = refs[:inputs], refs[inputs:]
    slope_ref, z_ref, u_ref = sources[:3]
    parts, sources = sources[3 : 3 + PARTS], sources[3 + PARTS :]
    out_ref, own_grad, peer_grad = refs[:3]
    g, slope, z, u, h, w, gw, mid, gain, top, goal, end_gain = refs[3:15]
    in_sems, w_sems, out_sems, gw_sems = refs[15:]
    features, slots = g.shape
    size = w.shape[-1]
    chunk_blocks = w.shape[2]
    blocks = features // size
    fold = size // blocks

    left_in = factor_copies(parts, layer, w, w_sems, 0)
    right_in = factor_copies(parts, layer, w, w_sems, 1)
    g_ref, h_ref = sources[:2]
    if turning:
        start_chunks(g_ref, top, in_sems.at[0])
        start_chunks(end_gain_ref, end_gain, in_sems.at[6])
        start_chunks(sources[2], goal, in_sems.at[5])
    else:
        start_chunks(g_ref, g, in_sems.at[0])
    for copy in right_in:
        copy.start()
    start_chunks(slope_ref, slope, in_sems.at[1])
    start_chunks(z_ref, z, in_sems.at[2])
    for copy in left_in:
        copy.start()
    start_chunks(u_ref, u, in_sems.at[3])
    start_chunks(gain_ref, gain, in_sems.at[7])
    start_chunks(h_ref, h, in_sems.at[4])

    if turning:
        zero = jnp.zeros((8, slots), jnp.float32)

        def sums(block, totals):
            rows = block_rows(block, size)
            part = top[rows, :]
            scaled = part * end_gain[rows, :].astype(jnp.float32)
            return (
                totals[0] + fold_rows(part * part),
                totals[1] + fold_rows(scaled * scaled),
                totals[2] + fold_rows(scaled * goal[rows, :].astype(jnp.float32)),
            )

        def arrive_top(chunk):
            chunk_copy(g_ref, top, in_sems.at[0], chunk).wait()
            chunk_copy(end_gain_ref, end_gain, in_sems.at[6], chunk).wait()
            chunk_copy(sources[2], goal, in_sems.at[5], chunk).wait()

        totals = by_chunk(blocks, sums, (zero, zero, zero), arrive_top)
        squares, gained, crossed = [jnp.sum(total, axis=0, keepdims=True) for total in totals]
        end_scale = lax.rsqrt(squares / features + EPSILON)
        end_back = end_scale * end_scale * end_scale * (end_scale * gained - crossed) / features

    for copy in right_in:
        copy.wait()

    def arrive_right(chunk):
        if not turning:
            chunk_copy(g_ref, g, in_sems.at[0], chunk).wait()
        chunk_copy(slope_ref, slope, in_sems.at[1], chunk).wait()
        chunk_copy(z_ref, z, in_sems.at[2], chunk).wait()

    def right(block, carry):
        rows = block_rows(block, size)
        place, home = table_ref[0, block], table_ref[1, block]
        at = (place // chunk_blocks, 1, place % chunk_blocks)
        to = (home // chunk_blocks, 1, home % chunk_blocks)
        if turning:
            part = top[rows, :]
            factor = end_gain[rows, :].astype(jnp.float32)
            error = (part * end_scale * factor - goal[rows, :].astype(jnp.float32)) * factor
            gradient = end_scale * error - part * end_back
            g[rows, :] = gradient
        else:
            gradient = g[rows, :]
        steep = (gradient * slope[rows, :].astype(jnp.float32)).astype(jnp.bfloat16)
        gw[to] = inner_dot(z[rows, :], steep, 1, 1).astype(jnp.bfloat16)
        mid[rows, :] = inner_dot(w[at], steep, 1, 0)
        return carry

    by_chunk(blocks, right, 0, arrive_right)
    right_out = gradient_copies(gw, (own_grad, peer_grad), gw_sems, 1)
    for copy in right_out:
        copy.start()
    for copy in left_in:
        copy.wait()
    scale = scale_ref[0:1, :]

    def arrive_left(chunk):
        chunk_copy(u_ref, u, in_sems.at[3], chunk).wait()
        chunk_copy(gain_ref, gain, in_sems.at[7], chunk).wait()
        chunk_copy(h_ref, h, in_sems.at[4], chunk).wait()

    def left(block, total):
        rows = block_rows(block, size)
        place, home = table_ref[0, block], table_ref[1, block]
        at = (place // chunk_blocks, 0, place % chunk_blocks)
        to = (home // chunk_blocks, 0, home % chunk_blocks)
        arrived = [mid[pl.ds(q * blocks + block, blocks, stride=size), :] for q in range(fold)]
        arrived = jnp.concatenate(arrived, axis=0).astype(jnp.bfloat16)
        gw[to] = inner_dot(u[rows, :], arrived, 1, 1).astype(jnp.bfloat16)
        weighted = inner_dot(w[at], arrived, 1, 0) * gain[rows, :].astype(jnp.float32)
        g[rows, :] = g[rows, :] + scale * weighted
        return total + fold_rows(weighted * h[rows, :].astype(jnp.float32))

    total = by_chunk(blocks, left, jnp.zeros((8, slots), jnp.float32), arrive_left)
    left_out = gradient_copies(gw, (own_grad, peer_grad), gw_sems, 0)
    for copy in left_out:
        copy.start()
    back = scale * scale * scale * jnp.sum(total, axis=0, keepdims=True) / features

    def finish(block, carry):
        rows = block_rows(block, size)
        ended = g[rows, :] - h[rows, :].astype(jnp.float32) * back
        if last:
            u[rows, :] = ended.astype(jnp.bfloat16)
        else:
            g[rows, :] = ended
        return carry

    ended = u if last else g
    by_chunk(blocks, finish, 0, None, lambda chunk: chunk_copy(ended, out_ref, out_sems, chunk).start())
    wait_chunks(ended, out_ref, out_sems)
    for copy in right_out + left_out:
        copy.wait()


def shape_of(shape, dtype):
    return jax.ShapeDtypeStruct(shape, dtype)


SMEM = pl.BlockSpec(memory_space=pltpu.SMEM)
INSIDE = pl.BlockSpec(memory_space=pltpu.VMEM)
OUTSIDE = pl.BlockSpec(memory_space=pl.ANY)


def run_forward(table, gain, sums, residual, weights, layer):
    first = residual.dtype == jnp.bfloat16
    whole = residual.shape
    sources = (*weights, residual)
    held = (PARTS * weights[0].shape[0],) + weights[0].shape[2:]
    out_shape = (
        shape_of(whole, jnp.float32),
        shape_of(whole, jnp.bfloat16),
        shape_of(whole, jnp.bfloat16),
        shape_of(whole, jnp.bfloat16),
        shape_of((8, whole[1]), jnp.float32),
        shape_of((8, whole[1]), jnp.float32),
    )
    return pl.pallas_call(
        lambda *refs: forward_kernel(first, layer, len(sources), *refs),
        in_specs=[SMEM, INSIDE, OUTSIDE] + [OUTSIDE] * len(sources),
        out_specs=[OUTSIDE] * 4 + [INSIDE] * 2,
        out_shape=out_shape,
        scratch_shapes=[
            pltpu.VMEM(whole if first else SMALL, jnp.bfloat16),
            pltpu.VMEM(whole, jnp.float32),
            pltpu.VMEM(held, jnp.bfloat16),
            pltpu.VMEM(whole, jnp.bfloat16),
            pltpu.VMEM(whole, jnp.bfloat16),
            pltpu.VMEM(whole, jnp.bfloat16),
            pltpu.VMEM(whole, jnp.float32),
            pltpu.VMEM(whole, jnp.bfloat16),
            pltpu.SemaphoreType.DMA((CHUNKS,)),
            pltpu.SemaphoreType.DMA((CHUNKS,)),
            pltpu.SemaphoreType.DMA((2, PARTS)),
            pltpu.SemaphoreType.DMA((4, CHUNKS)),
        ],
        compiler_params=pltpu.CompilerParams(vmem_limit_bytes=VMEM_LIMIT),
        cost_estimate=pl.CostEstimate(
            flops=FORWARD_COST, bytes_accessed=20 * whole[0] * whole[1], transcendentals=0
        ),
        name="forward_layer",
    )(table, sums, gain, *sources)


def run_backward(table, gain, end_gain, scale, kept, weights, layer, sources, turning, last):
    whole = kept[0].shape
    sources = (*kept, *weights, *sources)
    held = (PARTS * weights[0].shape[0],) + weights[0].shape[2:]
    half = (held[0] // 2,) + held[1:]
    out_shape = [shape_of(whole, jnp.bfloat16 if last else jnp.float32)] + [shape_of(half, jnp.bfloat16)] * 2
    return pl.pallas_call(
        lambda *refs: backward_kernel(turning, last, layer, len(sources), *refs),
        in_specs=[SMEM, INSIDE] + [OUTSIDE] * (2 + len(sources)),
        out_specs=[OUTSIDE] * len(out_shape),
        out_shape=out_shape,
        scratch_shapes=[
            pltpu.VMEM(whole, jnp.float32),
            pltpu.VMEM(whole, jnp.bfloat16),
            pltpu.VMEM(whole, jnp.bfloat16),
            pltpu.VMEM(whole, jnp.bfloat16),
            pltpu.VMEM(whole, jnp.bfloat16 if last else jnp.float32),
            pltpu.VMEM(held, jnp.bfloat16),
            pltpu.VMEM(held, jnp.bfloat16),
            pltpu.VMEM(whole, jnp.float32),
            pltpu.VMEM(whole, jnp.bfloat16),
            pltpu.VMEM(whole if turning else SMALL, jnp.float32),
            pltpu.VMEM(whole if turning else SMALL, jnp.bfloat16),
            pltpu.VMEM(whole if turning else SMALL, jnp.bfloat16),
            pltpu.SemaphoreType.DMA((8, CHUNKS)),
            pltpu.SemaphoreType.DMA((2, PARTS)),
            pltpu.SemaphoreType.DMA((CHUNKS,)),
            pltpu.SemaphoreType.DMA((2, PARTS)),
        ],
        compiler_params=pltpu.CompilerParams(vmem_limit_bytes=VMEM_LIMIT),
        cost_estimate=pl.CostEstimate(
            flops=BACKWARD_COST, bytes_accessed=30 * whole[0] * whole[1], transcendentals=0
        ),
        name="backward_layer",
    )(table, scale, gain, end_gain, *sources)


def join_kernel(rows, *refs):
    sources, whole, sems = refs[:-2], refs[-2], refs[-1]
    copies = [
        pltpu.make_async_copy(source.at[pl.ds(0, rows)], whole.at[pl.ds(at * rows, rows)], sems.at[at])
        for at, source in enumerate(sources)
    ]
    for copy in copies:
        copy.start()
    for copy in copies:
        copy.wait()


def joined(parts, rows=None):
    rows = parts[0].shape[0] if rows is None else rows
    whole = shape_of((rows * len(parts),) + parts[0].shape[1:], parts[0].dtype)
    return pl.pallas_call(
        lambda *refs: join_kernel(rows, *refs),
        in_specs=[OUTSIDE] * len(parts),
        out_specs=INSIDE,
        out_shape=whole,
        scratch_shapes=[pltpu.SemaphoreType.DMA((len(parts),))],
        compiler_params=pltpu.CompilerParams(vmem_limit_bytes=VMEM_LIMIT),
        cost_estimate=pl.CostEstimate(
            flops=0, bytes_accessed=4 * math.prod(whole.shape), transcendentals=0
        ),
        name="join",
    )(*parts)


def sum_kernel(terms, inputs, *refs):
    sources, outs = refs[:inputs], refs[inputs:]
    for group in range(inputs // terms):
        mine = sources[group * terms : (group + 1) * terms]
        for at, out in enumerate(outs):
            total = sum(ref[at].astype(jnp.float32) for ref in mine)
            out[group] = total.astype(jnp.bfloat16)


def run_sum(groups, outputs):
    flat = [term.reshape(outputs, -1, term.shape[-1]) for terms in groups for term in terms]
    _, rows, lanes = flat[0].shape
    steps = 4
    out_shape = [shape_of((len(groups), rows, lanes), jnp.bfloat16)] * outputs
    sums = pl.pallas_call(
        lambda *refs: sum_kernel(len(groups[0]), len(flat), *refs),
        grid=(steps,),
        in_specs=[pl.BlockSpec((outputs, rows // steps, lanes), lambda i: (0, i, 0))] * len(flat),
        out_specs=[pl.BlockSpec((len(groups), rows // steps, lanes), lambda i: (0, i, 0))] * outputs,
        out_shape=out_shape,
        compiler_params=pltpu.CompilerParams(vmem_limit_bytes=VMEM_LIMIT),
        cost_estimate=pl.CostEstimate(
            flops=flat[0].size * len(flat), bytes_accessed=2 * flat[0].size * (len(flat) + 1), transcendentals=0
        ),
        name="sum",
    )(*flat)
    return [out.reshape(-1, lanes) for out in sums]


def pieces_kernel(groups, chunk, place_ref, order_ref, left_ref, right_ref, gain_ref, *refs):
    outs, (held, left_sem, sems) = refs[:-3], refs[-3:]
    size = held.shape[-1]
    width = len(outs) // len(groups)
    half = held.shape[1]
    origin = place_ref[0] ^ place_ref[1]
    lefts = pltpu.make_async_copy(left_ref.at[:, pl.ds(place_ref[2] * half, half)], held, left_sem.at[0])
    lefts.start()
    copies = []
    turns = []
    for at, group in enumerate(groups):
        for j in range(width):
            out = outs[at * width + j]
            start = (origin ^ j) * chunk
            row = 0
            for layer in group:
                for inside in range(chunk):
                    turns.append((layer, start + inside, out, row))
                    row += size
                for inside in range(chunk):
                    source = right_ref.at[layer, place_ref[2] * half + start + inside]
                    copies.append((source, out.at[pl.ds(row, size)]))
                    row += size
            if group[0] == 0:
                copies.append((gain_ref, out.at[pl.ds(row, gain_ref.shape[0])]))
    copies = [
        pltpu.make_async_copy(source, target, sems.at[at]) for at, (source, target) in enumerate(copies)
    ]
    for copy in copies:
        copy.start()
    lefts.wait()
    for layer, block, out, row in turns:
        turned = inner_dot(held[layer, block], order_ref[...], 1, 0)
        out[pl.ds(row, size), :] = turned.astype(jnp.bfloat16)
    for copy in copies:
        copy.wait()


def factor_pieces(place, order, left, right, gain_rows, groups, chunk, width):
    layer_count, blocks, size = left.shape[:3]
    shapes = []
    for group in groups:
        rows = len(group) * 2 * chunk * size + (gain_rows.shape[0] if group[0] == 0 else 0)
        shapes += [shape_of((rows, size), jnp.bfloat16)] * width
    flat = pl.pallas_call(
        lambda *refs: pieces_kernel(groups, chunk, *refs),
        in_specs=[SMEM, INSIDE] + [OUTSIDE] * 3,
        out_specs=[INSIDE] * len(shapes),
        out_shape=shapes,
        scratch_shapes=[
            pltpu.VMEM((layer_count, blocks // 2, size, size), jnp.bfloat16),
            pltpu.SemaphoreType.DMA((1,)),
            pltpu.SemaphoreType.DMA((width * (layer_count * chunk + 1),)),
        ],
        compiler_params=pltpu.CompilerParams(vmem_limit_bytes=VMEM_LIMIT),
        cost_estimate=pl.CostEstimate(flops=left.size * size, bytes_accessed=4 * left.size, transcendentals=0),
        name="pieces",
    )(place, order, left, right, gain_rows)
    return [flat[at * width : (at + 1) * width] for at in range(len(groups))]


def choice(pairs, critic, slots):
    rows = pairs.shape[0]
    named = (pairs[:, 0:1] == critic) | (pairs[:, 1:2] == critic)
    named = jnp.broadcast_to(named.astype(jnp.float32), (rows, slots))
    before = lax.broadcasted_iota(jnp.int32, (rows, rows), 1) < lax.broadcasted_iota(jnp.int32, (rows, rows), 0)
    rank = inner_dot(before.astype(jnp.bfloat16), named.astype(jnp.bfloat16), 1, 0)
    at = lax.broadcasted_iota(jnp.int32, (rows, slots), 1).astype(jnp.float32)
    return jnp.where(rank == at, named, 0.0).astype(jnp.bfloat16)


def pick_kernel(pairs_ref, values_ref, out_ref):
    width, features, slots = out_ref.shape
    pairs = pairs_ref[...]
    chosen = [choice(pairs, critic, slots) for critic in range(width)]
    step = 512
    for start in range(0, features, step):
        part = values_ref[:, pl.ds(start, step)]
        for k in range(width):
            out_ref[k, pl.ds(start, step), :] = inner_dot(part, chosen[k], 0, 0).astype(jnp.bfloat16)


def run_pick(pairs, values, width, slots):
    rows, features = values.shape
    return pl.pallas_call(
        pick_kernel,
        in_specs=[INSIDE] * 2,
        out_specs=INSIDE,
        out_shape=shape_of((width, features, slots), jnp.bfloat16),
        compiler_params=pltpu.CompilerParams(vmem_limit_bytes=VMEM_LIMIT),
        cost_estimate=pl.CostEstimate(
            flops=2 * rows * features * slots * width, bytes_accessed=8 * rows * features, transcendentals=0
        ),
        name="pick",
    )(pairs, values)


def combine_kernel(pairs_ref, came_ref, out_ref):
    width, features, slots = came_ref.shape
    pairs = pairs_ref[...]
    chosen = [choice(pairs, critic, slots) for critic in range(width)]
    step = 512
    for start in range(0, features, step):
        total = sum(inner_dot(chosen[k], came_ref[k, pl.ds(start, step), :], 1, 1) for k in range(width))
        out_ref[:, pl.ds(start, step)] = (0.5 * total).astype(jnp.bfloat16)


def run_combine(pairs, came):
    rows = pairs.shape[0]
    return pl.pallas_call(
        combine_kernel,
        in_specs=[INSIDE] * 2,
        out_specs=INSIDE,
        out_shape=shape_of((rows, came.shape[1]), jnp.bfloat16),
        compiler_params=pltpu.CompilerParams(vmem_limit_bytes=VMEM_LIMIT),
        cost_estimate=pl.CostEstimate(
            flops=2 * rows * came.size, bytes_accessed=4 * came.size, transcendentals=0
        ),
        name="combine",
    )(pairs, came)


FORWARD_COST = 15_000_000_000
BACKWARD_COST = 18_000_000_000


def assemble_kernel(layers, factor, place_ref, order_ref, *refs):
    count = 2 * len(layers)
    sources, (left_ref, right_ref) = refs[:count], refs[count : count + 2]
    held, wide = refs[count + 2 : 2 * count + 2], refs[2 * count + 2 : 3 * count + 2]
    in_sems, out_sems = refs[3 * count + 2 :]
    origin, core = place_ref[0] ^ place_ref[1], place_ref[2]
    order = order_ref[...]
    arrivals = [
        pltpu.make_async_copy(source, held[at], in_sems.at[at]) for at, source in enumerate(sources)
    ]
    for copy in arrivals:
        copy.start()
    leaving = []
    for at in range(count):
        arrivals[at].wait()
        half = core if at % 2 == 0 else 1 - core
        width, _, _, chunk = held[at].shape[:4]
        for k in range(width):
            start = (half * width + (origin ^ k)) * chunk
            for inside, layer in enumerate(layers[at // 2]):
                for block in range(chunk):
                    left = inner_dot(held[at][k, inside, 0, block], order, 1, 1)
                    wide[at][k, inside, 0, block] = left * factor
                wide[at][k, inside, 1] = held[at][k, inside, 1].astype(jnp.float32) * factor
                for which, target in enumerate((left_ref, right_ref)):
                    copy = pltpu.make_async_copy(
                        wide[at].at[k, inside, which],
                        target.at[layer, pl.ds(start, chunk)],
                        out_sems.at[len(leaving)],
                    )
                    copy.start()
                    leaving.append(copy)
    for copy in leaving:
        copy.wait()


def run_assemble(place, order, pieces, layers, factor):
    piece = pieces[0].shape
    layer_count = sum(len(group) for group in layers)
    out = shape_of((layer_count, 2 * piece[0] * piece[3]) + piece[4:], jnp.float32)
    return pl.pallas_call(
        lambda *refs: assemble_kernel(layers, factor, *refs),
        in_specs=[SMEM, INSIDE] + [OUTSIDE] * len(pieces),
        out_specs=[OUTSIDE] * 2,
        out_shape=[out] * 2,
        scratch_shapes=[pltpu.VMEM(part.shape, jnp.bfloat16) for part in pieces]
        + [pltpu.VMEM(part.shape, jnp.float32) for part in pieces]
        + [
            pltpu.SemaphoreType.DMA((len(pieces),)),
            pltpu.SemaphoreType.DMA((4 * layer_count * piece[0],)),
        ],
        compiler_params=pltpu.CompilerParams(vmem_limit_bytes=VMEM_LIMIT),
        cost_estimate=pl.CostEstimate(flops=0, bytes_accessed=4 * math.prod(out.shape) * 3, transcendentals=0),
        name="assemble",
    )(place, order, *pieces)


def plane_routes(width, replicas):
    bits = width.bit_length() - 1
    orders = [[(step + d) % bits for step in range(bits)] for d in range(replicas)]
    every = [(s, t, d) for s in range(width) for t in range(width) for d in range(replicas)]

    def route(move):
        def index(s, t, d):
            return (s * width + t) * replicas + d

        return [(index(*place), index(*move(*place))) for place in every]

    ranks = [[0] * width for _ in range(replicas)]
    for d in range(replicas):
        for r in range(width):
            ranks[d][sum(((r >> at) & 1) << orders[d][at] for at in range(bits))] = r
    return {
        "spread": [route(lambda s, t, d, j=j: (s ^ t ^ j, t, d)) for j in range(width)],
        "lift": [route(lambda s, t, d, j=j: (s, t ^ s ^ j, d)) for j in range(width)],
        "across": [route(lambda s, t, d, at=at: (s ^ (1 << orders[d][at]), t, d)) for at in range(bits)],
        "cores": route(lambda s, t, d: (s, t, 1 - d)),
        "sections": [route(lambda s, t, d, k=k: (s ^ k, t, d)) for k in range(width)],
        "planes": [route(lambda s, t, d, k=k: (s, t ^ k, d)) for k in range(width)],
        "homes": [route(lambda s, t, d, j=j: (t, t ^ s ^ j, d)) for j in range(width)],
    }, ranks


def plane_shards(patches, teacher, critic_pairs, left_factors, right_factors, norm_gains):
    width = lax.axis_size("section")
    replicas = lax.axis_size("dp")
    tok_rows, feat_local = patches.shape
    layer_count, local_blocks, size = left_factors.shape[1:4]
    blocks = feat_local * width // size
    wide = 2 * tok_rows // 3
    chunk = local_blocks // (replicas * width)
    layer_rows = 2 * chunk * size
    routes, ranks = plane_routes(width, replicas)
    section = lax.axis_index("section")
    tensor = lax.axis_index("tensor")
    core = lax.axis_index("dp")
    place = jnp.stack([section, tensor, core]).astype(jnp.int32)
    tie = lax.optimization_barrier

    def move(value, route):
        return lax.ppermute(value, AXES, route)

    def move_all(values, name):
        return [move(value, route) for value, route in zip(values, routes[name])]

    def send(values, name):
        return [values[0]] + [move(values[k], routes[name][k]) for k in range(1, width)]

    def gather_one(mine):
        return joined([mine, move(mine, routes["across"][0])])

    def gather_two(pair):
        return pair, move(pair, routes["across"][1]), move(pair, routes["cores"])

    def gather_three(pair, other, peer):
        return [pair, other, peer, move(other, routes["cores"])]

    def as_weights(parts):
        return [part.reshape(2 * width, -1, 2, chunk, size, size) for part in parts]

    block = jnp.arange(blocks, dtype=jnp.int32)
    inside = block % local_blocks
    replica = inside // (width * chunk)
    part = (replica != core).astype(jnp.int32)
    distance = section ^ ((inside // chunk) % width)
    piece = tensor ^ (section ^ distance) ^ (block // local_blocks)
    rank = jnp.array(ranks, jnp.int32)[replica, distance]
    table = jnp.stack(
        [
            ((part * width + rank) * width + piece) * chunk + inside % chunk,
            ((part * width + distance) * width + piece) * chunk + inside % chunk,
        ]
    ).astype(jnp.int32)

    def to_planes(value):
        return lax.all_to_all(value, "tensor", split_axis=0, concat_axis=0, tiled=True)

    factors = (left_factors[0], right_factors[0])
    groups = [tuple(range(0, 2)), tuple(range(2, layer_count))]
    gain_rows = norm_gains[0].reshape(-1, size)
    fold = size // blocks
    columns = jnp.arange(size)
    order = (columns[:, None] == (columns % blocks) * fold + columns // blocks).astype(jnp.bfloat16)
    pieces = factor_pieces(place, order, *factors, gain_rows, groups, chunk, width)

    group_rows = [len(group) * layer_rows for group in groups]

    def lowest_of(came, at):
        return joined(came, group_rows[at]).reshape(width, group_rows[at], size)

    near = move_all(pieces[0], "spread")
    patch_sent = run_pick(critic_pairs, patches, width, wide)
    near, patch_sent, pieces[1] = tie((near, patch_sent, pieces[1]))
    came = move_all(near, "lift")
    far = move_all(pieces[1], "spread")
    came, far, patch_sent = tie((came, far, patch_sent))
    lowest = lowest_of(came, 0)
    beside = move(lowest, routes["across"][0])
    late = move_all(far, "lift")
    gains = jnp.stack([value[group_rows[0] :] for value in came])[jnp.arange(width) ^ section ^ tensor]
    gains = gains.reshape(width, layer_count + 1, feat_local).transpose(1, 0, 2).reshape(layer_count + 1, -1)
    columns = [jnp.broadcast_to(gain[:, None], (gain.shape[0], wide)) for gain in gains]
    lowest, beside, late, columns, patch_sent = tie((lowest, beside, late, columns, patch_sent))
    patch_came = to_planes(patch_sent).reshape(-1, wide)
    first_two = gather_two(joined([lowest, beside]))
    target_sent = run_pick(critic_pairs, teacher, width, wide)
    first_two, late, target_sent = tie((first_two, late, target_sent))
    weights = [as_weights(gather_three(*first_two))]
    later = lowest_of(late, 1)
    later = (later, move(later, routes["across"][0]))
    weights, later, patch_came = tie((weights, later, patch_came))

    residual = patch_came
    flying = gather_two(joined(list(later)))
    sums = jnp.zeros((8, wide), jnp.float32)
    stored = []
    for layer in range(layer_count):
        group = 0 if layer in groups[0] else 1
        following, u, z, slope, scale, sums = run_forward(
            table, columns[layer], sums, residual, weights[group], layer - groups[group][0]
        )
        stored.append(((slope, z, u), scale, residual))
        residual = following
        if layer == 0:
            residual, sums, flying, target_sent = tie((residual, sums, flying, target_sent))
            weights.append(as_weights(gather_three(*flying)))
            target = to_planes(target_sent).reshape(-1, wide)
        if layer == groups[0][-1]:
            residual, sums, weights[1] = tie((residual, sums, weights[1]))

    def core_sum(mine, other):
        return (mine, move(other, routes["cores"]))

    def plane_sum(mine, other):
        return send(run_sum([(mine, other)], width), "sections")

    def homeward(parts):
        return move_all(run_sum(parts, width), "homes")

    def both_halves(parts):
        whole = joined(parts)
        return [part.reshape(width, -1, 2, chunk, size, size) for part in (whole, move(whole, routes["cores"]))]

    steps = (core_sum, plane_sum)
    gradient = residual
    underway = []
    for layer in range(layer_count - 1, -1, -1):
        turning = layer == layer_count - 1
        last = layer == 0
        kept, scale, inputs = stored[layer]
        group = 0 if layer in groups[0] else 1
        sources = (gradient, inputs, target) if turning else (gradient, inputs)
        underway = [(at + 1, steps[at](*state)) if at < len(steps) else (at, state) for at, state in underway]
        gradient, mine, other = run_backward(
            table,
            columns[layer],
            columns[layer_count],
            scale,
            kept,
            weights[group],
            layer - groups[group][0],
            sources,
            turning,
            last,
        )
        gradient, mine, other, states = tie((gradient, mine, other, [state for _, state in underway]))
        underway = [(at, state) for (at, _), state in zip(underway, states)]
        underway.append((0, (mine, other)))

    returned = to_planes(gradient.reshape(width, feat_local, wide))
    ended = [steps[at](*state) if at < len(steps) else state for at, state in underway][::-1]
    ended = tie(ended)
    ended[0] = plane_sum(*ended[0])
    homes_of = [None, homeward(ended[1:])]
    ended[0], homes_of[1], returned = tie((ended[0], homes_of[1], returned))
    home = homeward(ended[:1])
    homes_of[1] = both_halves(homes_of[1])
    d_patches = run_combine(critic_pairs, returned)
    d_patches, home, homes_of[1] = tie((d_patches, home, homes_of[1]))
    homes_of[0] = both_halves(home)
    grad_factor = 1.0 / math.sqrt(2 * tok_rows * width * replicas)
    grad_left, grad_right = run_assemble(
        place, order, homes_of[0] + homes_of[1], [(0,), tuple(range(1, layer_count))], grad_factor
    )
    return (d_patches, grad_left[None], grad_right[None])


def solution(mesh):
    in_specs = (
        P(("section", "dp"), "tensor"),
        P(("section", "dp"), "tensor"),
        P(("section", "dp"), None),
        P("section", None, "tensor", None, None),
        P("section", None, "tensor", None, None),
        P("section", None, "tensor"),
    )
    out_specs = (
        P(("section", "dp"), "tensor"),
        P("section", None, "tensor", None, None),
        P("section", None, "tensor", None, None),
    )
    body = plane_shards if planes_fit(mesh) else layered_shards
    return jax.shard_map(
        body, mesh=mesh, in_specs=in_specs, out_specs=out_specs, check_vma=False)
```

```python
import math

import jax
import jax.numpy as jnp
from jax import lax
from jax.experimental import pallas as pl
from jax.experimental.pallas import tpu as pltpu
from jax.sharding import PartitionSpec as P

EPSILON = 1e-06
TANH_SLOPE = 0.7978845608028654
CUBIC_TERM = 0.044715


def shifted(value, axis, steps):
    count = lax.axis_size(axis)
    first, last = (max(0, -steps), min(count, count - steps))
    return lax.ppermute(value, axis, [(source, source + steps) for source in range(first, last)])


def gelu_value(values):
    tangent = jnp.tanh(TANH_SLOPE * (values + CUBIC_TERM * values * values * values))
    return 0.5 * values * (1.0 + tangent)


def gelu_slope(values):
    tangent = jnp.tanh(TANH_SLOPE * (values + CUBIC_TERM * values * values * values))
    return 0.5 * (1.0 + tangent) + 0.5 * values * (1.0 - tangent * tangent) * TANH_SLOPE * (
        1.0 + 3.0 * CUBIC_TERM * values * values
    )


def norm_pair(residuals, gain_pair, model_width):
    squares = lax.psum(
        (
            jnp.sum(residuals[0] * residuals[0], axis=(1, 2)),
            jnp.sum(residuals[1] * residuals[1], axis=(1, 2)),
        ),
        "tensor",
    )
    factors = [lax.rsqrt(squares[member] / model_width + EPSILON) for member in range(2)]
    normed = [
        residuals[member] * factors[member][:, None, None] * gain_pair[member][None]
        for member in range(2)
    ]
    return (factors, normed)


def norm_back_pair(residuals, factors, gain_pair, grad_normed, carried, model_width):
    weighted = [grad_normed[member] * gain_pair[member][None] for member in range(2)]
    inners = lax.psum(
        (
            jnp.sum(weighted[0] * residuals[0], axis=(1, 2)),
            jnp.sum(weighted[1] * residuals[1], axis=(1, 2)),
        ),
        "tensor",
    )
    return [
        carried[member]
        + factors[member][:, None, None] * weighted[member]
        - residuals[member] * (factors[member] ** 3 * inners[member] / model_width)[:, None, None]
        for member in range(2)
    ]


def layered_shards(patches, teacher, critic_pairs, left_factors, right_factors, norm_gains):
    sections = lax.axis_size("section")
    tensor_width = lax.axis_size("tensor")
    replicas = lax.axis_size("dp")
    tok_rows = patches.shape[0]
    feat_local = patches.shape[1]
    layer_count = left_factors.shape[1]
    local_blocks = left_factors.shape[2]
    block_size = left_factors.shape[3]
    all_blocks = local_blocks * tensor_width
    fold_ratio = block_size // all_blocks
    model_width = feat_local * tensor_width
    sixth_rows = tok_rows // 6
    leading = 2 * sixth_rows
    critic_ids = jnp.arange(4, dtype=jnp.int32)
    named_by = (
        (critic_pairs[:, 0:1] == critic_ids[None, :])
        | (critic_pairs[:, 1:2] == critic_ids[None, :])
    ).astype(jnp.int32)
    ranking = jnp.cumsum(named_by, axis=0) - 1
    wide_ids = critic_ids[None, :] < 2
    slot_width = 3 * sixth_rows
    spilled = wide_ids & (ranking >= 3 * sixth_rows)
    destination = jnp.where(spilled, critic_ids[None, :] + 2, critic_ids[None, :])
    slot_index = jnp.where(spilled, ranking - sixth_rows, ranking)
    flat_slot = destination * slot_width + slot_index
    chosen = jnp.take_along_axis(flat_slot, critic_pairs, axis=1)
    slot_total = sections * slot_width
    row_ids = jnp.broadcast_to(jnp.arange(tok_rows, dtype=jnp.int32)[:, None], chosen.shape)
    source_row = (
        jnp.full((slot_total,), tok_rows, jnp.int32).at[chosen.reshape(-1)].set(row_ids.reshape(-1))
    )
    send_patch = (
        patches.at[source_row]
        .get(mode="fill", fill_value=0)
        .reshape(sections, slot_width, local_blocks, block_size)
    )
    send_target = (
        teacher.at[source_row]
        .get(mode="fill", fill_value=0)
        .reshape(sections, slot_width, local_blocks, block_size)
    )
    recv_patch, recv_target = (
        lax.all_to_all(send_patch, "section", split_axis=0, concat_axis=0, tiled=True),
        lax.all_to_all(send_target, "section", split_axis=0, concat_axis=0, tiled=True),
    )
    residuals = [
        recv_patch[:, :leading].reshape(-1, local_blocks, block_size).astype(jnp.float32),
        recv_patch[:, leading:].reshape(-1, local_blocks, block_size).astype(jnp.float32),
    ]
    targets = [
        recv_target[:, :leading].reshape(-1, local_blocks, block_size).astype(jnp.float32),
        recv_target[:, leading:].reshape(-1, local_blocks, block_size).astype(jnp.float32),
    ]
    native = (left_factors[0], right_factors[0], norm_gains[0])
    borrowed = shifted((left_factors, right_factors, norm_gains), "section", 2)
    is_wide = lax.axis_index("section") < 2
    second = (
        jnp.where(is_wide, left_factors, borrowed[0])[0],
        jnp.where(is_wide, right_factors, borrowed[1])[0],
        jnp.where(is_wide, norm_gains, borrowed[2])[0],
    )
    left_sets = (native[0], second[0])
    right_sets = (native[1], second[1])
    gain_sets = (
        native[2].astype(jnp.float32).reshape(layer_count + 1, local_blocks, block_size),
        second[2].astype(jnp.float32).reshape(layer_count + 1, local_blocks, block_size),
    )
    stored = []
    for layer_index in range(layer_count):
        gain_pair = [gain_sets[0][layer_index], gain_sets[1][layer_index]]
        factors, normed = norm_pair(residuals, gain_pair, model_width)
        normed = [normed[member].astype(jnp.bfloat16) for member in range(2)]
        first_out = [
            jnp.einsum(
                "nki,kij->nkj",
                normed[member],
                left_sets[member][layer_index],
                preferred_element_type=jnp.float32,
            ).astype(jnp.bfloat16)
            for member in range(2)
        ]
        permuted = (
            lax.all_to_all(first_out[0], "tensor", split_axis=2, concat_axis=1, tiled=True),
            lax.all_to_all(first_out[1], "tensor", split_axis=2, concat_axis=1, tiled=True),
        )
        permuted = [
            permuted[member].reshape(
                permuted[member].shape[0], all_blocks, local_blocks, fold_ratio
            )
            for member in range(2)
        ]
        right_quads = [
            right_sets[member][layer_index].reshape(
                local_blocks, fold_ratio, all_blocks, block_size
            )
            for member in range(2)
        ]
        mixture = [
            jnp.einsum(
                "nkmp,mpkl->nml",
                permuted[member],
                right_quads[member],
                preferred_element_type=jnp.float32,
            )
            for member in range(2)
        ]
        stored.append((residuals, factors, normed, permuted, mixture, right_quads, gain_pair))
        residuals = [residuals[member] + gelu_value(mixture[member]) for member in range(2)]
    final_gains = [gain_sets[0][layer_count], gain_sets[1][layer_count]]
    factors, outputs = norm_pair(residuals, final_gains, model_width)
    gradients = norm_back_pair(
        residuals,
        factors,
        final_gains,
        [outputs[member] - targets[member] for member in range(2)],
        [jnp.zeros_like(residuals[member]) for member in range(2)],
        model_width,
    )
    left_terms = []
    right_terms = []
    for layer_index in range(layer_count - 1, -1, -1):
        inputs, factors, normed, permuted, mixture, right_quads, gain_pair = stored[layer_index]
        slopes = [
            (gradients[member] * gelu_slope(mixture[member])).astype(jnp.bfloat16)
            for member in range(2)
        ]
        right_grad = [
            jnp.einsum(
                "nkmp,nml->mpkl",
                permuted[member],
                slopes[member],
                preferred_element_type=jnp.float32,
            ).reshape(local_blocks, block_size, block_size)
            for member in range(2)
        ]
        back_moved = [
            jnp.einsum(
                "nml,mpkl->nkmp",
                slopes[member],
                right_quads[member],
                preferred_element_type=jnp.float32,
            )
            .astype(jnp.bfloat16)
            .reshape(slopes[member].shape[0], all_blocks, local_blocks * fold_ratio)
            for member in range(2)
        ]
        arrived = (
            lax.all_to_all(back_moved[0], "tensor", split_axis=1, concat_axis=2, tiled=True),
            lax.all_to_all(back_moved[1], "tensor", split_axis=1, concat_axis=2, tiled=True),
        )
        left_grad = [
            jnp.einsum(
                "nki,nkj->kij", normed[member], arrived[member], preferred_element_type=jnp.float32
            )
            for member in range(2)
        ]
        grad_normed = [
            jnp.einsum(
                "nkj,kij->nki",
                arrived[member],
                left_sets[member][layer_index],
                preferred_element_type=jnp.float32,
            )
            for member in range(2)
        ]
        gradients = norm_back_pair(inputs, factors, gain_pair, grad_normed, gradients, model_width)
        layer_left = jnp.stack(left_grad)
        layer_right = jnp.stack(right_grad)
        layer_left, layer_right = (
            lax.psum(layer_left.astype(jnp.bfloat16), "dp").astype(jnp.float32),
            lax.psum(layer_right.astype(jnp.bfloat16), "dp").astype(jnp.float32),
        )
        left_terms.insert(0, layer_left)
        right_terms.insert(0, layer_right)
    left_stack = jnp.stack(left_terms)
    right_stack = jnp.stack(right_terms)
    repaid = (
        shifted(left_stack[:, 1].astype(jnp.bfloat16), "section", -2).astype(jnp.float32),
        shifted(right_stack[:, 1].astype(jnp.bfloat16), "section", -2).astype(jnp.float32),
    )
    is_wide = lax.axis_index("section") < 2
    left_total = left_stack[:, 0] + jnp.where(is_wide, left_stack[:, 1] + repaid[0], 0.0)
    right_total = right_stack[:, 0] + jnp.where(is_wide, right_stack[:, 1] + repaid[1], 0.0)
    grad_factor = 1.0 / math.sqrt(2 * tok_rows * sections * replicas)
    returned = [
        gradients[member].astype(jnp.bfloat16).reshape(sections, -1, local_blocks, block_size)
        for member in range(2)
    ]
    back_lead, back_trail = (
        lax.all_to_all(returned[0], "section", split_axis=0, concat_axis=0, tiled=True),
        lax.all_to_all(returned[1], "section", split_axis=0, concat_axis=0, tiled=True),
    )
    gathered = jnp.concatenate((back_lead, back_trail), axis=1).reshape(
        slot_total, local_blocks, block_size
    )
    combined = (
        gathered[chosen[:, 0]].astype(jnp.float32) + gathered[chosen[:, 1]].astype(jnp.float32)
    ) * 0.5
    d_patches = combined.astype(jnp.bfloat16).reshape(tok_rows, feat_local)
    return (d_patches, (left_total * grad_factor)[None], (right_total * grad_factor)[None])


VMEM_LIMIT = 60 * 1024 * 1024
CHUNKS = 8
PARTS = 4
SMALL = (16, 128)
AXES = ("section", "tensor", "dp")


def planes_fit(mesh):
    sections = mesh.shape["section"]
    paired = mesh.shape["dp"] == 2 and sections & (sections - 1) == 0
    return paired and mesh.shape["tensor"] == sections


def inner_dot(left, right, left_dim, right_dim):
    return lax.dot_general(
        left,
        right,
        (((left_dim,), (right_dim,)), ((), ())),
        preferred_element_type=jnp.float32,
    )


def fold_rows(values):
    return jnp.sum(values.reshape(values.shape[0] // 8, 8, values.shape[1]), axis=0)


def block_rows(block, size):
    return pl.ds(pl.multiple_of(block * size, size), size)


def chunk_copy(source, target, sems, chunk):
    rows = target.shape[0] // CHUNKS
    at = pl.ds(pl.multiple_of(chunk * rows, rows), rows)
    return pltpu.make_async_copy(source.at[at], target.at[at], sems.at[chunk])


def start_chunks(source, target, sems):
    for chunk in range(CHUNKS):
        chunk_copy(source, target, sems, chunk).start()


def wait_chunks(source, target, sems):
    for chunk in range(CHUNKS):
        chunk_copy(source, target, sems, chunk).wait()


def factor_copies(parts, layer, held, sems, side):
    count = parts[0].shape[0]
    return [
        pltpu.make_async_copy(
            ref.at[:, layer, side], held.at[pl.ds(at * count, count), side], sems.at[side, at]
        )
        for at, ref in enumerate(parts)
    ]


def gradient_copies(held, parts, sems, side):
    count = parts[0].shape[0]
    return [
        pltpu.make_async_copy(
            held.at[pl.ds(at * count, count), side], ref.at[:, side], sems.at[side, at]
        )
        for at, ref in enumerate(parts)
    ]


def by_chunk(blocks, step, carry, before=None, after=None):
    per_chunk = blocks // CHUNKS

    def one(chunk, carry):
        if before is not None:
            before(chunk)
        carry = lax.fori_loop(
            0, per_chunk, lambda at, now: step(chunk * per_chunk + at, now), carry, unroll=True
        )
        if after is not None:
            after(chunk)
        return carry

    return lax.fori_loop(0, CHUNKS, one, carry)


def forward_kernel(first, layer, inputs, table_ref, sums_ref, gain_ref, *refs):
    sources, refs = refs[:inputs], refs[inputs:]
    parts, sources = sources[:PARTS], sources[PARTS:]
    out_ref, u_ref, z_ref, slope_ref, scale_ref, next_ref = refs[:6]
    raw, h, w, u, z, slope, mid, gain, in_sems, gain_sems, w_sems, out_sems = refs[6:]
    features, slots = h.shape
    size = w.shape[-1]
    chunk_blocks = w.shape[2]
    blocks = features // size
    fold = size // blocks

    left_in = factor_copies(parts, layer, w, w_sems, 0)
    right_in = factor_copies(parts, layer, w, w_sems, 1)
    if first:
        start_chunks(sources[0], raw, in_sems)
        for copy in left_in:
            copy.start()
        start_chunks(gain_ref, gain, gain_sems)
        for copy in right_in:
            copy.start()

        def squares(block, total):
            rows = block_rows(block, size)
            part = raw[rows, :].astype(jnp.float32)
            h[rows, :] = part
            return total + fold_rows(part * part)

        total = by_chunk(
            blocks,
            squares,
            jnp.zeros((8, slots), jnp.float32),
            lambda chunk: chunk_copy(sources[0], raw, in_sems, chunk).wait(),
        )
    else:
        for copy in left_in:
            copy.start()
        start_chunks(sources[0], h, in_sems)
        start_chunks(gain_ref, gain, gain_sems)
        for copy in right_in:
            copy.start()
        total = sums_ref[...]
    scale = lax.rsqrt(jnp.sum(total, axis=0, keepdims=True) / features + EPSILON)
    scale_ref[...] = jnp.broadcast_to(scale, scale_ref.shape)
    for copy in left_in:
        copy.wait()

    def arrive(chunk):
        chunk_copy(gain_ref, gain, gain_sems, chunk).wait()
        if not first:
            chunk_copy(sources[0], h, in_sems, chunk).wait()

    def left(block, carry):
        rows = block_rows(block, size)
        place = table_ref[0, block]
        normed = (h[rows, :] * scale * gain[rows, :].astype(jnp.float32)).astype(jnp.bfloat16)
        u[rows, :] = normed
        weight = w[place // chunk_blocks, 0, place % chunk_blocks]
        mid[rows, :] = inner_dot(weight, normed, 0, 0)
        return carry

    def leave_left(chunk):
        chunk_copy(u, u_ref, out_sems.at[0], chunk).start()

    by_chunk(blocks, left, 0, arrive, leave_left)
    for copy in right_in:
        copy.wait()

    def right(block, total):
        rows = block_rows(block, size)
        place = table_ref[0, block]
        moved = [mid[pl.ds(q * blocks + block, blocks, stride=size), :] for q in range(fold)]
        moved = jnp.concatenate(moved, axis=0).astype(jnp.bfloat16)
        z[rows, :] = moved
        weight = w[place // chunk_blocks, 1, place % chunk_blocks]
        mixture = inner_dot(weight, moved, 0, 0)
        squared = mixture * mixture
        tangent = jnp.tanh(mixture * (TANH_SLOPE + (TANH_SLOPE * CUBIC_TERM) * squared))
        half = 0.5 + 0.5 * tangent
        following = h[rows, :] + mixture * half
        h[rows, :] = following
        steep = half + mixture * (1.0 - tangent * tangent) * (
            0.5 * TANH_SLOPE + (1.5 * TANH_SLOPE * CUBIC_TERM) * squared
        )
        slope[rows, :] = steep.astype(jnp.bfloat16)
        return total + fold_rows(following * following)

    leaving = ((h, out_ref, 1), (z, z_ref, 2), (slope, slope_ref, 3))

    def leave_right(chunk):
        for source, target, at in leaving:
            chunk_copy(source, target, out_sems.at[at], chunk).start()

    next_ref[...] = by_chunk(blocks, right, jnp.zeros((8, slots), jnp.float32), None, leave_right)
    for source, target, at in ((u, u_ref, 0),) + leaving:
        wait_chunks(source, target, out_sems.at[at])


def backward_kernel(turning, last, layer, inputs, table_ref, scale_ref, gain_ref, end_gain_ref, *refs):
    sources, refs = refs[:inputs], refs[inputs:]
    slope_ref, z_ref, u_ref = sources[:3]
    parts, sources = sources[3 : 3 + PARTS], sources[3 + PARTS :]
    out_ref, own_grad, peer_grad = refs[:3]
    g, slope, z, u, h, w, gw, mid, gain, top, goal, end_gain = refs[3:15]
    in_sems, w_sems, out_sems, gw_sems = refs[15:]
    features, slots = g.shape
    size = w.shape[-1]
    chunk_blocks = w.shape[2]
    blocks = features // size
    fold = size // blocks

    left_in = factor_copies(parts, layer, w, w_sems, 0)
    right_in = factor_copies(parts, layer, w, w_sems, 1)
    g_ref, h_ref = sources[:2]
    if turning:
        start_chunks(g_ref, top, in_sems.at[0])
        start_chunks(end_gain_ref, end_gain, in_sems.at[6])
        start_chunks(sources[2], goal, in_sems.at[5])
    else:
        start_chunks(g_ref, g, in_sems.at[0])
    for copy in right_in:
        copy.start()
    start_chunks(slope_ref, slope, in_sems.at[1])
    start_chunks(z_ref, z, in_sems.at[2])
    for copy in left_in:
        copy.start()
    start_chunks(u_ref, u, in_sems.at[3])
    start_chunks(gain_ref, gain, in_sems.at[7])
    start_chunks(h_ref, h, in_sems.at[4])

    if turning:
        zero = jnp.zeros((8, slots), jnp.float32)

        def sums(block, totals):
            rows = block_rows(block, size)
            part = top[rows, :]
            scaled = part * end_gain[rows, :].astype(jnp.float32)
            return (
                totals[0] + fold_rows(part * part),
                totals[1] + fold_rows(scaled * scaled),
                totals[2] + fold_rows(scaled * goal[rows, :].astype(jnp.float32)),
            )

        def arrive_top(chunk):
            chunk_copy(g_ref, top, in_sems.at[0], chunk).wait()
            chunk_copy(end_gain_ref, end_gain, in_sems.at[6], chunk).wait()
            chunk_copy(sources[2], goal, in_sems.at[5], chunk).wait()

        totals = by_chunk(blocks, sums, (zero, zero, zero), arrive_top)
        squares, gained, crossed = [jnp.sum(total, axis=0, keepdims=True) for total in totals]
        end_scale = lax.rsqrt(squares / features + EPSILON)
        end_back = end_scale * end_scale * end_scale * (end_scale * gained - crossed) / features

    for copy in right_in:
        copy.wait()

    def arrive_right(chunk):
        if not turning:
            chunk_copy(g_ref, g, in_sems.at[0], chunk).wait()
        chunk_copy(slope_ref, slope, in_sems.at[1], chunk).wait()
        chunk_copy(z_ref, z, in_sems.at[2], chunk).wait()

    def right(block, carry):
        rows = block_rows(block, size)
        place, home = table_ref[0, block], table_ref[2 if last else 1, block]
        at = (place // chunk_blocks, 1, place % chunk_blocks)
        to = (home // chunk_blocks, 1, home % chunk_blocks)
        if turning:
            part = top[rows, :]
            factor = end_gain[rows, :].astype(jnp.float32)
            error = (part * end_scale * factor - goal[rows, :].astype(jnp.float32)) * factor
            gradient = end_scale * error - part * end_back
            g[rows, :] = gradient
        else:
            gradient = g[rows, :]
        steep = (gradient * slope[rows, :].astype(jnp.float32)).astype(jnp.bfloat16)
        gw[to] = inner_dot(z[rows, :], steep, 1, 1).astype(jnp.bfloat16)
        mid[rows, :] = inner_dot(w[at], steep, 1, 0)
        return carry

    by_chunk(blocks, right, 0, arrive_right)
    right_out = gradient_copies(gw, (own_grad, peer_grad), gw_sems, 1)
    for copy in right_out:
        copy.start()
    for copy in left_in:
        copy.wait()
    scale = scale_ref[0:1, :]

    def arrive_left(chunk):
        chunk_copy(u_ref, u, in_sems.at[3], chunk).wait()
        chunk_copy(gain_ref, gain, in_sems.at[7], chunk).wait()
        chunk_copy(h_ref, h, in_sems.at[4], chunk).wait()

    def left(block, total):
        rows = block_rows(block, size)
        place, home = table_ref[0, block], table_ref[2 if last else 1, block]
        at = (place // chunk_blocks, 0, place % chunk_blocks)
        to = (home // chunk_blocks, 0, home % chunk_blocks)
        arrived = [mid[pl.ds(q * blocks + block, blocks, stride=size), :] for q in range(fold)]
        arrived = jnp.concatenate(arrived, axis=0).astype(jnp.bfloat16)
        gw[to] = inner_dot(u[rows, :], arrived, 1, 1).astype(jnp.bfloat16)
        weighted = inner_dot(w[at], arrived, 1, 0) * gain[rows, :].astype(jnp.float32)
        g[rows, :] = g[rows, :] + scale * weighted
        return total + fold_rows(weighted * h[rows, :].astype(jnp.float32))

    total = by_chunk(blocks, left, jnp.zeros((8, slots), jnp.float32), arrive_left)
    left_out = gradient_copies(gw, (own_grad, peer_grad), gw_sems, 0)
    for copy in left_out:
        copy.start()
    back = scale * scale * scale * jnp.sum(total, axis=0, keepdims=True) / features

    def finish(block, carry):
        rows = block_rows(block, size)
        ended = g[rows, :] - h[rows, :].astype(jnp.float32) * back
        if last:
            u[rows, :] = ended.astype(jnp.bfloat16)
        else:
            g[rows, :] = ended
        return carry

    ended = u if last else g
    by_chunk(blocks, finish, 0, None, lambda chunk: chunk_copy(ended, out_ref, out_sems, chunk).start())
    wait_chunks(ended, out_ref, out_sems)
    for copy in right_out + left_out:
        copy.wait()


def shape_of(shape, dtype):
    return jax.ShapeDtypeStruct(shape, dtype)


SMEM = pl.BlockSpec(memory_space=pltpu.SMEM)
INSIDE = pl.BlockSpec(memory_space=pltpu.VMEM)
OUTSIDE = pl.BlockSpec(memory_space=pl.ANY)


def run_forward(table, gain, sums, residual, weights, layer):
    first = residual.dtype == jnp.bfloat16
    whole = residual.shape
    sources = (*weights, residual)
    held = (PARTS * weights[0].shape[0],) + weights[0].shape[2:]
    out_shape = (
        shape_of(whole, jnp.float32),
        shape_of(whole, jnp.bfloat16),
        shape_of(whole, jnp.bfloat16),
        shape_of(whole, jnp.bfloat16),
        shape_of((8, whole[1]), jnp.float32),
        shape_of((8, whole[1]), jnp.float32),
    )
    return pl.pallas_call(
        lambda *refs: forward_kernel(first, layer, len(sources), *refs),
        in_specs=[SMEM, INSIDE, OUTSIDE] + [OUTSIDE] * len(sources),
        out_specs=[OUTSIDE] * 4 + [INSIDE] * 2,
        out_shape=out_shape,
        scratch_shapes=[
            pltpu.VMEM(whole if first else SMALL, jnp.bfloat16),
            pltpu.VMEM(whole, jnp.float32),
            pltpu.VMEM(held, jnp.bfloat16),
            pltpu.VMEM(whole, jnp.bfloat16),
            pltpu.VMEM(whole, jnp.bfloat16),
            pltpu.VMEM(whole, jnp.bfloat16),
            pltpu.VMEM(whole, jnp.float32),
            pltpu.VMEM(whole, jnp.bfloat16),
            pltpu.SemaphoreType.DMA((CHUNKS,)),
            pltpu.SemaphoreType.DMA((CHUNKS,)),
            pltpu.SemaphoreType.DMA((2, PARTS)),
            pltpu.SemaphoreType.DMA((4, CHUNKS)),
        ],
        compiler_params=pltpu.CompilerParams(vmem_limit_bytes=VMEM_LIMIT),
        cost_estimate=pl.CostEstimate(
            flops=FORWARD_COST, bytes_accessed=20 * whole[0] * whole[1], transcendentals=0
        ),
        name="forward_layer",
    )(table, sums, gain, *sources)


def run_backward(table, gain, end_gain, scale, kept, weights, layer, sources, turning, last):
    whole = kept[0].shape
    sources = (*kept, *weights, *sources)
    held = (PARTS * weights[0].shape[0],) + weights[0].shape[2:]
    half = (held[0] // 2,) + held[1:]
    out_shape = [shape_of(whole, jnp.bfloat16 if last else jnp.float32)] + [shape_of(half, jnp.bfloat16)] * 2
    return pl.pallas_call(
        lambda *refs: backward_kernel(turning, last, layer, len(sources), *refs),
        in_specs=[SMEM, INSIDE] + [OUTSIDE] * (2 + len(sources)),
        out_specs=[OUTSIDE] * len(out_shape),
        out_shape=out_shape,
        scratch_shapes=[
            pltpu.VMEM(whole, jnp.float32),
            pltpu.VMEM(whole, jnp.bfloat16),
            pltpu.VMEM(whole, jnp.bfloat16),
            pltpu.VMEM(whole, jnp.bfloat16),
            pltpu.VMEM(whole, jnp.bfloat16 if last else jnp.float32),
            pltpu.VMEM(held, jnp.bfloat16),
            pltpu.VMEM(held, jnp.bfloat16),
            pltpu.VMEM(whole, jnp.float32),
            pltpu.VMEM(whole, jnp.bfloat16),
            pltpu.VMEM(whole if turning else SMALL, jnp.float32),
            pltpu.VMEM(whole if turning else SMALL, jnp.bfloat16),
            pltpu.VMEM(whole if turning else SMALL, jnp.bfloat16),
            pltpu.SemaphoreType.DMA((8, CHUNKS)),
            pltpu.SemaphoreType.DMA((2, PARTS)),
            pltpu.SemaphoreType.DMA((CHUNKS,)),
            pltpu.SemaphoreType.DMA((2, PARTS)),
        ],
        compiler_params=pltpu.CompilerParams(vmem_limit_bytes=VMEM_LIMIT),
        cost_estimate=pl.CostEstimate(
            flops=BACKWARD_COST, bytes_accessed=30 * whole[0] * whole[1], transcendentals=0
        ),
        name="backward_layer",
    )(table, scale, gain, end_gain, *sources)


def join_kernel(rows, *refs):
    sources, whole, sems = refs[:-2], refs[-2], refs[-1]
    copies = [
        pltpu.make_async_copy(source.at[pl.ds(0, rows)], whole.at[pl.ds(at * rows, rows)], sems.at[at])
        for at, source in enumerate(sources)
    ]
    for copy in copies:
        copy.start()
    for copy in copies:
        copy.wait()


def joined(parts, rows=None):
    rows = parts[0].shape[0] if rows is None else rows
    whole = shape_of((rows * len(parts),) + parts[0].shape[1:], parts[0].dtype)
    return pl.pallas_call(
        lambda *refs: join_kernel(rows, *refs),
        in_specs=[OUTSIDE] * len(parts),
        out_specs=INSIDE,
        out_shape=whole,
        scratch_shapes=[pltpu.SemaphoreType.DMA((len(parts),))],
        compiler_params=pltpu.CompilerParams(vmem_limit_bytes=VMEM_LIMIT),
        cost_estimate=pl.CostEstimate(
            flops=0, bytes_accessed=4 * math.prod(whole.shape), transcendentals=0
        ),
        name="join",
    )(*parts)


def sum_kernel(terms, inputs, *refs):
    sources, outs = refs[:inputs], refs[inputs:]
    for group in range(inputs // terms):
        mine = sources[group * terms : (group + 1) * terms]
        for at in range(mine[0].shape[0]):
            total = sum(ref[at].astype(jnp.float32) for ref in mine).astype(jnp.bfloat16)
            if len(outs) > 1:
                outs[at][group] = total
            else:
                outs[0][at, group] = total


def run_sum(groups, parts, apart=True):
    flat = [term.reshape(parts, -1, term.shape[-1]) for terms in groups for term in terms]
    _, rows, lanes = flat[0].shape
    steps = 4
    if apart:
        out_shape = [shape_of((len(groups), rows, lanes), jnp.bfloat16)] * parts
        out_specs = [pl.BlockSpec((len(groups), rows // steps, lanes), lambda i: (0, i, 0))] * parts
    else:
        out_shape = [shape_of((parts, len(groups), rows, lanes), jnp.bfloat16)]
        out_specs = [pl.BlockSpec((parts, len(groups), rows // steps, lanes), lambda i: (0, 0, i, 0))]
    sums = pl.pallas_call(
        lambda *refs: sum_kernel(len(groups[0]), len(flat), *refs),
        grid=(steps,),
        in_specs=[pl.BlockSpec((parts, rows // steps, lanes), lambda i: (0, i, 0))] * len(flat),
        out_specs=out_specs,
        out_shape=out_shape,
        compiler_params=pltpu.CompilerParams(vmem_limit_bytes=VMEM_LIMIT),
        cost_estimate=pl.CostEstimate(
            flops=flat[0].size * len(flat), bytes_accessed=2 * flat[0].size * (len(flat) + 1), transcendentals=0
        ),
        name="sum",
    )(*flat)
    return [out.reshape(-1, lanes) for out in sums] if apart else sums[0].reshape(parts, -1, lanes)


def pieces_kernel(chunk, place_ref, order_ref, left_ref, right_ref, gain_ref, out_ref, held, left_sem, sems):
    layer_count, half, size = held.shape[:3]
    first = place_ref[2] * half
    lefts = pltpu.make_async_copy(left_ref.at[:, pl.ds(first, half)], held, left_sem.at[0])
    lefts.start()
    copies = []
    turns = []
    for section in range(out_ref.shape[0]):
        row = 0
        for layer in range(layer_count):
            for inside in range(chunk):
                turns.append((layer, section * chunk + inside, section, row))
                row += size
            for inside in range(chunk):
                source = right_ref.at[layer, first + section * chunk + inside]
                copies.append((source, out_ref.at[section, pl.ds(row, size)]))
                row += size
        copies.append((gain_ref, out_ref.at[section, pl.ds(row, gain_ref.shape[0])]))
    copies = [
        pltpu.make_async_copy(source, target, sems.at[at]) for at, (source, target) in enumerate(copies)
    ]
    for copy in copies:
        copy.start()
    lefts.wait()
    for layer, block, section, row in turns:
        turned = inner_dot(held[layer, block], order_ref[...], 1, 0)
        out_ref[section, pl.ds(row, size), :] = turned.astype(jnp.bfloat16)
    for copy in copies:
        copy.wait()


def factor_pieces(place, order, left, right, gain_rows, chunk, width):
    layer_count, blocks, size = left.shape[:3]
    rows = layer_count * 2 * chunk * size + gain_rows.shape[0]
    return pl.pallas_call(
        lambda *refs: pieces_kernel(chunk, *refs),
        in_specs=[SMEM, INSIDE] + [OUTSIDE] * 3,
        out_specs=INSIDE,
        out_shape=shape_of((width, rows, size), jnp.bfloat16),
        scratch_shapes=[
            pltpu.VMEM((layer_count, blocks // 2, size, size), jnp.bfloat16),
            pltpu.SemaphoreType.DMA((1,)),
            pltpu.SemaphoreType.DMA((width * (layer_count * chunk + 1),)),
        ],
        compiler_params=pltpu.CompilerParams(vmem_limit_bytes=VMEM_LIMIT),
        cost_estimate=pl.CostEstimate(flops=left.size * size, bytes_accessed=4 * left.size, transcendentals=0),
        name="pieces",
    )(place, order, left, right, gain_rows)


def choice(pairs, critic, slots):
    rows = pairs.shape[0]
    named = (pairs[:, 0:1] == critic) | (pairs[:, 1:2] == critic)
    named = jnp.broadcast_to(named.astype(jnp.float32), (rows, slots))
    before = lax.broadcasted_iota(jnp.int32, (rows, rows), 1) < lax.broadcasted_iota(jnp.int32, (rows, rows), 0)
    rank = inner_dot(before.astype(jnp.bfloat16), named.astype(jnp.bfloat16), 1, 0)
    at = lax.broadcasted_iota(jnp.int32, (rows, slots), 1).astype(jnp.float32)
    return jnp.where(rank == at, named, 0.0).astype(jnp.bfloat16)


def pick_kernel(pairs_ref, values_ref, out_ref):
    width, features, slots = out_ref.shape
    pairs = pairs_ref[...]
    chosen = [choice(pairs, critic, slots) for critic in range(width)]
    step = 512
    for start in range(0, features, step):
        part = values_ref[:, pl.ds(start, step)]
        for k in range(width):
            out_ref[k, pl.ds(start, step), :] = inner_dot(part, chosen[k], 0, 0).astype(jnp.bfloat16)


def run_pick(pairs, values, width, slots):
    rows, features = values.shape
    return pl.pallas_call(
        pick_kernel,
        in_specs=[INSIDE] * 2,
        out_specs=INSIDE,
        out_shape=shape_of((width, features, slots), jnp.bfloat16),
        compiler_params=pltpu.CompilerParams(vmem_limit_bytes=VMEM_LIMIT),
        cost_estimate=pl.CostEstimate(
            flops=2 * rows * features * slots * width, bytes_accessed=8 * rows * features, transcendentals=0
        ),
        name="pick",
    )(pairs, values)


def combine_kernel(pairs_ref, came_ref, out_ref):
    width, features, slots = came_ref.shape
    pairs = pairs_ref[...]
    chosen = [choice(pairs, critic, slots) for critic in range(width)]
    step = 512
    for start in range(0, features, step):
        total = sum(inner_dot(chosen[k], came_ref[k, pl.ds(start, step), :], 1, 1) for k in range(width))
        out_ref[:, pl.ds(start, step)] = (0.5 * total).astype(jnp.bfloat16)


def run_combine(pairs, came):
    rows = pairs.shape[0]
    return pl.pallas_call(
        combine_kernel,
        in_specs=[INSIDE] * 2,
        out_specs=INSIDE,
        out_shape=shape_of((rows, came.shape[1]), jnp.bfloat16),
        compiler_params=pltpu.CompilerParams(vmem_limit_bytes=VMEM_LIMIT),
        cost_estimate=pl.CostEstimate(
            flops=2 * rows * came.size, bytes_accessed=4 * came.size, transcendentals=0
        ),
        name="combine",
    )(pairs, came)


FORWARD_COST = 15_000_000_000
BACKWARD_COST = 18_000_000_000


def assemble_kernel(layers, factor, place_ref, order_ref, *refs):
    count = 2 * len(layers)
    sources, (left_ref, right_ref) = refs[:count], refs[count : count + 2]
    held, wide = refs[count + 2 : 2 * count + 2], refs[2 * count + 2 : 3 * count + 2]
    in_sems, out_sems = refs[3 * count + 2 :]
    origin, core = place_ref[0] ^ place_ref[1], place_ref[2]
    order = order_ref[...]
    arrivals = [
        pltpu.make_async_copy(source, held[at], in_sems.at[at]) for at, source in enumerate(sources)
    ]
    for copy in arrivals:
        copy.start()
    leaving = []
    for at in range(count):
        arrivals[at].wait()
        half = core if at % 2 == 0 else 1 - core
        width, _, _, chunk = held[at].shape[:4]
        for k in range(width):
            start = (half * width + (origin ^ k if at < 2 else k)) * chunk
            for inside, layer in enumerate(layers[at // 2]):
                for block in range(chunk):
                    left = inner_dot(held[at][k, inside, 0, block], order, 1, 1)
                    wide[at][k, inside, 0, block] = left * factor
                wide[at][k, inside, 1] = held[at][k, inside, 1].astype(jnp.float32) * factor
                for which, target in enumerate((left_ref, right_ref)):
                    copy = pltpu.make_async_copy(
                        wide[at].at[k, inside, which],
                        target.at[layer, pl.ds(start, chunk)],
                        out_sems.at[len(leaving)],
                    )
                    copy.start()
                    leaving.append(copy)
    for copy in leaving:
        copy.wait()


def run_assemble(place, order, pieces, layers, factor):
    piece = pieces[0].shape
    layer_count = sum(len(group) for group in layers)
    out = shape_of((layer_count, 2 * piece[0] * piece[3]) + piece[4:], jnp.float32)
    return pl.pallas_call(
        lambda *refs: assemble_kernel(layers, factor, *refs),
        in_specs=[SMEM, INSIDE] + [OUTSIDE] * len(pieces),
        out_specs=[OUTSIDE] * 2,
        out_shape=[out] * 2,
        scratch_shapes=[pltpu.VMEM(part.shape, jnp.bfloat16) for part in pieces]
        + [pltpu.VMEM(part.shape, jnp.float32) for part in pieces]
        + [
            pltpu.SemaphoreType.DMA((len(pieces),)),
            pltpu.SemaphoreType.DMA((4 * layer_count * piece[0],)),
        ],
        compiler_params=pltpu.CompilerParams(vmem_limit_bytes=VMEM_LIMIT),
        cost_estimate=pl.CostEstimate(flops=0, bytes_accessed=4 * math.prod(out.shape) * 3, transcendentals=0),
        name="assemble",
    )(place, order, *pieces)


def plane_routes(width, replicas):
    bits = width.bit_length() - 1
    orders = [[(step + d) % bits for step in range(bits)] for d in range(replicas)]
    every = [(s, t, d) for s in range(width) for t in range(width) for d in range(replicas)]

    def route(move):
        def index(s, t, d):
            return (s * width + t) * replicas + d

        return [(index(*place), index(*move(*place))) for place in every]

    ranks = [[0] * width for _ in range(replicas)]
    for d in range(replicas):
        for r in range(width):
            ranks[d][sum(((r >> at) & 1) << orders[d][at] for at in range(bits))] = r
    return {
        "across": [route(lambda s, t, d, at=at: (s ^ (1 << orders[d][at]), t, d)) for at in range(bits)],
        "cores": route(lambda s, t, d: (s, t, 1 - d)),
        "sections": [route(lambda s, t, d, k=k: (s ^ k, t, d)) for k in range(width)],
        "homes": [route(lambda s, t, d, j=j: (t, t ^ s ^ j, d)) for j in range(width)],
    }, ranks


def plane_shards(patches, teacher, critic_pairs, left_factors, right_factors, norm_gains):
    width = lax.axis_size("section")
    replicas = lax.axis_size("dp")
    tok_rows, feat_local = patches.shape
    layer_count, local_blocks, size = left_factors.shape[1:4]
    blocks = feat_local * width // size
    wide = 2 * tok_rows // 3
    chunk = local_blocks // (replicas * width)
    layer_rows = 2 * chunk * size
    routes, ranks = plane_routes(width, replicas)
    section = lax.axis_index("section")
    tensor = lax.axis_index("tensor")
    core = lax.axis_index("dp")
    place = jnp.stack([section, tensor, core]).astype(jnp.int32)
    tie = lax.optimization_barrier

    def move(value, route):
        return lax.ppermute(value, AXES, route)

    def move_all(values, name):
        return [move(value, route) for value, route in zip(values, routes[name])]

    def send(values, name):
        return [values[0]] + [move(values[k], routes[name][k]) for k in range(1, width)]

    def gather_one(mine):
        return joined([mine, move(mine, routes["across"][0])])

    def gather_two(pair):
        return pair, move(pair, routes["across"][1]), move(pair, routes["cores"])

    def gather_three(pair, other, peer):
        return [pair, other, peer, move(other, routes["cores"])]

    def as_weights(parts):
        return [part.reshape(2 * width, -1, 2, chunk, size, size) for part in parts]

    block = jnp.arange(blocks, dtype=jnp.int32)
    inside = block % local_blocks
    replica = inside // (width * chunk)
    part = (replica != core).astype(jnp.int32)
    distance = section ^ ((inside // chunk) % width)
    quarter = block // local_blocks
    rank = jnp.array(ranks, jnp.int32)[replica, distance]
    table = jnp.stack(
        [
            ((part * width + index) * width + piece) * chunk + inside % chunk
            for index, piece in (
                (rank, quarter),
                (distance, quarter),
                (distance, tensor ^ section ^ distance ^ quarter),
            )
        ]
    ).astype(jnp.int32)

    def to_planes(value):
        return lax.all_to_all(value, "tensor", split_axis=0, concat_axis=0, tiled=True)

    def to_sections(value):
        return lax.all_to_all(value, "section", split_axis=0, concat_axis=0, tiled=True)

    half_layers = layer_count // 2
    groups = [tuple(range(half_layers)), tuple(range(half_layers, layer_count))]
    fold = size // blocks
    columns = jnp.arange(size)
    order = (columns[:, None] == (columns % blocks) * fold + columns // blocks).astype(jnp.bfloat16)
    gain_rows = norm_gains[0].reshape(-1, size)
    pieces = factor_pieces(place, order, left_factors[0], right_factors[0], gain_rows, chunk, width)
    pieces, patches, teacher = tie((pieces, patches, teacher))
    spread = to_sections(pieces)
    patch_sent = run_pick(critic_pairs, patches, width, wide)
    target_sent = run_pick(critic_pairs, teacher, width, wide)
    spread, patch_sent, target_sent = tie((spread, patch_sent, target_sent))
    lifted = to_planes(spread)
    lifted, patch_sent = tie((lifted, patch_sent))
    patch_came = to_planes(patch_sent).reshape(-1, wide)
    lowest = [lifted[:, group[0] * layer_rows : (group[-1] + 1) * layer_rows] for group in groups]
    beside = move(lowest[0], routes["across"][0])
    gains = lifted[:, layer_count * layer_rows :].reshape(width, layer_count + 1, feat_local)
    gains = gains.transpose(1, 0, 2).reshape(layer_count + 1, -1)
    columns = [jnp.broadcast_to(gain[:, None], (gain.shape[0], wide)) for gain in gains]
    lowest, beside, columns = tie((lowest, beside, columns))
    first_two = gather_two(joined([lowest[0], beside]))
    first_two, lowest[1] = tie((first_two, lowest[1]))
    weights = [as_weights(gather_three(*first_two))]
    later = (lowest[1], move(lowest[1], routes["across"][0]))
    weights, later, patch_came = tie((weights, later, patch_came))

    residual = patch_came
    flying = gather_two(joined(list(later)))
    sums = jnp.zeros((8, wide), jnp.float32)
    stored = []
    for layer in range(layer_count):
        group = 0 if layer in groups[0] else 1
        following, u, z, slope, scale, sums = run_forward(
            table, columns[layer], sums, residual, weights[group], layer - groups[group][0]
        )
        stored.append(((slope, z, u), scale, residual))
        residual = following
        if layer == 0:
            residual, sums, flying, target_sent = tie((residual, sums, flying, target_sent))
            weights.append(as_weights(gather_three(*flying)))
            target = to_planes(target_sent).reshape(-1, wide)
        if layer == groups[0][-1]:
            residual, sums, weights[1] = tie((residual, sums, weights[1]))

    def core_sum(mine, other):
        return (mine, move(other, routes["cores"]))

    def plane_sum(mine, other):
        return send(run_sum([(mine, other)], width), "sections")

    def homeward(parts):
        return move_all(run_sum(parts, width), "homes")

    def both_halves(whole):
        pair = (whole, move(whole, routes["cores"]))
        return [part.reshape(width, -1, 2, chunk, size, size) for part in pair]

    steps = (core_sum, plane_sum)
    gradient = residual
    underway = []
    for layer in range(layer_count - 1, -1, -1):
        turning = layer == layer_count - 1
        last = layer == 0
        kept, scale, inputs = stored[layer]
        group = 0 if layer in groups[0] else 1
        sources = (gradient, inputs, target) if turning else (gradient, inputs)
        underway = [(at + 1, steps[at](*state)) if at < len(steps) else (at, state) for at, state in underway]
        gradient, mine, other = run_backward(
            table,
            columns[layer],
            columns[layer_count],
            scale,
            kept,
            weights[group],
            layer - groups[group][0],
            sources,
            turning,
            last,
        )
        gradient, mine, other, states = tie((gradient, mine, other, [state for _, state in underway]))
        underway = [(at, state) for (at, _), state in zip(underway, states)]
        underway.append((0, (mine, other)))

    returned = to_planes(gradient.reshape(width, feat_local, wide))
    ended = [steps[at](*state) if at < len(steps) else state for at, state in underway][::-1]
    ended = tie(ended)
    ended[0] = plane_sum(*ended[0])
    others = to_planes(run_sum(ended[1:], width, apart=False))
    ended[0], returned = tie((ended[0], returned))
    home = homeward(ended[:1])
    d_patches = run_combine(critic_pairs, returned)
    others = to_sections(others)
    d_patches, home, others = tie((d_patches, home, others))
    homes_of = both_halves(joined(home)) + both_halves(others)
    grad_factor = 1.0 / math.sqrt(2 * tok_rows * width * replicas)
    grad_left, grad_right = run_assemble(
        place, order, homes_of, [(0,), tuple(range(1, layer_count))], grad_factor
    )
    return (d_patches, grad_left[None], grad_right[None])


def solution(mesh):
    in_specs = (
        P(("section", "dp"), "tensor"),
        P(("section", "dp"), "tensor"),
        P(("section", "dp"), None),
        P("section", None, "tensor", None, None),
        P("section", None, "tensor", None, None),
        P("section", None, "tensor"),
    )
    out_specs = (
        P(("section", "dp"), "tensor"),
        P("section", None, "tensor", None, None),
        P("section", None, "tensor", None, None),
    )
    body = plane_shards if planes_fit(mesh) else layered_shards
    return jax.shard_map(
        body, mesh=mesh, in_specs=in_specs, out_specs=out_specs, check_vma=False)
```

```python
import math

import jax
import jax.numpy as jnp
from jax import lax
from jax.experimental import pallas as pl
from jax.experimental.pallas import tpu as pltpu
from jax.sharding import PartitionSpec as P

EPSILON = 1e-06
TANH_SLOPE = 0.7978845608028654
CUBIC_TERM = 0.044715


def shifted(value, axis, steps):
    count = lax.axis_size(axis)
    first, last = (max(0, -steps), min(count, count - steps))
    return lax.ppermute(value, axis, [(source, source + steps) for source in range(first, last)])


def gelu_value(values):
    tangent = jnp.tanh(TANH_SLOPE * (values + CUBIC_TERM * values * values * values))
    return 0.5 * values * (1.0 + tangent)


def gelu_slope(values):
    tangent = jnp.tanh(TANH_SLOPE * (values + CUBIC_TERM * values * values * values))
    return 0.5 * (1.0 + tangent) + 0.5 * values * (1.0 - tangent * tangent) * TANH_SLOPE * (
        1.0 + 3.0 * CUBIC_TERM * values * values
    )


def norm_pair(residuals, gain_pair, model_width):
    squares = lax.psum(
        (
            jnp.sum(residuals[0] * residuals[0], axis=(1, 2)),
            jnp.sum(residuals[1] * residuals[1], axis=(1, 2)),
        ),
        "tensor",
    )
    factors = [lax.rsqrt(squares[member] / model_width + EPSILON) for member in range(2)]
    normed = [
        residuals[member] * factors[member][:, None, None] * gain_pair[member][None]
        for member in range(2)
    ]
    return (factors, normed)


def norm_back_pair(residuals, factors, gain_pair, grad_normed, carried, model_width):
    weighted = [grad_normed[member] * gain_pair[member][None] for member in range(2)]
    inners = lax.psum(
        (
            jnp.sum(weighted[0] * residuals[0], axis=(1, 2)),
            jnp.sum(weighted[1] * residuals[1], axis=(1, 2)),
        ),
        "tensor",
    )
    return [
        carried[member]
        + factors[member][:, None, None] * weighted[member]
        - residuals[member] * (factors[member] ** 3 * inners[member] / model_width)[:, None, None]
        for member in range(2)
    ]


def layered_shards(patches, teacher, critic_pairs, left_factors, right_factors, norm_gains):
    sections = lax.axis_size("section")
    tensor_width = lax.axis_size("tensor")
    replicas = lax.axis_size("dp")
    tok_rows = patches.shape[0]
    feat_local = patches.shape[1]
    layer_count = left_factors.shape[1]
    local_blocks = left_factors.shape[2]
    block_size = left_factors.shape[3]
    all_blocks = local_blocks * tensor_width
    fold_ratio = block_size // all_blocks
    model_width = feat_local * tensor_width
    sixth_rows = tok_rows // 6
    leading = 2 * sixth_rows
    critic_ids = jnp.arange(4, dtype=jnp.int32)
    named_by = (
        (critic_pairs[:, 0:1] == critic_ids[None, :])
        | (critic_pairs[:, 1:2] == critic_ids[None, :])
    ).astype(jnp.int32)
    ranking = jnp.cumsum(named_by, axis=0) - 1
    wide_ids = critic_ids[None, :] < 2
    slot_width = 3 * sixth_rows
    spilled = wide_ids & (ranking >= 3 * sixth_rows)
    destination = jnp.where(spilled, critic_ids[None, :] + 2, critic_ids[None, :])
    slot_index = jnp.where(spilled, ranking - sixth_rows, ranking)
    flat_slot = destination * slot_width + slot_index
    chosen = jnp.take_along_axis(flat_slot, critic_pairs, axis=1)
    slot_total = sections * slot_width
    row_ids = jnp.broadcast_to(jnp.arange(tok_rows, dtype=jnp.int32)[:, None], chosen.shape)
    source_row = (
        jnp.full((slot_total,), tok_rows, jnp.int32).at[chosen.reshape(-1)].set(row_ids.reshape(-1))
    )
    send_patch = (
        patches.at[source_row]
        .get(mode="fill", fill_value=0)
        .reshape(sections, slot_width, local_blocks, block_size)
    )
    send_target = (
        teacher.at[source_row]
        .get(mode="fill", fill_value=0)
        .reshape(sections, slot_width, local_blocks, block_size)
    )
    recv_patch, recv_target = (
        lax.all_to_all(send_patch, "section", split_axis=0, concat_axis=0, tiled=True),
        lax.all_to_all(send_target, "section", split_axis=0, concat_axis=0, tiled=True),
    )
    residuals = [
        recv_patch[:, :leading].reshape(-1, local_blocks, block_size).astype(jnp.float32),
        recv_patch[:, leading:].reshape(-1, local_blocks, block_size).astype(jnp.float32),
    ]
    targets = [
        recv_target[:, :leading].reshape(-1, local_blocks, block_size).astype(jnp.float32),
        recv_target[:, leading:].reshape(-1, local_blocks, block_size).astype(jnp.float32),
    ]
    native = (left_factors[0], right_factors[0], norm_gains[0])
    borrowed = shifted((left_factors, right_factors, norm_gains), "section", 2)
    is_wide = lax.axis_index("section") < 2
    second = (
        jnp.where(is_wide, left_factors, borrowed[0])[0],
        jnp.where(is_wide, right_factors, borrowed[1])[0],
        jnp.where(is_wide, norm_gains, borrowed[2])[0],
    )
    left_sets = (native[0], second[0])
    right_sets = (native[1], second[1])
    gain_sets = (
        native[2].astype(jnp.float32).reshape(layer_count + 1, local_blocks, block_size),
        second[2].astype(jnp.float32).reshape(layer_count + 1, local_blocks, block_size),
    )
    stored = []
    for layer_index in range(layer_count):
        gain_pair = [gain_sets[0][layer_index], gain_sets[1][layer_index]]
        factors, normed = norm_pair(residuals, gain_pair, model_width)
        normed = [normed[member].astype(jnp.bfloat16) for member in range(2)]
        first_out = [
            jnp.einsum(
                "nki,kij->nkj",
                normed[member],
                left_sets[member][layer_index],
                preferred_element_type=jnp.float32,
            ).astype(jnp.bfloat16)
            for member in range(2)
        ]
        permuted = (
            lax.all_to_all(first_out[0], "tensor", split_axis=2, concat_axis=1, tiled=True),
            lax.all_to_all(first_out[1], "tensor", split_axis=2, concat_axis=1, tiled=True),
        )
        permuted = [
            permuted[member].reshape(
                permuted[member].shape[0], all_blocks, local_blocks, fold_ratio
            )
            for member in range(2)
        ]
        right_quads = [
            right_sets[member][layer_index].reshape(
                local_blocks, fold_ratio, all_blocks, block_size
            )
            for member in range(2)
        ]
        mixture = [
            jnp.einsum(
                "nkmp,mpkl->nml",
                permuted[member],
                right_quads[member],
                preferred_element_type=jnp.float32,
            )
            for member in range(2)
        ]
        stored.append((residuals, factors, normed, permuted, mixture, right_quads, gain_pair))
        residuals = [residuals[member] + gelu_value(mixture[member]) for member in range(2)]
    final_gains = [gain_sets[0][layer_count], gain_sets[1][layer_count]]
    factors, outputs = norm_pair(residuals, final_gains, model_width)
    gradients = norm_back_pair(
        residuals,
        factors,
        final_gains,
        [outputs[member] - targets[member] for member in range(2)],
        [jnp.zeros_like(residuals[member]) for member in range(2)],
        model_width,
    )
    left_terms = []
    right_terms = []
    for layer_index in range(layer_count - 1, -1, -1):
        inputs, factors, normed, permuted, mixture, right_quads, gain_pair = stored[layer_index]
        slopes = [
            (gradients[member] * gelu_slope(mixture[member])).astype(jnp.bfloat16)
            for member in range(2)
        ]
        right_grad = [
            jnp.einsum(
                "nkmp,nml->mpkl",
                permuted[member],
                slopes[member],
                preferred_element_type=jnp.float32,
            ).reshape(local_blocks, block_size, block_size)
            for member in range(2)
        ]
        back_moved = [
            jnp.einsum(
                "nml,mpkl->nkmp",
                slopes[member],
                right_quads[member],
                preferred_element_type=jnp.float32,
            )
            .astype(jnp.bfloat16)
            .reshape(slopes[member].shape[0], all_blocks, local_blocks * fold_ratio)
            for member in range(2)
        ]
        arrived = (
            lax.all_to_all(back_moved[0], "tensor", split_axis=1, concat_axis=2, tiled=True),
            lax.all_to_all(back_moved[1], "tensor", split_axis=1, concat_axis=2, tiled=True),
        )
        left_grad = [
            jnp.einsum(
                "nki,nkj->kij", normed[member], arrived[member], preferred_element_type=jnp.float32
            )
            for member in range(2)
        ]
        grad_normed = [
            jnp.einsum(
                "nkj,kij->nki",
                arrived[member],
                left_sets[member][layer_index],
                preferred_element_type=jnp.float32,
            )
            for member in range(2)
        ]
        gradients = norm_back_pair(inputs, factors, gain_pair, grad_normed, gradients, model_width)
        layer_left = jnp.stack(left_grad)
        layer_right = jnp.stack(right_grad)
        layer_left, layer_right = (
            lax.psum(layer_left.astype(jnp.bfloat16), "dp").astype(jnp.float32),
            lax.psum(layer_right.astype(jnp.bfloat16), "dp").astype(jnp.float32),
        )
        left_terms.insert(0, layer_left)
        right_terms.insert(0, layer_right)
    left_stack = jnp.stack(left_terms)
    right_stack = jnp.stack(right_terms)
    repaid = (
        shifted(left_stack[:, 1].astype(jnp.bfloat16), "section", -2).astype(jnp.float32),
        shifted(right_stack[:, 1].astype(jnp.bfloat16), "section", -2).astype(jnp.float32),
    )
    is_wide = lax.axis_index("section") < 2
    left_total = left_stack[:, 0] + jnp.where(is_wide, left_stack[:, 1] + repaid[0], 0.0)
    right_total = right_stack[:, 0] + jnp.where(is_wide, right_stack[:, 1] + repaid[1], 0.0)
    grad_factor = 1.0 / math.sqrt(2 * tok_rows * sections * replicas)
    returned = [
        gradients[member].astype(jnp.bfloat16).reshape(sections, -1, local_blocks, block_size)
        for member in range(2)
    ]
    back_lead, back_trail = (
        lax.all_to_all(returned[0], "section", split_axis=0, concat_axis=0, tiled=True),
        lax.all_to_all(returned[1], "section", split_axis=0, concat_axis=0, tiled=True),
    )
    gathered = jnp.concatenate((back_lead, back_trail), axis=1).reshape(
        slot_total, local_blocks, block_size
    )
    combined = (
        gathered[chosen[:, 0]].astype(jnp.float32) + gathered[chosen[:, 1]].astype(jnp.float32)
    ) * 0.5
    d_patches = combined.astype(jnp.bfloat16).reshape(tok_rows, feat_local)
    return (d_patches, (left_total * grad_factor)[None], (right_total * grad_factor)[None])


VMEM_LIMIT = 60 * 1024 * 1024
CHUNKS = 8
PARTS = 4
SMALL = (16, 128)
AXES = ("section", "tensor", "dp")


def planes_fit(mesh):
    sections = mesh.shape["section"]
    paired = mesh.shape["dp"] == 2 and sections & (sections - 1) == 0
    return paired and mesh.shape["tensor"] == sections


def inner_dot(left, right, left_dim, right_dim):
    return lax.dot_general(
        left,
        right,
        (((left_dim,), (right_dim,)), ((), ())),
        preferred_element_type=jnp.float32,
    )


def fold_rows(values):
    return jnp.sum(values.reshape(values.shape[0] // 8, 8, values.shape[1]), axis=0)


def block_rows(block, size):
    return pl.ds(pl.multiple_of(block * size, size), size)


def column(gain_ref, block, slots):
    blocks = gain_ref.shape[1]
    picked = lax.broadcasted_iota(jnp.int32, (blocks, slots), 0) == block
    return inner_dot(gain_ref[...], picked.astype(jnp.bfloat16), 1, 0)


def chunk_copy(source, target, sems, chunk):
    rows = target.shape[0] // CHUNKS
    at = pl.ds(pl.multiple_of(chunk * rows, rows), rows)
    return pltpu.make_async_copy(source.at[at], target.at[at], sems.at[chunk])


def start_chunks(source, target, sems):
    for chunk in range(CHUNKS):
        chunk_copy(source, target, sems, chunk).start()


def wait_chunks(source, target, sems):
    for chunk in range(CHUNKS):
        chunk_copy(source, target, sems, chunk).wait()


def factor_copies(parts, layer, held, sems, side):
    count = parts[0].shape[0]
    return [
        pltpu.make_async_copy(
            ref.at[:, layer, side], held.at[pl.ds(at * count, count), side], sems.at[side, at]
        )
        for at, ref in enumerate(parts)
    ]


def gradient_copies(held, parts, sems, side):
    count = parts[0].shape[0]
    return [
        pltpu.make_async_copy(
            held.at[pl.ds(at * count, count), side], ref.at[:, side], sems.at[side, at]
        )
        for at, ref in enumerate(parts)
    ]


def by_chunk(blocks, step, carry, before=None, after=None):
    per_chunk = blocks // CHUNKS

    def one(chunk, carry):
        if before is not None:
            before(chunk)
        carry = lax.fori_loop(
            0, per_chunk, lambda at, now: step(chunk * per_chunk + at, now), carry, unroll=True
        )
        if after is not None:
            after(chunk)
        return carry

    return lax.fori_loop(0, CHUNKS, one, carry)


def forward_kernel(first, layer, inputs, table_ref, sums_ref, gain_ref, *refs):
    sources, refs = refs[:inputs], refs[inputs:]
    parts, sources = sources[:PARTS], sources[PARTS:]
    out_ref, u_ref, z_ref, slope_ref, scale_ref, next_ref = refs[:6]
    raw, h, w, u, z, slope, mid, in_sems, w_sems, out_sems = refs[6:]
    features, slots = h.shape
    size = w.shape[-1]
    chunk_blocks = w.shape[2]
    blocks = features // size
    fold = size // blocks

    left_in = factor_copies(parts, layer, w, w_sems, 0)
    right_in = factor_copies(parts, layer, w, w_sems, 1)
    if first:
        start_chunks(sources[0], raw, in_sems)
        for copy in left_in + right_in:
            copy.start()

        def squares(block, total):
            rows = block_rows(block, size)
            part = raw[rows, :].astype(jnp.float32)
            h[rows, :] = part
            return total + fold_rows(part * part)

        total = by_chunk(
            blocks,
            squares,
            jnp.zeros((8, slots), jnp.float32),
            lambda chunk: chunk_copy(sources[0], raw, in_sems, chunk).wait(),
        )
    else:
        for copy in left_in:
            copy.start()
        start_chunks(sources[0], h, in_sems)
        for copy in right_in:
            copy.start()
        total = sums_ref[...]
    scale = lax.rsqrt(jnp.sum(total, axis=0, keepdims=True) / features + EPSILON)
    scale_ref[...] = jnp.broadcast_to(scale, scale_ref.shape)
    for copy in left_in:
        copy.wait()

    def arrive(chunk):
        if not first:
            chunk_copy(sources[0], h, in_sems, chunk).wait()

    def left(block, carry):
        rows = block_rows(block, size)
        place = table_ref[0, block]
        normed = (h[rows, :] * scale * column(gain_ref, block, slots)).astype(jnp.bfloat16)
        u[rows, :] = normed
        weight = w[place // chunk_blocks, 0, place % chunk_blocks]
        mid[rows, :] = inner_dot(weight, normed, 0, 0)
        return carry

    def leave_left(chunk):
        chunk_copy(u, u_ref, out_sems.at[0], chunk).start()

    by_chunk(blocks, left, 0, arrive, leave_left)
    for copy in right_in:
        copy.wait()

    def right(block, total):
        rows = block_rows(block, size)
        place = table_ref[0, block]
        moved = [mid[pl.ds(q * blocks + block, blocks, stride=size), :] for q in range(fold)]
        moved = jnp.concatenate(moved, axis=0).astype(jnp.bfloat16)
        z[rows, :] = moved
        weight = w[place // chunk_blocks, 1, place % chunk_blocks]
        mixture = inner_dot(weight, moved, 0, 0)
        squared = mixture * mixture
        tangent = jnp.tanh(mixture * (TANH_SLOPE + (TANH_SLOPE * CUBIC_TERM) * squared))
        half = 0.5 + 0.5 * tangent
        following = h[rows, :] + mixture * half
        h[rows, :] = following
        steep = half + mixture * (1.0 - tangent * tangent) * (
            0.5 * TANH_SLOPE + (1.5 * TANH_SLOPE * CUBIC_TERM) * squared
        )
        slope[rows, :] = steep.astype(jnp.bfloat16)
        return total + fold_rows(following * following)

    leaving = ((h, out_ref, 1), (z, z_ref, 2), (slope, slope_ref, 3))

    def leave_right(chunk):
        for source, target, at in leaving:
            chunk_copy(source, target, out_sems.at[at], chunk).start()

    next_ref[...] = by_chunk(blocks, right, jnp.zeros((8, slots), jnp.float32), None, leave_right)
    for source, target, at in ((u, u_ref, 0),) + leaving:
        wait_chunks(source, target, out_sems.at[at])


def backward_kernel(turning, last, layer, inputs, table_ref, scale_ref, gain_ref, end_gain_ref, *refs):
    sources, refs = refs[:inputs], refs[inputs:]
    slope_ref, z_ref, u_ref = sources[:3]
    parts, sources = sources[3 : 3 + PARTS], sources[3 + PARTS :]
    out_ref, own_grad, peer_grad = refs[:3]
    g, slope, z, u, h, w, gw, mid, top, goal, end_gain = refs[3:14]
    in_sems, w_sems, out_sems, gw_sems = refs[14:]
    features, slots = g.shape
    size = w.shape[-1]
    chunk_blocks = w.shape[2]
    blocks = features // size
    fold = size // blocks

    left_in = factor_copies(parts, layer, w, w_sems, 0)
    right_in = factor_copies(parts, layer, w, w_sems, 1)
    g_ref, h_ref = sources[:2]
    if turning:
        start_chunks(g_ref, top, in_sems.at[0])
        start_chunks(end_gain_ref, end_gain, in_sems.at[6])
        start_chunks(sources[2], goal, in_sems.at[5])
    else:
        start_chunks(g_ref, g, in_sems.at[0])
    for copy in right_in:
        copy.start()
    start_chunks(slope_ref, slope, in_sems.at[1])
    start_chunks(z_ref, z, in_sems.at[2])
    for copy in left_in:
        copy.start()
    start_chunks(u_ref, u, in_sems.at[3])
    start_chunks(h_ref, h, in_sems.at[4])

    if turning:
        zero = jnp.zeros((8, slots), jnp.float32)

        def sums(block, totals):
            rows = block_rows(block, size)
            part = top[rows, :]
            scaled = part * end_gain[rows, :].astype(jnp.float32)
            return (
                totals[0] + fold_rows(part * part),
                totals[1] + fold_rows(scaled * scaled),
                totals[2] + fold_rows(scaled * goal[rows, :].astype(jnp.float32)),
            )

        def arrive_top(chunk):
            chunk_copy(g_ref, top, in_sems.at[0], chunk).wait()
            chunk_copy(end_gain_ref, end_gain, in_sems.at[6], chunk).wait()
            chunk_copy(sources[2], goal, in_sems.at[5], chunk).wait()

        totals = by_chunk(blocks, sums, (zero, zero, zero), arrive_top)
        squares, gained, crossed = [jnp.sum(total, axis=0, keepdims=True) for total in totals]
        end_scale = lax.rsqrt(squares / features + EPSILON)
        end_back = end_scale * end_scale * end_scale * (end_scale * gained - crossed) / features

    for copy in right_in:
        copy.wait()

    def arrive_right(chunk):
        if not turning:
            chunk_copy(g_ref, g, in_sems.at[0], chunk).wait()
        chunk_copy(slope_ref, slope, in_sems.at[1], chunk).wait()
        chunk_copy(z_ref, z, in_sems.at[2], chunk).wait()

    def right(block, carry):
        rows = block_rows(block, size)
        place, home = table_ref[0, block], table_ref[2 if last else 1, block]
        at = (place // chunk_blocks, 1, place % chunk_blocks)
        to = (home // chunk_blocks, 1, home % chunk_blocks)
        if turning:
            part = top[rows, :]
            factor = end_gain[rows, :].astype(jnp.float32)
            error = (part * end_scale * factor - goal[rows, :].astype(jnp.float32)) * factor
            gradient = end_scale * error - part * end_back
            g[rows, :] = gradient
        else:
            gradient = g[rows, :]
        steep = (gradient * slope[rows, :].astype(jnp.float32)).astype(jnp.bfloat16)
        gw[to] = inner_dot(z[rows, :], steep, 1, 1).astype(jnp.bfloat16)
        mid[rows, :] = inner_dot(w[at], steep, 1, 0)
        return carry

    by_chunk(blocks, right, 0, arrive_right)
    right_out = gradient_copies(gw, (own_grad, peer_grad), gw_sems, 1)
    for copy in right_out:
        copy.start()
    for copy in left_in:
        copy.wait()
    scale = scale_ref[0:1, :]

    def arrive_left(chunk):
        chunk_copy(u_ref, u, in_sems.at[3], chunk).wait()
        chunk_copy(h_ref, h, in_sems.at[4], chunk).wait()

    def left(block, total):
        rows = block_rows(block, size)
        place, home = table_ref[0, block], table_ref[2 if last else 1, block]
        at = (place // chunk_blocks, 0, place % chunk_blocks)
        to = (home // chunk_blocks, 0, home % chunk_blocks)
        arrived = [mid[pl.ds(q * blocks + block, blocks, stride=size), :] for q in range(fold)]
        arrived = jnp.concatenate(arrived, axis=0).astype(jnp.bfloat16)
        gw[to] = inner_dot(u[rows, :], arrived, 1, 1).astype(jnp.bfloat16)
        weighted = inner_dot(w[at], arrived, 1, 0) * column(gain_ref, block, slots)
        g[rows, :] = g[rows, :] + scale * weighted
        return total + fold_rows(weighted * h[rows, :].astype(jnp.float32))

    total = by_chunk(blocks, left, jnp.zeros((8, slots), jnp.float32), arrive_left)
    left_out = gradient_copies(gw, (own_grad, peer_grad), gw_sems, 0)
    for copy in left_out:
        copy.start()
    back = scale * scale * scale * jnp.sum(total, axis=0, keepdims=True) / features

    def finish(block, carry):
        rows = block_rows(block, size)
        ended = g[rows, :] - h[rows, :].astype(jnp.float32) * back
        if last:
            u[rows, :] = ended.astype(jnp.bfloat16)
        else:
            g[rows, :] = ended
        return carry

    ended = u if last else g
    by_chunk(blocks, finish, 0, None, lambda chunk: chunk_copy(ended, out_ref, out_sems, chunk).start())
    wait_chunks(ended, out_ref, out_sems)
    for copy in right_out + left_out:
        copy.wait()


def shape_of(shape, dtype):
    return jax.ShapeDtypeStruct(shape, dtype)


SMEM = pl.BlockSpec(memory_space=pltpu.SMEM)
INSIDE = pl.BlockSpec(memory_space=pltpu.VMEM)
OUTSIDE = pl.BlockSpec(memory_space=pl.ANY)


def run_forward(table, gain, sums, residual, weights, layer):
    first = residual.dtype == jnp.bfloat16
    whole = residual.shape
    sources = (*weights, residual)
    held = (PARTS * weights[0].shape[0],) + weights[0].shape[2:]
    out_shape = (
        shape_of(whole, jnp.float32),
        shape_of(whole, jnp.bfloat16),
        shape_of(whole, jnp.bfloat16),
        shape_of(whole, jnp.bfloat16),
        shape_of((8, whole[1]), jnp.float32),
        shape_of((8, whole[1]), jnp.float32),
    )
    return pl.pallas_call(
        lambda *refs: forward_kernel(first, layer, len(sources), *refs),
        in_specs=[SMEM, INSIDE, INSIDE] + [OUTSIDE] * len(sources),
        out_specs=[OUTSIDE] * 4 + [INSIDE] * 2,
        out_shape=out_shape,
        scratch_shapes=[
            pltpu.VMEM(whole if first else SMALL, jnp.bfloat16),
            pltpu.VMEM(whole, jnp.float32),
            pltpu.VMEM(held, jnp.bfloat16),
            pltpu.VMEM(whole, jnp.bfloat16),
            pltpu.VMEM(whole, jnp.bfloat16),
            pltpu.VMEM(whole, jnp.bfloat16),
            pltpu.VMEM(whole, jnp.float32),
            pltpu.SemaphoreType.DMA((CHUNKS,)),
            pltpu.SemaphoreType.DMA((2, PARTS)),
            pltpu.SemaphoreType.DMA((4, CHUNKS)),
        ],
        compiler_params=pltpu.CompilerParams(vmem_limit_bytes=VMEM_LIMIT),
        cost_estimate=pl.CostEstimate(
            flops=FORWARD_COST, bytes_accessed=20 * whole[0] * whole[1], transcendentals=0
        ),
        name="forward_layer",
    )(table, sums, gain, *sources)


def run_backward(table, gain, end_gain, scale, kept, weights, layer, sources, turning, last):
    whole = kept[0].shape
    sources = (*kept, *weights, *sources)
    held = (PARTS * weights[0].shape[0],) + weights[0].shape[2:]
    half = (held[0] // 2,) + held[1:]
    out_shape = [shape_of(whole, jnp.bfloat16 if last else jnp.float32)] + [shape_of(half, jnp.bfloat16)] * 2
    return pl.pallas_call(
        lambda *refs: backward_kernel(turning, last, layer, len(sources), *refs),
        in_specs=[SMEM, INSIDE, INSIDE] + [OUTSIDE] * (1 + len(sources)),
        out_specs=[OUTSIDE] * len(out_shape),
        out_shape=out_shape,
        scratch_shapes=[
            pltpu.VMEM(whole, jnp.float32),
            pltpu.VMEM(whole, jnp.bfloat16),
            pltpu.VMEM(whole, jnp.bfloat16),
            pltpu.VMEM(whole, jnp.bfloat16),
            pltpu.VMEM(whole, jnp.bfloat16 if last else jnp.float32),
            pltpu.VMEM(held, jnp.bfloat16),
            pltpu.VMEM(held, jnp.bfloat16),
            pltpu.VMEM(whole, jnp.float32),
            pltpu.VMEM(whole if turning else SMALL, jnp.float32),
            pltpu.VMEM(whole if turning else SMALL, jnp.bfloat16),
            pltpu.VMEM(whole if turning else SMALL, jnp.bfloat16),
            pltpu.SemaphoreType.DMA((7, CHUNKS)),
            pltpu.SemaphoreType.DMA((2, PARTS)),
            pltpu.SemaphoreType.DMA((CHUNKS,)),
            pltpu.SemaphoreType.DMA((2, PARTS)),
        ],
        compiler_params=pltpu.CompilerParams(vmem_limit_bytes=VMEM_LIMIT),
        cost_estimate=pl.CostEstimate(
            flops=BACKWARD_COST, bytes_accessed=30 * whole[0] * whole[1], transcendentals=0
        ),
        name="backward_layer",
    )(table, scale, gain, end_gain, *sources)


def join_kernel(rows, *refs):
    sources, whole, sems = refs[:-2], refs[-2], refs[-1]
    copies = [
        pltpu.make_async_copy(source.at[pl.ds(0, rows)], whole.at[pl.ds(at * rows, rows)], sems.at[at])
        for at, source in enumerate(sources)
    ]
    for copy in copies:
        copy.start()
    for copy in copies:
        copy.wait()


def joined(parts, rows=None):
    rows = parts[0].shape[0] if rows is None else rows
    whole = shape_of((rows * len(parts),) + parts[0].shape[1:], parts[0].dtype)
    return pl.pallas_call(
        lambda *refs: join_kernel(rows, *refs),
        in_specs=[OUTSIDE] * len(parts),
        out_specs=INSIDE,
        out_shape=whole,
        scratch_shapes=[pltpu.SemaphoreType.DMA((len(parts),))],
        compiler_params=pltpu.CompilerParams(vmem_limit_bytes=VMEM_LIMIT),
        cost_estimate=pl.CostEstimate(
            flops=0, bytes_accessed=4 * math.prod(whole.shape), transcendentals=0
        ),
        name="join",
    )(*parts)


def sum_kernel(terms, inputs, *refs):
    sources, outs = refs[:inputs], refs[inputs:]
    for group in range(inputs // terms):
        mine = sources[group * terms : (group + 1) * terms]
        for at in range(mine[0].shape[0]):
            total = sum(ref[at].astype(jnp.float32) for ref in mine).astype(jnp.bfloat16)
            if len(outs) > 1:
                outs[at][group] = total
            else:
                outs[0][at, group] = total


def run_sum(groups, parts, apart=True):
    flat = [term.reshape(parts, -1, term.shape[-1]) for terms in groups for term in terms]
    _, rows, lanes = flat[0].shape
    steps = 8
    if apart:
        out_shape = [shape_of((len(groups), rows, lanes), jnp.bfloat16)] * parts
        out_specs = [pl.BlockSpec((len(groups), rows // steps, lanes), lambda i: (0, i, 0))] * parts
    else:
        out_shape = [shape_of((parts, len(groups), rows, lanes), jnp.bfloat16)]
        out_specs = [pl.BlockSpec((parts, len(groups), rows // steps, lanes), lambda i: (0, 0, i, 0))]
    sums = pl.pallas_call(
        lambda *refs: sum_kernel(len(groups[0]), len(flat), *refs),
        grid=(steps,),
        in_specs=[pl.BlockSpec((parts, rows // steps, lanes), lambda i: (0, i, 0))] * len(flat),
        out_specs=out_specs,
        out_shape=out_shape,
        compiler_params=pltpu.CompilerParams(vmem_limit_bytes=VMEM_LIMIT),
        cost_estimate=pl.CostEstimate(
            flops=flat[0].size * len(flat), bytes_accessed=2 * flat[0].size * (len(flat) + 1), transcendentals=0
        ),
        name="sum",
    )(*flat)
    return [out.reshape(-1, lanes) for out in sums] if apart else sums[0].reshape(parts, -1, lanes)


def pieces_kernel(chunk, place_ref, order_ref, left_ref, right_ref, gain_ref, out_ref, held, left_sem, sems):
    layer_count, half, size = held.shape[:3]
    first = place_ref[2] * half
    lefts = pltpu.make_async_copy(left_ref.at[:, pl.ds(first, half)], held, left_sem.at[0])
    lefts.start()
    copies = []
    turns = []
    for section in range(out_ref.shape[0]):
        row = 0
        for layer in range(layer_count):
            for inside in range(chunk):
                turns.append((layer, section * chunk + inside, section, row))
                row += size
            for inside in range(chunk):
                source = right_ref.at[layer, first + section * chunk + inside]
                copies.append((source, out_ref.at[section, pl.ds(row, size)]))
                row += size
        copies.append((gain_ref, out_ref.at[section, pl.ds(row, gain_ref.shape[0])]))
    copies = [
        pltpu.make_async_copy(source, target, sems.at[at]) for at, (source, target) in enumerate(copies)
    ]
    for copy in copies:
        copy.start()
    lefts.wait()
    for layer, block, section, row in turns:
        turned = inner_dot(held[layer, block], order_ref[...], 1, 0)
        out_ref[section, pl.ds(row, size), :] = turned.astype(jnp.bfloat16)
    for copy in copies:
        copy.wait()


def factor_pieces(place, order, left, right, gain_rows, chunk, width):
    layer_count, blocks, size = left.shape[:3]
    rows = layer_count * 2 * chunk * size + gain_rows.shape[0]
    return pl.pallas_call(
        lambda *refs: pieces_kernel(chunk, *refs),
        in_specs=[SMEM, INSIDE] + [OUTSIDE] * 3,
        out_specs=INSIDE,
        out_shape=shape_of((width, rows, size), jnp.bfloat16),
        scratch_shapes=[
            pltpu.VMEM((layer_count, blocks // 2, size, size), jnp.bfloat16),
            pltpu.SemaphoreType.DMA((1,)),
            pltpu.SemaphoreType.DMA((width * (layer_count * chunk + 1),)),
        ],
        compiler_params=pltpu.CompilerParams(vmem_limit_bytes=VMEM_LIMIT),
        cost_estimate=pl.CostEstimate(flops=left.size * size, bytes_accessed=4 * left.size, transcendentals=0),
        name="pieces",
    )(place, order, left, right, gain_rows)


def choice(pairs, critic, slots):
    rows = pairs.shape[0]
    named = (pairs[:, 0:1] == critic) | (pairs[:, 1:2] == critic)
    named = jnp.broadcast_to(named.astype(jnp.float32), (rows, slots))
    before = lax.broadcasted_iota(jnp.int32, (rows, rows), 1) < lax.broadcasted_iota(jnp.int32, (rows, rows), 0)
    rank = inner_dot(before.astype(jnp.bfloat16), named.astype(jnp.bfloat16), 1, 0)
    at = lax.broadcasted_iota(jnp.int32, (rows, slots), 1).astype(jnp.float32)
    return jnp.where(rank == at, named, 0.0).astype(jnp.bfloat16)


def pick_kernel(pairs_ref, values_ref, out_ref):
    width, features, slots = out_ref.shape
    pairs = pairs_ref[...]
    chosen = [choice(pairs, critic, slots) for critic in range(width)]
    step = 512
    for start in range(0, features, step):
        part = values_ref[:, pl.ds(start, step)]
        for k in range(width):
            out_ref[k, pl.ds(start, step), :] = inner_dot(part, chosen[k], 0, 0).astype(jnp.bfloat16)


def run_pick(pairs, values, width, slots):
    rows, features = values.shape
    return pl.pallas_call(
        pick_kernel,
        in_specs=[INSIDE] * 2,
        out_specs=INSIDE,
        out_shape=shape_of((width, features, slots), jnp.bfloat16),
        compiler_params=pltpu.CompilerParams(vmem_limit_bytes=VMEM_LIMIT),
        cost_estimate=pl.CostEstimate(
            flops=2 * rows * features * slots * width, bytes_accessed=8 * rows * features, transcendentals=0
        ),
        name="pick",
    )(pairs, values)


def combine_kernel(pairs_ref, came_ref, out_ref):
    width, features, slots = came_ref.shape
    pairs = pairs_ref[...]
    chosen = [choice(pairs, critic, slots) for critic in range(width)]
    step = 512
    for start in range(0, features, step):
        total = sum(inner_dot(chosen[k], came_ref[k, pl.ds(start, step), :], 1, 1) for k in range(width))
        out_ref[:, pl.ds(start, step)] = (0.5 * total).astype(jnp.bfloat16)


def run_combine(pairs, came):
    rows = pairs.shape[0]
    return pl.pallas_call(
        combine_kernel,
        in_specs=[INSIDE] * 2,
        out_specs=INSIDE,
        out_shape=shape_of((rows, came.shape[1]), jnp.bfloat16),
        compiler_params=pltpu.CompilerParams(vmem_limit_bytes=VMEM_LIMIT),
        cost_estimate=pl.CostEstimate(
            flops=2 * rows * came.size, bytes_accessed=4 * came.size, transcendentals=0
        ),
        name="combine",
    )(pairs, came)


FORWARD_COST = 15_000_000_000
BACKWARD_COST = 18_000_000_000


def assemble_kernel(layers, factor, place_ref, order_ref, *refs):
    count = 2 * len(layers)
    sources, (left_ref, right_ref) = refs[:count], refs[count : count + 2]
    held, wide = refs[count + 2 : 2 * count + 2], refs[2 * count + 2 : 3 * count + 2]
    in_sems, out_sems = refs[3 * count + 2 :]
    origin, core = place_ref[0] ^ place_ref[1], place_ref[2]
    order = order_ref[...]
    arrivals = [
        pltpu.make_async_copy(source, held[at], in_sems.at[at]) for at, source in enumerate(sources)
    ]
    for copy in arrivals:
        copy.start()
    leaving = []
    for at in range(count):
        arrivals[at].wait()
        half = core if at % 2 == 0 else 1 - core
        width, _, _, chunk = held[at].shape[:4]
        for k in range(width):
            start = (half * width + (origin ^ k if at < 2 else k)) * chunk
            for inside, layer in enumerate(layers[at // 2]):
                for block in range(chunk):
                    left = inner_dot(held[at][k, inside, 0, block], order, 1, 1)
                    wide[at][k, inside, 0, block] = left * factor
                wide[at][k, inside, 1] = held[at][k, inside, 1].astype(jnp.float32) * factor
                for which, target in enumerate((left_ref, right_ref)):
                    copy = pltpu.make_async_copy(
                        wide[at].at[k, inside, which],
                        target.at[layer, pl.ds(start, chunk)],
                        out_sems.at[len(leaving)],
                    )
                    copy.start()
                    leaving.append(copy)
    for copy in leaving:
        copy.wait()


def run_assemble(place, order, pieces, layers, factor):
    piece = pieces[0].shape
    layer_count = sum(len(group) for group in layers)
    out = shape_of((layer_count, 2 * piece[0] * piece[3]) + piece[4:], jnp.float32)
    return pl.pallas_call(
        lambda *refs: assemble_kernel(layers, factor, *refs),
        in_specs=[SMEM, INSIDE] + [OUTSIDE] * len(pieces),
        out_specs=[OUTSIDE] * 2,
        out_shape=[out] * 2,
        scratch_shapes=[pltpu.VMEM(part.shape, jnp.bfloat16) for part in pieces]
        + [pltpu.VMEM(part.shape, jnp.float32) for part in pieces]
        + [
            pltpu.SemaphoreType.DMA((len(pieces),)),
            pltpu.SemaphoreType.DMA((4 * layer_count * piece[0],)),
        ],
        compiler_params=pltpu.CompilerParams(vmem_limit_bytes=VMEM_LIMIT),
        cost_estimate=pl.CostEstimate(flops=0, bytes_accessed=4 * math.prod(out.shape) * 3, transcendentals=0),
        name="assemble",
    )(place, order, *pieces)


def plane_routes(width, replicas):
    bits = width.bit_length() - 1
    orders = [[(step + d) % bits for step in range(bits)] for d in range(replicas)]
    every = [(s, t, d) for s in range(width) for t in range(width) for d in range(replicas)]

    def route(move):
        def index(s, t, d):
            return (s * width + t) * replicas + d

        return [(index(*place), index(*move(*place))) for place in every]

    ranks = [[0] * width for _ in range(replicas)]
    for d in range(replicas):
        for r in range(width):
            ranks[d][sum(((r >> at) & 1) << orders[d][at] for at in range(bits))] = r
    return {
        "across": [route(lambda s, t, d, at=at: (s ^ (1 << orders[d][at]), t, d)) for at in range(bits)],
        "cores": route(lambda s, t, d: (s, t, 1 - d)),
        "sections": [route(lambda s, t, d, k=k: (s ^ k, t, d)) for k in range(width)],
        "homes": [route(lambda s, t, d, j=j: (t, t ^ s ^ j, d)) for j in range(width)],
    }, ranks


def plane_shards(patches, teacher, critic_pairs, left_factors, right_factors, norm_gains):
    width = lax.axis_size("section")
    replicas = lax.axis_size("dp")
    tok_rows, feat_local = patches.shape
    layer_count, local_blocks, size = left_factors.shape[1:4]
    blocks = feat_local * width // size
    wide = 2 * tok_rows // 3
    chunk = local_blocks // (replicas * width)
    layer_rows = 2 * chunk * size
    routes, ranks = plane_routes(width, replicas)
    section = lax.axis_index("section")
    tensor = lax.axis_index("tensor")
    core = lax.axis_index("dp")
    place = jnp.stack([section, tensor, core]).astype(jnp.int32)
    tie = lax.optimization_barrier

    def move(value, route):
        return lax.ppermute(value, AXES, route)

    def move_all(values, name):
        return [move(value, route) for value, route in zip(values, routes[name])]

    def send(values, name):
        return [values[0]] + [move(values[k], routes[name][k]) for k in range(1, width)]

    def gather_one(mine):
        return joined([mine, move(mine, routes["across"][0])])

    def gather_two(pair):
        return pair, move(pair, routes["across"][1]), move(pair, routes["cores"])

    def gather_three(pair, other, peer):
        return [pair, other, peer, move(other, routes["cores"])]

    def as_weights(parts):
        return [part.reshape(2 * width, -1, 2, chunk, size, size) for part in parts]

    block = jnp.arange(blocks, dtype=jnp.int32)
    inside = block % local_blocks
    replica = inside // (width * chunk)
    part = (replica != core).astype(jnp.int32)
    distance = section ^ ((inside // chunk) % width)
    quarter = block // local_blocks
    rank = jnp.array(ranks, jnp.int32)[replica, distance]
    table = jnp.stack(
        [
            ((part * width + index) * width + piece) * chunk + inside % chunk
            for index, piece in (
                (rank, quarter),
                (distance, quarter),
                (distance, tensor ^ section ^ distance ^ quarter),
            )
        ]
    ).astype(jnp.int32)

    def to_planes(value):
        return lax.all_to_all(value, "tensor", split_axis=0, concat_axis=0, tiled=True)

    def to_sections(value):
        return lax.all_to_all(value, "section", split_axis=0, concat_axis=0, tiled=True)

    half_layers = layer_count // 2
    groups = [tuple(range(half_layers)), tuple(range(half_layers, layer_count))]
    fold = size // blocks
    columns = jnp.arange(size)
    order = (columns[:, None] == (columns % blocks) * fold + columns // blocks).astype(jnp.bfloat16)
    gain_rows = norm_gains[0].reshape(-1, size)
    pieces = factor_pieces(place, order, left_factors[0], right_factors[0], gain_rows, chunk, width)
    pieces, patches, teacher = tie((pieces, patches, teacher))
    spread = to_sections(pieces)
    patch_sent = run_pick(critic_pairs, patches, width, wide)
    target_sent = run_pick(critic_pairs, teacher, width, wide)
    spread, patch_sent, target_sent = tie((spread, patch_sent, target_sent))
    lifted = to_planes(spread)
    lifted, patch_sent = tie((lifted, patch_sent))
    patch_came = to_planes(patch_sent).reshape(-1, wide)
    lowest = [lifted[:, group[0] * layer_rows : (group[-1] + 1) * layer_rows] for group in groups]
    beside = move(lowest[0], routes["across"][0])
    gains = lifted[:, layer_count * layer_rows :].reshape(width, layer_count + 1, local_blocks, size)
    gains = gains.transpose(1, 3, 0, 2).reshape(layer_count + 1, size, blocks)
    end_column = jnp.broadcast_to(gains[layer_count].T[:, :, None], (blocks, size, wide)).reshape(-1, wide)
    lowest, beside = tie((lowest, beside))
    first_two = gather_two(joined([lowest[0], beside]))
    first_two, lowest[1], patch_came = tie((first_two, lowest[1], patch_came))
    weights = [as_weights(gather_three(*first_two))]
    later = (lowest[1], move(lowest[1], routes["across"][0]))
    weights, later, end_column = tie((weights, later, end_column))

    residual, target_sent = tie((patch_came, target_sent))
    target = to_planes(target_sent).reshape(-1, wide)
    flying = gather_two(joined(list(later)))
    sums = jnp.zeros((8, wide), jnp.float32)
    stored = []
    for layer in range(layer_count):
        group = 0 if layer in groups[0] else 1
        following, u, z, slope, scale, sums = run_forward(
            table, gains[layer], sums, residual, weights[group], layer - groups[group][0]
        )
        stored.append(((slope, z, u), scale, residual))
        residual = following
        if layer == 0:
            residual, sums, flying = tie((residual, sums, flying))
            weights.append(as_weights(gather_three(*flying)))
        if layer == groups[0][-1]:
            residual, sums, weights[1] = tie((residual, sums, weights[1]))
        if layer == layer_count - 2:
            residual, sums, target = tie((residual, sums, target))

    def core_sum(mine, other):
        return (mine, move(other, routes["cores"]))

    def plane_sum(mine, other):
        return send(run_sum([(mine, other)], width), "sections")

    def homeward(parts):
        return move_all(run_sum(parts, width), "homes")

    def both_halves(whole):
        pair = (whole, move(whole, routes["cores"]))
        return [part.reshape(width, -1, 2, chunk, size, size) for part in pair]

    steps = (core_sum, plane_sum)
    gradient = residual
    underway = []
    for layer in range(layer_count - 1, -1, -1):
        turning = layer == layer_count - 1
        last = layer == 0
        kept, scale, inputs = stored[layer]
        group = 0 if layer in groups[0] else 1
        sources = (gradient, inputs, target) if turning else (gradient, inputs)
        underway = [(at + 1, steps[at](*state)) if at < len(steps) else (at, state) for at, state in underway]
        gradient, mine, other = run_backward(
            table,
            gains[layer],
            end_column,
            scale,
            kept,
            weights[group],
            layer - groups[group][0],
            sources,
            turning,
            last,
        )
        gradient, mine, other, states = tie((gradient, mine, other, [state for _, state in underway]))
        underway = [(at, state) for (at, _), state in zip(underway, states)]
        underway.append((0, (mine, other)))

    returned = to_planes(gradient.reshape(width, feat_local, wide))
    ended = [steps[at](*state) if at < len(steps) else state for at, state in underway][::-1]
    ended = tie(ended)
    ended[0] = plane_sum(*ended[0])
    others = to_planes(run_sum(ended[1:], width, apart=False))
    ended[0], returned, others = tie((ended[0], returned, others))
    home = homeward(ended[:1])
    d_patches = run_combine(critic_pairs, returned)
    others = to_sections(others)
    d_patches, home, others = tie((d_patches, home, others))
    homes_of = both_halves(joined(home)) + both_halves(others)
    grad_factor = 1.0 / math.sqrt(2 * tok_rows * width * replicas)
    grad_left, grad_right = run_assemble(
        place, order, homes_of, [(0,), tuple(range(1, layer_count))], grad_factor
    )
    return (d_patches, grad_left[None], grad_right[None])


def solution(mesh):
    in_specs = (
        P(("section", "dp"), "tensor"),
        P(("section", "dp"), "tensor"),
        P(("section", "dp"), None),
        P("section", None, "tensor", None, None),
        P("section", None, "tensor", None, None),
        P("section", None, "tensor"),
    )
    out_specs = (
        P(("section", "dp"), "tensor"),
        P("section", None, "tensor", None, None),
        P("section", None, "tensor", None, None),
    )
    body = plane_shards if planes_fit(mesh) else layered_shards
    return jax.shard_map(
        body, mesh=mesh, in_specs=in_specs, out_specs=out_specs, check_vma=False)
```

```python
import math

import jax
import jax.numpy as jnp
from jax import lax
from jax.experimental import pallas as pl
from jax.experimental.pallas import tpu as pltpu
from jax.sharding import PartitionSpec as P

EPSILON = 1e-06
TANH_SLOPE = 0.7978845608028654
CUBIC_TERM = 0.044715


def shifted(value, axis, steps):
    count = lax.axis_size(axis)
    first, last = (max(0, -steps), min(count, count - steps))
    return lax.ppermute(value, axis, [(source, source + steps) for source in range(first, last)])


def gelu_value(values):
    tangent = jnp.tanh(TANH_SLOPE * (values + CUBIC_TERM * values * values * values))
    return 0.5 * values * (1.0 + tangent)


def gelu_slope(values):
    tangent = jnp.tanh(TANH_SLOPE * (values + CUBIC_TERM * values * values * values))
    return 0.5 * (1.0 + tangent) + 0.5 * values * (1.0 - tangent * tangent) * TANH_SLOPE * (
        1.0 + 3.0 * CUBIC_TERM * values * values
    )


def norm_pair(residuals, gain_pair, model_width):
    squares = lax.psum(
        (
            jnp.sum(residuals[0] * residuals[0], axis=(1, 2)),
            jnp.sum(residuals[1] * residuals[1], axis=(1, 2)),
        ),
        "tensor",
    )
    factors = [lax.rsqrt(squares[member] / model_width + EPSILON) for member in range(2)]
    normed = [
        residuals[member] * factors[member][:, None, None] * gain_pair[member][None]
        for member in range(2)
    ]
    return (factors, normed)


def norm_back_pair(residuals, factors, gain_pair, grad_normed, carried, model_width):
    weighted = [grad_normed[member] * gain_pair[member][None] for member in range(2)]
    inners = lax.psum(
        (
            jnp.sum(weighted[0] * residuals[0], axis=(1, 2)),
            jnp.sum(weighted[1] * residuals[1], axis=(1, 2)),
        ),
        "tensor",
    )
    return [
        carried[member]
        + factors[member][:, None, None] * weighted[member]
        - residuals[member] * (factors[member] ** 3 * inners[member] / model_width)[:, None, None]
        for member in range(2)
    ]


def layered_shards(patches, teacher, critic_pairs, left_factors, right_factors, norm_gains):
    sections = lax.axis_size("section")
    tensor_width = lax.axis_size("tensor")
    replicas = lax.axis_size("dp")
    tok_rows = patches.shape[0]
    feat_local = patches.shape[1]
    layer_count = left_factors.shape[1]
    local_blocks = left_factors.shape[2]
    block_size = left_factors.shape[3]
    all_blocks = local_blocks * tensor_width
    fold_ratio = block_size // all_blocks
    model_width = feat_local * tensor_width
    sixth_rows = tok_rows // 6
    leading = 2 * sixth_rows
    critic_ids = jnp.arange(4, dtype=jnp.int32)
    named_by = (
        (critic_pairs[:, 0:1] == critic_ids[None, :])
        | (critic_pairs[:, 1:2] == critic_ids[None, :])
    ).astype(jnp.int32)
    ranking = jnp.cumsum(named_by, axis=0) - 1
    wide_ids = critic_ids[None, :] < 2
    slot_width = 3 * sixth_rows
    spilled = wide_ids & (ranking >= 3 * sixth_rows)
    destination = jnp.where(spilled, critic_ids[None, :] + 2, critic_ids[None, :])
    slot_index = jnp.where(spilled, ranking - sixth_rows, ranking)
    flat_slot = destination * slot_width + slot_index
    chosen = jnp.take_along_axis(flat_slot, critic_pairs, axis=1)
    slot_total = sections * slot_width
    row_ids = jnp.broadcast_to(jnp.arange(tok_rows, dtype=jnp.int32)[:, None], chosen.shape)
    source_row = (
        jnp.full((slot_total,), tok_rows, jnp.int32).at[chosen.reshape(-1)].set(row_ids.reshape(-1))
    )
    send_patch = (
        patches.at[source_row]
        .get(mode="fill", fill_value=0)
        .reshape(sections, slot_width, local_blocks, block_size)
    )
    send_target = (
        teacher.at[source_row]
        .get(mode="fill", fill_value=0)
        .reshape(sections, slot_width, local_blocks, block_size)
    )
    recv_patch, recv_target = (
        lax.all_to_all(send_patch, "section", split_axis=0, concat_axis=0, tiled=True),
        lax.all_to_all(send_target, "section", split_axis=0, concat_axis=0, tiled=True),
    )
    residuals = [
        recv_patch[:, :leading].reshape(-1, local_blocks, block_size).astype(jnp.float32),
        recv_patch[:, leading:].reshape(-1, local_blocks, block_size).astype(jnp.float32),
    ]
    targets = [
        recv_target[:, :leading].reshape(-1, local_blocks, block_size).astype(jnp.float32),
        recv_target[:, leading:].reshape(-1, local_blocks, block_size).astype(jnp.float32),
    ]
    native = (left_factors[0], right_factors[0], norm_gains[0])
    borrowed = shifted((left_factors, right_factors, norm_gains), "section", 2)
    is_wide = lax.axis_index("section") < 2
    second = (
        jnp.where(is_wide, left_factors, borrowed[0])[0],
        jnp.where(is_wide, right_factors, borrowed[1])[0],
        jnp.where(is_wide, norm_gains, borrowed[2])[0],
    )
    left_sets = (native[0], second[0])
    right_sets = (native[1], second[1])
    gain_sets = (
        native[2].astype(jnp.float32).reshape(layer_count + 1, local_blocks, block_size),
        second[2].astype(jnp.float32).reshape(layer_count + 1, local_blocks, block_size),
    )
    stored = []
    for layer_index in range(layer_count):
        gain_pair = [gain_sets[0][layer_index], gain_sets[1][layer_index]]
        factors, normed = norm_pair(residuals, gain_pair, model_width)
        normed = [normed[member].astype(jnp.bfloat16) for member in range(2)]
        first_out = [
            jnp.einsum(
                "nki,kij->nkj",
                normed[member],
                left_sets[member][layer_index],
                preferred_element_type=jnp.float32,
            ).astype(jnp.bfloat16)
            for member in range(2)
        ]
        permuted = (
            lax.all_to_all(first_out[0], "tensor", split_axis=2, concat_axis=1, tiled=True),
            lax.all_to_all(first_out[1], "tensor", split_axis=2, concat_axis=1, tiled=True),
        )
        permuted = [
            permuted[member].reshape(
                permuted[member].shape[0], all_blocks, local_blocks, fold_ratio
            )
            for member in range(2)
        ]
        right_quads = [
            right_sets[member][layer_index].reshape(
                local_blocks, fold_ratio, all_blocks, block_size
            )
            for member in range(2)
        ]
        mixture = [
            jnp.einsum(
                "nkmp,mpkl->nml",
                permuted[member],
                right_quads[member],
                preferred_element_type=jnp.float32,
            )
            for member in range(2)
        ]
        stored.append((residuals, factors, normed, permuted, mixture, right_quads, gain_pair))
        residuals = [residuals[member] + gelu_value(mixture[member]) for member in range(2)]
    final_gains = [gain_sets[0][layer_count], gain_sets[1][layer_count]]
    factors, outputs = norm_pair(residuals, final_gains, model_width)
    gradients = norm_back_pair(
        residuals,
        factors,
        final_gains,
        [outputs[member] - targets[member] for member in range(2)],
        [jnp.zeros_like(residuals[member]) for member in range(2)],
        model_width,
    )
    left_terms = []
    right_terms = []
    for layer_index in range(layer_count - 1, -1, -1):
        inputs, factors, normed, permuted, mixture, right_quads, gain_pair = stored[layer_index]
        slopes = [
            (gradients[member] * gelu_slope(mixture[member])).astype(jnp.bfloat16)
            for member in range(2)
        ]
        right_grad = [
            jnp.einsum(
                "nkmp,nml->mpkl",
                permuted[member],
                slopes[member],
                preferred_element_type=jnp.float32,
            ).reshape(local_blocks, block_size, block_size)
            for member in range(2)
        ]
        back_moved = [
            jnp.einsum(
                "nml,mpkl->nkmp",
                slopes[member],
                right_quads[member],
                preferred_element_type=jnp.float32,
            )
            .astype(jnp.bfloat16)
            .reshape(slopes[member].shape[0], all_blocks, local_blocks * fold_ratio)
            for member in range(2)
        ]
        arrived = (
            lax.all_to_all(back_moved[0], "tensor", split_axis=1, concat_axis=2, tiled=True),
            lax.all_to_all(back_moved[1], "tensor", split_axis=1, concat_axis=2, tiled=True),
        )
        left_grad = [
            jnp.einsum(
                "nki,nkj->kij", normed[member], arrived[member], preferred_element_type=jnp.float32
            )
            for member in range(2)
        ]
        grad_normed = [
            jnp.einsum(
                "nkj,kij->nki",
                arrived[member],
                left_sets[member][layer_index],
                preferred_element_type=jnp.float32,
            )
            for member in range(2)
        ]
        gradients = norm_back_pair(inputs, factors, gain_pair, grad_normed, gradients, model_width)
        layer_left = jnp.stack(left_grad)
        layer_right = jnp.stack(right_grad)
        layer_left, layer_right = (
            lax.psum(layer_left.astype(jnp.bfloat16), "dp").astype(jnp.float32),
            lax.psum(layer_right.astype(jnp.bfloat16), "dp").astype(jnp.float32),
        )
        left_terms.insert(0, layer_left)
        right_terms.insert(0, layer_right)
    left_stack = jnp.stack(left_terms)
    right_stack = jnp.stack(right_terms)
    repaid = (
        shifted(left_stack[:, 1].astype(jnp.bfloat16), "section", -2).astype(jnp.float32),
        shifted(right_stack[:, 1].astype(jnp.bfloat16), "section", -2).astype(jnp.float32),
    )
    is_wide = lax.axis_index("section") < 2
    left_total = left_stack[:, 0] + jnp.where(is_wide, left_stack[:, 1] + repaid[0], 0.0)
    right_total = right_stack[:, 0] + jnp.where(is_wide, right_stack[:, 1] + repaid[1], 0.0)
    grad_factor = 1.0 / math.sqrt(2 * tok_rows * sections * replicas)
    returned = [
        gradients[member].astype(jnp.bfloat16).reshape(sections, -1, local_blocks, block_size)
        for member in range(2)
    ]
    back_lead, back_trail = (
        lax.all_to_all(returned[0], "section", split_axis=0, concat_axis=0, tiled=True),
        lax.all_to_all(returned[1], "section", split_axis=0, concat_axis=0, tiled=True),
    )
    gathered = jnp.concatenate((back_lead, back_trail), axis=1).reshape(
        slot_total, local_blocks, block_size
    )
    combined = (
        gathered[chosen[:, 0]].astype(jnp.float32) + gathered[chosen[:, 1]].astype(jnp.float32)
    ) * 0.5
    d_patches = combined.astype(jnp.bfloat16).reshape(tok_rows, feat_local)
    return (d_patches, (left_total * grad_factor)[None], (right_total * grad_factor)[None])


VMEM_LIMIT = 60 * 1024 * 1024
CHUNKS = 8
TOGETHER = 4
PARTS = 4
SMALL = (16, 128)
AXES = ("section", "tensor", "dp")


def planes_fit(mesh):
    sections = mesh.shape["section"]
    paired = mesh.shape["dp"] == 2 and sections & (sections - 1) == 0
    return paired and mesh.shape["tensor"] == sections


def inner_dot(left, right, left_dim, right_dim):
    return lax.dot_general(
        left,
        right,
        (((left_dim,), (right_dim,)), ((), ())),
        preferred_element_type=jnp.float32,
    )


def fold_rows(values):
    return jnp.sum(values.reshape(values.shape[0] // 8, 8, values.shape[1]), axis=0)


def block_rows(block, size):
    return pl.ds(pl.multiple_of(block * size, size), size)


def column(gain_ref, block, slots):
    blocks = gain_ref.shape[1]
    picked = lax.broadcasted_iota(jnp.int32, (blocks, slots), 0) == block
    return inner_dot(gain_ref[...], picked.astype(jnp.bfloat16), 1, 0)


def chunk_copy(source, target, sems, chunk):
    rows = target.shape[0] // CHUNKS
    at = pl.ds(pl.multiple_of(chunk * rows, rows), rows)
    return pltpu.make_async_copy(source.at[at], target.at[at], sems.at[chunk])


def start_chunks(source, target, sems):
    for chunk in range(CHUNKS):
        chunk_copy(source, target, sems, chunk).start()


def wait_chunks(source, target, sems):
    for chunk in range(CHUNKS):
        chunk_copy(source, target, sems, chunk).wait()


def factor_copies(parts, layer, held, sems, side):
    count = parts[0].shape[0]
    return [
        pltpu.make_async_copy(
            ref.at[:, layer, side], held.at[pl.ds(at * count, count), side], sems.at[side, at]
        )
        for at, ref in enumerate(parts)
    ]


def gradient_copies(held, parts, sems, side):
    count = parts[0].shape[0]
    return [
        pltpu.make_async_copy(
            held.at[pl.ds(at * count, count), side], ref.at[:, side], sems.at[side, at]
        )
        for at, ref in enumerate(parts)
    ]


def by_chunk(blocks, step, carry, before=None, after=None):
    per_chunk = blocks // CHUNKS

    def few(start, carry):
        stores = []
        for at in range(TOGETHER):
            made, carry = step(start + at, carry)
            stores += made
        for ref, index, value in stores:
            ref[index] = value
        return carry

    def one(chunk, carry):
        if before is not None:
            before(chunk)
        for at in range(0, per_chunk, TOGETHER):
            carry = few(chunk * per_chunk + at, carry)
        if after is not None:
            after(chunk)
        return carry

    return lax.fori_loop(0, CHUNKS, one, carry)


def forward_kernel(first, layer, inputs, table_ref, sums_ref, gain_ref, *refs):
    sources, refs = refs[:inputs], refs[inputs:]
    parts, sources = sources[:PARTS], sources[PARTS:]
    out_ref, u_ref, z_ref, slope_ref, scale_ref, next_ref = refs[:6]
    raw, h, w, u, z, slope, mid, in_sems, w_sems, out_sems = refs[6:]
    features, slots = h.shape
    size = w.shape[-1]
    chunk_blocks = w.shape[2]
    blocks = features // size
    fold = size // blocks

    left_in = factor_copies(parts, layer, w, w_sems, 0)
    right_in = factor_copies(parts, layer, w, w_sems, 1)
    if first:
        start_chunks(sources[0], raw, in_sems)
        for copy in left_in + right_in:
            copy.start()

        def squares(block, total):
            rows = block_rows(block, size)
            part = raw[rows, :].astype(jnp.float32)
            return [(h, (rows, slice(None)), part)], total + fold_rows(part * part)

        total = by_chunk(
            blocks,
            squares,
            jnp.zeros((8, slots), jnp.float32),
            lambda chunk: chunk_copy(sources[0], raw, in_sems, chunk).wait(),
        )
    else:
        for copy in left_in:
            copy.start()
        start_chunks(sources[0], h, in_sems)
        for copy in right_in:
            copy.start()
        total = sums_ref[...]
    scale = lax.rsqrt(jnp.sum(total, axis=0, keepdims=True) / features + EPSILON)
    scale_ref[...] = jnp.broadcast_to(scale, scale_ref.shape)
    for copy in left_in:
        copy.wait()

    def arrive(chunk):
        if not first:
            chunk_copy(sources[0], h, in_sems, chunk).wait()

    def left(block, carry):
        rows = block_rows(block, size)
        place = table_ref[0, block]
        normed = (h[rows, :] * scale * column(gain_ref, block, slots)).astype(jnp.bfloat16)
        weight = w[place // chunk_blocks, 0, place % chunk_blocks]
        first_out = inner_dot(weight, normed, 0, 0)
        at = (rows, slice(None))
        return [(u, at, normed), (mid, at, first_out)], carry

    def leave_left(chunk):
        chunk_copy(u, u_ref, out_sems.at[0], chunk).start()

    by_chunk(blocks, left, 0, arrive, leave_left)
    for copy in right_in:
        copy.wait()

    def right(block, total):
        rows = block_rows(block, size)
        place = table_ref[0, block]
        moved = [mid[pl.ds(q * blocks + block, blocks, stride=size), :] for q in range(fold)]
        moved = jnp.concatenate(moved, axis=0).astype(jnp.bfloat16)
        weight = w[place // chunk_blocks, 1, place % chunk_blocks]
        mixture = inner_dot(weight, moved, 0, 0)
        squared = mixture * mixture
        tangent = jnp.tanh(mixture * (TANH_SLOPE + (TANH_SLOPE * CUBIC_TERM) * squared))
        half = 0.5 + 0.5 * tangent
        following = h[rows, :] + mixture * half
        steep = half + mixture * (1.0 - tangent * tangent) * (
            0.5 * TANH_SLOPE + (1.5 * TANH_SLOPE * CUBIC_TERM) * squared
        )
        at = (rows, slice(None))
        stores = [(z, at, moved), (h, at, following), (slope, at, steep.astype(jnp.bfloat16))]
        return stores, total + fold_rows(following * following)

    leaving = ((h, out_ref, 1), (z, z_ref, 2), (slope, slope_ref, 3))

    def leave_right(chunk):
        for source, target, at in leaving:
            chunk_copy(source, target, out_sems.at[at], chunk).start()

    next_ref[...] = by_chunk(blocks, right, jnp.zeros((8, slots), jnp.float32), None, leave_right)
    for source, target, at in ((u, u_ref, 0),) + leaving:
        wait_chunks(source, target, out_sems.at[at])


def backward_kernel(turning, last, layer, inputs, table_ref, scale_ref, gain_ref, end_gain_ref, *refs):
    sources, refs = refs[:inputs], refs[inputs:]
    slope_ref, z_ref, u_ref = sources[:3]
    parts, sources = sources[3 : 3 + PARTS], sources[3 + PARTS :]
    out_ref, own_grad, peer_grad = refs[:3]
    g, slope, z, u, h, w, gw, mid, top, goal, end_gain = refs[3:14]
    in_sems, w_sems, out_sems, gw_sems = refs[14:]
    features, slots = g.shape
    size = w.shape[-1]
    chunk_blocks = w.shape[2]
    blocks = features // size
    fold = size // blocks

    left_in = factor_copies(parts, layer, w, w_sems, 0)
    right_in = factor_copies(parts, layer, w, w_sems, 1)
    g_ref, h_ref = sources[:2]
    if turning:
        start_chunks(g_ref, top, in_sems.at[0])
        start_chunks(end_gain_ref, end_gain, in_sems.at[6])
        start_chunks(sources[2], goal, in_sems.at[5])
    else:
        start_chunks(g_ref, g, in_sems.at[0])
    for copy in right_in:
        copy.start()
    start_chunks(slope_ref, slope, in_sems.at[1])
    start_chunks(z_ref, z, in_sems.at[2])
    for copy in left_in:
        copy.start()
    start_chunks(u_ref, u, in_sems.at[3])
    start_chunks(h_ref, h, in_sems.at[4])

    if turning:
        zero = jnp.zeros((8, slots), jnp.float32)

        def sums(block, totals):
            rows = block_rows(block, size)
            part = top[rows, :]
            scaled = part * end_gain[rows, :].astype(jnp.float32)
            return [], (
                totals[0] + fold_rows(part * part),
                totals[1] + fold_rows(scaled * scaled),
                totals[2] + fold_rows(scaled * goal[rows, :].astype(jnp.float32)),
            )

        def arrive_top(chunk):
            chunk_copy(g_ref, top, in_sems.at[0], chunk).wait()
            chunk_copy(end_gain_ref, end_gain, in_sems.at[6], chunk).wait()
            chunk_copy(sources[2], goal, in_sems.at[5], chunk).wait()

        totals = by_chunk(blocks, sums, (zero, zero, zero), arrive_top)
        squares, gained, crossed = [jnp.sum(total, axis=0, keepdims=True) for total in totals]
        end_scale = lax.rsqrt(squares / features + EPSILON)
        end_back = end_scale * end_scale * end_scale * (end_scale * gained - crossed) / features

    for copy in right_in:
        copy.wait()

    def arrive_right(chunk):
        if not turning:
            chunk_copy(g_ref, g, in_sems.at[0], chunk).wait()
        chunk_copy(slope_ref, slope, in_sems.at[1], chunk).wait()
        chunk_copy(z_ref, z, in_sems.at[2], chunk).wait()

    def right(block, carry):
        rows = block_rows(block, size)
        place, home = table_ref[0, block], table_ref[2 if last else 1, block]
        at = (place // chunk_blocks, 1, place % chunk_blocks)
        to = (home // chunk_blocks, 1, home % chunk_blocks)
        if turning:
            part = top[rows, :]
            factor = end_gain[rows, :].astype(jnp.float32)
            error = (part * end_scale * factor - goal[rows, :].astype(jnp.float32)) * factor
            gradient = end_scale * error - part * end_back
            stores = [(g, (rows, slice(None)), gradient)]
        else:
            gradient = g[rows, :]
            stores = []
        steep = (gradient * slope[rows, :].astype(jnp.float32)).astype(jnp.bfloat16)
        stores.append((gw, to, inner_dot(z[rows, :], steep, 1, 1).astype(jnp.bfloat16)))
        stores.append((mid, (rows, slice(None)), inner_dot(w[at], steep, 1, 0)))
        return stores, carry

    by_chunk(blocks, right, 0, arrive_right)
    right_out = gradient_copies(gw, (own_grad, peer_grad), gw_sems, 1)
    for copy in right_out:
        copy.start()
    for copy in left_in:
        copy.wait()
    scale = scale_ref[0:1, :]

    def arrive_left(chunk):
        chunk_copy(u_ref, u, in_sems.at[3], chunk).wait()
        chunk_copy(h_ref, h, in_sems.at[4], chunk).wait()

    def left(block, total):
        rows = block_rows(block, size)
        place, home = table_ref[0, block], table_ref[2 if last else 1, block]
        at = (place // chunk_blocks, 0, place % chunk_blocks)
        to = (home // chunk_blocks, 0, home % chunk_blocks)
        arrived = [mid[pl.ds(q * blocks + block, blocks, stride=size), :] for q in range(fold)]
        arrived = jnp.concatenate(arrived, axis=0).astype(jnp.bfloat16)
        factor_grad = inner_dot(u[rows, :], arrived, 1, 1).astype(jnp.bfloat16)
        weighted = inner_dot(w[at], arrived, 1, 0) * column(gain_ref, block, slots)
        carried = g[rows, :] + scale * weighted
        stores = [(gw, to, factor_grad), (g, (rows, slice(None)), carried)]
        return stores, total + fold_rows(weighted * h[rows, :].astype(jnp.float32))

    total = by_chunk(blocks, left, jnp.zeros((8, slots), jnp.float32), arrive_left)
    left_out = gradient_copies(gw, (own_grad, peer_grad), gw_sems, 0)
    for copy in left_out:
        copy.start()
    back = scale * scale * scale * jnp.sum(total, axis=0, keepdims=True) / features

    def finish(block, carry):
        rows = block_rows(block, size)
        ended = g[rows, :] - h[rows, :].astype(jnp.float32) * back
        at = (rows, slice(None))
        return [(u, at, ended.astype(jnp.bfloat16)) if last else (g, at, ended)], carry

    ended = u if last else g
    by_chunk(blocks, finish, 0, None, lambda chunk: chunk_copy(ended, out_ref, out_sems, chunk).start())
    wait_chunks(ended, out_ref, out_sems)
    for copy in right_out + left_out:
        copy.wait()


def shape_of(shape, dtype):
    return jax.ShapeDtypeStruct(shape, dtype)


SMEM = pl.BlockSpec(memory_space=pltpu.SMEM)
INSIDE = pl.BlockSpec(memory_space=pltpu.VMEM)
OUTSIDE = pl.BlockSpec(memory_space=pl.ANY)


def run_forward(table, gain, sums, residual, weights, layer):
    first = residual.dtype == jnp.bfloat16
    whole = residual.shape
    sources = (*weights, residual)
    held = (PARTS * weights[0].shape[0],) + weights[0].shape[2:]
    out_shape = (
        shape_of(whole, jnp.float32),
        shape_of(whole, jnp.bfloat16),
        shape_of(whole, jnp.bfloat16),
        shape_of(whole, jnp.bfloat16),
        shape_of((8, whole[1]), jnp.float32),
        shape_of((8, whole[1]), jnp.float32),
    )
    return pl.pallas_call(
        lambda *refs: forward_kernel(first, layer, len(sources), *refs),
        in_specs=[SMEM, INSIDE, INSIDE] + [OUTSIDE] * len(sources),
        out_specs=[OUTSIDE] * 4 + [INSIDE] * 2,
        out_shape=out_shape,
        scratch_shapes=[
            pltpu.VMEM(whole if first else SMALL, jnp.bfloat16),
            pltpu.VMEM(whole, jnp.float32),
            pltpu.VMEM(held, jnp.bfloat16),
            pltpu.VMEM(whole, jnp.bfloat16),
            pltpu.VMEM(whole, jnp.bfloat16),
            pltpu.VMEM(whole, jnp.bfloat16),
            pltpu.VMEM(whole, jnp.float32),
            pltpu.SemaphoreType.DMA((CHUNKS,)),
            pltpu.SemaphoreType.DMA((2, PARTS)),
            pltpu.SemaphoreType.DMA((4, CHUNKS)),
        ],
        compiler_params=pltpu.CompilerParams(vmem_limit_bytes=VMEM_LIMIT),
        cost_estimate=pl.CostEstimate(
            flops=FORWARD_COST, bytes_accessed=20 * whole[0] * whole[1], transcendentals=0
        ),
        name="forward_layer",
    )(table, sums, gain, *sources)


def run_backward(table, gain, end_gain, scale, kept, weights, layer, sources, turning, last):
    whole = kept[0].shape
    sources = (*kept, *weights, *sources)
    held = (PARTS * weights[0].shape[0],) + weights[0].shape[2:]
    half = (held[0] // 2,) + held[1:]
    out_shape = [shape_of(whole, jnp.bfloat16 if last else jnp.float32)] + [shape_of(half, jnp.bfloat16)] * 2
    return pl.pallas_call(
        lambda *refs: backward_kernel(turning, last, layer, len(sources), *refs),
        in_specs=[SMEM, INSIDE, INSIDE] + [OUTSIDE] * (1 + len(sources)),
        out_specs=[OUTSIDE] * len(out_shape),
        out_shape=out_shape,
        scratch_shapes=[
            pltpu.VMEM(whole, jnp.float32),
            pltpu.VMEM(whole, jnp.bfloat16),
            pltpu.VMEM(whole, jnp.bfloat16),
            pltpu.VMEM(whole, jnp.bfloat16),
            pltpu.VMEM(whole, jnp.bfloat16 if last else jnp.float32),
            pltpu.VMEM(held, jnp.bfloat16),
            pltpu.VMEM(held, jnp.bfloat16),
            pltpu.VMEM(whole, jnp.float32),
            pltpu.VMEM(whole if turning else SMALL, jnp.float32),
            pltpu.VMEM(whole if turning else SMALL, jnp.bfloat16),
            pltpu.VMEM(whole if turning else SMALL, jnp.bfloat16),
            pltpu.SemaphoreType.DMA((7, CHUNKS)),
            pltpu.SemaphoreType.DMA((2, PARTS)),
            pltpu.SemaphoreType.DMA((CHUNKS,)),
            pltpu.SemaphoreType.DMA((2, PARTS)),
        ],
        compiler_params=pltpu.CompilerParams(vmem_limit_bytes=VMEM_LIMIT),
        cost_estimate=pl.CostEstimate(
            flops=BACKWARD_COST, bytes_accessed=30 * whole[0] * whole[1], transcendentals=0
        ),
        name="backward_layer",
    )(table, scale, gain, end_gain, *sources)


def join_kernel(rows, *refs):
    sources, whole, sems = refs[:-2], refs[-2], refs[-1]
    copies = [
        pltpu.make_async_copy(source.at[pl.ds(0, rows)], whole.at[pl.ds(at * rows, rows)], sems.at[at])
        for at, source in enumerate(sources)
    ]
    for copy in copies:
        copy.start()
    for copy in copies:
        copy.wait()


def joined(parts, rows=None):
    rows = parts[0].shape[0] if rows is None else rows
    whole = shape_of((rows * len(parts),) + parts[0].shape[1:], parts[0].dtype)
    return pl.pallas_call(
        lambda *refs: join_kernel(rows, *refs),
        in_specs=[OUTSIDE] * len(parts),
        out_specs=INSIDE,
        out_shape=whole,
        scratch_shapes=[pltpu.SemaphoreType.DMA((len(parts),))],
        compiler_params=pltpu.CompilerParams(vmem_limit_bytes=VMEM_LIMIT),
        cost_estimate=pl.CostEstimate(
            flops=0, bytes_accessed=4 * math.prod(whole.shape), transcendentals=0
        ),
        name="join",
    )(*parts)


def sum_kernel(terms, inputs, *refs):
    sources, outs = refs[:inputs], refs[inputs:]
    for group in range(inputs // terms):
        mine = sources[group * terms : (group + 1) * terms]
        for at in range(mine[0].shape[0]):
            total = sum(ref[at].astype(jnp.float32) for ref in mine).astype(jnp.bfloat16)
            if len(outs) > 1:
                outs[at][group] = total
            else:
                outs[0][at, group] = total


def run_sum(groups, parts, apart=True):
    flat = [term.reshape(parts, -1, term.shape[-1]) for terms in groups for term in terms]
    _, rows, lanes = flat[0].shape
    steps = 2
    if apart:
        out_shape = [shape_of((len(groups), rows, lanes), jnp.bfloat16)] * parts
        out_specs = [pl.BlockSpec((len(groups), rows // steps, lanes), lambda i: (0, i, 0))] * parts
    else:
        out_shape = [shape_of((parts, len(groups), rows, lanes), jnp.bfloat16)]
        out_specs = [pl.BlockSpec((parts, len(groups), rows // steps, lanes), lambda i: (0, 0, i, 0))]
    sums = pl.pallas_call(
        lambda *refs: sum_kernel(len(groups[0]), len(flat), *refs),
        grid=(steps,),
        in_specs=[pl.BlockSpec((parts, rows // steps, lanes), lambda i: (0, i, 0))] * len(flat),
        out_specs=out_specs,
        out_shape=out_shape,
        compiler_params=pltpu.CompilerParams(vmem_limit_bytes=VMEM_LIMIT),
        cost_estimate=pl.CostEstimate(
            flops=flat[0].size * len(flat), bytes_accessed=2 * flat[0].size * (len(flat) + 1), transcendentals=0
        ),
        name="sum",
    )(*flat)
    return [out.reshape(-1, lanes) for out in sums] if apart else sums[0].reshape(parts, -1, lanes)


def pieces_kernel(chunk, place_ref, order_ref, left_ref, right_ref, gain_ref, out_ref, held, left_sem, sems):
    layer_count, half, size = held.shape[:3]
    first = place_ref[2] * half
    lefts = pltpu.make_async_copy(left_ref.at[:, pl.ds(first, half)], held, left_sem.at[0])
    lefts.start()
    copies = []
    turns = []
    for section in range(out_ref.shape[0]):
        row = 0
        for layer in range(layer_count):
            for inside in range(chunk):
                turns.append((layer, section * chunk + inside, section, row))
                row += size
            for inside in range(chunk):
                source = right_ref.at[layer, first + section * chunk + inside]
                copies.append((source, out_ref.at[section, pl.ds(row, size)]))
                row += size
        copies.append((gain_ref, out_ref.at[section, pl.ds(row, gain_ref.shape[0])]))
    copies = [
        pltpu.make_async_copy(source, target, sems.at[at]) for at, (source, target) in enumerate(copies)
    ]
    for copy in copies:
        copy.start()
    lefts.wait()
    for layer, block, section, row in turns:
        turned = inner_dot(held[layer, block], order_ref[...], 1, 0)
        out_ref[section, pl.ds(row, size), :] = turned.astype(jnp.bfloat16)
    for copy in copies:
        copy.wait()


def factor_pieces(place, order, left, right, gain_rows, chunk, width):
    layer_count, blocks, size = left.shape[:3]
    rows = layer_count * 2 * chunk * size + gain_rows.shape[0]
    return pl.pallas_call(
        lambda *refs: pieces_kernel(chunk, *refs),
        in_specs=[SMEM, INSIDE] + [OUTSIDE] * 3,
        out_specs=INSIDE,
        out_shape=shape_of((width, rows, size), jnp.bfloat16),
        scratch_shapes=[
            pltpu.VMEM((layer_count, blocks // 2, size, size), jnp.bfloat16),
            pltpu.SemaphoreType.DMA((1,)),
            pltpu.SemaphoreType.DMA((width * (layer_count * chunk + 1),)),
        ],
        compiler_params=pltpu.CompilerParams(vmem_limit_bytes=VMEM_LIMIT),
        cost_estimate=pl.CostEstimate(flops=left.size * size, bytes_accessed=4 * left.size, transcendentals=0),
        name="pieces",
    )(place, order, left, right, gain_rows)


def choice(pairs, critic, slots):
    rows = pairs.shape[0]
    named = (pairs[:, 0:1] == critic) | (pairs[:, 1:2] == critic)
    named = jnp.broadcast_to(named.astype(jnp.float32), (rows, slots))
    before = lax.broadcasted_iota(jnp.int32, (rows, rows), 1) < lax.broadcasted_iota(jnp.int32, (rows, rows), 0)
    rank = inner_dot(before.astype(jnp.bfloat16), named.astype(jnp.bfloat16), 1, 0)
    at = lax.broadcasted_iota(jnp.int32, (rows, slots), 1).astype(jnp.float32)
    return jnp.where(rank == at, named, 0.0).astype(jnp.bfloat16)


def pick_kernel(pairs_ref, values_ref, out_ref):
    width, features, slots = out_ref.shape
    pairs = pairs_ref[...]
    chosen = [choice(pairs, critic, slots) for critic in range(width)]
    step = 512
    for start in range(0, features, step):
        part = values_ref[:, pl.ds(start, step)]
        for k in range(width):
            out_ref[k, pl.ds(start, step), :] = inner_dot(part, chosen[k], 0, 0).astype(jnp.bfloat16)


def run_pick(pairs, values, width, slots):
    rows, features = values.shape
    return pl.pallas_call(
        pick_kernel,
        in_specs=[INSIDE] * 2,
        out_specs=INSIDE,
        out_shape=shape_of((width, features, slots), jnp.bfloat16),
        compiler_params=pltpu.CompilerParams(vmem_limit_bytes=VMEM_LIMIT),
        cost_estimate=pl.CostEstimate(
            flops=2 * rows * features * slots * width, bytes_accessed=8 * rows * features, transcendentals=0
        ),
        name="pick",
    )(pairs, values)


def combine_kernel(pairs_ref, came_ref, out_ref):
    width, features, slots = came_ref.shape
    pairs = pairs_ref[...]
    chosen = [choice(pairs, critic, slots) for critic in range(width)]
    step = 512
    for start in range(0, features, step):
        total = sum(inner_dot(chosen[k], came_ref[k, pl.ds(start, step), :], 1, 1) for k in range(width))
        out_ref[:, pl.ds(start, step)] = (0.5 * total).astype(jnp.bfloat16)


def run_combine(pairs, came):
    rows = pairs.shape[0]
    return pl.pallas_call(
        combine_kernel,
        in_specs=[INSIDE] * 2,
        out_specs=INSIDE,
        out_shape=shape_of((rows, came.shape[1]), jnp.bfloat16),
        compiler_params=pltpu.CompilerParams(vmem_limit_bytes=VMEM_LIMIT),
        cost_estimate=pl.CostEstimate(
            flops=2 * rows * came.size, bytes_accessed=4 * came.size, transcendentals=0
        ),
        name="combine",
    )(pairs, came)


FORWARD_COST = 15_000_000_000
BACKWARD_COST = 18_000_000_000


def assemble_kernel(layers, factor, place_ref, order_ref, *refs):
    count = 2 * len(layers)
    sources, (left_ref, right_ref) = refs[:count], refs[count : count + 2]
    held, wide = refs[count + 2 : 2 * count + 2], refs[2 * count + 2 : 3 * count + 2]
    in_sems, out_sems = refs[3 * count + 2 :]
    origin, core = place_ref[0] ^ place_ref[1], place_ref[2]
    order = order_ref[...]
    arrivals = [
        pltpu.make_async_copy(source, held[at], in_sems.at[at]) for at, source in enumerate(sources)
    ]
    for copy in arrivals:
        copy.start()
    leaving = []
    for at in range(count):
        arrivals[at].wait()
        half = core if at % 2 == 0 else 1 - core
        width, _, _, chunk = held[at].shape[:4]
        for k in range(width):
            start = (half * width + (origin ^ k if at < 2 else k)) * chunk
            for inside, layer in enumerate(layers[at // 2]):
                for block in range(chunk):
                    left = inner_dot(held[at][k, inside, 0, block], order, 1, 1)
                    wide[at][k, inside, 0, block] = left * factor
                wide[at][k, inside, 1] = held[at][k, inside, 1].astype(jnp.float32) * factor
                for which, target in enumerate((left_ref, right_ref)):
                    copy = pltpu.make_async_copy(
                        wide[at].at[k, inside, which],
                        target.at[layer, pl.ds(start, chunk)],
                        out_sems.at[len(leaving)],
                    )
                    copy.start()
                    leaving.append(copy)
    for copy in leaving:
        copy.wait()


def run_assemble(place, order, pieces, layers, factor):
    piece = pieces[0].shape
    layer_count = sum(len(group) for group in layers)
    out = shape_of((layer_count, 2 * piece[0] * piece[3]) + piece[4:], jnp.float32)
    return pl.pallas_call(
        lambda *refs: assemble_kernel(layers, factor, *refs),
        in_specs=[SMEM, INSIDE] + [OUTSIDE] * len(pieces),
        out_specs=[OUTSIDE] * 2,
        out_shape=[out] * 2,
        scratch_shapes=[pltpu.VMEM(part.shape, jnp.bfloat16) for part in pieces]
        + [pltpu.VMEM(part.shape, jnp.float32) for part in pieces]
        + [
            pltpu.SemaphoreType.DMA((len(pieces),)),
            pltpu.SemaphoreType.DMA((4 * layer_count * piece[0],)),
        ],
        compiler_params=pltpu.CompilerParams(vmem_limit_bytes=VMEM_LIMIT),
        cost_estimate=pl.CostEstimate(flops=0, bytes_accessed=4 * math.prod(out.shape) * 3, transcendentals=0),
        name="assemble",
    )(place, order, *pieces)


def plane_routes(width, replicas):
    bits = width.bit_length() - 1
    orders = [[(step + d) % bits for step in range(bits)] for d in range(replicas)]
    every = [(s, t, d) for s in range(width) for t in range(width) for d in range(replicas)]

    def route(move):
        def index(s, t, d):
            return (s * width + t) * replicas + d

        return [(index(*place), index(*move(*place))) for place in every]

    ranks = [[0] * width for _ in range(replicas)]
    for d in range(replicas):
        for r in range(width):
            ranks[d][sum(((r >> at) & 1) << orders[d][at] for at in range(bits))] = r
    return {
        "across": [route(lambda s, t, d, at=at: (s ^ (1 << orders[d][at]), t, d)) for at in range(bits)],
        "cores": route(lambda s, t, d: (s, t, 1 - d)),
        "sections": [route(lambda s, t, d, k=k: (s ^ k, t, d)) for k in range(width)],
        "homes": [route(lambda s, t, d, j=j: (t, t ^ s ^ j, d)) for j in range(width)],
    }, ranks


def plane_shards(patches, teacher, critic_pairs, left_factors, right_factors, norm_gains):
    width = lax.axis_size("section")
    replicas = lax.axis_size("dp")
    tok_rows, feat_local = patches.shape
    layer_count, local_blocks, size = left_factors.shape[1:4]
    blocks = feat_local * width // size
    wide = 2 * tok_rows // 3
    chunk = local_blocks // (replicas * width)
    layer_rows = 2 * chunk * size
    routes, ranks = plane_routes(width, replicas)
    section = lax.axis_index("section")
    tensor = lax.axis_index("tensor")
    core = lax.axis_index("dp")
    place = jnp.stack([section, tensor, core]).astype(jnp.int32)
    tie = lax.optimization_barrier

    def move(value, route):
        return lax.ppermute(value, AXES, route)

    def move_all(values, name):
        return [move(value, route) for value, route in zip(values, routes[name])]

    def send(values, name):
        return [values[0]] + [move(values[k], routes[name][k]) for k in range(1, width)]

    def gather_one(mine):
        return joined([mine, move(mine, routes["across"][0])])

    def gather_two(pair):
        return pair, move(pair, routes["across"][1]), move(pair, routes["cores"])

    def gather_three(pair, other, peer):
        return [pair, other, peer, move(other, routes["cores"])]

    def as_weights(parts):
        return [part.reshape(2 * width, -1, 2, chunk, size, size) for part in parts]

    block = jnp.arange(blocks, dtype=jnp.int32)
    inside = block % local_blocks
    replica = inside // (width * chunk)
    part = (replica != core).astype(jnp.int32)
    distance = section ^ ((inside // chunk) % width)
    quarter = block // local_blocks
    rank = jnp.array(ranks, jnp.int32)[replica, distance]
    table = jnp.stack(
        [
            ((part * width + index) * width + piece) * chunk + inside % chunk
            for index, piece in (
                (rank, quarter),
                (distance, quarter),
                (distance, tensor ^ section ^ distance ^ quarter),
            )
        ]
    ).astype(jnp.int32)

    def to_planes(value):
        return lax.all_to_all(value, "tensor", split_axis=0, concat_axis=0, tiled=True)

    def to_sections(value):
        return lax.all_to_all(value, "section", split_axis=0, concat_axis=0, tiled=True)

    half_layers = layer_count // 2
    groups = [tuple(range(half_layers)), tuple(range(half_layers, layer_count))]
    fold = size // blocks
    columns = jnp.arange(size)
    order = (columns[:, None] == (columns % blocks) * fold + columns // blocks).astype(jnp.bfloat16)
    gain_rows = norm_gains[0].reshape(-1, size)
    pieces = factor_pieces(place, order, left_factors[0], right_factors[0], gain_rows, chunk, width)
    pieces, patches, teacher = tie((pieces, patches, teacher))
    spread = to_sections(pieces)
    patch_sent = run_pick(critic_pairs, patches, width, wide)
    target_sent = run_pick(critic_pairs, teacher, width, wide)
    spread, patch_sent, target_sent = tie((spread, patch_sent, target_sent))
    lifted = to_planes(spread)
    lifted, patch_sent = tie((lifted, patch_sent))
    patch_came = to_planes(patch_sent).reshape(-1, wide)
    lowest = [lifted[:, group[0] * layer_rows : (group[-1] + 1) * layer_rows] for group in groups]
    beside = move(lowest[0], routes["across"][0])
    gains = lifted[:, layer_count * layer_rows :].reshape(width, layer_count + 1, local_blocks, size)
    gains = gains.transpose(1, 3, 0, 2).reshape(layer_count + 1, size, blocks)
    end_column = jnp.broadcast_to(gains[layer_count].T[:, :, None], (blocks, size, wide)).reshape(-1, wide)
    lowest, beside = tie((lowest, beside))
    first_two = gather_two(joined([lowest[0], beside]))
    later = (lowest[1], move(lowest[1], routes["across"][0]))
    first_two, later, patch_came = tie((first_two, later, patch_came))
    weights = [as_weights(gather_three(*first_two))]
    weights, later, end_column = tie((weights, later, end_column))

    residual, target_sent = tie((patch_came, target_sent))
    target = to_planes(target_sent).reshape(-1, wide)
    flying = gather_two(joined(list(later)))
    sums = jnp.zeros((8, wide), jnp.float32)
    stored = []
    for layer in range(layer_count):
        group = 0 if layer in groups[0] else 1
        following, u, z, slope, scale, sums = run_forward(
            table, gains[layer], sums, residual, weights[group], layer - groups[group][0]
        )
        stored.append(((slope, z, u), scale, residual))
        residual = following
        if layer == 0:
            residual, sums, flying = tie((residual, sums, flying))
            weights.append(as_weights(gather_three(*flying)))
        if layer == groups[0][-1]:
            residual, sums, weights[1], target = tie((residual, sums, weights[1], target))

    def core_sum(mine, other):
        return (mine, move(other, routes["cores"]))

    def plane_sum(mine, other):
        return send(run_sum([(mine, other)], width), "sections")

    def homeward(parts):
        return move_all(run_sum(parts, width), "homes")

    def both_halves(whole):
        pair = (whole, move(whole, routes["cores"]))
        return [part.reshape(width, -1, 2, chunk, size, size) for part in pair]

    steps = (core_sum, plane_sum)
    gradient = residual
    underway = []
    for layer in range(layer_count - 1, -1, -1):
        turning = layer == layer_count - 1
        last = layer == 0
        kept, scale, inputs = stored[layer]
        group = 0 if layer in groups[0] else 1
        sources = (gradient, inputs, target) if turning else (gradient, inputs)
        underway = [(at + 1, steps[at](*state)) if at < len(steps) else (at, state) for at, state in underway]
        gradient, mine, other = run_backward(
            table,
            gains[layer],
            end_column,
            scale,
            kept,
            weights[group],
            layer - groups[group][0],
            sources,
            turning,
            last,
        )
        gradient, mine, other, states = tie((gradient, mine, other, [state for _, state in underway]))
        underway = [(at, state) for (at, _), state in zip(underway, states)]
        underway.append((0, (mine, other)))

    returned = to_planes(gradient.reshape(width, feat_local, wide))
    ended = [steps[at](*state) if at < len(steps) else state for at, state in underway][::-1]
    ended = tie(ended)
    ended[0] = plane_sum(*ended[0])
    others = to_planes(run_sum(ended[1:], width, apart=False))
    ended[0], returned, others = tie((ended[0], returned, others))
    home = homeward(ended[:1])
    d_patches = run_combine(critic_pairs, returned)
    others = to_sections(others)
    d_patches, home, others = tie((d_patches, home, others))
    homes_of = both_halves(joined(home)) + both_halves(others)
    grad_factor = 1.0 / math.sqrt(2 * tok_rows * width * replicas)
    grad_left, grad_right = run_assemble(
        place, order, homes_of, [(0,), tuple(range(1, layer_count))], grad_factor
    )
    return (d_patches, grad_left[None], grad_right[None])


def solution(mesh):
    in_specs = (
        P(("section", "dp"), "tensor"),
        P(("section", "dp"), "tensor"),
        P(("section", "dp"), None),
        P("section", None, "tensor", None, None),
        P("section", None, "tensor", None, None),
        P("section", None, "tensor"),
    )
    out_specs = (
        P(("section", "dp"), "tensor"),
        P("section", None, "tensor", None, None),
        P("section", None, "tensor", None, None),
    )
    body = plane_shards if planes_fit(mesh) else layered_shards
    return jax.shard_map(
        body, mesh=mesh, in_specs=in_specs, out_specs=out_specs, check_vma=False)
```

```python
import math

import jax
import jax.numpy as jnp
from jax import lax
from jax.experimental import pallas as pl
from jax.experimental.pallas import tpu as pltpu
from jax.sharding import PartitionSpec as P

EPSILON = 1e-06
TANH_SLOPE = 0.7978845608028654
CUBIC_TERM = 0.044715


def shifted(value, axis, steps):
    count = lax.axis_size(axis)
    first, last = (max(0, -steps), min(count, count - steps))
    return lax.ppermute(value, axis, [(source, source + steps) for source in range(first, last)])


def gelu_value(values):
    tangent = jnp.tanh(TANH_SLOPE * (values + CUBIC_TERM * values * values * values))
    return 0.5 * values * (1.0 + tangent)


def gelu_slope(values):
    tangent = jnp.tanh(TANH_SLOPE * (values + CUBIC_TERM * values * values * values))
    return 0.5 * (1.0 + tangent) + 0.5 * values * (1.0 - tangent * tangent) * TANH_SLOPE * (
        1.0 + 3.0 * CUBIC_TERM * values * values
    )


def norm_pair(residuals, gain_pair, model_width):
    squares = lax.psum(
        (
            jnp.sum(residuals[0] * residuals[0], axis=(1, 2)),
            jnp.sum(residuals[1] * residuals[1], axis=(1, 2)),
        ),
        "tensor",
    )
    factors = [lax.rsqrt(squares[member] / model_width + EPSILON) for member in range(2)]
    normed = [
        residuals[member] * factors[member][:, None, None] * gain_pair[member][None]
        for member in range(2)
    ]
    return (factors, normed)


def norm_back_pair(residuals, factors, gain_pair, grad_normed, carried, model_width):
    weighted = [grad_normed[member] * gain_pair[member][None] for member in range(2)]
    inners = lax.psum(
        (
            jnp.sum(weighted[0] * residuals[0], axis=(1, 2)),
            jnp.sum(weighted[1] * residuals[1], axis=(1, 2)),
        ),
        "tensor",
    )
    return [
        carried[member]
        + factors[member][:, None, None] * weighted[member]
        - residuals[member] * (factors[member] ** 3 * inners[member] / model_width)[:, None, None]
        for member in range(2)
    ]


def layered_shards(patches, teacher, critic_pairs, left_factors, right_factors, norm_gains):
    sections = lax.axis_size("section")
    tensor_width = lax.axis_size("tensor")
    replicas = lax.axis_size("dp")
    tok_rows = patches.shape[0]
    feat_local = patches.shape[1]
    layer_count = left_factors.shape[1]
    local_blocks = left_factors.shape[2]
    block_size = left_factors.shape[3]
    all_blocks = local_blocks * tensor_width
    fold_ratio = block_size // all_blocks
    model_width = feat_local * tensor_width
    sixth_rows = tok_rows // 6
    leading = 2 * sixth_rows
    critic_ids = jnp.arange(4, dtype=jnp.int32)
    named_by = (
        (critic_pairs[:, 0:1] == critic_ids[None, :])
        | (critic_pairs[:, 1:2] == critic_ids[None, :])
    ).astype(jnp.int32)
    ranking = jnp.cumsum(named_by, axis=0) - 1
    wide_ids = critic_ids[None, :] < 2
    slot_width = 3 * sixth_rows
    spilled = wide_ids & (ranking >= 3 * sixth_rows)
    destination = jnp.where(spilled, critic_ids[None, :] + 2, critic_ids[None, :])
    slot_index = jnp.where(spilled, ranking - sixth_rows, ranking)
    flat_slot = destination * slot_width + slot_index
    chosen = jnp.take_along_axis(flat_slot, critic_pairs, axis=1)
    slot_total = sections * slot_width
    row_ids = jnp.broadcast_to(jnp.arange(tok_rows, dtype=jnp.int32)[:, None], chosen.shape)
    source_row = (
        jnp.full((slot_total,), tok_rows, jnp.int32).at[chosen.reshape(-1)].set(row_ids.reshape(-1))
    )
    send_patch = (
        patches.at[source_row]
        .get(mode="fill", fill_value=0)
        .reshape(sections, slot_width, local_blocks, block_size)
    )
    send_target = (
        teacher.at[source_row]
        .get(mode="fill", fill_value=0)
        .reshape(sections, slot_width, local_blocks, block_size)
    )
    recv_patch, recv_target = (
        lax.all_to_all(send_patch, "section", split_axis=0, concat_axis=0, tiled=True),
        lax.all_to_all(send_target, "section", split_axis=0, concat_axis=0, tiled=True),
    )
    residuals = [
        recv_patch[:, :leading].reshape(-1, local_blocks, block_size).astype(jnp.float32),
        recv_patch[:, leading:].reshape(-1, local_blocks, block_size).astype(jnp.float32),
    ]
    targets = [
        recv_target[:, :leading].reshape(-1, local_blocks, block_size).astype(jnp.float32),
        recv_target[:, leading:].reshape(-1, local_blocks, block_size).astype(jnp.float32),
    ]
    native = (left_factors[0], right_factors[0], norm_gains[0])
    borrowed = shifted((left_factors, right_factors, norm_gains), "section", 2)
    is_wide = lax.axis_index("section") < 2
    second = (
        jnp.where(is_wide, left_factors, borrowed[0])[0],
        jnp.where(is_wide, right_factors, borrowed[1])[0],
        jnp.where(is_wide, norm_gains, borrowed[2])[0],
    )
    left_sets = (native[0], second[0])
    right_sets = (native[1], second[1])
    gain_sets = (
        native[2].astype(jnp.float32).reshape(layer_count + 1, local_blocks, block_size),
        second[2].astype(jnp.float32).reshape(layer_count + 1, local_blocks, block_size),
    )
    stored = []
    for layer_index in range(layer_count):
        gain_pair = [gain_sets[0][layer_index], gain_sets[1][layer_index]]
        factors, normed = norm_pair(residuals, gain_pair, model_width)
        normed = [normed[member].astype(jnp.bfloat16) for member in range(2)]
        first_out = [
            jnp.einsum(
                "nki,kij->nkj",
                normed[member],
                left_sets[member][layer_index],
                preferred_element_type=jnp.float32,
            ).astype(jnp.bfloat16)
            for member in range(2)
        ]
        permuted = (
            lax.all_to_all(first_out[0], "tensor", split_axis=2, concat_axis=1, tiled=True),
            lax.all_to_all(first_out[1], "tensor", split_axis=2, concat_axis=1, tiled=True),
        )
        permuted = [
            permuted[member].reshape(
                permuted[member].shape[0], all_blocks, local_blocks, fold_ratio
            )
            for member in range(2)
        ]
        right_quads = [
            right_sets[member][layer_index].reshape(
                local_blocks, fold_ratio, all_blocks, block_size
            )
            for member in range(2)
        ]
        mixture = [
            jnp.einsum(
                "nkmp,mpkl->nml",
                permuted[member],
                right_quads[member],
                preferred_element_type=jnp.float32,
            )
            for member in range(2)
        ]
        stored.append((residuals, factors, normed, permuted, mixture, right_quads, gain_pair))
        residuals = [residuals[member] + gelu_value(mixture[member]) for member in range(2)]
    final_gains = [gain_sets[0][layer_count], gain_sets[1][layer_count]]
    factors, outputs = norm_pair(residuals, final_gains, model_width)
    gradients = norm_back_pair(
        residuals,
        factors,
        final_gains,
        [outputs[member] - targets[member] for member in range(2)],
        [jnp.zeros_like(residuals[member]) for member in range(2)],
        model_width,
    )
    left_terms = []
    right_terms = []
    for layer_index in range(layer_count - 1, -1, -1):
        inputs, factors, normed, permuted, mixture, right_quads, gain_pair = stored[layer_index]
        slopes = [
            (gradients[member] * gelu_slope(mixture[member])).astype(jnp.bfloat16)
            for member in range(2)
        ]
        right_grad = [
            jnp.einsum(
                "nkmp,nml->mpkl",
                permuted[member],
                slopes[member],
                preferred_element_type=jnp.float32,
            ).reshape(local_blocks, block_size, block_size)
            for member in range(2)
        ]
        back_moved = [
            jnp.einsum(
                "nml,mpkl->nkmp",
                slopes[member],
                right_quads[member],
                preferred_element_type=jnp.float32,
            )
            .astype(jnp.bfloat16)
            .reshape(slopes[member].shape[0], all_blocks, local_blocks * fold_ratio)
            for member in range(2)
        ]
        arrived = (
            lax.all_to_all(back_moved[0], "tensor", split_axis=1, concat_axis=2, tiled=True),
            lax.all_to_all(back_moved[1], "tensor", split_axis=1, concat_axis=2, tiled=True),
        )
        left_grad = [
            jnp.einsum(
                "nki,nkj->kij", normed[member], arrived[member], preferred_element_type=jnp.float32
            )
            for member in range(2)
        ]
        grad_normed = [
            jnp.einsum(
                "nkj,kij->nki",
                arrived[member],
                left_sets[member][layer_index],
                preferred_element_type=jnp.float32,
            )
            for member in range(2)
        ]
        gradients = norm_back_pair(inputs, factors, gain_pair, grad_normed, gradients, model_width)
        layer_left = jnp.stack(left_grad)
        layer_right = jnp.stack(right_grad)
        layer_left, layer_right = (
            lax.psum(layer_left.astype(jnp.bfloat16), "dp").astype(jnp.float32),
            lax.psum(layer_right.astype(jnp.bfloat16), "dp").astype(jnp.float32),
        )
        left_terms.insert(0, layer_left)
        right_terms.insert(0, layer_right)
    left_stack = jnp.stack(left_terms)
    right_stack = jnp.stack(right_terms)
    repaid = (
        shifted(left_stack[:, 1].astype(jnp.bfloat16), "section", -2).astype(jnp.float32),
        shifted(right_stack[:, 1].astype(jnp.bfloat16), "section", -2).astype(jnp.float32),
    )
    is_wide = lax.axis_index("section") < 2
    left_total = left_stack[:, 0] + jnp.where(is_wide, left_stack[:, 1] + repaid[0], 0.0)
    right_total = right_stack[:, 0] + jnp.where(is_wide, right_stack[:, 1] + repaid[1], 0.0)
    grad_factor = 1.0 / math.sqrt(2 * tok_rows * sections * replicas)
    returned = [
        gradients[member].astype(jnp.bfloat16).reshape(sections, -1, local_blocks, block_size)
        for member in range(2)
    ]
    back_lead, back_trail = (
        lax.all_to_all(returned[0], "section", split_axis=0, concat_axis=0, tiled=True),
        lax.all_to_all(returned[1], "section", split_axis=0, concat_axis=0, tiled=True),
    )
    gathered = jnp.concatenate((back_lead, back_trail), axis=1).reshape(
        slot_total, local_blocks, block_size
    )
    combined = (
        gathered[chosen[:, 0]].astype(jnp.float32) + gathered[chosen[:, 1]].astype(jnp.float32)
    ) * 0.5
    d_patches = combined.astype(jnp.bfloat16).reshape(tok_rows, feat_local)
    return (d_patches, (left_total * grad_factor)[None], (right_total * grad_factor)[None])


VMEM_LIMIT = 60 * 1024 * 1024
CHUNKS = 8
TOGETHER = 4
PARTS = 4
SMALL = (16, 128)
AXES = ("section", "tensor", "dp")


def planes_fit(mesh):
    sections = mesh.shape["section"]
    paired = mesh.shape["dp"] == 2 and sections & (sections - 1) == 0
    return paired and mesh.shape["tensor"] == sections


def inner_dot(left, right, left_dim, right_dim):
    return lax.dot_general(
        left,
        right,
        (((left_dim,), (right_dim,)), ((), ())),
        preferred_element_type=jnp.float32,
    )


def fold_rows(values):
    return jnp.sum(values.reshape(values.shape[0] // 8, 8, values.shape[1]), axis=0)


def block_rows(block, size):
    return pl.ds(pl.multiple_of(block * size, size), size)


def column(gain_ref, block, slots):
    blocks = gain_ref.shape[1]
    picked = lax.broadcasted_iota(jnp.int32, (blocks, slots), 0) == block
    return inner_dot(gain_ref[...], picked.astype(jnp.bfloat16), 1, 0)


def chunk_copy(source, target, sems, chunk):
    rows = target.shape[0] // CHUNKS
    at = pl.ds(pl.multiple_of(chunk * rows, rows), rows)
    return pltpu.make_async_copy(source.at[at], target.at[at], sems.at[chunk])


def start_chunks(source, target, sems):
    for chunk in range(CHUNKS):
        chunk_copy(source, target, sems, chunk).start()


def wait_chunks(source, target, sems):
    for chunk in range(CHUNKS):
        chunk_copy(source, target, sems, chunk).wait()


def factor_copies(parts, layer, held, sems, side):
    count = parts[0].shape[0]
    return [
        pltpu.make_async_copy(
            ref.at[:, layer, side], held.at[pl.ds(at * count, count), side], sems.at[side, at]
        )
        for at, ref in enumerate(parts)
    ]


def gradient_copies(held, parts, sems, side):
    count = parts[0].shape[0]
    return [
        pltpu.make_async_copy(
            held.at[pl.ds(at * count, count), side], ref.at[:, side], sems.at[side, at]
        )
        for at, ref in enumerate(parts)
    ]


def by_chunk(blocks, step, carry, before=None, after=None):
    per_chunk = blocks // CHUNKS

    def few(start, carry):
        stores = []
        for at in range(TOGETHER):
            made, carry = step(start + at, carry)
            stores += made
        for ref, index, value in stores:
            ref[index] = value
        return carry

    def one(chunk, carry):
        if before is not None:
            before(chunk)
        for at in range(0, per_chunk, TOGETHER):
            carry = few(chunk * per_chunk + at, carry)
        if after is not None:
            after(chunk)
        return carry

    return lax.fori_loop(0, CHUNKS, one, carry)


def forward_kernel(first, layer, inputs, table_ref, sums_ref, gain_ref, *refs):
    sources, refs = refs[:inputs], refs[inputs:]
    parts, sources = sources[:PARTS], sources[PARTS:]
    out_ref, u_ref, z_ref, slope_ref, scale_ref, next_ref = refs[:6]
    raw, h, w, u, z, slope, mid, in_sems, w_sems, out_sems = refs[6:]
    features, slots = h.shape
    size = w.shape[-1]
    chunk_blocks = w.shape[2]
    blocks = features // size
    fold = size // blocks

    left_in = factor_copies(parts, layer, w, w_sems, 0)
    right_in = factor_copies(parts, layer, w, w_sems, 1)
    if first:
        start_chunks(sources[0], raw, in_sems)
        for copy in left_in + right_in:
            copy.start()

        def squares(block, total):
            rows = block_rows(block, size)
            part = raw[rows, :].astype(jnp.float32)
            return [(h, (rows, slice(None)), part)], total + fold_rows(part * part)

        total = by_chunk(
            blocks,
            squares,
            jnp.zeros((8, slots), jnp.float32),
            lambda chunk: chunk_copy(sources[0], raw, in_sems, chunk).wait(),
        )
    else:
        for copy in left_in:
            copy.start()
        start_chunks(sources[0], h, in_sems)
        for copy in right_in:
            copy.start()
        total = sums_ref[...]
    scale = lax.rsqrt(jnp.sum(total, axis=0, keepdims=True) / features + EPSILON)
    scale_ref[...] = jnp.broadcast_to(scale, scale_ref.shape)
    for copy in left_in:
        copy.wait()

    def arrive(chunk):
        if not first:
            chunk_copy(sources[0], h, in_sems, chunk).wait()

    def left(block, carry):
        rows = block_rows(block, size)
        place = table_ref[0, block]
        normed = (h[rows, :] * scale * column(gain_ref, block, slots)).astype(jnp.bfloat16)
        weight = w[place // chunk_blocks, 0, place % chunk_blocks]
        first_out = inner_dot(weight, normed, 0, 0)
        at = (rows, slice(None))
        return [(u, at, normed), (mid, at, first_out)], carry

    def leave_left(chunk):
        chunk_copy(u, u_ref, out_sems.at[0], chunk).start()

    by_chunk(blocks, left, 0, arrive, leave_left)
    for copy in right_in:
        copy.wait()

    def right(block, total):
        rows = block_rows(block, size)
        place = table_ref[0, block]
        moved = [mid[pl.ds(q * blocks + block, blocks, stride=size), :] for q in range(fold)]
        moved = jnp.concatenate(moved, axis=0).astype(jnp.bfloat16)
        weight = w[place // chunk_blocks, 1, place % chunk_blocks]
        mixture = inner_dot(weight, moved, 0, 0)
        squared = mixture * mixture
        tangent = jnp.tanh(mixture * (TANH_SLOPE + (TANH_SLOPE * CUBIC_TERM) * squared))
        half = 0.5 + 0.5 * tangent
        following = h[rows, :] + mixture * half
        steep = half + mixture * (1.0 - tangent * tangent) * (
            0.5 * TANH_SLOPE + (1.5 * TANH_SLOPE * CUBIC_TERM) * squared
        )
        at = (rows, slice(None))
        stores = [(z, at, moved), (h, at, following), (slope, at, steep.astype(jnp.bfloat16))]
        return stores, total + fold_rows(following * following)

    leaving = ((h, out_ref, 1), (z, z_ref, 2), (slope, slope_ref, 3))

    def leave_right(chunk):
        for source, target, at in leaving:
            chunk_copy(source, target, out_sems.at[at], chunk).start()

    next_ref[...] = by_chunk(blocks, right, jnp.zeros((8, slots), jnp.float32), None, leave_right)
    for source, target, at in ((u, u_ref, 0),) + leaving:
        wait_chunks(source, target, out_sems.at[at])


def backward_kernel(turning, last, layer, inputs, table_ref, scale_ref, gain_ref, end_gain_ref, *refs):
    sources, refs = refs[:inputs], refs[inputs:]
    slope_ref, z_ref, u_ref = sources[:3]
    parts, sources = sources[3 : 3 + PARTS], sources[3 + PARTS :]
    out_ref, own_grad, peer_grad = refs[:3]
    g, slope, z, u, h, w, gw, mid, top, goal, end_gain = refs[3:14]
    in_sems, w_sems, out_sems, gw_sems = refs[14:]
    features, slots = g.shape
    size = w.shape[-1]
    chunk_blocks = w.shape[2]
    blocks = features // size
    fold = size // blocks

    left_in = factor_copies(parts, layer, w, w_sems, 0)
    right_in = factor_copies(parts, layer, w, w_sems, 1)
    g_ref, h_ref = sources[:2]
    if turning:
        for chunk in range(CHUNKS):
            chunk_copy(g_ref, top, in_sems.at[0], chunk).start()
            chunk_copy(end_gain_ref, end_gain, in_sems.at[6], chunk).start()
            chunk_copy(sources[2], goal, in_sems.at[5], chunk).start()
    for copy in right_in:
        copy.start()
    for chunk in range(CHUNKS):
        if not turning:
            chunk_copy(g_ref, g, in_sems.at[0], chunk).start()
        chunk_copy(slope_ref, slope, in_sems.at[1], chunk).start()
        chunk_copy(z_ref, z, in_sems.at[2], chunk).start()
    for copy in left_in:
        copy.start()
    for chunk in range(CHUNKS):
        chunk_copy(u_ref, u, in_sems.at[3], chunk).start()
        chunk_copy(h_ref, h, in_sems.at[4], chunk).start()

    if turning:
        zero = jnp.zeros((8, slots), jnp.float32)

        def sums(block, totals):
            rows = block_rows(block, size)
            part = top[rows, :]
            scaled = part * end_gain[rows, :].astype(jnp.float32)
            return [], (
                totals[0] + fold_rows(part * part),
                totals[1] + fold_rows(scaled * scaled),
                totals[2] + fold_rows(scaled * goal[rows, :].astype(jnp.float32)),
            )

        def arrive_top(chunk):
            chunk_copy(g_ref, top, in_sems.at[0], chunk).wait()
            chunk_copy(end_gain_ref, end_gain, in_sems.at[6], chunk).wait()
            chunk_copy(sources[2], goal, in_sems.at[5], chunk).wait()

        totals = by_chunk(blocks, sums, (zero, zero, zero), arrive_top)
        squares, gained, crossed = [jnp.sum(total, axis=0, keepdims=True) for total in totals]
        end_scale = lax.rsqrt(squares / features + EPSILON)
        end_back = end_scale * end_scale * end_scale * (end_scale * gained - crossed) / features

    for copy in right_in:
        copy.wait()

    def arrive_right(chunk):
        if not turning:
            chunk_copy(g_ref, g, in_sems.at[0], chunk).wait()
        chunk_copy(slope_ref, slope, in_sems.at[1], chunk).wait()
        chunk_copy(z_ref, z, in_sems.at[2], chunk).wait()

    def right(block, total):
        rows = block_rows(block, size)
        place, home = table_ref[0, block], table_ref[2 if last else 1, block]
        at = (place // chunk_blocks, 1, place % chunk_blocks)
        to = (home // chunk_blocks, 1, home % chunk_blocks)
        if turning:
            part = top[rows, :]
            factor = end_gain[rows, :].astype(jnp.float32)
            error = (part * end_scale * factor - goal[rows, :].astype(jnp.float32)) * factor
            gradient = end_scale * error - part * end_back
            stores = [(g, (rows, slice(None)), gradient)]
        else:
            gradient = g[rows, :]
            stores = []
        steep = (gradient * slope[rows, :].astype(jnp.float32)).astype(jnp.bfloat16)
        taken = z[rows, :]
        back = inner_dot(w[at], steep, 1, 0)
        stores.append((gw, to, inner_dot(taken, steep, 1, 1).astype(jnp.bfloat16)))
        stores.append((mid, (rows, slice(None)), back))
        return stores, total + fold_rows(taken.astype(jnp.float32) * back)

    total = by_chunk(blocks, right, jnp.zeros((8, slots), jnp.float32), arrive_right)
    right_out = gradient_copies(gw, (own_grad, peer_grad), gw_sems, 1)
    for copy in right_out:
        copy.start()
    for copy in left_in:
        copy.wait()
    scale = scale_ref[0:1, :]
    back = scale * scale * jnp.sum(total, axis=0, keepdims=True) / features

    def arrive_left(chunk):
        chunk_copy(u_ref, u, in_sems.at[3], chunk).wait()
        chunk_copy(h_ref, h, in_sems.at[4], chunk).wait()

    def left(block, carry):
        rows = block_rows(block, size)
        place, home = table_ref[0, block], table_ref[2 if last else 1, block]
        at = (place // chunk_blocks, 0, place % chunk_blocks)
        to = (home // chunk_blocks, 0, home % chunk_blocks)
        arrived = [mid[pl.ds(q * blocks + block, blocks, stride=size), :] for q in range(fold)]
        arrived = jnp.concatenate(arrived, axis=0).astype(jnp.bfloat16)
        factor_grad = inner_dot(u[rows, :], arrived, 1, 1).astype(jnp.bfloat16)
        weighted = inner_dot(w[at], arrived, 1, 0) * column(gain_ref, block, slots)
        ended = g[rows, :] + scale * weighted - h[rows, :].astype(jnp.float32) * back
        index = (rows, slice(None))
        stores = [(gw, to, factor_grad)]
        stores.append((u, index, ended.astype(jnp.bfloat16)) if last else (g, index, ended))
        return stores, carry

    ended = u if last else g
    by_chunk(
        blocks, left, 0, arrive_left, lambda chunk: chunk_copy(ended, out_ref, out_sems, chunk).start()
    )
    left_out = gradient_copies(gw, (own_grad, peer_grad), gw_sems, 0)
    for copy in left_out:
        copy.start()
    wait_chunks(ended, out_ref, out_sems)
    for copy in right_out + left_out:
        copy.wait()


def shape_of(shape, dtype):
    return jax.ShapeDtypeStruct(shape, dtype)


SMEM = pl.BlockSpec(memory_space=pltpu.SMEM)
INSIDE = pl.BlockSpec(memory_space=pltpu.VMEM)
OUTSIDE = pl.BlockSpec(memory_space=pl.ANY)


def run_forward(table, gain, sums, residual, weights, layer):
    first = residual.dtype == jnp.bfloat16
    whole = residual.shape
    sources = (*weights, residual)
    held = (PARTS * weights[0].shape[0],) + weights[0].shape[2:]
    out_shape = (
        shape_of(whole, jnp.float32),
        shape_of(whole, jnp.bfloat16),
        shape_of(whole, jnp.bfloat16),
        shape_of(whole, jnp.bfloat16),
        shape_of((8, whole[1]), jnp.float32),
        shape_of((8, whole[1]), jnp.float32),
    )
    return pl.pallas_call(
        lambda *refs: forward_kernel(first, layer, len(sources), *refs),
        in_specs=[SMEM, INSIDE, INSIDE] + [OUTSIDE] * len(sources),
        out_specs=[OUTSIDE] * 4 + [INSIDE] * 2,
        out_shape=out_shape,
        scratch_shapes=[
            pltpu.VMEM(whole if first else SMALL, jnp.bfloat16),
            pltpu.VMEM(whole, jnp.float32),
            pltpu.VMEM(held, jnp.bfloat16),
            pltpu.VMEM(whole, jnp.bfloat16),
            pltpu.VMEM(whole, jnp.bfloat16),
            pltpu.VMEM(whole, jnp.bfloat16),
            pltpu.VMEM(whole, jnp.float32),
            pltpu.SemaphoreType.DMA((CHUNKS,)),
            pltpu.SemaphoreType.DMA((2, PARTS)),
            pltpu.SemaphoreType.DMA((4, CHUNKS)),
        ],
        compiler_params=pltpu.CompilerParams(vmem_limit_bytes=VMEM_LIMIT),
        cost_estimate=pl.CostEstimate(
            flops=FORWARD_COST, bytes_accessed=20 * whole[0] * whole[1], transcendentals=0
        ),
        name="forward_layer",
    )(table, sums, gain, *sources)


def run_backward(table, gain, end_gain, scale, kept, weights, layer, sources, turning, last):
    whole = kept[0].shape
    sources = (*kept, *weights, *sources)
    held = (PARTS * weights[0].shape[0],) + weights[0].shape[2:]
    half = (held[0] // 2,) + held[1:]
    out_shape = [shape_of(whole, jnp.bfloat16 if last else jnp.float32)] + [shape_of(half, jnp.bfloat16)] * 2
    return pl.pallas_call(
        lambda *refs: backward_kernel(turning, last, layer, len(sources), *refs),
        in_specs=[SMEM, INSIDE, INSIDE] + [OUTSIDE] * (1 + len(sources)),
        out_specs=[OUTSIDE] * len(out_shape),
        out_shape=out_shape,
        scratch_shapes=[
            pltpu.VMEM(whole, jnp.float32),
            pltpu.VMEM(whole, jnp.bfloat16),
            pltpu.VMEM(whole, jnp.bfloat16),
            pltpu.VMEM(whole, jnp.bfloat16),
            pltpu.VMEM(whole, jnp.bfloat16 if last else jnp.float32),
            pltpu.VMEM(held, jnp.bfloat16),
            pltpu.VMEM(held, jnp.bfloat16),
            pltpu.VMEM(whole, jnp.float32),
            pltpu.VMEM(whole if turning else SMALL, jnp.float32),
            pltpu.VMEM(whole if turning else SMALL, jnp.bfloat16),
            pltpu.VMEM(whole if turning else SMALL, jnp.bfloat16),
            pltpu.SemaphoreType.DMA((7, CHUNKS)),
            pltpu.SemaphoreType.DMA((2, PARTS)),
            pltpu.SemaphoreType.DMA((CHUNKS,)),
            pltpu.SemaphoreType.DMA((2, PARTS)),
        ],
        compiler_params=pltpu.CompilerParams(vmem_limit_bytes=VMEM_LIMIT),
        cost_estimate=pl.CostEstimate(
            flops=BACKWARD_COST, bytes_accessed=30 * whole[0] * whole[1], transcendentals=0
        ),
        name="backward_layer",
    )(table, scale, gain, end_gain, *sources)


def join_kernel(rows, *refs):
    sources, whole, sems = refs[:-2], refs[-2], refs[-1]
    copies = [
        pltpu.make_async_copy(source.at[pl.ds(0, rows)], whole.at[pl.ds(at * rows, rows)], sems.at[at])
        for at, source in enumerate(sources)
    ]
    for copy in copies:
        copy.start()
    for copy in copies:
        copy.wait()


def joined(parts, rows=None):
    rows = parts[0].shape[0] if rows is None else rows
    whole = shape_of((rows * len(parts),) + parts[0].shape[1:], parts[0].dtype)
    return pl.pallas_call(
        lambda *refs: join_kernel(rows, *refs),
        in_specs=[OUTSIDE] * len(parts),
        out_specs=INSIDE,
        out_shape=whole,
        scratch_shapes=[pltpu.SemaphoreType.DMA((len(parts),))],
        compiler_params=pltpu.CompilerParams(vmem_limit_bytes=VMEM_LIMIT),
        cost_estimate=pl.CostEstimate(
            flops=0, bytes_accessed=4 * math.prod(whole.shape), transcendentals=0
        ),
        name="join",
    )(*parts)


def sum_kernel(terms, inputs, *refs):
    sources, outs = refs[:inputs], refs[inputs:]
    for group in range(inputs // terms):
        mine = sources[group * terms : (group + 1) * terms]
        for at in range(mine[0].shape[0]):
            total = sum(ref[at].astype(jnp.float32) for ref in mine).astype(jnp.bfloat16)
            if len(outs) > 1:
                outs[at][group] = total
            else:
                outs[0][at, group] = total


def run_sum(groups, parts, apart=True):
    flat = [term.reshape(parts, -1, term.shape[-1]) for terms in groups for term in terms]
    _, rows, lanes = flat[0].shape
    steps = 2
    if apart:
        out_shape = [shape_of((len(groups), rows, lanes), jnp.bfloat16)] * parts
        out_specs = [pl.BlockSpec((len(groups), rows // steps, lanes), lambda i: (0, i, 0))] * parts
    else:
        out_shape = [shape_of((parts, len(groups), rows, lanes), jnp.bfloat16)]
        out_specs = [pl.BlockSpec((parts, len(groups), rows // steps, lanes), lambda i: (0, 0, i, 0))]
    sums = pl.pallas_call(
        lambda *refs: sum_kernel(len(groups[0]), len(flat), *refs),
        grid=(steps,),
        in_specs=[pl.BlockSpec((parts, rows // steps, lanes), lambda i: (0, i, 0))] * len(flat),
        out_specs=out_specs,
        out_shape=out_shape,
        compiler_params=pltpu.CompilerParams(vmem_limit_bytes=VMEM_LIMIT),
        cost_estimate=pl.CostEstimate(
            flops=flat[0].size * len(flat), bytes_accessed=2 * flat[0].size * (len(flat) + 1), transcendentals=0
        ),
        name="sum",
    )(*flat)
    return [out.reshape(-1, lanes) for out in sums] if apart else sums[0].reshape(parts, -1, lanes)


def pieces_kernel(chunk, place_ref, order_ref, left_ref, right_ref, gain_ref, out_ref, held, left_sem, sems):
    layer_count, half, size = held.shape[:3]
    first = place_ref[2] * half
    lefts = pltpu.make_async_copy(left_ref.at[:, pl.ds(first, half)], held, left_sem.at[0])
    lefts.start()
    copies = []
    turns = []
    for section in range(out_ref.shape[0]):
        row = 0
        for layer in range(layer_count):
            for inside in range(chunk):
                turns.append((layer, section * chunk + inside, section, row))
                row += size
            for inside in range(chunk):
                source = right_ref.at[layer, first + section * chunk + inside]
                copies.append((source, out_ref.at[section, pl.ds(row, size)]))
                row += size
        copies.append((gain_ref, out_ref.at[section, pl.ds(row, gain_ref.shape[0])]))
    copies = [
        pltpu.make_async_copy(source, target, sems.at[at]) for at, (source, target) in enumerate(copies)
    ]
    for copy in copies:
        copy.start()
    lefts.wait()
    for layer, block, section, row in turns:
        turned = inner_dot(held[layer, block], order_ref[...], 1, 0)
        out_ref[section, pl.ds(row, size), :] = turned.astype(jnp.bfloat16)
    for copy in copies:
        copy.wait()


def factor_pieces(place, order, left, right, gain_rows, chunk, width):
    layer_count, blocks, size = left.shape[:3]
    rows = layer_count * 2 * chunk * size + gain_rows.shape[0]
    return pl.pallas_call(
        lambda *refs: pieces_kernel(chunk, *refs),
        in_specs=[SMEM, INSIDE] + [OUTSIDE] * 3,
        out_specs=INSIDE,
        out_shape=shape_of((width, rows, size), jnp.bfloat16),
        scratch_shapes=[
            pltpu.VMEM((layer_count, blocks // 2, size, size), jnp.bfloat16),
            pltpu.SemaphoreType.DMA((1,)),
            pltpu.SemaphoreType.DMA((width * (layer_count * chunk + 1),)),
        ],
        compiler_params=pltpu.CompilerParams(vmem_limit_bytes=VMEM_LIMIT),
        cost_estimate=pl.CostEstimate(flops=left.size * size, bytes_accessed=4 * left.size, transcendentals=0),
        name="pieces",
    )(place, order, left, right, gain_rows)


def choice(pairs, critic, slots):
    rows = pairs.shape[0]
    named = (pairs[:, 0:1] == critic) | (pairs[:, 1:2] == critic)
    named = jnp.broadcast_to(named.astype(jnp.float32), (rows, slots))
    before = lax.broadcasted_iota(jnp.int32, (rows, rows), 1) < lax.broadcasted_iota(jnp.int32, (rows, rows), 0)
    rank = inner_dot(before.astype(jnp.bfloat16), named.astype(jnp.bfloat16), 1, 0)
    at = lax.broadcasted_iota(jnp.int32, (rows, slots), 1).astype(jnp.float32)
    return jnp.where(rank == at, named, 0.0).astype(jnp.bfloat16)


def pick_kernel(pairs_ref, values_ref, out_ref):
    width, features, slots = out_ref.shape
    pairs = pairs_ref[...]
    chosen = [choice(pairs, critic, slots) for critic in range(width)]
    step = 512
    for start in range(0, features, step):
        part = values_ref[:, pl.ds(start, step)]
        for k in range(width):
            out_ref[k, pl.ds(start, step), :] = inner_dot(part, chosen[k], 0, 0).astype(jnp.bfloat16)


def run_pick(pairs, values, width, slots):
    rows, features = values.shape
    return pl.pallas_call(
        pick_kernel,
        in_specs=[INSIDE] * 2,
        out_specs=INSIDE,
        out_shape=shape_of((width, features, slots), jnp.bfloat16),
        compiler_params=pltpu.CompilerParams(vmem_limit_bytes=VMEM_LIMIT),
        cost_estimate=pl.CostEstimate(
            flops=2 * rows * features * slots * width, bytes_accessed=8 * rows * features, transcendentals=0
        ),
        name="pick",
    )(pairs, values)


def combine_kernel(pairs_ref, came_ref, out_ref):
    width, features, slots = came_ref.shape
    pairs = pairs_ref[...]
    chosen = [choice(pairs, critic, slots) for critic in range(width)]
    step = 512
    for start in range(0, features, step):
        total = sum(inner_dot(chosen[k], came_ref[k, pl.ds(start, step), :], 1, 1) for k in range(width))
        out_ref[:, pl.ds(start, step)] = (0.5 * total).astype(jnp.bfloat16)


def run_combine(pairs, came):
    rows = pairs.shape[0]
    return pl.pallas_call(
        combine_kernel,
        in_specs=[INSIDE] * 2,
        out_specs=INSIDE,
        out_shape=shape_of((rows, came.shape[1]), jnp.bfloat16),
        compiler_params=pltpu.CompilerParams(vmem_limit_bytes=VMEM_LIMIT),
        cost_estimate=pl.CostEstimate(
            flops=2 * rows * came.size, bytes_accessed=4 * came.size, transcendentals=0
        ),
        name="combine",
    )(pairs, came)


FORWARD_COST = 4_000_000_000
BACKWARD_COST = 5_000_000_000


def assemble_kernel(layers, factor, place_ref, order_ref, *refs):
    count = 2 * len(layers)
    sources, (left_ref, right_ref) = refs[:count], refs[count : count + 2]
    held, wide = refs[count + 2 : 2 * count + 2], refs[2 * count + 2 : 3 * count + 2]
    in_sems, out_sems = refs[3 * count + 2 :]
    origin, core = place_ref[0] ^ place_ref[1], place_ref[2]
    order = order_ref[...]
    arrivals = [
        pltpu.make_async_copy(source, held[at], in_sems.at[at]) for at, source in enumerate(sources)
    ]
    for copy in arrivals:
        copy.start()
    leaving = []
    for at in range(count):
        arrivals[at].wait()
        half = core if at % 2 == 0 else 1 - core
        width, _, _, chunk = held[at].shape[:4]
        for k in range(width):
            start = (half * width + (origin ^ k if at < 2 else k)) * chunk
            for inside, layer in enumerate(layers[at // 2]):
                for block in range(chunk):
                    left = inner_dot(held[at][k, inside, 0, block], order, 1, 1)
                    wide[at][k, inside, 0, block] = left * factor
                wide[at][k, inside, 1] = held[at][k, inside, 1].astype(jnp.float32) * factor
                for which, target in enumerate((left_ref, right_ref)):
                    copy = pltpu.make_async_copy(
                        wide[at].at[k, inside, which],
                        target.at[layer, pl.ds(start, chunk)],
                        out_sems.at[len(leaving)],
                    )
                    copy.start()
                    leaving.append(copy)
    for copy in leaving:
        copy.wait()


def run_assemble(place, order, pieces, layers, factor):
    piece = pieces[0].shape
    layer_count = sum(len(group) for group in layers)
    out = shape_of((layer_count, 2 * piece[0] * piece[3]) + piece[4:], jnp.float32)
    return pl.pallas_call(
        lambda *refs: assemble_kernel(layers, factor, *refs),
        in_specs=[SMEM, INSIDE] + [OUTSIDE] * len(pieces),
        out_specs=[OUTSIDE] * 2,
        out_shape=[out] * 2,
        scratch_shapes=[pltpu.VMEM(part.shape, jnp.bfloat16) for part in pieces]
        + [pltpu.VMEM(part.shape, jnp.float32) for part in pieces]
        + [
            pltpu.SemaphoreType.DMA((len(pieces),)),
            pltpu.SemaphoreType.DMA((4 * layer_count * piece[0],)),
        ],
        compiler_params=pltpu.CompilerParams(vmem_limit_bytes=VMEM_LIMIT),
        cost_estimate=pl.CostEstimate(flops=0, bytes_accessed=4 * math.prod(out.shape) * 3, transcendentals=0),
        name="assemble",
    )(place, order, *pieces)


def plane_routes(width, replicas):
    bits = width.bit_length() - 1
    orders = [[(step + d) % bits for step in range(bits)] for d in range(replicas)]
    every = [(s, t, d) for s in range(width) for t in range(width) for d in range(replicas)]

    def route(move):
        def index(s, t, d):
            return (s * width + t) * replicas + d

        return [(index(*place), index(*move(*place))) for place in every]

    ranks = [[0] * width for _ in range(replicas)]
    for d in range(replicas):
        for r in range(width):
            ranks[d][sum(((r >> at) & 1) << orders[d][at] for at in range(bits))] = r
    return {
        "across": [route(lambda s, t, d, at=at: (s ^ (1 << orders[d][at]), t, d)) for at in range(bits)],
        "cores": route(lambda s, t, d: (s, t, 1 - d)),
        "sections": [route(lambda s, t, d, k=k: (s ^ k, t, d)) for k in range(width)],
        "homes": [route(lambda s, t, d, j=j: (t, t ^ s ^ j, d)) for j in range(width)],
    }, ranks


def plane_shards(patches, teacher, critic_pairs, left_factors, right_factors, norm_gains):
    width = lax.axis_size("section")
    replicas = lax.axis_size("dp")
    tok_rows, feat_local = patches.shape
    layer_count, local_blocks, size = left_factors.shape[1:4]
    blocks = feat_local * width // size
    wide = 2 * tok_rows // 3
    chunk = local_blocks // (replicas * width)
    layer_rows = 2 * chunk * size
    routes, ranks = plane_routes(width, replicas)
    section = lax.axis_index("section")
    tensor = lax.axis_index("tensor")
    core = lax.axis_index("dp")
    place = jnp.stack([section, tensor, core]).astype(jnp.int32)
    tie = lax.optimization_barrier

    def move(value, route):
        return lax.ppermute(value, AXES, route)

    def move_all(values, name):
        return [move(value, route) for value, route in zip(values, routes[name])]

    def send(values, name):
        return [values[0]] + [move(values[k], routes[name][k]) for k in range(1, width)]

    def gather_one(mine):
        return joined([mine, move(mine, routes["across"][0])])

    def gather_two(pair):
        return pair, move(pair, routes["across"][1]), move(pair, routes["cores"])

    def gather_three(pair, other, peer):
        return [pair, other, peer, move(other, routes["cores"])]

    def as_weights(parts):
        return [part.reshape(2 * width, -1, 2, chunk, size, size) for part in parts]

    block = jnp.arange(blocks, dtype=jnp.int32)
    inside = block % local_blocks
    replica = inside // (width * chunk)
    part = (replica != core).astype(jnp.int32)
    distance = section ^ ((inside // chunk) % width)
    quarter = block // local_blocks
    rank = jnp.array(ranks, jnp.int32)[replica, distance]
    table = jnp.stack(
        [
            ((part * width + index) * width + piece) * chunk + inside % chunk
            for index, piece in (
                (rank, quarter),
                (distance, quarter),
                (distance, tensor ^ section ^ distance ^ quarter),
            )
        ]
    ).astype(jnp.int32)

    def to_planes(value):
        return lax.all_to_all(value, "tensor", split_axis=0, concat_axis=0, tiled=True)

    def to_sections(value):
        return lax.all_to_all(value, "section", split_axis=0, concat_axis=0, tiled=True)

    half_layers = layer_count // 2
    groups = [tuple(range(half_layers)), tuple(range(half_layers, layer_count))]
    fold = size // blocks
    columns = jnp.arange(size)
    order = (columns[:, None] == (columns % blocks) * fold + columns // blocks).astype(jnp.bfloat16)
    gain_rows = norm_gains[0].reshape(-1, size)
    pieces = factor_pieces(place, order, left_factors[0], right_factors[0], gain_rows, chunk, width)
    pieces, patches, teacher = tie((pieces, patches, teacher))
    spread = to_sections(pieces)
    patch_sent = run_pick(critic_pairs, patches, width, wide)
    target_sent = run_pick(critic_pairs, teacher, width, wide)
    spread, patch_sent, target_sent = tie((spread, patch_sent, target_sent))
    lifted = to_planes(spread)
    lifted, patch_sent = tie((lifted, patch_sent))
    patch_came = to_planes(patch_sent).reshape(-1, wide)
    lowest = [lifted[:, group[0] * layer_rows : (group[-1] + 1) * layer_rows] for group in groups]
    beside = move(lowest[0], routes["across"][0])
    gains = lifted[:, layer_count * layer_rows :].reshape(width, layer_count + 1, local_blocks, size)
    gains = gains.transpose(1, 3, 0, 2).reshape(layer_count + 1, size, blocks)
    end_column = jnp.broadcast_to(gains[layer_count].T[:, :, None], (blocks, size, wide)).reshape(-1, wide)
    lowest, beside, end_column = tie((lowest, beside, end_column))
    first_two = gather_two(joined([lowest[0], beside]))
    later = (lowest[1], move(lowest[1], routes["across"][0]))
    first_two, later, patch_came = tie((first_two, later, patch_came))
    weights = [as_weights(gather_three(*first_two))]
    weights, later = tie((weights, later))

    residual, target_sent = tie((patch_came, target_sent))
    target = to_planes(target_sent).reshape(-1, wide)
    flying = gather_two(joined(list(later)))
    sums = jnp.zeros((8, wide), jnp.float32)
    stored = []
    for layer in range(layer_count):
        group = 0 if layer in groups[0] else 1
        following, u, z, slope, scale, sums = run_forward(
            table, gains[layer], sums, residual, weights[group], layer - groups[group][0]
        )
        stored.append(((slope, z, u), scale, residual))
        residual = following
        if layer == 0:
            residual, sums, flying = tie((residual, sums, flying))
            weights.append(as_weights(gather_three(*flying)))
        if layer == groups[0][-1]:
            residual, sums, weights[1] = tie((residual, sums, weights[1]))
        if layer == layer_count - 2:
            residual, sums, target = tie((residual, sums, target))

    def core_sum(mine, other):
        return (mine, move(other, routes["cores"]))

    def plane_sum(mine, other):
        return send(run_sum([(mine, other)], width), "sections")

    def homeward(parts):
        return move_all(run_sum(parts, width), "homes")

    def both_halves(whole):
        pair = (whole, move(whole, routes["cores"]))
        return [part.reshape(width, -1, 2, chunk, size, size) for part in pair]

    steps = (core_sum, plane_sum)
    gradient = residual
    underway = []
    for layer in range(layer_count - 1, -1, -1):
        turning = layer == layer_count - 1
        last = layer == 0
        kept, scale, inputs = stored[layer]
        group = 0 if layer in groups[0] else 1
        sources = (gradient, inputs, target) if turning else (gradient, inputs)
        underway = [(at + 1, steps[at](*state)) if at < len(steps) else (at, state) for at, state in underway]
        gradient, mine, other = run_backward(
            table,
            gains[layer],
            end_column,
            scale,
            kept,
            weights[group],
            layer - groups[group][0],
            sources,
            turning,
            last,
        )
        gradient, mine, other, states = tie((gradient, mine, other, [state for _, state in underway]))
        underway = [(at, state) for (at, _), state in zip(underway, states)]
        underway.append((0, (mine, other)))

    returned = to_planes(gradient.reshape(width, feat_local, wide))
    ended = [steps[at](*state) if at < len(steps) else state for at, state in underway][::-1]
    ended = tie(ended)
    ended[0] = plane_sum(*ended[0])
    others = to_planes(run_sum(ended[1:], width, apart=False))
    ended[0], returned, others = tie((ended[0], returned, others))
    home = homeward(ended[:1])
    d_patches = run_combine(critic_pairs, returned)
    others = to_sections(others)
    d_patches, home, others = tie((d_patches, home, others))
    homes_of = both_halves(joined(home)) + both_halves(others)
    grad_factor = 1.0 / math.sqrt(2 * tok_rows * width * replicas)
    grad_left, grad_right = run_assemble(
        place, order, homes_of, [(0,), tuple(range(1, layer_count))], grad_factor
    )
    return (d_patches, grad_left[None], grad_right[None])


def solution(mesh):
    in_specs = (
        P(("section", "dp"), "tensor"),
        P(("section", "dp"), "tensor"),
        P(("section", "dp"), None),
        P("section", None, "tensor", None, None),
        P("section", None, "tensor", None, None),
        P("section", None, "tensor"),
    )
    out_specs = (
        P(("section", "dp"), "tensor"),
        P("section", None, "tensor", None, None),
        P("section", None, "tensor", None, None),
    )
    body = plane_shards if planes_fit(mesh) else layered_shards
    return jax.shard_map(
        body, mesh=mesh, in_specs=in_specs, out_specs=out_specs, check_vma=False)
```

```python
import math

import jax
import jax.numpy as jnp
from jax import lax
from jax.experimental import pallas as pl
from jax.experimental.pallas import tpu as pltpu
from jax.sharding import PartitionSpec as P

EPSILON = 1e-06
TANH_SLOPE = 0.7978845608028654
CUBIC_TERM = 0.044715


def shifted(value, axis, steps):
    count = lax.axis_size(axis)
    first, last = (max(0, -steps), min(count, count - steps))
    return lax.ppermute(value, axis, [(source, source + steps) for source in range(first, last)])


def gelu_value(values):
    tangent = jnp.tanh(TANH_SLOPE * (values + CUBIC_TERM * values * values * values))
    return 0.5 * values * (1.0 + tangent)


def gelu_slope(values):
    tangent = jnp.tanh(TANH_SLOPE * (values + CUBIC_TERM * values * values * values))
    return 0.5 * (1.0 + tangent) + 0.5 * values * (1.0 - tangent * tangent) * TANH_SLOPE * (
        1.0 + 3.0 * CUBIC_TERM * values * values
    )


def norm_pair(residuals, gain_pair, model_width):
    squares = lax.psum(
        (
            jnp.sum(residuals[0] * residuals[0], axis=(1, 2)),
            jnp.sum(residuals[1] * residuals[1], axis=(1, 2)),
        ),
        "tensor",
    )
    factors = [lax.rsqrt(squares[member] / model_width + EPSILON) for member in range(2)]
    normed = [
        residuals[member] * factors[member][:, None, None] * gain_pair[member][None]
        for member in range(2)
    ]
    return (factors, normed)


def norm_back_pair(residuals, factors, gain_pair, grad_normed, carried, model_width):
    weighted = [grad_normed[member] * gain_pair[member][None] for member in range(2)]
    inners = lax.psum(
        (
            jnp.sum(weighted[0] * residuals[0], axis=(1, 2)),
            jnp.sum(weighted[1] * residuals[1], axis=(1, 2)),
        ),
        "tensor",
    )
    return [
        carried[member]
        + factors[member][:, None, None] * weighted[member]
        - residuals[member] * (factors[member] ** 3 * inners[member] / model_width)[:, None, None]
        for member in range(2)
    ]


def layered_shards(patches, teacher, critic_pairs, left_factors, right_factors, norm_gains):
    sections = lax.axis_size("section")
    tensor_width = lax.axis_size("tensor")
    replicas = lax.axis_size("dp")
    tok_rows = patches.shape[0]
    feat_local = patches.shape[1]
    layer_count = left_factors.shape[1]
    local_blocks = left_factors.shape[2]
    block_size = left_factors.shape[3]
    all_blocks = local_blocks * tensor_width
    fold_ratio = block_size // all_blocks
    model_width = feat_local * tensor_width
    sixth_rows = tok_rows // 6
    leading = 2 * sixth_rows
    critic_ids = jnp.arange(4, dtype=jnp.int32)
    named_by = (
        (critic_pairs[:, 0:1] == critic_ids[None, :])
        | (critic_pairs[:, 1:2] == critic_ids[None, :])
    ).astype(jnp.int32)
    ranking = jnp.cumsum(named_by, axis=0) - 1
    wide_ids = critic_ids[None, :] < 2
    slot_width = 3 * sixth_rows
    spilled = wide_ids & (ranking >= 3 * sixth_rows)
    destination = jnp.where(spilled, critic_ids[None, :] + 2, critic_ids[None, :])
    slot_index = jnp.where(spilled, ranking - sixth_rows, ranking)
    flat_slot = destination * slot_width + slot_index
    chosen = jnp.take_along_axis(flat_slot, critic_pairs, axis=1)
    slot_total = sections * slot_width
    row_ids = jnp.broadcast_to(jnp.arange(tok_rows, dtype=jnp.int32)[:, None], chosen.shape)
    source_row = (
        jnp.full((slot_total,), tok_rows, jnp.int32).at[chosen.reshape(-1)].set(row_ids.reshape(-1))
    )
    send_patch = (
        patches.at[source_row]
        .get(mode="fill", fill_value=0)
        .reshape(sections, slot_width, local_blocks, block_size)
    )
    send_target = (
        teacher.at[source_row]
        .get(mode="fill", fill_value=0)
        .reshape(sections, slot_width, local_blocks, block_size)
    )
    recv_patch, recv_target = (
        lax.all_to_all(send_patch, "section", split_axis=0, concat_axis=0, tiled=True),
        lax.all_to_all(send_target, "section", split_axis=0, concat_axis=0, tiled=True),
    )
    residuals = [
        recv_patch[:, :leading].reshape(-1, local_blocks, block_size).astype(jnp.float32),
        recv_patch[:, leading:].reshape(-1, local_blocks, block_size).astype(jnp.float32),
    ]
    targets = [
        recv_target[:, :leading].reshape(-1, local_blocks, block_size).astype(jnp.float32),
        recv_target[:, leading:].reshape(-1, local_blocks, block_size).astype(jnp.float32),
    ]
    native = (left_factors[0], right_factors[0], norm_gains[0])
    borrowed = shifted((left_factors, right_factors, norm_gains), "section", 2)
    is_wide = lax.axis_index("section") < 2
    second = (
        jnp.where(is_wide, left_factors, borrowed[0])[0],
        jnp.where(is_wide, right_factors, borrowed[1])[0],
        jnp.where(is_wide, norm_gains, borrowed[2])[0],
    )
    left_sets = (native[0], second[0])
    right_sets = (native[1], second[1])
    gain_sets = (
        native[2].astype(jnp.float32).reshape(layer_count + 1, local_blocks, block_size),
        second[2].astype(jnp.float32).reshape(layer_count + 1, local_blocks, block_size),
    )
    stored = []
    for layer_index in range(layer_count):
        gain_pair = [gain_sets[0][layer_index], gain_sets[1][layer_index]]
        factors, normed = norm_pair(residuals, gain_pair, model_width)
        normed = [normed[member].astype(jnp.bfloat16) for member in range(2)]
        first_out = [
            jnp.einsum(
                "nki,kij->nkj",
                normed[member],
                left_sets[member][layer_index],
                preferred_element_type=jnp.float32,
            ).astype(jnp.bfloat16)
            for member in range(2)
        ]
        permuted = (
            lax.all_to_all(first_out[0], "tensor", split_axis=2, concat_axis=1, tiled=True),
            lax.all_to_all(first_out[1], "tensor", split_axis=2, concat_axis=1, tiled=True),
        )
        permuted = [
            permuted[member].reshape(
                permuted[member].shape[0], all_blocks, local_blocks, fold_ratio
            )
            for member in range(2)
        ]
        right_quads = [
            right_sets[member][layer_index].reshape(
                local_blocks, fold_ratio, all_blocks, block_size
            )
            for member in range(2)
        ]
        mixture = [
            jnp.einsum(
                "nkmp,mpkl->nml",
                permuted[member],
                right_quads[member],
                preferred_element_type=jnp.float32,
            )
            for member in range(2)
        ]
        stored.append((residuals, factors, normed, permuted, mixture, right_quads, gain_pair))
        residuals = [residuals[member] + gelu_value(mixture[member]) for member in range(2)]
    final_gains = [gain_sets[0][layer_count], gain_sets[1][layer_count]]
    factors, outputs = norm_pair(residuals, final_gains, model_width)
    gradients = norm_back_pair(
        residuals,
        factors,
        final_gains,
        [outputs[member] - targets[member] for member in range(2)],
        [jnp.zeros_like(residuals[member]) for member in range(2)],
        model_width,
    )
    left_terms = []
    right_terms = []
    for layer_index in range(layer_count - 1, -1, -1):
        inputs, factors, normed, permuted, mixture, right_quads, gain_pair = stored[layer_index]
        slopes = [
            (gradients[member] * gelu_slope(mixture[member])).astype(jnp.bfloat16)
            for member in range(2)
        ]
        right_grad = [
            jnp.einsum(
                "nkmp,nml->mpkl",
                permuted[member],
                slopes[member],
                preferred_element_type=jnp.float32,
            ).reshape(local_blocks, block_size, block_size)
            for member in range(2)
        ]
        back_moved = [
            jnp.einsum(
                "nml,mpkl->nkmp",
                slopes[member],
                right_quads[member],
                preferred_element_type=jnp.float32,
            )
            .astype(jnp.bfloat16)
            .reshape(slopes[member].shape[0], all_blocks, local_blocks * fold_ratio)
            for member in range(2)
        ]
        arrived = (
            lax.all_to_all(back_moved[0], "tensor", split_axis=1, concat_axis=2, tiled=True),
            lax.all_to_all(back_moved[1], "tensor", split_axis=1, concat_axis=2, tiled=True),
        )
        left_grad = [
            jnp.einsum(
                "nki,nkj->kij", normed[member], arrived[member], preferred_element_type=jnp.float32
            )
            for member in range(2)
        ]
        grad_normed = [
            jnp.einsum(
                "nkj,kij->nki",
                arrived[member],
                left_sets[member][layer_index],
                preferred_element_type=jnp.float32,
            )
            for member in range(2)
        ]
        gradients = norm_back_pair(inputs, factors, gain_pair, grad_normed, gradients, model_width)
        layer_left = jnp.stack(left_grad)
        layer_right = jnp.stack(right_grad)
        layer_left, layer_right = (
            lax.psum(layer_left.astype(jnp.bfloat16), "dp").astype(jnp.float32),
            lax.psum(layer_right.astype(jnp.bfloat16), "dp").astype(jnp.float32),
        )
        left_terms.insert(0, layer_left)
        right_terms.insert(0, layer_right)
    left_stack = jnp.stack(left_terms)
    right_stack = jnp.stack(right_terms)
    repaid = (
        shifted(left_stack[:, 1].astype(jnp.bfloat16), "section", -2).astype(jnp.float32),
        shifted(right_stack[:, 1].astype(jnp.bfloat16), "section", -2).astype(jnp.float32),
    )
    is_wide = lax.axis_index("section") < 2
    left_total = left_stack[:, 0] + jnp.where(is_wide, left_stack[:, 1] + repaid[0], 0.0)
    right_total = right_stack[:, 0] + jnp.where(is_wide, right_stack[:, 1] + repaid[1], 0.0)
    grad_factor = 1.0 / math.sqrt(2 * tok_rows * sections * replicas)
    returned = [
        gradients[member].astype(jnp.bfloat16).reshape(sections, -1, local_blocks, block_size)
        for member in range(2)
    ]
    back_lead, back_trail = (
        lax.all_to_all(returned[0], "section", split_axis=0, concat_axis=0, tiled=True),
        lax.all_to_all(returned[1], "section", split_axis=0, concat_axis=0, tiled=True),
    )
    gathered = jnp.concatenate((back_lead, back_trail), axis=1).reshape(
        slot_total, local_blocks, block_size
    )
    combined = (
        gathered[chosen[:, 0]].astype(jnp.float32) + gathered[chosen[:, 1]].astype(jnp.float32)
    ) * 0.5
    d_patches = combined.astype(jnp.bfloat16).reshape(tok_rows, feat_local)
    return (d_patches, (left_total * grad_factor)[None], (right_total * grad_factor)[None])


VMEM_LIMIT = 60 * 1024 * 1024
CHUNKS = 8
TOGETHER = 4
PARTS = 4
SMALL = (16, 128)
AXES = ("section", "tensor", "dp")


def planes_fit(mesh):
    sections = mesh.shape["section"]
    paired = mesh.shape["dp"] == 2 and sections & (sections - 1) == 0
    return paired and mesh.shape["tensor"] == sections


def inner_dot(left, right, left_dim, right_dim):
    return lax.dot_general(
        left,
        right,
        (((left_dim,), (right_dim,)), ((), ())),
        preferred_element_type=jnp.float32,
    )


def fold_rows(values):
    return jnp.sum(values.reshape(values.shape[0] // 8, 8, values.shape[1]), axis=0)


def block_rows(block, size):
    return pl.ds(pl.multiple_of(block * size, size), size)


def column(gain_ref, block, at, slots):
    gains = gain_ref[block // gain_ref.shape[2]]
    return jnp.broadcast_to(gains[:, at : at + 1], (gains.shape[0], slots))


def chunk_copy(source, target, sems, chunk):
    rows = target.shape[0] // CHUNKS
    at = pl.ds(pl.multiple_of(chunk * rows, rows), rows)
    return pltpu.make_async_copy(source.at[at], target.at[at], sems.at[chunk])


def start_chunks(source, target, sems):
    for chunk in range(CHUNKS):
        chunk_copy(source, target, sems, chunk).start()


def wait_chunks(source, target, sems):
    for chunk in range(CHUNKS):
        chunk_copy(source, target, sems, chunk).wait()


def factor_copies(parts, layer, held, sems, side):
    count = parts[0].shape[0]
    return [
        pltpu.make_async_copy(
            ref.at[:, layer, side], held.at[pl.ds(at * count, count), side], sems.at[side, at]
        )
        for at, ref in enumerate(parts)
    ]


def gradient_copies(held, parts, sems, side):
    count = parts[0].shape[0]
    return [
        pltpu.make_async_copy(
            held.at[pl.ds(at * count, count), side], ref.at[:, side], sems.at[side, at]
        )
        for at, ref in enumerate(parts)
    ]


def by_chunk(blocks, step, carry, before=None, after=None):
    per_chunk = blocks // CHUNKS

    def few(start, first, carry):
        stores = []
        for at in range(TOGETHER):
            made, carry = step(start + at, first + at, carry)
            stores += made
        for ref, index, value in stores:
            ref[index] = value
        return carry

    def one(chunk, carry):
        if before is not None:
            before(chunk)
        for at in range(0, per_chunk, TOGETHER):
            carry = few(chunk * per_chunk + at, at, carry)
        if after is not None:
            after(chunk)
        return carry

    return lax.fori_loop(0, CHUNKS, one, carry)


def forward_kernel(first, layer, inputs, table_ref, sums_ref, gain_ref, *refs):
    sources, refs = refs[:inputs], refs[inputs:]
    parts, sources = sources[:PARTS], sources[PARTS:]
    out_ref, u_ref, z_ref, slope_ref, scale_ref, next_ref = refs[:6]
    raw, h, w, u, z, slope, mid, in_sems, w_sems, out_sems = refs[6:]
    features, slots = h.shape
    size = w.shape[-1]
    chunk_blocks = w.shape[2]
    blocks = features // size
    fold = size // blocks

    left_in = factor_copies(parts, layer, w, w_sems, 0)
    right_in = factor_copies(parts, layer, w, w_sems, 1)
    if first:
        start_chunks(sources[0], raw, in_sems)
        for copy in left_in + right_in:
            copy.start()

        def squares(block, _, total):
            rows = block_rows(block, size)
            part = raw[rows, :].astype(jnp.float32)
            return [(h, (rows, slice(None)), part)], total + fold_rows(part * part)

        total = by_chunk(
            blocks,
            squares,
            jnp.zeros((8, slots), jnp.float32),
            lambda chunk: chunk_copy(sources[0], raw, in_sems, chunk).wait(),
        )
    else:
        for copy in left_in:
            copy.start()
        start_chunks(sources[0], h, in_sems)
        for copy in right_in:
            copy.start()
        total = sums_ref[...]
    scale = lax.rsqrt(jnp.sum(total, axis=0, keepdims=True) / features + EPSILON)
    scale_ref[...] = jnp.broadcast_to(scale, scale_ref.shape)
    for copy in left_in:
        copy.wait()

    def arrive(chunk):
        if not first:
            chunk_copy(sources[0], h, in_sems, chunk).wait()

    def left(block, nth, carry):
        rows = block_rows(block, size)
        place = table_ref[0, block]
        normed = (h[rows, :] * scale * column(gain_ref, block, nth, slots)).astype(jnp.bfloat16)
        weight = w[place // chunk_blocks, 0, place % chunk_blocks]
        first_out = inner_dot(weight, normed, 0, 0)
        at = (rows, slice(None))
        return [(u, at, normed), (mid, at, first_out)], carry

    def leave_left(chunk):
        chunk_copy(u, u_ref, out_sems.at[0], chunk).start()

    by_chunk(blocks, left, 0, arrive, leave_left)
    for copy in right_in:
        copy.wait()

    def right(block, nth, total):
        rows = block_rows(block, size)
        place = table_ref[0, block]
        moved = [mid[pl.ds(q * blocks + block, blocks, stride=size), :] for q in range(fold)]
        moved = jnp.concatenate(moved, axis=0).astype(jnp.bfloat16)
        weight = w[place // chunk_blocks, 1, place % chunk_blocks]
        mixture = inner_dot(weight, moved, 0, 0)
        squared = mixture * mixture
        tangent = jnp.tanh(mixture * (TANH_SLOPE + (TANH_SLOPE * CUBIC_TERM) * squared))
        half = 0.5 + 0.5 * tangent
        following = h[rows, :] + mixture * half
        steep = half + mixture * (1.0 - tangent * tangent) * (
            0.5 * TANH_SLOPE + (1.5 * TANH_SLOPE * CUBIC_TERM) * squared
        )
        at = (rows, slice(None))
        stores = [(z, at, moved), (h, at, following), (slope, at, steep.astype(jnp.bfloat16))]
        return stores, total + fold_rows(following * following)

    leaving = ((h, out_ref, 1), (z, z_ref, 2), (slope, slope_ref, 3))

    def leave_right(chunk):
        for source, target, at in leaving:
            chunk_copy(source, target, out_sems.at[at], chunk).start()

    next_ref[...] = by_chunk(blocks, right, jnp.zeros((8, slots), jnp.float32), None, leave_right)
    for source, target, at in ((u, u_ref, 0),) + leaving:
        wait_chunks(source, target, out_sems.at[at])


def backward_kernel(turning, last, layer, inputs, table_ref, scale_ref, gain_ref, end_gain_ref, *refs):
    sources, refs = refs[:inputs], refs[inputs:]
    slope_ref, z_ref, u_ref = sources[:3]
    parts, sources = sources[3 : 3 + PARTS], sources[3 + PARTS :]
    out_ref, own_grad, peer_grad = refs[:3]
    g, slope, z, u, h, w, gw, mid, top, goal = refs[3:13]
    in_sems, w_sems, out_sems, gw_sems = refs[13:]
    features, slots = g.shape
    size = w.shape[-1]
    chunk_blocks = w.shape[2]
    blocks = features // size
    fold = size // blocks

    left_in = factor_copies(parts, layer, w, w_sems, 0)
    right_in = factor_copies(parts, layer, w, w_sems, 1)
    g_ref, h_ref = sources[:2]
    if turning:
        for chunk in range(CHUNKS):
            chunk_copy(g_ref, top, in_sems.at[0], chunk).start()
            chunk_copy(sources[2], goal, in_sems.at[5], chunk).start()
    for copy in right_in:
        copy.start()
    for chunk in range(CHUNKS):
        if not turning:
            chunk_copy(g_ref, g, in_sems.at[0], chunk).start()
        chunk_copy(slope_ref, slope, in_sems.at[1], chunk).start()
        chunk_copy(z_ref, z, in_sems.at[2], chunk).start()
    for copy in left_in:
        copy.start()
    for chunk in range(CHUNKS):
        chunk_copy(u_ref, u, in_sems.at[3], chunk).start()
        chunk_copy(h_ref, h, in_sems.at[4], chunk).start()

    if turning:
        zero = jnp.zeros((8, slots), jnp.float32)

        def sums(block, nth, totals):
            rows = block_rows(block, size)
            part = top[rows, :]
            scaled = part * column(end_gain_ref, block, nth, slots)
            return [], (
                totals[0] + fold_rows(part * part),
                totals[1] + fold_rows(scaled * scaled),
                totals[2] + fold_rows(scaled * goal[rows, :].astype(jnp.float32)),
            )

        def arrive_top(chunk):
            chunk_copy(g_ref, top, in_sems.at[0], chunk).wait()
            chunk_copy(sources[2], goal, in_sems.at[5], chunk).wait()

        totals = by_chunk(blocks, sums, (zero, zero, zero), arrive_top)
        squares, gained, crossed = [jnp.sum(total, axis=0, keepdims=True) for total in totals]
        end_scale = lax.rsqrt(squares / features + EPSILON)
        end_back = end_scale * end_scale * end_scale * (end_scale * gained - crossed) / features

    for copy in right_in:
        copy.wait()

    def arrive_right(chunk):
        if not turning:
            chunk_copy(g_ref, g, in_sems.at[0], chunk).wait()
        chunk_copy(slope_ref, slope, in_sems.at[1], chunk).wait()
        chunk_copy(z_ref, z, in_sems.at[2], chunk).wait()

    def right(block, nth, total):
        rows = block_rows(block, size)
        place, home = table_ref[0, block], table_ref[2 if last else 1, block]
        at = (place // chunk_blocks, 1, place % chunk_blocks)
        to = (home // chunk_blocks, 1, home % chunk_blocks)
        if turning:
            part = top[rows, :]
            factor = column(end_gain_ref, block, nth, slots)
            error = (part * end_scale * factor - goal[rows, :].astype(jnp.float32)) * factor
            gradient = end_scale * error - part * end_back
            stores = [(g, (rows, slice(None)), gradient)]
        else:
            gradient = g[rows, :]
            stores = []
        steep = (gradient * slope[rows, :].astype(jnp.float32)).astype(jnp.bfloat16)
        taken = z[rows, :]
        back = inner_dot(w[at], steep, 1, 0)
        stores.append((gw, to, inner_dot(taken, steep, 1, 1).astype(jnp.bfloat16)))
        stores.append((mid, (rows, slice(None)), back))
        return stores, total + fold_rows(taken.astype(jnp.float32) * back)

    total = by_chunk(blocks, right, jnp.zeros((8, slots), jnp.float32), arrive_right)
    right_out = gradient_copies(gw, (own_grad, peer_grad), gw_sems, 1)
    for copy in right_out:
        copy.start()
    for copy in left_in:
        copy.wait()
    scale = scale_ref[0:1, :]
    back = scale * scale * jnp.sum(total, axis=0, keepdims=True) / features

    def arrive_left(chunk):
        chunk_copy(u_ref, u, in_sems.at[3], chunk).wait()
        chunk_copy(h_ref, h, in_sems.at[4], chunk).wait()

    def left(block, nth, carry):
        rows = block_rows(block, size)
        place, home = table_ref[0, block], table_ref[2 if last else 1, block]
        at = (place // chunk_blocks, 0, place % chunk_blocks)
        to = (home // chunk_blocks, 0, home % chunk_blocks)
        arrived = [mid[pl.ds(q * blocks + block, blocks, stride=size), :] for q in range(fold)]
        arrived = jnp.concatenate(arrived, axis=0).astype(jnp.bfloat16)
        factor_grad = inner_dot(u[rows, :], arrived, 1, 1).astype(jnp.bfloat16)
        weighted = inner_dot(w[at], arrived, 1, 0) * column(gain_ref, block, nth, slots)
        ended = g[rows, :] + scale * weighted - h[rows, :].astype(jnp.float32) * back
        index = (rows, slice(None))
        stores = [(gw, to, factor_grad)]
        stores.append((u, index, ended.astype(jnp.bfloat16)) if last else (g, index, ended))
        return stores, carry

    ended = u if last else g
    by_chunk(
        blocks, left, 0, arrive_left, lambda chunk: chunk_copy(ended, out_ref, out_sems, chunk).start()
    )
    left_out = gradient_copies(gw, (own_grad, peer_grad), gw_sems, 0)
    for copy in left_out:
        copy.start()
    wait_chunks(ended, out_ref, out_sems)
    for copy in right_out + left_out:
        copy.wait()


def shape_of(shape, dtype):
    return jax.ShapeDtypeStruct(shape, dtype)


SMEM = pl.BlockSpec(memory_space=pltpu.SMEM)
INSIDE = pl.BlockSpec(memory_space=pltpu.VMEM)
OUTSIDE = pl.BlockSpec(memory_space=pl.ANY)


def run_forward(table, gain, sums, residual, weights, layer):
    first = residual.dtype == jnp.bfloat16
    whole = residual.shape
    sources = (*weights, residual)
    held = (PARTS * weights[0].shape[0],) + weights[0].shape[2:]
    out_shape = (
        shape_of(whole, jnp.float32),
        shape_of(whole, jnp.bfloat16),
        shape_of(whole, jnp.bfloat16),
        shape_of(whole, jnp.bfloat16),
        shape_of((8, whole[1]), jnp.float32),
        shape_of((8, whole[1]), jnp.float32),
    )
    return pl.pallas_call(
        lambda *refs: forward_kernel(first, layer, len(sources), *refs),
        in_specs=[SMEM, INSIDE, INSIDE] + [OUTSIDE] * len(sources),
        out_specs=[OUTSIDE] * 4 + [INSIDE] * 2,
        out_shape=out_shape,
        scratch_shapes=[
            pltpu.VMEM(whole if first else SMALL, jnp.bfloat16),
            pltpu.VMEM(whole, jnp.float32),
            pltpu.VMEM(held, jnp.bfloat16),
            pltpu.VMEM(whole, jnp.bfloat16),
            pltpu.VMEM(whole, jnp.bfloat16),
            pltpu.VMEM(whole, jnp.bfloat16),
            pltpu.VMEM(whole, jnp.float32),
            pltpu.SemaphoreType.DMA((CHUNKS,)),
            pltpu.SemaphoreType.DMA((2, PARTS)),
            pltpu.SemaphoreType.DMA((4, CHUNKS)),
        ],
        compiler_params=pltpu.CompilerParams(vmem_limit_bytes=VMEM_LIMIT),
        cost_estimate=pl.CostEstimate(
            flops=FORWARD_COST, bytes_accessed=20 * whole[0] * whole[1], transcendentals=0
        ),
        name="forward_layer",
    )(table, sums, gain, *sources)


def run_backward(table, gain, end_gain, scale, kept, weights, layer, sources, turning, last):
    whole = kept[0].shape
    sources = (*kept, *weights, *sources)
    held = (PARTS * weights[0].shape[0],) + weights[0].shape[2:]
    half = (held[0] // 2,) + held[1:]
    out_shape = [shape_of(whole, jnp.bfloat16 if last else jnp.float32)] + [shape_of(half, jnp.bfloat16)] * 2
    return pl.pallas_call(
        lambda *refs: backward_kernel(turning, last, layer, len(sources), *refs),
        in_specs=[SMEM] + [INSIDE] * 3 + [OUTSIDE] * len(sources),
        out_specs=[OUTSIDE] * len(out_shape),
        out_shape=out_shape,
        scratch_shapes=[
            pltpu.VMEM(whole, jnp.float32),
            pltpu.VMEM(whole, jnp.bfloat16),
            pltpu.VMEM(whole, jnp.bfloat16),
            pltpu.VMEM(whole, jnp.bfloat16),
            pltpu.VMEM(whole, jnp.bfloat16 if last else jnp.float32),
            pltpu.VMEM(held, jnp.bfloat16),
            pltpu.VMEM(held, jnp.bfloat16),
            pltpu.VMEM(whole, jnp.float32),
            pltpu.VMEM(whole if turning else SMALL, jnp.float32),
            pltpu.VMEM(whole if turning else SMALL, jnp.bfloat16),
            pltpu.SemaphoreType.DMA((6, CHUNKS)),
            pltpu.SemaphoreType.DMA((2, PARTS)),
            pltpu.SemaphoreType.DMA((CHUNKS,)),
            pltpu.SemaphoreType.DMA((2, PARTS)),
        ],
        compiler_params=pltpu.CompilerParams(vmem_limit_bytes=VMEM_LIMIT),
        cost_estimate=pl.CostEstimate(
            flops=BACKWARD_COST, bytes_accessed=30 * whole[0] * whole[1], transcendentals=0
        ),
        name="backward_layer",
    )(table, scale, gain, end_gain, *sources)


def join_kernel(rows, *refs):
    sources, whole, sems = refs[:-2], refs[-2], refs[-1]
    copies = [
        pltpu.make_async_copy(source.at[pl.ds(0, rows)], whole.at[pl.ds(at * rows, rows)], sems.at[at])
        for at, source in enumerate(sources)
    ]
    for copy in copies:
        copy.start()
    for copy in copies:
        copy.wait()


def joined(parts, rows=None):
    rows = parts[0].shape[0] if rows is None else rows
    whole = shape_of((rows * len(parts),) + parts[0].shape[1:], parts[0].dtype)
    return pl.pallas_call(
        lambda *refs: join_kernel(rows, *refs),
        in_specs=[OUTSIDE] * len(parts),
        out_specs=INSIDE,
        out_shape=whole,
        scratch_shapes=[pltpu.SemaphoreType.DMA((len(parts),))],
        compiler_params=pltpu.CompilerParams(vmem_limit_bytes=VMEM_LIMIT),
        cost_estimate=pl.CostEstimate(
            flops=0, bytes_accessed=4 * math.prod(whole.shape), transcendentals=0
        ),
        name="join",
    )(*parts)


def sum_kernel(terms, inputs, *refs):
    sources, outs = refs[:inputs], refs[inputs:]
    for group in range(inputs // terms):
        mine = sources[group * terms : (group + 1) * terms]
        for at in range(mine[0].shape[0]):
            total = sum(ref[at].astype(jnp.float32) for ref in mine).astype(jnp.bfloat16)
            if len(outs) > 1:
                outs[at][group] = total
            else:
                outs[0][at, group] = total


def run_sum(groups, parts, apart=True):
    flat = [term.reshape(parts, -1, term.shape[-1]) for terms in groups for term in terms]
    _, rows, lanes = flat[0].shape
    steps = 2
    if apart:
        out_shape = [shape_of((len(groups), rows, lanes), jnp.bfloat16)] * parts
        out_specs = [pl.BlockSpec((len(groups), rows // steps, lanes), lambda i: (0, i, 0))] * parts
    else:
        out_shape = [shape_of((parts, len(groups), rows, lanes), jnp.bfloat16)]
        out_specs = [pl.BlockSpec((parts, len(groups), rows // steps, lanes), lambda i: (0, 0, i, 0))]
    sums = pl.pallas_call(
        lambda *refs: sum_kernel(len(groups[0]), len(flat), *refs),
        grid=(steps,),
        in_specs=[pl.BlockSpec((parts, rows // steps, lanes), lambda i: (0, i, 0))] * len(flat),
        out_specs=out_specs,
        out_shape=out_shape,
        compiler_params=pltpu.CompilerParams(vmem_limit_bytes=VMEM_LIMIT),
        cost_estimate=pl.CostEstimate(
            flops=flat[0].size * len(flat), bytes_accessed=2 * flat[0].size * (len(flat) + 1), transcendentals=0
        ),
        name="sum",
    )(*flat)
    return [out.reshape(-1, lanes) for out in sums] if apart else sums[0].reshape(parts, -1, lanes)


def pieces_kernel(chunk, place_ref, order_ref, left_ref, right_ref, gain_ref, out_ref, held, left_sem, sems):
    layer_count, half, size = held.shape[:3]
    first = place_ref[2] * half
    lefts = pltpu.make_async_copy(left_ref.at[:, pl.ds(first, half)], held, left_sem.at[0])
    lefts.start()
    copies = []
    turns = []
    for section in range(out_ref.shape[0]):
        row = 0
        for layer in range(layer_count):
            for inside in range(chunk):
                turns.append((layer, section * chunk + inside, section, row))
                row += size
            for inside in range(chunk):
                source = right_ref.at[layer, first + section * chunk + inside]
                copies.append((source, out_ref.at[section, pl.ds(row, size)]))
                row += size
        copies.append((gain_ref, out_ref.at[section, pl.ds(row, gain_ref.shape[0])]))
    copies = [
        pltpu.make_async_copy(source, target, sems.at[at]) for at, (source, target) in enumerate(copies)
    ]
    for copy in copies:
        copy.start()
    lefts.wait()
    for layer, block, section, row in turns:
        turned = inner_dot(held[layer, block], order_ref[...], 1, 0)
        out_ref[section, pl.ds(row, size), :] = turned.astype(jnp.bfloat16)
    for copy in copies:
        copy.wait()


def factor_pieces(place, order, left, right, gain_rows, chunk, width):
    layer_count, blocks, size = left.shape[:3]
    rows = layer_count * 2 * chunk * size + gain_rows.shape[0]
    return pl.pallas_call(
        lambda *refs: pieces_kernel(chunk, *refs),
        in_specs=[SMEM, INSIDE] + [OUTSIDE] * 3,
        out_specs=INSIDE,
        out_shape=shape_of((width, rows, size), jnp.bfloat16),
        scratch_shapes=[
            pltpu.VMEM((layer_count, blocks // 2, size, size), jnp.bfloat16),
            pltpu.SemaphoreType.DMA((1,)),
            pltpu.SemaphoreType.DMA((width * (layer_count * chunk + 1),)),
        ],
        compiler_params=pltpu.CompilerParams(vmem_limit_bytes=VMEM_LIMIT),
        cost_estimate=pl.CostEstimate(flops=left.size * size, bytes_accessed=4 * left.size, transcendentals=0),
        name="pieces",
    )(place, order, left, right, gain_rows)


def choice(pairs, critic, slots):
    rows = pairs.shape[0]
    named = (pairs[:, 0:1] == critic) | (pairs[:, 1:2] == critic)
    named = jnp.broadcast_to(named.astype(jnp.float32), (rows, slots))
    before = lax.broadcasted_iota(jnp.int32, (rows, rows), 1) < lax.broadcasted_iota(jnp.int32, (rows, rows), 0)
    rank = inner_dot(before.astype(jnp.bfloat16), named.astype(jnp.bfloat16), 1, 0)
    at = lax.broadcasted_iota(jnp.int32, (rows, slots), 1).astype(jnp.float32)
    return jnp.where(rank == at, named, 0.0).astype(jnp.bfloat16)


def pick_kernel(pairs_ref, values_ref, out_ref):
    width, features, slots = out_ref.shape
    pairs = pairs_ref[...]
    chosen = [choice(pairs, critic, slots) for critic in range(width)]
    step = 512
    for start in range(0, features, step):
        part = values_ref[:, pl.ds(start, step)]
        for k in range(width):
            out_ref[k, pl.ds(start, step), :] = inner_dot(part, chosen[k], 0, 0).astype(jnp.bfloat16)


def run_pick(pairs, values, width, slots):
    rows, features = values.shape
    return pl.pallas_call(
        pick_kernel,
        in_specs=[INSIDE] * 2,
        out_specs=INSIDE,
        out_shape=shape_of((width, features, slots), jnp.bfloat16),
        compiler_params=pltpu.CompilerParams(vmem_limit_bytes=VMEM_LIMIT),
        cost_estimate=pl.CostEstimate(
            flops=2 * rows * features * slots * width, bytes_accessed=8 * rows * features, transcendentals=0
        ),
        name="pick",
    )(pairs, values)


def combine_kernel(pairs_ref, came_ref, out_ref):
    width, features, slots = came_ref.shape
    pairs = pairs_ref[...]
    chosen = [choice(pairs, critic, slots) for critic in range(width)]
    step = 512
    for start in range(0, features, step):
        total = sum(inner_dot(chosen[k], came_ref[k, pl.ds(start, step), :], 1, 1) for k in range(width))
        out_ref[:, pl.ds(start, step)] = (0.5 * total).astype(jnp.bfloat16)


def run_combine(pairs, came):
    rows = pairs.shape[0]
    return pl.pallas_call(
        combine_kernel,
        in_specs=[INSIDE] * 2,
        out_specs=INSIDE,
        out_shape=shape_of((rows, came.shape[1]), jnp.bfloat16),
        compiler_params=pltpu.CompilerParams(vmem_limit_bytes=VMEM_LIMIT),
        cost_estimate=pl.CostEstimate(
            flops=2 * rows * came.size, bytes_accessed=4 * came.size, transcendentals=0
        ),
        name="combine",
    )(pairs, came)


FORWARD_COST = 4_000_000_000
BACKWARD_COST = 5_000_000_000


def assemble_kernel(layers, factor, place_ref, order_ref, *refs):
    count = 2 * len(layers)
    sources, (left_ref, right_ref) = refs[:count], refs[count : count + 2]
    held, wide = refs[count + 2 : 2 * count + 2], refs[2 * count + 2 : 3 * count + 2]
    in_sems, out_sems = refs[3 * count + 2 :]
    origin, core = place_ref[0] ^ place_ref[1], place_ref[2]
    order = order_ref[...]
    arrivals = [
        pltpu.make_async_copy(source, held[at], in_sems.at[at]) for at, source in enumerate(sources)
    ]
    for copy in arrivals:
        copy.start()
    leaving = []
    for at in range(count):
        arrivals[at].wait()
        half = core if at % 2 == 0 else 1 - core
        width, _, _, chunk = held[at].shape[:4]
        for k in range(width):
            start = (half * width + (origin ^ k if at < 2 else k)) * chunk
            for inside, layer in enumerate(layers[at // 2]):
                for block in range(chunk):
                    left = inner_dot(held[at][k, inside, 0, block], order, 1, 1)
                    wide[at][k, inside, 0, block] = left * factor
                wide[at][k, inside, 1] = held[at][k, inside, 1].astype(jnp.float32) * factor
                for which, target in enumerate((left_ref, right_ref)):
                    copy = pltpu.make_async_copy(
                        wide[at].at[k, inside, which],
                        target.at[layer, pl.ds(start, chunk)],
                        out_sems.at[len(leaving)],
                    )
                    copy.start()
                    leaving.append(copy)
    for copy in leaving:
        copy.wait()


def run_assemble(place, order, pieces, layers, factor):
    piece = pieces[0].shape
    layer_count = sum(len(group) for group in layers)
    out = shape_of((layer_count, 2 * piece[0] * piece[3]) + piece[4:], jnp.float32)
    return pl.pallas_call(
        lambda *refs: assemble_kernel(layers, factor, *refs),
        in_specs=[SMEM, INSIDE] + [OUTSIDE] * len(pieces),
        out_specs=[OUTSIDE] * 2,
        out_shape=[out] * 2,
        scratch_shapes=[pltpu.VMEM(part.shape, jnp.bfloat16) for part in pieces]
        + [pltpu.VMEM(part.shape, jnp.float32) for part in pieces]
        + [
            pltpu.SemaphoreType.DMA((len(pieces),)),
            pltpu.SemaphoreType.DMA((4 * layer_count * piece[0],)),
        ],
        compiler_params=pltpu.CompilerParams(vmem_limit_bytes=VMEM_LIMIT),
        cost_estimate=pl.CostEstimate(flops=0, bytes_accessed=4 * math.prod(out.shape) * 3, transcendentals=0),
        name="assemble",
    )(place, order, *pieces)


def plane_routes(width, replicas):
    bits = width.bit_length() - 1
    orders = [[(step + d) % bits for step in range(bits)] for d in range(replicas)]
    every = [(s, t, d) for s in range(width) for t in range(width) for d in range(replicas)]

    def route(move):
        def index(s, t, d):
            return (s * width + t) * replicas + d

        return [(index(*place), index(*move(*place))) for place in every]

    ranks = [[0] * width for _ in range(replicas)]
    for d in range(replicas):
        for r in range(width):
            ranks[d][sum(((r >> at) & 1) << orders[d][at] for at in range(bits))] = r
    return {
        "across": [route(lambda s, t, d, at=at: (s ^ (1 << orders[d][at]), t, d)) for at in range(bits)],
        "cores": route(lambda s, t, d: (s, t, 1 - d)),
        "sections": [route(lambda s, t, d, k=k: (s ^ k, t, d)) for k in range(width)],
        "homes": [route(lambda s, t, d, j=j: (t, t ^ s ^ j, d)) for j in range(width)],
    }, ranks


def plane_shards(patches, teacher, critic_pairs, left_factors, right_factors, norm_gains):
    width = lax.axis_size("section")
    replicas = lax.axis_size("dp")
    tok_rows, feat_local = patches.shape
    layer_count, local_blocks, size = left_factors.shape[1:4]
    blocks = feat_local * width // size
    wide = 2 * tok_rows // 3
    chunk = local_blocks // (replicas * width)
    layer_rows = 2 * chunk * size
    routes, ranks = plane_routes(width, replicas)
    section = lax.axis_index("section")
    tensor = lax.axis_index("tensor")
    core = lax.axis_index("dp")
    place = jnp.stack([section, tensor, core]).astype(jnp.int32)
    tie = lax.optimization_barrier

    def move(value, route):
        return lax.ppermute(value, AXES, route)

    def move_all(values, name):
        return [move(value, route) for value, route in zip(values, routes[name])]

    def send(values, name):
        return [values[0]] + [move(values[k], routes[name][k]) for k in range(1, width)]

    def gather_one(mine):
        return joined([mine, move(mine, routes["across"][0])])

    def gather_two(pair):
        return pair, move(pair, routes["across"][1]), move(pair, routes["cores"])

    def gather_three(pair, other, peer):
        return [pair, other, peer, move(other, routes["cores"])]

    def as_weights(parts):
        return [part.reshape(2 * width, -1, 2, chunk, size, size) for part in parts]

    block = jnp.arange(blocks, dtype=jnp.int32)
    inside = block % local_blocks
    replica = inside // (width * chunk)
    part = (replica != core).astype(jnp.int32)
    distance = section ^ ((inside // chunk) % width)
    quarter = block // local_blocks
    rank = jnp.array(ranks, jnp.int32)[replica, distance]
    table = jnp.stack(
        [
            ((part * width + index) * width + piece) * chunk + inside % chunk
            for index, piece in (
                (rank, quarter),
                (distance, quarter),
                (distance, tensor ^ section ^ distance ^ quarter),
            )
        ]
    ).astype(jnp.int32)

    def to_planes(value):
        return lax.all_to_all(value, "tensor", split_axis=0, concat_axis=0, tiled=True)

    def to_sections(value):
        return lax.all_to_all(value, "section", split_axis=0, concat_axis=0, tiled=True)

    half_layers = layer_count // 2
    groups = [tuple(range(half_layers)), tuple(range(half_layers, layer_count))]
    fold = size // blocks
    columns = jnp.arange(size)
    order = (columns[:, None] == (columns % blocks) * fold + columns // blocks).astype(jnp.bfloat16)
    gain_rows = norm_gains[0].reshape(-1, size)
    pieces = factor_pieces(place, order, left_factors[0], right_factors[0], gain_rows, chunk, width)
    pieces, patches, teacher = tie((pieces, patches, teacher))
    spread = to_sections(pieces)
    patch_sent = run_pick(critic_pairs, patches, width, wide)
    target_sent = run_pick(critic_pairs, teacher, width, wide)
    spread, patch_sent, target_sent = tie((spread, patch_sent, target_sent))
    lifted = to_planes(spread)
    lifted, patch_sent = tie((lifted, patch_sent))
    patch_came = to_planes(patch_sent).reshape(-1, wide)
    lowest = [lifted[:, group[0] * layer_rows : (group[-1] + 1) * layer_rows] for group in groups]
    beside = move(lowest[0], routes["across"][0])
    gains = lifted[:, layer_count * layer_rows :].reshape(width, layer_count + 1, local_blocks, size)
    gains = gains.transpose(1, 3, 0, 2).reshape(layer_count + 1, size, CHUNKS, blocks // CHUNKS)
    gains = gains.transpose(0, 2, 1, 3).astype(jnp.float32)
    later = (lowest[1], move(lowest[1], routes["across"][0]))
    lowest[0], beside, later, gains = tie((lowest[0], beside, later, gains))
    first_two = gather_two(joined([lowest[0], beside]))
    later = joined(list(later))
    first_two, later, patch_came = tie((first_two, later, patch_came))
    weights = [as_weights(gather_three(*first_two))]
    weights, later = tie((weights, later))

    residual, target_sent = tie((patch_came, target_sent))
    target = to_planes(target_sent).reshape(-1, wide)
    flying = gather_two(later)
    sums = jnp.zeros((8, wide), jnp.float32)
    stored = []
    for layer in range(layer_count):
        group = 0 if layer in groups[0] else 1
        following, u, z, slope, scale, sums = run_forward(
            table, gains[layer], sums, residual, weights[group], layer - groups[group][0]
        )
        stored.append(((slope, z, u), scale, residual))
        residual = following
        if layer == 0:
            residual, sums, flying = tie((residual, sums, flying))
            weights.append(as_weights(gather_three(*flying)))
        if layer == groups[0][-1]:
            residual, sums, weights[1] = tie((residual, sums, weights[1]))
        if layer == layer_count - 2:
            residual, sums, target = tie((residual, sums, target))

    def core_sum(mine, other):
        return (mine, move(other, routes["cores"]))

    def plane_sum(mine, other):
        return send(run_sum([(mine, other)], width), "sections")

    def homeward(parts):
        return move_all(run_sum(parts, width), "homes")

    def both_halves(whole):
        pair = (whole, move(whole, routes["cores"]))
        return [part.reshape(width, -1, 2, chunk, size, size) for part in pair]

    steps = (core_sum, plane_sum)
    gradient = residual
    underway = []
    for layer in range(layer_count - 1, -1, -1):
        turning = layer == layer_count - 1
        last = layer == 0
        kept, scale, inputs = stored[layer]
        group = 0 if layer in groups[0] else 1
        sources = (gradient, inputs, target) if turning else (gradient, inputs)
        underway = [(at + 1, steps[at](*state)) if at < len(steps) else (at, state) for at, state in underway]
        gradient, mine, other = run_backward(
            table,
            gains[layer],
            gains[layer_count],
            scale,
            kept,
            weights[group],
            layer - groups[group][0],
            sources,
            turning,
            last,
        )
        gradient, mine, other, states = tie((gradient, mine, other, [state for _, state in underway]))
        underway = [(at, state) for (at, _), state in zip(underway, states)]
        underway.append((0, (mine, other)))

    returned = to_planes(gradient.reshape(width, feat_local, wide))
    ended = [steps[at](*state) if at < len(steps) else state for at, state in underway][::-1]
    ended = tie(ended)
    ended[0] = plane_sum(*ended[0])
    others = to_planes(run_sum(ended[1:], width, apart=False))
    ended[0], returned, others = tie((ended[0], returned, others))
    home = homeward(ended[:1])
    d_patches = run_combine(critic_pairs, returned)
    others = to_sections(others)
    d_patches, home, others = tie((d_patches, home, others))
    homes_of = both_halves(joined(home)) + both_halves(others)
    grad_factor = 1.0 / math.sqrt(2 * tok_rows * width * replicas)
    grad_left, grad_right = run_assemble(
        place, order, homes_of, [(0,), tuple(range(1, layer_count))], grad_factor
    )
    return (d_patches, grad_left[None], grad_right[None])


def solution(mesh):
    in_specs = (
        P(("section", "dp"), "tensor"),
        P(("section", "dp"), "tensor"),
        P(("section", "dp"), None),
        P("section", None, "tensor", None, None),
        P("section", None, "tensor", None, None),
        P("section", None, "tensor"),
    )
    out_specs = (
        P(("section", "dp"), "tensor"),
        P("section", None, "tensor", None, None),
        P("section", None, "tensor", None, None),
    )
    body = plane_shards if planes_fit(mesh) else layered_shards
    return jax.shard_map(
        body, mesh=mesh, in_specs=in_specs, out_specs=out_specs, check_vma=False)
```

```python
import math

import jax
import jax.numpy as jnp
from jax import lax
from jax.experimental import pallas as pl
from jax.experimental.pallas import tpu as pltpu
from jax.sharding import PartitionSpec as P

EPSILON = 1e-06
TANH_SLOPE = 0.7978845608028654
CUBIC_TERM = 0.044715


def shifted(value, axis, steps):
    count = lax.axis_size(axis)
    first, last = (max(0, -steps), min(count, count - steps))
    return lax.ppermute(value, axis, [(source, source + steps) for source in range(first, last)])


def gelu_value(values):
    tangent = jnp.tanh(TANH_SLOPE * (values + CUBIC_TERM * values * values * values))
    return 0.5 * values * (1.0 + tangent)


def gelu_slope(values):
    tangent = jnp.tanh(TANH_SLOPE * (values + CUBIC_TERM * values * values * values))
    return 0.5 * (1.0 + tangent) + 0.5 * values * (1.0 - tangent * tangent) * TANH_SLOPE * (
        1.0 + 3.0 * CUBIC_TERM * values * values
    )


def norm_pair(residuals, gain_pair, model_width):
    squares = lax.psum(
        (
            jnp.sum(residuals[0] * residuals[0], axis=(1, 2)),
            jnp.sum(residuals[1] * residuals[1], axis=(1, 2)),
        ),
        "tensor",
    )
    factors = [lax.rsqrt(squares[member] / model_width + EPSILON) for member in range(2)]
    normed = [
        residuals[member] * factors[member][:, None, None] * gain_pair[member][None]
        for member in range(2)
    ]
    return (factors, normed)


def norm_back_pair(residuals, factors, gain_pair, grad_normed, carried, model_width):
    weighted = [grad_normed[member] * gain_pair[member][None] for member in range(2)]
    inners = lax.psum(
        (
            jnp.sum(weighted[0] * residuals[0], axis=(1, 2)),
            jnp.sum(weighted[1] * residuals[1], axis=(1, 2)),
        ),
        "tensor",
    )
    return [
        carried[member]
        + factors[member][:, None, None] * weighted[member]
        - residuals[member] * (factors[member] ** 3 * inners[member] / model_width)[:, None, None]
        for member in range(2)
    ]


def layered_shards(patches, teacher, critic_pairs, left_factors, right_factors, norm_gains):
    sections = lax.axis_size("section")
    tensor_width = lax.axis_size("tensor")
    replicas = lax.axis_size("dp")
    tok_rows = patches.shape[0]
    feat_local = patches.shape[1]
    layer_count = left_factors.shape[1]
    local_blocks = left_factors.shape[2]
    block_size = left_factors.shape[3]
    all_blocks = local_blocks * tensor_width
    fold_ratio = block_size // all_blocks
    model_width = feat_local * tensor_width
    sixth_rows = tok_rows // 6
    leading = 2 * sixth_rows
    critic_ids = jnp.arange(4, dtype=jnp.int32)
    named_by = (
        (critic_pairs[:, 0:1] == critic_ids[None, :])
        | (critic_pairs[:, 1:2] == critic_ids[None, :])
    ).astype(jnp.int32)
    ranking = jnp.cumsum(named_by, axis=0) - 1
    wide_ids = critic_ids[None, :] < 2
    slot_width = 3 * sixth_rows
    spilled = wide_ids & (ranking >= 3 * sixth_rows)
    destination = jnp.where(spilled, critic_ids[None, :] + 2, critic_ids[None, :])
    slot_index = jnp.where(spilled, ranking - sixth_rows, ranking)
    flat_slot = destination * slot_width + slot_index
    chosen = jnp.take_along_axis(flat_slot, critic_pairs, axis=1)
    slot_total = sections * slot_width
    row_ids = jnp.broadcast_to(jnp.arange(tok_rows, dtype=jnp.int32)[:, None], chosen.shape)
    source_row = (
        jnp.full((slot_total,), tok_rows, jnp.int32).at[chosen.reshape(-1)].set(row_ids.reshape(-1))
    )
    send_patch = (
        patches.at[source_row]
        .get(mode="fill", fill_value=0)
        .reshape(sections, slot_width, local_blocks, block_size)
    )
    send_target = (
        teacher.at[source_row]
        .get(mode="fill", fill_value=0)
        .reshape(sections, slot_width, local_blocks, block_size)
    )
    recv_patch, recv_target = (
        lax.all_to_all(send_patch, "section", split_axis=0, concat_axis=0, tiled=True),
        lax.all_to_all(send_target, "section", split_axis=0, concat_axis=0, tiled=True),
    )
    residuals = [
        recv_patch[:, :leading].reshape(-1, local_blocks, block_size).astype(jnp.float32),
        recv_patch[:, leading:].reshape(-1, local_blocks, block_size).astype(jnp.float32),
    ]
    targets = [
        recv_target[:, :leading].reshape(-1, local_blocks, block_size).astype(jnp.float32),
        recv_target[:, leading:].reshape(-1, local_blocks, block_size).astype(jnp.float32),
    ]
    native = (left_factors[0], right_factors[0], norm_gains[0])
    borrowed = shifted((left_factors, right_factors, norm_gains), "section", 2)
    is_wide = lax.axis_index("section") < 2
    second = (
        jnp.where(is_wide, left_factors, borrowed[0])[0],
        jnp.where(is_wide, right_factors, borrowed[1])[0],
        jnp.where(is_wide, norm_gains, borrowed[2])[0],
    )
    left_sets = (native[0], second[0])
    right_sets = (native[1], second[1])
    gain_sets = (
        native[2].astype(jnp.float32).reshape(layer_count + 1, local_blocks, block_size),
        second[2].astype(jnp.float32).reshape(layer_count + 1, local_blocks, block_size),
    )
    stored = []
    for layer_index in range(layer_count):
        gain_pair = [gain_sets[0][layer_index], gain_sets[1][layer_index]]
        factors, normed = norm_pair(residuals, gain_pair, model_width)
        normed = [normed[member].astype(jnp.bfloat16) for member in range(2)]
        first_out = [
            jnp.einsum(
                "nki,kij->nkj",
                normed[member],
                left_sets[member][layer_index],
                preferred_element_type=jnp.float32,
            ).astype(jnp.bfloat16)
            for member in range(2)
        ]
        permuted = (
            lax.all_to_all(first_out[0], "tensor", split_axis=2, concat_axis=1, tiled=True),
            lax.all_to_all(first_out[1], "tensor", split_axis=2, concat_axis=1, tiled=True),
        )
        permuted = [
            permuted[member].reshape(
                permuted[member].shape[0], all_blocks, local_blocks, fold_ratio
            )
            for member in range(2)
        ]
        right_quads = [
            right_sets[member][layer_index].reshape(
                local_blocks, fold_ratio, all_blocks, block_size
            )
            for member in range(2)
        ]
        mixture = [
            jnp.einsum(
                "nkmp,mpkl->nml",
                permuted[member],
                right_quads[member],
                preferred_element_type=jnp.float32,
            )
            for member in range(2)
        ]
        stored.append((residuals, factors, normed, permuted, mixture, right_quads, gain_pair))
        residuals = [residuals[member] + gelu_value(mixture[member]) for member in range(2)]
    final_gains = [gain_sets[0][layer_count], gain_sets[1][layer_count]]
    factors, outputs = norm_pair(residuals, final_gains, model_width)
    gradients = norm_back_pair(
        residuals,
        factors,
        final_gains,
        [outputs[member] - targets[member] for member in range(2)],
        [jnp.zeros_like(residuals[member]) for member in range(2)],
        model_width,
    )
    left_terms = []
    right_terms = []
    for layer_index in range(layer_count - 1, -1, -1):
        inputs, factors, normed, permuted, mixture, right_quads, gain_pair = stored[layer_index]
        slopes = [
            (gradients[member] * gelu_slope(mixture[member])).astype(jnp.bfloat16)
            for member in range(2)
        ]
        right_grad = [
            jnp.einsum(
                "nkmp,nml->mpkl",
                permuted[member],
                slopes[member],
                preferred_element_type=jnp.float32,
            ).reshape(local_blocks, block_size, block_size)
            for member in range(2)
        ]
        back_moved = [
            jnp.einsum(
                "nml,mpkl->nkmp",
                slopes[member],
                right_quads[member],
                preferred_element_type=jnp.float32,
            )
            .astype(jnp.bfloat16)
            .reshape(slopes[member].shape[0], all_blocks, local_blocks * fold_ratio)
            for member in range(2)
        ]
        arrived = (
            lax.all_to_all(back_moved[0], "tensor", split_axis=1, concat_axis=2, tiled=True),
            lax.all_to_all(back_moved[1], "tensor", split_axis=1, concat_axis=2, tiled=True),
        )
        left_grad = [
            jnp.einsum(
                "nki,nkj->kij", normed[member], arrived[member], preferred_element_type=jnp.float32
            )
            for member in range(2)
        ]
        grad_normed = [
            jnp.einsum(
                "nkj,kij->nki",
                arrived[member],
                left_sets[member][layer_index],
                preferred_element_type=jnp.float32,
            )
            for member in range(2)
        ]
        gradients = norm_back_pair(inputs, factors, gain_pair, grad_normed, gradients, model_width)
        layer_left = jnp.stack(left_grad)
        layer_right = jnp.stack(right_grad)
        layer_left, layer_right = (
            lax.psum(layer_left.astype(jnp.bfloat16), "dp").astype(jnp.float32),
            lax.psum(layer_right.astype(jnp.bfloat16), "dp").astype(jnp.float32),
        )
        left_terms.insert(0, layer_left)
        right_terms.insert(0, layer_right)
    left_stack = jnp.stack(left_terms)
    right_stack = jnp.stack(right_terms)
    repaid = (
        shifted(left_stack[:, 1].astype(jnp.bfloat16), "section", -2).astype(jnp.float32),
        shifted(right_stack[:, 1].astype(jnp.bfloat16), "section", -2).astype(jnp.float32),
    )
    is_wide = lax.axis_index("section") < 2
    left_total = left_stack[:, 0] + jnp.where(is_wide, left_stack[:, 1] + repaid[0], 0.0)
    right_total = right_stack[:, 0] + jnp.where(is_wide, right_stack[:, 1] + repaid[1], 0.0)
    grad_factor = 1.0 / math.sqrt(2 * tok_rows * sections * replicas)
    returned = [
        gradients[member].astype(jnp.bfloat16).reshape(sections, -1, local_blocks, block_size)
        for member in range(2)
    ]
    back_lead, back_trail = (
        lax.all_to_all(returned[0], "section", split_axis=0, concat_axis=0, tiled=True),
        lax.all_to_all(returned[1], "section", split_axis=0, concat_axis=0, tiled=True),
    )
    gathered = jnp.concatenate((back_lead, back_trail), axis=1).reshape(
        slot_total, local_blocks, block_size
    )
    combined = (
        gathered[chosen[:, 0]].astype(jnp.float32) + gathered[chosen[:, 1]].astype(jnp.float32)
    ) * 0.5
    d_patches = combined.astype(jnp.bfloat16).reshape(tok_rows, feat_local)
    return (d_patches, (left_total * grad_factor)[None], (right_total * grad_factor)[None])


VMEM_LIMIT = 60 * 1024 * 1024
CHUNKS = 8
TOGETHER = 4
PARTS = 4
SMALL = (16, 128)
AXES = ("section", "tensor", "dp")


def planes_fit(mesh):
    sections = mesh.shape["section"]
    paired = mesh.shape["dp"] == 2 and sections & (sections - 1) == 0
    return paired and mesh.shape["tensor"] == sections


def inner_dot(left, right, left_dim, right_dim):
    return lax.dot_general(
        left,
        right,
        (((left_dim,), (right_dim,)), ((), ())),
        preferred_element_type=jnp.float32,
    )


def fold_rows(values):
    return jnp.sum(values.reshape(values.shape[0] // 8, 8, values.shape[1]), axis=0)


def block_rows(block, size):
    return pl.ds(pl.multiple_of(block * size, size), size)


def column(gain_ref, block, at, slots):
    if len(gain_ref.shape) == 3:
        gains = gain_ref[block // gain_ref.shape[2]]
        return jnp.broadcast_to(gains[:, at : at + 1], (gains.shape[0], slots))
    picked = lax.broadcasted_iota(jnp.int32, (gain_ref.shape[1], slots), 0) == block
    return inner_dot(gain_ref[...], picked.astype(jnp.bfloat16), 1, 0)


def chunk_copy(source, target, sems, chunk):
    rows = target.shape[0] // CHUNKS
    at = pl.ds(pl.multiple_of(chunk * rows, rows), rows)
    return pltpu.make_async_copy(source.at[at], target.at[at], sems.at[chunk])


def start_chunks(source, target, sems):
    for chunk in range(CHUNKS):
        chunk_copy(source, target, sems, chunk).start()


def wait_chunks(source, target, sems):
    for chunk in range(CHUNKS):
        chunk_copy(source, target, sems, chunk).wait()


def factor_copies(parts, layer, held, sems, side):
    count = parts[0].shape[0]
    return [
        pltpu.make_async_copy(
            ref.at[:, layer, side], held.at[pl.ds(at * count, count), side], sems.at[side, at]
        )
        for at, ref in enumerate(parts)
    ]


def gradient_copies(held, parts, sems, side):
    count = parts[0].shape[0]
    return [
        pltpu.make_async_copy(
            held.at[pl.ds(at * count, count), side], ref.at[:, side], sems.at[side, at]
        )
        for at, ref in enumerate(parts)
    ]


def by_chunk(blocks, step, carry, before=None, after=None):
    per_chunk = blocks // CHUNKS

    def few(start, first, carry):
        stores = []
        for at in range(TOGETHER):
            made, carry = step(start + at, first + at, carry)
            stores += made
        for ref, index, value in stores:
            ref[index] = value
        return carry

    def one(chunk, carry):
        if before is not None:
            before(chunk)
        for at in range(0, per_chunk, TOGETHER):
            carry = few(chunk * per_chunk + at, at, carry)
        if after is not None:
            after(chunk)
        return carry

    return lax.fori_loop(0, CHUNKS, one, carry)


def forward_kernel(first, layer, inputs, table_ref, sums_ref, gain_ref, *refs):
    sources, refs = refs[:inputs], refs[inputs:]
    parts, sources = sources[:PARTS], sources[PARTS:]
    out_ref, u_ref, z_ref, slope_ref, scale_ref, next_ref = refs[:6]
    raw, h, w, u, z, slope, mid, in_sems, w_sems, out_sems = refs[6:]
    features, slots = h.shape
    size = w.shape[-1]
    chunk_blocks = w.shape[2]
    blocks = features // size
    fold = size // blocks

    left_in = factor_copies(parts, layer, w, w_sems, 0)
    right_in = factor_copies(parts, layer, w, w_sems, 1)
    if first:
        start_chunks(sources[0], raw, in_sems)
        for copy in left_in + right_in:
            copy.start()

        def squares(block, _, total):
            rows = block_rows(block, size)
            part = raw[rows, :].astype(jnp.float32)
            return [(h, (rows, slice(None)), part)], total + fold_rows(part * part)

        total = by_chunk(
            blocks,
            squares,
            jnp.zeros((8, slots), jnp.float32),
            lambda chunk: chunk_copy(sources[0], raw, in_sems, chunk).wait(),
        )
    else:
        for copy in left_in:
            copy.start()
        start_chunks(sources[0], h, in_sems)
        for copy in right_in:
            copy.start()
        total = sums_ref[...]
    scale = lax.rsqrt(jnp.sum(total, axis=0, keepdims=True) / features + EPSILON)
    scale_ref[...] = jnp.broadcast_to(scale, scale_ref.shape)
    for copy in left_in:
        copy.wait()

    def arrive(chunk):
        if not first:
            chunk_copy(sources[0], h, in_sems, chunk).wait()

    def left(block, nth, carry):
        rows = block_rows(block, size)
        place = table_ref[0, block]
        normed = (h[rows, :] * scale * column(gain_ref, block, nth, slots)).astype(jnp.bfloat16)
        weight = w[place // chunk_blocks, 0, place % chunk_blocks]
        first_out = inner_dot(weight, normed, 0, 0)
        at = (rows, slice(None))
        return [(u, at, normed), (mid, at, first_out)], carry

    def leave_left(chunk):
        chunk_copy(u, u_ref, out_sems.at[0], chunk).start()

    by_chunk(blocks, left, 0, arrive, leave_left)
    for copy in right_in:
        copy.wait()

    def right(block, nth, total):
        rows = block_rows(block, size)
        place = table_ref[0, block]
        moved = [mid[pl.ds(q * blocks + block, blocks, stride=size), :] for q in range(fold)]
        moved = jnp.concatenate(moved, axis=0).astype(jnp.bfloat16)
        weight = w[place // chunk_blocks, 1, place % chunk_blocks]
        mixture = inner_dot(weight, moved, 0, 0)
        squared = mixture * mixture
        tangent = jnp.tanh(mixture * (TANH_SLOPE + (TANH_SLOPE * CUBIC_TERM) * squared))
        half = 0.5 + 0.5 * tangent
        following = h[rows, :] + mixture * half
        steep = half + mixture * (1.0 - tangent * tangent) * (
            0.5 * TANH_SLOPE + (1.5 * TANH_SLOPE * CUBIC_TERM) * squared
        )
        at = (rows, slice(None))
        stores = [(z, at, moved), (h, at, following), (slope, at, steep.astype(jnp.bfloat16))]
        return stores, total + fold_rows(following * following)

    leaving = ((h, out_ref, 1), (z, z_ref, 2), (slope, slope_ref, 3))

    def leave_right(chunk):
        for source, target, at in leaving:
            chunk_copy(source, target, out_sems.at[at], chunk).start()

    next_ref[...] = by_chunk(blocks, right, jnp.zeros((8, slots), jnp.float32), None, leave_right)
    for source, target, at in ((u, u_ref, 0),) + leaving:
        wait_chunks(source, target, out_sems.at[at])


def backward_kernel(turning, last, layer, inputs, table_ref, scale_ref, gain_ref, end_gain_ref, *refs):
    sources, refs = refs[:inputs], refs[inputs:]
    slope_ref, z_ref, u_ref = sources[:3]
    parts, sources = sources[3 : 3 + PARTS], sources[3 + PARTS :]
    out_ref, own_grad, peer_grad = refs[:3]
    g, slope, z, u, h, w, gw, mid, top, goal = refs[3:13]
    in_sems, w_sems, out_sems, gw_sems = refs[13:]
    features, slots = g.shape
    size = w.shape[-1]
    chunk_blocks = w.shape[2]
    blocks = features // size
    fold = size // blocks

    left_in = factor_copies(parts, layer, w, w_sems, 0)
    right_in = factor_copies(parts, layer, w, w_sems, 1)
    g_ref, h_ref = sources[:2]
    if turning:
        for chunk in range(CHUNKS):
            chunk_copy(g_ref, top, in_sems.at[0], chunk).start()
            chunk_copy(sources[2], goal, in_sems.at[5], chunk).start()
    for copy in right_in:
        copy.start()
    for chunk in range(CHUNKS):
        if not turning:
            chunk_copy(g_ref, g, in_sems.at[0], chunk).start()
        chunk_copy(slope_ref, slope, in_sems.at[1], chunk).start()
        chunk_copy(z_ref, z, in_sems.at[2], chunk).start()
    for copy in left_in:
        copy.start()
    for chunk in range(CHUNKS):
        chunk_copy(u_ref, u, in_sems.at[3], chunk).start()
        chunk_copy(h_ref, h, in_sems.at[4], chunk).start()

    if turning:
        zero = jnp.zeros((8, slots), jnp.float32)

        def sums(block, nth, totals):
            rows = block_rows(block, size)
            part = top[rows, :]
            scaled = part * column(end_gain_ref, block, nth, slots)
            return [], (
                totals[0] + fold_rows(part * part),
                totals[1] + fold_rows(scaled * scaled),
                totals[2] + fold_rows(scaled * goal[rows, :].astype(jnp.float32)),
            )

        def arrive_top(chunk):
            chunk_copy(g_ref, top, in_sems.at[0], chunk).wait()
            chunk_copy(sources[2], goal, in_sems.at[5], chunk).wait()

        totals = by_chunk(blocks, sums, (zero, zero, zero), arrive_top)
        squares, gained, crossed = [jnp.sum(total, axis=0, keepdims=True) for total in totals]
        end_scale = lax.rsqrt(squares / features + EPSILON)
        end_back = end_scale * end_scale * end_scale * (end_scale * gained - crossed) / features

    for copy in right_in:
        copy.wait()

    def arrive_right(chunk):
        if not turning:
            chunk_copy(g_ref, g, in_sems.at[0], chunk).wait()
        chunk_copy(slope_ref, slope, in_sems.at[1], chunk).wait()
        chunk_copy(z_ref, z, in_sems.at[2], chunk).wait()

    def right(block, nth, total):
        rows = block_rows(block, size)
        place, home = table_ref[0, block], table_ref[2 if last else 1, block]
        at = (place // chunk_blocks, 1, place % chunk_blocks)
        to = (home // chunk_blocks, 1, home % chunk_blocks)
        if turning:
            part = top[rows, :]
            factor = column(end_gain_ref, block, nth, slots)
            error = (part * end_scale * factor - goal[rows, :].astype(jnp.float32)) * factor
            gradient = end_scale * error - part * end_back
            stores = [(g, (rows, slice(None)), gradient)]
        else:
            gradient = g[rows, :]
            stores = []
        steep = (gradient * slope[rows, :].astype(jnp.float32)).astype(jnp.bfloat16)
        taken = z[rows, :]
        back = inner_dot(w[at], steep, 1, 0)
        stores.append((gw, to, inner_dot(taken, steep, 1, 1).astype(jnp.bfloat16)))
        stores.append((mid, (rows, slice(None)), back))
        return stores, total + fold_rows(taken.astype(jnp.float32) * back)

    total = by_chunk(blocks, right, jnp.zeros((8, slots), jnp.float32), arrive_right)
    right_out = gradient_copies(gw, (own_grad, peer_grad), gw_sems, 1)
    for copy in right_out:
        copy.start()
    for copy in left_in:
        copy.wait()
    scale = scale_ref[0:1, :]
    back = scale * scale * jnp.sum(total, axis=0, keepdims=True) / features

    def arrive_left(chunk):
        chunk_copy(u_ref, u, in_sems.at[3], chunk).wait()
        chunk_copy(h_ref, h, in_sems.at[4], chunk).wait()

    def left(block, nth, carry):
        rows = block_rows(block, size)
        place, home = table_ref[0, block], table_ref[2 if last else 1, block]
        at = (place // chunk_blocks, 0, place % chunk_blocks)
        to = (home // chunk_blocks, 0, home % chunk_blocks)
        arrived = [mid[pl.ds(q * blocks + block, blocks, stride=size), :] for q in range(fold)]
        arrived = jnp.concatenate(arrived, axis=0).astype(jnp.bfloat16)
        factor_grad = inner_dot(u[rows, :], arrived, 1, 1).astype(jnp.bfloat16)
        weighted = inner_dot(w[at], arrived, 1, 0) * column(gain_ref, block, nth, slots)
        ended = g[rows, :] + scale * weighted - h[rows, :].astype(jnp.float32) * back
        index = (rows, slice(None))
        stores = [(gw, to, factor_grad)]
        stores.append((u, index, ended.astype(jnp.bfloat16)) if last else (g, index, ended))
        return stores, carry

    ended = u if last else g
    by_chunk(
        blocks, left, 0, arrive_left, lambda chunk: chunk_copy(ended, out_ref, out_sems, chunk).start()
    )
    left_out = gradient_copies(gw, (own_grad, peer_grad), gw_sems, 0)
    for copy in left_out:
        copy.start()
    wait_chunks(ended, out_ref, out_sems)
    for copy in right_out + left_out:
        copy.wait()


def shape_of(shape, dtype):
    return jax.ShapeDtypeStruct(shape, dtype)


SMEM = pl.BlockSpec(memory_space=pltpu.SMEM)
INSIDE = pl.BlockSpec(memory_space=pltpu.VMEM)
OUTSIDE = pl.BlockSpec(memory_space=pl.ANY)


def run_forward(table, gain, sums, residual, weights, layer):
    first = residual.dtype == jnp.bfloat16
    whole = residual.shape
    sources = (*weights, residual)
    held = (PARTS * weights[0].shape[0],) + weights[0].shape[2:]
    out_shape = (
        shape_of(whole, jnp.float32),
        shape_of(whole, jnp.bfloat16),
        shape_of(whole, jnp.bfloat16),
        shape_of(whole, jnp.bfloat16),
        shape_of((8, whole[1]), jnp.float32),
        shape_of((8, whole[1]), jnp.float32),
    )
    return pl.pallas_call(
        lambda *refs: forward_kernel(first, layer, len(sources), *refs),
        in_specs=[SMEM, INSIDE, INSIDE] + [OUTSIDE] * len(sources),
        out_specs=[OUTSIDE] * 4 + [INSIDE] * 2,
        out_shape=out_shape,
        scratch_shapes=[
            pltpu.VMEM(whole if first else SMALL, jnp.bfloat16),
            pltpu.VMEM(whole, jnp.float32),
            pltpu.VMEM(held, jnp.bfloat16),
            pltpu.VMEM(whole, jnp.bfloat16),
            pltpu.VMEM(whole, jnp.bfloat16),
            pltpu.VMEM(whole, jnp.bfloat16),
            pltpu.VMEM(whole, jnp.float32),
            pltpu.SemaphoreType.DMA((CHUNKS,)),
            pltpu.SemaphoreType.DMA((2, PARTS)),
            pltpu.SemaphoreType.DMA((4, CHUNKS)),
        ],
        compiler_params=pltpu.CompilerParams(vmem_limit_bytes=VMEM_LIMIT),
        cost_estimate=pl.CostEstimate(
            flops=FORWARD_COST, bytes_accessed=20 * whole[0] * whole[1], transcendentals=0
        ),
        name="forward_layer",
    )(table, sums, gain, *sources)


def run_backward(table, gain, end_gain, scale, kept, weights, layer, sources, turning, last):
    whole = kept[0].shape
    sources = (*kept, *weights, *sources)
    held = (PARTS * weights[0].shape[0],) + weights[0].shape[2:]
    half = (held[0] // 2,) + held[1:]
    out_shape = [shape_of(whole, jnp.bfloat16 if last else jnp.float32)] + [shape_of(half, jnp.bfloat16)] * 2
    return pl.pallas_call(
        lambda *refs: backward_kernel(turning, last, layer, len(sources), *refs),
        in_specs=[SMEM] + [INSIDE] * 3 + [OUTSIDE] * len(sources),
        out_specs=[OUTSIDE] * len(out_shape),
        out_shape=out_shape,
        scratch_shapes=[
            pltpu.VMEM(whole, jnp.float32),
            pltpu.VMEM(whole, jnp.bfloat16),
            pltpu.VMEM(whole, jnp.bfloat16),
            pltpu.VMEM(whole, jnp.bfloat16),
            pltpu.VMEM(whole, jnp.bfloat16 if last else jnp.float32),
            pltpu.VMEM(held, jnp.bfloat16),
            pltpu.VMEM(held, jnp.bfloat16),
            pltpu.VMEM(whole, jnp.float32),
            pltpu.VMEM(whole if turning else SMALL, jnp.float32),
            pltpu.VMEM(whole if turning else SMALL, jnp.bfloat16),
            pltpu.SemaphoreType.DMA((6, CHUNKS)),
            pltpu.SemaphoreType.DMA((2, PARTS)),
            pltpu.SemaphoreType.DMA((CHUNKS,)),
            pltpu.SemaphoreType.DMA((2, PARTS)),
        ],
        compiler_params=pltpu.CompilerParams(vmem_limit_bytes=VMEM_LIMIT),
        cost_estimate=pl.CostEstimate(
            flops=BACKWARD_COST, bytes_accessed=30 * whole[0] * whole[1], transcendentals=0
        ),
        name="backward_layer",
    )(table, scale, gain, end_gain, *sources)


def join_kernel(rows, *refs):
    sources, whole, sems = refs[:-2], refs[-2], refs[-1]
    copies = [
        pltpu.make_async_copy(source.at[pl.ds(0, rows)], whole.at[pl.ds(at * rows, rows)], sems.at[at])
        for at, source in enumerate(sources)
    ]
    for copy in copies:
        copy.start()
    for copy in copies:
        copy.wait()


def joined(parts, rows=None):
    rows = parts[0].shape[0] if rows is None else rows
    whole = shape_of((rows * len(parts),) + parts[0].shape[1:], parts[0].dtype)
    return pl.pallas_call(
        lambda *refs: join_kernel(rows, *refs),
        in_specs=[OUTSIDE] * len(parts),
        out_specs=INSIDE,
        out_shape=whole,
        scratch_shapes=[pltpu.SemaphoreType.DMA((len(parts),))],
        compiler_params=pltpu.CompilerParams(vmem_limit_bytes=VMEM_LIMIT),
        cost_estimate=pl.CostEstimate(
            flops=0, bytes_accessed=4 * math.prod(whole.shape), transcendentals=0
        ),
        name="join",
    )(*parts)


def order_kernel(ranges, place_ref, *refs):
    sources, whole, sems = refs[:-2], refs[-2], refs[-1]
    copies = []
    for distance, source in enumerate(sources):
        row = 0
        for start, count in ranges:
            target = whole.at[place_ref[0] ^ distance, pl.ds(row, count)]
            copies.append(pltpu.make_async_copy(source.at[pl.ds(start, count)], target, sems.at[len(copies)]))
            row += count
    for copy in copies:
        copy.start()
    for copy in copies:
        copy.wait()


def by_section(place, parts, ranges):
    rows = sum(count for _, count in ranges)
    whole = shape_of((len(parts), rows) + parts[0].shape[1:], parts[0].dtype)
    return pl.pallas_call(
        lambda *refs: order_kernel(ranges, *refs),
        in_specs=[SMEM] + [OUTSIDE] * len(parts),
        out_specs=INSIDE,
        out_shape=whole,
        scratch_shapes=[pltpu.SemaphoreType.DMA((len(parts) * len(ranges),))],
        compiler_params=pltpu.CompilerParams(vmem_limit_bytes=VMEM_LIMIT),
        cost_estimate=pl.CostEstimate(
            flops=0, bytes_accessed=4 * math.prod(whole.shape), transcendentals=0
        ),
        name="by_section",
    )(place, *parts)


def sum_kernel(terms, inputs, *refs):
    sources, outs = refs[:inputs], refs[inputs:]
    for group in range(inputs // terms):
        mine = sources[group * terms : (group + 1) * terms]
        for at in range(mine[0].shape[0]):
            total = sum(ref[at].astype(jnp.float32) for ref in mine).astype(jnp.bfloat16)
            if len(outs) > 1:
                outs[at][group] = total
            else:
                outs[0][at, group] = total


def run_sum(groups, parts, apart=True):
    flat = [term.reshape(parts, -1, term.shape[-1]) for terms in groups for term in terms]
    _, rows, lanes = flat[0].shape
    steps = 2
    if apart:
        out_shape = [shape_of((len(groups), rows, lanes), jnp.bfloat16)] * parts
        out_specs = [pl.BlockSpec((len(groups), rows // steps, lanes), lambda i: (0, i, 0))] * parts
    else:
        out_shape = [shape_of((parts, len(groups), rows, lanes), jnp.bfloat16)]
        out_specs = [pl.BlockSpec((parts, len(groups), rows // steps, lanes), lambda i: (0, 0, i, 0))]
    sums = pl.pallas_call(
        lambda *refs: sum_kernel(len(groups[0]), len(flat), *refs),
        grid=(steps,),
        in_specs=[pl.BlockSpec((parts, rows // steps, lanes), lambda i: (0, i, 0))] * len(flat),
        out_specs=out_specs,
        out_shape=out_shape,
        compiler_params=pltpu.CompilerParams(vmem_limit_bytes=VMEM_LIMIT),
        cost_estimate=pl.CostEstimate(
            flops=flat[0].size * len(flat), bytes_accessed=2 * flat[0].size * (len(flat) + 1), transcendentals=0
        ),
        name="sum",
    )(*flat)
    return [out.reshape(-1, lanes) for out in sums] if apart else sums[0].reshape(parts, -1, lanes)


def pieces_kernel(chunk, place_ref, order_ref, left_ref, right_ref, gain_ref, *refs):
    outs, (held, left_sem, sems) = refs[:-3], refs[-3:]
    layer_count, half, size = held.shape[:3]
    first = place_ref[2] * half
    lefts = pltpu.make_async_copy(left_ref.at[:, pl.ds(first, half)], held, left_sem.at[0])
    lefts.start()
    copies = []
    turns = []
    for distance, out in enumerate(outs):
        start = (place_ref[0] ^ distance) * chunk
        row = 0
        for layer in range(layer_count):
            for inside in range(chunk):
                turns.append((layer, start + inside, out, row))
                row += size
            for inside in range(chunk):
                source = right_ref.at[layer, first + start + inside]
                copies.append((source, out.at[pl.ds(row, size)]))
                row += size
        copies.append((gain_ref, out.at[pl.ds(row, gain_ref.shape[0])]))
    copies = [
        pltpu.make_async_copy(source, target, sems.at[at]) for at, (source, target) in enumerate(copies)
    ]
    for copy in copies:
        copy.start()
    lefts.wait()
    for layer, block, out, row in turns:
        turned = inner_dot(held[layer, block], order_ref[...], 1, 0)
        out[pl.ds(row, size), :] = turned.astype(jnp.bfloat16)
    for copy in copies:
        copy.wait()


def factor_pieces(place, order, left, right, gain_rows, chunk, width):
    layer_count, blocks, size = left.shape[:3]
    rows = layer_count * 2 * chunk * size + gain_rows.shape[0]
    return pl.pallas_call(
        lambda *refs: pieces_kernel(chunk, *refs),
        in_specs=[SMEM, INSIDE] + [OUTSIDE] * 3,
        out_specs=[INSIDE] * width,
        out_shape=[shape_of((rows, size), jnp.bfloat16)] * width,
        scratch_shapes=[
            pltpu.VMEM((layer_count, blocks // 2, size, size), jnp.bfloat16),
            pltpu.SemaphoreType.DMA((1,)),
            pltpu.SemaphoreType.DMA((width * (layer_count * chunk + 1),)),
        ],
        compiler_params=pltpu.CompilerParams(vmem_limit_bytes=VMEM_LIMIT),
        cost_estimate=pl.CostEstimate(flops=left.size * size, bytes_accessed=4 * left.size, transcendentals=0),
        name="pieces",
    )(place, order, left, right, gain_rows)


def choice(pairs, critic, slots):
    rows = pairs.shape[0]
    named = (pairs[:, 0:1] == critic) | (pairs[:, 1:2] == critic)
    named = jnp.broadcast_to(named.astype(jnp.float32), (rows, slots))
    before = lax.broadcasted_iota(jnp.int32, (rows, rows), 1) < lax.broadcasted_iota(jnp.int32, (rows, rows), 0)
    rank = inner_dot(before.astype(jnp.bfloat16), named.astype(jnp.bfloat16), 1, 0)
    at = lax.broadcasted_iota(jnp.int32, (rows, slots), 1).astype(jnp.float32)
    return jnp.where(rank == at, named, 0.0).astype(jnp.bfloat16)


def pick_kernel(pairs_ref, values_ref, out_ref):
    width, features, slots = out_ref.shape
    pairs = pairs_ref[...]
    chosen = [choice(pairs, critic, slots) for critic in range(width)]
    step = 512
    for start in range(0, features, step):
        part = values_ref[:, pl.ds(start, step)]
        for k in range(width):
            out_ref[k, pl.ds(start, step), :] = inner_dot(part, chosen[k], 0, 0).astype(jnp.bfloat16)


def run_pick(pairs, values, width, slots):
    rows, features = values.shape
    return pl.pallas_call(
        pick_kernel,
        in_specs=[INSIDE] * 2,
        out_specs=INSIDE,
        out_shape=shape_of((width, features, slots), jnp.bfloat16),
        compiler_params=pltpu.CompilerParams(vmem_limit_bytes=VMEM_LIMIT),
        cost_estimate=pl.CostEstimate(
            flops=2 * rows * features * slots * width, bytes_accessed=8 * rows * features, transcendentals=0
        ),
        name="pick",
    )(pairs, values)


def combine_kernel(pairs_ref, came_ref, out_ref):
    width, features, slots = came_ref.shape
    pairs = pairs_ref[...]
    chosen = [choice(pairs, critic, slots) for critic in range(width)]
    step = 512
    for start in range(0, features, step):
        total = sum(inner_dot(chosen[k], came_ref[k, pl.ds(start, step), :], 1, 1) for k in range(width))
        out_ref[:, pl.ds(start, step)] = (0.5 * total).astype(jnp.bfloat16)


def run_combine(pairs, came):
    rows = pairs.shape[0]
    return pl.pallas_call(
        combine_kernel,
        in_specs=[INSIDE] * 2,
        out_specs=INSIDE,
        out_shape=shape_of((rows, came.shape[1]), jnp.bfloat16),
        compiler_params=pltpu.CompilerParams(vmem_limit_bytes=VMEM_LIMIT),
        cost_estimate=pl.CostEstimate(
            flops=2 * rows * came.size, bytes_accessed=4 * came.size, transcendentals=0
        ),
        name="combine",
    )(pairs, came)


FORWARD_COST = 4_000_000_000
BACKWARD_COST = 5_000_000_000


def assemble_kernel(layers, factor, place_ref, order_ref, *refs):
    count = 2 * len(layers)
    sources, (left_ref, right_ref) = refs[:count], refs[count : count + 2]
    held, wide = refs[count + 2 : 2 * count + 2], refs[2 * count + 2 : 3 * count + 2]
    in_sems, out_sems = refs[3 * count + 2 :]
    origin, core = place_ref[0] ^ place_ref[1], place_ref[2]
    order = order_ref[...]
    arrivals = [
        pltpu.make_async_copy(source, held[at], in_sems.at[at]) for at, source in enumerate(sources)
    ]
    for copy in arrivals:
        copy.start()
    leaving = []
    for at in range(count):
        arrivals[at].wait()
        half = core if at % 2 == 0 else 1 - core
        width, _, _, chunk = held[at].shape[:4]
        for k in range(width):
            start = (half * width + (origin ^ k if at < 2 else k)) * chunk
            for inside, layer in enumerate(layers[at // 2]):
                for block in range(chunk):
                    left = inner_dot(held[at][k, inside, 0, block], order, 1, 1)
                    wide[at][k, inside, 0, block] = left * factor
                wide[at][k, inside, 1] = held[at][k, inside, 1].astype(jnp.float32) * factor
                for which, target in enumerate((left_ref, right_ref)):
                    copy = pltpu.make_async_copy(
                        wide[at].at[k, inside, which],
                        target.at[layer, pl.ds(start, chunk)],
                        out_sems.at[len(leaving)],
                    )
                    copy.start()
                    leaving.append(copy)
    for copy in leaving:
        copy.wait()


def run_assemble(place, order, pieces, layers, factor):
    piece = pieces[0].shape
    layer_count = sum(len(group) for group in layers)
    out = shape_of((layer_count, 2 * piece[0] * piece[3]) + piece[4:], jnp.float32)
    return pl.pallas_call(
        lambda *refs: assemble_kernel(layers, factor, *refs),
        in_specs=[SMEM, INSIDE] + [OUTSIDE] * len(pieces),
        out_specs=[OUTSIDE] * 2,
        out_shape=[out] * 2,
        scratch_shapes=[pltpu.VMEM(part.shape, jnp.bfloat16) for part in pieces]
        + [pltpu.VMEM(part.shape, jnp.float32) for part in pieces]
        + [
            pltpu.SemaphoreType.DMA((len(pieces),)),
            pltpu.SemaphoreType.DMA((4 * layer_count * piece[0],)),
        ],
        compiler_params=pltpu.CompilerParams(vmem_limit_bytes=VMEM_LIMIT),
        cost_estimate=pl.CostEstimate(flops=0, bytes_accessed=4 * math.prod(out.shape) * 3, transcendentals=0),
        name="assemble",
    )(place, order, *pieces)


def plane_routes(width, replicas):
    bits = width.bit_length() - 1
    orders = [[(step + d) % bits for step in range(bits)] for d in range(replicas)]
    every = [(s, t, d) for s in range(width) for t in range(width) for d in range(replicas)]

    def route(move):
        def index(s, t, d):
            return (s * width + t) * replicas + d

        return [(index(*place), index(*move(*place))) for place in every]

    ranks = [[0] * width for _ in range(replicas)]
    for d in range(replicas):
        for r in range(width):
            ranks[d][sum(((r >> at) & 1) << orders[d][at] for at in range(bits))] = r
    return {
        "across": [route(lambda s, t, d, at=at: (s ^ (1 << orders[d][at]), t, d)) for at in range(bits)],
        "cores": route(lambda s, t, d: (s, t, 1 - d)),
        "sections": [route(lambda s, t, d, k=k: (s ^ k, t, d)) for k in range(width)],
        "homes": [route(lambda s, t, d, j=j: (t, t ^ s ^ j, d)) for j in range(width)],
    }, ranks


def plane_shards(patches, teacher, critic_pairs, left_factors, right_factors, norm_gains):
    width = lax.axis_size("section")
    replicas = lax.axis_size("dp")
    tok_rows, feat_local = patches.shape
    layer_count, local_blocks, size = left_factors.shape[1:4]
    blocks = feat_local * width // size
    wide = 2 * tok_rows // 3
    chunk = local_blocks // (replicas * width)
    layer_rows = 2 * chunk * size
    routes, ranks = plane_routes(width, replicas)
    section = lax.axis_index("section")
    tensor = lax.axis_index("tensor")
    core = lax.axis_index("dp")
    place = jnp.stack([section, tensor, core]).astype(jnp.int32)
    tie = lax.optimization_barrier

    def move(value, route):
        return lax.ppermute(value, AXES, route)

    def move_all(values, name):
        return [move(value, route) for value, route in zip(values, routes[name])]

    def send(values, name):
        return [values[0]] + [move(values[k], routes[name][k]) for k in range(1, width)]

    def gather_one(mine):
        return joined([mine, move(mine, routes["across"][0])])

    def gather_two(pair):
        return pair, move(pair, routes["across"][1]), move(pair, routes["cores"])

    def gather_three(pair, other, peer):
        return [pair, other, peer, move(other, routes["cores"])]

    def as_weights(parts):
        return [part.reshape(2 * width, -1, 2, chunk, size, size) for part in parts]

    block = jnp.arange(blocks, dtype=jnp.int32)
    inside = block % local_blocks
    replica = inside // (width * chunk)
    part = (replica != core).astype(jnp.int32)
    distance = section ^ ((inside // chunk) % width)
    quarter = block // local_blocks
    rank = jnp.array(ranks, jnp.int32)[replica, distance]
    table = jnp.stack(
        [
            ((part * width + index) * width + piece) * chunk + inside % chunk
            for index, piece in (
                (rank, quarter),
                (distance, quarter),
                (distance, tensor ^ section ^ distance ^ quarter),
            )
        ]
    ).astype(jnp.int32)

    def to_planes(value):
        return lax.all_to_all(value, "tensor", split_axis=0, concat_axis=0, tiled=True)

    def to_sections(value):
        return lax.all_to_all(value, "section", split_axis=0, concat_axis=0, tiled=True)

    half_layers = layer_count // 2
    groups = [tuple(range(half_layers)), tuple(range(half_layers, layer_count))]
    fold = size // blocks
    columns = jnp.arange(size)
    order = (columns[:, None] == (columns % blocks) * fold + columns // blocks).astype(jnp.bfloat16)
    gain_rows = norm_gains[0].reshape(-1, size)
    patch_sent = run_pick(critic_pairs, patches, width, wide)
    patch_sent, left, right, teacher = tie((patch_sent, left_factors[0], right_factors[0], teacher))
    patch_came = to_planes(patch_sent).reshape(-1, wide)
    pieces = factor_pieces(place, order, left, right, gain_rows, chunk, width)
    spread = send(pieces, "sections")
    cut, end = half_layers * layer_rows, layer_count * layer_rows
    first = by_section(place, spread, [(0, cut), (end, gain_rows.shape[0])])
    second = by_section(place, spread, [(cut, end - cut)])
    target_sent = run_pick(critic_pairs, teacher, width, wide)
    patch_came, first, second, target_sent = tie((patch_came, first, second, target_sent))
    first = to_planes(first)
    first, second = tie((first, second))
    second = to_planes(second)
    lowest = first[:, :cut]
    beside = move(lowest, routes["across"][0])
    gains = first[:, cut:].reshape(width, layer_count + 1, local_blocks, size)
    gains = gains.transpose(1, 3, 0, 2).reshape(layer_count + 1, size, blocks)
    end_gain = gains[layer_count].reshape(size, CHUNKS, blocks // CHUNKS).transpose(1, 0, 2)
    end_gain = end_gain.astype(jnp.float32)
    lowest, beside, gains, end_gain = tie((lowest, beside, gains, end_gain))
    first_two = gather_two(joined([lowest, beside]))
    first_two, second, target_sent = tie((first_two, second, target_sent))
    target = to_planes(target_sent).reshape(-1, wide)
    weights = [as_weights(gather_three(*first_two))]
    later = gather_one(second)
    weights, later = tie((weights, later))

    residual = patch_came
    flying = gather_two(later)
    sums = jnp.zeros((8, wide), jnp.float32)
    stored = []
    for layer in range(layer_count):
        group = 0 if layer in groups[0] else 1
        following, u, z, slope, scale, sums = run_forward(
            table, gains[layer], sums, residual, weights[group], layer - groups[group][0]
        )
        stored.append(((slope, z, u), scale, residual))
        residual = following
        if layer == 0:
            residual, sums, flying = tie((residual, sums, flying))
            weights.append(as_weights(gather_three(*flying)))
        if layer == groups[0][-1]:
            residual, sums, weights[1] = tie((residual, sums, weights[1]))
        if layer == layer_count - 2:
            residual, sums, target = tie((residual, sums, target))

    def core_sum(mine, other):
        return (mine, move(other, routes["cores"]))

    def plane_sum(mine, other):
        return send(run_sum([(mine, other)], width), "sections")

    def homeward(parts):
        return move_all(run_sum(parts, width), "homes")

    def both_halves(whole):
        pair = (whole, move(whole, routes["cores"]))
        return [part.reshape(width, -1, 2, chunk, size, size) for part in pair]

    steps = (core_sum, plane_sum)
    gradient = residual
    underway = []
    for layer in range(layer_count - 1, -1, -1):
        turning = layer == layer_count - 1
        last = layer == 0
        kept, scale, inputs = stored[layer]
        group = 0 if layer in groups[0] else 1
        sources = (gradient, inputs, target) if turning else (gradient, inputs)
        underway = [(at + 1, steps[at](*state)) if at < len(steps) else (at, state) for at, state in underway]
        gradient, mine, other = run_backward(
            table,
            gains[layer],
            end_gain,
            scale,
            kept,
            weights[group],
            layer - groups[group][0],
            sources,
            turning,
            last,
        )
        gradient, mine, other, states = tie((gradient, mine, other, [state for _, state in underway]))
        underway = [(at, state) for (at, _), state in zip(underway, states)]
        underway.append((0, (mine, other)))

    returned = to_planes(gradient.reshape(width, feat_local, wide))
    ended = [steps[at](*state) if at < len(steps) else state for at, state in underway][::-1]
    ended = tie(ended)
    ended[0] = plane_sum(*ended[0])
    others = to_planes(run_sum(ended[1:], width, apart=False))
    ended[0], returned, others = tie((ended[0], returned, others))
    home = homeward(ended[:1])
    d_patches = run_combine(critic_pairs, returned)
    others = to_sections(others)
    d_patches, home, others = tie((d_patches, home, others))
    homes_of = both_halves(joined(home)) + both_halves(others)
    grad_factor = 1.0 / math.sqrt(2 * tok_rows * width * replicas)
    grad_left, grad_right = run_assemble(
        place, order, homes_of, [(0,), tuple(range(1, layer_count))], grad_factor
    )
    return (d_patches, grad_left[None], grad_right[None])


def solution(mesh):
    in_specs = (
        P(("section", "dp"), "tensor"),
        P(("section", "dp"), "tensor"),
        P(("section", "dp"), None),
        P("section", None, "tensor", None, None),
        P("section", None, "tensor", None, None),
        P("section", None, "tensor"),
    )
    out_specs = (
        P(("section", "dp"), "tensor"),
        P("section", None, "tensor", None, None),
        P("section", None, "tensor", None, None),
    )
    body = plane_shards if planes_fit(mesh) else layered_shards
    return jax.shard_map(
        body, mesh=mesh, in_specs=in_specs, out_specs=out_specs, check_vma=False)
```

```python
import math

import jax
import jax.numpy as jnp
from jax import lax
from jax.experimental import pallas as pl
from jax.experimental.pallas import tpu as pltpu
from jax.sharding import PartitionSpec as P

EPSILON = 1e-06
TANH_SLOPE = 0.7978845608028654
CUBIC_TERM = 0.044715


def shifted(value, axis, steps):
    count = lax.axis_size(axis)
    first, last = (max(0, -steps), min(count, count - steps))
    return lax.ppermute(value, axis, [(source, source + steps) for source in range(first, last)])


def gelu_value(values):
    tangent = jnp.tanh(TANH_SLOPE * (values + CUBIC_TERM * values * values * values))
    return 0.5 * values * (1.0 + tangent)


def gelu_slope(values):
    tangent = jnp.tanh(TANH_SLOPE * (values + CUBIC_TERM * values * values * values))
    return 0.5 * (1.0 + tangent) + 0.5 * values * (1.0 - tangent * tangent) * TANH_SLOPE * (
        1.0 + 3.0 * CUBIC_TERM * values * values
    )


def norm_pair(residuals, gain_pair, model_width):
    squares = lax.psum(
        (
            jnp.sum(residuals[0] * residuals[0], axis=(1, 2)),
            jnp.sum(residuals[1] * residuals[1], axis=(1, 2)),
        ),
        "tensor",
    )
    factors = [lax.rsqrt(squares[member] / model_width + EPSILON) for member in range(2)]
    normed = [
        residuals[member] * factors[member][:, None, None] * gain_pair[member][None]
        for member in range(2)
    ]
    return (factors, normed)


def norm_back_pair(residuals, factors, gain_pair, grad_normed, carried, model_width):
    weighted = [grad_normed[member] * gain_pair[member][None] for member in range(2)]
    inners = lax.psum(
        (
            jnp.sum(weighted[0] * residuals[0], axis=(1, 2)),
            jnp.sum(weighted[1] * residuals[1], axis=(1, 2)),
        ),
        "tensor",
    )
    return [
        carried[member]
        + factors[member][:, None, None] * weighted[member]
        - residuals[member] * (factors[member] ** 3 * inners[member] / model_width)[:, None, None]
        for member in range(2)
    ]


def layered_shards(patches, teacher, critic_pairs, left_factors, right_factors, norm_gains):
    sections = lax.axis_size("section")
    tensor_width = lax.axis_size("tensor")
    replicas = lax.axis_size("dp")
    tok_rows = patches.shape[0]
    feat_local = patches.shape[1]
    layer_count = left_factors.shape[1]
    local_blocks = left_factors.shape[2]
    block_size = left_factors.shape[3]
    all_blocks = local_blocks * tensor_width
    fold_ratio = block_size // all_blocks
    model_width = feat_local * tensor_width
    sixth_rows = tok_rows // 6
    leading = 2 * sixth_rows
    critic_ids = jnp.arange(4, dtype=jnp.int32)
    named_by = (
        (critic_pairs[:, 0:1] == critic_ids[None, :])
        | (critic_pairs[:, 1:2] == critic_ids[None, :])
    ).astype(jnp.int32)
    ranking = jnp.cumsum(named_by, axis=0) - 1
    wide_ids = critic_ids[None, :] < 2
    slot_width = 3 * sixth_rows
    spilled = wide_ids & (ranking >= 3 * sixth_rows)
    destination = jnp.where(spilled, critic_ids[None, :] + 2, critic_ids[None, :])
    slot_index = jnp.where(spilled, ranking - sixth_rows, ranking)
    flat_slot = destination * slot_width + slot_index
    chosen = jnp.take_along_axis(flat_slot, critic_pairs, axis=1)
    slot_total = sections * slot_width
    row_ids = jnp.broadcast_to(jnp.arange(tok_rows, dtype=jnp.int32)[:, None], chosen.shape)
    source_row = (
        jnp.full((slot_total,), tok_rows, jnp.int32).at[chosen.reshape(-1)].set(row_ids.reshape(-1))
    )
    send_patch = (
        patches.at[source_row]
        .get(mode="fill", fill_value=0)
        .reshape(sections, slot_width, local_blocks, block_size)
    )
    send_target = (
        teacher.at[source_row]
        .get(mode="fill", fill_value=0)
        .reshape(sections, slot_width, local_blocks, block_size)
    )
    recv_patch, recv_target = (
        lax.all_to_all(send_patch, "section", split_axis=0, concat_axis=0, tiled=True),
        lax.all_to_all(send_target, "section", split_axis=0, concat_axis=0, tiled=True),
    )
    residuals = [
        recv_patch[:, :leading].reshape(-1, local_blocks, block_size).astype(jnp.float32),
        recv_patch[:, leading:].reshape(-1, local_blocks, block_size).astype(jnp.float32),
    ]
    targets = [
        recv_target[:, :leading].reshape(-1, local_blocks, block_size).astype(jnp.float32),
        recv_target[:, leading:].reshape(-1, local_blocks, block_size).astype(jnp.float32),
    ]
    native = (left_factors[0], right_factors[0], norm_gains[0])
    borrowed = shifted((left_factors, right_factors, norm_gains), "section", 2)
    is_wide = lax.axis_index("section") < 2
    second = (
        jnp.where(is_wide, left_factors, borrowed[0])[0],
        jnp.where(is_wide, right_factors, borrowed[1])[0],
        jnp.where(is_wide, norm_gains, borrowed[2])[0],
    )
    left_sets = (native[0], second[0])
    right_sets = (native[1], second[1])
    gain_sets = (
        native[2].astype(jnp.float32).reshape(layer_count + 1, local_blocks, block_size),
        second[2].astype(jnp.float32).reshape(layer_count + 1, local_blocks, block_size),
    )
    stored = []
    for layer_index in range(layer_count):
        gain_pair = [gain_sets[0][layer_index], gain_sets[1][layer_index]]
        factors, normed = norm_pair(residuals, gain_pair, model_width)
        normed = [normed[member].astype(jnp.bfloat16) for member in range(2)]
        first_out = [
            jnp.einsum(
                "nki,kij->nkj",
                normed[member],
                left_sets[member][layer_index],
                preferred_element_type=jnp.float32,
            ).astype(jnp.bfloat16)
            for member in range(2)
        ]
        permuted = (
            lax.all_to_all(first_out[0], "tensor", split_axis=2, concat_axis=1, tiled=True),
            lax.all_to_all(first_out[1], "tensor", split_axis=2, concat_axis=1, tiled=True),
        )
        permuted = [
            permuted[member].reshape(
                permuted[member].shape[0], all_blocks, local_blocks, fold_ratio
            )
            for member in range(2)
        ]
        right_quads = [
            right_sets[member][layer_index].reshape(
                local_blocks, fold_ratio, all_blocks, block_size
            )
            for member in range(2)
        ]
        mixture = [
            jnp.einsum(
                "nkmp,mpkl->nml",
                permuted[member],
                right_quads[member],
                preferred_element_type=jnp.float32,
            )
            for member in range(2)
        ]
        stored.append((residuals, factors, normed, permuted, mixture, right_quads, gain_pair))
        residuals = [residuals[member] + gelu_value(mixture[member]) for member in range(2)]
    final_gains = [gain_sets[0][layer_count], gain_sets[1][layer_count]]
    factors, outputs = norm_pair(residuals, final_gains, model_width)
    gradients = norm_back_pair(
        residuals,
        factors,
        final_gains,
        [outputs[member] - targets[member] for member in range(2)],
        [jnp.zeros_like(residuals[member]) for member in range(2)],
        model_width,
    )
    left_terms = []
    right_terms = []
    for layer_index in range(layer_count - 1, -1, -1):
        inputs, factors, normed, permuted, mixture, right_quads, gain_pair = stored[layer_index]
        slopes = [
            (gradients[member] * gelu_slope(mixture[member])).astype(jnp.bfloat16)
            for member in range(2)
        ]
        right_grad = [
            jnp.einsum(
                "nkmp,nml->mpkl",
                permuted[member],
                slopes[member],
                preferred_element_type=jnp.float32,
            ).reshape(local_blocks, block_size, block_size)
            for member in range(2)
        ]
        back_moved = [
            jnp.einsum(
                "nml,mpkl->nkmp",
                slopes[member],
                right_quads[member],
                preferred_element_type=jnp.float32,
            )
            .astype(jnp.bfloat16)
            .reshape(slopes[member].shape[0], all_blocks, local_blocks * fold_ratio)
            for member in range(2)
        ]
        arrived = (
            lax.all_to_all(back_moved[0], "tensor", split_axis=1, concat_axis=2, tiled=True),
            lax.all_to_all(back_moved[1], "tensor", split_axis=1, concat_axis=2, tiled=True),
        )
        left_grad = [
            jnp.einsum(
                "nki,nkj->kij", normed[member], arrived[member], preferred_element_type=jnp.float32
            )
            for member in range(2)
        ]
        grad_normed = [
            jnp.einsum(
                "nkj,kij->nki",
                arrived[member],
                left_sets[member][layer_index],
                preferred_element_type=jnp.float32,
            )
            for member in range(2)
        ]
        gradients = norm_back_pair(inputs, factors, gain_pair, grad_normed, gradients, model_width)
        layer_left = jnp.stack(left_grad)
        layer_right = jnp.stack(right_grad)
        layer_left, layer_right = (
            lax.psum(layer_left.astype(jnp.bfloat16), "dp").astype(jnp.float32),
            lax.psum(layer_right.astype(jnp.bfloat16), "dp").astype(jnp.float32),
        )
        left_terms.insert(0, layer_left)
        right_terms.insert(0, layer_right)
    left_stack = jnp.stack(left_terms)
    right_stack = jnp.stack(right_terms)
    repaid = (
        shifted(left_stack[:, 1].astype(jnp.bfloat16), "section", -2).astype(jnp.float32),
        shifted(right_stack[:, 1].astype(jnp.bfloat16), "section", -2).astype(jnp.float32),
    )
    is_wide = lax.axis_index("section") < 2
    left_total = left_stack[:, 0] + jnp.where(is_wide, left_stack[:, 1] + repaid[0], 0.0)
    right_total = right_stack[:, 0] + jnp.where(is_wide, right_stack[:, 1] + repaid[1], 0.0)
    grad_factor = 1.0 / math.sqrt(2 * tok_rows * sections * replicas)
    returned = [
        gradients[member].astype(jnp.bfloat16).reshape(sections, -1, local_blocks, block_size)
        for member in range(2)
    ]
    back_lead, back_trail = (
        lax.all_to_all(returned[0], "section", split_axis=0, concat_axis=0, tiled=True),
        lax.all_to_all(returned[1], "section", split_axis=0, concat_axis=0, tiled=True),
    )
    gathered = jnp.concatenate((back_lead, back_trail), axis=1).reshape(
        slot_total, local_blocks, block_size
    )
    combined = (
        gathered[chosen[:, 0]].astype(jnp.float32) + gathered[chosen[:, 1]].astype(jnp.float32)
    ) * 0.5
    d_patches = combined.astype(jnp.bfloat16).reshape(tok_rows, feat_local)
    return (d_patches, (left_total * grad_factor)[None], (right_total * grad_factor)[None])


VMEM_LIMIT = 60 * 1024 * 1024
CHUNKS = 8
TOGETHER = 4
PARTS = 4
SMALL = (16, 128)
AXES = ("section", "tensor", "dp")


def planes_fit(mesh):
    sections = mesh.shape["section"]
    paired = mesh.shape["dp"] == 2 and sections & (sections - 1) == 0
    return paired and mesh.shape["tensor"] == sections


def inner_dot(left, right, left_dim, right_dim):
    return lax.dot_general(
        left,
        right,
        (((left_dim,), (right_dim,)), ((), ())),
        preferred_element_type=jnp.float32,
    )


def fold_rows(values):
    return jnp.sum(values.reshape(values.shape[0] // 8, 8, values.shape[1]), axis=0)


def block_rows(block, size):
    return pl.ds(pl.multiple_of(block * size, size), size)


def column(gain_ref, block, at, slots):
    if len(gain_ref.shape) == 3:
        gains = gain_ref[block // gain_ref.shape[2]]
        return jnp.broadcast_to(gains[:, at : at + 1], (gains.shape[0], slots))
    picked = lax.broadcasted_iota(jnp.int32, (gain_ref.shape[1], slots), 0) == block
    return inner_dot(gain_ref[...], picked.astype(jnp.bfloat16), 1, 0)


def chunk_copy(source, target, sems, chunk):
    rows = target.shape[0] // CHUNKS
    at = pl.ds(pl.multiple_of(chunk * rows, rows), rows)
    return pltpu.make_async_copy(source.at[at], target.at[at], sems.at[chunk])


def start_chunks(source, target, sems):
    for chunk in range(CHUNKS):
        chunk_copy(source, target, sems, chunk).start()


def wait_chunks(source, target, sems):
    for chunk in range(CHUNKS):
        chunk_copy(source, target, sems, chunk).wait()


def factor_copies(parts, layer, held, sems, side):
    count = parts[0].shape[0]
    return [
        pltpu.make_async_copy(
            ref.at[:, layer, side], held.at[pl.ds(at * count, count), side], sems.at[side, at]
        )
        for at, ref in enumerate(parts)
    ]


def gradient_copies(held, parts, sems, side):
    count = parts[0].shape[0]
    return [
        pltpu.make_async_copy(
            held.at[pl.ds(at * count, count), side], ref.at[:, side], sems.at[side, at]
        )
        for at, ref in enumerate(parts)
    ]


def by_chunk(blocks, step, carry, before=None, after=None):
    per_chunk = blocks // CHUNKS

    def few(start, first, carry):
        stores = []
        for at in range(TOGETHER):
            made, carry = step(start + at, first + at, carry)
            stores += made
        for ref, index, value in stores:
            ref[index] = value
        return carry

    def one(chunk, carry):
        if before is not None:
            before(chunk)
        for at in range(0, per_chunk, TOGETHER):
            carry = few(chunk * per_chunk + at, at, carry)
        if after is not None:
            after(chunk)
        return carry

    return lax.fori_loop(0, CHUNKS, one, carry)


def forward_kernel(first, layer, inputs, table_ref, sums_ref, gain_ref, *refs):
    sources, refs = refs[:inputs], refs[inputs:]
    parts, sources = sources[:PARTS], sources[PARTS:]
    out_ref, u_ref, z_ref, slope_ref, scale_ref, next_ref = refs[:6]
    raw, h, w, u, z, slope, mid, in_sems, w_sems, out_sems = refs[6:]
    features, slots = h.shape
    size = w.shape[-1]
    chunk_blocks = w.shape[2]
    blocks = features // size
    fold = size // blocks

    left_in = factor_copies(parts, layer, w, w_sems, 0)
    right_in = factor_copies(parts, layer, w, w_sems, 1)
    if first:
        start_chunks(sources[0], raw, in_sems)
        for copy in left_in + right_in:
            copy.start()

        def squares(block, _, total):
            rows = block_rows(block, size)
            part = raw[rows, :].astype(jnp.float32)
            return [(h, (rows, slice(None)), part)], total + fold_rows(part * part)

        total = by_chunk(
            blocks,
            squares,
            jnp.zeros((8, slots), jnp.float32),
            lambda chunk: chunk_copy(sources[0], raw, in_sems, chunk).wait(),
        )
    else:
        for copy in left_in:
            copy.start()
        start_chunks(sources[0], h, in_sems)
        for copy in right_in:
            copy.start()
        total = sums_ref[...]
    scale = lax.rsqrt(jnp.sum(total, axis=0, keepdims=True) / features + EPSILON)
    scale_ref[...] = jnp.broadcast_to(scale, scale_ref.shape)
    for copy in left_in:
        copy.wait()

    def arrive(chunk):
        if not first:
            chunk_copy(sources[0], h, in_sems, chunk).wait()

    def left(block, nth, carry):
        rows = block_rows(block, size)
        place = table_ref[0, block]
        normed = (h[rows, :] * scale * column(gain_ref, block, nth, slots)).astype(jnp.bfloat16)
        weight = w[place // chunk_blocks, 0, place % chunk_blocks]
        first_out = inner_dot(weight, normed, 0, 0)
        at = (rows, slice(None))
        return [(u, at, normed), (mid, at, first_out)], carry

    def leave_left(chunk):
        chunk_copy(u, u_ref, out_sems.at[0], chunk).start()

    by_chunk(blocks, left, 0, arrive, leave_left)
    for copy in right_in:
        copy.wait()

    def right(block, nth, total):
        rows = block_rows(block, size)
        place = table_ref[0, block]
        moved = [mid[pl.ds(q * blocks + block, blocks, stride=size), :] for q in range(fold)]
        moved = jnp.concatenate(moved, axis=0).astype(jnp.bfloat16)
        weight = w[place // chunk_blocks, 1, place % chunk_blocks]
        mixture = inner_dot(weight, moved, 0, 0)
        squared = mixture * mixture
        tangent = jnp.tanh(mixture * (TANH_SLOPE + (TANH_SLOPE * CUBIC_TERM) * squared))
        half = 0.5 + 0.5 * tangent
        following = h[rows, :] + mixture * half
        steep = half + mixture * (1.0 - tangent * tangent) * (
            0.5 * TANH_SLOPE + (1.5 * TANH_SLOPE * CUBIC_TERM) * squared
        )
        at = (rows, slice(None))
        stores = [(z, at, moved), (h, at, following), (slope, at, steep.astype(jnp.bfloat16))]
        return stores, total + fold_rows(following * following)

    leaving = ((h, out_ref, 1), (z, z_ref, 2), (slope, slope_ref, 3))

    def leave_right(chunk):
        for source, target, at in leaving:
            chunk_copy(source, target, out_sems.at[at], chunk).start()

    next_ref[...] = by_chunk(blocks, right, jnp.zeros((8, slots), jnp.float32), None, leave_right)
    for source, target, at in ((u, u_ref, 0),) + leaving:
        wait_chunks(source, target, out_sems.at[at])


def backward_kernel(turning, last, layer, inputs, table_ref, scale_ref, gain_ref, end_gain_ref, *refs):
    sources, refs = refs[:inputs], refs[inputs:]
    slope_ref, z_ref, u_ref = sources[:3]
    parts, sources = sources[3 : 3 + PARTS], sources[3 + PARTS :]
    out_ref, own_grad, peer_grad = refs[:3]
    g, slope, z, u, h, w, gw, mid, top, goal = refs[3:13]
    in_sems, w_sems, out_sems, gw_sems = refs[13:]
    features, slots = g.shape
    size = w.shape[-1]
    chunk_blocks = w.shape[2]
    blocks = features // size
    fold = size // blocks

    left_in = factor_copies(parts, layer, w, w_sems, 0)
    right_in = factor_copies(parts, layer, w, w_sems, 1)
    g_ref, h_ref = sources[:2]
    if turning:
        for chunk in range(CHUNKS):
            chunk_copy(g_ref, top, in_sems.at[0], chunk).start()
            chunk_copy(sources[2], goal, in_sems.at[5], chunk).start()
    for copy in right_in:
        copy.start()
    for chunk in range(CHUNKS):
        if not turning:
            chunk_copy(g_ref, g, in_sems.at[0], chunk).start()
        chunk_copy(slope_ref, slope, in_sems.at[1], chunk).start()
        chunk_copy(z_ref, z, in_sems.at[2], chunk).start()
    for copy in left_in:
        copy.start()
    for chunk in range(CHUNKS):
        chunk_copy(u_ref, u, in_sems.at[3], chunk).start()
        chunk_copy(h_ref, h, in_sems.at[4], chunk).start()

    if turning:
        zero = jnp.zeros((8, slots), jnp.float32)

        def sums(block, nth, totals):
            rows = block_rows(block, size)
            part = top[rows, :]
            scaled = part * column(end_gain_ref, block, nth, slots)
            return [], (
                totals[0] + fold_rows(part * part),
                totals[1] + fold_rows(scaled * scaled),
                totals[2] + fold_rows(scaled * goal[rows, :].astype(jnp.float32)),
            )

        def arrive_top(chunk):
            chunk_copy(g_ref, top, in_sems.at[0], chunk).wait()
            chunk_copy(sources[2], goal, in_sems.at[5], chunk).wait()

        totals = by_chunk(blocks, sums, (zero, zero, zero), arrive_top)
        squares, gained, crossed = [jnp.sum(total, axis=0, keepdims=True) for total in totals]
        end_scale = lax.rsqrt(squares / features + EPSILON)
        end_back = end_scale * end_scale * end_scale * (end_scale * gained - crossed) / features

    for copy in right_in:
        copy.wait()

    def arrive_right(chunk):
        if not turning:
            chunk_copy(g_ref, g, in_sems.at[0], chunk).wait()
        chunk_copy(slope_ref, slope, in_sems.at[1], chunk).wait()
        chunk_copy(z_ref, z, in_sems.at[2], chunk).wait()

    def right(block, nth, total):
        rows = block_rows(block, size)
        place, home = table_ref[0, block], table_ref[2 if last else 1, block]
        at = (place // chunk_blocks, 1, place % chunk_blocks)
        to = (home // chunk_blocks, 1, home % chunk_blocks)
        if turning:
            part = top[rows, :]
            factor = column(end_gain_ref, block, nth, slots)
            error = (part * end_scale * factor - goal[rows, :].astype(jnp.float32)) * factor
            gradient = end_scale * error - part * end_back
            stores = [(g, (rows, slice(None)), gradient)]
        else:
            gradient = g[rows, :]
            stores = []
        steep = (gradient * slope[rows, :].astype(jnp.float32)).astype(jnp.bfloat16)
        taken = z[rows, :]
        back = inner_dot(w[at], steep, 1, 0)
        stores.append((gw, to, inner_dot(taken, steep, 1, 1).astype(jnp.bfloat16)))
        stores.append((mid, (rows, slice(None)), back))
        return stores, total + fold_rows(taken.astype(jnp.float32) * back)

    total = by_chunk(blocks, right, jnp.zeros((8, slots), jnp.float32), arrive_right)
    right_out = gradient_copies(gw, (own_grad, peer_grad), gw_sems, 1)
    for copy in right_out:
        copy.start()
    for copy in left_in:
        copy.wait()
    scale = scale_ref[0:1, :]
    back = scale * scale * jnp.sum(total, axis=0, keepdims=True) / features

    def arrive_left(chunk):
        chunk_copy(u_ref, u, in_sems.at[3], chunk).wait()
        chunk_copy(h_ref, h, in_sems.at[4], chunk).wait()

    def left(block, nth, carry):
        rows = block_rows(block, size)
        place, home = table_ref[0, block], table_ref[2 if last else 1, block]
        at = (place // chunk_blocks, 0, place % chunk_blocks)
        to = (home // chunk_blocks, 0, home % chunk_blocks)
        arrived = [mid[pl.ds(q * blocks + block, blocks, stride=size), :] for q in range(fold)]
        arrived = jnp.concatenate(arrived, axis=0).astype(jnp.bfloat16)
        factor_grad = inner_dot(u[rows, :], arrived, 1, 1).astype(jnp.bfloat16)
        weighted = inner_dot(w[at], arrived, 1, 0) * column(gain_ref, block, nth, slots)
        ended = g[rows, :] + scale * weighted - h[rows, :].astype(jnp.float32) * back
        index = (rows, slice(None))
        stores = [(gw, to, factor_grad)]
        stores.append((u, index, ended.astype(jnp.bfloat16)) if last else (g, index, ended))
        return stores, carry

    ended = u if last else g
    by_chunk(
        blocks, left, 0, arrive_left, lambda chunk: chunk_copy(ended, out_ref, out_sems, chunk).start()
    )
    left_out = gradient_copies(gw, (own_grad, peer_grad), gw_sems, 0)
    for copy in left_out:
        copy.start()
    wait_chunks(ended, out_ref, out_sems)
    for copy in right_out + left_out:
        copy.wait()


def shape_of(shape, dtype):
    return jax.ShapeDtypeStruct(shape, dtype)


SMEM = pl.BlockSpec(memory_space=pltpu.SMEM)
INSIDE = pl.BlockSpec(memory_space=pltpu.VMEM)
OUTSIDE = pl.BlockSpec(memory_space=pl.ANY)


def run_forward(table, gain, sums, residual, weights, layer):
    first = residual.dtype == jnp.bfloat16
    whole = residual.shape
    sources = (*weights, residual)
    held = (PARTS * weights[0].shape[0],) + weights[0].shape[2:]
    out_shape = (
        shape_of(whole, jnp.float32),
        shape_of(whole, jnp.bfloat16),
        shape_of(whole, jnp.bfloat16),
        shape_of(whole, jnp.bfloat16),
        shape_of((8, whole[1]), jnp.float32),
        shape_of((8, whole[1]), jnp.float32),
    )
    return pl.pallas_call(
        lambda *refs: forward_kernel(first, layer, len(sources), *refs),
        in_specs=[SMEM, INSIDE, INSIDE] + [OUTSIDE] * len(sources),
        out_specs=[OUTSIDE] * 4 + [INSIDE] * 2,
        out_shape=out_shape,
        scratch_shapes=[
            pltpu.VMEM(whole if first else SMALL, jnp.bfloat16),
            pltpu.VMEM(whole, jnp.float32),
            pltpu.VMEM(held, jnp.bfloat16),
            pltpu.VMEM(whole, jnp.bfloat16),
            pltpu.VMEM(whole, jnp.bfloat16),
            pltpu.VMEM(whole, jnp.bfloat16),
            pltpu.VMEM(whole, jnp.float32),
            pltpu.SemaphoreType.DMA((CHUNKS,)),
            pltpu.SemaphoreType.DMA((2, PARTS)),
            pltpu.SemaphoreType.DMA((4, CHUNKS)),
        ],
        compiler_params=pltpu.CompilerParams(vmem_limit_bytes=VMEM_LIMIT),
        cost_estimate=pl.CostEstimate(
            flops=FORWARD_COST, bytes_accessed=20 * whole[0] * whole[1], transcendentals=0
        ),
        name="forward_layer",
    )(table, sums, gain, *sources)


def run_backward(table, gain, end_gain, scale, kept, weights, layer, sources, turning, last):
    whole = kept[0].shape
    sources = (*kept, *weights, *sources)
    held = (PARTS * weights[0].shape[0],) + weights[0].shape[2:]
    half = (held[0] // 2,) + held[1:]
    out_shape = [shape_of(whole, jnp.bfloat16 if last else jnp.float32)] + [shape_of(half, jnp.bfloat16)] * 2
    return pl.pallas_call(
        lambda *refs: backward_kernel(turning, last, layer, len(sources), *refs),
        in_specs=[SMEM] + [INSIDE] * 3 + [OUTSIDE] * len(sources),
        out_specs=[OUTSIDE] * len(out_shape),
        out_shape=out_shape,
        scratch_shapes=[
            pltpu.VMEM(whole, jnp.float32),
            pltpu.VMEM(whole, jnp.bfloat16),
            pltpu.VMEM(whole, jnp.bfloat16),
            pltpu.VMEM(whole, jnp.bfloat16),
            pltpu.VMEM(whole, jnp.bfloat16 if last else jnp.float32),
            pltpu.VMEM(held, jnp.bfloat16),
            pltpu.VMEM(held, jnp.bfloat16),
            pltpu.VMEM(whole, jnp.float32),
            pltpu.VMEM(whole if turning else SMALL, jnp.float32),
            pltpu.VMEM(whole if turning else SMALL, jnp.bfloat16),
            pltpu.SemaphoreType.DMA((6, CHUNKS)),
            pltpu.SemaphoreType.DMA((2, PARTS)),
            pltpu.SemaphoreType.DMA((CHUNKS,)),
            pltpu.SemaphoreType.DMA((2, PARTS)),
        ],
        compiler_params=pltpu.CompilerParams(vmem_limit_bytes=VMEM_LIMIT),
        cost_estimate=pl.CostEstimate(
            flops=BACKWARD_COST, bytes_accessed=30 * whole[0] * whole[1], transcendentals=0
        ),
        name="backward_layer",
    )(table, scale, gain, end_gain, *sources)


def join_kernel(rows, *refs):
    sources, whole, sems = refs[:-2], refs[-2], refs[-1]
    copies = [
        pltpu.make_async_copy(source.at[pl.ds(0, rows)], whole.at[pl.ds(at * rows, rows)], sems.at[at])
        for at, source in enumerate(sources)
    ]
    for copy in copies:
        copy.start()
    for copy in copies:
        copy.wait()


def joined(parts, rows=None):
    rows = parts[0].shape[0] if rows is None else rows
    whole = shape_of((rows * len(parts),) + parts[0].shape[1:], parts[0].dtype)
    return pl.pallas_call(
        lambda *refs: join_kernel(rows, *refs),
        in_specs=[OUTSIDE] * len(parts),
        out_specs=INSIDE,
        out_shape=whole,
        scratch_shapes=[pltpu.SemaphoreType.DMA((len(parts),))],
        compiler_params=pltpu.CompilerParams(vmem_limit_bytes=VMEM_LIMIT),
        cost_estimate=pl.CostEstimate(
            flops=0, bytes_accessed=4 * math.prod(whole.shape), transcendentals=0
        ),
        name="join",
    )(*parts)


def order_kernel(ranges, place_ref, *refs):
    sources, whole, sems = refs[:-2], refs[-2], refs[-1]
    copies = []
    for distance, source in enumerate(sources):
        row = 0
        for start, count in ranges:
            target = whole.at[place_ref[0] ^ distance, pl.ds(row, count)]
            copies.append(pltpu.make_async_copy(source.at[pl.ds(start, count)], target, sems.at[len(copies)]))
            row += count
    for copy in copies:
        copy.start()
    for copy in copies:
        copy.wait()


def by_section(place, parts, ranges):
    rows = sum(count for _, count in ranges)
    whole = shape_of((len(parts), rows) + parts[0].shape[1:], parts[0].dtype)
    return pl.pallas_call(
        lambda *refs: order_kernel(ranges, *refs),
        in_specs=[SMEM] + [OUTSIDE] * len(parts),
        out_specs=INSIDE,
        out_shape=whole,
        scratch_shapes=[pltpu.SemaphoreType.DMA((len(parts) * len(ranges),))],
        compiler_params=pltpu.CompilerParams(vmem_limit_bytes=VMEM_LIMIT),
        cost_estimate=pl.CostEstimate(
            flops=0, bytes_accessed=4 * math.prod(whole.shape), transcendentals=0
        ),
        name="by_section",
    )(place, *parts)


def sum_kernel(terms, inputs, *refs):
    sources, outs = refs[:inputs], refs[inputs:]
    for group in range(inputs // terms):
        mine = sources[group * terms : (group + 1) * terms]
        for at in range(mine[0].shape[0]):
            total = sum(ref[at].astype(jnp.float32) for ref in mine).astype(jnp.bfloat16)
            if len(outs) > 1:
                outs[at][group] = total
            else:
                outs[0][at, group] = total


def run_sum(groups, parts, apart=True):
    flat = [term.reshape(parts, -1, term.shape[-1]) for terms in groups for term in terms]
    _, rows, lanes = flat[0].shape
    steps = 2
    if apart:
        out_shape = [shape_of((len(groups), rows, lanes), jnp.bfloat16)] * parts
        out_specs = [pl.BlockSpec((len(groups), rows // steps, lanes), lambda i: (0, i, 0))] * parts
    else:
        out_shape = [shape_of((parts, len(groups), rows, lanes), jnp.bfloat16)]
        out_specs = [pl.BlockSpec((parts, len(groups), rows // steps, lanes), lambda i: (0, 0, i, 0))]
    sums = pl.pallas_call(
        lambda *refs: sum_kernel(len(groups[0]), len(flat), *refs),
        grid=(steps,),
        in_specs=[pl.BlockSpec((parts, rows // steps, lanes), lambda i: (0, i, 0))] * len(flat),
        out_specs=out_specs,
        out_shape=out_shape,
        compiler_params=pltpu.CompilerParams(vmem_limit_bytes=VMEM_LIMIT),
        cost_estimate=pl.CostEstimate(
            flops=flat[0].size * len(flat), bytes_accessed=2 * flat[0].size * (len(flat) + 1), transcendentals=0
        ),
        name="sum",
    )(*flat)
    return [out.reshape(-1, lanes) for out in sums] if apart else sums[0].reshape(parts, -1, lanes)


def pieces_kernel(chunk, place_ref, order_ref, left_ref, right_ref, gain_ref, *refs):
    outs, (held, left_sem, sems) = refs[:-3], refs[-3:]
    layer_count, half, size = held.shape[:3]
    first = place_ref[2] * half
    lefts = pltpu.make_async_copy(left_ref.at[:, pl.ds(first, half)], held, left_sem.at[0])
    lefts.start()
    copies = []
    turns = []
    for distance, out in enumerate(outs):
        start = (place_ref[0] ^ distance) * chunk
        row = 0
        for layer in range(layer_count):
            for inside in range(chunk):
                turns.append((layer, start + inside, out, row))
                row += size
            for inside in range(chunk):
                source = right_ref.at[layer, first + start + inside]
                copies.append((source, out.at[pl.ds(row, size)]))
                row += size
        copies.append((gain_ref, out.at[pl.ds(row, gain_ref.shape[0])]))
    copies = [
        pltpu.make_async_copy(source, target, sems.at[at]) for at, (source, target) in enumerate(copies)
    ]
    for copy in copies:
        copy.start()
    lefts.wait()
    for layer, block, out, row in turns:
        turned = inner_dot(held[layer, block], order_ref[...], 1, 0)
        out[pl.ds(row, size), :] = turned.astype(jnp.bfloat16)
    for copy in copies:
        copy.wait()


def factor_pieces(place, order, left, right, gain_rows, chunk, width):
    layer_count, blocks, size = left.shape[:3]
    rows = layer_count * 2 * chunk * size + gain_rows.shape[0]
    return pl.pallas_call(
        lambda *refs: pieces_kernel(chunk, *refs),
        in_specs=[SMEM, INSIDE] + [OUTSIDE] * 3,
        out_specs=[INSIDE] * width,
        out_shape=[shape_of((rows, size), jnp.bfloat16)] * width,
        scratch_shapes=[
            pltpu.VMEM((layer_count, blocks // 2, size, size), jnp.bfloat16),
            pltpu.SemaphoreType.DMA((1,)),
            pltpu.SemaphoreType.DMA((width * (layer_count * chunk + 1),)),
        ],
        compiler_params=pltpu.CompilerParams(vmem_limit_bytes=VMEM_LIMIT),
        cost_estimate=pl.CostEstimate(flops=left.size * size, bytes_accessed=4 * left.size, transcendentals=0),
        name="pieces",
    )(place, order, left, right, gain_rows)


def choice(pairs, critic, slots):
    rows = pairs.shape[0]
    named = (pairs[:, 0:1] == critic) | (pairs[:, 1:2] == critic)
    named = jnp.broadcast_to(named.astype(jnp.float32), (rows, slots))
    before = lax.broadcasted_iota(jnp.int32, (rows, rows), 1) < lax.broadcasted_iota(jnp.int32, (rows, rows), 0)
    rank = inner_dot(before.astype(jnp.bfloat16), named.astype(jnp.bfloat16), 1, 0)
    at = lax.broadcasted_iota(jnp.int32, (rows, slots), 1).astype(jnp.float32)
    return jnp.where(rank == at, named, 0.0).astype(jnp.bfloat16)


def pick_kernel(pairs_ref, values_ref, out_ref):
    width, features, slots = out_ref.shape
    pairs = pairs_ref[...]
    chosen = [choice(pairs, critic, slots) for critic in range(width)]
    step = 512
    for start in range(0, features, step):
        part = values_ref[:, pl.ds(start, step)]
        for k in range(width):
            out_ref[k, pl.ds(start, step), :] = inner_dot(part, chosen[k], 0, 0).astype(jnp.bfloat16)


def run_pick(pairs, values, width, slots):
    rows, features = values.shape
    return pl.pallas_call(
        pick_kernel,
        in_specs=[INSIDE] * 2,
        out_specs=INSIDE,
        out_shape=shape_of((width, features, slots), jnp.bfloat16),
        compiler_params=pltpu.CompilerParams(vmem_limit_bytes=VMEM_LIMIT),
        cost_estimate=pl.CostEstimate(
            flops=2 * rows * features * slots * width, bytes_accessed=8 * rows * features, transcendentals=0
        ),
        name="pick",
    )(pairs, values)


def combine_kernel(pairs_ref, came_ref, out_ref):
    width, features, slots = came_ref.shape
    pairs = pairs_ref[...]
    chosen = [choice(pairs, critic, slots) for critic in range(width)]
    step = 512
    for start in range(0, features, step):
        total = sum(inner_dot(chosen[k], came_ref[k, pl.ds(start, step), :], 1, 1) for k in range(width))
        out_ref[:, pl.ds(start, step)] = (0.5 * total).astype(jnp.bfloat16)


def run_combine(pairs, came):
    rows = pairs.shape[0]
    return pl.pallas_call(
        combine_kernel,
        in_specs=[INSIDE] * 2,
        out_specs=INSIDE,
        out_shape=shape_of((rows, came.shape[1]), jnp.bfloat16),
        compiler_params=pltpu.CompilerParams(vmem_limit_bytes=VMEM_LIMIT),
        cost_estimate=pl.CostEstimate(
            flops=2 * rows * came.size, bytes_accessed=4 * came.size, transcendentals=0
        ),
        name="combine",
    )(pairs, came)


FORWARD_COST = 4_000_000_000
BACKWARD_COST = 5_000_000_000


def assemble_kernel(layers, factor, place_ref, order_ref, *refs):
    count = 2 * len(layers)
    sources, (left_ref, right_ref) = refs[:count], refs[count : count + 2]
    held, wide = refs[count + 2 : 2 * count + 2], refs[2 * count + 2 : 3 * count + 2]
    in_sems, out_sems = refs[3 * count + 2 :]
    origin, core = place_ref[0] ^ place_ref[1], place_ref[2]
    order = order_ref[...]
    arrivals = [
        pltpu.make_async_copy(source, held[at], in_sems.at[at]) for at, source in enumerate(sources)
    ]
    for copy in arrivals:
        copy.start()
    leaving = []
    for at in range(count):
        arrivals[at].wait()
        half = core if at % 2 == 0 else 1 - core
        width, _, _, chunk = held[at].shape[:4]
        for k in range(width):
            start = (half * width + (origin ^ k if at < 2 else k)) * chunk
            for inside, layer in enumerate(layers[at // 2]):
                for block in range(chunk):
                    left = inner_dot(held[at][k, inside, 0, block], order, 1, 1)
                    wide[at][k, inside, 0, block] = left * factor
                wide[at][k, inside, 1] = held[at][k, inside, 1].astype(jnp.float32) * factor
                for which, target in enumerate((left_ref, right_ref)):
                    copy = pltpu.make_async_copy(
                        wide[at].at[k, inside, which],
                        target.at[layer, pl.ds(start, chunk)],
                        out_sems.at[len(leaving)],
                    )
                    copy.start()
                    leaving.append(copy)
    for copy in leaving:
        copy.wait()


def run_assemble(place, order, pieces, layers, factor):
    piece = pieces[0].shape
    layer_count = sum(len(group) for group in layers)
    out = shape_of((layer_count, 2 * piece[0] * piece[3]) + piece[4:], jnp.float32)
    return pl.pallas_call(
        lambda *refs: assemble_kernel(layers, factor, *refs),
        in_specs=[SMEM, INSIDE] + [OUTSIDE] * len(pieces),
        out_specs=[OUTSIDE] * 2,
        out_shape=[out] * 2,
        scratch_shapes=[pltpu.VMEM(part.shape, jnp.bfloat16) for part in pieces]
        + [pltpu.VMEM(part.shape, jnp.float32) for part in pieces]
        + [
            pltpu.SemaphoreType.DMA((len(pieces),)),
            pltpu.SemaphoreType.DMA((4 * layer_count * piece[0],)),
        ],
        compiler_params=pltpu.CompilerParams(vmem_limit_bytes=VMEM_LIMIT),
        cost_estimate=pl.CostEstimate(flops=0, bytes_accessed=4 * math.prod(out.shape) * 3, transcendentals=0),
        name="assemble",
    )(place, order, *pieces)


def plane_routes(width, replicas):
    bits = width.bit_length() - 1
    orders = [[(step + d) % bits for step in range(bits)] for d in range(replicas)]
    every = [(s, t, d) for s in range(width) for t in range(width) for d in range(replicas)]

    def route(move):
        def index(s, t, d):
            return (s * width + t) * replicas + d

        return [(index(*place), index(*move(*place))) for place in every]

    ranks = [[0] * width for _ in range(replicas)]
    for d in range(replicas):
        for r in range(width):
            ranks[d][sum(((r >> at) & 1) << orders[d][at] for at in range(bits))] = r
    return {
        "across": [route(lambda s, t, d, at=at: (s ^ (1 << orders[d][at]), t, d)) for at in range(bits)],
        "cores": route(lambda s, t, d: (s, t, 1 - d)),
        "sections": [route(lambda s, t, d, k=k: (s ^ k, t, d)) for k in range(width)],
        "homes": [route(lambda s, t, d, j=j: (t, t ^ s ^ j, d)) for j in range(width)],
    }, ranks


def plane_shards(patches, teacher, critic_pairs, left_factors, right_factors, norm_gains):
    width = lax.axis_size("section")
    replicas = lax.axis_size("dp")
    tok_rows, feat_local = patches.shape
    layer_count, local_blocks, size = left_factors.shape[1:4]
    blocks = feat_local * width // size
    wide = 2 * tok_rows // 3
    chunk = local_blocks // (replicas * width)
    layer_rows = 2 * chunk * size
    routes, ranks = plane_routes(width, replicas)
    section = lax.axis_index("section")
    tensor = lax.axis_index("tensor")
    core = lax.axis_index("dp")
    place = jnp.stack([section, tensor, core]).astype(jnp.int32)
    tie = lax.optimization_barrier

    def move(value, route):
        return lax.ppermute(value, AXES, route)

    def move_all(values, name):
        return [move(value, route) for value, route in zip(values, routes[name])]

    def send(values, name):
        return [values[0]] + [move(values[k], routes[name][k]) for k in range(1, width)]

    def gather_one(mine):
        return joined([mine, move(mine, routes["across"][0])])

    def gather_two(pair):
        return pair, move(pair, routes["across"][1]), move(pair, routes["cores"])

    def gather_three(pair, other, peer):
        return [pair, other, peer, move(other, routes["cores"])]

    def as_weights(parts):
        return [part.reshape(2 * width, -1, 2, chunk, size, size) for part in parts]

    block = jnp.arange(blocks, dtype=jnp.int32)
    inside = block % local_blocks
    replica = inside // (width * chunk)
    part = (replica != core).astype(jnp.int32)
    distance = section ^ ((inside // chunk) % width)
    quarter = block // local_blocks
    rank = jnp.array(ranks, jnp.int32)[replica, distance]
    table = jnp.stack(
        [
            ((part * width + index) * width + piece) * chunk + inside % chunk
            for index, piece in (
                (rank, quarter),
                (distance, quarter),
                (distance, tensor ^ section ^ distance ^ quarter),
            )
        ]
    ).astype(jnp.int32)

    def to_planes(value):
        return lax.all_to_all(value, "tensor", split_axis=0, concat_axis=0, tiled=True)

    def to_sections(value):
        return lax.all_to_all(value, "section", split_axis=0, concat_axis=0, tiled=True)

    half_layers = layer_count // 2
    fold = size // blocks
    columns = jnp.arange(size)
    order = (columns[:, None] == (columns % blocks) * fold + columns // blocks).astype(jnp.bfloat16)
    gain_rows = norm_gains[0].reshape(-1, size)
    patch_sent = run_pick(critic_pairs, patches, width, wide)
    patch_sent, left, right, teacher = tie((patch_sent, left_factors[0], right_factors[0], teacher))
    patch_came = to_planes(patch_sent).reshape(-1, wide)
    pieces = factor_pieces(place, order, left, right, gain_rows, chunk, width)
    spread = send(pieces, "sections")
    cut, end = half_layers * layer_rows, layer_count * layer_rows
    first = by_section(place, spread, [(0, cut), (end, gain_rows.shape[0])])
    second = by_section(place, spread, [(cut, end - cut)])
    target_sent = run_pick(critic_pairs, teacher, width, wide)
    patch_came, first, second, target_sent = tie((patch_came, first, second, target_sent))
    first = to_planes(first)
    first, second = tie((first, second))
    second = to_planes(second)
    lowest = [first[:, at * layer_rows : (at + 1) * layer_rows] for at in range(half_layers)]
    beside = [move(value, routes["across"][0]) for value in lowest[:2]]
    gains = first[:, cut:].reshape(width, layer_count + 1, local_blocks, size)
    gains = gains.transpose(1, 3, 0, 2).reshape(layer_count + 1, size, blocks)
    end_gain = gains[layer_count].reshape(size, CHUNKS, blocks // CHUNKS).transpose(1, 0, 2)
    end_gain = end_gain.astype(jnp.float32)
    lowest, beside, gains, end_gain = tie((lowest, beside, gains, end_gain))
    flying = {0: gather_two(joined([lowest[0], beside[0]]))}
    flying, second, target_sent = tie((flying, second, target_sent))
    for layer in range(half_layers, layer_count):
        at = (layer - half_layers) * layer_rows
        lowest.append(second[:, at : at + layer_rows])
    target = to_planes(target_sent).reshape(-1, wide)
    weights = [as_weights(gather_three(*flying.pop(0)))]
    flying[1] = gather_two(joined([lowest[1], beside[1]]))
    steps = {2: (lowest[2], move(lowest[2], routes["across"][0]))}
    weights, flying, steps = tie((weights, flying, steps))

    residual = patch_came
    sums = jnp.zeros((8, wide), jnp.float32)
    stored = []
    for layer in range(layer_count):
        ahead = {}
        if layer + 1 < layer_count:
            ahead["weights"] = gather_three(*flying.pop(layer + 1))
        if layer + 2 < layer_count:
            ahead["two"] = gather_two(joined(list(steps.pop(layer + 2))))
        if layer + 3 < layer_count:
            ahead["one"] = (lowest[layer + 3], move(lowest[layer + 3], routes["across"][0]))
        following, u, z, slope, scale, sums = run_forward(
            table, gains[layer], sums, residual, weights[layer], 0
        )
        stored.append(((slope, z, u), scale, residual))
        residual, sums, ahead = tie((following, sums, ahead))
        if layer + 1 < layer_count:
            weights.append(as_weights(ahead["weights"]))
        if layer + 2 < layer_count:
            flying[layer + 2] = ahead["two"]
        if layer + 3 < layer_count:
            steps[layer + 3] = ahead["one"]
        if layer == layer_count - 2:
            residual, sums, target = tie((residual, sums, target))

    def core_sum(mine, other):
        return (mine, move(other, routes["cores"]))

    def plane_sum(mine, other):
        return send(run_sum([(mine, other)], width), "sections")

    def both_halves(whole):
        pair = (whole, move(whole, routes["cores"]))
        return [part.reshape(width, -1, 2, chunk, size, size) for part in pair]

    steps = (core_sum, plane_sum)
    gradient = residual
    underway = []
    for layer in range(layer_count - 1, -1, -1):
        turning = layer == layer_count - 1
        last = layer == 0
        kept, scale, inputs = stored[layer]
        sources = (gradient, inputs, target) if turning else (gradient, inputs)
        underway = [(at + 1, steps[at](*state)) if at < len(steps) else (at, state) for at, state in underway]
        gradient, mine, other = run_backward(
            table,
            gains[layer],
            end_gain,
            scale,
            kept,
            weights[layer],
            0,
            sources,
            turning,
            last,
        )
        gradient, mine, other, states = tie((gradient, mine, other, [state for _, state in underway]))
        underway = [(at, state) for (at, _), state in zip(underway, states)]
        underway.append((0, (mine, other)))

    returned = to_planes(gradient.reshape(width, feat_local, wide))
    ended = [steps[at](*state) if at < len(steps) else state for at, state in underway][::-1]
    ended = tie(ended)
    ended[0] = plane_sum(*ended[0])
    others = to_planes(run_sum(ended[1:], width, apart=False))
    home = run_sum(ended[:1], width)
    home, returned, others = tie((home, returned, others))
    home = move_all(home, "homes")
    d_patches = run_combine(critic_pairs, returned)
    others = to_sections(others)
    d_patches, home, others = tie((d_patches, home, others))
    homes_of = both_halves(joined(home)) + both_halves(others)
    grad_factor = 1.0 / math.sqrt(2 * tok_rows * width * replicas)
    grad_left, grad_right = run_assemble(
        place, order, homes_of, [(0,), tuple(range(1, layer_count))], grad_factor
    )
    return (d_patches, grad_left[None], grad_right[None])


def solution(mesh):
    in_specs = (
        P(("section", "dp"), "tensor"),
        P(("section", "dp"), "tensor"),
        P(("section", "dp"), None),
        P("section", None, "tensor", None, None),
        P("section", None, "tensor", None, None),
        P("section", None, "tensor"),
    )
    out_specs = (
        P(("section", "dp"), "tensor"),
        P("section", None, "tensor", None, None),
        P("section", None, "tensor", None, None),
    )
    body = plane_shards if planes_fit(mesh) else layered_shards
    return jax.shard_map(
        body, mesh=mesh, in_specs=in_specs, out_specs=out_specs, check_vma=False)
```

```python
import math

import jax
import jax.numpy as jnp
from jax import lax
from jax.experimental import pallas as pl
from jax.experimental.pallas import tpu as pltpu
from jax.sharding import PartitionSpec as P

EPSILON = 1e-06
TANH_SLOPE = 0.7978845608028654
CUBIC_TERM = 0.044715


def shifted(value, axis, steps):
    count = lax.axis_size(axis)
    first, last = (max(0, -steps), min(count, count - steps))
    return lax.ppermute(value, axis, [(source, source + steps) for source in range(first, last)])


def gelu_value(values):
    tangent = jnp.tanh(TANH_SLOPE * (values + CUBIC_TERM * values * values * values))
    return 0.5 * values * (1.0 + tangent)


def gelu_slope(values):
    tangent = jnp.tanh(TANH_SLOPE * (values + CUBIC_TERM * values * values * values))
    return 0.5 * (1.0 + tangent) + 0.5 * values * (1.0 - tangent * tangent) * TANH_SLOPE * (
        1.0 + 3.0 * CUBIC_TERM * values * values
    )


def norm_pair(residuals, gain_pair, model_width):
    squares = lax.psum(
        (
            jnp.sum(residuals[0] * residuals[0], axis=(1, 2)),
            jnp.sum(residuals[1] * residuals[1], axis=(1, 2)),
        ),
        "tensor",
    )
    factors = [lax.rsqrt(squares[member] / model_width + EPSILON) for member in range(2)]
    normed = [
        residuals[member] * factors[member][:, None, None] * gain_pair[member][None]
        for member in range(2)
    ]
    return (factors, normed)


def norm_back_pair(residuals, factors, gain_pair, grad_normed, carried, model_width):
    weighted = [grad_normed[member] * gain_pair[member][None] for member in range(2)]
    inners = lax.psum(
        (
            jnp.sum(weighted[0] * residuals[0], axis=(1, 2)),
            jnp.sum(weighted[1] * residuals[1], axis=(1, 2)),
        ),
        "tensor",
    )
    return [
        carried[member]
        + factors[member][:, None, None] * weighted[member]
        - residuals[member] * (factors[member] ** 3 * inners[member] / model_width)[:, None, None]
        for member in range(2)
    ]


def layered_shards(patches, teacher, critic_pairs, left_factors, right_factors, norm_gains):
    sections = lax.axis_size("section")
    tensor_width = lax.axis_size("tensor")
    replicas = lax.axis_size("dp")
    tok_rows = patches.shape[0]
    feat_local = patches.shape[1]
    layer_count = left_factors.shape[1]
    local_blocks = left_factors.shape[2]
    block_size = left_factors.shape[3]
    all_blocks = local_blocks * tensor_width
    fold_ratio = block_size // all_blocks
    model_width = feat_local * tensor_width
    sixth_rows = tok_rows // 6
    leading = 2 * sixth_rows
    critic_ids = jnp.arange(4, dtype=jnp.int32)
    named_by = (
        (critic_pairs[:, 0:1] == critic_ids[None, :])
        | (critic_pairs[:, 1:2] == critic_ids[None, :])
    ).astype(jnp.int32)
    ranking = jnp.cumsum(named_by, axis=0) - 1
    wide_ids = critic_ids[None, :] < 2
    slot_width = 3 * sixth_rows
    spilled = wide_ids & (ranking >= 3 * sixth_rows)
    destination = jnp.where(spilled, critic_ids[None, :] + 2, critic_ids[None, :])
    slot_index = jnp.where(spilled, ranking - sixth_rows, ranking)
    flat_slot = destination * slot_width + slot_index
    chosen = jnp.take_along_axis(flat_slot, critic_pairs, axis=1)
    slot_total = sections * slot_width
    row_ids = jnp.broadcast_to(jnp.arange(tok_rows, dtype=jnp.int32)[:, None], chosen.shape)
    source_row = (
        jnp.full((slot_total,), tok_rows, jnp.int32).at[chosen.reshape(-1)].set(row_ids.reshape(-1))
    )
    send_patch = (
        patches.at[source_row]
        .get(mode="fill", fill_value=0)
        .reshape(sections, slot_width, local_blocks, block_size)
    )
    send_target = (
        teacher.at[source_row]
        .get(mode="fill", fill_value=0)
        .reshape(sections, slot_width, local_blocks, block_size)
    )
    recv_patch, recv_target = (
        lax.all_to_all(send_patch, "section", split_axis=0, concat_axis=0, tiled=True),
        lax.all_to_all(send_target, "section", split_axis=0, concat_axis=0, tiled=True),
    )
    residuals = [
        recv_patch[:, :leading].reshape(-1, local_blocks, block_size).astype(jnp.float32),
        recv_patch[:, leading:].reshape(-1, local_blocks, block_size).astype(jnp.float32),
    ]
    targets = [
        recv_target[:, :leading].reshape(-1, local_blocks, block_size).astype(jnp.float32),
        recv_target[:, leading:].reshape(-1, local_blocks, block_size).astype(jnp.float32),
    ]
    native = (left_factors[0], right_factors[0], norm_gains[0])
    borrowed = shifted((left_factors, right_factors, norm_gains), "section", 2)
    is_wide = lax.axis_index("section") < 2
    second = (
        jnp.where(is_wide, left_factors, borrowed[0])[0],
        jnp.where(is_wide, right_factors, borrowed[1])[0],
        jnp.where(is_wide, norm_gains, borrowed[2])[0],
    )
    left_sets = (native[0], second[0])
    right_sets = (native[1], second[1])
    gain_sets = (
        native[2].astype(jnp.float32).reshape(layer_count + 1, local_blocks, block_size),
        second[2].astype(jnp.float32).reshape(layer_count + 1, local_blocks, block_size),
    )
    stored = []
    for layer_index in range(layer_count):
        gain_pair = [gain_sets[0][layer_index], gain_sets[1][layer_index]]
        factors, normed = norm_pair(residuals, gain_pair, model_width)
        normed = [normed[member].astype(jnp.bfloat16) for member in range(2)]
        first_out = [
            jnp.einsum(
                "nki,kij->nkj",
                normed[member],
                left_sets[member][layer_index],
                preferred_element_type=jnp.float32,
            ).astype(jnp.bfloat16)
            for member in range(2)
        ]
        permuted = (
            lax.all_to_all(first_out[0], "tensor", split_axis=2, concat_axis=1, tiled=True),
            lax.all_to_all(first_out[1], "tensor", split_axis=2, concat_axis=1, tiled=True),
        )
        permuted = [
            permuted[member].reshape(
                permuted[member].shape[0], all_blocks, local_blocks, fold_ratio
            )
            for member in range(2)
        ]
        right_quads = [
            right_sets[member][layer_index].reshape(
                local_blocks, fold_ratio, all_blocks, block_size
            )
            for member in range(2)
        ]
        mixture = [
            jnp.einsum(
                "nkmp,mpkl->nml",
                permuted[member],
                right_quads[member],
                preferred_element_type=jnp.float32,
            )
            for member in range(2)
        ]
        stored.append((residuals, factors, normed, permuted, mixture, right_quads, gain_pair))
        residuals = [residuals[member] + gelu_value(mixture[member]) for member in range(2)]
    final_gains = [gain_sets[0][layer_count], gain_sets[1][layer_count]]
    factors, outputs = norm_pair(residuals, final_gains, model_width)
    gradients = norm_back_pair(
        residuals,
        factors,
        final_gains,
        [outputs[member] - targets[member] for member in range(2)],
        [jnp.zeros_like(residuals[member]) for member in range(2)],
        model_width,
    )
    left_terms = []
    right_terms = []
    for layer_index in range(layer_count - 1, -1, -1):
        inputs, factors, normed, permuted, mixture, right_quads, gain_pair = stored[layer_index]
        slopes = [
            (gradients[member] * gelu_slope(mixture[member])).astype(jnp.bfloat16)
            for member in range(2)
        ]
        right_grad = [
            jnp.einsum(
                "nkmp,nml->mpkl",
                permuted[member],
                slopes[member],
                preferred_element_type=jnp.float32,
            ).reshape(local_blocks, block_size, block_size)
            for member in range(2)
        ]
        back_moved = [
            jnp.einsum(
                "nml,mpkl->nkmp",
                slopes[member],
                right_quads[member],
                preferred_element_type=jnp.float32,
            )
            .astype(jnp.bfloat16)
            .reshape(slopes[member].shape[0], all_blocks, local_blocks * fold_ratio)
            for member in range(2)
        ]
        arrived = (
            lax.all_to_all(back_moved[0], "tensor", split_axis=1, concat_axis=2, tiled=True),
            lax.all_to_all(back_moved[1], "tensor", split_axis=1, concat_axis=2, tiled=True),
        )
        left_grad = [
            jnp.einsum(
                "nki,nkj->kij", normed[member], arrived[member], preferred_element_type=jnp.float32
            )
            for member in range(2)
        ]
        grad_normed = [
            jnp.einsum(
                "nkj,kij->nki",
                arrived[member],
                left_sets[member][layer_index],
                preferred_element_type=jnp.float32,
            )
            for member in range(2)
        ]
        gradients = norm_back_pair(inputs, factors, gain_pair, grad_normed, gradients, model_width)
        layer_left = jnp.stack(left_grad)
        layer_right = jnp.stack(right_grad)
        layer_left, layer_right = (
            lax.psum(layer_left.astype(jnp.bfloat16), "dp").astype(jnp.float32),
            lax.psum(layer_right.astype(jnp.bfloat16), "dp").astype(jnp.float32),
        )
        left_terms.insert(0, layer_left)
        right_terms.insert(0, layer_right)
    left_stack = jnp.stack(left_terms)
    right_stack = jnp.stack(right_terms)
    repaid = (
        shifted(left_stack[:, 1].astype(jnp.bfloat16), "section", -2).astype(jnp.float32),
        shifted(right_stack[:, 1].astype(jnp.bfloat16), "section", -2).astype(jnp.float32),
    )
    is_wide = lax.axis_index("section") < 2
    left_total = left_stack[:, 0] + jnp.where(is_wide, left_stack[:, 1] + repaid[0], 0.0)
    right_total = right_stack[:, 0] + jnp.where(is_wide, right_stack[:, 1] + repaid[1], 0.0)
    grad_factor = 1.0 / math.sqrt(2 * tok_rows * sections * replicas)
    returned = [
        gradients[member].astype(jnp.bfloat16).reshape(sections, -1, local_blocks, block_size)
        for member in range(2)
    ]
    back_lead, back_trail = (
        lax.all_to_all(returned[0], "section", split_axis=0, concat_axis=0, tiled=True),
        lax.all_to_all(returned[1], "section", split_axis=0, concat_axis=0, tiled=True),
    )
    gathered = jnp.concatenate((back_lead, back_trail), axis=1).reshape(
        slot_total, local_blocks, block_size
    )
    combined = (
        gathered[chosen[:, 0]].astype(jnp.float32) + gathered[chosen[:, 1]].astype(jnp.float32)
    ) * 0.5
    d_patches = combined.astype(jnp.bfloat16).reshape(tok_rows, feat_local)
    return (d_patches, (left_total * grad_factor)[None], (right_total * grad_factor)[None])


VMEM_LIMIT = 60 * 1024 * 1024
CHUNKS = 8
TOGETHER = 4
PARTS = 4
SMALL = (16, 128)
AXES = ("section", "tensor", "dp")


def planes_fit(mesh):
    sections = mesh.shape["section"]
    paired = mesh.shape["dp"] == 2 and sections & (sections - 1) == 0
    return paired and mesh.shape["tensor"] == sections


def inner_dot(left, right, left_dim, right_dim):
    return lax.dot_general(
        left,
        right,
        (((left_dim,), (right_dim,)), ((), ())),
        preferred_element_type=jnp.float32,
    )


def fold_rows(values):
    return jnp.sum(values.reshape(values.shape[0] // 8, 8, values.shape[1]), axis=0)


def block_rows(block, size):
    return pl.ds(pl.multiple_of(block * size, size), size)


def column(gain_ref, block, at, slots):
    if len(gain_ref.shape) == 3:
        gains = gain_ref[block // gain_ref.shape[2]]
        return jnp.broadcast_to(gains[:, at : at + 1], (gains.shape[0], slots))
    picked = lax.broadcasted_iota(jnp.int32, (gain_ref.shape[1], slots), 0) == block
    return inner_dot(gain_ref[...], picked.astype(jnp.bfloat16), 1, 0)


def chunk_copy(source, target, sems, chunk):
    rows = target.shape[0] // CHUNKS
    at = pl.ds(pl.multiple_of(chunk * rows, rows), rows)
    return pltpu.make_async_copy(source.at[at], target.at[at], sems.at[chunk])


def start_chunks(source, target, sems):
    for chunk in range(CHUNKS):
        chunk_copy(source, target, sems, chunk).start()


def wait_chunks(source, target, sems):
    for chunk in range(CHUNKS):
        chunk_copy(source, target, sems, chunk).wait()


def factor_copies(parts, layer, held, sems, side):
    count = parts[0].shape[0]
    return [
        pltpu.make_async_copy(
            ref.at[:, layer, side], held.at[pl.ds(at * count, count), side], sems.at[side, at]
        )
        for at, ref in enumerate(parts)
    ]


def gradient_copies(held, parts, sems, side):
    count = parts[0].shape[0]
    return [
        pltpu.make_async_copy(
            held.at[pl.ds(at * count, count), side], ref.at[:, side], sems.at[side, at]
        )
        for at, ref in enumerate(parts)
    ]


def by_chunk(blocks, step, carry, before=None, after=None):
    per_chunk = blocks // CHUNKS

    def few(start, first, carry):
        stores = []
        for at in range(TOGETHER):
            made, carry = step(start + at, first + at, carry)
            stores += made
        for ref, index, value in stores:
            ref[index] = value
        return carry

    def one(chunk, carry):
        if before is not None:
            before(chunk)
        for at in range(0, per_chunk, TOGETHER):
            carry = few(chunk * per_chunk + at, at, carry)
        if after is not None:
            after(chunk)
        return carry

    return lax.fori_loop(0, CHUNKS, one, carry)


def forward_kernel(first, layer, inputs, table_ref, sums_ref, gain_ref, *refs):
    sources, refs = refs[:inputs], refs[inputs:]
    parts, sources = sources[:PARTS], sources[PARTS:]
    out_ref, u_ref, z_ref, slope_ref, scale_ref, next_ref = refs[:6]
    raw, h, w, u, z, slope, mid, in_sems, w_sems, out_sems = refs[6:]
    features, slots = h.shape
    size = w.shape[-1]
    chunk_blocks = w.shape[2]
    blocks = features // size
    fold = size // blocks

    left_in = factor_copies(parts, layer, w, w_sems, 0)
    right_in = factor_copies(parts, layer, w, w_sems, 1)
    if first:
        start_chunks(sources[0], raw, in_sems)
        for copy in left_in + right_in:
            copy.start()

        def squares(block, _, total):
            rows = block_rows(block, size)
            part = raw[rows, :].astype(jnp.float32)
            return [(h, (rows, slice(None)), part)], total + fold_rows(part * part)

        total = by_chunk(
            blocks,
            squares,
            jnp.zeros((8, slots), jnp.float32),
            lambda chunk: chunk_copy(sources[0], raw, in_sems, chunk).wait(),
        )
    else:
        for copy in left_in:
            copy.start()
        start_chunks(sources[0], h, in_sems)
        for copy in right_in:
            copy.start()
        total = sums_ref[...]
    scale = lax.rsqrt(jnp.sum(total, axis=0, keepdims=True) / features + EPSILON)
    scale_ref[...] = jnp.broadcast_to(scale, scale_ref.shape)
    for copy in left_in:
        copy.wait()

    def arrive(chunk):
        if not first:
            chunk_copy(sources[0], h, in_sems, chunk).wait()

    def left(block, nth, carry):
        rows = block_rows(block, size)
        place = table_ref[0, block]
        normed = (h[rows, :] * scale * column(gain_ref, block, nth, slots)).astype(jnp.bfloat16)
        weight = w[place // chunk_blocks, 0, place % chunk_blocks]
        first_out = inner_dot(weight, normed, 0, 0)
        at = (rows, slice(None))
        return [(u, at, normed), (mid, at, first_out)], carry

    def leave_left(chunk):
        chunk_copy(u, u_ref, out_sems.at[0], chunk).start()

    by_chunk(blocks, left, 0, arrive, leave_left)
    for copy in right_in:
        copy.wait()

    def right(block, nth, total):
        rows = block_rows(block, size)
        place = table_ref[0, block]
        moved = [mid[pl.ds(q * blocks + block, blocks, stride=size), :] for q in range(fold)]
        moved = jnp.concatenate(moved, axis=0).astype(jnp.bfloat16)
        weight = w[place // chunk_blocks, 1, place % chunk_blocks]
        mixture = inner_dot(weight, moved, 0, 0)
        squared = mixture * mixture
        tangent = jnp.tanh(mixture * (TANH_SLOPE + (TANH_SLOPE * CUBIC_TERM) * squared))
        half = 0.5 + 0.5 * tangent
        following = h[rows, :] + mixture * half
        steep = half + mixture * (1.0 - tangent * tangent) * (
            0.5 * TANH_SLOPE + (1.5 * TANH_SLOPE * CUBIC_TERM) * squared
        )
        at = (rows, slice(None))
        stores = [(z, at, moved), (h, at, following), (slope, at, steep.astype(jnp.bfloat16))]
        return stores, total + fold_rows(following * following)

    leaving = ((h, out_ref, 1), (z, z_ref, 2), (slope, slope_ref, 3))

    def leave_right(chunk):
        for source, target, at in leaving:
            chunk_copy(source, target, out_sems.at[at], chunk).start()

    next_ref[...] = by_chunk(blocks, right, jnp.zeros((8, slots), jnp.float32), None, leave_right)
    for source, target, at in ((u, u_ref, 0),) + leaving:
        wait_chunks(source, target, out_sems.at[at])


def backward_kernel(turning, last, home_row, layer, inputs, table_ref, scale_ref, gain_ref, end_gain_ref, *refs):
    sources, refs = refs[:inputs], refs[inputs:]
    slope_ref, z_ref, u_ref = sources[:3]
    parts, sources = sources[3 : 3 + PARTS], sources[3 + PARTS :]
    out_ref, own_grad, peer_grad = refs[:3]
    g, slope, z, u, h, w, gw, mid, top, goal = refs[3:13]
    in_sems, w_sems, out_sems, gw_sems = refs[13:]
    features, slots = g.shape
    size = w.shape[-1]
    chunk_blocks = w.shape[2]
    blocks = features // size
    fold = size // blocks

    left_in = factor_copies(parts, layer, w, w_sems, 0)
    right_in = factor_copies(parts, layer, w, w_sems, 1)
    g_ref, h_ref = sources[:2]
    if turning:
        for chunk in range(CHUNKS):
            chunk_copy(g_ref, top, in_sems.at[0], chunk).start()
            chunk_copy(sources[2], goal, in_sems.at[5], chunk).start()
    for copy in right_in:
        copy.start()
    for chunk in range(CHUNKS):
        if not turning:
            chunk_copy(g_ref, g, in_sems.at[0], chunk).start()
        chunk_copy(slope_ref, slope, in_sems.at[1], chunk).start()
        chunk_copy(z_ref, z, in_sems.at[2], chunk).start()
    for copy in left_in:
        copy.start()
    for chunk in range(CHUNKS):
        chunk_copy(u_ref, u, in_sems.at[3], chunk).start()
        chunk_copy(h_ref, h, in_sems.at[4], chunk).start()

    if turning:
        zero = jnp.zeros((8, slots), jnp.float32)

        def sums(block, nth, totals):
            rows = block_rows(block, size)
            part = top[rows, :]
            scaled = part * column(end_gain_ref, block, nth, slots)
            return [], (
                totals[0] + fold_rows(part * part),
                totals[1] + fold_rows(scaled * scaled),
                totals[2] + fold_rows(scaled * goal[rows, :].astype(jnp.float32)),
            )

        def arrive_top(chunk):
            chunk_copy(g_ref, top, in_sems.at[0], chunk).wait()
            chunk_copy(sources[2], goal, in_sems.at[5], chunk).wait()

        totals = by_chunk(blocks, sums, (zero, zero, zero), arrive_top)
        squares, gained, crossed = [jnp.sum(total, axis=0, keepdims=True) for total in totals]
        end_scale = lax.rsqrt(squares / features + EPSILON)
        end_back = end_scale * end_scale * end_scale * (end_scale * gained - crossed) / features

    for copy in right_in:
        copy.wait()

    def arrive_right(chunk):
        if not turning:
            chunk_copy(g_ref, g, in_sems.at[0], chunk).wait()
        chunk_copy(slope_ref, slope, in_sems.at[1], chunk).wait()
        chunk_copy(z_ref, z, in_sems.at[2], chunk).wait()

    def right(block, nth, total):
        rows = block_rows(block, size)
        place, home = table_ref[0, block], table_ref[home_row, block]
        at = (place // chunk_blocks, 1, place % chunk_blocks)
        to = (home // chunk_blocks, 1, home % chunk_blocks)
        if turning:
            part = top[rows, :]
            factor = column(end_gain_ref, block, nth, slots)
            error = (part * end_scale * factor - goal[rows, :].astype(jnp.float32)) * factor
            gradient = end_scale * error - part * end_back
            stores = [(g, (rows, slice(None)), gradient)]
        else:
            gradient = g[rows, :]
            stores = []
        steep = (gradient * slope[rows, :].astype(jnp.float32)).astype(jnp.bfloat16)
        taken = z[rows, :]
        back = inner_dot(w[at], steep, 1, 0)
        stores.append((gw, to, inner_dot(taken, steep, 1, 1).astype(jnp.bfloat16)))
        stores.append((mid, (rows, slice(None)), back))
        return stores, total + fold_rows(taken.astype(jnp.float32) * back)

    total = by_chunk(blocks, right, jnp.zeros((8, slots), jnp.float32), arrive_right)
    right_out = gradient_copies(gw, (own_grad, peer_grad), gw_sems, 1)
    for copy in right_out:
        copy.start()
    for copy in left_in:
        copy.wait()
    scale = scale_ref[0:1, :]
    back = scale * scale * jnp.sum(total, axis=0, keepdims=True) / features

    def arrive_left(chunk):
        chunk_copy(u_ref, u, in_sems.at[3], chunk).wait()
        chunk_copy(h_ref, h, in_sems.at[4], chunk).wait()

    def left(block, nth, carry):
        rows = block_rows(block, size)
        place, home = table_ref[0, block], table_ref[home_row, block]
        at = (place // chunk_blocks, 0, place % chunk_blocks)
        to = (home // chunk_blocks, 0, home % chunk_blocks)
        arrived = [mid[pl.ds(q * blocks + block, blocks, stride=size), :] for q in range(fold)]
        arrived = jnp.concatenate(arrived, axis=0).astype(jnp.bfloat16)
        factor_grad = inner_dot(u[rows, :], arrived, 1, 1).astype(jnp.bfloat16)
        weighted = inner_dot(w[at], arrived, 1, 0) * column(gain_ref, block, nth, slots)
        ended = g[rows, :] + scale * weighted - h[rows, :].astype(jnp.float32) * back
        index = (rows, slice(None))
        stores = [(gw, to, factor_grad)]
        stores.append((u, index, ended.astype(jnp.bfloat16)) if last else (g, index, ended))
        return stores, carry

    ended = u if last else g
    by_chunk(
        blocks, left, 0, arrive_left, lambda chunk: chunk_copy(ended, out_ref, out_sems, chunk).start()
    )
    left_out = gradient_copies(gw, (own_grad, peer_grad), gw_sems, 0)
    for copy in left_out:
        copy.start()
    wait_chunks(ended, out_ref, out_sems)
    for copy in right_out + left_out:
        copy.wait()


def shape_of(shape, dtype):
    return jax.ShapeDtypeStruct(shape, dtype)


SMEM = pl.BlockSpec(memory_space=pltpu.SMEM)
INSIDE = pl.BlockSpec(memory_space=pltpu.VMEM)
OUTSIDE = pl.BlockSpec(memory_space=pl.ANY)


def run_forward(table, gain, sums, residual, weights, layer):
    first = residual.dtype == jnp.bfloat16
    whole = residual.shape
    sources = (*weights, residual)
    held = (PARTS * weights[0].shape[0],) + weights[0].shape[2:]
    out_shape = (
        shape_of(whole, jnp.float32),
        shape_of(whole, jnp.bfloat16),
        shape_of(whole, jnp.bfloat16),
        shape_of(whole, jnp.bfloat16),
        shape_of((8, whole[1]), jnp.float32),
        shape_of((8, whole[1]), jnp.float32),
    )
    return pl.pallas_call(
        lambda *refs: forward_kernel(first, layer, len(sources), *refs),
        in_specs=[SMEM, INSIDE, INSIDE] + [OUTSIDE] * len(sources),
        out_specs=[OUTSIDE] * 4 + [INSIDE] * 2,
        out_shape=out_shape,
        scratch_shapes=[
            pltpu.VMEM(whole if first else SMALL, jnp.bfloat16),
            pltpu.VMEM(whole, jnp.float32),
            pltpu.VMEM(held, jnp.bfloat16),
            pltpu.VMEM(whole, jnp.bfloat16),
            pltpu.VMEM(whole, jnp.bfloat16),
            pltpu.VMEM(whole, jnp.bfloat16),
            pltpu.VMEM(whole, jnp.float32),
            pltpu.SemaphoreType.DMA((CHUNKS,)),
            pltpu.SemaphoreType.DMA((2, PARTS)),
            pltpu.SemaphoreType.DMA((4, CHUNKS)),
        ],
        compiler_params=pltpu.CompilerParams(vmem_limit_bytes=VMEM_LIMIT),
        cost_estimate=pl.CostEstimate(
            flops=FORWARD_COST, bytes_accessed=20 * whole[0] * whole[1], transcendentals=0
        ),
        name="forward_layer",
    )(table, sums, gain, *sources)


def run_backward(table, gain, end_gain, scale, kept, weights, layer, sources, turning, last, home_row):
    whole = kept[0].shape
    sources = (*kept, *weights, *sources)
    held = (PARTS * weights[0].shape[0],) + weights[0].shape[2:]
    half = (held[0] // 2,) + held[1:]
    out_shape = [shape_of(whole, jnp.bfloat16 if last else jnp.float32)] + [shape_of(half, jnp.bfloat16)] * 2
    return pl.pallas_call(
        lambda *refs: backward_kernel(turning, last, home_row, layer, len(sources), *refs),
        in_specs=[SMEM] + [INSIDE] * 3 + [OUTSIDE] * len(sources),
        out_specs=[OUTSIDE] * len(out_shape),
        out_shape=out_shape,
        scratch_shapes=[
            pltpu.VMEM(whole, jnp.float32),
            pltpu.VMEM(whole, jnp.bfloat16),
            pltpu.VMEM(whole, jnp.bfloat16),
            pltpu.VMEM(whole, jnp.bfloat16),
            pltpu.VMEM(whole, jnp.bfloat16 if last else jnp.float32),
            pltpu.VMEM(held, jnp.bfloat16),
            pltpu.VMEM(held, jnp.bfloat16),
            pltpu.VMEM(whole, jnp.float32),
            pltpu.VMEM(whole if turning else SMALL, jnp.float32),
            pltpu.VMEM(whole if turning else SMALL, jnp.bfloat16),
            pltpu.SemaphoreType.DMA((6, CHUNKS)),
            pltpu.SemaphoreType.DMA((2, PARTS)),
            pltpu.SemaphoreType.DMA((CHUNKS,)),
            pltpu.SemaphoreType.DMA((2, PARTS)),
        ],
        compiler_params=pltpu.CompilerParams(vmem_limit_bytes=VMEM_LIMIT),
        cost_estimate=pl.CostEstimate(
            flops=BACKWARD_COST, bytes_accessed=30 * whole[0] * whole[1], transcendentals=0
        ),
        name="backward_layer",
    )(table, scale, gain, end_gain, *sources)


def join_kernel(rows, *refs):
    sources, whole, sems = refs[:-2], refs[-2], refs[-1]
    copies = [
        pltpu.make_async_copy(source.at[pl.ds(0, rows)], whole.at[pl.ds(at * rows, rows)], sems.at[at])
        for at, source in enumerate(sources)
    ]
    for copy in copies:
        copy.start()
    for copy in copies:
        copy.wait()


def joined(parts, rows=None):
    rows = parts[0].shape[0] if rows is None else rows
    whole = shape_of((rows * len(parts),) + parts[0].shape[1:], parts[0].dtype)
    return pl.pallas_call(
        lambda *refs: join_kernel(rows, *refs),
        in_specs=[OUTSIDE] * len(parts),
        out_specs=INSIDE,
        out_shape=whole,
        scratch_shapes=[pltpu.SemaphoreType.DMA((len(parts),))],
        compiler_params=pltpu.CompilerParams(vmem_limit_bytes=VMEM_LIMIT),
        cost_estimate=pl.CostEstimate(
            flops=0, bytes_accessed=4 * math.prod(whole.shape), transcendentals=0
        ),
        name="join",
    )(*parts)


def order_kernel(ranges, place_ref, *refs):
    sources, whole, sems = refs[:-2], refs[-2], refs[-1]
    copies = []
    for distance, source in enumerate(sources):
        row = 0
        for start, count in ranges:
            target = whole.at[place_ref[0] ^ distance, pl.ds(row, count)]
            copies.append(pltpu.make_async_copy(source.at[pl.ds(start, count)], target, sems.at[len(copies)]))
            row += count
    for copy in copies:
        copy.start()
    for copy in copies:
        copy.wait()


def by_section(place, parts, ranges):
    rows = sum(count for _, count in ranges)
    whole = shape_of((len(parts), rows) + parts[0].shape[1:], parts[0].dtype)
    return pl.pallas_call(
        lambda *refs: order_kernel(ranges, *refs),
        in_specs=[SMEM] + [OUTSIDE] * len(parts),
        out_specs=INSIDE,
        out_shape=whole,
        scratch_shapes=[pltpu.SemaphoreType.DMA((len(parts) * len(ranges),))],
        compiler_params=pltpu.CompilerParams(vmem_limit_bytes=VMEM_LIMIT),
        cost_estimate=pl.CostEstimate(
            flops=0, bytes_accessed=4 * math.prod(whole.shape), transcendentals=0
        ),
        name="by_section",
    )(place, *parts)


def sum_kernel(terms, inputs, *refs):
    sources, outs = refs[:inputs], refs[inputs:]
    for group in range(inputs // terms):
        mine = sources[group * terms : (group + 1) * terms]
        for at in range(mine[0].shape[0]):
            total = sum(ref[at].astype(jnp.float32) for ref in mine).astype(jnp.bfloat16)
            if len(outs) > 1:
                outs[at][group] = total
            else:
                outs[0][at, group] = total


def run_sum(groups, parts, apart=True):
    flat = [term.reshape(parts, -1, term.shape[-1]) for terms in groups for term in terms]
    _, rows, lanes = flat[0].shape
    steps = 2
    if apart:
        out_shape = [shape_of((len(groups), rows, lanes), jnp.bfloat16)] * parts
        out_specs = [pl.BlockSpec((len(groups), rows // steps, lanes), lambda i: (0, i, 0))] * parts
    else:
        out_shape = [shape_of((parts, len(groups), rows, lanes), jnp.bfloat16)]
        out_specs = [pl.BlockSpec((parts, len(groups), rows // steps, lanes), lambda i: (0, 0, i, 0))]
    sums = pl.pallas_call(
        lambda *refs: sum_kernel(len(groups[0]), len(flat), *refs),
        grid=(steps,),
        in_specs=[pl.BlockSpec((parts, rows // steps, lanes), lambda i: (0, i, 0))] * len(flat),
        out_specs=out_specs,
        out_shape=out_shape,
        compiler_params=pltpu.CompilerParams(vmem_limit_bytes=VMEM_LIMIT),
        cost_estimate=pl.CostEstimate(
            flops=flat[0].size * len(flat), bytes_accessed=2 * flat[0].size * (len(flat) + 1), transcendentals=0
        ),
        name="sum",
    )(*flat)
    return [out.reshape(-1, lanes) for out in sums] if apart else sums[0].reshape(parts, -1, lanes)


def pieces_kernel(chunk, place_ref, order_ref, left_ref, right_ref, gain_ref, *refs):
    outs, (held, left_sem, sems) = refs[:-3], refs[-3:]
    layer_count, half, size = held.shape[:3]
    first = place_ref[2] * half
    lefts = pltpu.make_async_copy(left_ref.at[:, pl.ds(first, half)], held, left_sem.at[0])
    lefts.start()
    copies = []
    turns = []
    for distance, out in enumerate(outs):
        start = (place_ref[0] ^ distance) * chunk
        row = 0
        for layer in range(layer_count):
            for inside in range(chunk):
                turns.append((layer, start + inside, out, row))
                row += size
            for inside in range(chunk):
                source = right_ref.at[layer, first + start + inside]
                copies.append((source, out.at[pl.ds(row, size)]))
                row += size
        copies.append((gain_ref, out.at[pl.ds(row, gain_ref.shape[0])]))
    copies = [
        pltpu.make_async_copy(source, target, sems.at[at]) for at, (source, target) in enumerate(copies)
    ]
    for copy in copies:
        copy.start()
    lefts.wait()
    for layer, block, out, row in turns:
        turned = inner_dot(held[layer, block], order_ref[...], 1, 0)
        out[pl.ds(row, size), :] = turned.astype(jnp.bfloat16)
    for copy in copies:
        copy.wait()


def factor_pieces(place, order, left, right, gain_rows, chunk, width):
    layer_count, blocks, size = left.shape[:3]
    rows = layer_count * 2 * chunk * size + gain_rows.shape[0]
    return pl.pallas_call(
        lambda *refs: pieces_kernel(chunk, *refs),
        in_specs=[SMEM, INSIDE] + [OUTSIDE] * 3,
        out_specs=[INSIDE] * width,
        out_shape=[shape_of((rows, size), jnp.bfloat16)] * width,
        scratch_shapes=[
            pltpu.VMEM((layer_count, blocks // 2, size, size), jnp.bfloat16),
            pltpu.SemaphoreType.DMA((1,)),
            pltpu.SemaphoreType.DMA((width * (layer_count * chunk + 1),)),
        ],
        compiler_params=pltpu.CompilerParams(vmem_limit_bytes=VMEM_LIMIT),
        cost_estimate=pl.CostEstimate(flops=left.size * size, bytes_accessed=4 * left.size, transcendentals=0),
        name="pieces",
    )(place, order, left, right, gain_rows)


def choice(pairs, critic, slots):
    rows = pairs.shape[0]
    named = (pairs[:, 0:1] == critic) | (pairs[:, 1:2] == critic)
    named = jnp.broadcast_to(named.astype(jnp.float32), (rows, slots))
    before = lax.broadcasted_iota(jnp.int32, (rows, rows), 1) < lax.broadcasted_iota(jnp.int32, (rows, rows), 0)
    rank = inner_dot(before.astype(jnp.bfloat16), named.astype(jnp.bfloat16), 1, 0)
    at = lax.broadcasted_iota(jnp.int32, (rows, slots), 1).astype(jnp.float32)
    return jnp.where(rank == at, named, 0.0).astype(jnp.bfloat16)


def pick_kernel(pairs_ref, values_ref, out_ref):
    width, features, slots = out_ref.shape
    pairs = pairs_ref[...]
    chosen = [choice(pairs, critic, slots) for critic in range(width)]
    step = 512
    for start in range(0, features, step):
        part = values_ref[:, pl.ds(start, step)]
        for k in range(width):
            out_ref[k, pl.ds(start, step), :] = inner_dot(part, chosen[k], 0, 0).astype(jnp.bfloat16)


def run_pick(pairs, values, width, slots):
    rows, features = values.shape
    return pl.pallas_call(
        pick_kernel,
        in_specs=[INSIDE] * 2,
        out_specs=INSIDE,
        out_shape=shape_of((width, features, slots), jnp.bfloat16),
        compiler_params=pltpu.CompilerParams(vmem_limit_bytes=VMEM_LIMIT),
        cost_estimate=pl.CostEstimate(
            flops=2 * rows * features * slots * width, bytes_accessed=8 * rows * features, transcendentals=0
        ),
        name="pick",
    )(pairs, values)


def combine_kernel(pairs_ref, came_ref, out_ref):
    width, features, slots = came_ref.shape
    pairs = pairs_ref[...]
    chosen = [choice(pairs, critic, slots) for critic in range(width)]
    step = 512
    for start in range(0, features, step):
        total = sum(inner_dot(chosen[k], came_ref[k, pl.ds(start, step), :], 1, 1) for k in range(width))
        out_ref[:, pl.ds(start, step)] = (0.5 * total).astype(jnp.bfloat16)


def run_combine(pairs, came):
    rows = pairs.shape[0]
    return pl.pallas_call(
        combine_kernel,
        in_specs=[INSIDE] * 2,
        out_specs=INSIDE,
        out_shape=shape_of((rows, came.shape[1]), jnp.bfloat16),
        compiler_params=pltpu.CompilerParams(vmem_limit_bytes=VMEM_LIMIT),
        cost_estimate=pl.CostEstimate(
            flops=2 * rows * came.size, bytes_accessed=4 * came.size, transcendentals=0
        ),
        name="combine",
    )(pairs, came)


FORWARD_COST = 4_000_000_000
BACKWARD_COST = 5_000_000_000


def assemble_kernel(layers, factor, place_ref, order_ref, *refs):
    count = 2 * len(layers)
    sources, (left_ref, right_ref) = refs[:count], refs[count : count + 2]
    held, wide = refs[count + 2 : 2 * count + 2], refs[2 * count + 2 : 3 * count + 2]
    in_sems, out_sems = refs[3 * count + 2 :]
    origin, core = place_ref[0] ^ place_ref[1], place_ref[2]
    order = order_ref[...]
    arrivals = [
        pltpu.make_async_copy(source, held[at], in_sems.at[at]) for at, source in enumerate(sources)
    ]
    for copy in arrivals:
        copy.start()
    leaving = []
    for at in range(count):
        arrivals[at].wait()
        half = core if at % 2 == 0 else 1 - core
        width, _, _, chunk = held[at].shape[:4]
        for k in range(width):
            start = (half * width + (origin ^ k if at < 2 else k)) * chunk
            for inside, layer in enumerate(layers[at // 2]):
                for block in range(chunk):
                    left = inner_dot(held[at][k, inside, 0, block], order, 1, 1)
                    wide[at][k, inside, 0, block] = left * factor
                wide[at][k, inside, 1] = held[at][k, inside, 1].astype(jnp.float32) * factor
                for which, target in enumerate((left_ref, right_ref)):
                    copy = pltpu.make_async_copy(
                        wide[at].at[k, inside, which],
                        target.at[layer, pl.ds(start, chunk)],
                        out_sems.at[len(leaving)],
                    )
                    copy.start()
                    leaving.append(copy)
    for copy in leaving:
        copy.wait()


def run_assemble(place, order, pieces, layers, factor):
    piece = pieces[0].shape
    layer_count = sum(len(group) for group in layers)
    out = shape_of((layer_count, 2 * piece[0] * piece[3]) + piece[4:], jnp.float32)
    return pl.pallas_call(
        lambda *refs: assemble_kernel(layers, factor, *refs),
        in_specs=[SMEM, INSIDE] + [OUTSIDE] * len(pieces),
        out_specs=[OUTSIDE] * 2,
        out_shape=[out] * 2,
        scratch_shapes=[pltpu.VMEM(part.shape, jnp.bfloat16) for part in pieces]
        + [pltpu.VMEM(part.shape, jnp.float32) for part in pieces]
        + [
            pltpu.SemaphoreType.DMA((len(pieces),)),
            pltpu.SemaphoreType.DMA((4 * layer_count * piece[0],)),
        ],
        compiler_params=pltpu.CompilerParams(vmem_limit_bytes=VMEM_LIMIT),
        cost_estimate=pl.CostEstimate(flops=0, bytes_accessed=4 * math.prod(out.shape) * 3, transcendentals=0),
        name="assemble",
    )(place, order, *pieces)


def plane_routes(width, replicas):
    bits = width.bit_length() - 1
    orders = [[(step + d) % bits for step in range(bits)] for d in range(replicas)]
    every = [(s, t, d) for s in range(width) for t in range(width) for d in range(replicas)]

    def route(move):
        def index(s, t, d):
            return (s * width + t) * replicas + d

        return [(index(*place), index(*move(*place))) for place in every]

    ranks = [[0] * width for _ in range(replicas)]
    for d in range(replicas):
        for r in range(width):
            ranks[d][sum(((r >> at) & 1) << orders[d][at] for at in range(bits))] = r
    return {
        "across": [route(lambda s, t, d, at=at: (s ^ (1 << orders[d][at]), t, d)) for at in range(bits)],
        "cores": route(lambda s, t, d: (s, t, 1 - d)),
        "sections": [route(lambda s, t, d, k=k: (s ^ k, t, d)) for k in range(width)],
        "homes": [route(lambda s, t, d, j=j: (t, t ^ s ^ j, d)) for j in range(width)],
    }, ranks


def plane_shards(patches, teacher, critic_pairs, left_factors, right_factors, norm_gains):
    width = lax.axis_size("section")
    replicas = lax.axis_size("dp")
    tok_rows, feat_local = patches.shape
    layer_count, local_blocks, size = left_factors.shape[1:4]
    blocks = feat_local * width // size
    wide = 2 * tok_rows // 3
    chunk = local_blocks // (replicas * width)
    layer_rows = 2 * chunk * size
    routes, ranks = plane_routes(width, replicas)
    section = lax.axis_index("section")
    tensor = lax.axis_index("tensor")
    core = lax.axis_index("dp")
    place = jnp.stack([section, tensor, core]).astype(jnp.int32)
    tie = lax.optimization_barrier

    def move(value, route):
        return lax.ppermute(value, AXES, route)

    def move_all(values, name):
        return [move(value, route) for value, route in zip(values, routes[name])]

    def send(values, name):
        return [values[0]] + [move(values[k], routes[name][k]) for k in range(1, width)]

    def gather_two(pair):
        return pair, move(pair, routes["across"][1]), move(pair, routes["cores"])

    def gather_three(pair, other, peer):
        return [pair, other, peer, move(other, routes["cores"])]

    def as_weights(parts):
        return [part.reshape(2 * width, -1, 2, chunk, size, size) for part in parts]

    block = jnp.arange(blocks, dtype=jnp.int32)
    inside = block % local_blocks
    replica = inside // (width * chunk)
    part = (replica != core).astype(jnp.int32)
    distance = section ^ ((inside // chunk) % width)
    quarter = block // local_blocks
    rank = jnp.array(ranks, jnp.int32)[replica, distance]
    table = jnp.stack(
        [
            ((part * width + index) * width + piece) * chunk + inside % chunk
            for index, piece in (
                (rank, quarter),
                (distance, quarter),
                (distance, tensor ^ section ^ distance ^ quarter),
            )
        ]
    ).astype(jnp.int32)

    def to_planes(value):
        return lax.all_to_all(value, "tensor", split_axis=0, concat_axis=0, tiled=True)

    def to_sections(value):
        return lax.all_to_all(value, "section", split_axis=0, concat_axis=0, tiled=True)

    half_layers = layer_count // 2
    groups = [tuple(range(half_layers)), tuple(range(half_layers, layer_count))]
    fold = size // blocks
    columns = jnp.arange(size)
    order = (columns[:, None] == (columns % blocks) * fold + columns // blocks).astype(jnp.bfloat16)
    gain_rows = norm_gains[0].reshape(-1, size)
    patch_sent = run_pick(critic_pairs, patches, width, wide)
    patch_sent, left, right, teacher = tie((patch_sent, left_factors[0], right_factors[0], teacher))
    patch_came = to_planes(patch_sent).reshape(-1, wide)
    pieces = factor_pieces(place, order, left, right, gain_rows, chunk, width)
    spread = send(pieces, "sections")
    cut, end = half_layers * layer_rows, layer_count * layer_rows
    first = by_section(place, spread, [(0, cut), (end, gain_rows.shape[0])])
    second = by_section(place, spread, [(cut, end - cut)])
    target_sent = run_pick(critic_pairs, teacher, width, wide)
    patch_came, first, second, target_sent = tie((patch_came, first, second, target_sent))
    first = to_planes(first)
    first, second = tie((first, second))
    second = to_planes(second)
    lowest = [first[:, at * layer_rows : (at + 1) * layer_rows] for at in range(half_layers)]
    beside = [move(value, routes["across"][0]) for value in lowest[:2]]
    gains = first[:, cut:].reshape(width, layer_count + 1, local_blocks, size)
    gains = gains.transpose(1, 3, 0, 2).reshape(layer_count + 1, size, blocks)
    end_gain = gains[layer_count].reshape(size, CHUNKS, blocks // CHUNKS).transpose(1, 0, 2)
    end_gain = end_gain.astype(jnp.float32)
    lowest, beside, gains, end_gain = tie((lowest, beside, gains, end_gain))
    flying = {0: gather_two(joined([lowest[0], beside[0]]))}
    flying, second, target_sent = tie((flying, second, target_sent))
    for layer in range(half_layers, layer_count):
        at = (layer - half_layers) * layer_rows
        lowest.append(second[:, at : at + layer_rows])
    target = to_planes(target_sent).reshape(-1, wide)
    weights = [as_weights(gather_three(*flying.pop(0)))]
    flying[1] = gather_two(joined([lowest[1], beside[1]]))
    steps = {2: (lowest[2], move(lowest[2], routes["across"][0]))}
    weights, flying, steps = tie((weights, flying, steps))

    residual = patch_came
    sums = jnp.zeros((8, wide), jnp.float32)
    stored = []
    for layer in range(layer_count):
        ahead = {}
        if layer + 1 < layer_count:
            ahead["weights"] = gather_three(*flying.pop(layer + 1))
        if layer + 2 < layer_count:
            ahead["two"] = gather_two(joined(list(steps.pop(layer + 2))))
        if layer + 3 < layer_count:
            ahead["one"] = (lowest[layer + 3], move(lowest[layer + 3], routes["across"][0]))
        following, u, z, slope, scale, sums = run_forward(
            table, gains[layer], sums, residual, weights[layer], 0
        )
        stored.append(((slope, z, u), scale, residual))
        residual, sums, ahead = tie((following, sums, ahead))
        if layer + 1 < layer_count:
            weights.append(as_weights(ahead["weights"]))
        if layer + 2 < layer_count:
            flying[layer + 2] = ahead["two"]
        if layer + 3 < layer_count:
            steps[layer + 3] = ahead["one"]
        if layer == layer_count - 2:
            residual, sums, target = tie((residual, sums, target))

    def core_sum(mine, other):
        return (mine, move(other, routes["cores"]))

    def plane_sum(mine, other):
        return send(run_sum([(mine, other)], width), "sections")

    def both_halves(whole):
        pair = (whole, move(whole, routes["cores"]))
        return [part.reshape(width, -1, 2, chunk, size, size) for part in pair]

    steps = (core_sum, plane_sum)
    gradient = residual
    underway = []
    for layer in range(layer_count - 1, -1, -1):
        turning = layer == layer_count - 1
        last = layer == 0
        kept, scale, inputs = stored[layer]
        sources = (gradient, inputs, target) if turning else (gradient, inputs)
        underway = [(at + 1, steps[at](*state)) if at < len(steps) else (at, state) for at, state in underway]
        gradient, mine, other = run_backward(
            table,
            gains[layer],
            end_gain,
            scale,
            kept,
            weights[layer],
            0,
            sources,
            turning,
            last,
            2 if layer < half_layers else 1,
        )
        gradient, mine, other, states = tie((gradient, mine, other, [state for _, state in underway]))
        underway = [(at, state) for (at, _), state in zip(underway, states)]
        underway.append((0, (mine, other)))

    returned = to_planes(gradient.reshape(width, feat_local, wide))
    ended = [steps[at](*state) if at < len(steps) else state for at, state in underway][::-1]
    others = run_sum(ended[half_layers:], width, apart=False)
    ended, others = tie((ended, others))
    payload = run_sum([ended[0]], width)
    payload, others = tie((payload, others))
    ended[0] = send(payload, "sections")
    others = to_planes(others)
    home = run_sum(ended[:half_layers], width)
    home, returned, others = tie((home, returned, others))
    home = move_all(home, "homes")
    d_patches = run_combine(critic_pairs, returned)
    others = to_sections(others)
    d_patches, home, others = tie((d_patches, home, others))
    homes_of = both_halves(joined(home)) + both_halves(others)
    grad_factor = 1.0 / math.sqrt(2 * tok_rows * width * replicas)
    grad_left, grad_right = run_assemble(
        place, order, homes_of, groups, grad_factor
    )
    return (d_patches, grad_left[None], grad_right[None])


def solution(mesh):
    in_specs = (
        P(("section", "dp"), "tensor"),
        P(("section", "dp"), "tensor"),
        P(("section", "dp"), None),
        P("section", None, "tensor", None, None),
        P("section", None, "tensor", None, None),
        P("section", None, "tensor"),
    )
    out_specs = (
        P(("section", "dp"), "tensor"),
        P("section", None, "tensor", None, None),
        P("section", None, "tensor", None, None),
    )
    body = plane_shards if planes_fit(mesh) else layered_shards
    return jax.shard_map(
        body, mesh=mesh, in_specs=in_specs, out_specs=out_specs, check_vma=False)
```

```python
import math

import jax
import jax.numpy as jnp
from jax import lax
from jax.experimental import pallas as pl
from jax.experimental.pallas import tpu as pltpu
from jax.sharding import PartitionSpec as P

EPSILON = 1e-06
TANH_SLOPE = 0.7978845608028654
CUBIC_TERM = 0.044715


def shifted(value, axis, steps):
    count = lax.axis_size(axis)
    first, last = (max(0, -steps), min(count, count - steps))
    return lax.ppermute(value, axis, [(source, source + steps) for source in range(first, last)])


def gelu_value(values):
    tangent = jnp.tanh(TANH_SLOPE * (values + CUBIC_TERM * values * values * values))
    return 0.5 * values * (1.0 + tangent)


def gelu_slope(values):
    tangent = jnp.tanh(TANH_SLOPE * (values + CUBIC_TERM * values * values * values))
    return 0.5 * (1.0 + tangent) + 0.5 * values * (1.0 - tangent * tangent) * TANH_SLOPE * (
        1.0 + 3.0 * CUBIC_TERM * values * values
    )


def norm_pair(residuals, gain_pair, model_width):
    squares = lax.psum(
        (
            jnp.sum(residuals[0] * residuals[0], axis=(1, 2)),
            jnp.sum(residuals[1] * residuals[1], axis=(1, 2)),
        ),
        "tensor",
    )
    factors = [lax.rsqrt(squares[member] / model_width + EPSILON) for member in range(2)]
    normed = [
        residuals[member] * factors[member][:, None, None] * gain_pair[member][None]
        for member in range(2)
    ]
    return (factors, normed)


def norm_back_pair(residuals, factors, gain_pair, grad_normed, carried, model_width):
    weighted = [grad_normed[member] * gain_pair[member][None] for member in range(2)]
    inners = lax.psum(
        (
            jnp.sum(weighted[0] * residuals[0], axis=(1, 2)),
            jnp.sum(weighted[1] * residuals[1], axis=(1, 2)),
        ),
        "tensor",
    )
    return [
        carried[member]
        + factors[member][:, None, None] * weighted[member]
        - residuals[member] * (factors[member] ** 3 * inners[member] / model_width)[:, None, None]
        for member in range(2)
    ]


def layered_shards(patches, teacher, critic_pairs, left_factors, right_factors, norm_gains):
    sections = lax.axis_size("section")
    tensor_width = lax.axis_size("tensor")
    replicas = lax.axis_size("dp")
    tok_rows = patches.shape[0]
    feat_local = patches.shape[1]
    layer_count = left_factors.shape[1]
    local_blocks = left_factors.shape[2]
    block_size = left_factors.shape[3]
    all_blocks = local_blocks * tensor_width
    fold_ratio = block_size // all_blocks
    model_width = feat_local * tensor_width
    sixth_rows = tok_rows // 6
    leading = 2 * sixth_rows
    critic_ids = jnp.arange(4, dtype=jnp.int32)
    named_by = (
        (critic_pairs[:, 0:1] == critic_ids[None, :])
        | (critic_pairs[:, 1:2] == critic_ids[None, :])
    ).astype(jnp.int32)
    ranking = jnp.cumsum(named_by, axis=0) - 1
    wide_ids = critic_ids[None, :] < 2
    slot_width = 3 * sixth_rows
    spilled = wide_ids & (ranking >= 3 * sixth_rows)
    destination = jnp.where(spilled, critic_ids[None, :] + 2, critic_ids[None, :])
    slot_index = jnp.where(spilled, ranking - sixth_rows, ranking)
    flat_slot = destination * slot_width + slot_index
    chosen = jnp.take_along_axis(flat_slot, critic_pairs, axis=1)
    slot_total = sections * slot_width
    row_ids = jnp.broadcast_to(jnp.arange(tok_rows, dtype=jnp.int32)[:, None], chosen.shape)
    source_row = (
        jnp.full((slot_total,), tok_rows, jnp.int32).at[chosen.reshape(-1)].set(row_ids.reshape(-1))
    )
    send_patch = (
        patches.at[source_row]
        .get(mode="fill", fill_value=0)
        .reshape(sections, slot_width, local_blocks, block_size)
    )
    send_target = (
        teacher.at[source_row]
        .get(mode="fill", fill_value=0)
        .reshape(sections, slot_width, local_blocks, block_size)
    )
    recv_patch, recv_target = (
        lax.all_to_all(send_patch, "section", split_axis=0, concat_axis=0, tiled=True),
        lax.all_to_all(send_target, "section", split_axis=0, concat_axis=0, tiled=True),
    )
    residuals = [
        recv_patch[:, :leading].reshape(-1, local_blocks, block_size).astype(jnp.float32),
        recv_patch[:, leading:].reshape(-1, local_blocks, block_size).astype(jnp.float32),
    ]
    targets = [
        recv_target[:, :leading].reshape(-1, local_blocks, block_size).astype(jnp.float32),
        recv_target[:, leading:].reshape(-1, local_blocks, block_size).astype(jnp.float32),
    ]
    native = (left_factors[0], right_factors[0], norm_gains[0])
    borrowed = shifted((left_factors, right_factors, norm_gains), "section", 2)
    is_wide = lax.axis_index("section") < 2
    second = (
        jnp.where(is_wide, left_factors, borrowed[0])[0],
        jnp.where(is_wide, right_factors, borrowed[1])[0],
        jnp.where(is_wide, norm_gains, borrowed[2])[0],
    )
    left_sets = (native[0], second[0])
    right_sets = (native[1], second[1])
    gain_sets = (
        native[2].astype(jnp.float32).reshape(layer_count + 1, local_blocks, block_size),
        second[2].astype(jnp.float32).reshape(layer_count + 1, local_blocks, block_size),
    )
    stored = []
    for layer_index in range(layer_count):
        gain_pair = [gain_sets[0][layer_index], gain_sets[1][layer_index]]
        factors, normed = norm_pair(residuals, gain_pair, model_width)
        normed = [normed[member].astype(jnp.bfloat16) for member in range(2)]
        first_out = [
            jnp.einsum(
                "nki,kij->nkj",
                normed[member],
                left_sets[member][layer_index],
                preferred_element_type=jnp.float32,
            ).astype(jnp.bfloat16)
            for member in range(2)
        ]
        permuted = (
            lax.all_to_all(first_out[0], "tensor", split_axis=2, concat_axis=1, tiled=True),
            lax.all_to_all(first_out[1], "tensor", split_axis=2, concat_axis=1, tiled=True),
        )
        permuted = [
            permuted[member].reshape(
                permuted[member].shape[0], all_blocks, local_blocks, fold_ratio
            )
            for member in range(2)
        ]
        right_quads = [
            right_sets[member][layer_index].reshape(
                local_blocks, fold_ratio, all_blocks, block_size
            )
            for member in range(2)
        ]
        mixture = [
            jnp.einsum(
                "nkmp,mpkl->nml",
                permuted[member],
                right_quads[member],
                preferred_element_type=jnp.float32,
            )
            for member in range(2)
        ]
        stored.append((residuals, factors, normed, permuted, mixture, right_quads, gain_pair))
        residuals = [residuals[member] + gelu_value(mixture[member]) for member in range(2)]
    final_gains = [gain_sets[0][layer_count], gain_sets[1][layer_count]]
    factors, outputs = norm_pair(residuals, final_gains, model_width)
    gradients = norm_back_pair(
        residuals,
        factors,
        final_gains,
        [outputs[member] - targets[member] for member in range(2)],
        [jnp.zeros_like(residuals[member]) for member in range(2)],
        model_width,
    )
    left_terms = []
    right_terms = []
    for layer_index in range(layer_count - 1, -1, -1):
        inputs, factors, normed, permuted, mixture, right_quads, gain_pair = stored[layer_index]
        slopes = [
            (gradients[member] * gelu_slope(mixture[member])).astype(jnp.bfloat16)
            for member in range(2)
        ]
        right_grad = [
            jnp.einsum(
                "nkmp,nml->mpkl",
                permuted[member],
                slopes[member],
                preferred_element_type=jnp.float32,
            ).reshape(local_blocks, block_size, block_size)
            for member in range(2)
        ]
        back_moved = [
            jnp.einsum(
                "nml,mpkl->nkmp",
                slopes[member],
                right_quads[member],
                preferred_element_type=jnp.float32,
            )
            .astype(jnp.bfloat16)
            .reshape(slopes[member].shape[0], all_blocks, local_blocks * fold_ratio)
            for member in range(2)
        ]
        arrived = (
            lax.all_to_all(back_moved[0], "tensor", split_axis=1, concat_axis=2, tiled=True),
            lax.all_to_all(back_moved[1], "tensor", split_axis=1, concat_axis=2, tiled=True),
        )
        left_grad = [
            jnp.einsum(
                "nki,nkj->kij", normed[member], arrived[member], preferred_element_type=jnp.float32
            )
            for member in range(2)
        ]
        grad_normed = [
            jnp.einsum(
                "nkj,kij->nki",
                arrived[member],
                left_sets[member][layer_index],
                preferred_element_type=jnp.float32,
            )
            for member in range(2)
        ]
        gradients = norm_back_pair(inputs, factors, gain_pair, grad_normed, gradients, model_width)
        layer_left = jnp.stack(left_grad)
        layer_right = jnp.stack(right_grad)
        layer_left, layer_right = (
            lax.psum(layer_left.astype(jnp.bfloat16), "dp").astype(jnp.float32),
            lax.psum(layer_right.astype(jnp.bfloat16), "dp").astype(jnp.float32),
        )
        left_terms.insert(0, layer_left)
        right_terms.insert(0, layer_right)
    left_stack = jnp.stack(left_terms)
    right_stack = jnp.stack(right_terms)
    repaid = (
        shifted(left_stack[:, 1].astype(jnp.bfloat16), "section", -2).astype(jnp.float32),
        shifted(right_stack[:, 1].astype(jnp.bfloat16), "section", -2).astype(jnp.float32),
    )
    is_wide = lax.axis_index("section") < 2
    left_total = left_stack[:, 0] + jnp.where(is_wide, left_stack[:, 1] + repaid[0], 0.0)
    right_total = right_stack[:, 0] + jnp.where(is_wide, right_stack[:, 1] + repaid[1], 0.0)
    grad_factor = 1.0 / math.sqrt(2 * tok_rows * sections * replicas)
    returned = [
        gradients[member].astype(jnp.bfloat16).reshape(sections, -1, local_blocks, block_size)
        for member in range(2)
    ]
    back_lead, back_trail = (
        lax.all_to_all(returned[0], "section", split_axis=0, concat_axis=0, tiled=True),
        lax.all_to_all(returned[1], "section", split_axis=0, concat_axis=0, tiled=True),
    )
    gathered = jnp.concatenate((back_lead, back_trail), axis=1).reshape(
        slot_total, local_blocks, block_size
    )
    combined = (
        gathered[chosen[:, 0]].astype(jnp.float32) + gathered[chosen[:, 1]].astype(jnp.float32)
    ) * 0.5
    d_patches = combined.astype(jnp.bfloat16).reshape(tok_rows, feat_local)
    return (d_patches, (left_total * grad_factor)[None], (right_total * grad_factor)[None])


VMEM_LIMIT = 60 * 1024 * 1024
CHUNKS = 8
TOGETHER = 4
PARTS = 4
SMALL = (16, 128)
AXES = ("section", "tensor", "dp")


def planes_fit(mesh):
    sections = mesh.shape["section"]
    paired = mesh.shape["dp"] == 2 and sections & (sections - 1) == 0
    return paired and mesh.shape["tensor"] == sections


def inner_dot(left, right, left_dim, right_dim):
    return lax.dot_general(
        left,
        right,
        (((left_dim,), (right_dim,)), ((), ())),
        preferred_element_type=jnp.float32,
    )


def fold_rows(values):
    return jnp.sum(values.reshape(values.shape[0] // 8, 8, values.shape[1]), axis=0)


def block_rows(block, size):
    return pl.ds(pl.multiple_of(block * size, size), size)


def column(gain_ref, block, at, slots):
    if len(gain_ref.shape) == 3:
        gains = gain_ref[block // gain_ref.shape[2]]
        return jnp.broadcast_to(gains[:, at : at + 1], (gains.shape[0], slots))
    picked = lax.broadcasted_iota(jnp.int32, (gain_ref.shape[1], slots), 0) == block
    return inner_dot(gain_ref[...], picked.astype(jnp.bfloat16), 1, 0)


def chunk_copy(source, target, sems, chunk):
    rows = target.shape[0] // CHUNKS
    at = pl.ds(pl.multiple_of(chunk * rows, rows), rows)
    return pltpu.make_async_copy(source.at[at], target.at[at], sems.at[chunk])


def start_chunks(source, target, sems):
    for chunk in range(CHUNKS):
        chunk_copy(source, target, sems, chunk).start()


def wait_chunks(source, target, sems):
    for chunk in range(CHUNKS):
        chunk_copy(source, target, sems, chunk).wait()


def factor_copies(parts, layer, held, sems, side):
    count = parts[0].shape[0]
    return [
        pltpu.make_async_copy(
            ref.at[:, layer, side], held.at[pl.ds(at * count, count), side], sems.at[side, at]
        )
        for at, ref in enumerate(parts)
    ]


def gradient_copies(held, parts, sems, side):
    count = parts[0].shape[0]
    return [
        pltpu.make_async_copy(
            held.at[pl.ds(at * count, count), side], ref.at[:, side], sems.at[side, at]
        )
        for at, ref in enumerate(parts)
    ]


def by_chunk(blocks, step, carry, before=None, after=None):
    per_chunk = blocks // CHUNKS

    def few(start, first, carry):
        stores = []
        for at in range(TOGETHER):
            made, carry = step(start + at, first + at, carry)
            stores += made
        for ref, index, value in stores:
            ref[index] = value
        return carry

    def one(chunk, carry):
        if before is not None:
            before(chunk)
        for at in range(0, per_chunk, TOGETHER):
            carry = few(chunk * per_chunk + at, at, carry)
        if after is not None:
            after(chunk)
        return carry

    return lax.fori_loop(0, CHUNKS, one, carry)


def forward_kernel(first, layer, inputs, table_ref, sums_ref, gain_ref, *refs):
    sources, refs = refs[:inputs], refs[inputs:]
    parts, sources = sources[:PARTS], sources[PARTS:]
    out_ref, u_ref, z_ref, slope_ref, scale_ref, next_ref = refs[:6]
    raw, h, w, u, z, slope, mid, in_sems, w_sems, out_sems = refs[6:]
    features, slots = h.shape
    size = w.shape[-1]
    chunk_blocks = w.shape[2]
    blocks = features // size
    fold = size // blocks

    left_in = factor_copies(parts, layer, w, w_sems, 0)
    right_in = factor_copies(parts, layer, w, w_sems, 1)
    if first:
        start_chunks(sources[0], raw, in_sems)
        for copy in left_in + right_in:
            copy.start()

        def squares(block, _, total):
            rows = block_rows(block, size)
            part = raw[rows, :].astype(jnp.float32)
            return [(h, (rows, slice(None)), part)], total + fold_rows(part * part)

        total = by_chunk(
            blocks,
            squares,
            jnp.zeros((8, slots), jnp.float32),
            lambda chunk: chunk_copy(sources[0], raw, in_sems, chunk).wait(),
        )
    else:
        for copy in left_in:
            copy.start()
        start_chunks(sources[0], h, in_sems)
        for copy in right_in:
            copy.start()
        total = sums_ref[...]
    scale = lax.rsqrt(jnp.sum(total, axis=0, keepdims=True) / features + EPSILON)
    scale_ref[...] = jnp.broadcast_to(scale, scale_ref.shape)
    for copy in left_in:
        copy.wait()

    def arrive(chunk):
        if not first:
            chunk_copy(sources[0], h, in_sems, chunk).wait()

    def left(block, nth, carry):
        rows = block_rows(block, size)
        place = table_ref[0, block]
        normed = (h[rows, :] * scale * column(gain_ref, block, nth, slots)).astype(jnp.bfloat16)
        weight = w[place // chunk_blocks, 0, place % chunk_blocks]
        first_out = inner_dot(weight, normed, 0, 0)
        at = (rows, slice(None))
        return [(u, at, normed), (mid, at, first_out)], carry

    def leave_left(chunk):
        chunk_copy(u, u_ref, out_sems.at[0], chunk).start()

    by_chunk(blocks, left, 0, arrive, leave_left)
    for copy in right_in:
        copy.wait()

    eye = lax.broadcasted_iota(jnp.int32, (size, size), 0) == lax.broadcasted_iota(jnp.int32, (size, size), 1)
    eye = eye.astype(jnp.bfloat16)

    def right(block, nth, total):
        rows = block_rows(block, size)
        place = table_ref[0, block]
        moved = [mid[pl.ds(q * blocks + block, blocks, stride=size), :] for q in range(fold)]
        moved = jnp.concatenate(moved, axis=0).astype(jnp.bfloat16)
        weight = w[place // chunk_blocks, 1, place % chunk_blocks]
        turned = inner_dot(eye, weight, 1, 1).astype(jnp.bfloat16)
        mixture = inner_dot(turned, moved, 1, 0)
        squared = mixture * mixture
        tangent = jnp.tanh(mixture * (TANH_SLOPE + (TANH_SLOPE * CUBIC_TERM) * squared))
        half = 0.5 + 0.5 * tangent
        following = h[rows, :] + mixture * half
        steep = half + mixture * (1.0 - tangent * tangent) * (
            0.5 * TANH_SLOPE + (1.5 * TANH_SLOPE * CUBIC_TERM) * squared
        )
        at = (rows, slice(None))
        stores = [(z, at, moved), (h, at, following), (slope, at, steep.astype(jnp.bfloat16))]
        return stores, total + fold_rows(following * following)

    leaving = ((h, out_ref, 1), (z, z_ref, 2), (slope, slope_ref, 3))

    def leave_right(chunk):
        for source, target, at in leaving:
            chunk_copy(source, target, out_sems.at[at], chunk).start()

    next_ref[...] = by_chunk(blocks, right, jnp.zeros((8, slots), jnp.float32), None, leave_right)
    for source, target, at in ((u, u_ref, 0),) + leaving:
        wait_chunks(source, target, out_sems.at[at])


def backward_kernel(turning, last, layer, inputs, table_ref, scale_ref, gain_ref, end_gain_ref, *refs):
    sources, refs = refs[:inputs], refs[inputs:]
    slope_ref, z_ref, u_ref = sources[:3]
    parts, sources = sources[3 : 3 + PARTS], sources[3 + PARTS :]
    out_ref, own_grad, peer_grad = refs[:3]
    g, slope, z, u, h, w, gw, mid, top, goal = refs[3:13]
    in_sems, w_sems, out_sems, gw_sems = refs[13:]
    features, slots = g.shape
    size = w.shape[-1]
    chunk_blocks = w.shape[2]
    blocks = features // size
    fold = size // blocks

    left_in = factor_copies(parts, layer, w, w_sems, 0)
    right_in = factor_copies(parts, layer, w, w_sems, 1)
    g_ref, h_ref = sources[:2]
    if turning:
        for chunk in range(CHUNKS):
            chunk_copy(g_ref, top, in_sems.at[0], chunk).start()
            chunk_copy(sources[2], goal, in_sems.at[5], chunk).start()
    for copy in right_in:
        copy.start()
    for chunk in range(CHUNKS):
        if not turning:
            chunk_copy(g_ref, g, in_sems.at[0], chunk).start()
        chunk_copy(slope_ref, slope, in_sems.at[1], chunk).start()
        chunk_copy(z_ref, z, in_sems.at[2], chunk).start()
    for copy in left_in:
        copy.start()
    for chunk in range(CHUNKS):
        chunk_copy(u_ref, u, in_sems.at[3], chunk).start()
        chunk_copy(h_ref, h, in_sems.at[4], chunk).start()

    if turning:
        zero = jnp.zeros((8, slots), jnp.float32)

        def sums(block, nth, totals):
            rows = block_rows(block, size)
            part = top[rows, :]
            scaled = part * column(end_gain_ref, block, nth, slots)
            return [], (
                totals[0] + fold_rows(part * part),
                totals[1] + fold_rows(scaled * scaled),
                totals[2] + fold_rows(scaled * goal[rows, :].astype(jnp.float32)),
            )

        def arrive_top(chunk):
            chunk_copy(g_ref, top, in_sems.at[0], chunk).wait()
            chunk_copy(sources[2], goal, in_sems.at[5], chunk).wait()

        totals = by_chunk(blocks, sums, (zero, zero, zero), arrive_top)
        squares, gained, crossed = [jnp.sum(total, axis=0, keepdims=True) for total in totals]
        end_scale = lax.rsqrt(squares / features + EPSILON)
        end_back = end_scale * end_scale * end_scale * (end_scale * gained - crossed) / features

    for copy in right_in:
        copy.wait()

    def arrive_right(chunk):
        if not turning:
            chunk_copy(g_ref, g, in_sems.at[0], chunk).wait()
        chunk_copy(slope_ref, slope, in_sems.at[1], chunk).wait()
        chunk_copy(z_ref, z, in_sems.at[2], chunk).wait()

    def right(block, nth, total):
        rows = block_rows(block, size)
        place, home = table_ref[0, block], table_ref[2 if last else 1, block]
        at = (place // chunk_blocks, 1, place % chunk_blocks)
        to = (home // chunk_blocks, 1, home % chunk_blocks)
        if turning:
            part = top[rows, :]
            factor = column(end_gain_ref, block, nth, slots)
            error = (part * end_scale * factor - goal[rows, :].astype(jnp.float32)) * factor
            gradient = end_scale * error - part * end_back
            stores = [(g, (rows, slice(None)), gradient)]
        else:
            gradient = g[rows, :]
            stores = []
        steep = (gradient * slope[rows, :].astype(jnp.float32)).astype(jnp.bfloat16)
        taken = z[rows, :]
        back = inner_dot(w[at], steep, 1, 0)
        stores.append((gw, to, inner_dot(taken, steep, 1, 1).astype(jnp.bfloat16)))
        stores.append((mid, (rows, slice(None)), back))
        return stores, total + fold_rows(taken.astype(jnp.float32) * back)

    total = by_chunk(blocks, right, jnp.zeros((8, slots), jnp.float32), arrive_right)
    right_out = gradient_copies(gw, (own_grad, peer_grad), gw_sems, 1)
    for copy in right_out:
        copy.start()
    for copy in left_in:
        copy.wait()
    scale = scale_ref[0:1, :]
    back = scale * scale * jnp.sum(total, axis=0, keepdims=True) / features

    def arrive_left(chunk):
        chunk_copy(u_ref, u, in_sems.at[3], chunk).wait()
        chunk_copy(h_ref, h, in_sems.at[4], chunk).wait()

    def left(block, nth, carry):
        rows = block_rows(block, size)
        place, home = table_ref[0, block], table_ref[2 if last else 1, block]
        at = (place // chunk_blocks, 0, place % chunk_blocks)
        to = (home // chunk_blocks, 0, home % chunk_blocks)
        arrived = [mid[pl.ds(q * blocks + block, blocks, stride=size), :] for q in range(fold)]
        arrived = jnp.concatenate(arrived, axis=0).astype(jnp.bfloat16)
        factor_grad = inner_dot(u[rows, :], arrived, 1, 1).astype(jnp.bfloat16)
        weighted = inner_dot(w[at], arrived, 1, 0) * column(gain_ref, block, nth, slots)
        ended = g[rows, :] + scale * weighted - h[rows, :].astype(jnp.float32) * back
        index = (rows, slice(None))
        stores = [(gw, to, factor_grad)]
        stores.append((u, index, ended.astype(jnp.bfloat16)) if last else (g, index, ended))
        return stores, carry

    ended = u if last else g
    by_chunk(
        blocks, left, 0, arrive_left, lambda chunk: chunk_copy(ended, out_ref, out_sems, chunk).start()
    )
    left_out = gradient_copies(gw, (own_grad, peer_grad), gw_sems, 0)
    for copy in left_out:
        copy.start()
    wait_chunks(ended, out_ref, out_sems)
    for copy in right_out + left_out:
        copy.wait()


def shape_of(shape, dtype):
    return jax.ShapeDtypeStruct(shape, dtype)


SMEM = pl.BlockSpec(memory_space=pltpu.SMEM)
INSIDE = pl.BlockSpec(memory_space=pltpu.VMEM)
OUTSIDE = pl.BlockSpec(memory_space=pl.ANY)


def run_forward(table, gain, sums, residual, weights, layer):
    first = residual.dtype == jnp.bfloat16
    whole = residual.shape
    sources = (*weights, residual)
    held = (PARTS * weights[0].shape[0],) + weights[0].shape[2:]
    out_shape = (
        shape_of(whole, jnp.float32),
        shape_of(whole, jnp.bfloat16),
        shape_of(whole, jnp.bfloat16),
        shape_of(whole, jnp.bfloat16),
        shape_of((8, whole[1]), jnp.float32),
        shape_of((8, whole[1]), jnp.float32),
    )
    return pl.pallas_call(
        lambda *refs: forward_kernel(first, layer, len(sources), *refs),
        in_specs=[SMEM, INSIDE, INSIDE] + [OUTSIDE] * len(sources),
        out_specs=[OUTSIDE] * 4 + [INSIDE] * 2,
        out_shape=out_shape,
        scratch_shapes=[
            pltpu.VMEM(whole if first else SMALL, jnp.bfloat16),
            pltpu.VMEM(whole, jnp.float32),
            pltpu.VMEM(held, jnp.bfloat16),
            pltpu.VMEM(whole, jnp.bfloat16),
            pltpu.VMEM(whole, jnp.bfloat16),
            pltpu.VMEM(whole, jnp.bfloat16),
            pltpu.VMEM(whole, jnp.float32),
            pltpu.SemaphoreType.DMA((CHUNKS,)),
            pltpu.SemaphoreType.DMA((2, PARTS)),
            pltpu.SemaphoreType.DMA((4, CHUNKS)),
        ],
        compiler_params=pltpu.CompilerParams(vmem_limit_bytes=VMEM_LIMIT),
        cost_estimate=pl.CostEstimate(
            flops=FORWARD_COST, bytes_accessed=20 * whole[0] * whole[1], transcendentals=0
        ),
        name="forward_layer",
    )(table, sums, gain, *sources)


def run_backward(table, gain, end_gain, scale, kept, weights, layer, sources, turning, last):
    whole = kept[0].shape
    sources = (*kept, *weights, *sources)
    held = (PARTS * weights[0].shape[0],) + weights[0].shape[2:]
    half = (held[0] // 2,) + held[1:]
    out_shape = [shape_of(whole, jnp.bfloat16 if last else jnp.float32)] + [shape_of(half, jnp.bfloat16)] * 2
    return pl.pallas_call(
        lambda *refs: backward_kernel(turning, last, layer, len(sources), *refs),
        in_specs=[SMEM] + [INSIDE] * 3 + [OUTSIDE] * len(sources),
        out_specs=[OUTSIDE] * len(out_shape),
        out_shape=out_shape,
        scratch_shapes=[
            pltpu.VMEM(whole, jnp.float32),
            pltpu.VMEM(whole, jnp.bfloat16),
            pltpu.VMEM(whole, jnp.bfloat16),
            pltpu.VMEM(whole, jnp.bfloat16),
            pltpu.VMEM(whole, jnp.bfloat16 if last else jnp.float32),
            pltpu.VMEM(held, jnp.bfloat16),
            pltpu.VMEM(held, jnp.bfloat16),
            pltpu.VMEM(whole, jnp.float32),
            pltpu.VMEM(whole if turning else SMALL, jnp.float32),
            pltpu.VMEM(whole if turning else SMALL, jnp.bfloat16),
            pltpu.SemaphoreType.DMA((6, CHUNKS)),
            pltpu.SemaphoreType.DMA((2, PARTS)),
            pltpu.SemaphoreType.DMA((CHUNKS,)),
            pltpu.SemaphoreType.DMA((2, PARTS)),
        ],
        compiler_params=pltpu.CompilerParams(vmem_limit_bytes=VMEM_LIMIT),
        cost_estimate=pl.CostEstimate(
            flops=BACKWARD_COST, bytes_accessed=30 * whole[0] * whole[1], transcendentals=0
        ),
        name="backward_layer",
    )(table, scale, gain, end_gain, *sources)


def join_kernel(rows, *refs):
    sources, whole, sems = refs[:-2], refs[-2], refs[-1]
    copies = [
        pltpu.make_async_copy(source.at[pl.ds(0, rows)], whole.at[pl.ds(at * rows, rows)], sems.at[at])
        for at, source in enumerate(sources)
    ]
    for copy in copies:
        copy.start()
    for copy in copies:
        copy.wait()


def joined(parts, rows=None):
    rows = parts[0].shape[0] if rows is None else rows
    whole = shape_of((rows * len(parts),) + parts[0].shape[1:], parts[0].dtype)
    return pl.pallas_call(
        lambda *refs: join_kernel(rows, *refs),
        in_specs=[OUTSIDE] * len(parts),
        out_specs=INSIDE,
        out_shape=whole,
        scratch_shapes=[pltpu.SemaphoreType.DMA((len(parts),))],
        compiler_params=pltpu.CompilerParams(vmem_limit_bytes=VMEM_LIMIT),
        cost_estimate=pl.CostEstimate(
            flops=0, bytes_accessed=4 * math.prod(whole.shape), transcendentals=0
        ),
        name="join",
    )(*parts)


def order_kernel(ranges, place_ref, *refs):
    sources, whole, sems = refs[:-2], refs[-2], refs[-1]
    copies = []
    for distance, source in enumerate(sources):
        row = 0
        for start, count in ranges:
            target = whole.at[place_ref[0] ^ distance, pl.ds(row, count)]
            copies.append(pltpu.make_async_copy(source.at[pl.ds(start, count)], target, sems.at[len(copies)]))
            row += count
    for copy in copies:
        copy.start()
    for copy in copies:
        copy.wait()


def by_section(place, parts, ranges):
    rows = sum(count for _, count in ranges)
    whole = shape_of((len(parts), rows) + parts[0].shape[1:], parts[0].dtype)
    return pl.pallas_call(
        lambda *refs: order_kernel(ranges, *refs),
        in_specs=[SMEM] + [OUTSIDE] * len(parts),
        out_specs=INSIDE,
        out_shape=whole,
        scratch_shapes=[pltpu.SemaphoreType.DMA((len(parts) * len(ranges),))],
        compiler_params=pltpu.CompilerParams(vmem_limit_bytes=VMEM_LIMIT),
        cost_estimate=pl.CostEstimate(
            flops=0, bytes_accessed=4 * math.prod(whole.shape), transcendentals=0
        ),
        name="by_section",
    )(place, *parts)


def sum_kernel(terms, inputs, *refs):
    sources, outs = refs[:inputs], refs[inputs:]
    for group in range(inputs // terms):
        mine = sources[group * terms : (group + 1) * terms]
        for at in range(mine[0].shape[0]):
            total = sum(ref[at].astype(jnp.float32) for ref in mine).astype(jnp.bfloat16)
            if len(outs) > 1:
                outs[at][group] = total
            else:
                outs[0][at, group] = total


def run_sum(groups, parts, apart=True):
    flat = [term.reshape(parts, -1, term.shape[-1]) for terms in groups for term in terms]
    _, rows, lanes = flat[0].shape
    steps = 2
    if apart:
        out_shape = [shape_of((len(groups), rows, lanes), jnp.bfloat16)] * parts
        out_specs = [pl.BlockSpec((len(groups), rows // steps, lanes), lambda i: (0, i, 0))] * parts
    else:
        out_shape = [shape_of((parts, len(groups), rows, lanes), jnp.bfloat16)]
        out_specs = [pl.BlockSpec((parts, len(groups), rows // steps, lanes), lambda i: (0, 0, i, 0))]
    sums = pl.pallas_call(
        lambda *refs: sum_kernel(len(groups[0]), len(flat), *refs),
        grid=(steps,),
        in_specs=[pl.BlockSpec((parts, rows // steps, lanes), lambda i: (0, i, 0))] * len(flat),
        out_specs=out_specs,
        out_shape=out_shape,
        compiler_params=pltpu.CompilerParams(vmem_limit_bytes=VMEM_LIMIT),
        cost_estimate=pl.CostEstimate(
            flops=flat[0].size * len(flat), bytes_accessed=2 * flat[0].size * (len(flat) + 1), transcendentals=0
        ),
        name="sum",
    )(*flat)
    return [out.reshape(-1, lanes) for out in sums] if apart else sums[0].reshape(parts, -1, lanes)


def pieces_kernel(chunk, place_ref, order_ref, left_ref, right_ref, gain_ref, *refs):
    outs, (held, left_sem, sems) = refs[:-3], refs[-3:]
    layer_count, half, size = held.shape[:3]
    first = place_ref[2] * half
    lefts = pltpu.make_async_copy(left_ref.at[:, pl.ds(first, half)], held, left_sem.at[0])
    lefts.start()
    copies = []
    turns = []
    for distance, out in enumerate(outs):
        start = (place_ref[0] ^ distance) * chunk
        row = 0
        for layer in range(layer_count):
            for inside in range(chunk):
                turns.append((layer, start + inside, out, row))
                row += size
            for inside in range(chunk):
                source = right_ref.at[layer, first + start + inside]
                copies.append((source, out.at[pl.ds(row, size)]))
                row += size
        copies.append((gain_ref, out.at[pl.ds(row, gain_ref.shape[0])]))
    copies = [
        pltpu.make_async_copy(source, target, sems.at[at]) for at, (source, target) in enumerate(copies)
    ]
    for copy in copies:
        copy.start()
    lefts.wait()
    for layer, block, out, row in turns:
        turned = inner_dot(held[layer, block], order_ref[...], 1, 0)
        out[pl.ds(row, size), :] = turned.astype(jnp.bfloat16)
    for copy in copies:
        copy.wait()


def factor_pieces(place, order, left, right, gain_rows, chunk, width):
    layer_count, blocks, size = left.shape[:3]
    rows = layer_count * 2 * chunk * size + gain_rows.shape[0]
    return pl.pallas_call(
        lambda *refs: pieces_kernel(chunk, *refs),
        in_specs=[SMEM, INSIDE] + [OUTSIDE] * 3,
        out_specs=[INSIDE] * width,
        out_shape=[shape_of((rows, size), jnp.bfloat16)] * width,
        scratch_shapes=[
            pltpu.VMEM((layer_count, blocks // 2, size, size), jnp.bfloat16),
            pltpu.SemaphoreType.DMA((1,)),
            pltpu.SemaphoreType.DMA((width * (layer_count * chunk + 1),)),
        ],
        compiler_params=pltpu.CompilerParams(vmem_limit_bytes=VMEM_LIMIT),
        cost_estimate=pl.CostEstimate(flops=left.size * size, bytes_accessed=4 * left.size, transcendentals=0),
        name="pieces",
    )(place, order, left, right, gain_rows)


def choice(pairs, critic, slots):
    rows = pairs.shape[0]
    named = (pairs[:, 0:1] == critic) | (pairs[:, 1:2] == critic)
    named = jnp.broadcast_to(named.astype(jnp.float32), (rows, slots))
    before = lax.broadcasted_iota(jnp.int32, (rows, rows), 1) < lax.broadcasted_iota(jnp.int32, (rows, rows), 0)
    rank = inner_dot(before.astype(jnp.bfloat16), named.astype(jnp.bfloat16), 1, 0)
    at = lax.broadcasted_iota(jnp.int32, (rows, slots), 1).astype(jnp.float32)
    return jnp.where(rank == at, named, 0.0).astype(jnp.bfloat16)


def pick_kernel(pairs_ref, values_ref, out_ref):
    width, features, slots = out_ref.shape
    pairs = pairs_ref[...]
    chosen = [choice(pairs, critic, slots) for critic in range(width)]
    step = 512
    for start in range(0, features, step):
        part = values_ref[:, pl.ds(start, step)]
        for k in range(width):
            out_ref[k, pl.ds(start, step), :] = inner_dot(part, chosen[k], 0, 0).astype(jnp.bfloat16)


def run_pick(pairs, values, width, slots):
    rows, features = values.shape
    return pl.pallas_call(
        pick_kernel,
        in_specs=[INSIDE] * 2,
        out_specs=INSIDE,
        out_shape=shape_of((width, features, slots), jnp.bfloat16),
        compiler_params=pltpu.CompilerParams(vmem_limit_bytes=VMEM_LIMIT),
        cost_estimate=pl.CostEstimate(
            flops=2 * rows * features * slots * width, bytes_accessed=8 * rows * features, transcendentals=0
        ),
        name="pick",
    )(pairs, values)


def combine_kernel(pairs_ref, came_ref, out_ref):
    width, features, slots = came_ref.shape
    pairs = pairs_ref[...]
    chosen = [choice(pairs, critic, slots) for critic in range(width)]
    step = 512
    for start in range(0, features, step):
        total = sum(inner_dot(chosen[k], came_ref[k, pl.ds(start, step), :], 1, 1) for k in range(width))
        out_ref[:, pl.ds(start, step)] = (0.5 * total).astype(jnp.bfloat16)


def run_combine(pairs, came):
    rows = pairs.shape[0]
    return pl.pallas_call(
        combine_kernel,
        in_specs=[INSIDE] * 2,
        out_specs=INSIDE,
        out_shape=shape_of((rows, came.shape[1]), jnp.bfloat16),
        compiler_params=pltpu.CompilerParams(vmem_limit_bytes=VMEM_LIMIT),
        cost_estimate=pl.CostEstimate(
            flops=2 * rows * came.size, bytes_accessed=4 * came.size, transcendentals=0
        ),
        name="combine",
    )(pairs, came)


FORWARD_COST = 4_000_000_000
BACKWARD_COST = 5_000_000_000


def assemble_kernel(layers, factor, place_ref, order_ref, *refs):
    count = 2 * len(layers)
    sources, (left_ref, right_ref) = refs[:count], refs[count : count + 2]
    held, wide = refs[count + 2 : 2 * count + 2], refs[2 * count + 2 : 3 * count + 2]
    in_sems, out_sems = refs[3 * count + 2 :]
    origin, core = place_ref[0] ^ place_ref[1], place_ref[2]
    order = order_ref[...]
    arrivals = [
        pltpu.make_async_copy(source, held[at], in_sems.at[at]) for at, source in enumerate(sources)
    ]
    for copy in arrivals:
        copy.start()
    leaving = []
    for at in range(count):
        arrivals[at].wait()
        half = core if at % 2 == 0 else 1 - core
        width, _, _, chunk = held[at].shape[:4]
        for k in range(width):
            start = (half * width + (origin ^ k if at < 2 else k)) * chunk
            for inside, layer in enumerate(layers[at // 2]):
                for block in range(chunk):
                    left = inner_dot(held[at][k, inside, 0, block], order, 1, 1)
                    wide[at][k, inside, 0, block] = left * factor
                wide[at][k, inside, 1] = held[at][k, inside, 1].astype(jnp.float32) * factor
                for which, target in enumerate((left_ref, right_ref)):
                    copy = pltpu.make_async_copy(
                        wide[at].at[k, inside, which],
                        target.at[layer, pl.ds(start, chunk)],
                        out_sems.at[len(leaving)],
                    )
                    copy.start()
                    leaving.append(copy)
    for copy in leaving:
        copy.wait()


def run_assemble(place, order, pieces, layers, factor):
    piece = pieces[0].shape
    layer_count = sum(len(group) for group in layers)
    out = shape_of((layer_count, 2 * piece[0] * piece[3]) + piece[4:], jnp.float32)
    return pl.pallas_call(
        lambda *refs: assemble_kernel(layers, factor, *refs),
        in_specs=[SMEM, INSIDE] + [OUTSIDE] * len(pieces),
        out_specs=[OUTSIDE] * 2,
        out_shape=[out] * 2,
        scratch_shapes=[pltpu.VMEM(part.shape, jnp.bfloat16) for part in pieces]
        + [pltpu.VMEM(part.shape, jnp.float32) for part in pieces]
        + [
            pltpu.SemaphoreType.DMA((len(pieces),)),
            pltpu.SemaphoreType.DMA((4 * layer_count * piece[0],)),
        ],
        compiler_params=pltpu.CompilerParams(vmem_limit_bytes=VMEM_LIMIT),
        cost_estimate=pl.CostEstimate(flops=0, bytes_accessed=4 * math.prod(out.shape) * 3, transcendentals=0),
        name="assemble",
    )(place, order, *pieces)


def plane_routes(width, replicas):
    bits = width.bit_length() - 1
    orders = [[(step + d) % bits for step in range(bits)] for d in range(replicas)]
    every = [(s, t, d) for s in range(width) for t in range(width) for d in range(replicas)]

    def route(move):
        def index(s, t, d):
            return (s * width + t) * replicas + d

        return [(index(*place), index(*move(*place))) for place in every]

    ranks = [[0] * width for _ in range(replicas)]
    for d in range(replicas):
        for r in range(width):
            ranks[d][sum(((r >> at) & 1) << orders[d][at] for at in range(bits))] = r
    return {
        "across": [route(lambda s, t, d, at=at: (s ^ (1 << orders[d][at]), t, d)) for at in range(bits)],
        "cores": route(lambda s, t, d: (s, t, 1 - d)),
        "sections": [route(lambda s, t, d, k=k: (s ^ k, t, d)) for k in range(width)],
        "homes": [route(lambda s, t, d, j=j: (t, t ^ s ^ j, d)) for j in range(width)],
    }, ranks


def plane_shards(patches, teacher, critic_pairs, left_factors, right_factors, norm_gains):
    width = lax.axis_size("section")
    replicas = lax.axis_size("dp")
    tok_rows, feat_local = patches.shape
    layer_count, local_blocks, size = left_factors.shape[1:4]
    blocks = feat_local * width // size
    wide = 2 * tok_rows // 3
    chunk = local_blocks // (replicas * width)
    layer_rows = 2 * chunk * size
    routes, ranks = plane_routes(width, replicas)
    section = lax.axis_index("section")
    tensor = lax.axis_index("tensor")
    core = lax.axis_index("dp")
    place = jnp.stack([section, tensor, core]).astype(jnp.int32)
    tie = lax.optimization_barrier

    def move(value, route):
        return lax.ppermute(value, AXES, route)

    def move_all(values, name):
        return [move(value, route) for value, route in zip(values, routes[name])]

    def send(values, name):
        return [values[0]] + [move(values[k], routes[name][k]) for k in range(1, width)]

    def gather_two(pair):
        return pair, move(pair, routes["across"][1]), move(pair, routes["cores"])

    def gather_three(pair, other, peer):
        return [pair, other, peer, move(other, routes["cores"])]

    def as_weights(parts):
        return [part.reshape(2 * width, -1, 2, chunk, size, size) for part in parts]

    block = jnp.arange(blocks, dtype=jnp.int32)
    inside = block % local_blocks
    replica = inside // (width * chunk)
    part = (replica != core).astype(jnp.int32)
    distance = section ^ ((inside // chunk) % width)
    quarter = block // local_blocks
    rank = jnp.array(ranks, jnp.int32)[replica, distance]
    table = jnp.stack(
        [
            ((part * width + index) * width + piece) * chunk + inside % chunk
            for index, piece in (
                (rank, quarter),
                (distance, quarter),
                (distance, tensor ^ section ^ distance ^ quarter),
            )
        ]
    ).astype(jnp.int32)

    def to_planes(value):
        return lax.all_to_all(value, "tensor", split_axis=0, concat_axis=0, tiled=True)

    def to_sections(value):
        return lax.all_to_all(value, "section", split_axis=0, concat_axis=0, tiled=True)

    half_layers = layer_count // 2
    fold = size // blocks
    columns = jnp.arange(size)
    order = (columns[:, None] == (columns % blocks) * fold + columns // blocks).astype(jnp.bfloat16)
    gain_rows = norm_gains[0].reshape(-1, size)
    patch_sent = run_pick(critic_pairs, patches, width, wide)
    patch_sent, left, right, teacher = tie((patch_sent, left_factors[0], right_factors[0], teacher))
    patch_came = to_planes(patch_sent).reshape(-1, wide)
    pieces = factor_pieces(place, order, left, right, gain_rows, chunk, width)
    spread = send(pieces, "sections")
    cut, end = half_layers * layer_rows, layer_count * layer_rows
    first = by_section(place, spread, [(0, cut), (end, gain_rows.shape[0])])
    second = by_section(place, spread, [(cut, end - cut)])
    target_sent = run_pick(critic_pairs, teacher, width, wide)
    patch_came, first, second, target_sent = tie((patch_came, first, second, target_sent))
    first = to_planes(first)
    first, second = tie((first, second))
    second = to_planes(second)
    lowest = [first[:, at * layer_rows : (at + 1) * layer_rows] for at in range(half_layers)]
    beside = [move(value, routes["across"][0]) for value in lowest[:2]]
    gains = first[:, cut:].reshape(width, layer_count + 1, local_blocks, size)
    gains = gains.transpose(1, 3, 0, 2).reshape(layer_count + 1, size, blocks)
    end_gain = gains[layer_count].reshape(size, CHUNKS, blocks // CHUNKS).transpose(1, 0, 2)
    end_gain = end_gain.astype(jnp.float32)
    lowest, beside, gains, end_gain = tie((lowest, beside, gains, end_gain))
    flying = {0: gather_two(joined([lowest[0], beside[0]]))}
    flying, second, target_sent = tie((flying, second, target_sent))
    for layer in range(half_layers, layer_count):
        at = (layer - half_layers) * layer_rows
        lowest.append(second[:, at : at + layer_rows])
    target = to_planes(target_sent).reshape(-1, wide)
    weights = [as_weights(gather_three(*flying.pop(0)))]
    flying[1] = gather_two(joined([lowest[1], beside[1]]))
    steps = {2: (lowest[2], move(lowest[2], routes["across"][0]))}
    weights, flying, steps = tie((weights, flying, steps))

    residual = patch_came
    sums = jnp.zeros((8, wide), jnp.float32)
    stored = []
    for layer in range(layer_count):
        ahead = {}
        if layer + 1 < layer_count:
            ahead["weights"] = gather_three(*flying.pop(layer + 1))
        if layer + 2 < layer_count:
            ahead["two"] = gather_two(joined(list(steps.pop(layer + 2))))
        if layer + 3 < layer_count:
            ahead["one"] = (lowest[layer + 3], move(lowest[layer + 3], routes["across"][0]))
        following, u, z, slope, scale, sums = run_forward(
            table, gains[layer], sums, residual, weights[layer], 0
        )
        stored.append(((slope, z, u), scale, residual))
        residual, sums, ahead = tie((following, sums, ahead))
        if layer + 1 < layer_count:
            weights.append(as_weights(ahead["weights"]))
        if layer + 2 < layer_count:
            flying[layer + 2] = ahead["two"]
        if layer + 3 < layer_count:
            steps[layer + 3] = ahead["one"]
        if layer == layer_count - 2:
            residual, sums, target = tie((residual, sums, target))

    def core_sum(mine, other):
        return (mine, move(other, routes["cores"]))

    def plane_sum(mine, other):
        return send(run_sum([(mine, other)], width), "sections")

    def both_halves(whole):
        pair = (whole, move(whole, routes["cores"]))
        return [part.reshape(width, -1, 2, chunk, size, size) for part in pair]

    steps = (core_sum, plane_sum)
    gradient = residual
    underway = []
    for layer in range(layer_count - 1, -1, -1):
        turning = layer == layer_count - 1
        last = layer == 0
        kept, scale, inputs = stored[layer]
        sources = (gradient, inputs, target) if turning else (gradient, inputs)
        underway = [(at + 1, steps[at](*state)) if at < len(steps) else (at, state) for at, state in underway]
        gradient, mine, other = run_backward(
            table,
            gains[layer],
            end_gain,
            scale,
            kept,
            weights[layer],
            0,
            sources,
            turning,
            last,
        )
        gradient, mine, other, states = tie((gradient, mine, other, [state for _, state in underway]))
        underway = [(at, state) for (at, _), state in zip(underway, states)]
        underway.append((0, (mine, other)))

    returned = to_planes(gradient.reshape(width, feat_local, wide))
    ended = [steps[at](*state) if at < len(steps) else state for at, state in underway][::-1]
    ended = tie(ended)
    ended[0] = plane_sum(*ended[0])
    others = to_planes(run_sum(ended[1:], width, apart=False))
    home = run_sum(ended[:1], width)
    home, returned, others = tie((home, returned, others))
    home = move_all(home, "homes")
    d_patches = run_combine(critic_pairs, returned)
    others = to_sections(others)
    d_patches, home, others = tie((d_patches, home, others))
    homes_of = both_halves(joined(home)) + both_halves(others)
    grad_factor = 1.0 / math.sqrt(2 * tok_rows * width * replicas)
    grad_left, grad_right = run_assemble(
        place, order, homes_of, [(0,), tuple(range(1, layer_count))], grad_factor
    )
    return (d_patches, grad_left[None], grad_right[None])


def solution(mesh):
    in_specs = (
        P(("section", "dp"), "tensor"),
        P(("section", "dp"), "tensor"),
        P(("section", "dp"), None),
        P("section", None, "tensor", None, None),
        P("section", None, "tensor", None, None),
        P("section", None, "tensor"),
    )
    out_specs = (
        P(("section", "dp"), "tensor"),
        P("section", None, "tensor", None, None),
        P("section", None, "tensor", None, None),
    )
    body = plane_shards if planes_fit(mesh) else layered_shards
    return jax.shard_map(
        body, mesh=mesh, in_specs=in_specs, out_specs=out_specs, check_vma=False)
```

```python
import math

import jax
import jax.numpy as jnp
from jax import lax
from jax.experimental import pallas as pl
from jax.experimental.pallas import tpu as pltpu
from jax.sharding import PartitionSpec as P

EPSILON = 1e-06
TANH_SLOPE = 0.7978845608028654
CUBIC_TERM = 0.044715


def shifted(value, axis, steps):
    count = lax.axis_size(axis)
    first, last = (max(0, -steps), min(count, count - steps))
    return lax.ppermute(value, axis, [(source, source + steps) for source in range(first, last)])


def gelu_value(values):
    tangent = jnp.tanh(TANH_SLOPE * (values + CUBIC_TERM * values * values * values))
    return 0.5 * values * (1.0 + tangent)


def gelu_slope(values):
    tangent = jnp.tanh(TANH_SLOPE * (values + CUBIC_TERM * values * values * values))
    return 0.5 * (1.0 + tangent) + 0.5 * values * (1.0 - tangent * tangent) * TANH_SLOPE * (
        1.0 + 3.0 * CUBIC_TERM * values * values
    )


def norm_pair(residuals, gain_pair, model_width):
    squares = lax.psum(
        (
            jnp.sum(residuals[0] * residuals[0], axis=(1, 2)),
            jnp.sum(residuals[1] * residuals[1], axis=(1, 2)),
        ),
        "tensor",
    )
    factors = [lax.rsqrt(squares[member] / model_width + EPSILON) for member in range(2)]
    normed = [
        residuals[member] * factors[member][:, None, None] * gain_pair[member][None]
        for member in range(2)
    ]
    return (factors, normed)


def norm_back_pair(residuals, factors, gain_pair, grad_normed, carried, model_width):
    weighted = [grad_normed[member] * gain_pair[member][None] for member in range(2)]
    inners = lax.psum(
        (
            jnp.sum(weighted[0] * residuals[0], axis=(1, 2)),
            jnp.sum(weighted[1] * residuals[1], axis=(1, 2)),
        ),
        "tensor",
    )
    return [
        carried[member]
        + factors[member][:, None, None] * weighted[member]
        - residuals[member] * (factors[member] ** 3 * inners[member] / model_width)[:, None, None]
        for member in range(2)
    ]


def layered_shards(patches, teacher, critic_pairs, left_factors, right_factors, norm_gains):
    sections = lax.axis_size("section")
    tensor_width = lax.axis_size("tensor")
    replicas = lax.axis_size("dp")
    tok_rows = patches.shape[0]
    feat_local = patches.shape[1]
    layer_count = left_factors.shape[1]
    local_blocks = left_factors.shape[2]
    block_size = left_factors.shape[3]
    all_blocks = local_blocks * tensor_width
    fold_ratio = block_size // all_blocks
    model_width = feat_local * tensor_width
    sixth_rows = tok_rows // 6
    leading = 2 * sixth_rows
    critic_ids = jnp.arange(4, dtype=jnp.int32)
    named_by = (
        (critic_pairs[:, 0:1] == critic_ids[None, :])
        | (critic_pairs[:, 1:2] == critic_ids[None, :])
    ).astype(jnp.int32)
    ranking = jnp.cumsum(named_by, axis=0) - 1
    wide_ids = critic_ids[None, :] < 2
    slot_width = 3 * sixth_rows
    spilled = wide_ids & (ranking >= 3 * sixth_rows)
    destination = jnp.where(spilled, critic_ids[None, :] + 2, critic_ids[None, :])
    slot_index = jnp.where(spilled, ranking - sixth_rows, ranking)
    flat_slot = destination * slot_width + slot_index
    chosen = jnp.take_along_axis(flat_slot, critic_pairs, axis=1)
    slot_total = sections * slot_width
    row_ids = jnp.broadcast_to(jnp.arange(tok_rows, dtype=jnp.int32)[:, None], chosen.shape)
    source_row = (
        jnp.full((slot_total,), tok_rows, jnp.int32).at[chosen.reshape(-1)].set(row_ids.reshape(-1))
    )
    send_patch = (
        patches.at[source_row]
        .get(mode="fill", fill_value=0)
        .reshape(sections, slot_width, local_blocks, block_size)
    )
    send_target = (
        teacher.at[source_row]
        .get(mode="fill", fill_value=0)
        .reshape(sections, slot_width, local_blocks, block_size)
    )
    recv_patch, recv_target = (
        lax.all_to_all(send_patch, "section", split_axis=0, concat_axis=0, tiled=True),
        lax.all_to_all(send_target, "section", split_axis=0, concat_axis=0, tiled=True),
    )
    residuals = [
        recv_patch[:, :leading].reshape(-1, local_blocks, block_size).astype(jnp.float32),
        recv_patch[:, leading:].reshape(-1, local_blocks, block_size).astype(jnp.float32),
    ]
    targets = [
        recv_target[:, :leading].reshape(-1, local_blocks, block_size).astype(jnp.float32),
        recv_target[:, leading:].reshape(-1, local_blocks, block_size).astype(jnp.float32),
    ]
    native = (left_factors[0], right_factors[0], norm_gains[0])
    borrowed = shifted((left_factors, right_factors, norm_gains), "section", 2)
    is_wide = lax.axis_index("section") < 2
    second = (
        jnp.where(is_wide, left_factors, borrowed[0])[0],
        jnp.where(is_wide, right_factors, borrowed[1])[0],
        jnp.where(is_wide, norm_gains, borrowed[2])[0],
    )
    left_sets = (native[0], second[0])
    right_sets = (native[1], second[1])
    gain_sets = (
        native[2].astype(jnp.float32).reshape(layer_count + 1, local_blocks, block_size),
        second[2].astype(jnp.float32).reshape(layer_count + 1, local_blocks, block_size),
    )
    stored = []
    for layer_index in range(layer_count):
        gain_pair = [gain_sets[0][layer_index], gain_sets[1][layer_index]]
        factors, normed = norm_pair(residuals, gain_pair, model_width)
        normed = [normed[member].astype(jnp.bfloat16) for member in range(2)]
        first_out = [
            jnp.einsum(
                "nki,kij->nkj",
                normed[member],
                left_sets[member][layer_index],
                preferred_element_type=jnp.float32,
            ).astype(jnp.bfloat16)
            for member in range(2)
        ]
        permuted = (
            lax.all_to_all(first_out[0], "tensor", split_axis=2, concat_axis=1, tiled=True),
            lax.all_to_all(first_out[1], "tensor", split_axis=2, concat_axis=1, tiled=True),
        )
        permuted = [
            permuted[member].reshape(
                permuted[member].shape[0], all_blocks, local_blocks, fold_ratio
            )
            for member in range(2)
        ]
        right_quads = [
            right_sets[member][layer_index].reshape(
                local_blocks, fold_ratio, all_blocks, block_size
            )
            for member in range(2)
        ]
        mixture = [
            jnp.einsum(
                "nkmp,mpkl->nml",
                permuted[member],
                right_quads[member],
                preferred_element_type=jnp.float32,
            )
            for member in range(2)
        ]
        stored.append((residuals, factors, normed, permuted, mixture, right_quads, gain_pair))
        residuals = [residuals[member] + gelu_value(mixture[member]) for member in range(2)]
    final_gains = [gain_sets[0][layer_count], gain_sets[1][layer_count]]
    factors, outputs = norm_pair(residuals, final_gains, model_width)
    gradients = norm_back_pair(
        residuals,
        factors,
        final_gains,
        [outputs[member] - targets[member] for member in range(2)],
        [jnp.zeros_like(residuals[member]) for member in range(2)],
        model_width,
    )
    left_terms = []
    right_terms = []
    for layer_index in range(layer_count - 1, -1, -1):
        inputs, factors, normed, permuted, mixture, right_quads, gain_pair = stored[layer_index]
        slopes = [
            (gradients[member] * gelu_slope(mixture[member])).astype(jnp.bfloat16)
            for member in range(2)
        ]
        right_grad = [
            jnp.einsum(
                "nkmp,nml->mpkl",
                permuted[member],
                slopes[member],
                preferred_element_type=jnp.float32,
            ).reshape(local_blocks, block_size, block_size)
            for member in range(2)
        ]
        back_moved = [
            jnp.einsum(
                "nml,mpkl->nkmp",
                slopes[member],
                right_quads[member],
                preferred_element_type=jnp.float32,
            )
            .astype(jnp.bfloat16)
            .reshape(slopes[member].shape[0], all_blocks, local_blocks * fold_ratio)
            for member in range(2)
        ]
        arrived = (
            lax.all_to_all(back_moved[0], "tensor", split_axis=1, concat_axis=2, tiled=True),
            lax.all_to_all(back_moved[1], "tensor", split_axis=1, concat_axis=2, tiled=True),
        )
        left_grad = [
            jnp.einsum(
                "nki,nkj->kij", normed[member], arrived[member], preferred_element_type=jnp.float32
            )
            for member in range(2)
        ]
        grad_normed = [
            jnp.einsum(
                "nkj,kij->nki",
                arrived[member],
                left_sets[member][layer_index],
                preferred_element_type=jnp.float32,
            )
            for member in range(2)
        ]
        gradients = norm_back_pair(inputs, factors, gain_pair, grad_normed, gradients, model_width)
        layer_left = jnp.stack(left_grad)
        layer_right = jnp.stack(right_grad)
        layer_left, layer_right = (
            lax.psum(layer_left.astype(jnp.bfloat16), "dp").astype(jnp.float32),
            lax.psum(layer_right.astype(jnp.bfloat16), "dp").astype(jnp.float32),
        )
        left_terms.insert(0, layer_left)
        right_terms.insert(0, layer_right)
    left_stack = jnp.stack(left_terms)
    right_stack = jnp.stack(right_terms)
    repaid = (
        shifted(left_stack[:, 1].astype(jnp.bfloat16), "section", -2).astype(jnp.float32),
        shifted(right_stack[:, 1].astype(jnp.bfloat16), "section", -2).astype(jnp.float32),
    )
    is_wide = lax.axis_index("section") < 2
    left_total = left_stack[:, 0] + jnp.where(is_wide, left_stack[:, 1] + repaid[0], 0.0)
    right_total = right_stack[:, 0] + jnp.where(is_wide, right_stack[:, 1] + repaid[1], 0.0)
    grad_factor = 1.0 / math.sqrt(2 * tok_rows * sections * replicas)
    returned = [
        gradients[member].astype(jnp.bfloat16).reshape(sections, -1, local_blocks, block_size)
        for member in range(2)
    ]
    back_lead, back_trail = (
        lax.all_to_all(returned[0], "section", split_axis=0, concat_axis=0, tiled=True),
        lax.all_to_all(returned[1], "section", split_axis=0, concat_axis=0, tiled=True),
    )
    gathered = jnp.concatenate((back_lead, back_trail), axis=1).reshape(
        slot_total, local_blocks, block_size
    )
    combined = (
        gathered[chosen[:, 0]].astype(jnp.float32) + gathered[chosen[:, 1]].astype(jnp.float32)
    ) * 0.5
    d_patches = combined.astype(jnp.bfloat16).reshape(tok_rows, feat_local)
    return (d_patches, (left_total * grad_factor)[None], (right_total * grad_factor)[None])


VMEM_LIMIT = 60 * 1024 * 1024
CHUNKS = 8
TOGETHER = 4
PARTS = 4
SMALL = (16, 128)
AXES = ("section", "tensor", "dp")


def planes_fit(mesh):
    sections = mesh.shape["section"]
    paired = mesh.shape["dp"] == 2 and sections & (sections - 1) == 0
    return paired and mesh.shape["tensor"] == sections


def inner_dot(left, right, left_dim, right_dim):
    return lax.dot_general(
        left,
        right,
        (((left_dim,), (right_dim,)), ((), ())),
        preferred_element_type=jnp.float32,
    )


def fold_rows(values):
    return jnp.sum(values.reshape(values.shape[0] // 8, 8, values.shape[1]), axis=0)


def block_rows(block, size):
    return pl.ds(pl.multiple_of(block * size, size), size)


def column(gain_ref, block, at, slots):
    if len(gain_ref.shape) == 3:
        gains = gain_ref[block // gain_ref.shape[2]]
        return jnp.broadcast_to(gains[:, at : at + 1], (gains.shape[0], slots))
    picked = lax.broadcasted_iota(jnp.int32, (gain_ref.shape[1], slots), 0) == block
    return inner_dot(gain_ref[...], picked.astype(jnp.bfloat16), 1, 0)


def chunk_copy(source, target, sems, chunk):
    rows = target.shape[0] // CHUNKS
    at = pl.ds(pl.multiple_of(chunk * rows, rows), rows)
    return pltpu.make_async_copy(source.at[at], target.at[at], sems.at[chunk])


def start_chunks(source, target, sems):
    for chunk in range(CHUNKS):
        chunk_copy(source, target, sems, chunk).start()


def wait_chunks(source, target, sems):
    for chunk in range(CHUNKS):
        chunk_copy(source, target, sems, chunk).wait()


def factor_copies(parts, layer, held, sems, side):
    count = parts[0].shape[0]
    return [
        pltpu.make_async_copy(
            ref.at[:, layer, side], held.at[pl.ds(at * count, count), side], sems.at[side, at]
        )
        for at, ref in enumerate(parts)
    ]


def gradient_copies(held, parts, sems, side):
    count = parts[0].shape[0]
    return [
        pltpu.make_async_copy(
            held.at[pl.ds(at * count, count), side], ref.at[:, side], sems.at[side, at]
        )
        for at, ref in enumerate(parts)
    ]


def by_chunk(blocks, step, carry, before=None, after=None):
    per_chunk = blocks // CHUNKS

    def few(start, first, carry):
        stores = []
        for at in range(TOGETHER):
            made, carry = step(start + at, first + at, carry)
            stores += made
        for ref, index, value in stores:
            ref[index] = value
        return carry

    def one(chunk, carry):
        if before is not None:
            before(chunk)
        for at in range(0, per_chunk, TOGETHER):
            carry = few(chunk * per_chunk + at, at, carry)
        if after is not None:
            after(chunk)
        return carry

    return lax.fori_loop(0, CHUNKS, one, carry)


def forward_kernel(first, layer, inputs, table_ref, sums_ref, gain_ref, *refs):
    sources, refs = refs[:inputs], refs[inputs:]
    parts, sources = sources[:PARTS], sources[PARTS:]
    out_ref, u_ref, z_ref, slope_ref, scale_ref, next_ref = refs[:6]
    raw, h, w, u, z, slope, mid, in_sems, w_sems, out_sems = refs[6:]
    features, slots = h.shape
    size = w.shape[-1]
    chunk_blocks = w.shape[2]
    blocks = features // size
    fold = size // blocks

    left_in = factor_copies(parts, layer, w, w_sems, 0)
    right_in = factor_copies(parts, layer, w, w_sems, 1)
    if first:
        start_chunks(sources[0], raw, in_sems)
        for copy in left_in + right_in:
            copy.start()

        def squares(block, _, total):
            rows = block_rows(block, size)
            part = raw[rows, :].astype(jnp.float32)
            return [(h, (rows, slice(None)), part)], total + fold_rows(part * part)

        total = by_chunk(
            blocks,
            squares,
            jnp.zeros((8, slots), jnp.float32),
            lambda chunk: chunk_copy(sources[0], raw, in_sems, chunk).wait(),
        )
    else:
        for copy in left_in:
            copy.start()
        start_chunks(sources[0], h, in_sems)
        for copy in right_in:
            copy.start()
        total = sums_ref[...]
    scale = lax.rsqrt(jnp.sum(total, axis=0, keepdims=True) / features + EPSILON)
    scale_ref[...] = jnp.broadcast_to(scale, scale_ref.shape)
    for copy in left_in:
        copy.wait()

    def arrive(chunk):
        if not first:
            chunk_copy(sources[0], h, in_sems, chunk).wait()

    def left(block, nth, carry):
        rows = block_rows(block, size)
        place = table_ref[0, block]
        normed = (h[rows, :] * scale * column(gain_ref, block, nth, slots)).astype(jnp.bfloat16)
        weight = w[place // chunk_blocks, 0, place % chunk_blocks]
        first_out = inner_dot(weight, normed, 0, 0)
        at = (rows, slice(None))
        return [(u, at, normed), (mid, at, first_out)], carry

    def leave_left(chunk):
        chunk_copy(u, u_ref, out_sems.at[0], chunk).start()

    by_chunk(blocks, left, 0, arrive, leave_left)
    for copy in right_in:
        copy.wait()

    def right(block, nth, total):
        rows = block_rows(block, size)
        place = table_ref[0, block]
        moved = [mid[pl.ds(q * blocks + block, blocks, stride=size), :] for q in range(fold)]
        moved = jnp.concatenate(moved, axis=0).astype(jnp.bfloat16)
        weight = w[place // chunk_blocks, 1, place % chunk_blocks]
        mixture = inner_dot(weight, moved, 0, 0)
        squared = mixture * mixture
        tangent = jnp.tanh(mixture * (TANH_SLOPE + (TANH_SLOPE * CUBIC_TERM) * squared))
        half = 0.5 + 0.5 * tangent
        following = h[rows, :] + mixture * half
        steep = half + mixture * (1.0 - tangent * tangent) * (
            0.5 * TANH_SLOPE + (1.5 * TANH_SLOPE * CUBIC_TERM) * squared
        )
        at = (rows, slice(None))
        stores = [(z, at, moved), (h, at, following), (slope, at, steep.astype(jnp.bfloat16))]
        return stores, total + fold_rows(following * following)

    leaving = ((h, out_ref, 1), (z, z_ref, 2), (slope, slope_ref, 3))

    def leave_right(chunk):
        for source, target, at in leaving:
            chunk_copy(source, target, out_sems.at[at], chunk).start()

    next_ref[...] = by_chunk(blocks, right, jnp.zeros((8, slots), jnp.float32), None, leave_right)
    for source, target, at in ((u, u_ref, 0),) + leaving:
        wait_chunks(source, target, out_sems.at[at])


def backward_kernel(turning, last, layer, inputs, table_ref, scale_ref, gain_ref, end_gain_ref, *refs):
    sources, refs = refs[:inputs], refs[inputs:]
    slope_ref, z_ref, u_ref = sources[:3]
    parts, sources = sources[3 : 3 + PARTS], sources[3 + PARTS :]
    out_ref, own_grad, peer_grad = refs[:3]
    g, slope, z, u, h, w, gw, mid, top, goal = refs[3:13]
    in_sems, w_sems, out_sems, gw_sems = refs[13:]
    features, slots = g.shape
    size = w.shape[-1]
    chunk_blocks = w.shape[2]
    blocks = features // size
    fold = size // blocks

    left_in = factor_copies(parts, layer, w, w_sems, 0)
    right_in = factor_copies(parts, layer, w, w_sems, 1)
    g_ref, h_ref = sources[:2]
    if turning:
        for chunk in range(CHUNKS):
            chunk_copy(g_ref, top, in_sems.at[0], chunk).start()
            chunk_copy(sources[2], goal, in_sems.at[5], chunk).start()
    for copy in right_in:
        copy.start()
    for chunk in range(CHUNKS):
        if not turning:
            chunk_copy(g_ref, g, in_sems.at[0], chunk).start()
        chunk_copy(slope_ref, slope, in_sems.at[1], chunk).start()
        chunk_copy(z_ref, z, in_sems.at[2], chunk).start()
    for copy in left_in:
        copy.start()
    for chunk in range(CHUNKS):
        chunk_copy(u_ref, u, in_sems.at[3], chunk).start()
        chunk_copy(h_ref, h, in_sems.at[4], chunk).start()

    if turning:
        zero = jnp.zeros((8, slots), jnp.float32)

        def sums(block, nth, totals):
            rows = block_rows(block, size)
            part = top[rows, :]
            scaled = part * column(end_gain_ref, block, nth, slots)
            return [], (
                totals[0] + fold_rows(part * part),
                totals[1] + fold_rows(scaled * scaled),
                totals[2] + fold_rows(scaled * goal[rows, :].astype(jnp.float32)),
            )

        def arrive_top(chunk):
            chunk_copy(g_ref, top, in_sems.at[0], chunk).wait()
            chunk_copy(sources[2], goal, in_sems.at[5], chunk).wait()

        totals = by_chunk(blocks, sums, (zero, zero, zero), arrive_top)
        squares, gained, crossed = [jnp.sum(total, axis=0, keepdims=True) for total in totals]
        end_scale = lax.rsqrt(squares / features + EPSILON)
        end_back = end_scale * end_scale * end_scale * (end_scale * gained - crossed) / features

    for copy in right_in:
        copy.wait()

    def arrive_right(chunk):
        if not turning:
            chunk_copy(g_ref, g, in_sems.at[0], chunk).wait()
        chunk_copy(slope_ref, slope, in_sems.at[1], chunk).wait()
        chunk_copy(z_ref, z, in_sems.at[2], chunk).wait()

    def right(block, nth, total):
        rows = block_rows(block, size)
        place, home = table_ref[0, block], table_ref[2 if last else 1, block]
        at = (place // chunk_blocks, 1, place % chunk_blocks)
        to = (home // chunk_blocks, 1, home % chunk_blocks)
        if turning:
            part = top[rows, :]
            factor = column(end_gain_ref, block, nth, slots)
            error = (part * end_scale * factor - goal[rows, :].astype(jnp.float32)) * factor
            gradient = end_scale * error - part * end_back
            stores = [(g, (rows, slice(None)), gradient)]
        else:
            gradient = g[rows, :]
            stores = []
        steep = (gradient * slope[rows, :].astype(jnp.float32)).astype(jnp.bfloat16)
        taken = z[rows, :]
        back = inner_dot(w[at], steep, 1, 0)
        stores.append((gw, to, inner_dot(taken, steep, 1, 1).astype(jnp.bfloat16)))
        stores.append((mid, (rows, slice(None)), back))
        return stores, total + fold_rows(taken.astype(jnp.float32) * back)

    total = by_chunk(blocks, right, jnp.zeros((8, slots), jnp.float32), arrive_right)
    right_out = gradient_copies(gw, (own_grad, peer_grad), gw_sems, 1)
    for copy in right_out:
        copy.start()
    for copy in left_in:
        copy.wait()
    scale = scale_ref[0:1, :]
    back = scale * scale * jnp.sum(total, axis=0, keepdims=True) / features

    def arrive_left(chunk):
        chunk_copy(u_ref, u, in_sems.at[3], chunk).wait()
        chunk_copy(h_ref, h, in_sems.at[4], chunk).wait()

    def left(block, nth, carry):
        rows = block_rows(block, size)
        place, home = table_ref[0, block], table_ref[2 if last else 1, block]
        at = (place // chunk_blocks, 0, place % chunk_blocks)
        to = (home // chunk_blocks, 0, home % chunk_blocks)
        arrived = [mid[pl.ds(q * blocks + block, blocks, stride=size), :] for q in range(fold)]
        arrived = jnp.concatenate(arrived, axis=0).astype(jnp.bfloat16)
        factor_grad = inner_dot(u[rows, :], arrived, 1, 1).astype(jnp.bfloat16)
        weighted = inner_dot(w[at], arrived, 1, 0) * column(gain_ref, block, nth, slots)
        ended = g[rows, :] + scale * weighted - h[rows, :].astype(jnp.float32) * back
        index = (rows, slice(None))
        stores = [(gw, to, factor_grad)]
        stores.append((u, index, ended.astype(jnp.bfloat16)) if last else (g, index, ended))
        return stores, carry

    ended = u if last else g
    by_chunk(
        blocks, left, 0, arrive_left, lambda chunk: chunk_copy(ended, out_ref, out_sems, chunk).start()
    )
    left_out = gradient_copies(gw, (own_grad, peer_grad), gw_sems, 0)
    for copy in left_out:
        copy.start()
    wait_chunks(ended, out_ref, out_sems)
    for copy in right_out + left_out:
        copy.wait()


def shape_of(shape, dtype):
    return jax.ShapeDtypeStruct(shape, dtype)


SMEM = pl.BlockSpec(memory_space=pltpu.SMEM)
INSIDE = pl.BlockSpec(memory_space=pltpu.VMEM)
OUTSIDE = pl.BlockSpec(memory_space=pl.ANY)


def run_forward(table, gain, sums, residual, weights, layer):
    first = residual.dtype == jnp.bfloat16
    whole = residual.shape
    sources = (*weights, residual)
    held = (PARTS * weights[0].shape[0],) + weights[0].shape[2:]
    out_shape = (
        shape_of(whole, jnp.float32),
        shape_of(whole, jnp.bfloat16),
        shape_of(whole, jnp.bfloat16),
        shape_of(whole, jnp.bfloat16),
        shape_of((8, whole[1]), jnp.float32),
        shape_of((8, whole[1]), jnp.float32),
    )
    return pl.pallas_call(
        lambda *refs: forward_kernel(first, layer, len(sources), *refs),
        in_specs=[SMEM, INSIDE, INSIDE] + [OUTSIDE] * len(sources),
        out_specs=[OUTSIDE] * 4 + [INSIDE] * 2,
        out_shape=out_shape,
        scratch_shapes=[
            pltpu.VMEM(whole if first else SMALL, jnp.bfloat16),
            pltpu.VMEM(whole, jnp.float32),
            pltpu.VMEM(held, jnp.bfloat16),
            pltpu.VMEM(whole, jnp.bfloat16),
            pltpu.VMEM(whole, jnp.bfloat16),
            pltpu.VMEM(whole, jnp.bfloat16),
            pltpu.VMEM((whole[0] + held[-1], whole[1]), jnp.float32),
            pltpu.SemaphoreType.DMA((CHUNKS,)),
            pltpu.SemaphoreType.DMA((2, PARTS)),
            pltpu.SemaphoreType.DMA((4, CHUNKS)),
        ],
        compiler_params=pltpu.CompilerParams(vmem_limit_bytes=VMEM_LIMIT),
        cost_estimate=pl.CostEstimate(
            flops=FORWARD_COST, bytes_accessed=20 * whole[0] * whole[1], transcendentals=0
        ),
        name="forward_layer",
    )(table, sums, gain, *sources)


def run_backward(table, gain, end_gain, scale, kept, weights, layer, sources, turning, last):
    whole = kept[0].shape
    sources = (*kept, *weights, *sources)
    held = (PARTS * weights[0].shape[0],) + weights[0].shape[2:]
    half = (held[0] // 2,) + held[1:]
    out_shape = [shape_of(whole, jnp.bfloat16 if last else jnp.float32)] + [shape_of(half, jnp.bfloat16)] * 2
    return pl.pallas_call(
        lambda *refs: backward_kernel(turning, last, layer, len(sources), *refs),
        in_specs=[SMEM] + [INSIDE] * 3 + [OUTSIDE] * len(sources),
        out_specs=[OUTSIDE] * len(out_shape),
        out_shape=out_shape,
        scratch_shapes=[
            pltpu.VMEM(whole, jnp.float32),
            pltpu.VMEM(whole, jnp.bfloat16),
            pltpu.VMEM(whole, jnp.bfloat16),
            pltpu.VMEM(whole, jnp.bfloat16),
            pltpu.VMEM(whole, jnp.bfloat16 if last else jnp.float32),
            pltpu.VMEM(held, jnp.bfloat16),
            pltpu.VMEM(held, jnp.bfloat16),
            pltpu.VMEM((whole[0] + held[-1], whole[1]), jnp.float32),
            pltpu.VMEM(whole if turning else SMALL, jnp.float32),
            pltpu.VMEM(whole if turning else SMALL, jnp.bfloat16),
            pltpu.SemaphoreType.DMA((6, CHUNKS)),
            pltpu.SemaphoreType.DMA((2, PARTS)),
            pltpu.SemaphoreType.DMA((CHUNKS,)),
            pltpu.SemaphoreType.DMA((2, PARTS)),
        ],
        compiler_params=pltpu.CompilerParams(vmem_limit_bytes=VMEM_LIMIT),
        cost_estimate=pl.CostEstimate(
            flops=BACKWARD_COST, bytes_accessed=30 * whole[0] * whole[1], transcendentals=0
        ),
        name="backward_layer",
    )(table, scale, gain, end_gain, *sources)


def join_kernel(rows, *refs):
    sources, whole, sems = refs[:-2], refs[-2], refs[-1]
    copies = [
        pltpu.make_async_copy(source.at[pl.ds(0, rows)], whole.at[pl.ds(at * rows, rows)], sems.at[at])
        for at, source in enumerate(sources)
    ]
    for copy in copies:
        copy.start()
    for copy in copies:
        copy.wait()


def joined(parts, rows=None):
    rows = parts[0].shape[0] if rows is None else rows
    whole = shape_of((rows * len(parts),) + parts[0].shape[1:], parts[0].dtype)
    return pl.pallas_call(
        lambda *refs: join_kernel(rows, *refs),
        in_specs=[OUTSIDE] * len(parts),
        out_specs=INSIDE,
        out_shape=whole,
        scratch_shapes=[pltpu.SemaphoreType.DMA((len(parts),))],
        compiler_params=pltpu.CompilerParams(vmem_limit_bytes=VMEM_LIMIT),
        cost_estimate=pl.CostEstimate(
            flops=0, bytes_accessed=4 * math.prod(whole.shape), transcendentals=0
        ),
        name="join",
    )(*parts)


def order_kernel(ranges, place_ref, *refs):
    sources, whole, sems = refs[:-2], refs[-2], refs[-1]
    copies = []
    for distance, source in enumerate(sources):
        row = 0
        for start, count in ranges:
            target = whole.at[place_ref[0] ^ distance, pl.ds(row, count)]
            copies.append(pltpu.make_async_copy(source.at[pl.ds(start, count)], target, sems.at[len(copies)]))
            row += count
    for copy in copies:
        copy.start()
    for copy in copies:
        copy.wait()


def by_section(place, parts, ranges):
    rows = sum(count for _, count in ranges)
    whole = shape_of((len(parts), rows) + parts[0].shape[1:], parts[0].dtype)
    return pl.pallas_call(
        lambda *refs: order_kernel(ranges, *refs),
        in_specs=[SMEM] + [OUTSIDE] * len(parts),
        out_specs=INSIDE,
        out_shape=whole,
        scratch_shapes=[pltpu.SemaphoreType.DMA((len(parts) * len(ranges),))],
        compiler_params=pltpu.CompilerParams(vmem_limit_bytes=VMEM_LIMIT),
        cost_estimate=pl.CostEstimate(
            flops=0, bytes_accessed=4 * math.prod(whole.shape), transcendentals=0
        ),
        name="by_section",
    )(place, *parts)


def sum_kernel(terms, inputs, *refs):
    sources, outs = refs[:inputs], refs[inputs:]
    for group in range(inputs // terms):
        mine = sources[group * terms : (group + 1) * terms]
        for at in range(mine[0].shape[0]):
            total = sum(ref[at].astype(jnp.float32) for ref in mine).astype(jnp.bfloat16)
            if len(outs) > 1:
                outs[at][group] = total
            else:
                outs[0][at, group] = total


def run_sum(groups, parts, apart=True):
    flat = [term.reshape(parts, -1, term.shape[-1]) for terms in groups for term in terms]
    _, rows, lanes = flat[0].shape
    steps = 2
    if apart:
        out_shape = [shape_of((len(groups), rows, lanes), jnp.bfloat16)] * parts
        out_specs = [pl.BlockSpec((len(groups), rows // steps, lanes), lambda i: (0, i, 0))] * parts
    else:
        out_shape = [shape_of((parts, len(groups), rows, lanes), jnp.bfloat16)]
        out_specs = [pl.BlockSpec((parts, len(groups), rows // steps, lanes), lambda i: (0, 0, i, 0))]
    sums = pl.pallas_call(
        lambda *refs: sum_kernel(len(groups[0]), len(flat), *refs),
        grid=(steps,),
        in_specs=[pl.BlockSpec((parts, rows // steps, lanes), lambda i: (0, i, 0))] * len(flat),
        out_specs=out_specs,
        out_shape=out_shape,
        compiler_params=pltpu.CompilerParams(vmem_limit_bytes=VMEM_LIMIT),
        cost_estimate=pl.CostEstimate(
            flops=flat[0].size * len(flat), bytes_accessed=2 * flat[0].size * (len(flat) + 1), transcendentals=0
        ),
        name="sum",
    )(*flat)
    return [out.reshape(-1, lanes) for out in sums] if apart else sums[0].reshape(parts, -1, lanes)


def pieces_kernel(chunk, place_ref, order_ref, left_ref, right_ref, gain_ref, *refs):
    outs, (held, left_sem, sems) = refs[:-3], refs[-3:]
    layer_count, half, size = held.shape[:3]
    first = place_ref[2] * half
    lefts = pltpu.make_async_copy(left_ref.at[:, pl.ds(first, half)], held, left_sem.at[0])
    lefts.start()
    copies = []
    turns = []
    for distance, out in enumerate(outs):
        start = (place_ref[0] ^ distance) * chunk
        row = 0
        for layer in range(layer_count):
            for inside in range(chunk):
                turns.append((layer, start + inside, out, row))
                row += size
            for inside in range(chunk):
                source = right_ref.at[layer, first + start + inside]
                copies.append((source, out.at[pl.ds(row, size)]))
                row += size
        copies.append((gain_ref, out.at[pl.ds(row, gain_ref.shape[0])]))
    copies = [
        pltpu.make_async_copy(source, target, sems.at[at]) for at, (source, target) in enumerate(copies)
    ]
    for copy in copies:
        copy.start()
    lefts.wait()
    for layer, block, out, row in turns:
        turned = inner_dot(held[layer, block], order_ref[...], 1, 0)
        out[pl.ds(row, size), :] = turned.astype(jnp.bfloat16)
    for copy in copies:
        copy.wait()


def factor_pieces(place, order, left, right, gain_rows, chunk, width):
    layer_count, blocks, size = left.shape[:3]
    rows = layer_count * 2 * chunk * size + gain_rows.shape[0]
    return pl.pallas_call(
        lambda *refs: pieces_kernel(chunk, *refs),
        in_specs=[SMEM, INSIDE] + [OUTSIDE] * 3,
        out_specs=[INSIDE] * width,
        out_shape=[shape_of((rows, size), jnp.bfloat16)] * width,
        scratch_shapes=[
            pltpu.VMEM((layer_count, blocks // 2, size, size), jnp.bfloat16),
            pltpu.SemaphoreType.DMA((1,)),
            pltpu.SemaphoreType.DMA((width * (layer_count * chunk + 1),)),
        ],
        compiler_params=pltpu.CompilerParams(vmem_limit_bytes=VMEM_LIMIT),
        cost_estimate=pl.CostEstimate(flops=left.size * size, bytes_accessed=4 * left.size, transcendentals=0),
        name="pieces",
    )(place, order, left, right, gain_rows)


def choice(pairs, critic, slots):
    rows = pairs.shape[0]
    named = (pairs[:, 0:1] == critic) | (pairs[:, 1:2] == critic)
    named = jnp.broadcast_to(named.astype(jnp.float32), (rows, slots))
    before = lax.broadcasted_iota(jnp.int32, (rows, rows), 1) < lax.broadcasted_iota(jnp.int32, (rows, rows), 0)
    rank = inner_dot(before.astype(jnp.bfloat16), named.astype(jnp.bfloat16), 1, 0)
    at = lax.broadcasted_iota(jnp.int32, (rows, slots), 1).astype(jnp.float32)
    return jnp.where(rank == at, named, 0.0).astype(jnp.bfloat16)


def pick_kernel(pairs_ref, values_ref, out_ref):
    width, features, slots = out_ref.shape
    pairs = pairs_ref[...]
    chosen = [choice(pairs, critic, slots) for critic in range(width)]
    step = 512
    for start in range(0, features, step):
        part = values_ref[:, pl.ds(start, step)]
        for k in range(width):
            out_ref[k, pl.ds(start, step), :] = inner_dot(part, chosen[k], 0, 0).astype(jnp.bfloat16)


def run_pick(pairs, values, width, slots):
    rows, features = values.shape
    return pl.pallas_call(
        pick_kernel,
        in_specs=[INSIDE] * 2,
        out_specs=INSIDE,
        out_shape=shape_of((width, features, slots), jnp.bfloat16),
        compiler_params=pltpu.CompilerParams(vmem_limit_bytes=VMEM_LIMIT),
        cost_estimate=pl.CostEstimate(
            flops=2 * rows * features * slots * width, bytes_accessed=8 * rows * features, transcendentals=0
        ),
        name="pick",
    )(pairs, values)


def combine_kernel(pairs_ref, came_ref, out_ref):
    width, features, slots = came_ref.shape
    pairs = pairs_ref[...]
    chosen = [choice(pairs, critic, slots) for critic in range(width)]
    step = 512
    for start in range(0, features, step):
        total = sum(inner_dot(chosen[k], came_ref[k, pl.ds(start, step), :], 1, 1) for k in range(width))
        out_ref[:, pl.ds(start, step)] = (0.5 * total).astype(jnp.bfloat16)


def run_combine(pairs, came):
    rows = pairs.shape[0]
    return pl.pallas_call(
        combine_kernel,
        in_specs=[INSIDE] * 2,
        out_specs=INSIDE,
        out_shape=shape_of((rows, came.shape[1]), jnp.bfloat16),
        compiler_params=pltpu.CompilerParams(vmem_limit_bytes=VMEM_LIMIT),
        cost_estimate=pl.CostEstimate(
            flops=2 * rows * came.size, bytes_accessed=4 * came.size, transcendentals=0
        ),
        name="combine",
    )(pairs, came)


FORWARD_COST = 4_000_000_000
BACKWARD_COST = 5_000_000_000


def assemble_kernel(layers, factor, place_ref, order_ref, *refs):
    count = 2 * len(layers)
    sources, (left_ref, right_ref) = refs[:count], refs[count : count + 2]
    held, wide = refs[count + 2 : 2 * count + 2], refs[2 * count + 2 : 3 * count + 2]
    in_sems, out_sems = refs[3 * count + 2 :]
    origin, core = place_ref[0] ^ place_ref[1], place_ref[2]
    order = order_ref[...]
    arrivals = [
        pltpu.make_async_copy(source, held[at], in_sems.at[at]) for at, source in enumerate(sources)
    ]
    for copy in arrivals:
        copy.start()
    leaving = []
    for at in range(count):
        arrivals[at].wait()
        half = core if at % 2 == 0 else 1 - core
        width, _, _, chunk = held[at].shape[:4]
        for k in range(width):
            start = (half * width + (origin ^ k if at < 2 else k)) * chunk
            for inside, layer in enumerate(layers[at // 2]):
                for block in range(chunk):
                    left = inner_dot(held[at][k, inside, 0, block], order, 1, 1)
                    wide[at][k, inside, 0, block] = left * factor
                wide[at][k, inside, 1] = held[at][k, inside, 1].astype(jnp.float32) * factor
                for which, target in enumerate((left_ref, right_ref)):
                    copy = pltpu.make_async_copy(
                        wide[at].at[k, inside, which],
                        target.at[layer, pl.ds(start, chunk)],
                        out_sems.at[len(leaving)],
                    )
                    copy.start()
                    leaving.append(copy)
    for copy in leaving:
        copy.wait()


def run_assemble(place, order, pieces, layers, factor):
    piece = pieces[0].shape
    layer_count = sum(len(group) for group in layers)
    out = shape_of((layer_count, 2 * piece[0] * piece[3]) + piece[4:], jnp.float32)
    return pl.pallas_call(
        lambda *refs: assemble_kernel(layers, factor, *refs),
        in_specs=[SMEM, INSIDE] + [OUTSIDE] * len(pieces),
        out_specs=[OUTSIDE] * 2,
        out_shape=[out] * 2,
        scratch_shapes=[pltpu.VMEM(part.shape, jnp.bfloat16) for part in pieces]
        + [pltpu.VMEM(part.shape, jnp.float32) for part in pieces]
        + [
            pltpu.SemaphoreType.DMA((len(pieces),)),
            pltpu.SemaphoreType.DMA((4 * layer_count * piece[0],)),
        ],
        compiler_params=pltpu.CompilerParams(vmem_limit_bytes=VMEM_LIMIT),
        cost_estimate=pl.CostEstimate(flops=0, bytes_accessed=4 * math.prod(out.shape) * 3, transcendentals=0),
        name="assemble",
    )(place, order, *pieces)


def plane_routes(width, replicas):
    bits = width.bit_length() - 1
    orders = [[(step + d) % bits for step in range(bits)] for d in range(replicas)]
    every = [(s, t, d) for s in range(width) for t in range(width) for d in range(replicas)]

    def route(move):
        def index(s, t, d):
            return (s * width + t) * replicas + d

        return [(index(*place), index(*move(*place))) for place in every]

    ranks = [[0] * width for _ in range(replicas)]
    for d in range(replicas):
        for r in range(width):
            ranks[d][sum(((r >> at) & 1) << orders[d][at] for at in range(bits))] = r
    return {
        "across": [route(lambda s, t, d, at=at: (s ^ (1 << orders[d][at]), t, d)) for at in range(bits)],
        "cores": route(lambda s, t, d: (s, t, 1 - d)),
        "sections": [route(lambda s, t, d, k=k: (s ^ k, t, d)) for k in range(width)],
        "homes": [route(lambda s, t, d, j=j: (t, t ^ s ^ j, d)) for j in range(width)],
    }, ranks


def plane_shards(patches, teacher, critic_pairs, left_factors, right_factors, norm_gains):
    width = lax.axis_size("section")
    replicas = lax.axis_size("dp")
    tok_rows, feat_local = patches.shape
    layer_count, local_blocks, size = left_factors.shape[1:4]
    blocks = feat_local * width // size
    wide = 2 * tok_rows // 3
    chunk = local_blocks // (replicas * width)
    layer_rows = 2 * chunk * size
    routes, ranks = plane_routes(width, replicas)
    section = lax.axis_index("section")
    tensor = lax.axis_index("tensor")
    core = lax.axis_index("dp")
    place = jnp.stack([section, tensor, core]).astype(jnp.int32)
    tie = lax.optimization_barrier

    def move(value, route):
        return lax.ppermute(value, AXES, route)

    def move_all(values, name):
        return [move(value, route) for value, route in zip(values, routes[name])]

    def send(values, name):
        return [values[0]] + [move(values[k], routes[name][k]) for k in range(1, width)]

    def gather_two(pair):
        return pair, move(pair, routes["across"][1]), move(pair, routes["cores"])

    def gather_three(pair, other, peer):
        return [pair, other, peer, move(other, routes["cores"])]

    def as_weights(parts):
        return [part.reshape(2 * width, -1, 2, chunk, size, size) for part in parts]

    block = jnp.arange(blocks, dtype=jnp.int32)
    inside = block % local_blocks
    replica = inside // (width * chunk)
    part = (replica != core).astype(jnp.int32)
    distance = section ^ ((inside // chunk) % width)
    quarter = block // local_blocks
    rank = jnp.array(ranks, jnp.int32)[replica, distance]
    table = jnp.stack(
        [
            ((part * width + index) * width + piece) * chunk + inside % chunk
            for index, piece in (
                (rank, quarter),
                (distance, quarter),
                (distance, tensor ^ section ^ distance ^ quarter),
            )
        ]
    ).astype(jnp.int32)

    def to_planes(value):
        return lax.all_to_all(value, "tensor", split_axis=0, concat_axis=0, tiled=True)

    def to_sections(value):
        return lax.all_to_all(value, "section", split_axis=0, concat_axis=0, tiled=True)

    half_layers = layer_count // 2
    fold = size // blocks
    columns = jnp.arange(size)
    order = (columns[:, None] == (columns % blocks) * fold + columns // blocks).astype(jnp.bfloat16)
    gain_rows = norm_gains[0].reshape(-1, size)
    patch_sent = run_pick(critic_pairs, patches, width, wide)
    patch_sent, left, right, teacher = tie((patch_sent, left_factors[0], right_factors[0], teacher))
    patch_came = to_planes(patch_sent).reshape(-1, wide)
    pieces = factor_pieces(place, order, left, right, gain_rows, chunk, width)
    spread = send(pieces, "sections")
    cut, end = half_layers * layer_rows, layer_count * layer_rows
    first = by_section(place, spread, [(0, cut), (end, gain_rows.shape[0])])
    second = by_section(place, spread, [(cut, end - cut)])
    target_sent = run_pick(critic_pairs, teacher, width, wide)
    patch_came, first, second, target_sent = tie((patch_came, first, second, target_sent))
    first = to_planes(first)
    first, second = tie((first, second))
    second = to_planes(second)
    lowest = [first[:, at * layer_rows : (at + 1) * layer_rows] for at in range(half_layers)]
    beside = [move(value, routes["across"][0]) for value in lowest[:2]]
    gains = first[:, cut:].reshape(width, layer_count + 1, local_blocks, size)
    gains = gains.transpose(1, 3, 0, 2).reshape(layer_count + 1, size, blocks)
    end_gain = gains[layer_count].reshape(size, CHUNKS, blocks // CHUNKS).transpose(1, 0, 2)
    end_gain = end_gain.astype(jnp.float32)
    lowest, beside, gains, end_gain = tie((lowest, beside, gains, end_gain))
    flying = {0: gather_two(joined([lowest[0], beside[0]]))}
    flying, second, target_sent = tie((flying, second, target_sent))
    for layer in range(half_layers, layer_count):
        at = (layer - half_layers) * layer_rows
        lowest.append(second[:, at : at + layer_rows])
    target = to_planes(target_sent).reshape(-1, wide)
    weights = [as_weights(gather_three(*flying.pop(0)))]
    flying[1] = gather_two(joined([lowest[1], beside[1]]))
    steps = {2: (lowest[2], move(lowest[2], routes["across"][0]))}
    weights, flying, steps = tie((weights, flying, steps))

    residual = patch_came
    sums = jnp.zeros((8, wide), jnp.float32)
    stored = []
    for layer in range(layer_count):
        ahead = {}
        if layer + 1 < layer_count:
            ahead["weights"] = gather_three(*flying.pop(layer + 1))
        if layer + 2 < layer_count:
            ahead["two"] = gather_two(joined(list(steps.pop(layer + 2))))
        if layer + 3 < layer_count:
            ahead["one"] = (lowest[layer + 3], move(lowest[layer + 3], routes["across"][0]))
        following, u, z, slope, scale, sums = run_forward(
            table, gains[layer], sums, residual, weights[layer], 0
        )
        stored.append(((slope, z, u), scale, residual))
        residual, sums, ahead = tie((following, sums, ahead))
        if layer + 1 < layer_count:
            weights.append(as_weights(ahead["weights"]))
        if layer + 2 < layer_count:
            flying[layer + 2] = ahead["two"]
        if layer + 3 < layer_count:
            steps[layer + 3] = ahead["one"]
        if layer == layer_count - 2:
            residual, sums, target = tie((residual, sums, target))

    def core_sum(mine, other):
        return (mine, move(other, routes["cores"]))

    def plane_sum(mine, other):
        return send(run_sum([(mine, other)], width), "sections")

    def both_halves(whole):
        pair = (whole, move(whole, routes["cores"]))
        return [part.reshape(width, -1, 2, chunk, size, size) for part in pair]

    steps = (core_sum, plane_sum)
    gradient = residual
    underway = []
    for layer in range(layer_count - 1, -1, -1):
        turning = layer == layer_count - 1
        last = layer == 0
        kept, scale, inputs = stored[layer]
        sources = (gradient, inputs, target) if turning else (gradient, inputs)
        underway = [(at + 1, steps[at](*state)) if at < len(steps) else (at, state) for at, state in underway]
        gradient, mine, other = run_backward(
            table,
            gains[layer],
            end_gain,
            scale,
            kept,
            weights[layer],
            0,
            sources,
            turning,
            last,
        )
        gradient, mine, other, states = tie((gradient, mine, other, [state for _, state in underway]))
        underway = [(at, state) for (at, _), state in zip(underway, states)]
        underway.append((0, (mine, other)))

    returned = to_planes(gradient.reshape(width, feat_local, wide))
    ended = [steps[at](*state) if at < len(steps) else state for at, state in underway][::-1]
    ended = tie(ended)
    ended[0] = plane_sum(*ended[0])
    others = to_planes(run_sum(ended[1:], width, apart=False))
    home = run_sum(ended[:1], width)
    home, returned, others = tie((home, returned, others))
    home = move_all(home, "homes")
    d_patches = run_combine(critic_pairs, returned)
    others = to_sections(others)
    d_patches, home, others = tie((d_patches, home, others))
    homes_of = both_halves(joined(home)) + both_halves(others)
    grad_factor = 1.0 / math.sqrt(2 * tok_rows * width * replicas)
    grad_left, grad_right = run_assemble(
        place, order, homes_of, [(0,), tuple(range(1, layer_count))], grad_factor
    )
    return (d_patches, grad_left[None], grad_right[None])


def solution(mesh):
    in_specs = (
        P(("section", "dp"), "tensor"),
        P(("section", "dp"), "tensor"),
        P(("section", "dp"), None),
        P("section", None, "tensor", None, None),
        P("section", None, "tensor", None, None),
        P("section", None, "tensor"),
    )
    out_specs = (
        P(("section", "dp"), "tensor"),
        P("section", None, "tensor", None, None),
        P("section", None, "tensor", None, None),
    )
    body = plane_shards if planes_fit(mesh) else layered_shards
    return jax.shard_map(
        body, mesh=mesh, in_specs=in_specs, out_specs=out_specs, check_vma=False)
```

```python
import math

import jax
import jax.numpy as jnp
from jax import lax
from jax.experimental import pallas as pl
from jax.experimental.pallas import tpu as pltpu
from jax.sharding import PartitionSpec as P

EPSILON = 1e-06
TANH_SLOPE = 0.7978845608028654
CUBIC_TERM = 0.044715


def shifted(value, axis, steps):
    count = lax.axis_size(axis)
    first, last = (max(0, -steps), min(count, count - steps))
    return lax.ppermute(value, axis, [(source, source + steps) for source in range(first, last)])


def gelu_value(values):
    tangent = jnp.tanh(TANH_SLOPE * (values + CUBIC_TERM * values * values * values))
    return 0.5 * values * (1.0 + tangent)


def gelu_slope(values):
    tangent = jnp.tanh(TANH_SLOPE * (values + CUBIC_TERM * values * values * values))
    return 0.5 * (1.0 + tangent) + 0.5 * values * (1.0 - tangent * tangent) * TANH_SLOPE * (
        1.0 + 3.0 * CUBIC_TERM * values * values
    )


def norm_pair(residuals, gain_pair, model_width):
    squares = lax.psum(
        (
            jnp.sum(residuals[0] * residuals[0], axis=(1, 2)),
            jnp.sum(residuals[1] * residuals[1], axis=(1, 2)),
        ),
        "tensor",
    )
    factors = [lax.rsqrt(squares[member] / model_width + EPSILON) for member in range(2)]
    normed = [
        residuals[member] * factors[member][:, None, None] * gain_pair[member][None]
        for member in range(2)
    ]
    return (factors, normed)


def norm_back_pair(residuals, factors, gain_pair, grad_normed, carried, model_width):
    weighted = [grad_normed[member] * gain_pair[member][None] for member in range(2)]
    inners = lax.psum(
        (
            jnp.sum(weighted[0] * residuals[0], axis=(1, 2)),
            jnp.sum(weighted[1] * residuals[1], axis=(1, 2)),
        ),
        "tensor",
    )
    return [
        carried[member]
        + factors[member][:, None, None] * weighted[member]
        - residuals[member] * (factors[member] ** 3 * inners[member] / model_width)[:, None, None]
        for member in range(2)
    ]


def layered_shards(patches, teacher, critic_pairs, left_factors, right_factors, norm_gains):
    sections = lax.axis_size("section")
    tensor_width = lax.axis_size("tensor")
    replicas = lax.axis_size("dp")
    tok_rows = patches.shape[0]
    feat_local = patches.shape[1]
    layer_count = left_factors.shape[1]
    local_blocks = left_factors.shape[2]
    block_size = left_factors.shape[3]
    all_blocks = local_blocks * tensor_width
    fold_ratio = block_size // all_blocks
    model_width = feat_local * tensor_width
    sixth_rows = tok_rows // 6
    leading = 2 * sixth_rows
    critic_ids = jnp.arange(4, dtype=jnp.int32)
    named_by = (
        (critic_pairs[:, 0:1] == critic_ids[None, :])
        | (critic_pairs[:, 1:2] == critic_ids[None, :])
    ).astype(jnp.int32)
    ranking = jnp.cumsum(named_by, axis=0) - 1
    wide_ids = critic_ids[None, :] < 2
    slot_width = 3 * sixth_rows
    spilled = wide_ids & (ranking >= 3 * sixth_rows)
    destination = jnp.where(spilled, critic_ids[None, :] + 2, critic_ids[None, :])
    slot_index = jnp.where(spilled, ranking - sixth_rows, ranking)
    flat_slot = destination * slot_width + slot_index
    chosen = jnp.take_along_axis(flat_slot, critic_pairs, axis=1)
    slot_total = sections * slot_width
    row_ids = jnp.broadcast_to(jnp.arange(tok_rows, dtype=jnp.int32)[:, None], chosen.shape)
    source_row = (
        jnp.full((slot_total,), tok_rows, jnp.int32).at[chosen.reshape(-1)].set(row_ids.reshape(-1))
    )
    send_patch = (
        patches.at[source_row]
        .get(mode="fill", fill_value=0)
        .reshape(sections, slot_width, local_blocks, block_size)
    )
    send_target = (
        teacher.at[source_row]
        .get(mode="fill", fill_value=0)
        .reshape(sections, slot_width, local_blocks, block_size)
    )
    recv_patch, recv_target = (
        lax.all_to_all(send_patch, "section", split_axis=0, concat_axis=0, tiled=True),
        lax.all_to_all(send_target, "section", split_axis=0, concat_axis=0, tiled=True),
    )
    residuals = [
        recv_patch[:, :leading].reshape(-1, local_blocks, block_size).astype(jnp.float32),
        recv_patch[:, leading:].reshape(-1, local_blocks, block_size).astype(jnp.float32),
    ]
    targets = [
        recv_target[:, :leading].reshape(-1, local_blocks, block_size).astype(jnp.float32),
        recv_target[:, leading:].reshape(-1, local_blocks, block_size).astype(jnp.float32),
    ]
    native = (left_factors[0], right_factors[0], norm_gains[0])
    borrowed = shifted((left_factors, right_factors, norm_gains), "section", 2)
    is_wide = lax.axis_index("section") < 2
    second = (
        jnp.where(is_wide, left_factors, borrowed[0])[0],
        jnp.where(is_wide, right_factors, borrowed[1])[0],
        jnp.where(is_wide, norm_gains, borrowed[2])[0],
    )
    left_sets = (native[0], second[0])
    right_sets = (native[1], second[1])
    gain_sets = (
        native[2].astype(jnp.float32).reshape(layer_count + 1, local_blocks, block_size),
        second[2].astype(jnp.float32).reshape(layer_count + 1, local_blocks, block_size),
    )
    stored = []
    for layer_index in range(layer_count):
        gain_pair = [gain_sets[0][layer_index], gain_sets[1][layer_index]]
        factors, normed = norm_pair(residuals, gain_pair, model_width)
        normed = [normed[member].astype(jnp.bfloat16) for member in range(2)]
        first_out = [
            jnp.einsum(
                "nki,kij->nkj",
                normed[member],
                left_sets[member][layer_index],
                preferred_element_type=jnp.float32,
            ).astype(jnp.bfloat16)
            for member in range(2)
        ]
        permuted = (
            lax.all_to_all(first_out[0], "tensor", split_axis=2, concat_axis=1, tiled=True),
            lax.all_to_all(first_out[1], "tensor", split_axis=2, concat_axis=1, tiled=True),
        )
        permuted = [
            permuted[member].reshape(
                permuted[member].shape[0], all_blocks, local_blocks, fold_ratio
            )
            for member in range(2)
        ]
        right_quads = [
            right_sets[member][layer_index].reshape(
                local_blocks, fold_ratio, all_blocks, block_size
            )
            for member in range(2)
        ]
        mixture = [
            jnp.einsum(
                "nkmp,mpkl->nml",
                permuted[member],
                right_quads[member],
                preferred_element_type=jnp.float32,
            )
            for member in range(2)
        ]
        stored.append((residuals, factors, normed, permuted, mixture, right_quads, gain_pair))
        residuals = [residuals[member] + gelu_value(mixture[member]) for member in range(2)]
    final_gains = [gain_sets[0][layer_count], gain_sets[1][layer_count]]
    factors, outputs = norm_pair(residuals, final_gains, model_width)
    gradients = norm_back_pair(
        residuals,
        factors,
        final_gains,
        [outputs[member] - targets[member] for member in range(2)],
        [jnp.zeros_like(residuals[member]) for member in range(2)],
        model_width,
    )
    left_terms = []
    right_terms = []
    for layer_index in range(layer_count - 1, -1, -1):
        inputs, factors, normed, permuted, mixture, right_quads, gain_pair = stored[layer_index]
        slopes = [
            (gradients[member] * gelu_slope(mixture[member])).astype(jnp.bfloat16)
            for member in range(2)
        ]
        right_grad = [
            jnp.einsum(
                "nkmp,nml->mpkl",
                permuted[member],
                slopes[member],
                preferred_element_type=jnp.float32,
            ).reshape(local_blocks, block_size, block_size)
            for member in range(2)
        ]
        back_moved = [
            jnp.einsum(
                "nml,mpkl->nkmp",
                slopes[member],
                right_quads[member],
                preferred_element_type=jnp.float32,
            )
            .astype(jnp.bfloat16)
            .reshape(slopes[member].shape[0], all_blocks, local_blocks * fold_ratio)
            for member in range(2)
        ]
        arrived = (
            lax.all_to_all(back_moved[0], "tensor", split_axis=1, concat_axis=2, tiled=True),
            lax.all_to_all(back_moved[1], "tensor", split_axis=1, concat_axis=2, tiled=True),
        )
        left_grad = [
            jnp.einsum(
                "nki,nkj->kij", normed[member], arrived[member], preferred_element_type=jnp.float32
            )
            for member in range(2)
        ]
        grad_normed = [
            jnp.einsum(
                "nkj,kij->nki",
                arrived[member],
                left_sets[member][layer_index],
                preferred_element_type=jnp.float32,
            )
            for member in range(2)
        ]
        gradients = norm_back_pair(inputs, factors, gain_pair, grad_normed, gradients, model_width)
        layer_left = jnp.stack(left_grad)
        layer_right = jnp.stack(right_grad)
        layer_left, layer_right = (
            lax.psum(layer_left.astype(jnp.bfloat16), "dp").astype(jnp.float32),
            lax.psum(layer_right.astype(jnp.bfloat16), "dp").astype(jnp.float32),
        )
        left_terms.insert(0, layer_left)
        right_terms.insert(0, layer_right)
    left_stack = jnp.stack(left_terms)
    right_stack = jnp.stack(right_terms)
    repaid = (
        shifted(left_stack[:, 1].astype(jnp.bfloat16), "section", -2).astype(jnp.float32),
        shifted(right_stack[:, 1].astype(jnp.bfloat16), "section", -2).astype(jnp.float32),
    )
    is_wide = lax.axis_index("section") < 2
    left_total = left_stack[:, 0] + jnp.where(is_wide, left_stack[:, 1] + repaid[0], 0.0)
    right_total = right_stack[:, 0] + jnp.where(is_wide, right_stack[:, 1] + repaid[1], 0.0)
    grad_factor = 1.0 / math.sqrt(2 * tok_rows * sections * replicas)
    returned = [
        gradients[member].astype(jnp.bfloat16).reshape(sections, -1, local_blocks, block_size)
        for member in range(2)
    ]
    back_lead, back_trail = (
        lax.all_to_all(returned[0], "section", split_axis=0, concat_axis=0, tiled=True),
        lax.all_to_all(returned[1], "section", split_axis=0, concat_axis=0, tiled=True),
    )
    gathered = jnp.concatenate((back_lead, back_trail), axis=1).reshape(
        slot_total, local_blocks, block_size
    )
    combined = (
        gathered[chosen[:, 0]].astype(jnp.float32) + gathered[chosen[:, 1]].astype(jnp.float32)
    ) * 0.5
    d_patches = combined.astype(jnp.bfloat16).reshape(tok_rows, feat_local)
    return (d_patches, (left_total * grad_factor)[None], (right_total * grad_factor)[None])


VMEM_LIMIT = 60 * 1024 * 1024
CHUNKS = 8
TOGETHER = 4
PARTS = 4
SMALL = (16, 128)
AXES = ("section", "tensor", "dp")


def planes_fit(mesh):
    sections = mesh.shape["section"]
    paired = mesh.shape["dp"] == 2 and sections & (sections - 1) == 0
    return paired and mesh.shape["tensor"] == sections


def inner_dot(left, right, left_dim, right_dim):
    return lax.dot_general(
        left,
        right,
        (((left_dim,), (right_dim,)), ((), ())),
        preferred_element_type=jnp.float32,
    )


def fold_rows(values):
    return jnp.sum(values.reshape(values.shape[0] // 8, 8, values.shape[1]), axis=0)


def block_rows(block, size):
    return pl.ds(pl.multiple_of(block * size, size), size)


def column(gain_ref, block, at, slots):
    if len(gain_ref.shape) == 3:
        gains = gain_ref[block // gain_ref.shape[2]]
        return jnp.broadcast_to(gains[:, at : at + 1], (gains.shape[0], slots))
    picked = lax.broadcasted_iota(jnp.int32, (gain_ref.shape[1], slots), 0) == block
    return inner_dot(gain_ref[...], picked.astype(jnp.bfloat16), 1, 0)


def chunk_copy(source, target, sems, chunk):
    rows = target.shape[0] // CHUNKS
    at = pl.ds(pl.multiple_of(chunk * rows, rows), rows)
    return pltpu.make_async_copy(source.at[at], target.at[at], sems.at[chunk])


def start_chunks(source, target, sems):
    for chunk in range(CHUNKS):
        chunk_copy(source, target, sems, chunk).start()


def wait_chunks(source, target, sems):
    for chunk in range(CHUNKS):
        chunk_copy(source, target, sems, chunk).wait()


def factor_copies(parts, layer, held, sems, side):
    count = parts[0].shape[0]
    return [
        pltpu.make_async_copy(
            ref.at[:, layer, side], held.at[pl.ds(at * count, count), side], sems.at[side, at]
        )
        for at, ref in enumerate(parts)
    ]


def gradient_copies(held, parts, sems, side):
    count = parts[0].shape[0]
    return [
        pltpu.make_async_copy(
            held.at[pl.ds(at * count, count), side], ref.at[:, side], sems.at[side, at]
        )
        for at, ref in enumerate(parts)
    ]


def by_chunk(blocks, step, carry, before=None, after=None):
    per_chunk = blocks // CHUNKS

    def few(start, first, carry):
        stores = []
        for at in range(TOGETHER):
            made, carry = step(start + at, first + at, carry)
            stores += made
        for ref, index, value in stores:
            ref[index] = value
        return carry

    def one(chunk, carry):
        if before is not None:
            before(chunk)
        for at in range(0, per_chunk, TOGETHER):
            carry = few(chunk * per_chunk + at, at, carry)
        if after is not None:
            after(chunk)
        return carry

    return lax.fori_loop(0, CHUNKS, one, carry)


def forward_kernel(first, layer, inputs, table_ref, sums_ref, gain_ref, *refs):
    sources, refs = refs[:inputs], refs[inputs:]
    parts, sources = sources[:PARTS], sources[PARTS:]
    out_ref, u_ref, z_ref, slope_ref, scale_ref, next_ref = refs[:6]
    raw, h, w, u, z, slope, mid, in_sems, w_sems, out_sems = refs[6:]
    features, slots = h.shape
    size = w.shape[-1]
    chunk_blocks = w.shape[2]
    blocks = features // size
    fold = size // blocks

    left_in = factor_copies(parts, layer, w, w_sems, 0)
    right_in = factor_copies(parts, layer, w, w_sems, 1)
    if first:
        start_chunks(sources[0], raw, in_sems)
        for copy in left_in + right_in:
            copy.start()

        def squares(block, _, total):
            rows = block_rows(block, size)
            part = raw[rows, :].astype(jnp.float32)
            return [(h, (rows, slice(None)), part)], total + fold_rows(part * part)

        total = by_chunk(
            blocks,
            squares,
            jnp.zeros((8, slots), jnp.float32),
            lambda chunk: chunk_copy(sources[0], raw, in_sems, chunk).wait(),
        )
    else:
        for copy in left_in:
            copy.start()
        start_chunks(sources[0], h, in_sems)
        for copy in right_in:
            copy.start()
        total = sums_ref[...]
    scale = lax.rsqrt(jnp.sum(total, axis=0, keepdims=True) / features + EPSILON)
    scale_ref[...] = jnp.broadcast_to(scale, scale_ref.shape)
    for copy in left_in:
        copy.wait()

    def arrive(chunk):
        if not first:
            chunk_copy(sources[0], h, in_sems, chunk).wait()

    def left(block, nth, carry):
        rows = block_rows(block, size)
        place = table_ref[0, block]
        normed = (h[rows, :] * scale * column(gain_ref, block, nth, slots)).astype(jnp.bfloat16)
        weight = w[place // chunk_blocks, 0, place % chunk_blocks]
        first_out = inner_dot(weight, normed, 0, 0)
        at = (rows, slice(None))
        return [(u, at, normed), (mid, at, first_out)], carry

    def leave_left(chunk):
        chunk_copy(u, u_ref, out_sems.at[0], chunk).start()

    by_chunk(blocks, left, 0, arrive, leave_left)
    for copy in right_in:
        copy.wait()

    def right(block, nth, total):
        rows = block_rows(block, size)
        place = table_ref[0, block]
        moved = [mid[pl.ds(q * blocks + block, blocks, stride=size), :] for q in range(fold)]
        moved = jnp.concatenate(moved, axis=0).astype(jnp.bfloat16)
        weight = w[place // chunk_blocks, 1, place % chunk_blocks]
        mixture = inner_dot(weight, moved, 0, 0)
        squared = mixture * mixture
        tangent = jnp.tanh(mixture * (TANH_SLOPE + (TANH_SLOPE * CUBIC_TERM) * squared))
        half = 0.5 + 0.5 * tangent
        following = h[rows, :] + mixture * half
        steep = half + mixture * (1.0 - tangent * tangent) * (
            0.5 * TANH_SLOPE + (1.5 * TANH_SLOPE * CUBIC_TERM) * squared
        )
        at = (rows, slice(None))
        stores = [(z, at, moved), (h, at, following), (slope, at, steep.astype(jnp.bfloat16))]
        return stores, total + fold_rows(following * following)

    leaving = ((h, out_ref, 1), (z, z_ref, 2), (slope, slope_ref, 3))

    def leave_right(chunk):
        for source, target, at in leaving:
            chunk_copy(source, target, out_sems.at[at], chunk).start()

    next_ref[...] = by_chunk(blocks, right, jnp.zeros((8, slots), jnp.float32), None, leave_right)
    for source, target, at in ((u, u_ref, 0),) + leaving:
        wait_chunks(source, target, out_sems.at[at])


def backward_kernel(turning, last, layer, inputs, table_ref, scale_ref, gain_ref, end_gain_ref, *refs):
    sources, refs = refs[:inputs], refs[inputs:]
    slope_ref, z_ref, u_ref = sources[:3]
    parts, sources = sources[3 : 3 + PARTS], sources[3 + PARTS :]
    out_ref, own_grad, peer_grad = refs[:3]
    g, slope, z, u, h, w, gw, mid, top, goal = refs[3:13]
    in_sems, w_sems, out_sems, gw_sems = refs[13:]
    features, slots = g.shape
    size = w.shape[-1]
    chunk_blocks = w.shape[2]
    blocks = features // size
    fold = size // blocks

    left_in = factor_copies(parts, layer, w, w_sems, 0)
    right_in = factor_copies(parts, layer, w, w_sems, 1)
    g_ref, h_ref = sources[:2]
    if turning:
        for chunk in range(CHUNKS):
            chunk_copy(g_ref, top, in_sems.at[0], chunk).start()
            chunk_copy(sources[2], goal, in_sems.at[5], chunk).start()
    for copy in right_in:
        copy.start()
    for chunk in range(CHUNKS):
        if not turning:
            chunk_copy(g_ref, g, in_sems.at[0], chunk).start()
        chunk_copy(slope_ref, slope, in_sems.at[1], chunk).start()
        chunk_copy(z_ref, z, in_sems.at[2], chunk).start()
    for copy in left_in:
        copy.start()
    for chunk in range(CHUNKS):
        chunk_copy(u_ref, u, in_sems.at[3], chunk).start()
        chunk_copy(h_ref, h, in_sems.at[4], chunk).start()

    if turning:
        zero = jnp.zeros((8, slots), jnp.float32)

        def sums(block, nth, totals):
            rows = block_rows(block, size)
            part = top[rows, :]
            scaled = part * column(end_gain_ref, block, nth, slots)
            return [], (
                totals[0] + fold_rows(part * part),
                totals[1] + fold_rows(scaled * scaled),
                totals[2] + fold_rows(scaled * goal[rows, :].astype(jnp.float32)),
            )

        def arrive_top(chunk):
            chunk_copy(g_ref, top, in_sems.at[0], chunk).wait()
            chunk_copy(sources[2], goal, in_sems.at[5], chunk).wait()

        totals = by_chunk(blocks, sums, (zero, zero, zero), arrive_top)
        squares, gained, crossed = [jnp.sum(total, axis=0, keepdims=True) for total in totals]
        end_scale = lax.rsqrt(squares / features + EPSILON)
        end_back = end_scale * end_scale * end_scale * (end_scale * gained - crossed) / features

    for copy in right_in:
        copy.wait()

    def arrive_right(chunk):
        if not turning:
            chunk_copy(g_ref, g, in_sems.at[0], chunk).wait()
        chunk_copy(slope_ref, slope, in_sems.at[1], chunk).wait()
        chunk_copy(z_ref, z, in_sems.at[2], chunk).wait()

    def right(block, nth, total):
        rows = block_rows(block, size)
        place, home = table_ref[0, block], table_ref[2 if last else 1, block]
        at = (place // chunk_blocks, 1, place % chunk_blocks)
        to = (home // chunk_blocks, 1, home % chunk_blocks)
        if turning:
            part = top[rows, :]
            factor = column(end_gain_ref, block, nth, slots)
            error = (part * end_scale * factor - goal[rows, :].astype(jnp.float32)) * factor
            gradient = end_scale * error - part * end_back
            stores = [(g, (rows, slice(None)), gradient)]
        else:
            gradient = g[rows, :]
            stores = []
        steep = (gradient * slope[rows, :].astype(jnp.float32)).astype(jnp.bfloat16)
        taken = z[rows, :]
        back = inner_dot(w[at], steep, 1, 0)
        stores.append((gw, to, inner_dot(taken, steep, 1, 1).astype(jnp.bfloat16)))
        stores.append((mid, (rows, slice(None)), back))
        return stores, total + fold_rows(taken.astype(jnp.float32) * back)

    total = by_chunk(blocks, right, jnp.zeros((8, slots), jnp.float32), arrive_right)
    right_out = gradient_copies(gw, (own_grad, peer_grad), gw_sems, 1)
    for copy in right_out:
        copy.start()
    for copy in left_in:
        copy.wait()
    scale = scale_ref[0:1, :]
    back = scale * scale * jnp.sum(total, axis=0, keepdims=True) / features

    def arrive_left(chunk):
        chunk_copy(u_ref, u, in_sems.at[3], chunk).wait()
        chunk_copy(h_ref, h, in_sems.at[4], chunk).wait()

    def left(block, nth, carry):
        rows = block_rows(block, size)
        place, home = table_ref[0, block], table_ref[2 if last else 1, block]
        at = (place // chunk_blocks, 0, place % chunk_blocks)
        to = (home // chunk_blocks, 0, home % chunk_blocks)
        arrived = [mid[pl.ds(q * blocks + block, blocks, stride=size), :] for q in range(fold)]
        arrived = jnp.concatenate(arrived, axis=0).astype(jnp.bfloat16)
        factor_grad = inner_dot(u[rows, :], arrived, 1, 1).astype(jnp.bfloat16)
        weighted = inner_dot(w[at], arrived, 1, 0) * column(gain_ref, block, nth, slots)
        ended = g[rows, :] + scale * weighted - h[rows, :].astype(jnp.float32) * back
        index = (rows, slice(None))
        stores = [(gw, to, factor_grad)]
        stores.append((u, index, ended.astype(jnp.bfloat16)) if last else (g, index, ended))
        return stores, carry

    ended = u if last else g
    by_chunk(
        blocks, left, 0, arrive_left, lambda chunk: chunk_copy(ended, out_ref, out_sems, chunk).start()
    )
    left_out = gradient_copies(gw, (own_grad, peer_grad), gw_sems, 0)
    for copy in left_out:
        copy.start()
    wait_chunks(ended, out_ref, out_sems)
    for copy in right_out + left_out:
        copy.wait()


def shape_of(shape, dtype):
    return jax.ShapeDtypeStruct(shape, dtype)


SMEM = pl.BlockSpec(memory_space=pltpu.SMEM)
INSIDE = pl.BlockSpec(memory_space=pltpu.VMEM)
OUTSIDE = pl.BlockSpec(memory_space=pl.ANY)


def run_forward(table, gain, sums, residual, weights, layer):
    first = residual.dtype == jnp.bfloat16
    whole = residual.shape
    sources = (*weights, residual)
    held = (PARTS * weights[0].shape[0],) + weights[0].shape[2:]
    out_shape = (
        shape_of(whole, jnp.float32),
        shape_of(whole, jnp.bfloat16),
        shape_of(whole, jnp.bfloat16),
        shape_of(whole, jnp.bfloat16),
        shape_of((8, whole[1]), jnp.float32),
        shape_of((8, whole[1]), jnp.float32),
    )
    return pl.pallas_call(
        lambda *refs: forward_kernel(first, layer, len(sources), *refs),
        in_specs=[SMEM, INSIDE, INSIDE] + [OUTSIDE] * len(sources),
        out_specs=[OUTSIDE] * 4 + [INSIDE] * 2,
        out_shape=out_shape,
        scratch_shapes=[
            pltpu.VMEM(whole if first else SMALL, jnp.bfloat16),
            pltpu.VMEM(whole, jnp.float32),
            pltpu.VMEM(held, jnp.bfloat16),
            pltpu.VMEM(whole, jnp.bfloat16),
            pltpu.VMEM(whole, jnp.bfloat16),
            pltpu.VMEM(whole, jnp.bfloat16),
            pltpu.VMEM((whole[0] + held[-1], whole[1]), jnp.float32),
            pltpu.SemaphoreType.DMA((CHUNKS,)),
            pltpu.SemaphoreType.DMA((2, PARTS)),
            pltpu.SemaphoreType.DMA((4, CHUNKS)),
        ],
        compiler_params=pltpu.CompilerParams(vmem_limit_bytes=VMEM_LIMIT),
        cost_estimate=pl.CostEstimate(
            flops=FORWARD_COST, bytes_accessed=20 * whole[0] * whole[1], transcendentals=0
        ),
        name="forward_layer",
    )(table, sums, gain, *sources)


def run_backward(table, gain, end_gain, scale, kept, weights, layer, sources, turning, last):
    whole = kept[0].shape
    sources = (*kept, *weights, *sources)
    held = (PARTS * weights[0].shape[0],) + weights[0].shape[2:]
    half = (held[0] // 2,) + held[1:]
    out_shape = [shape_of(whole, jnp.bfloat16 if last else jnp.float32)] + [shape_of(half, jnp.bfloat16)] * 2
    return pl.pallas_call(
        lambda *refs: backward_kernel(turning, last, layer, len(sources), *refs),
        in_specs=[SMEM] + [INSIDE] * 3 + [OUTSIDE] * len(sources),
        out_specs=[OUTSIDE] * len(out_shape),
        out_shape=out_shape,
        scratch_shapes=[
            pltpu.VMEM(whole, jnp.float32),
            pltpu.VMEM(whole, jnp.bfloat16),
            pltpu.VMEM(whole, jnp.bfloat16),
            pltpu.VMEM(whole, jnp.bfloat16),
            pltpu.VMEM(whole, jnp.bfloat16 if last else jnp.float32),
            pltpu.VMEM(held, jnp.bfloat16),
            pltpu.VMEM(held, jnp.bfloat16),
            pltpu.VMEM((whole[0] + held[-1], whole[1]), jnp.float32),
            pltpu.VMEM(whole if turning else SMALL, jnp.float32),
            pltpu.VMEM(whole if turning else SMALL, jnp.bfloat16),
            pltpu.SemaphoreType.DMA((6, CHUNKS)),
            pltpu.SemaphoreType.DMA((2, PARTS)),
            pltpu.SemaphoreType.DMA((CHUNKS,)),
            pltpu.SemaphoreType.DMA((2, PARTS)),
        ],
        compiler_params=pltpu.CompilerParams(vmem_limit_bytes=VMEM_LIMIT),
        cost_estimate=pl.CostEstimate(
            flops=BACKWARD_COST, bytes_accessed=30 * whole[0] * whole[1], transcendentals=0
        ),
        name="backward_layer",
    )(table, scale, gain, end_gain, *sources)


def join_kernel(rows, *refs):
    sources, whole, sems = refs[:-2], refs[-2], refs[-1]
    copies = [
        pltpu.make_async_copy(source.at[pl.ds(0, rows)], whole.at[pl.ds(at * rows, rows)], sems.at[at])
        for at, source in enumerate(sources)
    ]
    for copy in copies:
        copy.start()
    for copy in copies:
        copy.wait()


def joined(parts, rows=None):
    rows = parts[0].shape[0] if rows is None else rows
    whole = shape_of((rows * len(parts),) + parts[0].shape[1:], parts[0].dtype)
    return pl.pallas_call(
        lambda *refs: join_kernel(rows, *refs),
        in_specs=[OUTSIDE] * len(parts),
        out_specs=INSIDE,
        out_shape=whole,
        scratch_shapes=[pltpu.SemaphoreType.DMA((len(parts),))],
        compiler_params=pltpu.CompilerParams(vmem_limit_bytes=VMEM_LIMIT),
        cost_estimate=pl.CostEstimate(
            flops=0, bytes_accessed=4 * math.prod(whole.shape), transcendentals=0
        ),
        name="join",
    )(*parts)


def order_kernel(ranges, place_ref, *refs):
    sources, whole, sems = refs[:-2], refs[-2], refs[-1]
    copies = []
    for distance, source in enumerate(sources):
        row = 0
        for start, count in ranges:
            target = whole.at[place_ref[0] ^ distance, pl.ds(row, count)]
            copies.append(pltpu.make_async_copy(source.at[pl.ds(start, count)], target, sems.at[len(copies)]))
            row += count
    for copy in copies:
        copy.start()
    for copy in copies:
        copy.wait()


def by_section(place, parts, ranges):
    rows = sum(count for _, count in ranges)
    whole = shape_of((len(parts), rows) + parts[0].shape[1:], parts[0].dtype)
    return pl.pallas_call(
        lambda *refs: order_kernel(ranges, *refs),
        in_specs=[SMEM] + [OUTSIDE] * len(parts),
        out_specs=INSIDE,
        out_shape=whole,
        scratch_shapes=[pltpu.SemaphoreType.DMA((len(parts) * len(ranges),))],
        compiler_params=pltpu.CompilerParams(vmem_limit_bytes=VMEM_LIMIT),
        cost_estimate=pl.CostEstimate(
            flops=0, bytes_accessed=4 * math.prod(whole.shape), transcendentals=0
        ),
        name="by_section",
    )(place, *parts)


def sum_kernel(terms, inputs, *refs):
    sources, outs = refs[:inputs], refs[inputs:]
    for group in range(inputs // terms):
        mine = sources[group * terms : (group + 1) * terms]
        for at in range(mine[0].shape[0]):
            total = sum(ref[at].astype(jnp.float32) for ref in mine).astype(jnp.bfloat16)
            if len(outs) > 1:
                outs[at][group] = total
            else:
                outs[0][at, group] = total


def run_sum(groups, parts, apart=True):
    flat = [term.reshape(parts, -1, term.shape[-1]) for terms in groups for term in terms]
    _, rows, lanes = flat[0].shape
    steps = 2
    if apart:
        out_shape = [shape_of((len(groups), rows, lanes), jnp.bfloat16)] * parts
        out_specs = [pl.BlockSpec((len(groups), rows // steps, lanes), lambda i: (0, i, 0))] * parts
    else:
        out_shape = [shape_of((parts, len(groups), rows, lanes), jnp.bfloat16)]
        out_specs = [pl.BlockSpec((parts, len(groups), rows // steps, lanes), lambda i: (0, 0, i, 0))]
    sums = pl.pallas_call(
        lambda *refs: sum_kernel(len(groups[0]), len(flat), *refs),
        grid=(steps,),
        in_specs=[pl.BlockSpec((parts, rows // steps, lanes), lambda i: (0, i, 0))] * len(flat),
        out_specs=out_specs,
        out_shape=out_shape,
        compiler_params=pltpu.CompilerParams(vmem_limit_bytes=VMEM_LIMIT),
        cost_estimate=pl.CostEstimate(
            flops=flat[0].size * len(flat), bytes_accessed=2 * flat[0].size * (len(flat) + 1), transcendentals=0
        ),
        name="sum",
    )(*flat)
    return [out.reshape(-1, lanes) for out in sums] if apart else sums[0].reshape(parts, -1, lanes)


def pieces_kernel(chunk, place_ref, order_ref, left_ref, right_ref, gain_ref, *refs):
    outs, (held, left_sem, sems) = refs[:-3], refs[-3:]
    layer_count, half, size = held.shape[:3]
    first = place_ref[2] * half
    lefts = pltpu.make_async_copy(left_ref.at[:, pl.ds(first, half)], held, left_sem.at[0])
    lefts.start()
    copies = []
    turns = []
    for distance, out in enumerate(outs):
        start = (place_ref[0] ^ distance) * chunk
        row = 0
        for layer in range(layer_count):
            for inside in range(chunk):
                turns.append((layer, start + inside, out, row))
                row += size
            for inside in range(chunk):
                source = right_ref.at[layer, first + start + inside]
                copies.append((source, out.at[pl.ds(row, size)]))
                row += size
        copies.append((gain_ref, out.at[pl.ds(row, gain_ref.shape[0])]))
    copies = [
        pltpu.make_async_copy(source, target, sems.at[at]) for at, (source, target) in enumerate(copies)
    ]
    for copy in copies:
        copy.start()
    lefts.wait()
    for layer, block, out, row in turns:
        turned = inner_dot(held[layer, block], order_ref[...], 1, 0)
        out[pl.ds(row, size), :] = turned.astype(jnp.bfloat16)
    for copy in copies:
        copy.wait()


def factor_pieces(place, order, left, right, gain_rows, chunk, width):
    layer_count, blocks, size = left.shape[:3]
    rows = layer_count * 2 * chunk * size + gain_rows.shape[0]
    return pl.pallas_call(
        lambda *refs: pieces_kernel(chunk, *refs),
        in_specs=[SMEM, INSIDE] + [OUTSIDE] * 3,
        out_specs=[INSIDE] * width,
        out_shape=[shape_of((rows, size), jnp.bfloat16)] * width,
        scratch_shapes=[
            pltpu.VMEM((layer_count, blocks // 2, size, size), jnp.bfloat16),
            pltpu.SemaphoreType.DMA((1,)),
            pltpu.SemaphoreType.DMA((width * (layer_count * chunk + 1),)),
        ],
        compiler_params=pltpu.CompilerParams(vmem_limit_bytes=VMEM_LIMIT),
        cost_estimate=pl.CostEstimate(flops=left.size * size, bytes_accessed=4 * left.size, transcendentals=0),
        name="pieces",
    )(place, order, left, right, gain_rows)


def choice(pairs, critic, slots):
    rows = pairs.shape[0]
    named = (pairs[:, 0:1] == critic) | (pairs[:, 1:2] == critic)
    named = jnp.broadcast_to(named.astype(jnp.float32), (rows, slots))
    before = lax.broadcasted_iota(jnp.int32, (rows, rows), 1) < lax.broadcasted_iota(jnp.int32, (rows, rows), 0)
    rank = inner_dot(before.astype(jnp.bfloat16), named.astype(jnp.bfloat16), 1, 0)
    at = lax.broadcasted_iota(jnp.int32, (rows, slots), 1).astype(jnp.float32)
    return jnp.where(rank == at, named, 0.0).astype(jnp.bfloat16)


def pick_kernel(pairs_ref, values_ref, out_ref):
    width, features, slots = out_ref.shape
    pairs = pairs_ref[...]
    chosen = [choice(pairs, critic, slots) for critic in range(width)]
    step = 512
    for start in range(0, features, step):
        part = values_ref[:, pl.ds(start, step)]
        for k in range(width):
            out_ref[k, pl.ds(start, step), :] = inner_dot(part, chosen[k], 0, 0).astype(jnp.bfloat16)


def run_pick(pairs, values, width, slots):
    rows, features = values.shape
    return pl.pallas_call(
        pick_kernel,
        in_specs=[INSIDE] * 2,
        out_specs=INSIDE,
        out_shape=shape_of((width, features, slots), jnp.bfloat16),
        compiler_params=pltpu.CompilerParams(vmem_limit_bytes=VMEM_LIMIT),
        cost_estimate=pl.CostEstimate(
            flops=2 * rows * features * slots * width, bytes_accessed=8 * rows * features, transcendentals=0
        ),
        name="pick",
    )(pairs, values)


def combine_kernel(pairs_ref, came_ref, out_ref):
    width, features, slots = came_ref.shape
    pairs = pairs_ref[...]
    chosen = [choice(pairs, critic, slots) for critic in range(width)]
    step = 512
    for start in range(0, features, step):
        total = sum(inner_dot(chosen[k], came_ref[k, pl.ds(start, step), :], 1, 1) for k in range(width))
        out_ref[:, pl.ds(start, step)] = (0.5 * total).astype(jnp.bfloat16)


def run_combine(pairs, came):
    rows = pairs.shape[0]
    return pl.pallas_call(
        combine_kernel,
        in_specs=[INSIDE] * 2,
        out_specs=INSIDE,
        out_shape=shape_of((rows, came.shape[1]), jnp.bfloat16),
        compiler_params=pltpu.CompilerParams(vmem_limit_bytes=VMEM_LIMIT),
        cost_estimate=pl.CostEstimate(
            flops=2 * rows * came.size, bytes_accessed=4 * came.size, transcendentals=0
        ),
        name="combine",
    )(pairs, came)


FORWARD_COST = 4_000_000_000
BACKWARD_COST = 5_000_000_000


def assemble_kernel(layers, factor, place_ref, order_ref, *refs):
    count = 2 * len(layers)
    sources, (left_ref, right_ref) = refs[:count], refs[count : count + 2]
    held, wide = refs[count + 2 : 2 * count + 2], refs[2 * count + 2 : 3 * count + 2]
    in_sems, out_sems = refs[3 * count + 2 :]
    origin, core = place_ref[0] ^ place_ref[1], place_ref[2]
    order = order_ref[...]
    arrivals = [
        pltpu.make_async_copy(source, held[at], in_sems.at[at]) for at, source in enumerate(sources)
    ]
    for copy in arrivals:
        copy.start()
    leaving = []
    for at in range(count):
        arrivals[at].wait()
        half = core if at % 2 == 0 else 1 - core
        width, _, _, chunk = held[at].shape[:4]
        for k in range(width):
            start = (half * width + (origin ^ k if at < 2 else k)) * chunk
            for inside, layer in enumerate(layers[at // 2]):
                for block in range(chunk):
                    left = inner_dot(held[at][k, inside, 0, block], order, 1, 1)
                    wide[at][k, inside, 0, block] = left * factor
                wide[at][k, inside, 1] = held[at][k, inside, 1].astype(jnp.float32) * factor
                for which, target in enumerate((left_ref, right_ref)):
                    copy = pltpu.make_async_copy(
                        wide[at].at[k, inside, which],
                        target.at[layer, pl.ds(start, chunk)],
                        out_sems.at[len(leaving)],
                    )
                    copy.start()
                    leaving.append(copy)
    for copy in leaving:
        copy.wait()


def run_assemble(place, order, pieces, layers, factor):
    piece = pieces[0].shape
    layer_count = sum(len(group) for group in layers)
    out = shape_of((layer_count, 2 * piece[0] * piece[3]) + piece[4:], jnp.float32)
    return pl.pallas_call(
        lambda *refs: assemble_kernel(layers, factor, *refs),
        in_specs=[SMEM, INSIDE] + [OUTSIDE] * len(pieces),
        out_specs=[OUTSIDE] * 2,
        out_shape=[out] * 2,
        scratch_shapes=[pltpu.VMEM(part.shape, jnp.bfloat16) for part in pieces]
        + [pltpu.VMEM(part.shape, jnp.float32) for part in pieces]
        + [
            pltpu.SemaphoreType.DMA((len(pieces),)),
            pltpu.SemaphoreType.DMA((4 * layer_count * piece[0],)),
        ],
        compiler_params=pltpu.CompilerParams(vmem_limit_bytes=VMEM_LIMIT),
        cost_estimate=pl.CostEstimate(flops=0, bytes_accessed=4 * math.prod(out.shape) * 3, transcendentals=0),
        name="assemble",
    )(place, order, *pieces)


def plane_routes(width, replicas):
    bits = width.bit_length() - 1
    orders = [[(step + d) % bits for step in range(bits)] for d in range(replicas)]
    every = [(s, t, d) for s in range(width) for t in range(width) for d in range(replicas)]

    def route(move):
        def index(s, t, d):
            return (s * width + t) * replicas + d

        return [(index(*place), index(*move(*place))) for place in every]

    ranks = [[0] * width for _ in range(replicas)]
    for d in range(replicas):
        for r in range(width):
            ranks[d][sum(((r >> at) & 1) << orders[d][at] for at in range(bits))] = r
    return {
        "across": [route(lambda s, t, d, at=at: (s ^ (1 << orders[d][at]), t, d)) for at in range(bits)],
        "cores": route(lambda s, t, d: (s, t, 1 - d)),
        "sections": [route(lambda s, t, d, k=k: (s ^ k, t, d)) for k in range(width)],
        "homes": [route(lambda s, t, d, j=j: (t, t ^ s ^ j, d)) for j in range(width)],
    }, ranks


def plane_shards(patches, teacher, critic_pairs, left_factors, right_factors, norm_gains):
    width = lax.axis_size("section")
    replicas = lax.axis_size("dp")
    tok_rows, feat_local = patches.shape
    layer_count, local_blocks, size = left_factors.shape[1:4]
    blocks = feat_local * width // size
    wide = 2 * tok_rows // 3
    chunk = local_blocks // (replicas * width)
    layer_rows = 2 * chunk * size
    routes, ranks = plane_routes(width, replicas)
    section = lax.axis_index("section")
    tensor = lax.axis_index("tensor")
    core = lax.axis_index("dp")
    place = jnp.stack([section, tensor, core]).astype(jnp.int32)
    tie = lax.optimization_barrier

    def move(value, route):
        return lax.ppermute(value, AXES, route)

    def move_all(values, name):
        return [move(value, route) for value, route in zip(values, routes[name])]

    def send(values, name):
        return [values[0]] + [move(values[k], routes[name][k]) for k in range(1, width)]

    def gather_two(pair):
        return pair, move(pair, routes["across"][1]), move(pair, routes["cores"])

    def gather_three(pair, other, peer):
        return [pair, other, peer, move(other, routes["cores"])]

    def as_weights(parts):
        return [part.reshape(2 * width, -1, 2, chunk, size, size) for part in parts]

    block = jnp.arange(blocks, dtype=jnp.int32)
    inside = block % local_blocks
    replica = inside // (width * chunk)
    part = (replica != core).astype(jnp.int32)
    distance = section ^ ((inside // chunk) % width)
    quarter = block // local_blocks
    rank = jnp.array(ranks, jnp.int32)[replica, distance]
    table = jnp.stack(
        [
            ((part * width + index) * width + piece) * chunk + inside % chunk
            for index, piece in (
                (rank, quarter),
                (distance, quarter),
                (distance, tensor ^ section ^ distance ^ quarter),
            )
        ]
    ).astype(jnp.int32)

    def to_planes(value):
        return lax.all_to_all(value, "tensor", split_axis=0, concat_axis=0, tiled=True)

    def to_sections(value):
        return lax.all_to_all(value, "section", split_axis=0, concat_axis=0, tiled=True)

    half_layers = layer_count // 2
    fold = size // blocks
    columns = jnp.arange(size)
    order = (columns[:, None] == (columns % blocks) * fold + columns // blocks).astype(jnp.bfloat16)
    gain_rows = norm_gains[0].reshape(-1, size)
    patch_sent = run_pick(critic_pairs, patches, width, wide)
    patch_sent, left, right, teacher = tie((patch_sent, left_factors[0], right_factors[0], teacher))
    patch_came = to_planes(patch_sent).reshape(-1, wide)
    pieces = factor_pieces(place, order, left, right, gain_rows, chunk, width)
    spread = send(pieces, "sections")
    cut, end = half_layers * layer_rows, layer_count * layer_rows
    first = by_section(place, spread, [(0, cut), (end, gain_rows.shape[0])])
    second = by_section(place, spread, [(cut, end - cut)])
    target_sent = run_pick(critic_pairs, teacher, width, wide)
    patch_came, first, second, target_sent = tie((patch_came, first, second, target_sent))
    first = to_planes(first)
    first, second = tie((first, second))
    second = to_planes(second)
    lowest = [first[:, at * layer_rows : (at + 1) * layer_rows] for at in range(half_layers)]
    beside = [move(value, routes["across"][0]) for value in lowest[:2]]
    gains = first[:, cut:].reshape(width, layer_count + 1, local_blocks, size)
    gains = gains.transpose(1, 3, 0, 2).reshape(layer_count + 1, size, blocks)
    end_gain = gains[layer_count].reshape(size, CHUNKS, blocks // CHUNKS).transpose(1, 0, 2)
    end_gain = end_gain.astype(jnp.float32)
    lowest, beside, gains, end_gain = tie((lowest, beside, gains, end_gain))
    flying = {0: gather_two(joined([lowest[0], beside[0]]))}
    flying, second, target_sent = tie((flying, second, target_sent))
    for layer in range(half_layers, layer_count):
        at = (layer - half_layers) * layer_rows
        lowest.append(second[:, at : at + layer_rows])
    target = to_planes(target_sent).reshape(-1, wide)
    weights = [as_weights(gather_three(*flying.pop(0)))]
    flying[1] = gather_two(joined([lowest[1], beside[1]]))
    steps = {2: (lowest[2], move(lowest[2], routes["across"][0]))}
    weights, flying, steps = tie((weights, flying, steps))

    residual = patch_came
    sums = jnp.zeros((8, wide), jnp.float32)
    stored = []
    for layer in range(layer_count):
        ahead = {}
        if layer + 1 < layer_count:
            ahead["weights"] = gather_three(*flying.pop(layer + 1))
        if layer + 2 < layer_count:
            ahead["two"] = gather_two(joined(list(steps.pop(layer + 2))))
        if layer + 3 < layer_count:
            ahead["one"] = (lowest[layer + 3], move(lowest[layer + 3], routes["across"][0]))
        following, u, z, slope, scale, sums = run_forward(
            table, gains[layer], sums, residual, weights[layer], 0
        )
        stored.append(((slope, z, u), scale, residual))
        residual, sums, ahead = tie((following, sums, ahead))
        if layer + 1 < layer_count:
            weights.append(as_weights(ahead["weights"]))
        if layer + 2 < layer_count:
            flying[layer + 2] = ahead["two"]
        if layer + 3 < layer_count:
            steps[layer + 3] = ahead["one"]
        if layer == layer_count - 2:
            residual, sums, target = tie((residual, sums, target))

    def core_sum(mine, other):
        return (mine, move(other, routes["cores"]))

    def plane_sum(mine, other):
        return send(run_sum([(mine, other)], width), "sections")

    def both_halves(whole):
        pair = (whole, move(whole, routes["cores"]))
        return [part.reshape(width, -1, 2, chunk, size, size) for part in pair]

    steps = (core_sum, plane_sum)
    gradient = residual
    underway = []
    for layer in range(layer_count - 1, -1, -1):
        turning = layer == layer_count - 1
        last = layer == 0
        kept, scale, inputs = stored[layer]
        sources = (gradient, inputs, target) if turning else (gradient, inputs)
        underway = [(at + 1, steps[at](*state)) if at < len(steps) else (at, state) for at, state in underway]
        gradient, mine, other = run_backward(
            table,
            gains[layer],
            end_gain,
            scale,
            kept,
            weights[layer],
            0,
            sources,
            turning,
            last,
        )
        gradient, mine, other, states = tie((gradient, mine, other, [state for _, state in underway]))
        underway = [(at, state) for (at, _), state in zip(underway, states)]
        underway.append((0, (mine, other)))

    returned = to_planes(gradient.reshape(width, feat_local, wide))
    ended = [steps[at](*state) if at < len(steps) else state for at, state in underway][::-1]
    ended = tie(ended)
    ended[0] = plane_sum(*ended[0])
    others = to_planes(run_sum(ended[1:], width, apart=False))
    home = run_sum(ended[:1], width)
    home, returned = tie((home, returned))
    home = move_all(home, "homes")
    d_patches = run_combine(critic_pairs, returned)
    others = to_sections(others)
    d_patches, home, others = tie((d_patches, home, others))
    homes_of = both_halves(joined(home)) + both_halves(others)
    grad_factor = 1.0 / math.sqrt(2 * tok_rows * width * replicas)
    grad_left, grad_right = run_assemble(
        place, order, homes_of, [(0,), tuple(range(1, layer_count))], grad_factor
    )
    return (d_patches, grad_left[None], grad_right[None])


def solution(mesh):
    in_specs = (
        P(("section", "dp"), "tensor"),
        P(("section", "dp"), "tensor"),
        P(("section", "dp"), None),
        P("section", None, "tensor", None, None),
        P("section", None, "tensor", None, None),
        P("section", None, "tensor"),
    )
    out_specs = (
        P(("section", "dp"), "tensor"),
        P("section", None, "tensor", None, None),
        P("section", None, "tensor", None, None),
    )
    body = plane_shards if planes_fit(mesh) else layered_shards
    return jax.shard_map(
        body, mesh=mesh, in_specs=in_specs, out_specs=out_specs, check_vma=False)
```
